32 devices in a mesh: wide: 16 (over z, y, x), narrow: 2 (over core).
Axes of the slice: x: 2, y: 2, z: 4, core: 2. Of those that a mesh axis runs over, the one named last changes fastest.
Arguments:
- tokens: bfloat16 [64, 1024, 768], P(('wide', 'narrow')), may hold values from -6 to 6
- lengths: int32 [64], P(('wide', 'narrow')), may hold values from 64 to 1024, as said below
- rand_mix: bfloat16 [12288, 1024], P(('wide', 'narrow')), may hold values from -6 to 6
- w_value: bfloat16 [768, 768], P(('wide', 'narrow')), may hold values from -0.21875 to 0.21875
- w_out: bfloat16 [768, 768], P(('wide', 'narrow')), may hold values from -0.875 to 0.875
- w_up: bfloat16 [768, 3072], P(('wide', 'narrow')), may hold values from -0.21875 to 0.21875
- w_down: bfloat16 [3072, 768], P(('wide', 'narrow')), may hold values from -0.109375 to 0.109375
- gain_mix: bfloat16 [768], P(('wide', 'narrow')), may hold values from 0.099609375 to 1.8984375
- gain_ffn: bfloat16 [768], P(('wide', 'narrow')), may hold values from 0.099609375 to 1.8984375
- grad_out: bfloat16 [64, 1024, 768], P(('wide', 'narrow')), may hold values from -6 to 6
Outputs:
- output: float32 [64, 1024, 768], P(('wide', 'narrow'))
- grad_tokens: float32 [64, 1024, 768], P(('wide', 'narrow'))
- grad_rand: float32 [12288, 1024], P(('wide', 'narrow'))
- grad_value: float32 [768, 768], P(('wide', 'narrow'))
- grad_outproj: float32 [768, 768], P(('wide', 'narrow'))
- grad_up: float32 [768, 3072], P(('wide', 'narrow'))
- grad_down: float32 [3072, 768], P(('wide', 'narrow'))
- grad_gain_mix: float32 [768], P(('wide', 'narrow'))
- grad_gain_ffn: float32 [768], P(('wide', 'narrow'))
The draws below stay inside these ranges and needn't reach their ends.
Inputs may be any that keep to these rules, and one draw needn't show every extreme that they name: `lengths`: some item has exactly 1024 valid tokens and some exactly 64.
All inputs are finite; a program needn't handle non-finite values.
Results may differ from the reference program's by a relative error of at most 0.009.
Values may be sent and summed in bfloat16 or wider, within the bound.
No kernel may reach another device: no remote copies, remote signals or barrier semaphores. Data moves between devices by JAX's collectives and lax.ppermute only.
A program may use at most 448 MiB of HBM per device.

```python
import jax
import jax.numpy as jnp
from jax import lax

D = 768
HEADS = 12
HEAD = 64
FF = 3072
LMAX = 1024
MINLEN = 64
ITEMS = 64


def draw_lengths(key, part):
    key = jax.random.fold_in(key, 11)
    first_key, second_key = jax.random.split(key)
    drawn = jax.random.randint(first_key, (ITEMS,), MINLEN, LMAX + 1)
    order = jax.random.permutation(second_key, ITEMS)
    drawn = drawn.at[order[0]].set(LMAX)
    drawn = drawn.at[order[1]].set(MINLEN)
    return drawn.astype(jnp.int32)


def level_of(rng, extent, cuts, smallest, top_value):
    def one(position, shards_of):
        draws = jax.random.uniform(jax.random.fold_in(jax.random.fold_in(rng, 6), position), (shards_of,), jnp.float32, smallest / len(cuts), top_value / len(cuts))
        return jnp.repeat(jnp.exp(draws), extent[position] // shards_of).reshape((-1,) + (1,) * (len(extent) - position - 1))

    loudness = one(*cuts[0])
    for cut in cuts[1:]:
        loudness = loudness * one(*cut)
    return loudness


def noise(key, shape, spread, most, cuts=(), held_as=jnp.bfloat16):
    factor_of = level_of(key, shape, cuts, -0.22, 0.18) if cuts else 1.0
    result = jax.random.normal(key, shape, jnp.float32) * spread * factor_of
    return jnp.minimum(jnp.maximum(result, -most), most).astype(held_as)


def setup_inputs(seed: int = 0) -> dict:
    arg_keys = jax.random.split(jax.random.key(seed), 11)
    return {
        "tokens": noise(arg_keys[0], (ITEMS, LMAX, D), 1.0, 6.0, ((0, 32),)),
        "lengths": draw_lengths(jax.random.fold_in(arg_keys[10], 71), 0),
        "rand_mix": noise(arg_keys[2], (HEADS * LMAX, LMAX), 1.5, 6.0, ((0, 32),)),
        "w_value": noise(arg_keys[3], (D, D), D ** -0.5, 0.21875, ((0, 32),)),
        "w_out": noise(arg_keys[4], (D, D), (D // 16) ** -0.5, 0.875, ((0, 32),)),
        "w_up": noise(arg_keys[5], (D, FF), D ** -0.5, 0.21875, ((0, 32),)),
        "w_down": noise(arg_keys[6], (FF, D), FF ** -0.5, 0.109375, ((0, 32),)),
        "gain_mix": jnp.clip(1.0 + 0.18 * jax.random.normal(arg_keys[7], (D,), jnp.float32), 0.099609375, 1.8984375).astype(jnp.bfloat16),
        "gain_ffn": jnp.clip(1.0 + 0.18 * jax.random.normal(arg_keys[8], (D,), jnp.float32), 0.099609375, 1.8984375).astype(jnp.bfloat16),
        "grad_out": noise(arg_keys[9], (ITEMS, LMAX, D), 1.0, 6.0, ((0, 32),)),
    }


EPSILON = 1e-05

@jax.custom_vjp
def low(v):
    return lax.optimization_barrier(v.astype(jnp.bfloat16)).astype(jnp.float32)

@jax.custom_vjp
def low_back(v):
    return v

def low_keep(v):
    return (low(v), None)

def low_pass(kept, grad):
    return (grad,)

def back_keep(v):
    return (v, None)

def back_low(kept, grad):
    return (low(grad),)
low.defvjp(low_keep, low_pass)
low_back.defvjp(back_keep, back_low)

def rms_norm(values, gain):
    scale = lax.rsqrt(lax.optimization_barrier(jnp.mean(values * values, axis=-1, keepdims=True)) + EPSILON)
    return values * scale * gain

def layer_forward(item_tokens, length, rand_mix, w_value, w_out, w_up, w_down, gain_mix, gain_ffn):
    highest = lax.Precision.HIGHEST
    positions = jnp.arange(LMAX, dtype=jnp.int32)
    row_valid = (positions < length).astype(jnp.float32)
    normed = low(rms_norm(item_tokens, gain_mix))
    values = low(low_back(jnp.dot(normed, w_value, precision=highest)))
    heads_value = values.reshape(LMAX, HEADS, HEAD).transpose(1, 0, 2)
    scores = jnp.where(row_valid[None, None, :] > 0, rand_mix.reshape(HEADS, LMAX, LMAX), -1e+30)
    row_peak = lax.optimization_barrier(jnp.max(scores, axis=-1, keepdims=True))
    exponent = jnp.exp(scores - row_peak)
    attention = low(exponent / lax.optimization_barrier(jnp.sum(exponent, axis=-1, keepdims=True)) * row_valid[None, :, None])
    mixed = jnp.einsum('hij,hjd->ihd', attention, heads_value, precision=highest).reshape(LMAX, HEADS * HEAD)
    mixed = low(low_back(mixed))
    residual = item_tokens + low_back(jnp.dot(mixed, w_out, precision=highest))
    normed_two = low(rms_norm(residual, gain_ffn))
    up_proj = low_back(jnp.dot(normed_two, w_up, precision=highest))
    active = low(jax.nn.gelu(up_proj))
    branch = low_back(jnp.dot(active, w_down, precision=highest))
    return row_valid[:, None] * (residual + branch)

def reference(tokens, lengths, rand_mix, w_value, w_out, w_up, w_down, gain_mix, gain_ffn, grad_out):
    weights = tuple((weight.astype(jnp.float32) for weight in (rand_mix, w_value, w_out, w_up, w_down, gain_mix, gain_ffn)))
    initial = tuple((jnp.zeros_like(weight) for weight in weights))

    def item_step(totals, paired):
        item_tokens, length, cotangent = paired

        def forward(tokens_float, *weights_float):
            return layer_forward(tokens_float, length, *weights_float)
        outputs, pullback = jax.vjp(forward, item_tokens.astype(jnp.float32), *weights)
        gradients = pullback(cotangent.astype(jnp.float32))
        totals = tuple((total + gradient for total, gradient in zip(totals, gradients[1:])))
        return (totals, (outputs, gradients[0]))
    totals, (output, grad_tokens) = lax.scan(item_step, initial, (tokens, lengths, grad_out))
    return (output, grad_tokens, totals[0], totals[1], totals[2], totals[3], totals[4], totals[5], totals[6])
```

```python
from functools import partial

import jax
import jax.numpy as jnp
from jax import lax
from jax.experimental import pallas as pl
from jax.experimental.pallas import tpu as pltpu
from jax.sharding import PartitionSpec as P

HEADS = 12
HEAD = 64
LMAX = 1024
WIDTH = 768
FF = 3072
EPSILON = 1e-05

BOTH = ("wide", "narrow")
BF16 = jnp.bfloat16
F32 = jnp.float32
MIB = 1 << 20

PARTS = 2
SUBS = 6 // PARTS
RUNS = 8 // PARTS
HALF = 64
HROWS = RUNS * HALF
PLANES = 4
PHEADS = HEADS // PLANES
COL_A, COL_B, COL_C = 384, 384, 256
FSTEP = 384


def dot(a, b, ca, cb):
    return lax.dot_general(a, b, (((ca,), (cb,)), ((), ())), preferred_element_type=F32)


CORE, PLANE, PLACE, LENGTHS = 0, 1, 2, 3


def spec(shape, index):
    return pl.BlockSpec(shape, index)


def held(shape):
    zeros = (0,) * len(shape)
    return pl.BlockSpec(shape, lambda *_: zeros, pipeline_mode=pl.Buffered(1))


def params(limit):
    return pltpu.CompilerParams(vmem_limit_bytes=limit * MIB)


def values_kernel(sc, tok, gain, weight, out):
    step = pl.program_id(0)
    rows = tok.shape[1]
    position = step * rows + lax.broadcasted_iota(jnp.int32, (rows, 1), 0)
    for item in range(2):
        x = tok[item].astype(F32)
        scale = lax.rsqrt(jnp.mean(x * x, axis=-1, keepdims=True) + EPSILON)
        normed = (x * scale * gain[...]).astype(BF16)
        found = dot(normed, weight[...], 1, 0)
        found = jnp.where(position < sc[LENGTHS + item], found, 0.0).astype(BF16)
        for head in range(HEADS):
            out[head, :, item * HEAD : (item + 1) * HEAD] = found[:, head * HEAD : (head + 1) * HEAD]


def run_values(sc, tokens, gain, weight):
    rows = 256
    return pl.pallas_call(
        values_kernel,
        grid_spec=pltpu.PrefetchScalarGridSpec(
            num_scalar_prefetch=1,
            grid=(LMAX // rows,),
            in_specs=[
                spec((2, rows, WIDTH), lambda j, s: (0, j, 0)),
                held((1, WIDTH)),
                held((WIDTH, WIDTH)),
            ],
            out_specs=spec((HEADS, rows, 2 * HEAD), lambda j, s: (0, j, 0)),
        ),
        out_shape=jax.ShapeDtypeStruct((HEADS, LMAX, 2 * HEAD), BF16),
        compiler_params=params(32),
        cost_estimate=pl.CostEstimate(
            flops=2 * 2 * LMAX * WIDTH * WIDTH, bytes_accessed=8 * LMAX * WIDTH, transcendentals=0
        ),
        name="values",
    )(sc, tokens, gain, weight)


def fill_exponents(place, rand, scratch):
    a_near, a_far, b_near, b_far, c_all = rand
    for rel in range(4):
        ry, rx = rel // 2, rel % 2
        where = place ^ rel
        a = (a_near, a_far)[ry]
        b = (b_near, b_far)[rx]
        for k in range(SUBS):
            row = where * SUBS + k
            scratch[row, :, :COL_A] = jnp.exp(a[rx, 0, k].astype(F32)).astype(BF16)
            scratch[row, :, COL_A : COL_A + COL_B] = jnp.exp(b[ry, 0, k].astype(F32)).astype(BF16)
            scratch[row, :, COL_A + COL_B :] = jnp.exp(c_all[0, rel, k].astype(F32)).astype(BF16)


def lane_lengths(sc, shape):
    slot = lax.broadcasted_iota(jnp.int32, shape, 1) // HEAD
    length = jnp.where(slot == 0, sc[LENGTHS], sc[LENGTHS + 1])
    return jnp.where(slot >= 2, jnp.where(slot == 2, sc[LENGTHS + 2], sc[LENGTHS + 3]), length)


def mix_kernel(part, sc, a_near, a_far, b_near, b_far, c_all, v_own, v_far, own, far, mean, inverse, exps, mask):
    @pl.when(pl.program_id(0) == 0)
    def _():
        shape = (LMAX, 4 * HEAD)
        column = lax.broadcasted_iota(jnp.int32, shape, 0)
        mask[...] = (column < lane_lengths(sc, shape)).astype(F32).astype(BF16)

    fill_exponents(sc[PLACE], (a_near, a_far, b_near, b_far, c_all), exps)
    shape = (HROWS, 4 * HEAD)
    line = lax.broadcasted_iota(jnp.int32, shape, 0)
    position = 128 * (PARTS * (line // HALF) + part) + HALF * sc[CORE] + line % HALF
    valid = position < lane_lengths(sc, shape)
    for head in range(PHEADS):
        weights = exps[head * RUNS : (head + 1) * RUNS].reshape(HROWS, LMAX)
        total = dot(weights, mask[...], 1, 0)
        flip = jnp.where(valid, 1.0 / total, 0.0)
        mixed = dot(weights, jnp.concatenate([v_own[head], v_far[head]], axis=1), 1, 0) * flip
        inverse[head] = flip
        mean[head] = mixed
        low = mixed.astype(BF16)
        own[head] = low[:, : 2 * HEAD]
        far[head] = low[:, 2 * HEAD :]


def plane_of(k, sc):
    return lax.rem(sc[PLANE] + PLANES - k, PLANES)


def rand_specs():
    return [
        spec((2, 1, SUBS, HALF, COL_A), lambda k, s: (0, k, 0, 0, 0)),
        spec((2, 1, SUBS, HALF, COL_A), lambda k, s: (0, k, 0, 0, 0)),
        spec((2, 1, SUBS, HALF, COL_B), lambda k, s: (0, k, 0, 0, 0)),
        spec((2, 1, SUBS, HALF, COL_B), lambda k, s: (0, k, 0, 0, 0)),
        spec((1, 4, SUBS, HALF, COL_C), lambda k, s: (k, 0, 0, 0, 0)),
    ]


def plane_spec(rows, lanes):
    return spec((PHEADS, rows, lanes), lambda k, s: (plane_of(k, s), 0, 0))


def run_mix(part, sc, rand, v_own, v_far):
    return pl.pallas_call(
        partial(mix_kernel, part),
        grid_spec=pltpu.PrefetchScalarGridSpec(
            num_scalar_prefetch=1,
            grid=(PLANES,),
            in_specs=rand_specs() + [plane_spec(LMAX, 2 * HEAD)] * 2,
            out_specs=[
                plane_spec(HROWS, 2 * HEAD),
                plane_spec(HROWS, 2 * HEAD),
                plane_spec(HROWS, 4 * HEAD),
                plane_spec(HROWS, 4 * HEAD),
            ],
            scratch_shapes=[
                pltpu.VMEM((4 * SUBS, HALF, LMAX), BF16),
                pltpu.VMEM((LMAX, 4 * HEAD), BF16),
            ],
        ),
        out_shape=[
            jax.ShapeDtypeStruct((HEADS, HROWS, 2 * HEAD), BF16),
            jax.ShapeDtypeStruct((HEADS, HROWS, 2 * HEAD), BF16),
            jax.ShapeDtypeStruct((HEADS, HROWS, 4 * HEAD), F32),
            jax.ShapeDtypeStruct((HEADS, HROWS, 4 * HEAD), F32),
        ],
        compiler_params=params(40),
        cost_estimate=pl.CostEstimate(
            flops=4 * HEADS * HROWS * LMAX * 4 * HEAD,
            bytes_accessed=HEADS * (2 * HROWS * LMAX + 10 * HROWS * 256),
            transcendentals=HEADS * HROWS * LMAX,
        ),
        name="mix",
    )(sc, *rand, v_own, v_far)


def feed_kernel(part, carried, *refs):
    (sc, tok, cot, near, far, w_out, gain, up_w, down_w, *rest) = refs
    if carried:
        (down_in, up_in, out_in, gain_in, _, _, *rest) = rest
    last = part == PARTS - 1
    (output, res_grad, g_own, g_far, d_down, d_up, d_out, d_gain, mixed, resid, normed, branch_grad, back) = rest
    step = pl.program_id(0)
    core = sc[CORE]
    tile = RUNS * 128
    shape = (tile, 1)
    line = lax.broadcasted_iota(jnp.int32, shape, 0)
    position = 128 * (PARTS * (line // 128) + part) + line % 128

    @pl.when(step == 0)
    def _():
        for item in range(2):
            for source, slot in ((near, core), (far, 1 - core)):
                for pair in range(HEADS // 2):
                    for run in range(RUNS):
                        rows = slice(run * HALF, (run + 1) * HALF)
                        lanes = slice(item * HEAD, (item + 1) * HEAD)
                        both = jnp.concatenate(
                            [source[2 * pair, rows, lanes], source[2 * pair + 1, rows, lanes]], axis=1
                        )
                        mixed[item, run, slot, :, pair * 128 : (pair + 1) * 128] = both
        for item in range(2):
            rows = pl.ds(item * tile, tile)
            x = tok[item, :, 0].reshape(tile, WIDTH).astype(F32)
            res = x + dot(mixed[item].reshape(tile, WIDTH), w_out[...], 1, 0)
            resid[rows] = res
            scale = lax.rsqrt(jnp.mean(res * res, axis=-1, keepdims=True) + EPSILON)
            normed[rows] = (res * scale * gain[...]).astype(BF16)
            valid = position < sc[LENGTHS + item]
            grad = cot[item, :, 0].reshape(tile, WIDTH).astype(F32)
            branch_grad[rows] = jnp.where(valid, grad, 0.0).astype(BF16)

    up_block = up_w[0]
    down_block = down_w[...]
    for piece in range(2):
        rows = pl.ds(piece * tile, tile)
        two = normed[rows]
        grad = branch_grad[rows]
        up = dot(two, up_block, 1, 0)
        square = up * up
        inner = 0.7978845608028654 * (up * (1.0 + 0.044715 * square))
        bend = jnp.tanh(inner)
        share = 0.5 * (1.0 + bend)
        active = (up * share).astype(BF16)
        slope = share + 0.5 * up * (1.0 - bend * bend) * (0.7978845608028654 * (1.0 + 3 * 0.044715 * square))
        branch = dot(active, down_block, 1, 0)
        up_grad = (dot(grad, down_block, 1, 1) * slope).astype(BF16)
        two_grad = dot(up_grad, up_block, 1, 1)
        add_down = dot(active, grad, 0, 0)
        add_up = dot(two, up_grad, 0, 0)
        view = output.at[piece, :, 0]
        if piece == 0:
            total_down, total_up = add_down, add_up
        else:
            total_down, total_up = total_down + add_down, total_up + add_up

        @pl.when(step == 0)
        def _():
            view[...] = branch.reshape(RUNS, 2, HALF, WIDTH)
            back[rows] = two_grad

        @pl.when(step > 0)
        def _():
            view[...] += branch.reshape(RUNS, 2, HALF, WIDTH)
            back[rows] += two_grad

    if carried:
        total_down = total_down + down_in[...]
        total_up = total_up + up_in[0]
    if last:
        low = total_down.astype(BF16)
        d_down[0] = low[:, : WIDTH // 2]
        d_down[1] = low[:, WIDTH // 2 :]
        d_up[0] = total_up.astype(BF16)
    else:
        d_down[...] = total_down
        d_up[0] = total_up

    @pl.when(step == pl.num_programs(0) - 1)
    def _():
        for item in range(2):
            rows = pl.ds(item * tile, tile)
            valid = position < sc[LENGTHS + item]
            res = resid[rows]
            branch = output[item, :, 0].reshape(tile, WIDTH)
            output[item, :, 0] = jnp.where(valid, res + branch, 0.0).reshape(RUNS, 2, HALF, WIDTH)
            scale = lax.rsqrt(jnp.mean(res * res, axis=-1, keepdims=True) + EPSILON)
            unit = res * scale
            two_grad = back[rows]
            gained = two_grad * gain[...]
            grad = branch_grad[rows].astype(F32) + scale * (
                gained - unit * jnp.mean(gained * unit, axis=-1, keepdims=True)
            )
            res_grad[item, :, 0] = grad.reshape(RUNS, 2, HALF, WIDTH)
            low = grad.astype(BF16)
            gain_sum = jnp.sum(two_grad * unit, axis=0, keepdims=True)
            out_sum = dot(mixed[item].reshape(tile, WIDTH), low, 0, 0)
            if item == 0:
                gain_total, out_total = gain_sum, out_sum
            else:
                gain_total, out_total = gain_total + gain_sum, out_total + out_sum
            spread = dot(low, w_out[...], 1, 1).astype(BF16)
            mixed[item] = spread.reshape(RUNS, 2, HALF, WIDTH)
        if carried:
            gain_total = gain_total + gain_in[...]
            out_total = out_total + out_in[...]
        d_gain[...] = gain_total
        if last:
            low = out_total.astype(BF16)
            d_out[0] = low[:, : WIDTH // 2]
            d_out[1] = low[:, WIDTH // 2 :]
        else:
            d_out[...] = out_total
        for target, slot in ((g_own, core), (g_far, 1 - core)):
            for pair in range(HEADS // 2):
                for run in range(RUNS):
                    rows = slice(run * HALF, (run + 1) * HALF)
                    lanes = slice(pair * 128, (pair + 1) * 128)
                    one, two = mixed[0, run, slot, :, lanes], mixed[1, run, slot, :, lanes]
                    target[2 * pair, rows, :] = jnp.concatenate([one[:, :HEAD], two[:, :HEAD]], axis=1)
                    target[2 * pair + 1, rows, :] = jnp.concatenate([one[:, HEAD:], two[:, HEAD:]], axis=1)


def run_feed(part, sc, tokens, cotangent, near, far, w_out, gain, up_blocks, w_down, carry):
    last = part == PARTS - 1
    rows = 2 * RUNS * 128
    slab = (2, RUNS, PARTS, 2, HALF, WIDTH)
    block = (2, RUNS, 1, 2, HALF, WIDTH)
    here = lambda f, s: (0, 0, part, 0, 0, 0)
    fixed = lambda shape: pl.BlockSpec(shape, here, pipeline_mode=pl.Buffered(1))
    in_specs = [
        fixed(block),
        fixed(block),
        held((HEADS, HROWS, 2 * HEAD)),
        held((HEADS, HROWS, 2 * HEAD)),
        held((WIDTH, WIDTH)),
        held((1, WIDTH)),
        spec((1, WIDTH, FSTEP), lambda f, s: (f, 0, 0)),
        spec((FSTEP, WIDTH), lambda f, s: (f, 0)),
    ]
    args = [tokens.reshape(slab), cotangent.reshape(slab), near, far, w_out, gain, up_blocks, w_down]
    aliases = {}
    if carry is not None:
        in_specs += [
            spec((FSTEP, WIDTH), lambda f, s: (f, 0)),
            spec((1, WIDTH, FSTEP), lambda f, s: (f, 0, 0)),
            held((WIDTH, WIDTH)),
            held((1, WIDTH)),
            pl.BlockSpec(memory_space=pl.ANY),
            pl.BlockSpec(memory_space=pl.ANY),
        ]
        output, res_grad, d_down, d_up, d_out, d_gain = carry
        args += [d_down, d_up, d_out, d_gain, output, res_grad]
        aliases = {len(args) - 1: 0, len(args): 1}
    if last:
        grad_specs = [
            spec((2, FSTEP, WIDTH // 2), lambda f, s: (0, f, 0)),
            spec((1, WIDTH, FSTEP), lambda f, s: (f, 0, 0)),
            held((2, WIDTH, WIDTH // 2)),
            held((1, WIDTH)),
        ]
        grad_shapes = [
            jax.ShapeDtypeStruct((2, FF, WIDTH // 2), BF16),
            jax.ShapeDtypeStruct((FF // FSTEP, WIDTH, FSTEP), BF16),
            jax.ShapeDtypeStruct((2, WIDTH, WIDTH // 2), BF16),
            jax.ShapeDtypeStruct((1, WIDTH), F32),
        ]
    else:
        grad_specs = [
            spec((FSTEP, WIDTH), lambda f, s: (f, 0)),
            spec((1, WIDTH, FSTEP), lambda f, s: (f, 0, 0)),
            held((WIDTH, WIDTH)),
            held((1, WIDTH)),
        ]
        grad_shapes = [
            jax.ShapeDtypeStruct((FF, WIDTH), F32),
            jax.ShapeDtypeStruct((FF // FSTEP, WIDTH, FSTEP), F32),
            jax.ShapeDtypeStruct((WIDTH, WIDTH), F32),
            jax.ShapeDtypeStruct((1, WIDTH), F32),
        ]
    return pl.pallas_call(
        partial(feed_kernel, part, carry is not None),
        grid_spec=pltpu.PrefetchScalarGridSpec(
            num_scalar_prefetch=1,
            grid=(FF // FSTEP,),
            in_specs=in_specs,
            out_specs=[
                fixed(block),
                fixed(block),
                held((HEADS, HROWS, 2 * HEAD)),
                held((HEADS, HROWS, 2 * HEAD)),
                *grad_specs,
            ],
            scratch_shapes=[
                pltpu.VMEM((2, RUNS, 2, HALF, WIDTH), BF16),
                pltpu.VMEM((rows, WIDTH), F32),
                pltpu.VMEM((rows, WIDTH), BF16),
                pltpu.VMEM((rows, WIDTH), BF16),
                pltpu.VMEM((rows, WIDTH), F32),
            ],
        ),
        out_shape=[
            jax.ShapeDtypeStruct(slab, F32),
            jax.ShapeDtypeStruct(slab, F32),
            jax.ShapeDtypeStruct((HEADS, HROWS, 2 * HEAD), BF16),
            jax.ShapeDtypeStruct((HEADS, HROWS, 2 * HEAD), BF16),
            *grad_shapes,
        ],
        input_output_aliases=aliases,
        compiler_params=params(60),
        cost_estimate=pl.CostEstimate(
            flops=2 * rows * (6 * WIDTH * FF + 3 * WIDTH * WIDTH),
            bytes_accessed=16 * rows * WIDTH + 8 * WIDTH * FF,
            transcendentals=rows * FF,
        ),
        name="feed",
    )(sc, *args)


def unmix_kernel(part, carried, *refs):
    (sc, a_near, a_far, b_near, b_far, c_all, v_own, v_far, g_own, g_far, mean, inverse, *rest) = refs
    if carried:
        (own_in, far_in, *rest) = rest
    (ga_keep, ga_send, gb_keep, gb_send, gc_all, own, far, exps, grads) = rest
    place = sc[PLACE]
    fill_exponents(place, (a_near, a_far, b_near, b_far, c_all), exps)
    column = lax.broadcasted_iota(jnp.int32, (1, LMAX), 1)
    line = lax.broadcasted_iota(jnp.int32, (LMAX, 2 * HEAD), 0)
    slot = lax.broadcasted_iota(jnp.int32, (LMAX, 2 * HEAD), 1) // HEAD
    for head in range(PHEADS):
        weights = exps[head * RUNS : (head + 1) * RUNS].reshape(HROWS, LMAX)
        scaled = jnp.concatenate([g_own[head], g_far[head]], axis=1).astype(F32) * inverse[head]
        low = scaled.astype(BF16)
        product = low.astype(F32) * mean[head]
        score = dot(low, jnp.concatenate([v_own[head], v_far[head]], axis=1), 1, 1)
        for item in range(4):
            delta = jnp.sum(product[:, item * HEAD : (item + 1) * HEAD], axis=-1, keepdims=True)
            score = score - delta * (column < sc[LENGTHS + item]).astype(F32)
        score = score * weights.astype(F32)
        grads[head * RUNS : (head + 1) * RUNS] = score.astype(BF16).reshape(RUNS, HALF, LMAX)
        back = dot(weights, low, 0, 0)
        for target, extra, first in ((own, own_in if carried else None, 0), (far, far_in if carried else None, 2)):
            found = back[:, first * HEAD : (first + 2) * HEAD]
            length = jnp.where(slot == 0, sc[LENGTHS + first], sc[LENGTHS + first + 1])
            found = jnp.where(line < length, found, 0.0)
            if carried:
                found = found + extra[head]
            target[head] = found.astype(target.dtype)
    for rel in range(4):
        ry, rx = rel // 2, rel % 2
        a = (ga_keep, ga_send)[ry]
        b = (gb_keep, gb_send)[rx]
        for k in range(SUBS):
            row = (place ^ rel) * SUBS + k
            a[rx, 0, k] = grads[row, :, :COL_A]
            b[ry, 0, k] = grads[row, :, COL_A : COL_A + COL_B]
            gc_all[0, rel, k] = grads[row, :, COL_A + COL_B :]


def run_unmix(part, sc, rand, v_own, v_far, g_own, g_far, mean, inverse, carry):
    last = part == PARTS - 1
    in_specs = rand_specs() + [
        plane_spec(LMAX, 2 * HEAD),
        plane_spec(LMAX, 2 * HEAD),
        plane_spec(HROWS, 2 * HEAD),
        plane_spec(HROWS, 2 * HEAD),
        plane_spec(HROWS, 4 * HEAD),
        plane_spec(HROWS, 4 * HEAD),
    ]
    args = [*rand, v_own, v_far, g_own, g_far, mean, inverse]
    if carry is not None:
        in_specs += [plane_spec(LMAX, 2 * HEAD)] * 2
        args += list(carry)
    return pl.pallas_call(
        partial(unmix_kernel, part, carry is not None),
        grid_spec=pltpu.PrefetchScalarGridSpec(
            num_scalar_prefetch=1,
            grid=(PLANES,),
            in_specs=in_specs,
            out_specs=rand_specs() + [plane_spec(LMAX, 2 * HEAD)] * 2,
            scratch_shapes=[
                pltpu.VMEM((4 * SUBS, HALF, LMAX), BF16),
                pltpu.VMEM((4 * SUBS, HALF, LMAX), BF16),
            ],
        ),
        out_shape=[jax.ShapeDtypeStruct((2, PLANES, SUBS, HALF, COL_A), BF16)] * 2
        + [jax.ShapeDtypeStruct((2, PLANES, SUBS, HALF, COL_B), BF16)] * 2
        + [jax.ShapeDtypeStruct((PLANES, 4, SUBS, HALF, COL_C), BF16)]
        + [
            jax.ShapeDtypeStruct((HEADS, LMAX, 2 * HEAD), F32),
            jax.ShapeDtypeStruct((HEADS, LMAX, 2 * HEAD), BF16 if last else F32),
        ],
        compiler_params=params(56),
        cost_estimate=pl.CostEstimate(
            flops=4 * HEADS * HROWS * LMAX * 4 * HEAD,
            bytes_accessed=HEADS * (4 * HROWS * LMAX + 10 * HROWS * 256 + 8 * LMAX * 256),
            transcendentals=HEADS * HROWS * LMAX,
        ),
        name="unmix",
    )(sc, *args)


def close_kernel(sc, tok, res_grad, own, far, gain, weight, tok_grad, d_value, d_gain, total):
    step = pl.program_id(0)
    rows = tok.shape[1]
    for item in range(2):
        lanes = slice(item * HEAD, (item + 1) * HEAD)
        pieces = [
            (own[head, :, lanes] + far[head, :, lanes].astype(F32)).astype(BF16) for head in range(HEADS)
        ]
        back = jnp.concatenate(pieces, axis=1)
        x = tok[item].astype(F32)
        scale = lax.rsqrt(jnp.mean(x * x, axis=-1, keepdims=True) + EPSILON)
        unit = x * scale
        normed = (unit * gain[...]).astype(BF16)
        normed_grad = dot(back, weight[...], 1, 1)
        gained = normed_grad * gain[...]
        tok_grad[item] = res_grad[item] + scale * (gained - unit * jnp.mean(gained * unit, axis=-1, keepdims=True))
        gain_sum = jnp.sum(normed_grad * unit, axis=0, keepdims=True)
        value_sum = dot(normed, back, 0, 0)
        if item == 0:
            gain_total, value_total = gain_sum, value_sum
        else:
            gain_total, value_total = gain_total + gain_sum, value_total + value_sum

    @pl.when(step == 0)
    def _():
        d_gain[...] = gain_total
        total[...] = value_total

    @pl.when(step > 0)
    def _():
        d_gain[...] += gain_total
        total[...] += value_total

    @pl.when(step == pl.num_programs(0) - 1)
    def _():
        low = total[...].astype(BF16)
        d_value[0] = low[:, : WIDTH // 2]
        d_value[1] = low[:, WIDTH // 2 :]


def run_close(sc, tokens, res_grad, own, far, gain, weight):
    rows = 256
    return pl.pallas_call(
        close_kernel,
        grid_spec=pltpu.PrefetchScalarGridSpec(
            num_scalar_prefetch=1,
            grid=(LMAX // rows,),
            in_specs=[
                spec((2, rows, WIDTH), lambda j, s: (0, j, 0)),
                spec((2, rows, WIDTH), lambda j, s: (0, j, 0)),
                spec((HEADS, rows, 2 * HEAD), lambda j, s: (0, j, 0)),
                spec((HEADS, rows, 2 * HEAD), lambda j, s: (0, j, 0)),
                held((1, WIDTH)),
                held((WIDTH, WIDTH)),
            ],
            out_specs=[
                spec((2, rows, WIDTH), lambda j, s: (0, j, 0)),
                held((2, WIDTH, WIDTH // 2)),
                held((1, WIDTH)),
            ],
            scratch_shapes=[pltpu.VMEM((WIDTH, WIDTH), F32)],
        ),
        out_shape=[
            jax.ShapeDtypeStruct((2, LMAX, WIDTH), F32),
            jax.ShapeDtypeStruct((2, WIDTH, WIDTH // 2), BF16),
            jax.ShapeDtypeStruct((1, WIDTH), F32),
        ],
        compiler_params=params(40),
        cost_estimate=pl.CostEstimate(
            flops=4 * 2 * LMAX * WIDTH * WIDTH, bytes_accessed=26 * LMAX * WIDTH, transcendentals=0
        ),
        name="close",
    )(sc, tokens, res_grad, own, far, gain, weight)


DEVICES = 32
TO_CORE, TO_X, TO_Y = 1, 2, 4


def swap(x, bit):
    return lax.ppermute(x, BOTH, [(d, d ^ bit) for d in range(DEVICES)])


def ring(x):
    return lax.ppermute(x, BOTH, [(d, (d + 8) % DEVICES) for d in range(DEVICES)])


def pick(x, index, axis=0):
    return lax.dynamic_index_in_dim(x, index, axis, keepdims=False)


def ordered(flag, one, two, axis=0, joined=jnp.stack):
    return jnp.where(flag == 0, joined([one, two], axis), joined([two, one], axis))


def ring_pieces(x):
    pieces = [x]
    for _ in range(PLANES - 1):
        pieces.append(ring(pieces[-1]))
    return pieces


def gather_rand(shard):
    both = jnp.stack([shard[..., :COL_A], shard[..., COL_A : COL_A + COL_B]])
    c_own = shard[..., COL_A + COL_B :]
    c_line = jnp.stack([c_own, swap(c_own, TO_X)])
    c_plane = jnp.concatenate([c_line, swap(c_line, TO_Y)])
    pieces = ring_pieces(both)
    c_all = jnp.stack(ring_pieces(c_plane))
    a_own = jnp.stack([p[0] for p in pieces])
    b_own = jnp.stack([p[1] for p in pieces])
    a_near = jnp.stack([a_own, swap(a_own, TO_X)])
    b_near = jnp.stack([b_own, swap(b_own, TO_Y)])
    return a_near, swap(a_near, TO_Y), b_near, swap(b_near, TO_X), c_all


def add_low(one, two):
    return (one.astype(F32) + two.astype(F32)).astype(BF16)


def ring_sum(pieces):
    moving = pieces[1]
    for k in (2, 3):
        moving = add_low(ring(moving), pieces[k])
    return ring(moving).astype(F32) + pieces[0].astype(F32)


def scatter_rand(a_keep, a_send, b_keep, b_send, c_all):
    a_line = add_low(a_keep, swap(a_send, TO_Y))
    b_line = add_low(b_keep, swap(b_send, TO_X))
    a_own = add_low(a_line[0], swap(a_line[1], TO_X))
    b_own = add_low(b_line[0], swap(b_line[1], TO_Y))
    c_plane = ring_sum([c_all[k] for k in range(PLANES)])
    c_line = c_plane[:2] + swap(c_plane[2:].astype(BF16), TO_Y).astype(F32)
    c_own = c_line[0] + swap(c_line[1].astype(BF16), TO_X).astype(F32)
    both = ring_sum([jnp.stack([a_own[k], b_own[k]]) for k in range(PLANES)])
    return jnp.concatenate([both[0], both[1], c_own], axis=-1)


def gather_chips(x, place, order):
    z, y, x_at = place
    done = []
    for axis in order:
        at = sorted(done + [axis]).index(axis)
        if axis == 0:
            own = ring_pieces(x)
            line = jnp.stack([own[k] for k in (3, 2, 1, 0, 3, 2, 1)], at)
            x = lax.dynamic_slice_in_dim(line, PLANES - 1 - z, PLANES, at)
        elif axis == 1:
            x = ordered(y, x, swap(x, TO_Y), at)
        else:
            x = ordered(x_at, x, swap(x, TO_X), at)
        done.append(axis)
    return x.reshape((16,) + x.shape[3:])


def scatter_chips(x, place, order, lead=0):
    z, y, x_at = place
    x = x.reshape(x.shape[:lead] + (4, 2, 2) + x.shape[lead + 1 :])
    left = [0, 1, 2]
    for axis in order:
        at = lead + left.index(axis)
        if axis == 0:
            x = ring_sum([pick(x, lax.rem(z + PLANES - k, PLANES), at).astype(BF16) for k in range(PLANES)])
        else:
            mine, bit = (y, TO_Y) if axis == 1 else (x_at, TO_X)
            got = swap(pick(x, 1 - mine, at).astype(BF16), bit)
            x = pick(x, mine, at).astype(F32) + got.astype(F32)
        left.remove(axis)
    return x


def chip_shards(tokens, lengths, rand_mix, w_value, w_out, w_up, w_down, gain_mix, gain_ffn, grad_out):
    wide = lax.axis_index("wide")
    core = lax.axis_index("narrow")
    place = (wide // 4, (wide // 2) % 2, wide % 2)
    half = WIDTH // 2

    far_lengths = swap(lengths, TO_CORE)
    head = jnp.stack([core, place[0], wide % 4]).astype(jnp.int32)
    sc = jnp.concatenate([head, lengths, far_lengths])

    gains = jnp.pad(jnp.concatenate([gain_mix, gain_ffn])[None], ((0, 7), (0, half - 48)))
    halves = [
        jnp.concatenate(
            [
                w_value[:, c * half : (c + 1) * half],
                gains,
                w_out[:, c * half : (c + 1) * half],
                *[w_up[:, (4 * c + j) * half : (4 * c + j + 1) * half] for j in range(4)],
                w_down[:, c * half : (c + 1) * half],
            ]
        )
        for c in range(2)
    ]
    both = jnp.stack(halves)
    joined = ordered(core, pick(both, core), swap(pick(both, 1 - core), TO_CORE))
    part_of = lambda start, rows: joined[:, start : start + rows].reshape(2 * rows, half)
    rand = rand_mix.reshape(3, 2, HALF, LMAX)
    blocks = ordered(core, pick(rand, core, 1), swap(pick(rand, 1 - core, 1), TO_CORE), 0, jnp.concatenate)

    first = gather_chips(joined[:, :32].reshape(64, half), place, (2, 1, 0))
    rands = [gather_rand(blocks[part::PARTS]) for part in range(PARTS)]
    up_rows = joined[:, 56:152].reshape(2, 4, 24, half).transpose(1, 0, 2, 3).reshape(4, 48, half)
    second = gather_chips(jnp.concatenate([part_of(32, 24)[None], up_rows]), place, (0, 1, 2))
    third = gather_chips(part_of(152, 96), place, (0, 2, 1))

    first_far = swap(first, TO_CORE)
    second_far = swap(second, TO_CORE)
    third_far = swap(third, TO_CORE)
    side = partial(ordered, core, joined=jnp.concatenate)
    split_first = lambda x: x.reshape(16, 2, 32, half)[:, :, :24].reshape(WIDTH, half)
    value_all = side(split_first(first), split_first(first_far), 1)
    gain_rows = first.reshape(16, 2, 32, half)[:, :, 24]
    gain_one = gain_rows[..., :24].reshape(1, WIDTH).astype(F32)
    gain_two = gain_rows[..., 24:48].reshape(1, WIDTH).astype(F32)
    out_all = side(second[:, 0].reshape(WIDTH, half), second_far[:, 0].reshape(WIDTH, half), 1)
    up_part = lambda x: x[:, 1:].transpose(1, 0, 2, 3).reshape(4, WIDTH, half)
    up_all = side(up_part(second), up_part(second_far), 0)
    down_all = side(third.reshape(FF, half), third_far.reshape(FF, half), 1)

    v_own = run_values(sc, tokens, gain_one, value_all)
    v_far = swap(v_own, TO_CORE)

    carry = None
    back = None
    rand_grads = []
    for part in range(PARTS):
        own, far, mean, inverse = run_mix(part, sc, rands[part], v_own, v_far)
        got = swap(far, TO_CORE)
        output, res_grad, g_own, g_far, d_down, d_up, d_out, d_gain_two = run_feed(
            part, sc, tokens, grad_out, own, got, out_all, gain_two, up_all, down_all, carry
        )
        carry = (output, res_grad, d_down, d_up, d_out, d_gain_two)
        g_got = swap(g_far, TO_CORE)
        *pieces, back_own, back_far = run_unmix(
            part, sc, rands[part], v_own, v_far, g_own, g_got, mean, inverse, back
        )
        back = (back_own, back_far)
        rand_grads.append(pieces)
    back_got = swap(back_far, TO_CORE)
    tokens_grad, d_value, d_gain_one = run_close(
        sc, tokens, res_grad.reshape(2, LMAX, WIDTH), back_own, back_got, gain_one, value_all
    )

    def over_cores(x):
        return add_low(pick(x, core), swap(pick(x, 1 - core), TO_CORE))

    down_sum = scatter_chips(over_cores(d_down).reshape(16, 192, half), place, (1, 2, 0))
    up_sum = scatter_chips(
        over_cores(d_up.reshape(2, 4, WIDTH, half)).reshape(4, 16, 48, half), place, (2, 1, 0), 1
    )
    gain_pair = jnp.concatenate([d_gain_one, d_gain_two]).reshape(2, 16, 1, 48).astype(BF16)
    gain_pair = jnp.pad(gain_pair, ((0, 0), (0, 0), (0, 15), (0, half - 48)))
    small = jnp.concatenate([d_out.reshape(2, 16, 48, half), d_value.reshape(2, 16, 48, half), gain_pair], 2)
    small_sum = scatter_chips(over_cores(small), place, (2, 1, 0))
    rand_sums = [scatter_rand(*pieces) for pieces in rand_grads]

    weights = jnp.concatenate([small_sum, up_sum.reshape(192, half), down_sum])
    weights_far = swap(weights, TO_CORE)
    rows_of = lambda x, rows: pick(x.reshape(x.shape[0] // (2 * rows), 2, rows, half), core, 1)
    mine = lambda start, rows: side(
        rows_of(weights[start : start + 2 * rows], rows)[0], rows_of(weights_far[start : start + 2 * rows], rows)[0], 1
    )
    outproj_shard = mine(0, 24)
    value_shard = mine(48, 24)
    down_shard = mine(304, 96)
    up_side = lambda x: rows_of(x[112:304], 24).transpose(1, 0, 2).reshape(24, 4 * half)
    up_shard = side(up_side(weights), up_side(weights_far), 1)
    gains_pair = ordered(core, weights[96, :48], weights_far[96, :48])
    gain_pair = pick(gains_pair.reshape(2, 2, 24), core, 1)

    blocks = jnp.stack(rand_sums, 1).reshape(6, HALF, LMAX)
    blocks = blocks.reshape(2, 3, HALF, LMAX)
    rand_shard = ordered(core, pick(blocks, core), swap(pick(blocks, 1 - core), TO_CORE), 1)

    return (
        output.reshape(2, LMAX, WIDTH),
        tokens_grad,
        rand_shard.reshape(3 * 128, LMAX),
        value_shard,
        outproj_shard,
        up_shard,
        down_shard,
        gain_pair[0],
        gain_pair[1],
    )


def rms_norm(values, gain):
    scale = lax.rsqrt(jnp.mean(values * values, axis=-1, keepdims=True) + EPSILON)
    return values * scale * gain


def split_heads(block):
    return block.reshape(LMAX, HEADS, HEAD).transpose(1, 0, 2)


def merge_heads(block):
    return block.transpose(1, 0, 2).reshape(LMAX, HEADS * HEAD)


def masked_scores(key_mask, rand_head):
    return jnp.where(key_mask[None, :] > 0, rand_head.astype(jnp.float32), -1e30)


def head_forward(key_mask, paired):
    rand_head, value_head = paired
    scores = masked_scores(key_mask, rand_head)
    row_peak = jnp.max(scores, axis=-1, keepdims=True)
    exponent = jnp.exp(scores - row_peak)
    denom_sum = jnp.sum(exponent, axis=-1, keepdims=True)
    attention = exponent / denom_sum * key_mask[:, None]
    mixed = jnp.dot(attention.astype(jnp.bfloat16), value_head, preferred_element_type=jnp.float32)
    return (mixed.astype(jnp.bfloat16), row_peak + jnp.log(denom_sum))


def head_backward(key_mask, paired):
    rand_head, value_head, mix_grad, log_total = paired
    scores = masked_scores(key_mask, rand_head)
    attention = jnp.exp(scores - log_total) * key_mask[:, None]
    prob_grad = jnp.einsum("id,jd->ij", mix_grad, value_head, preferred_element_type=jnp.float32)
    value_grad = jnp.einsum(
        "ij,id->jd", attention.astype(jnp.bfloat16), mix_grad, preferred_element_type=jnp.float32
    )
    score_grad = attention * (prob_grad - jnp.sum(prob_grad * attention, axis=-1, keepdims=True))
    return (score_grad, value_grad)


def shards(tokens, lengths, rand_mix, w_value, w_out, w_up, w_down, gain_mix, gain_ffn, grad_out):
    item_count = tokens.shape[0]
    width = tokens.shape[2]
    row_count = item_count * LMAX
    tokens_flat = tokens.reshape(row_count, width).astype(jnp.float32)
    positions = jnp.arange(LMAX, dtype=jnp.int32)
    valid_table = (positions[None, :] < lengths[:, None]).astype(jnp.float32)
    row_valid = valid_table.reshape(row_count, 1)
    forward_set = (
        lax.all_gather(rand_mix, ("wide", "narrow"), axis=0, tiled=True),
        lax.all_gather(w_value, ("wide", "narrow"), axis=0, tiled=True),
        lax.all_gather(w_out, ("wide", "narrow"), axis=0, tiled=True),
        lax.all_gather(w_up, ("wide", "narrow"), axis=0, tiled=True),
        lax.all_gather(w_down, ("wide", "narrow"), axis=0, tiled=True),
        lax.all_gather(gain_mix, ("wide", "narrow"), axis=0, tiled=True),
        lax.all_gather(gain_ffn, ("wide", "narrow"), axis=0, tiled=True),
    )
    rand_all, value_all, out_all, up_all, down_all, gain_first, gain_second = forward_set
    normed = rms_norm(tokens_flat, gain_first.astype(jnp.float32)).astype(jnp.bfloat16)
    values = jnp.dot(normed, value_all, preferred_element_type=jnp.float32).astype(jnp.bfloat16)
    rand_heads = rand_all.reshape(HEADS, LMAX, LMAX)
    mixed_parts = []
    totals_kept = []
    for item_index in range(item_count):
        item_values = split_heads(values[item_index * LMAX : (item_index + 1) * LMAX])
        mixed_heads, log_total = lax.map(
            partial(head_forward, valid_table[item_index]), (rand_heads, item_values)
        )
        mixed_parts.append(merge_heads(mixed_heads))
        totals_kept.append(log_total)
    mixed = jnp.concatenate(mixed_parts, axis=0)
    residual = tokens_flat + jnp.dot(mixed, out_all, preferred_element_type=jnp.float32)
    normed_two = rms_norm(residual, gain_second.astype(jnp.float32)).astype(jnp.bfloat16)
    up_proj = jnp.dot(normed_two, up_all, preferred_element_type=jnp.float32)
    active = jax.nn.gelu(up_proj).astype(jnp.bfloat16)
    branch = jnp.dot(active, down_all, preferred_element_type=jnp.float32)
    output = row_valid * (residual + branch)
    back_set = (
        lax.all_gather(rand_mix, ("wide", "narrow"), axis=0, tiled=True),
        lax.all_gather(w_value, ("wide", "narrow"), axis=0, tiled=True),
        lax.all_gather(w_out, ("wide", "narrow"), axis=0, tiled=True),
        lax.all_gather(w_up, ("wide", "narrow"), axis=0, tiled=True),
        lax.all_gather(w_down, ("wide", "narrow"), axis=0, tiled=True),
        lax.all_gather(gain_mix, ("wide", "narrow"), axis=0, tiled=True),
        lax.all_gather(gain_ffn, ("wide", "narrow"), axis=0, tiled=True),
    )
    rand_back, value_back, out_back, up_back, down_back, gain_back_one, gain_back_two = back_set
    cotangent = grad_out.reshape(row_count, width).astype(jnp.float32)
    masked = row_valid * cotangent
    branch_grad = masked.astype(jnp.bfloat16)
    grad_down = jnp.einsum("rk,rd->kd", active, branch_grad, preferred_element_type=jnp.float32)
    active_grad = jnp.einsum(
        "rd,kd->rk", branch_grad, down_back, preferred_element_type=jnp.float32
    )
    gelu_value, gelu_pull = jax.vjp(jax.nn.gelu, up_proj)
    up_grad = gelu_pull(active_grad)[0].astype(jnp.bfloat16)
    grad_up = jnp.einsum("rd,rk->dk", normed_two, up_grad, preferred_element_type=jnp.float32)
    normed_two_grad = jnp.einsum("rk,dk->rd", up_grad, up_back, preferred_element_type=jnp.float32)
    norm_value, norm_pull = jax.vjp(rms_norm, residual, gain_back_two.astype(jnp.float32))
    residual_part, gain_two_grad = norm_pull(normed_two_grad)
    residual_grad = masked + residual_part
    attn_grad = residual_grad.astype(jnp.bfloat16)
    grad_outproj = jnp.einsum("rd,re->de", mixed, attn_grad, preferred_element_type=jnp.float32)
    mixed_grad = jnp.einsum(
        "re,de->rd", attn_grad, out_back, preferred_element_type=jnp.float32
    ).astype(jnp.bfloat16)
    rand_heads_back = rand_back.reshape(HEADS, LMAX, LMAX)
    rand_grad = jnp.zeros((HEADS, LMAX, LMAX), jnp.float32)
    value_parts = []
    for item_index in range(item_count):
        lower_row = item_index * LMAX
        upper_row = lower_row + LMAX
        item_values = split_heads(values[lower_row:upper_row])
        item_mix_grad = split_heads(mixed_grad[lower_row:upper_row])
        score_grad, value_grad = lax.map(
            partial(head_backward, valid_table[item_index]),
            (rand_heads_back, item_values, item_mix_grad, totals_kept[item_index]),
        )
        rand_grad = rand_grad + score_grad
        value_parts.append(merge_heads(value_grad))
    values_grad = jnp.concatenate(value_parts, axis=0).astype(jnp.bfloat16)
    grad_value = jnp.einsum("rd,re->de", normed, values_grad, preferred_element_type=jnp.float32)
    normed_grad = jnp.einsum(
        "re,de->rd", values_grad, value_back, preferred_element_type=jnp.float32
    )
    norm_first, first_pull = jax.vjp(rms_norm, tokens_flat, gain_back_one.astype(jnp.float32))
    token_part, gain_one_grad = first_pull(normed_grad)
    tokens_grad = residual_grad + token_part
    rand_flat = rand_grad.reshape(HEADS * LMAX, LMAX)
    all_shards = (
        lax.psum_scatter(rand_flat, ("wide", "narrow"), scatter_dimension=0, tiled=True),
        lax.psum_scatter(grad_value, ("wide", "narrow"), scatter_dimension=0, tiled=True),
        lax.psum_scatter(grad_outproj, ("wide", "narrow"), scatter_dimension=0, tiled=True),
        lax.psum_scatter(grad_up, ("wide", "narrow"), scatter_dimension=0, tiled=True),
        lax.psum_scatter(grad_down, ("wide", "narrow"), scatter_dimension=0, tiled=True),
        lax.psum_scatter(gain_one_grad, ("wide", "narrow"), scatter_dimension=0, tiled=True),
        lax.psum_scatter(gain_two_grad, ("wide", "narrow"), scatter_dimension=0, tiled=True),
    )
    rand_shard, value_shard, outproj_shard, up_shard, down_shard, gain_one_shard, gain_two_shard = (
        all_shards
    )
    return (
        output.reshape(item_count, LMAX, width),
        tokens_grad.reshape(item_count, LMAX, width),
        rand_shard,
        value_shard,
        outproj_shard,
        up_shard,
        down_shard,
        gain_one_shard,
        gain_two_shard,
    )


def solution(mesh):
    in_specs = (
        P(("wide", "narrow"), None, None),
        P(("wide", "narrow")),
        P(("wide", "narrow"), None),
        P(("wide", "narrow"), None),
        P(("wide", "narrow"), None),
        P(("wide", "narrow"), None),
        P(("wide", "narrow"), None),
        P(("wide", "narrow")),
        P(("wide", "narrow")),
        P(("wide", "narrow"), None, None),
    )
    out_specs = (
        P(("wide", "narrow"), None, None),
        P(("wide", "narrow"), None, None),
        P(("wide", "narrow"), None),
        P(("wide", "narrow"), None),
        P(("wide", "narrow"), None),
        P(("wide", "narrow"), None),
        P(("wide", "narrow"), None),
        P(("wide", "narrow")),
        P(("wide", "narrow")),
    )
    fits = dict(mesh.shape) == {"wide": 16, "narrow": 2}
    return jax.shard_map(chip_shards if fits else shards, mesh=mesh, in_specs=in_specs, out_specs=out_specs, check_vma=False)
```

```python
from functools import partial

import jax
import jax.numpy as jnp
from jax import lax
from jax.experimental import pallas as pl
from jax.experimental.pallas import tpu as pltpu
from jax.sharding import PartitionSpec as P

HEADS = 12
HEAD = 64
LMAX = 1024
WIDTH = 768
FF = 3072
EPSILON = 1e-05

BOTH = ("wide", "narrow")
BF16 = jnp.bfloat16
F32 = jnp.float32
MIB = 1 << 20

SUBS = 6
RUNS = 8
HALF = 64
HROWS = RUNS * HALF
PLANES = 4
PHEADS = HEADS // PLANES
ROWS = 2 * LMAX
FSTEP = 512
FSIDE = FF // 2 // FSTEP
TILE = 512
SIDE = WIDTH // 2


def dot(a, b, ca, cb):
    return lax.dot_general(a, b, (((ca,), (cb,)), ((), ())), preferred_element_type=F32)


CORE, PLANE, PLACE, LENGTHS = 0, 1, 2, 3


def spec(shape, index):
    return pl.BlockSpec(shape, index)


def held(shape):
    zeros = (0,) * len(shape)
    return pl.BlockSpec(shape, lambda *_: zeros, pipeline_mode=pl.Buffered(1))


def params(limit):
    return pltpu.CompilerParams(vmem_limit_bytes=limit * MIB)


def whole_weight(sc, step, own, far, weight):
    @pl.when(step == 0)
    def _():
        weight[:, pl.ds(pl.multiple_of(sc[CORE] * SIDE, 128), SIDE)] = own[...]
        weight[:, pl.ds(pl.multiple_of((1 - sc[CORE]) * SIDE, 128), SIDE)] = far[...]


def values_kernel(sc, tok, gain, w_own, w_far, out, weight):
    step = pl.program_id(0)
    whole_weight(sc, step, w_own, w_far, weight)
    rows = tok.shape[1]
    position = step * rows + lax.broadcasted_iota(jnp.int32, (rows, 1), 0)
    for item in range(2):
        x = tok[item].astype(F32)
        scale = lax.rsqrt(jnp.mean(x * x, axis=-1, keepdims=True) + EPSILON)
        normed = (x * scale * gain[...]).astype(BF16)
        found = dot(normed, weight[...], 1, 0)
        found = jnp.where(position < sc[LENGTHS + item], found, 0.0).astype(BF16)
        for head in range(HEADS):
            out[head, :, item * HEAD : (item + 1) * HEAD] = found[:, head * HEAD : (head + 1) * HEAD]


def run_values(sc, tokens, gain, w_own, w_far):
    rows = 256
    return pl.pallas_call(
        values_kernel,
        grid_spec=pltpu.PrefetchScalarGridSpec(
            num_scalar_prefetch=1,
            grid=(LMAX // rows,),
            in_specs=[
                spec((2, rows, WIDTH), lambda j, s: (0, j, 0)),
                held((1, WIDTH)),
                held((WIDTH, SIDE)),
                held((WIDTH, SIDE)),
            ],
            out_specs=spec((HEADS, rows, 2 * HEAD), lambda j, s: (0, j, 0)),
            scratch_shapes=[pltpu.VMEM((WIDTH, WIDTH), BF16)],
        ),
        out_shape=jax.ShapeDtypeStruct((HEADS, LMAX, 2 * HEAD), BF16),
        compiler_params=params(32),
        cost_estimate=pl.CostEstimate(
            flops=2 * 2 * LMAX * WIDTH * WIDTH, bytes_accessed=8 * LMAX * WIDTH, transcendentals=0
        ),
        name="values",
    )(sc, tokens, gain, w_own, w_far)


def lane_lengths(sc, shape):
    slot = lax.broadcasted_iota(jnp.int32, shape, 1) // HEAD
    length = jnp.where(slot == 0, sc[LENGTHS], sc[LENGTHS + 1])
    return jnp.where(slot >= 2, jnp.where(slot == 2, sc[LENGTHS + 2], sc[LENGTHS + 3]), length)


def plane_of(k, sc):
    return lax.rem(sc[PLANE] + PLANES - k, PLANES)


def plane_spec(planes, rows, lanes):
    def index(step, sc):
        k = planes[0] + step * (planes[1] - planes[0])
        return (plane_of(k, sc), 0, 0)

    return spec((PHEADS, rows, lanes), index)


def in_hbm(count):
    return [pl.BlockSpec(memory_space=pltpu.HBM)] * count


def plane_fetch(place, shards, raw, sems, slot):
    return [
        pltpu.make_async_copy(
            shards[4 * slot + rel].at[pl.ds(0, SUBS * HALF)],
            raw.at[slot, pl.ds(pl.multiple_of((place ^ rel) * SUBS * HALF, SUBS * HALF), SUBS * HALF)],
            sems.at[slot, rel],
        )
        for rel in range(4)
    ]


def take_plane(place, shards, raw, sems):
    step = pl.program_id(0)

    @pl.when(step == 0)
    def _():
        for slot in range(2):
            for copy in plane_fetch(place, shards, raw, sems, slot):
                copy.start()

    for slot in range(2):

        @pl.when(step == slot)
        def _():
            for copy in plane_fetch(place, shards, raw, sems, slot):
                copy.wait()

    return step


def exponents(raw, slot, head):
    return jnp.exp(raw[slot, head * HROWS : (head + 1) * HROWS].astype(F32)).astype(BF16)


def mix_kernel(carried, sc, *refs):
    shards, (v_own, v_far, *rest) = refs[:8], refs[8:]
    mixed, mean, inverse, raw, mask, sems = rest[3:] if carried else rest

    @pl.when(pl.program_id(0) == 0)
    def _():
        shape = (LMAX, 4 * HEAD)
        column = lax.broadcasted_iota(jnp.int32, shape, 0)
        mask[...] = (column < lane_lengths(sc, shape)).astype(F32).astype(BF16)

    slot = take_plane(sc[PLACE], shards, raw, sems)
    shape = (HROWS, 4 * HEAD)
    line = lax.broadcasted_iota(jnp.int32, shape, 0)
    position = 128 * (line // HALF) + HALF * sc[CORE] + line % HALF
    valid = position < lane_lengths(sc, shape)
    for head in range(PHEADS):
        weights = exponents(raw, slot, head)
        total = dot(weights, mask[...], 1, 0)
        flip = jnp.where(valid, 1.0 / total, 0.0)
        found = dot(weights, jnp.concatenate([v_own[head], v_far[head]], axis=1), 1, 0) * flip
        inverse[head] = flip
        mean[head] = found
        mixed[head] = found.astype(BF16)


def run_mix(sc, planes, shards, v_own, v_far, carry):
    out_shape = [
        jax.ShapeDtypeStruct((HEADS, HROWS, 4 * HEAD), BF16),
        jax.ShapeDtypeStruct((HEADS, HROWS, 4 * HEAD), F32),
        jax.ShapeDtypeStruct((HEADS, HROWS, 4 * HEAD), F32),
    ]
    carry = list(carry)
    return pl.pallas_call(
        partial(mix_kernel, bool(carry)),
        grid_spec=pltpu.PrefetchScalarGridSpec(
            num_scalar_prefetch=1,
            grid=(2,),
            in_specs=in_hbm(8) + [plane_spec(planes, LMAX, 2 * HEAD)] * 2 + in_hbm(len(carry)),
            out_specs=[plane_spec(planes, HROWS, 4 * HEAD)] * 3,
            scratch_shapes=[
                pltpu.VMEM((2, 4 * SUBS * HALF, LMAX), BF16),
                pltpu.VMEM((LMAX, 4 * HEAD), BF16),
                pltpu.SemaphoreType.DMA((2, 4)),
            ],
        ),
        out_shape=out_shape,
        input_output_aliases={11 + i: i for i in range(len(carry))},
        compiler_params=params(48),
        cost_estimate=pl.CostEstimate(
            flops=2 * HEADS * HROWS * LMAX * 4 * HEAD,
            bytes_accessed=HEADS * (HROWS * LMAX + 5 * HROWS * 256),
            transcendentals=HEADS * HROWS * LMAX // 2,
        ),
        name="mix",
    )(sc, *shards, v_own, v_far, *carry)


def row_valid(sc, step):
    line = lax.broadcasted_iota(jnp.int32, (256, 1), 0)
    item = line // HALF
    low = jnp.where(item == 0, sc[LENGTHS], sc[LENGTHS + 1])
    high = jnp.where(item == 2, sc[LENGTHS + 2], sc[LENGTHS + 3])
    return 128 * step + HALF * sc[CORE] + line % HALF < jnp.where(item >= 2, high, low)


def four_items(own, far):
    return jnp.concatenate([own[:, 0, 0], far[:, 0]], axis=0).reshape(256, WIDTH)


def pre_kernel(sc, tok, tok_far, cot, cot_far, heads, wo_own, wo_far, gain, mixed, resid, normed, grad, weight):
    step = pl.program_id(0)
    whole_weight(sc, step, wo_own, wo_far, weight)
    for item in range(4):
        lanes = slice(item * HEAD, (item + 1) * HEAD)
        for pair in range(HEADS // 2):
            both = jnp.concatenate([heads[2 * pair, :, lanes], heads[2 * pair + 1, :, lanes]], axis=1)
            mixed[item, :, pair * 128 : (pair + 1) * 128] = both
    res = four_items(tok, tok_far).astype(F32) + dot(mixed[...].reshape(256, WIDTH), weight[...], 1, 0)
    resid[...] = res.reshape(4, HALF, WIDTH)
    scale = lax.rsqrt(jnp.mean(res * res, axis=-1, keepdims=True) + EPSILON)
    valid = row_valid(sc, step)
    normed[...] = jnp.where(valid, res * scale * gain[...], 0.0).astype(BF16).reshape(4, HALF, WIDTH)
    masked = jnp.where(valid, four_items(cot, cot_far).astype(F32), 0.0)
    grad[...] = masked.astype(BF16).reshape(4, HALF, WIDTH)


def slab_spec(items=4):
    return spec((items, HALF, WIDTH), lambda r, s: (0, r, 0))


def half_specs():
    return [
        spec((2, 1, 1, HALF, WIDTH), lambda r, s: (0, r, s[CORE], 0, 0)),
        spec((2, 1, HALF, WIDTH), lambda r, s: (0, r, 0, 0)),
    ]


def heads_spec():
    return spec((HEADS, HALF, 4 * HEAD), lambda r, s: (0, r, 0))


def run_pre(sc, tokens, tokens_far, cotangent, cotangent_far, heads, wo, gain):
    return pl.pallas_call(
        pre_kernel,
        grid_spec=pltpu.PrefetchScalarGridSpec(
            num_scalar_prefetch=1,
            grid=(RUNS,),
            in_specs=half_specs()
            + half_specs()
            + [heads_spec(), held((WIDTH, SIDE)), held((WIDTH, SIDE)), held((1, WIDTH))],
            out_specs=[slab_spec()] * 4,
            scratch_shapes=[pltpu.VMEM((WIDTH, WIDTH), BF16)],
        ),
        out_shape=[
            jax.ShapeDtypeStruct((4, HROWS, WIDTH), BF16),
            jax.ShapeDtypeStruct((4, HROWS, WIDTH), F32),
            jax.ShapeDtypeStruct((4, HROWS, WIDTH), BF16),
            jax.ShapeDtypeStruct((4, HROWS, WIDTH), BF16),
        ],
        compiler_params=params(32),
        cost_estimate=pl.CostEstimate(
            flops=2 * ROWS * WIDTH * WIDTH, bytes_accessed=16 * ROWS * WIDTH, transcendentals=0
        ),
        name="pre",
    )(sc, tokens, tokens_far, cotangent, cotangent_far, heads, *wo, gain)


def feed_kernel(sc, normed, cot, up_own, up_far, dn_own, dn_far, *refs):
    (branch, back, d_down_own, d_down_far, d_up_own, d_up_far, w_down, active, up_grad) = refs
    step = pl.program_id(0)
    core = sc[CORE]
    own_lanes = pl.ds(pl.multiple_of(core * SIDE, 128), SIDE)
    far_lanes = pl.ds(pl.multiple_of((1 - core) * SIDE, 128), SIDE)
    w_down[:, own_lanes] = dn_own[...]
    w_down[:, far_lanes] = dn_far[...]

    def units(up_w, d_up):
        for piece in range(ROWS // TILE):
            rows = slice(piece * TILE, (piece + 1) * TILE)
            up = dot(normed[rows], up_w[...], 1, 0)
            square = up * up
            bend = jnp.tanh(up * (0.7978845608028654 + (0.044715 * 0.7978845608028654) * square))
            share = 0.5 + 0.5 * bend
            act = (up * share).astype(BF16)
            active[rows] = act
            slope = share + (0.5 * up) * (1.0 - bend * bend) * (
                0.7978845608028654 + (3 * 0.044715 * 0.7978845608028654) * square
            )
            low = (dot(cot[rows], w_down[...], 1, 1) * slope).astype(BF16)
            up_grad[rows] = low
            out = dot(act, w_down[...], 1, 0)
            two_grad = dot(low, up_w[...], 1, 1)

            @pl.when(step == 0)
            def _():
                branch[rows] = out
                back[rows] = two_grad

            @pl.when(step > 0)
            def _():
                branch[rows] += out
                back[rows] += two_grad

        d_up[...] = dot(normed[...], up_grad[...], 0, 0).astype(BF16)

    @pl.when(step < FSIDE)
    def _():
        units(up_own, d_up_own)

    @pl.when(step >= FSIDE)
    def _():
        units(up_far, d_up_far)

    w_down[...] = dot(active[...], cot[...], 0, 0).astype(BF16)
    d_down_own[...] = w_down[:, own_lanes]
    d_down_far[...] = w_down[:, far_lanes]


def run_feed(sc, normed, cotangent, up, down):
    units = lambda f, s: (lax.rem(FSIDE * s[CORE] + f, 2 * FSIDE), 0)
    early = lambda f, s: (0, lax.min(f, FSIDE - 1))
    late = lambda f, s: (0, lax.max(f - FSIDE, 0))
    return pl.pallas_call(
        feed_kernel,
        grid_spec=pltpu.PrefetchScalarGridSpec(
            num_scalar_prefetch=1,
            grid=(FF // FSTEP,),
            in_specs=[
                held((ROWS, WIDTH)),
                held((ROWS, WIDTH)),
                spec((WIDTH, FSTEP), early),
                spec((WIDTH, FSTEP), late),
                spec((FSTEP, SIDE), units),
                spec((FSTEP, SIDE), units),
            ],
            out_specs=[
                held((ROWS, WIDTH)),
                held((ROWS, WIDTH)),
                spec((FSTEP, SIDE), units),
                spec((FSTEP, SIDE), units),
                spec((WIDTH, FSTEP), early),
                spec((WIDTH, FSTEP), late),
            ],
            scratch_shapes=[
                pltpu.VMEM((FSTEP, WIDTH), BF16),
                pltpu.VMEM((ROWS, FSTEP), BF16),
                pltpu.VMEM((ROWS, FSTEP), BF16),
            ],
        ),
        out_shape=[
            jax.ShapeDtypeStruct((ROWS, WIDTH), F32),
            jax.ShapeDtypeStruct((ROWS, WIDTH), F32),
            jax.ShapeDtypeStruct((FF, SIDE), BF16),
            jax.ShapeDtypeStruct((FF, SIDE), BF16),
            jax.ShapeDtypeStruct((WIDTH, FF // 2), BF16),
            jax.ShapeDtypeStruct((WIDTH, FF // 2), BF16),
        ],
        compiler_params=params(56),
        cost_estimate=pl.CostEstimate(
            flops=12 * ROWS * WIDTH * FF, bytes_accessed=12 * ROWS * WIDTH + 8 * WIDTH * FF, transcendentals=ROWS * FF
        ),
        name="feed",
    )(sc, normed.reshape(ROWS, WIDTH), cotangent.reshape(ROWS, WIDTH), *up, *down)


def post_kernel(sc, resid, branch, back, cot, mixed, wo_own, wo_far, gain, *refs):
    (out_own, out_far, res_own, res_far, heads, d_out_own, d_out_far, d_gain, weight, total, spread) = refs
    step = pl.program_id(0)
    whole_weight(sc, step, wo_own, wo_far, weight)
    core = sc[CORE]
    shape, slab = (256, WIDTH), (4, HALF, WIDTH)
    valid = row_valid(sc, step)
    res = resid[...].reshape(shape)
    output = jnp.where(valid, res + branch[...].reshape(shape), 0.0).reshape(slab)
    out_own[...] = output[:2]
    out_far[...] = output[2:].astype(BF16)
    scale = lax.rsqrt(jnp.mean(res * res, axis=-1, keepdims=True) + EPSILON)
    unit = res * scale
    two_grad = jnp.where(valid, back[...].reshape(shape), 0.0)
    gained = two_grad * gain[...]
    masked = cot[...].reshape(shape).astype(F32)
    grad = masked + scale * (gained - unit * jnp.mean(gained * unit, axis=-1, keepdims=True))
    low = grad.astype(BF16)
    res_own[...] = grad.reshape(slab)[:2]
    res_far[...] = low.reshape(slab)[2:]
    gain_sum = jnp.sum(two_grad * unit, axis=0, keepdims=True)
    out_sum = dot(mixed[...].reshape(shape), low, 0, 0)

    @pl.when(step == 0)
    def _():
        d_gain[...] = gain_sum
        total[...] = out_sum

    @pl.when(step > 0)
    def _():
        d_gain[...] += gain_sum
        total[...] += out_sum

    spread[...] = dot(low, weight[...], 1, 1).astype(BF16).reshape(slab)
    for pair in range(HEADS // 2):
        lanes = slice(pair * 128, (pair + 1) * 128)
        for side in range(2):
            one, two = spread[2 * side, :, lanes], spread[2 * side + 1, :, lanes]
            half = slice(side * 128, (side + 1) * 128)
            heads[2 * pair, :, half] = jnp.concatenate([one[:, :HEAD], two[:, :HEAD]], axis=1)
            heads[2 * pair + 1, :, half] = jnp.concatenate([one[:, HEAD:], two[:, HEAD:]], axis=1)

    @pl.when(step == pl.num_programs(0) - 1)
    def _():
        weight[...] = total[...].astype(BF16)
        d_out_own[...] = weight[:, pl.ds(pl.multiple_of(core * SIDE, 128), SIDE)]
        d_out_far[...] = weight[:, pl.ds(pl.multiple_of((1 - core) * SIDE, 128), SIDE)]


def run_post(sc, resid, branch, back, cotangent, mixed, wo, gain):
    whole = (4, HROWS, WIDTH)
    return pl.pallas_call(
        post_kernel,
        grid_spec=pltpu.PrefetchScalarGridSpec(
            num_scalar_prefetch=1,
            grid=(RUNS,),
            in_specs=[slab_spec()] * 5 + [held((WIDTH, SIDE)), held((WIDTH, SIDE)), held((1, WIDTH))],
            out_specs=[slab_spec(2)] * 4
            + [heads_spec(), held((WIDTH, SIDE)), held((WIDTH, SIDE)), held((1, WIDTH))],
            scratch_shapes=[
                pltpu.VMEM((WIDTH, WIDTH), BF16),
                pltpu.VMEM((WIDTH, WIDTH), F32),
                pltpu.VMEM((4, HALF, WIDTH), BF16),
            ],
        ),
        out_shape=[
            jax.ShapeDtypeStruct((2, HROWS, WIDTH), F32),
            jax.ShapeDtypeStruct((2, HROWS, WIDTH), BF16),
            jax.ShapeDtypeStruct((2, HROWS, WIDTH), F32),
            jax.ShapeDtypeStruct((2, HROWS, WIDTH), BF16),
            jax.ShapeDtypeStruct((HEADS, HROWS, 4 * HEAD), BF16),
            jax.ShapeDtypeStruct((WIDTH, SIDE), BF16),
            jax.ShapeDtypeStruct((WIDTH, SIDE), BF16),
            jax.ShapeDtypeStruct((1, WIDTH), F32),
        ],
        compiler_params=params(40),
        cost_estimate=pl.CostEstimate(
            flops=4 * ROWS * WIDTH * WIDTH, bytes_accessed=28 * ROWS * WIDTH, transcendentals=0
        ),
        name="post",
    )(sc, resid, branch.reshape(whole), back.reshape(whole), cotangent, mixed, *wo, gain)


def unmix_kernel(carried, sc, *refs):
    shards, (v_own, v_far, grad_heads, mean, inverse, *rest) = refs[:8], refs[8:]
    rest = rest[2:] if carried else rest
    outs, (own, far, raw, grads, sems, out_sems) = rest[:8], rest[8:]
    place = sc[PLACE]
    step = pl.program_id(0)

    def leave(slot):
        return [
            pltpu.make_async_copy(
                grads.at[slot, pl.ds(pl.multiple_of((place ^ rel) * SUBS * HALF, SUBS * HALF), SUBS * HALF)],
                outs[4 * slot + rel],
                out_sems.at[slot, rel],
            )
            for rel in range(4)
        ]

    slot = take_plane(place, shards, raw, sems)
    column = lax.broadcasted_iota(jnp.int32, (1, LMAX), 1)
    line = lax.broadcasted_iota(jnp.int32, (LMAX, 2 * HEAD), 0)
    side = lax.broadcasted_iota(jnp.int32, (LMAX, 2 * HEAD), 1) // HEAD
    for head in range(PHEADS):
        weights = exponents(raw, slot, head)
        low = (grad_heads[head].astype(F32) * inverse[head]).astype(BF16)
        product = low.astype(F32) * mean[head]
        score = dot(low, jnp.concatenate([v_own[head], v_far[head]], axis=1), 1, 1)
        for item in range(4):
            delta = jnp.sum(product[:, item * HEAD : (item + 1) * HEAD], axis=-1, keepdims=True)
            score = score - delta * (column < sc[LENGTHS + item]).astype(F32)
        score = score * weights.astype(F32)
        grads[slot, head * HROWS : (head + 1) * HROWS] = score.astype(BF16)
        back = dot(weights, low, 0, 0)
        for target, first in ((own, 0), (far, 2)):
            found = back[:, first * HEAD : (first + 2) * HEAD]
            length = jnp.where(side == 0, sc[LENGTHS + first], sc[LENGTHS + first + 1])
            target[head] = jnp.where(line < length, found, 0.0).astype(target.dtype)
    for which in range(2):

        @pl.when(step == which)
        def _():
            for copy in leave(which):
                copy.start()
            if which == 1:
                for copy in leave(0) + leave(1):
                    copy.wait()


def run_unmix(sc, planes, shards, v_own, v_far, grad_heads, mean, inverse, carry):
    carry = list(carry)
    return pl.pallas_call(
        partial(unmix_kernel, bool(carry)),
        grid_spec=pltpu.PrefetchScalarGridSpec(
            num_scalar_prefetch=1,
            grid=(2,),
            in_specs=in_hbm(8)
            + [plane_spec(planes, LMAX, 2 * HEAD)] * 2
            + [plane_spec(planes, HROWS, 4 * HEAD)] * 3
            + in_hbm(len(carry)),
            out_specs=in_hbm(8) + [plane_spec(planes, LMAX, 2 * HEAD)] * 2,
            scratch_shapes=[
                pltpu.VMEM((2, 4 * SUBS * HALF, LMAX), BF16),
                pltpu.VMEM((2, 4 * SUBS * HALF, LMAX), BF16),
                pltpu.SemaphoreType.DMA((2, 4)),
                pltpu.SemaphoreType.DMA((2, 4)),
            ],
        ),
        out_shape=[jax.ShapeDtypeStruct((SUBS * HALF, LMAX), BF16)] * 8
        + [
            jax.ShapeDtypeStruct((HEADS, LMAX, 2 * HEAD), F32),
            jax.ShapeDtypeStruct((HEADS, LMAX, 2 * HEAD), BF16),
        ],
        input_output_aliases={14 + i: 8 + i for i in range(len(carry))},
        compiler_params=params(56),
        cost_estimate=pl.CostEstimate(
            flops=2 * HEADS * HROWS * LMAX * 4 * HEAD,
            bytes_accessed=HEADS * (2 * HROWS * LMAX + 5 * HROWS * 256 + 4 * LMAX * 256),
            transcendentals=HEADS * HROWS * LMAX // 2,
        ),
        name="unmix",
    )(sc, *shards, v_own, v_far, grad_heads, mean, inverse, *carry)


def close_kernel(sc, tok, res_own, res_got, out_own, out_got, own, far, gain, w_own, w_far, *refs):
    (output, tok_grad, d_value, d_gain, total, weight) = refs
    step = pl.program_id(0)
    whole_weight(sc, step, w_own, w_far, weight)
    core = sc[CORE]
    output[:, :, core] = out_own[...]
    output[:, :, 1 - core] = out_got[...].astype(F32)
    tok_grad[:, :, core] = res_own[...]
    tok_grad[:, :, 1 - core] = res_got[...].astype(F32)
    runs = tok.shape[1]
    rows = runs * 128
    for item in range(2):
        lanes = slice(item * HEAD, (item + 1) * HEAD)
        pieces = [
            (own[head, :, lanes] + far[head, :, lanes].astype(F32)).astype(BF16) for head in range(HEADS)
        ]
        back = jnp.concatenate(pieces, axis=1)
        x = tok[item].reshape(rows, WIDTH).astype(F32)
        scale = lax.rsqrt(jnp.mean(x * x, axis=-1, keepdims=True) + EPSILON)
        unit = x * scale
        normed = (unit * gain[...]).astype(BF16)
        normed_grad = dot(back, weight[...], 1, 1)
        gained = normed_grad * gain[...]
        update = scale * (gained - unit * jnp.mean(gained * unit, axis=-1, keepdims=True))
        tok_grad[item] += update.reshape(runs, 2, HALF, WIDTH)
        gain_sum = jnp.sum(normed_grad * unit, axis=0, keepdims=True)
        value_sum = dot(normed, back, 0, 0)
        if item == 0:
            gain_total, value_total = gain_sum, value_sum
        else:
            gain_total, value_total = gain_total + gain_sum, value_total + value_sum

    @pl.when(step == 0)
    def _():
        d_gain[...] = gain_total
        total[...] = value_total

    @pl.when(step > 0)
    def _():
        d_gain[...] += gain_total
        total[...] += value_total

    @pl.when(step == pl.num_programs(0) - 1)
    def _():
        low = total[...].astype(BF16)
        d_value[0] = low[:, :SIDE]
        d_value[1] = low[:, SIDE:]


def run_close(sc, tokens, res_own, res_got, out_own, out_got, own, far, gain, w_own, w_far):
    runs = 2
    slab = (2, RUNS, 2, HALF, WIDTH)
    half = (2, RUNS, HALF, WIDTH)
    whole_spec = spec((2, runs, 2, HALF, WIDTH), lambda j, s: (0, j, 0, 0, 0))
    half_spec = spec((2, runs, HALF, WIDTH), lambda j, s: (0, j, 0, 0))
    back_spec = spec((HEADS, runs * 128, 2 * HEAD), lambda j, s: (0, j, 0))
    return pl.pallas_call(
        close_kernel,
        grid_spec=pltpu.PrefetchScalarGridSpec(
            num_scalar_prefetch=1,
            grid=(RUNS // runs,),
            in_specs=[whole_spec]
            + [half_spec] * 4
            + [back_spec, back_spec, held((1, WIDTH)), held((WIDTH, SIDE)), held((WIDTH, SIDE))],
            out_specs=[whole_spec, whole_spec, held((2, WIDTH, SIDE)), held((1, WIDTH))],
            scratch_shapes=[pltpu.VMEM((WIDTH, WIDTH), F32), pltpu.VMEM((WIDTH, WIDTH), BF16)],
        ),
        out_shape=[
            jax.ShapeDtypeStruct(slab, F32),
            jax.ShapeDtypeStruct(slab, F32),
            jax.ShapeDtypeStruct((2, WIDTH, SIDE), BF16),
            jax.ShapeDtypeStruct((1, WIDTH), F32),
        ],
        compiler_params=params(48),
        cost_estimate=pl.CostEstimate(
            flops=4 * 2 * LMAX * WIDTH * WIDTH, bytes_accessed=38 * LMAX * WIDTH, transcendentals=0
        ),
        name="close",
    )(
        sc,
        tokens.reshape(slab),
        *(x.reshape(half) for x in (res_own, res_got, out_own, out_got)),
        own,
        far,
        gain,
        w_own,
        w_far,
    )


PACK_DOWN, PACK_UP, PACK_OUT, PACK = 0, 192, 384, 432
SHARE = SUBS * HALF + 32


def chip_of(sc, k, rel):
    return plane_of(k, sc) * 4 + (sc[PLACE] ^ rel)


def place_kernel(moves, sc, *refs):
    pieces, targets, sems = refs[:16], refs[16:-1], refs[-1]
    copies = []
    for index, piece in enumerate(pieces):
        chip = chip_of(sc, index // 4, index % 4)
        for which, (start, count, lane, target, step, offset, column) in enumerate(moves):
            rows = pl.ds(pl.multiple_of(chip * step + offset, 16), count)
            copies.append(
                pltpu.make_async_copy(
                    piece.at[pl.ds(start, count), pl.ds(lane, SIDE)],
                    targets[target].at[rows, pl.ds(column, SIDE)],
                    sems.at[index, which],
                )
            )
    for copy in copies:
        copy.start()
    for copy in copies:
        copy.wait()


def run_place(sc, pieces, moves, shapes):
    return pl.pallas_call(
        partial(place_kernel, moves),
        grid_spec=pltpu.PrefetchScalarGridSpec(
            num_scalar_prefetch=1,
            grid=(1,),
            in_specs=in_hbm(16),
            out_specs=in_hbm(len(shapes)),
            scratch_shapes=[pltpu.SemaphoreType.DMA((16, len(moves)))],
        ),
        out_shape=[jax.ShapeDtypeStruct(shape, BF16) for shape in shapes],
        compiler_params=params(16),
        cost_estimate=pl.CostEstimate(
            flops=0, bytes_accessed=4 * sum(a * b for a, b in shapes), transcendentals=0
        ),
        name="place",
    )(sc, *pieces)


def place_values(sc, shares):
    start = SUBS * HALF
    moves = (
        (start, 32, 0, 0, 48, 0, 0),
        (start, 16, SIDE, 0, 48, 32, 0),
        (start + 16, 16, SIDE, 1, 16, 0, 0),
    )
    return run_place(sc, shares, moves, [(WIDTH, SIDE), (256, SIDE)])


def place_weights(sc, pieces):
    moves = (
        (PACK_DOWN, 192, 0, 0, 192, 0, 0),
        *((PACK_UP + 48 * j, 48, 0, 1, 48, 0, j * SIDE) for j in range(4)),
        (PACK_OUT, 48, 0, 2, 48, 0, 0),
    )
    return run_place(sc, pieces, moves, [(FF, SIDE), (WIDTH, FF // 2), (WIDTH, SIDE)])


def collect_kernel(sc, down, down_got, up, up_got, out, out_got, packed):
    both = lambda a, b: (a.astype(F32) + b.astype(F32)).astype(BF16)
    packed[0, 0:192] = both(down[...], down_got[...])
    for j in range(4):
        lanes = slice(j * SIDE, (j + 1) * SIDE)
        packed[0, 192 + 48 * j : 240 + 48 * j] = both(up[:, lanes], up_got[:, lanes])
    packed[0, 384:432] = both(out[...], out_got[...])


def run_collect(sc, down, down_got, up, up_got, out, out_got):
    chip = lambda i, s: (chip_of(s, i // 4, i % 4), 0)
    rows = lambda x: spec((x.shape[0] // 16, x.shape[1]), chip)
    args = (down, down_got, up, up_got, out, out_got)
    return pl.pallas_call(
        collect_kernel,
        grid_spec=pltpu.PrefetchScalarGridSpec(
            num_scalar_prefetch=1,
            grid=(16,),
            in_specs=[rows(x) for x in args],
            out_specs=spec((1, PACK, SIDE), lambda i, s: (i, 0, 0)),
        ),
        out_shape=jax.ShapeDtypeStruct((16, PACK, SIDE), BF16),
        compiler_params=params(16),
        cost_estimate=pl.CostEstimate(flops=0, bytes_accessed=3 * 16 * PACK * SIDE * 2, transcendentals=0),
        name="collect",
    )(sc, *args)


DEVICES = 32
TO_CORE, TO_X, TO_Y = 1, 2, 4


def swap(x, bit):
    return lax.ppermute(x, BOTH, [(d, d ^ bit) for d in range(DEVICES)])


def ring(x, way=1):
    return lax.ppermute(x, BOTH, [(d, (d + 8 * way) % DEVICES) for d in range(DEVICES)])


def pick(x, index, axis=0):
    return lax.dynamic_index_in_dim(x, index, axis, keepdims=False)


def ordered(flag, one, two, axis=0, joined=jnp.stack):
    return jnp.where(flag == 0, joined([one, two], axis), joined([two, one], axis))


def add_low(one, two):
    return (one.astype(F32) + two.astype(F32)).astype(BF16)


STEPS = (
    ((0, 0, 1), (0, 1, 0), (1, 0, 0)),
    ((1, 0, 1), (0, 1, 1), (2, 0, 0)),
    ((2, 0, 1), (1, 1, 0), (3, 0, 0)),
    ((3, 0, 1), (2, 1, 0), (1, 1, 1)),
    ((2, 1, 1), (3, 1, 1), (3, 1, 0)),
)


def gather16(own, works=(), made=()):
    have = {(0, 0, 0): own}
    for step, (by_x, by_y, by_z) in enumerate(STEPS):
        got = {
            by_z: ring(have[by_z[0] - 1, by_z[1], by_z[2]]),
            by_x: swap(have[by_x[0], by_x[1], 0], TO_X),
            by_y: swap(have[by_y[0], 0, by_y[2]], TO_Y),
        }
        if step < len(works):
            made = works[step](made)
        have, made = lax.optimization_barrier(({**have, **got}, made))
    return [have[k, y, x] for k in range(4) for y in range(2) for x in range(2)], made


def scatter16(shares, works=(), made=()):
    have = {(k, y, x): shares[4 * k + 2 * y + x] for k in range(4) for y in range(2) for x in range(2)}
    for step, (by_x, by_y, by_z) in enumerate(reversed(STEPS)):
        got = [
            ((by_z[0] - 1, by_z[1], by_z[2]), ring(have[by_z], -1)),
            ((by_x[0], by_x[1], 0), swap(have[by_x], TO_X)),
            ((by_y[0], 0, by_y[2]), swap(have[by_y], TO_Y)),
        ]
        for at in (by_x, by_y, by_z):
            del have[at]
        if step < len(works):
            made = works[step](made)
        values, have, made = lax.optimization_barrier(([value for _, value in got], have, made))
        for at in dict.fromkeys(at for at, _ in got):
            total = have[at].astype(F32)
            for (target, _), value in zip(got, values):
                if target == at:
                    total = total + value.astype(F32)
            have[at] = total if step == len(STEPS) - 1 else total.astype(BF16)
    return have[0, 0, 0], made


def after(x, *others):
    return lax.optimization_barrier((x, others))[0]


def chip_shards(tokens, lengths, rand_mix, w_value, w_out, w_up, w_down, gain_mix, gain_ffn, grad_out):
    wide = lax.axis_index("wide")
    core = lax.axis_index("narrow")
    z, y, x = wide // 4, (wide // 2) % 2, wide % 2
    other = lambda value: swap(value, TO_CORE)
    side = partial(ordered, core, joined=jnp.concatenate)

    gains = jnp.pad(jnp.concatenate([gain_mix, gain_ffn])[None], ((0, 7), (0, SIDE - 48)))
    halves = [
        jnp.concatenate(
            [
                w_value[:, c * SIDE : (c + 1) * SIDE],
                gains,
                w_down[:, c * SIDE : (c + 1) * SIDE],
                *[w_up[:, (4 * c + j) * SIDE : (4 * c + j + 1) * SIDE] for j in range(4)],
                w_out[:, c * SIDE : (c + 1) * SIDE],
            ]
        )
        for c in range(2)
    ]
    both = jnp.stack(halves)
    joined = ordered(core, pick(both, core), other(pick(both, 1 - core)))
    part_of = lambda start, rows: joined[:, start : start + rows].reshape(2 * rows, SIDE)
    up_rows = joined[:, 128:224].reshape(2, 4, 24, SIDE).transpose(1, 0, 2, 3).reshape(192, SIDE)
    packed = jnp.concatenate([part_of(32, 96), up_rows, part_of(224, 24)])
    first = jnp.concatenate([part_of(0, 24), part_of(24, 8)])
    first = jnp.pad(jnp.concatenate([first[:32], first[32:]], axis=1), ((0, 0), (0, LMAX - WIDTH)))
    rand = rand_mix.reshape(3, 2, HALF, LMAX)
    blocks = side(pick(rand, core, 1), other(pick(rand, 1 - core, 1)), 0)
    share = jnp.concatenate([blocks.reshape(SUBS * HALF, LMAX), first])
    share, packed = lax.optimization_barrier((share, packed))

    slab = (2, RUNS, 2, HALF, WIDTH)
    tokens, grad_out = tokens.reshape(slab), grad_out.reshape(slab)

    def from_other(_):
        return other(lengths), other(pick(tokens, 1 - core, 2)), other(pick(grad_out, 1 - core, 2))

    shares, (far_lengths, tokens_far, grad_far) = gather16(share, [from_other])
    sc = jnp.concatenate([jnp.stack([core, z, wide % 4]).astype(jnp.int32), lengths, far_lengths])

    def make_values(_):
        value, gain_rows = place_values(sc, shares)
        value_far = other(value)
        gain_rows = gain_rows.reshape(16, 2, 8, SIDE)[:, :, 0]
        gain_one = gain_rows[..., :24].reshape(1, WIDTH).astype(F32)
        gain_two = gain_rows[..., 24:48].reshape(1, WIDTH).astype(F32)
        v_own = run_values(sc, tokens.reshape(2, LMAX, WIDTH), gain_one, value, value_far)
        return value, value_far, gain_one, gain_two, v_own

    def share_values(made):
        return *made, other(made[-1])

    def mix_near(made):
        return *made, run_mix(sc, (0, 1), shares[:8], made[-2], made[-1], ())

    def mix_far(made):
        *made, near = made
        return *made, run_mix(sc, (2, 3), shares[8:], made[-2], made[-1], near)

    pieces, made = gather16(after(packed, *shares[-3:]), [make_values, share_values, mix_near, mix_far])
    value, value_far, gain_one, gain_two, v_own, v_far, (heads, mean, inverse) = made
    down, up, out = place_weights(sc, pieces)
    down_far, up_far, out_far = other(down), other(up), other(out)

    mixed, resid, normed, masked = run_pre(
        sc, tokens, tokens_far, grad_out, grad_far, heads, (out, out_far), gain_two
    )
    branch, back, down_own, down_far, up_own, up_far = run_feed(sc, normed, masked, (up, up_far), (down, down_far))
    down_got, up_got = other(down_far), other(up_far)
    out_own, out_far, res_own, res_far, grad_heads, d_out_own, d_out_far, d_gain_two = run_post(
        sc, resid, branch, back, masked, mixed, (out, out_far), gain_two
    )

    packed = run_collect(sc, down_own, down_got, up_own, up_got, d_out_own, other(d_out_far))

    def unmix_far(_):
        return run_unmix(sc, (3, 2), shares[12:] + shares[8:12], v_own, v_far, grad_heads, mean, inverse, ())

    def unmix_near(made):
        *far, back_own, back_far = made
        near = run_unmix(
            sc, (1, 0), shares[4:8] + shares[:4], v_own, v_far, grad_heads, mean, inverse, (back_own, back_far)
        )
        return far, near

    def exchange(made):
        far, (*near, back_own, back_far) = made
        return far, near, back_own, other(back_far), other(out_far), other(res_far)

    big_sum, made = scatter16([packed[i] for i in range(16)], [unmix_far, unmix_near, exchange])
    far, near, back_own, back_got, out_got, res_got = made
    rand_grads = near[4:] + near[:4] + far[4:] + far[:4]

    def finish(_):
        output, tokens_grad, d_value, d_gain_one = run_close(
            sc, tokens, res_own, res_got, out_own, out_got, back_own, back_got, gain_one, value, value_far
        )
        gain_pair = jnp.concatenate([d_gain_one, d_gain_two]).reshape(2, 16, 1, 48).astype(BF16)
        gain_pair = jnp.pad(gain_pair, ((0, 0), (0, 0), (0, 15), (0, SIDE - 48)))
        small = jnp.concatenate([d_value.reshape(2, 16, 48, SIDE), gain_pair], 2)
        return output, tokens_grad, small, other(big_sum)

    def small_core(made):
        *kept, small, big_far = made
        small = add_low(pick(small, core), other(pick(small, 1 - core))).reshape(4, 2, 2, 64, SIDE)
        return *kept, big_far, small

    def small_line(made):
        *kept, small = made
        return *kept, add_low(pick(small, x, 2), swap(pick(small, 1 - x, 2), TO_X))

    def small_plane(made):
        *kept, small = made
        return *kept, add_low(pick(small, y, 1), swap(pick(small, 1 - y, 1), TO_Y))

    def small_planes(made):
        *kept, small = made
        total = pick(small, z).astype(F32)
        for k in range(1, PLANES):
            total = total + ring(pick(small, lax.rem(z + PLANES - k, PLANES)), -k).astype(F32)
        return *kept, total

    rand_sum, made = scatter16(
        after(rand_grads, big_sum), [finish, small_core, small_line, small_plane, small_planes]
    )
    output, tokens_grad, big_far, small_sum = made
    small_far = other(small_sum)

    rows_of = lambda value, rows: pick(value.reshape(-1, 2, rows, SIDE), core, 1)
    mine = lambda own, far, rows: side(rows_of(own, rows)[0], rows_of(far, rows)[0], 1)
    down_shard = mine(big_sum[PACK_DOWN:PACK_UP], big_far[PACK_DOWN:PACK_UP], 96)
    up_side = lambda value: rows_of(value[PACK_UP:PACK_OUT], 24).transpose(1, 0, 2).reshape(24, 4 * SIDE)
    up_shard = side(up_side(big_sum), up_side(big_far), 1)
    outproj_shard = mine(big_sum[PACK_OUT:], big_far[PACK_OUT:], 24)
    value_shard = mine(small_sum[:48], small_far[:48], 24)
    gains_pair = ordered(core, small_sum[48, :48], small_far[48, :48])
    gain_pair = pick(gains_pair.reshape(2, 2, 24), core, 1)

    blocks = rand_sum.reshape(2, 3, HALF, LMAX)
    rand_shard = ordered(core, pick(blocks, core), other(pick(blocks, 1 - core)), 1)

    return (
        output.reshape(2, LMAX, WIDTH),
        tokens_grad.reshape(2, LMAX, WIDTH),
        rand_shard.reshape(3 * 128, LMAX),
        value_shard,
        outproj_shard,
        up_shard,
        down_shard,
        gain_pair[0],
        gain_pair[1],
    )


def rms_norm(values, gain):
    scale = lax.rsqrt(jnp.mean(values * values, axis=-1, keepdims=True) + EPSILON)
    return values * scale * gain


def split_heads(block):
    return block.reshape(LMAX, HEADS, HEAD).transpose(1, 0, 2)


def merge_heads(block):
    return block.transpose(1, 0, 2).reshape(LMAX, HEADS * HEAD)


def masked_scores(key_mask, rand_head):
    return jnp.where(key_mask[None, :] > 0, rand_head.astype(jnp.float32), -1e30)


def head_forward(key_mask, paired):
    rand_head, value_head = paired
    scores = masked_scores(key_mask, rand_head)
    row_peak = jnp.max(scores, axis=-1, keepdims=True)
    exponent = jnp.exp(scores - row_peak)
    denom_sum = jnp.sum(exponent, axis=-1, keepdims=True)
    attention = exponent / denom_sum * key_mask[:, None]
    mixed = jnp.dot(attention.astype(jnp.bfloat16), value_head, preferred_element_type=jnp.float32)
    return (mixed.astype(jnp.bfloat16), row_peak + jnp.log(denom_sum))


def head_backward(key_mask, paired):
    rand_head, value_head, mix_grad, log_total = paired
    scores = masked_scores(key_mask, rand_head)
    attention = jnp.exp(scores - log_total) * key_mask[:, None]
    prob_grad = jnp.einsum("id,jd->ij", mix_grad, value_head, preferred_element_type=jnp.float32)
    value_grad = jnp.einsum(
        "ij,id->jd", attention.astype(jnp.bfloat16), mix_grad, preferred_element_type=jnp.float32
    )
    score_grad = attention * (prob_grad - jnp.sum(prob_grad * attention, axis=-1, keepdims=True))
    return (score_grad, value_grad)


def shards(tokens, lengths, rand_mix, w_value, w_out, w_up, w_down, gain_mix, gain_ffn, grad_out):
    item_count = tokens.shape[0]
    width = tokens.shape[2]
    row_count = item_count * LMAX
    tokens_flat = tokens.reshape(row_count, width).astype(jnp.float32)
    positions = jnp.arange(LMAX, dtype=jnp.int32)
    valid_table = (positions[None, :] < lengths[:, None]).astype(jnp.float32)
    row_valid = valid_table.reshape(row_count, 1)
    forward_set = (
        lax.all_gather(rand_mix, ("wide", "narrow"), axis=0, tiled=True),
        lax.all_gather(w_value, ("wide", "narrow"), axis=0, tiled=True),
        lax.all_gather(w_out, ("wide", "narrow"), axis=0, tiled=True),
        lax.all_gather(w_up, ("wide", "narrow"), axis=0, tiled=True),
        lax.all_gather(w_down, ("wide", "narrow"), axis=0, tiled=True),
        lax.all_gather(gain_mix, ("wide", "narrow"), axis=0, tiled=True),
        lax.all_gather(gain_ffn, ("wide", "narrow"), axis=0, tiled=True),
    )
    rand_all, value_all, out_all, up_all, down_all, gain_first, gain_second = forward_set
    normed = rms_norm(tokens_flat, gain_first.astype(jnp.float32)).astype(jnp.bfloat16)
    values = jnp.dot(normed, value_all, preferred_element_type=jnp.float32).astype(jnp.bfloat16)
    rand_heads = rand_all.reshape(HEADS, LMAX, LMAX)
    mixed_parts = []
    totals_kept = []
    for item_index in range(item_count):
        item_values = split_heads(values[item_index * LMAX : (item_index + 1) * LMAX])
        mixed_heads, log_total = lax.map(
            partial(head_forward, valid_table[item_index]), (rand_heads, item_values)
        )
        mixed_parts.append(merge_heads(mixed_heads))
        totals_kept.append(log_total)
    mixed = jnp.concatenate(mixed_parts, axis=0)
    residual = tokens_flat + jnp.dot(mixed, out_all, preferred_element_type=jnp.float32)
    normed_two = rms_norm(residual, gain_second.astype(jnp.float32)).astype(jnp.bfloat16)
    up_proj = jnp.dot(normed_two, up_all, preferred_element_type=jnp.float32)
    active = jax.nn.gelu(up_proj).astype(jnp.bfloat16)
    branch = jnp.dot(active, down_all, preferred_element_type=jnp.float32)
    output = row_valid * (residual + branch)
    back_set = (
        lax.all_gather(rand_mix, ("wide", "narrow"), axis=0, tiled=True),
        lax.all_gather(w_value, ("wide", "narrow"), axis=0, tiled=True),
        lax.all_gather(w_out, ("wide", "narrow"), axis=0, tiled=True),
        lax.all_gather(w_up, ("wide", "narrow"), axis=0, tiled=True),
        lax.all_gather(w_down, ("wide", "narrow"), axis=0, tiled=True),
        lax.all_gather(gain_mix, ("wide", "narrow"), axis=0, tiled=True),
        lax.all_gather(gain_ffn, ("wide", "narrow"), axis=0, tiled=True),
    )
    rand_back, value_back, out_back, up_back, down_back, gain_back_one, gain_back_two = back_set
    cotangent = grad_out.reshape(row_count, width).astype(jnp.float32)
    masked = row_valid * cotangent
    branch_grad = masked.astype(jnp.bfloat16)
    grad_down = jnp.einsum("rk,rd->kd", active, branch_grad, preferred_element_type=jnp.float32)
    active_grad = jnp.einsum(
        "rd,kd->rk", branch_grad, down_back, preferred_element_type=jnp.float32
    )
    gelu_value, gelu_pull = jax.vjp(jax.nn.gelu, up_proj)
    up_grad = gelu_pull(active_grad)[0].astype(jnp.bfloat16)
    grad_up = jnp.einsum("rd,rk->dk", normed_two, up_grad, preferred_element_type=jnp.float32)
    normed_two_grad = jnp.einsum("rk,dk->rd", up_grad, up_back, preferred_element_type=jnp.float32)
    norm_value, norm_pull = jax.vjp(rms_norm, residual, gain_back_two.astype(jnp.float32))
    residual_part, gain_two_grad = norm_pull(normed_two_grad)
    residual_grad = masked + residual_part
    attn_grad = residual_grad.astype(jnp.bfloat16)
    grad_outproj = jnp.einsum("rd,re->de", mixed, attn_grad, preferred_element_type=jnp.float32)
    mixed_grad = jnp.einsum(
        "re,de->rd", attn_grad, out_back, preferred_element_type=jnp.float32
    ).astype(jnp.bfloat16)
    rand_heads_back = rand_back.reshape(HEADS, LMAX, LMAX)
    rand_grad = jnp.zeros((HEADS, LMAX, LMAX), jnp.float32)
    value_parts = []
    for item_index in range(item_count):
        lower_row = item_index * LMAX
        upper_row = lower_row + LMAX
        item_values = split_heads(values[lower_row:upper_row])
        item_mix_grad = split_heads(mixed_grad[lower_row:upper_row])
        score_grad, value_grad = lax.map(
            partial(head_backward, valid_table[item_index]),
            (rand_heads_back, item_values, item_mix_grad, totals_kept[item_index]),
        )
        rand_grad = rand_grad + score_grad
        value_parts.append(merge_heads(value_grad))
    values_grad = jnp.concatenate(value_parts, axis=0).astype(jnp.bfloat16)
    grad_value = jnp.einsum("rd,re->de", normed, values_grad, preferred_element_type=jnp.float32)
    normed_grad = jnp.einsum(
        "re,de->rd", values_grad, value_back, preferred_element_type=jnp.float32
    )
    norm_first, first_pull = jax.vjp(rms_norm, tokens_flat, gain_back_one.astype(jnp.float32))
    token_part, gain_one_grad = first_pull(normed_grad)
    tokens_grad = residual_grad + token_part
    rand_flat = rand_grad.reshape(HEADS * LMAX, LMAX)
    all_shards = (
        lax.psum_scatter(rand_flat, ("wide", "narrow"), scatter_dimension=0, tiled=True),
        lax.psum_scatter(grad_value, ("wide", "narrow"), scatter_dimension=0, tiled=True),
        lax.psum_scatter(grad_outproj, ("wide", "narrow"), scatter_dimension=0, tiled=True),
        lax.psum_scatter(grad_up, ("wide", "narrow"), scatter_dimension=0, tiled=True),
        lax.psum_scatter(grad_down, ("wide", "narrow"), scatter_dimension=0, tiled=True),
        lax.psum_scatter(gain_one_grad, ("wide", "narrow"), scatter_dimension=0, tiled=True),
        lax.psum_scatter(gain_two_grad, ("wide", "narrow"), scatter_dimension=0, tiled=True),
    )
    rand_shard, value_shard, outproj_shard, up_shard, down_shard, gain_one_shard, gain_two_shard = (
        all_shards
    )
    return (
        output.reshape(item_count, LMAX, width),
        tokens_grad.reshape(item_count, LMAX, width),
        rand_shard,
        value_shard,
        outproj_shard,
        up_shard,
        down_shard,
        gain_one_shard,
        gain_two_shard,
    )


def solution(mesh):
    in_specs = (
        P(("wide", "narrow"), None, None),
        P(("wide", "narrow")),
        P(("wide", "narrow"), None),
        P(("wide", "narrow"), None),
        P(("wide", "narrow"), None),
        P(("wide", "narrow"), None),
        P(("wide", "narrow"), None),
        P(("wide", "narrow")),
        P(("wide", "narrow")),
        P(("wide", "narrow"), None, None),
    )
    out_specs = (
        P(("wide", "narrow"), None, None),
        P(("wide", "narrow"), None, None),
        P(("wide", "narrow"), None),
        P(("wide", "narrow"), None),
        P(("wide", "narrow"), None),
        P(("wide", "narrow"), None),
        P(("wide", "narrow"), None),
        P(("wide", "narrow")),
        P(("wide", "narrow")),
    )
    fits = dict(mesh.shape) == {"wide": 16, "narrow": 2}
    return jax.shard_map(chip_shards if fits else shards, mesh=mesh, in_specs=in_specs, out_specs=out_specs, check_vma=False)
```

```python
from functools import partial

import jax
import jax.numpy as jnp
from jax import lax
from jax.experimental import pallas as pl
from jax.experimental.pallas import tpu as pltpu
from jax.sharding import PartitionSpec as P

HEADS = 12
HEAD = 64
LMAX = 1024
WIDTH = 768
FF = 3072
EPSILON = 1e-05

BOTH = ("wide", "narrow")
BF16 = jnp.bfloat16
F32 = jnp.float32
MIB = 1 << 20

SUBS = 6
RUNS = 8
HALF = 64
HROWS = RUNS * HALF
PLANES = 4
PHEADS = HEADS // PLANES
ROWS = 2 * LMAX
FSTEP = 768
FSIDE = FF // 2 // FSTEP
TILE = 512
SIDE = WIDTH // 2


def dot(a, b, ca, cb):
    return lax.dot_general(a, b, (((ca,), (cb,)), ((), ())), preferred_element_type=F32)


CORE, PLANE, PLACE, LENGTHS = 0, 1, 2, 3


def spec(shape, index):
    return pl.BlockSpec(shape, index)


def held(shape):
    zeros = (0,) * len(shape)
    return pl.BlockSpec(shape, lambda *_: zeros, pipeline_mode=pl.Buffered(1))


def params(limit):
    return pltpu.CompilerParams(vmem_limit_bytes=limit * MIB)


def whole_weight(sc, step, own, far, weight):
    @pl.when(step == 0)
    def _():
        weight[:, pl.ds(pl.multiple_of(sc[CORE] * SIDE, 128), SIDE)] = own[...]
        weight[:, pl.ds(pl.multiple_of((1 - sc[CORE]) * SIDE, 128), SIDE)] = far[...]


def values_kernel(sc, tok, gain, w_own, w_far, out, weight):
    step = pl.program_id(0)
    whole_weight(sc, step, w_own, w_far, weight)
    rows = tok.shape[1]
    position = step * rows + lax.broadcasted_iota(jnp.int32, (rows, 1), 0)
    for item in range(2):
        x = tok[item].astype(F32)
        scale = lax.rsqrt(jnp.mean(x * x, axis=-1, keepdims=True) + EPSILON)
        normed = (x * scale * gain[...]).astype(BF16)
        found = dot(normed, weight[...], 1, 0)
        found = jnp.where(position < sc[LENGTHS + item], found, 0.0).astype(BF16)
        for head in range(HEADS):
            out[head, :, item * HEAD : (item + 1) * HEAD] = found[:, head * HEAD : (head + 1) * HEAD]


def run_values(sc, tokens, gain, w_own, w_far):
    rows = 256
    return pl.pallas_call(
        values_kernel,
        grid_spec=pltpu.PrefetchScalarGridSpec(
            num_scalar_prefetch=1,
            grid=(LMAX // rows,),
            in_specs=[
                spec((2, rows, WIDTH), lambda j, s: (0, j, 0)),
                held((1, WIDTH)),
                held((WIDTH, SIDE)),
                held((WIDTH, SIDE)),
            ],
            out_specs=spec((HEADS, rows, 2 * HEAD), lambda j, s: (0, j, 0)),
            scratch_shapes=[pltpu.VMEM((WIDTH, WIDTH), BF16)],
        ),
        out_shape=jax.ShapeDtypeStruct((HEADS, LMAX, 2 * HEAD), BF16),
        compiler_params=params(32),
        cost_estimate=pl.CostEstimate(
            flops=2 * 2 * LMAX * WIDTH * WIDTH, bytes_accessed=8 * LMAX * WIDTH, transcendentals=0
        ),
        name="values",
    )(sc, tokens, gain, w_own, w_far)


def lane_lengths(sc, shape):
    slot = lax.broadcasted_iota(jnp.int32, shape, 1) // HEAD
    length = jnp.where(slot == 0, sc[LENGTHS], sc[LENGTHS + 1])
    return jnp.where(slot >= 2, jnp.where(slot == 2, sc[LENGTHS + 2], sc[LENGTHS + 3]), length)


def plane_of(k, sc):
    return lax.rem(sc[PLANE] + PLANES - k, PLANES)


def head_spec(planes, rows, lanes):
    def index(step, sc):
        k = planes[0] + step // PHEADS * (planes[1] - planes[0])
        return (plane_of(k, sc) * PHEADS + step % PHEADS, 0, 0)

    return spec((1, rows, lanes), index)


def anywhere(count):
    return [pl.BlockSpec(memory_space=pl.ANY)] * count


def plane_fetch(place, shards, raw, sems, slot):
    return [
        pltpu.make_async_copy(
            shards[4 * slot + rel].at[pl.ds(0, SUBS * HALF)],
            raw.at[slot, pl.ds(pl.multiple_of((place ^ rel) * SUBS * HALF, SUBS * HALF), SUBS * HALF)],
            sems.at[slot, rel],
        )
        for rel in range(4)
    ]


def take_plane(place, shards, raw, sems):
    step = pl.program_id(0)

    @pl.when(step == 0)
    def _():
        for slot in range(2):
            for copy in plane_fetch(place, shards, raw, sems, slot):
                copy.start()

    for slot in range(2):

        @pl.when(step == slot * PHEADS)
        def _():
            for copy in plane_fetch(place, shards, raw, sems, slot):
                copy.wait()

    return step // PHEADS, pl.ds(pl.multiple_of(step % PHEADS * HROWS, HROWS), HROWS)


def fill_mask(sc, mask):
    @pl.when(pl.program_id(0) == 0)
    def _():
        shape = (LMAX, 4 * HEAD)
        column = lax.broadcasted_iota(jnp.int32, shape, 0)
        mask[...] = (column < lane_lengths(sc, shape)).astype(F32).astype(BF16)


def inverse_sums(sc, weights, mask):
    shape = (HROWS, 4 * HEAD)
    line = lax.broadcasted_iota(jnp.int32, shape, 0)
    position = 128 * (line // HALF) + HALF * sc[CORE] + line % HALF
    return jnp.where(position < lane_lengths(sc, shape), 1.0 / dot(weights, mask[...], 1, 0), 0.0)


def mix_kernel(carried, sc, *refs):
    shards, (v_own, v_far, *rest) = refs[:8], refs[8:]
    mixed, mean, raw, mask, sems = rest[2:] if carried else rest
    fill_mask(sc, mask)
    slot, rows = take_plane(sc[PLACE], shards, raw, sems)
    weights = jnp.exp(raw[slot, rows].astype(F32)).astype(BF16)
    found = dot(weights, jnp.concatenate([v_own[0], v_far[0]], axis=1), 1, 0) * inverse_sums(sc, weights, mask)
    mean[0] = found
    mixed[0] = found.astype(BF16)


def run_mix(sc, planes, shards, v_own, v_far, carry):
    carry = list(carry)
    return pl.pallas_call(
        partial(mix_kernel, bool(carry)),
        grid_spec=pltpu.PrefetchScalarGridSpec(
            num_scalar_prefetch=1,
            grid=(2 * PHEADS,),
            in_specs=anywhere(8) + [head_spec(planes, LMAX, 2 * HEAD)] * 2 + anywhere(len(carry)),
            out_specs=[head_spec(planes, HROWS, 4 * HEAD)] * 2,
            scratch_shapes=[
                pltpu.VMEM((2, 4 * SUBS * HALF, LMAX), BF16),
                pltpu.VMEM((LMAX, 4 * HEAD), BF16),
                pltpu.SemaphoreType.DMA((2, 4)),
            ],
        ),
        out_shape=[
            jax.ShapeDtypeStruct((HEADS, HROWS, 4 * HEAD), BF16),
            jax.ShapeDtypeStruct((HEADS, HROWS, 4 * HEAD), F32),
        ],
        input_output_aliases={11 + i: i for i in range(len(carry))},
        compiler_params=params(60),
        cost_estimate=pl.CostEstimate(
            flops=2 * HEADS * HROWS * LMAX * 4 * HEAD,
            bytes_accessed=HEADS * (HROWS * LMAX + 5 * HROWS * 256),
            transcendentals=HEADS * HROWS * LMAX // 2,
        ),
        name="mix",
    )(sc, *shards, v_own, v_far, *carry)


def row_valid(sc, step):
    line = lax.broadcasted_iota(jnp.int32, (256, 1), 0)
    item = line // HALF
    low = jnp.where(item == 0, sc[LENGTHS], sc[LENGTHS + 1])
    high = jnp.where(item == 2, sc[LENGTHS + 2], sc[LENGTHS + 3])
    return 128 * step + HALF * sc[CORE] + line % HALF < jnp.where(item >= 2, high, low)


def four_items(own, far):
    return jnp.concatenate([own[:, 0, 0], far[:, 0]], axis=0).reshape(256, WIDTH)


def pre_kernel(sc, tok, tok_far, cot, cot_far, heads, wo_own, wo_far, gain, mixed, resid, normed, grad, weight):
    step = pl.program_id(0)
    whole_weight(sc, step, wo_own, wo_far, weight)
    for item in range(4):
        lanes = slice(item * HEAD, (item + 1) * HEAD)
        for pair in range(HEADS // 2):
            both = jnp.concatenate([heads[2 * pair, :, lanes], heads[2 * pair + 1, :, lanes]], axis=1)
            mixed[item, :, pair * 128 : (pair + 1) * 128] = both
    res = four_items(tok, tok_far).astype(F32) + dot(mixed[...].reshape(256, WIDTH), weight[...], 1, 0)
    resid[...] = res.reshape(4, HALF, WIDTH)
    scale = lax.rsqrt(jnp.mean(res * res, axis=-1, keepdims=True) + EPSILON)
    valid = row_valid(sc, step)
    normed[...] = jnp.where(valid, res * scale * gain[...], 0.0).astype(BF16).reshape(4, HALF, WIDTH)
    masked = jnp.where(valid, four_items(cot, cot_far).astype(F32), 0.0)
    grad[...] = masked.astype(BF16).reshape(4, HALF, WIDTH)


def slab_spec(items=4):
    return spec((items, HALF, WIDTH), lambda r, s: (0, r, 0))


def half_specs():
    return [
        spec((2, 1, 1, HALF, WIDTH), lambda r, s: (0, r, s[CORE], 0, 0)),
        spec((2, 1, HALF, WIDTH), lambda r, s: (0, r, 0, 0)),
    ]


def heads_spec():
    return spec((HEADS, HALF, 4 * HEAD), lambda r, s: (0, r, 0))


def run_pre(sc, tokens, tokens_far, cotangent, cotangent_far, heads, wo, gain):
    return pl.pallas_call(
        pre_kernel,
        grid_spec=pltpu.PrefetchScalarGridSpec(
            num_scalar_prefetch=1,
            grid=(RUNS,),
            in_specs=half_specs()
            + half_specs()
            + [heads_spec(), held((WIDTH, SIDE)), held((WIDTH, SIDE)), held((1, WIDTH))],
            out_specs=[slab_spec()] * 4,
            scratch_shapes=[pltpu.VMEM((WIDTH, WIDTH), BF16)],
        ),
        out_shape=[
            jax.ShapeDtypeStruct((4, HROWS, WIDTH), BF16),
            jax.ShapeDtypeStruct((4, HROWS, WIDTH), F32),
            jax.ShapeDtypeStruct((4, HROWS, WIDTH), BF16),
            jax.ShapeDtypeStruct((4, HROWS, WIDTH), BF16),
        ],
        compiler_params=params(32),
        cost_estimate=pl.CostEstimate(
            flops=2 * ROWS * WIDTH * WIDTH, bytes_accessed=16 * ROWS * WIDTH, transcendentals=0
        ),
        name="pre",
    )(sc, tokens, tokens_far, cotangent, cotangent_far, heads, *wo, gain)


def own_lanes(sc):
    return pl.ds(pl.multiple_of(sc[CORE] * SIDE, 128), SIDE)


def far_lanes(sc):
    return pl.ds(pl.multiple_of((1 - sc[CORE]) * SIDE, 128), SIDE)


def unit_rows(f, sc):
    return (lax.rem(FSIDE * sc[CORE] + f, 2 * FSIDE), 0)


def unit_columns(f, sc):
    return (0, lax.rem(FSIDE * sc[CORE] + f, 2 * FSIDE))


def early(f, sc):
    return (0, lax.min(f, FSIDE - 1))


def late(f, sc):
    return (0, lax.max(f - FSIDE, 0))


def units_kernel(sc, normed, cot, up_own, up_far, dn_own, dn_far, active, up_grad, back, w_down):
    step = pl.program_id(0)
    w_down[:, own_lanes(sc)] = dn_own[...]
    w_down[:, far_lanes(sc)] = dn_far[...]

    def units(up_w):
        for piece in range(ROWS // TILE):
            rows = slice(piece * TILE, (piece + 1) * TILE)
            up = dot(normed[rows], up_w[...], 1, 0)
            square = up * up
            bend = jnp.tanh(up * (0.7978845608028654 + (0.044715 * 0.7978845608028654) * square))
            share = 0.5 + 0.5 * bend
            act = up * share
            active[rows] = act.astype(BF16)
            slope = share + act * (1.0 - share) * (
                2 * 0.7978845608028654 + (6 * 0.044715 * 0.7978845608028654) * square
            )
            low = (dot(cot[rows], w_down[...], 1, 1) * slope).astype(BF16)
            up_grad[rows] = low
            two_grad = dot(low, up_w[...], 1, 1)

            @pl.when(step == 0)
            def _():
                back[rows] = two_grad

            @pl.when(step > 0)
            def _():
                back[rows] += two_grad

    @pl.when(step < FSIDE)
    def _():
        units(up_own)

    @pl.when(step >= FSIDE)
    def _():
        units(up_far)


def run_units(sc, normed, cotangent, up, down):
    return pl.pallas_call(
        units_kernel,
        grid_spec=pltpu.PrefetchScalarGridSpec(
            num_scalar_prefetch=1,
            grid=(2 * FSIDE,),
            in_specs=[
                held((ROWS, WIDTH)),
                held((ROWS, WIDTH)),
                spec((WIDTH, FSTEP), early),
                spec((WIDTH, FSTEP), late),
                spec((FSTEP, SIDE), unit_rows),
                spec((FSTEP, SIDE), unit_rows),
            ],
            out_specs=[spec((ROWS, FSTEP), unit_columns), spec((ROWS, FSTEP), unit_columns), held((ROWS, WIDTH))],
            scratch_shapes=[pltpu.VMEM((FSTEP, WIDTH), BF16)],
        ),
        out_shape=[
            jax.ShapeDtypeStruct((ROWS, FF), BF16),
            jax.ShapeDtypeStruct((ROWS, FF), BF16),
            jax.ShapeDtypeStruct((ROWS, WIDTH), F32),
        ],
        compiler_params=params(56),
        cost_estimate=pl.CostEstimate(
            flops=6 * ROWS * WIDTH * FF, bytes_accessed=8 * ROWS * WIDTH + 4 * ROWS * FF, transcendentals=ROWS * FF
        ),
        name="units",
    )(sc, normed.reshape(ROWS, WIDTH), cotangent.reshape(ROWS, WIDTH), *up, *down)


def down_grad_kernel(sc, active, cot, own, far, total):
    total[...] = dot(active[...], cot[...], 0, 0).astype(BF16)
    own[...] = total[:, own_lanes(sc)]
    far[...] = total[:, far_lanes(sc)]


def run_down_grad(sc, active, cotangent):
    return pl.pallas_call(
        down_grad_kernel,
        grid_spec=pltpu.PrefetchScalarGridSpec(
            num_scalar_prefetch=1,
            grid=(FF // 512,),
            in_specs=[spec((ROWS, 512), lambda f, s: (0, f)), held((ROWS, WIDTH))],
            out_specs=[spec((512, SIDE), lambda f, s: (f, 0))] * 2,
            scratch_shapes=[pltpu.VMEM((512, WIDTH), BF16)],
        ),
        out_shape=[jax.ShapeDtypeStruct((FF, SIDE), BF16)] * 2,
        compiler_params=params(48),
        cost_estimate=pl.CostEstimate(
            flops=2 * ROWS * WIDTH * FF, bytes_accessed=2 * ROWS * (WIDTH + FF), transcendentals=0
        ),
        name="down_grad",
    )(sc, active, cotangent.reshape(ROWS, WIDTH))


def up_grad_kernel(sc, normed, up_grad, own, far):
    total = dot(normed[...], up_grad[...], 0, 0).astype(BF16)

    @pl.when(pl.program_id(0) < FSIDE)
    def _():
        own[...] = total

    @pl.when(pl.program_id(0) >= FSIDE)
    def _():
        far[...] = total


def run_up_grad(sc, normed, up_grad):
    return pl.pallas_call(
        up_grad_kernel,
        grid_spec=pltpu.PrefetchScalarGridSpec(
            num_scalar_prefetch=1,
            grid=(2 * FSIDE,),
            in_specs=[held((ROWS, WIDTH)), spec((ROWS, FSTEP), unit_columns)],
            out_specs=[spec((WIDTH, FSTEP), early), spec((WIDTH, FSTEP), late)],
        ),
        out_shape=[jax.ShapeDtypeStruct((WIDTH, FF // 2), BF16)] * 2,
        compiler_params=params(48),
        cost_estimate=pl.CostEstimate(
            flops=2 * ROWS * WIDTH * FF, bytes_accessed=2 * ROWS * (WIDTH + FF), transcendentals=0
        ),
        name="up_grad",
    )(sc, normed.reshape(ROWS, WIDTH), up_grad)


def out_kernel(sc, active, resid, dn_own, dn_far, own, far, w_down):
    step = pl.program_id(0)

    @pl.when(step == 0)
    def _():
        w_down[:, own_lanes(sc)] = dn_own[...]
        w_down[:, far_lanes(sc)] = dn_far[...]

    branch = dot(active[...].reshape(256, FF), w_down[...], 1, 0)
    output = jnp.where(row_valid(sc, step), resid[...].reshape(256, WIDTH) + branch, 0.0)
    output = output.reshape(4, HALF, WIDTH)
    own[...] = output[:2]
    far[...] = output[2:].astype(BF16)


def run_out(sc, active, resid, down):
    return pl.pallas_call(
        out_kernel,
        grid_spec=pltpu.PrefetchScalarGridSpec(
            num_scalar_prefetch=1,
            grid=(RUNS,),
            in_specs=[
                spec((4, HALF, FF), lambda r, s: (0, r, 0)),
                slab_spec(),
                held((FF, SIDE)),
                held((FF, SIDE)),
            ],
            out_specs=[slab_spec(2)] * 2,
            scratch_shapes=[pltpu.VMEM((FF, WIDTH), BF16)],
        ),
        out_shape=[
            jax.ShapeDtypeStruct((2, HROWS, WIDTH), F32),
            jax.ShapeDtypeStruct((2, HROWS, WIDTH), BF16),
        ],
        compiler_params=params(48),
        cost_estimate=pl.CostEstimate(
            flops=2 * ROWS * WIDTH * FF, bytes_accessed=ROWS * (2 * FF + 7 * WIDTH), transcendentals=0
        ),
        name="out",
    )(sc, active.reshape(4, HROWS, FF), resid, *down)


def post_kernel(sc, resid, back, cot, mixed, wo_own, wo_far, gain, *refs):
    (res_own, res_far, heads, d_out_own, d_out_far, d_gain, weight, total, spread) = refs
    step = pl.program_id(0)
    whole_weight(sc, step, wo_own, wo_far, weight)
    shape, slab = (256, WIDTH), (4, HALF, WIDTH)
    valid = row_valid(sc, step)
    res = resid[...].reshape(shape)
    scale = lax.rsqrt(jnp.mean(res * res, axis=-1, keepdims=True) + EPSILON)
    unit = res * scale
    two_grad = jnp.where(valid, back[...].reshape(shape), 0.0)
    gained = two_grad * gain[...]
    masked = cot[...].reshape(shape).astype(F32)
    grad = masked + scale * (gained - unit * jnp.mean(gained * unit, axis=-1, keepdims=True))
    low = grad.astype(BF16)
    res_own[...] = grad.reshape(slab)[:2]
    res_far[...] = low.reshape(slab)[2:]
    gain_sum = jnp.sum(two_grad * unit, axis=0, keepdims=True)
    out_sum = dot(mixed[...].reshape(shape), low, 0, 0)

    @pl.when(step == 0)
    def _():
        d_gain[...] = gain_sum
        total[...] = out_sum

    @pl.when(step > 0)
    def _():
        d_gain[...] += gain_sum
        total[...] += out_sum

    spread[...] = dot(low, weight[...], 1, 1).astype(BF16).reshape(slab)
    for pair in range(HEADS // 2):
        lanes = slice(pair * 128, (pair + 1) * 128)
        for side in range(2):
            one, two = spread[2 * side, :, lanes], spread[2 * side + 1, :, lanes]
            half = slice(side * 128, (side + 1) * 128)
            heads[2 * pair, :, half] = jnp.concatenate([one[:, :HEAD], two[:, :HEAD]], axis=1)
            heads[2 * pair + 1, :, half] = jnp.concatenate([one[:, HEAD:], two[:, HEAD:]], axis=1)

    @pl.when(step == pl.num_programs(0) - 1)
    def _():
        weight[...] = total[...].astype(BF16)
        d_out_own[...] = weight[:, own_lanes(sc)]
        d_out_far[...] = weight[:, far_lanes(sc)]


def run_post(sc, resid, back, cotangent, mixed, wo, gain):
    whole = (4, HROWS, WIDTH)
    return pl.pallas_call(
        post_kernel,
        grid_spec=pltpu.PrefetchScalarGridSpec(
            num_scalar_prefetch=1,
            grid=(RUNS,),
            in_specs=[slab_spec()] * 4 + [held((WIDTH, SIDE)), held((WIDTH, SIDE)), held((1, WIDTH))],
            out_specs=[slab_spec(2)] * 2
            + [heads_spec(), held((WIDTH, SIDE)), held((WIDTH, SIDE)), held((1, WIDTH))],
            scratch_shapes=[
                pltpu.VMEM((WIDTH, WIDTH), BF16),
                pltpu.VMEM((WIDTH, WIDTH), F32),
                pltpu.VMEM((4, HALF, WIDTH), BF16),
            ],
        ),
        out_shape=[
            jax.ShapeDtypeStruct((2, HROWS, WIDTH), F32),
            jax.ShapeDtypeStruct((2, HROWS, WIDTH), BF16),
            jax.ShapeDtypeStruct((HEADS, HROWS, 4 * HEAD), BF16),
            jax.ShapeDtypeStruct((WIDTH, SIDE), BF16),
            jax.ShapeDtypeStruct((WIDTH, SIDE), BF16),
            jax.ShapeDtypeStruct((1, WIDTH), F32),
        ],
        compiler_params=params(40),
        cost_estimate=pl.CostEstimate(
            flops=4 * ROWS * WIDTH * WIDTH, bytes_accessed=28 * ROWS * WIDTH, transcendentals=0
        ),
        name="post",
    )(sc, resid, back.reshape(whole), cotangent, mixed, *wo, gain)


def unmix_kernel(carried, sc, *refs):
    shards, (v_own, v_far, grad_heads, mean, *rest) = refs[:8], refs[8:]
    rest = rest[2:] if carried else rest
    outs, (own, far, raw, grads, mask, sems, out_sems) = rest[:8], rest[8:]
    place = sc[PLACE]
    step = pl.program_id(0)

    def leave(slot):
        return [
            pltpu.make_async_copy(
                grads.at[slot, pl.ds(pl.multiple_of((place ^ rel) * SUBS * HALF, SUBS * HALF), SUBS * HALF)],
                outs[4 * slot + rel],
                out_sems.at[slot, rel],
            )
            for rel in range(4)
        ]

    fill_mask(sc, mask)
    slot, rows = take_plane(place, shards, raw, sems)
    weights = jnp.exp(raw[slot, rows].astype(F32)).astype(BF16)
    low = (grad_heads[0].astype(F32) * inverse_sums(sc, weights, mask)).astype(BF16)
    product = low.astype(F32) * mean[0]
    score = dot(low, jnp.concatenate([v_own[0], v_far[0]], axis=1), 1, 1)
    column = lax.broadcasted_iota(jnp.int32, (1, LMAX), 1)
    for item in range(4):
        delta = jnp.sum(product[:, item * HEAD : (item + 1) * HEAD], axis=-1, keepdims=True)
        score = score - delta * (column < sc[LENGTHS + item]).astype(F32)
    grads[slot, rows] = (score * weights.astype(F32)).astype(BF16)
    back = (dot(weights, low, 0, 0) * mask[...].astype(F32)).astype(BF16)
    own[0] = back[:, : 2 * HEAD]
    far[0] = back[:, 2 * HEAD :]
    for which in range(2):

        @pl.when(step == which * PHEADS + PHEADS - 1)
        def _():
            for copy in leave(which):
                copy.start()
            if which == 1:
                for copy in leave(0) + leave(1):
                    copy.wait()


def run_unmix(sc, planes, shards, v_own, v_far, grad_heads, mean, carry):
    carry = list(carry)
    return pl.pallas_call(
        partial(unmix_kernel, bool(carry)),
        grid_spec=pltpu.PrefetchScalarGridSpec(
            num_scalar_prefetch=1,
            grid=(2 * PHEADS,),
            in_specs=anywhere(8)
            + [head_spec(planes, LMAX, 2 * HEAD)] * 2
            + [head_spec(planes, HROWS, 4 * HEAD)] * 2
            + anywhere(len(carry)),
            out_specs=anywhere(8) + [head_spec(planes, LMAX, 2 * HEAD)] * 2,
            scratch_shapes=[
                pltpu.VMEM((2, 4 * SUBS * HALF, LMAX), BF16),
                pltpu.VMEM((2, 4 * SUBS * HALF, LMAX), BF16),
                pltpu.VMEM((LMAX, 4 * HEAD), BF16),
                pltpu.SemaphoreType.DMA((2, 4)),
                pltpu.SemaphoreType.DMA((2, 4)),
            ],
        ),
        out_shape=[jax.ShapeDtypeStruct((SUBS * HALF, LMAX), BF16)] * 8
        + [jax.ShapeDtypeStruct((HEADS, LMAX, 2 * HEAD), BF16)] * 2,
        input_output_aliases={13 + i: 8 + i for i in range(len(carry))},
        compiler_params=params(60),
        cost_estimate=pl.CostEstimate(
            flops=3 * HEADS * HROWS * LMAX * 4 * HEAD,
            bytes_accessed=HEADS * (2 * HROWS * LMAX + 4 * HROWS * 256 + 4 * LMAX * 256),
            transcendentals=HEADS * HROWS * LMAX // 2,
        ),
        name="unmix",
    )(sc, *shards, v_own, v_far, grad_heads, mean, *carry)


def close_kernel(sc, tok, res_own, res_got, out_own, out_got, own, far, gain, w_own, w_far, *refs):
    (output, tok_grad, d_value, d_gain, total, weight) = refs
    step = pl.program_id(0)
    whole_weight(sc, step, w_own, w_far, weight)
    core = sc[CORE]
    output[:, :, core] = out_own[...]
    output[:, :, 1 - core] = out_got[...].astype(F32)
    tok_grad[:, :, core] = res_own[...]
    tok_grad[:, :, 1 - core] = res_got[...].astype(F32)
    runs = tok.shape[1]
    rows = runs * 128
    for item in range(2):
        lanes = slice(item * HEAD, (item + 1) * HEAD)
        pieces = [
            add_low(own[head, :, lanes], far[head, :, lanes]) for head in range(HEADS)
        ]
        back = jnp.concatenate(pieces, axis=1)
        x = tok[item].reshape(rows, WIDTH).astype(F32)
        scale = lax.rsqrt(jnp.mean(x * x, axis=-1, keepdims=True) + EPSILON)
        unit = x * scale
        normed = (unit * gain[...]).astype(BF16)
        normed_grad = dot(back, weight[...], 1, 1)
        gained = normed_grad * gain[...]
        update = scale * (gained - unit * jnp.mean(gained * unit, axis=-1, keepdims=True))
        tok_grad[item] += update.reshape(runs, 2, HALF, WIDTH)
        gain_sum = jnp.sum(normed_grad * unit, axis=0, keepdims=True)
        value_sum = dot(normed, back, 0, 0)
        if item == 0:
            gain_total, value_total = gain_sum, value_sum
        else:
            gain_total, value_total = gain_total + gain_sum, value_total + value_sum

    @pl.when(step == 0)
    def _():
        d_gain[...] = gain_total
        total[...] = value_total

    @pl.when(step > 0)
    def _():
        d_gain[...] += gain_total
        total[...] += value_total

    @pl.when(step == pl.num_programs(0) - 1)
    def _():
        low = total[...].astype(BF16)
        d_value[0] = low[:, :SIDE]
        d_value[1] = low[:, SIDE:]


def run_close(sc, tokens, res_own, res_got, out_own, out_got, own, far, gain, w_own, w_far):
    runs = 2
    slab = (2, RUNS, 2, HALF, WIDTH)
    half = (2, RUNS, HALF, WIDTH)
    whole_spec = spec((2, runs, 2, HALF, WIDTH), lambda j, s: (0, j, 0, 0, 0))
    half_spec = spec((2, runs, HALF, WIDTH), lambda j, s: (0, j, 0, 0))
    back_spec = spec((HEADS, runs * 128, 2 * HEAD), lambda j, s: (0, j, 0))
    return pl.pallas_call(
        close_kernel,
        grid_spec=pltpu.PrefetchScalarGridSpec(
            num_scalar_prefetch=1,
            grid=(RUNS // runs,),
            in_specs=[whole_spec]
            + [half_spec] * 4
            + [back_spec, back_spec, held((1, WIDTH)), held((WIDTH, SIDE)), held((WIDTH, SIDE))],
            out_specs=[whole_spec, whole_spec, held((2, WIDTH, SIDE)), held((1, WIDTH))],
            scratch_shapes=[pltpu.VMEM((WIDTH, WIDTH), F32), pltpu.VMEM((WIDTH, WIDTH), BF16)],
        ),
        out_shape=[
            jax.ShapeDtypeStruct(slab, F32),
            jax.ShapeDtypeStruct(slab, F32),
            jax.ShapeDtypeStruct((2, WIDTH, SIDE), BF16),
            jax.ShapeDtypeStruct((1, WIDTH), F32),
        ],
        compiler_params=params(48),
        cost_estimate=pl.CostEstimate(
            flops=4 * 2 * LMAX * WIDTH * WIDTH, bytes_accessed=38 * LMAX * WIDTH, transcendentals=0
        ),
        name="close",
    )(
        sc,
        tokens.reshape(slab),
        *(x.reshape(half) for x in (res_own, res_got, out_own, out_got)),
        own,
        far,
        gain,
        w_own,
        w_far,
    )


PACK_DOWN, PACK_UP, PACK_OUT, PACK = 0, 192, 384, 432
SHARE = SUBS * HALF + 32


def chip_of(sc, k, rel):
    return plane_of(k, sc) * 4 + (sc[PLACE] ^ rel)


def place_kernel(moves, sc, *refs):
    pieces, targets, sems = refs[:16], refs[16:-1], refs[-1]
    copies = []
    for index, piece in enumerate(pieces):
        chip = chip_of(sc, index // 4, index % 4)
        for which, (start, count, lane, target, step, offset, column) in enumerate(moves):
            rows = pl.ds(pl.multiple_of(chip * step + offset, 16), count)
            copies.append(
                pltpu.make_async_copy(
                    piece.at[pl.ds(start, count), pl.ds(lane, SIDE)],
                    targets[target].at[rows, pl.ds(column, SIDE)],
                    sems.at[index, which],
                )
            )
    for copy in copies:
        copy.start()
    for copy in copies:
        copy.wait()


def run_place(sc, pieces, moves, shapes):
    return pl.pallas_call(
        partial(place_kernel, moves),
        grid_spec=pltpu.PrefetchScalarGridSpec(
            num_scalar_prefetch=1,
            grid=(1,),
            in_specs=anywhere(16),
            out_specs=anywhere(len(shapes)),
            scratch_shapes=[pltpu.SemaphoreType.DMA((16, len(moves)))],
        ),
        out_shape=[jax.ShapeDtypeStruct(shape, BF16) for shape in shapes],
        compiler_params=params(60),
        cost_estimate=pl.CostEstimate(
            flops=0, bytes_accessed=4 * sum(a * b for a, b in shapes), transcendentals=0
        ),
        name="place",
    )(sc, *pieces)


def place_values(sc, shares):
    start = SUBS * HALF
    moves = (
        (start, 32, 0, 0, 48, 0, 0),
        (start, 16, SIDE, 0, 48, 32, 0),
        (start + 16, 16, SIDE, 1, 16, 0, 0),
    )
    return run_place(sc, shares, moves, [(WIDTH, SIDE), (256, SIDE)])


def place_weights(sc, pieces):
    moves = (
        (PACK_DOWN, 192, 0, 0, 192, 0, 0),
        *((PACK_UP + 48 * j, 48, 0, 1, 48, 0, j * SIDE) for j in range(4)),
        (PACK_OUT, 48, 0, 2, 48, 0, 0),
    )
    return run_place(sc, pieces, moves, [(FF, SIDE), (WIDTH, FF // 2), (WIDTH, SIDE)])


def collect_kernel(sc, down, down_got, up, up_got, out, out_got, packed):
    both = lambda a, b: (a.astype(F32) + b.astype(F32)).astype(BF16)
    packed[0, 0:192] = both(down[...], down_got[...])
    for j in range(4):
        lanes = slice(j * SIDE, (j + 1) * SIDE)
        packed[0, 192 + 48 * j : 240 + 48 * j] = both(up[:, lanes], up_got[:, lanes])
    packed[0, 384:432] = both(out[...], out_got[...])


def run_collect(sc, down, down_got, up, up_got, out, out_got):
    chip = lambda i, s: (chip_of(s, i // 4, i % 4), 0)
    rows = lambda x: spec((x.shape[0] // 16, x.shape[1]), chip)
    args = (down, down_got, up, up_got, out, out_got)
    return pl.pallas_call(
        collect_kernel,
        grid_spec=pltpu.PrefetchScalarGridSpec(
            num_scalar_prefetch=1,
            grid=(16,),
            in_specs=[rows(x) for x in args],
            out_specs=spec((1, PACK, SIDE), lambda i, s: (i, 0, 0)),
        ),
        out_shape=jax.ShapeDtypeStruct((16, PACK, SIDE), BF16),
        compiler_params=params(16),
        cost_estimate=pl.CostEstimate(flops=0, bytes_accessed=3 * 16 * PACK * SIDE * 2, transcendentals=0),
        name="collect",
    )(sc, *args)


DEVICES = 32
TO_CORE, TO_X, TO_Y = 1, 2, 4


def swap(x, bit):
    return lax.ppermute(x, BOTH, [(d, d ^ bit) for d in range(DEVICES)])


def ring(x, way=1):
    return lax.ppermute(x, BOTH, [(d, (d + 8 * way) % DEVICES) for d in range(DEVICES)])


def pick(x, index, axis=0):
    return lax.dynamic_index_in_dim(x, index, axis, keepdims=False)


def ordered(flag, one, two, axis=0, joined=jnp.stack):
    return jnp.where(flag == 0, joined([one, two], axis), joined([two, one], axis))


def add_low(one, two):
    return (one.astype(F32) + two.astype(F32)).astype(BF16)


STEPS = (
    ((0, 0, 1), (0, 1, 0), (1, 0, 0)),
    ((1, 0, 1), (0, 1, 1), (2, 0, 0)),
    ((2, 0, 1), (1, 1, 0), (3, 0, 0)),
    ((3, 0, 1), (2, 1, 0), (1, 1, 1)),
    ((2, 1, 1), (3, 1, 1), (3, 1, 0)),
)


def gather16(own, works=(), made=()):
    have = {(0, 0, 0): own}
    for step, (by_x, by_y, by_z) in enumerate(STEPS):
        got = {
            by_z: ring(have[by_z[0] - 1, by_z[1], by_z[2]]),
            by_x: swap(have[by_x[0], by_x[1], 0], TO_X),
            by_y: swap(have[by_y[0], 0, by_y[2]], TO_Y),
        }
        if step < len(works):
            made = works[step](made)
        have, made = lax.optimization_barrier(({**have, **got}, made))
    return [have[k, y, x] for k in range(4) for y in range(2) for x in range(2)], made


def scatter16(shares, works=(), made=()):
    have = {}

    def put(planes, values):
        for index, value in enumerate(values):
            have[planes[index // 4], index // 2 % 2, index % 2] = value

    put((0, 1, 2, 3) if len(shares) == 16 else (3, 2), shares)
    for step, (by_x, by_y, by_z) in enumerate(reversed(STEPS)):
        got = [
            ((by_z[0] - 1, by_z[1], by_z[2]), ring(have[by_z], -1)),
            ((by_x[0], by_x[1], 0), swap(have[by_x], TO_X)),
            ((by_y[0], 0, by_y[2]), swap(have[by_y], TO_Y)),
        ]
        for at in (by_x, by_y, by_z):
            del have[at]
        if step < len(works):
            made = works[step](made)
        values, have, made = lax.optimization_barrier(([value for _, value in got], have, made))
        if step == 0 and len(shares) == 8:
            put((1, 0), made[0])
        for at in dict.fromkeys(at for at, _ in got):
            total = have[at].astype(F32)
            for (target, _), value in zip(got, values):
                if target == at:
                    total = total + value.astype(F32)
            have[at] = total if step == len(STEPS) - 1 else total.astype(BF16)
    return have[0, 0, 0], made


def after(x, *others):
    return lax.optimization_barrier((x, others))[0]


def chip_shards(tokens, lengths, rand_mix, w_value, w_out, w_up, w_down, gain_mix, gain_ffn, grad_out):
    wide = lax.axis_index("wide")
    core = lax.axis_index("narrow")
    z, y, x = wide // 4, (wide // 2) % 2, wide % 2
    other = lambda value: swap(value, TO_CORE)
    side = partial(ordered, core, joined=jnp.concatenate)

    gains = jnp.pad(jnp.concatenate([gain_mix, gain_ffn])[None], ((0, 7), (0, SIDE - 48)))
    halves = [
        jnp.concatenate(
            [
                w_value[:, c * SIDE : (c + 1) * SIDE],
                gains,
                w_down[:, c * SIDE : (c + 1) * SIDE],
                *[w_up[:, (4 * c + j) * SIDE : (4 * c + j + 1) * SIDE] for j in range(4)],
                w_out[:, c * SIDE : (c + 1) * SIDE],
            ]
        )
        for c in range(2)
    ]
    both = jnp.stack(halves)
    joined = ordered(core, pick(both, core), other(pick(both, 1 - core)))
    part_of = lambda start, rows: joined[:, start : start + rows].reshape(2 * rows, SIDE)
    up_rows = joined[:, 128:224].reshape(2, 4, 24, SIDE).transpose(1, 0, 2, 3).reshape(192, SIDE)
    packed = jnp.concatenate([part_of(32, 96), up_rows, part_of(224, 24)])
    first = jnp.concatenate([part_of(0, 24), part_of(24, 8)])
    first = jnp.pad(jnp.concatenate([first[:32], first[32:]], axis=1), ((0, 0), (0, LMAX - WIDTH)))
    rand = rand_mix.reshape(3, 2, HALF, LMAX)
    blocks = side(pick(rand, core, 1), other(pick(rand, 1 - core, 1)), 0)
    share = jnp.concatenate([blocks.reshape(SUBS * HALF, LMAX), first])
    share, packed = lax.optimization_barrier((share, packed))

    slab = (2, RUNS, 2, HALF, WIDTH)
    tokens, grad_out = tokens.reshape(slab), grad_out.reshape(slab)

    def from_other(_):
        return other(lengths), other(pick(tokens, 1 - core, 2)), other(pick(grad_out, 1 - core, 2))

    shares, (far_lengths, tokens_far, grad_far) = gather16(share, [from_other])
    sc = jnp.concatenate([jnp.stack([core, z, wide % 4]).astype(jnp.int32), lengths, far_lengths])

    def make_values(_):
        value, gain_rows = place_values(sc, shares)
        value_far = other(value)
        gain_rows = gain_rows.reshape(16, 2, 8, SIDE)[:, :, 0]
        gain_one = gain_rows[..., :24].reshape(1, WIDTH).astype(F32)
        gain_two = gain_rows[..., 24:48].reshape(1, WIDTH).astype(F32)
        v_own = run_values(sc, tokens.reshape(2, LMAX, WIDTH), gain_one, value, value_far)
        return value, value_far, gain_one, gain_two, v_own

    def share_values(made):
        return *made, other(made[-1])

    def mix_near(made):
        return *made, run_mix(sc, (0, 1), shares[:8], made[-2], made[-1], ())

    def mix_far(made):
        *made, near = made
        return *made, run_mix(sc, (2, 3), shares[8:], made[-2], made[-1], near)

    pieces, made = gather16(after(packed, *shares[-3:]), [make_values, share_values, mix_near, mix_far])
    value, value_far, gain_one, gain_two, v_own, v_far, (heads, mean) = made
    down, up, out = place_weights(sc, pieces)
    down, up, out = (down, other(down)), (up, other(up)), (out, other(out))

    mixed, resid, normed, masked = run_pre(sc, tokens, tokens_far, grad_out, grad_far, heads, out, gain_two)
    active, up_grad, back = run_units(sc, normed, masked, up, down)
    res_own, res_far, grad_heads, d_out_own, d_out_far, d_gain_two = run_post(
        sc, resid, back, masked, mixed, out, gain_two
    )
    *far, back_own, back_far = run_unmix(
        sc, (3, 2), shares[12:] + shares[8:12], v_own, v_far, grad_heads, mean, ()
    )

    def unmix_near(_):
        *near, own, far = run_unmix(
            sc, (1, 0), shares[4:8] + shares[:4], v_own, v_far, grad_heads, mean, (back_own, back_far)
        )
        return near, own, far, other(res_far), other(d_out_far)

    def make_output(made):
        near, own, far, *rest = made
        return near, own, other(far), *rest, *run_out(sc, active, resid, down)

    def make_down(made):
        *rest, out_own, out_far = made
        return *rest, out_own, other(out_far), *run_down_grad(sc, active, masked)

    def make_up(made):
        *rest, down_own, down_far = made
        return *rest, (down_own, other(down_far)), run_up_grad(sc, normed, up_grad)

    def finish(made):
        _, own, got, res_got, d_out_got, out_own, out_got, down_sides, (up_own, up_far) = made
        output, tokens_grad, d_value, d_gain_one = run_close(
            sc, tokens, res_own, res_got, out_own, out_got, own, got, gain_one, value, value_far
        )
        gain_pair = jnp.concatenate([d_gain_one, d_gain_two]).reshape(2, 16, 1, 48).astype(BF16)
        gain_pair = jnp.pad(gain_pair, ((0, 0), (0, 0), (0, 15), (0, SIDE - 48)))
        small = jnp.concatenate([d_value.reshape(2, 16, 48, SIDE), gain_pair], 2)
        return output, tokens_grad, small, (*down_sides, up_own, other(up_far), d_out_own, d_out_got)

    rand_sum, made = scatter16(far, [unmix_near, make_output, make_down, make_up, finish])
    output, tokens_grad, small, sides = made
    packed = run_collect(sc, *sides)

    def small_core(_):
        return add_low(pick(small, core), other(pick(small, 1 - core))).reshape(4, 2, 2, 64, SIDE)

    def small_line(made):
        return add_low(pick(made, x, 2), swap(pick(made, 1 - x, 2), TO_X))

    def small_plane(made):
        return add_low(pick(made, y, 1), swap(pick(made, 1 - y, 1), TO_Y))

    def small_planes(made):
        total = pick(made, z).astype(F32)
        for k in range(1, PLANES):
            total = total + ring(pick(made, lax.rem(z + PLANES - k, PLANES)), -k).astype(F32)
        return total

    def rand_home(made):
        blocks = rand_sum.reshape(2, 3, HALF, LMAX)
        return made, pick(blocks, core), other(pick(blocks, 1 - core))

    big_sum, made = scatter16(
        after([packed[i] for i in range(16)], rand_sum), [small_core, small_line, small_plane, small_planes, rand_home]
    )
    small_sum, blocks, blocks_far = made
    big_far, small_far = other(big_sum), other(small_sum)

    rows_of = lambda value, rows: pick(value.reshape(-1, 2, rows, SIDE), core, 1)
    mine = lambda own, far, rows: side(rows_of(own, rows)[0], rows_of(far, rows)[0], 1)
    down_shard = mine(big_sum[PACK_DOWN:PACK_UP], big_far[PACK_DOWN:PACK_UP], 96)
    up_side = lambda value: rows_of(value[PACK_UP:PACK_OUT], 24).transpose(1, 0, 2).reshape(24, 4 * SIDE)
    up_shard = side(up_side(big_sum), up_side(big_far), 1)
    outproj_shard = mine(big_sum[PACK_OUT:], big_far[PACK_OUT:], 24)
    value_shard = mine(small_sum[:48], small_far[:48], 24)
    gains_pair = ordered(core, small_sum[48, :48], small_far[48, :48])
    gain_pair = pick(gains_pair.reshape(2, 2, 24), core, 1)

    rand_shard = ordered(core, blocks, blocks_far, 1)

    return (
        output.reshape(2, LMAX, WIDTH),
        tokens_grad.reshape(2, LMAX, WIDTH),
        rand_shard.reshape(3 * 128, LMAX),
        value_shard,
        outproj_shard,
        up_shard,
        down_shard,
        gain_pair[0],
        gain_pair[1],
    )


def rms_norm(values, gain):
    scale = lax.rsqrt(jnp.mean(values * values, axis=-1, keepdims=True) + EPSILON)
    return values * scale * gain


def split_heads(block):
    return block.reshape(LMAX, HEADS, HEAD).transpose(1, 0, 2)


def merge_heads(block):
    return block.transpose(1, 0, 2).reshape(LMAX, HEADS * HEAD)


def masked_scores(key_mask, rand_head):
    return jnp.where(key_mask[None, :] > 0, rand_head.astype(jnp.float32), -1e30)


def head_forward(key_mask, paired):
    rand_head, value_head = paired
    scores = masked_scores(key_mask, rand_head)
    row_peak = jnp.max(scores, axis=-1, keepdims=True)
    exponent = jnp.exp(scores - row_peak)
    denom_sum = jnp.sum(exponent, axis=-1, keepdims=True)
    attention = exponent / denom_sum * key_mask[:, None]
    mixed = jnp.dot(attention.astype(jnp.bfloat16), value_head, preferred_element_type=jnp.float32)
    return (mixed.astype(jnp.bfloat16), row_peak + jnp.log(denom_sum))


def head_backward(key_mask, paired):
    rand_head, value_head, mix_grad, log_total = paired
    scores = masked_scores(key_mask, rand_head)
    attention = jnp.exp(scores - log_total) * key_mask[:, None]
    prob_grad = jnp.einsum("id,jd->ij", mix_grad, value_head, preferred_element_type=jnp.float32)
    value_grad = jnp.einsum(
        "ij,id->jd", attention.astype(jnp.bfloat16), mix_grad, preferred_element_type=jnp.float32
    )
    score_grad = attention * (prob_grad - jnp.sum(prob_grad * attention, axis=-1, keepdims=True))
    return (score_grad, value_grad)


def shards(tokens, lengths, rand_mix, w_value, w_out, w_up, w_down, gain_mix, gain_ffn, grad_out):
    item_count = tokens.shape[0]
    width = tokens.shape[2]
    row_count = item_count * LMAX
    tokens_flat = tokens.reshape(row_count, width).astype(jnp.float32)
    positions = jnp.arange(LMAX, dtype=jnp.int32)
    valid_table = (positions[None, :] < lengths[:, None]).astype(jnp.float32)
    row_valid = valid_table.reshape(row_count, 1)
    forward_set = (
        lax.all_gather(rand_mix, ("wide", "narrow"), axis=0, tiled=True),
        lax.all_gather(w_value, ("wide", "narrow"), axis=0, tiled=True),
        lax.all_gather(w_out, ("wide", "narrow"), axis=0, tiled=True),
        lax.all_gather(w_up, ("wide", "narrow"), axis=0, tiled=True),
        lax.all_gather(w_down, ("wide", "narrow"), axis=0, tiled=True),
        lax.all_gather(gain_mix, ("wide", "narrow"), axis=0, tiled=True),
        lax.all_gather(gain_ffn, ("wide", "narrow"), axis=0, tiled=True),
    )
    rand_all, value_all, out_all, up_all, down_all, gain_first, gain_second = forward_set
    normed = rms_norm(tokens_flat, gain_first.astype(jnp.float32)).astype(jnp.bfloat16)
    values = jnp.dot(normed, value_all, preferred_element_type=jnp.float32).astype(jnp.bfloat16)
    rand_heads = rand_all.reshape(HEADS, LMAX, LMAX)
    mixed_parts = []
    totals_kept = []
    for item_index in range(item_count):
        item_values = split_heads(values[item_index * LMAX : (item_index + 1) * LMAX])
        mixed_heads, log_total = lax.map(
            partial(head_forward, valid_table[item_index]), (rand_heads, item_values)
        )
        mixed_parts.append(merge_heads(mixed_heads))
        totals_kept.append(log_total)
    mixed = jnp.concatenate(mixed_parts, axis=0)
    residual = tokens_flat + jnp.dot(mixed, out_all, preferred_element_type=jnp.float32)
    normed_two = rms_norm(residual, gain_second.astype(jnp.float32)).astype(jnp.bfloat16)
    up_proj = jnp.dot(normed_two, up_all, preferred_element_type=jnp.float32)
    active = jax.nn.gelu(up_proj).astype(jnp.bfloat16)
    branch = jnp.dot(active, down_all, preferred_element_type=jnp.float32)
    output = row_valid * (residual + branch)
    back_set = (
        lax.all_gather(rand_mix, ("wide", "narrow"), axis=0, tiled=True),
        lax.all_gather(w_value, ("wide", "narrow"), axis=0, tiled=True),
        lax.all_gather(w_out, ("wide", "narrow"), axis=0, tiled=True),
        lax.all_gather(w_up, ("wide", "narrow"), axis=0, tiled=True),
        lax.all_gather(w_down, ("wide", "narrow"), axis=0, tiled=True),
        lax.all_gather(gain_mix, ("wide", "narrow"), axis=0, tiled=True),
        lax.all_gather(gain_ffn, ("wide", "narrow"), axis=0, tiled=True),
    )
    rand_back, value_back, out_back, up_back, down_back, gain_back_one, gain_back_two = back_set
    cotangent = grad_out.reshape(row_count, width).astype(jnp.float32)
    masked = row_valid * cotangent
    branch_grad = masked.astype(jnp.bfloat16)
    grad_down = jnp.einsum("rk,rd->kd", active, branch_grad, preferred_element_type=jnp.float32)
    active_grad = jnp.einsum(
        "rd,kd->rk", branch_grad, down_back, preferred_element_type=jnp.float32
    )
    gelu_value, gelu_pull = jax.vjp(jax.nn.gelu, up_proj)
    up_grad = gelu_pull(active_grad)[0].astype(jnp.bfloat16)
    grad_up = jnp.einsum("rd,rk->dk", normed_two, up_grad, preferred_element_type=jnp.float32)
    normed_two_grad = jnp.einsum("rk,dk->rd", up_grad, up_back, preferred_element_type=jnp.float32)
    norm_value, norm_pull = jax.vjp(rms_norm, residual, gain_back_two.astype(jnp.float32))
    residual_part, gain_two_grad = norm_pull(normed_two_grad)
    residual_grad = masked + residual_part
    attn_grad = residual_grad.astype(jnp.bfloat16)
    grad_outproj = jnp.einsum("rd,re->de", mixed, attn_grad, preferred_element_type=jnp.float32)
    mixed_grad = jnp.einsum(
        "re,de->rd", attn_grad, out_back, preferred_element_type=jnp.float32
    ).astype(jnp.bfloat16)
    rand_heads_back = rand_back.reshape(HEADS, LMAX, LMAX)
    rand_grad = jnp.zeros((HEADS, LMAX, LMAX), jnp.float32)
    value_parts = []
    for item_index in range(item_count):
        lower_row = item_index * LMAX
        upper_row = lower_row + LMAX
        item_values = split_heads(values[lower_row:upper_row])
        item_mix_grad = split_heads(mixed_grad[lower_row:upper_row])
        score_grad, value_grad = lax.map(
            partial(head_backward, valid_table[item_index]),
            (rand_heads_back, item_values, item_mix_grad, totals_kept[item_index]),
        )
        rand_grad = rand_grad + score_grad
        value_parts.append(merge_heads(value_grad))
    values_grad = jnp.concatenate(value_parts, axis=0).astype(jnp.bfloat16)
    grad_value = jnp.einsum("rd,re->de", normed, values_grad, preferred_element_type=jnp.float32)
    normed_grad = jnp.einsum(
        "re,de->rd", values_grad, value_back, preferred_element_type=jnp.float32
    )
    norm_first, first_pull = jax.vjp(rms_norm, tokens_flat, gain_back_one.astype(jnp.float32))
    token_part, gain_one_grad = first_pull(normed_grad)
    tokens_grad = residual_grad + token_part
    rand_flat = rand_grad.reshape(HEADS * LMAX, LMAX)
    all_shards = (
        lax.psum_scatter(rand_flat, ("wide", "narrow"), scatter_dimension=0, tiled=True),
        lax.psum_scatter(grad_value, ("wide", "narrow"), scatter_dimension=0, tiled=True),
        lax.psum_scatter(grad_outproj, ("wide", "narrow"), scatter_dimension=0, tiled=True),
        lax.psum_scatter(grad_up, ("wide", "narrow"), scatter_dimension=0, tiled=True),
        lax.psum_scatter(grad_down, ("wide", "narrow"), scatter_dimension=0, tiled=True),
        lax.psum_scatter(gain_one_grad, ("wide", "narrow"), scatter_dimension=0, tiled=True),
        lax.psum_scatter(gain_two_grad, ("wide", "narrow"), scatter_dimension=0, tiled=True),
    )
    rand_shard, value_shard, outproj_shard, up_shard, down_shard, gain_one_shard, gain_two_shard = (
        all_shards
    )
    return (
        output.reshape(item_count, LMAX, width),
        tokens_grad.reshape(item_count, LMAX, width),
        rand_shard,
        value_shard,
        outproj_shard,
        up_shard,
        down_shard,
        gain_one_shard,
        gain_two_shard,
    )


def solution(mesh):
    in_specs = (
        P(("wide", "narrow"), None, None),
        P(("wide", "narrow")),
        P(("wide", "narrow"), None),
        P(("wide", "narrow"), None),
        P(("wide", "narrow"), None),
        P(("wide", "narrow"), None),
        P(("wide", "narrow"), None),
        P(("wide", "narrow")),
        P(("wide", "narrow")),
        P(("wide", "narrow"), None, None),
    )
    out_specs = (
        P(("wide", "narrow"), None, None),
        P(("wide", "narrow"), None, None),
        P(("wide", "narrow"), None),
        P(("wide", "narrow"), None),
        P(("wide", "narrow"), None),
        P(("wide", "narrow"), None),
        P(("wide", "narrow"), None),
        P(("wide", "narrow")),
        P(("wide", "narrow")),
    )
    fits = dict(mesh.shape) == {"wide": 16, "narrow": 2}
    return jax.shard_map(chip_shards if fits else shards, mesh=mesh, in_specs=in_specs, out_specs=out_specs, check_vma=False)
```

```python
from functools import partial

import jax
import jax.numpy as jnp
from jax import lax
from jax.experimental import pallas as pl
from jax.experimental.pallas import tpu as pltpu
from jax.sharding import PartitionSpec as P

HEADS = 12
HEAD = 64
LMAX = 1024
WIDTH = 768
FF = 3072
EPSILON = 1e-05

BOTH = ("wide", "narrow")
BF16 = jnp.bfloat16
F32 = jnp.float32
MIB = 1 << 20

SUBS = 6
RUNS = 8
HALF = 64
HROWS = RUNS * HALF
PLANES = 4
PHEADS = HEADS // PLANES
ROWS = 2 * LMAX
FSTEP = 768
FSIDE = FF // 2 // FSTEP
TILE = 512
SIDE = WIDTH // 2
SPAN = 2 * HALF


def dot(a, b, ca, cb):
    return lax.dot_general(a, b, (((ca,), (cb,)), ((), ())), preferred_element_type=F32)


CORE, PLANE, PLACE, LENGTHS = 0, 1, 2, 3


def spec(shape, index):
    return pl.BlockSpec(shape, index)


def held(shape):
    zeros = (0,) * len(shape)
    return pl.BlockSpec(shape, lambda *_: zeros, pipeline_mode=pl.Buffered(1))


def params(limit):
    return pltpu.CompilerParams(vmem_limit_bytes=limit * MIB)


def whole_weight(sc, step, own, far, weight):
    @pl.when(step == 0)
    def _():
        weight[:, pl.ds(pl.multiple_of(sc[CORE] * SIDE, 128), SIDE)] = own[...]
        weight[:, pl.ds(pl.multiple_of((1 - sc[CORE]) * SIDE, 128), SIDE)] = far[...]


def values_kernel(sc, tok, gain, w_own, w_far, out, weight):
    step = pl.program_id(0)
    whole_weight(sc, step, w_own, w_far, weight)
    rows = tok.shape[1]
    position = step * rows + lax.broadcasted_iota(jnp.int32, (rows, 1), 0)
    for item in range(2):
        x = tok[item].astype(F32)
        scale = lax.rsqrt(jnp.mean(x * x, axis=-1, keepdims=True) + EPSILON)
        normed = (x * scale * gain[...]).astype(BF16)
        found = dot(normed, weight[...], 1, 0)
        found = jnp.where(position < sc[LENGTHS + item], found, 0.0).astype(BF16)
        for head in range(HEADS):
            out[head, :, item * HEAD : (item + 1) * HEAD] = found[:, head * HEAD : (head + 1) * HEAD]


def run_values(sc, tokens, gain, w_own, w_far):
    rows = 256
    return pl.pallas_call(
        values_kernel,
        grid_spec=pltpu.PrefetchScalarGridSpec(
            num_scalar_prefetch=1,
            grid=(LMAX // rows,),
            in_specs=[
                spec((2, rows, WIDTH), lambda j, s: (0, j, 0)),
                held((1, WIDTH)),
                held((WIDTH, SIDE)),
                held((WIDTH, SIDE)),
            ],
            out_specs=spec((HEADS, rows, 2 * HEAD), lambda j, s: (0, j, 0)),
            scratch_shapes=[pltpu.VMEM((WIDTH, WIDTH), BF16)],
        ),
        out_shape=jax.ShapeDtypeStruct((HEADS, LMAX, 2 * HEAD), BF16),
        compiler_params=params(32),
        cost_estimate=pl.CostEstimate(
            flops=2 * 2 * LMAX * WIDTH * WIDTH, bytes_accessed=8 * LMAX * WIDTH, transcendentals=0
        ),
        name="values",
    )(sc, tokens, gain, w_own, w_far)


def lane_lengths(sc, shape):
    slot = lax.broadcasted_iota(jnp.int32, shape, 1) // HEAD
    length = jnp.where(slot == 0, sc[LENGTHS], sc[LENGTHS + 1])
    return jnp.where(slot >= 2, jnp.where(slot == 2, sc[LENGTHS + 2], sc[LENGTHS + 3]), length)


def plane_of(k, sc):
    return lax.rem(sc[PLANE] + PLANES - k, PLANES)


def plane_spec(planes, rows, lanes):
    def index(step, sc):
        return (plane_of(planes[0] + step * (planes[1] - planes[0]), sc), 0, 0)

    return spec((PHEADS, rows, lanes), index)


def anywhere(count):
    return [pl.BlockSpec(memory_space=pl.ANY)] * count


def plane_fetch(place, shards, raw, sems, slot):
    return [
        pltpu.make_async_copy(
            shards[4 * slot + rel].at[pl.ds(0, SUBS * HALF)],
            raw.at[slot, pl.ds(pl.multiple_of((place ^ rel) * SUBS * HALF, SUBS * HALF), SUBS * HALF)],
            sems.at[slot, rel],
        )
        for rel in range(4)
    ]


def take_plane(place, shards, raw, sems):
    step = pl.program_id(0)

    @pl.when(step == 0)
    def _():
        for slot in range(2):
            for copy in plane_fetch(place, shards, raw, sems, slot):
                copy.start()

    for slot in range(2):

        @pl.when(step == slot)
        def _():
            for copy in plane_fetch(place, shards, raw, sems, slot):
                copy.wait()

    return step


def head_rows(head):
    return slice(head * HROWS, (head + 1) * HROWS)


def fill_mask(sc, mask):
    @pl.when(pl.program_id(0) == 0)
    def _():
        shape = (LMAX, 4 * HEAD)
        column = lax.broadcasted_iota(jnp.int32, shape, 0)
        mask[...] = (column < lane_lengths(sc, shape)).astype(F32).astype(BF16)


def inverse_sums(sc, weights, mask):
    shape = (HROWS, 4 * HEAD)
    line = lax.broadcasted_iota(jnp.int32, shape, 0)
    position = 128 * (line // HALF) + HALF * sc[CORE] + line % HALF
    return jnp.where(position < lane_lengths(sc, shape), 1.0 / dot(weights, mask[...], 1, 0), 0.0)


def mix_kernel(carried, sc, *refs):
    shards, (v_own, v_far, *rest) = refs[:8], refs[8:]
    mixed, mean, raw, mask, sems = rest[2:] if carried else rest
    fill_mask(sc, mask)
    slot = take_plane(sc[PLACE], shards, raw, sems)
    for head in range(PHEADS):
        weights = jnp.exp(raw[slot, head_rows(head)].astype(F32)).astype(BF16)
        values = jnp.concatenate([v_own[head], v_far[head]], axis=1)
        found = dot(weights, values, 1, 0) * inverse_sums(sc, weights, mask)
        mean[head] = found
        mixed[head] = found.astype(BF16)


def run_mix(sc, planes, shards, v_own, v_far, carry):
    carry = list(carry)
    return pl.pallas_call(
        partial(mix_kernel, bool(carry)),
        grid_spec=pltpu.PrefetchScalarGridSpec(
            num_scalar_prefetch=1,
            grid=(2,),
            in_specs=anywhere(8) + [plane_spec(planes, LMAX, 2 * HEAD)] * 2 + anywhere(len(carry)),
            out_specs=[plane_spec(planes, HROWS, 4 * HEAD)] * 2,
            scratch_shapes=[
                pltpu.VMEM((2, 4 * SUBS * HALF, LMAX), BF16),
                pltpu.VMEM((LMAX, 4 * HEAD), BF16),
                pltpu.SemaphoreType.DMA((2, 4)),
            ],
        ),
        out_shape=[
            jax.ShapeDtypeStruct((HEADS, HROWS, 4 * HEAD), BF16),
            jax.ShapeDtypeStruct((HEADS, HROWS, 4 * HEAD), F32),
        ],
        input_output_aliases={11 + i: i for i in range(len(carry))},
        compiler_params=params(60),
        cost_estimate=pl.CostEstimate(
            flops=2 * HEADS * HROWS * LMAX * 4 * HEAD,
            bytes_accessed=HEADS * (HROWS * LMAX + 5 * HROWS * 256),
            transcendentals=HEADS * HROWS * LMAX // 2,
        ),
        name="mix",
    )(sc, *shards, v_own, v_far, *carry)


def row_valid(sc, step):
    line = lax.broadcasted_iota(jnp.int32, (4 * SPAN, 1), 0)
    item = line // SPAN
    row = step * SPAN + line % SPAN
    low = jnp.where(item == 0, sc[LENGTHS], sc[LENGTHS + 1])
    high = jnp.where(item == 2, sc[LENGTHS + 2], sc[LENGTHS + 3])
    return 128 * (row // HALF) + HALF * sc[CORE] + row % HALF < jnp.where(item >= 2, high, low)


def four_items(own, far):
    return jnp.concatenate([own[:, :, 0], far[...]], axis=0).reshape(4 * SPAN, WIDTH)


def pre_kernel(sc, tok, tok_far, cot, cot_far, heads, wo_own, wo_far, gain, mixed, resid, normed, grad, weight):
    step = pl.program_id(0)
    whole_weight(sc, step, wo_own, wo_far, weight)
    for item in range(4):
        lanes = slice(item * HEAD, (item + 1) * HEAD)
        for pair in range(HEADS // 2):
            both = jnp.concatenate([heads[2 * pair, :, lanes], heads[2 * pair + 1, :, lanes]], axis=1)
            mixed[item, :, pair * 128 : (pair + 1) * 128] = both
    res = four_items(tok, tok_far).astype(F32) + dot(mixed[...].reshape(4 * SPAN, WIDTH), weight[...], 1, 0)
    resid[...] = res.reshape(4, SPAN, WIDTH)
    scale = lax.rsqrt(jnp.mean(res * res, axis=-1, keepdims=True) + EPSILON)
    valid = row_valid(sc, step)
    normed[...] = jnp.where(valid, res * scale * gain[...], 0.0).astype(BF16).reshape(4, SPAN, WIDTH)
    masked = jnp.where(valid, four_items(cot, cot_far).astype(F32), 0.0)
    grad[...] = masked.astype(BF16).reshape(4, SPAN, WIDTH)


def slab_spec(items=4):
    return spec((items, SPAN, WIDTH), lambda r, s: (0, r, 0))


def half_specs():
    return [
        spec((2, SPAN // HALF, 1, HALF, WIDTH), lambda r, s: (0, r, s[CORE], 0, 0)),
        spec((2, SPAN // HALF, HALF, WIDTH), lambda r, s: (0, r, 0, 0)),
    ]


def heads_spec():
    return spec((HEADS, SPAN, 4 * HEAD), lambda r, s: (0, r, 0))


def run_pre(sc, tokens, tokens_far, cotangent, cotangent_far, heads, wo, gain):
    return pl.pallas_call(
        pre_kernel,
        grid_spec=pltpu.PrefetchScalarGridSpec(
            num_scalar_prefetch=1,
            grid=(HROWS // SPAN,),
            in_specs=half_specs()
            + half_specs()
            + [heads_spec(), held((WIDTH, SIDE)), held((WIDTH, SIDE)), held((1, WIDTH))],
            out_specs=[slab_spec()] * 4,
            scratch_shapes=[pltpu.VMEM((WIDTH, WIDTH), BF16)],
        ),
        out_shape=[
            jax.ShapeDtypeStruct((4, HROWS, WIDTH), BF16),
            jax.ShapeDtypeStruct((4, HROWS, WIDTH), F32),
            jax.ShapeDtypeStruct((4, HROWS, WIDTH), BF16),
            jax.ShapeDtypeStruct((4, HROWS, WIDTH), BF16),
        ],
        compiler_params=params(32),
        cost_estimate=pl.CostEstimate(
            flops=2 * ROWS * WIDTH * WIDTH, bytes_accessed=16 * ROWS * WIDTH, transcendentals=0
        ),
        name="pre",
    )(sc, tokens, tokens_far, cotangent, cotangent_far, heads, *wo, gain)


def own_lanes(sc):
    return pl.ds(pl.multiple_of(sc[CORE] * SIDE, 128), SIDE)


def far_lanes(sc):
    return pl.ds(pl.multiple_of((1 - sc[CORE]) * SIDE, 128), SIDE)


def unit_rows(f, sc):
    return (lax.rem(FSIDE * sc[CORE] + f, 2 * FSIDE), 0)


def unit_columns(f, sc):
    return (0, lax.rem(FSIDE * sc[CORE] + f, 2 * FSIDE))


def early(f, sc):
    return (0, lax.min(f, FSIDE - 1))


def late(f, sc):
    return (0, lax.max(f - FSIDE, 0))


def units_kernel(sc, normed, cot, up_own, up_far, dn_own, dn_far, active, up_grad, back, w_up, w_down):
    step = pl.program_id(0)
    w_down[:, own_lanes(sc)] = dn_own[...]
    w_down[:, far_lanes(sc)] = dn_far[...]

    @pl.when(step < FSIDE)
    def _():
        w_up[...] = up_own[...]

    @pl.when(step >= FSIDE)
    def _():
        w_up[...] = up_far[...]

    for piece in range(ROWS // TILE):
        rows = slice(piece * TILE, (piece + 1) * TILE)
        up = dot(normed[rows], w_up[...], 1, 0)
        square = up * up
        bend = jnp.tanh(up * (0.7978845608028654 + (0.044715 * 0.7978845608028654) * square))
        share = 0.5 + 0.5 * bend
        act = up * share
        active[rows] = act.astype(BF16)
        slope = share + act * (1.0 - share) * (
            2 * 0.7978845608028654 + (6 * 0.044715 * 0.7978845608028654) * square
        )
        low = (dot(cot[rows], w_down[...], 1, 1) * slope).astype(BF16)
        up_grad[rows] = low
        two_grad = dot(low, w_up[...], 1, 1)

        @pl.when(step == 0)
        def _():
            back[rows] = two_grad

        @pl.when(step > 0)
        def _():
            back[rows] += two_grad


def run_units(sc, normed, cotangent, up, down):
    return pl.pallas_call(
        units_kernel,
        grid_spec=pltpu.PrefetchScalarGridSpec(
            num_scalar_prefetch=1,
            grid=(2 * FSIDE,),
            in_specs=[
                held((ROWS, WIDTH)),
                held((ROWS, WIDTH)),
                spec((WIDTH, FSTEP), early),
                spec((WIDTH, FSTEP), late),
                spec((FSTEP, SIDE), unit_rows),
                spec((FSTEP, SIDE), unit_rows),
            ],
            out_specs=[spec((ROWS, FSTEP), unit_columns), spec((ROWS, FSTEP), unit_columns), held((ROWS, WIDTH))],
            scratch_shapes=[pltpu.VMEM((WIDTH, FSTEP), BF16), pltpu.VMEM((FSTEP, WIDTH), BF16)],
        ),
        out_shape=[
            jax.ShapeDtypeStruct((ROWS, FF), BF16),
            jax.ShapeDtypeStruct((ROWS, FF), BF16),
            jax.ShapeDtypeStruct((ROWS, WIDTH), F32),
        ],
        compiler_params=params(56),
        cost_estimate=pl.CostEstimate(
            flops=6 * ROWS * WIDTH * FF, bytes_accessed=8 * ROWS * WIDTH + 4 * ROWS * FF, transcendentals=ROWS * FF
        ),
        name="units",
    )(sc, normed.reshape(ROWS, WIDTH), cotangent.reshape(ROWS, WIDTH), *up, *down)


def down_grad_kernel(sc, active, cot, own, far, total):
    total[...] = dot(active[...], cot[...], 0, 0).astype(BF16)
    own[...] = total[:, own_lanes(sc)]
    far[...] = total[:, far_lanes(sc)]


def run_down_grad(sc, active, cotangent):
    return pl.pallas_call(
        down_grad_kernel,
        grid_spec=pltpu.PrefetchScalarGridSpec(
            num_scalar_prefetch=1,
            grid=(FF // 512,),
            in_specs=[spec((ROWS, 512), lambda f, s: (0, f)), held((ROWS, WIDTH))],
            out_specs=[spec((512, SIDE), lambda f, s: (f, 0))] * 2,
            scratch_shapes=[pltpu.VMEM((512, WIDTH), BF16)],
        ),
        out_shape=[jax.ShapeDtypeStruct((FF, SIDE), BF16)] * 2,
        compiler_params=params(48),
        cost_estimate=pl.CostEstimate(
            flops=2 * ROWS * WIDTH * FF, bytes_accessed=2 * ROWS * (WIDTH + FF), transcendentals=0
        ),
        name="down_grad",
    )(sc, active, cotangent.reshape(ROWS, WIDTH))


def up_grad_kernel(sc, normed, up_grad, own, far):
    total = dot(normed[...], up_grad[...], 0, 0).astype(BF16)

    @pl.when(pl.program_id(0) < FSIDE)
    def _():
        own[...] = total

    @pl.when(pl.program_id(0) >= FSIDE)
    def _():
        far[...] = total


def run_up_grad(sc, normed, up_grad):
    return pl.pallas_call(
        up_grad_kernel,
        grid_spec=pltpu.PrefetchScalarGridSpec(
            num_scalar_prefetch=1,
            grid=(2 * FSIDE,),
            in_specs=[held((ROWS, WIDTH)), spec((ROWS, FSTEP), unit_columns)],
            out_specs=[spec((WIDTH, FSTEP), early), spec((WIDTH, FSTEP), late)],
        ),
        out_shape=[jax.ShapeDtypeStruct((WIDTH, FF // 2), BF16)] * 2,
        compiler_params=params(48),
        cost_estimate=pl.CostEstimate(
            flops=2 * ROWS * WIDTH * FF, bytes_accessed=2 * ROWS * (WIDTH + FF), transcendentals=0
        ),
        name="up_grad",
    )(sc, normed.reshape(ROWS, WIDTH), up_grad)


def out_kernel(sc, active, resid, dn_own, dn_far, own, far, w_down):
    step = pl.program_id(0)

    @pl.when(step == 0)
    def _():
        w_down[:, own_lanes(sc)] = dn_own[...]
        w_down[:, far_lanes(sc)] = dn_far[...]

    branch = dot(active[...].reshape(4 * SPAN, FF), w_down[...], 1, 0)
    output = jnp.where(row_valid(sc, step), resid[...].reshape(4 * SPAN, WIDTH) + branch, 0.0)
    output = output.reshape(4, SPAN, WIDTH)
    own[...] = output[:2]
    far[...] = output[2:].astype(BF16)


def run_out(sc, active, resid, down):
    return pl.pallas_call(
        out_kernel,
        grid_spec=pltpu.PrefetchScalarGridSpec(
            num_scalar_prefetch=1,
            grid=(HROWS // SPAN,),
            in_specs=[
                spec((4, SPAN, FF), lambda r, s: (0, r, 0)),
                slab_spec(),
                held((FF, SIDE)),
                held((FF, SIDE)),
            ],
            out_specs=[slab_spec(2)] * 2,
            scratch_shapes=[pltpu.VMEM((FF, WIDTH), BF16)],
        ),
        out_shape=[
            jax.ShapeDtypeStruct((2, HROWS, WIDTH), F32),
            jax.ShapeDtypeStruct((2, HROWS, WIDTH), BF16),
        ],
        compiler_params=params(48),
        cost_estimate=pl.CostEstimate(
            flops=2 * ROWS * WIDTH * FF, bytes_accessed=ROWS * (2 * FF + 7 * WIDTH), transcendentals=0
        ),
        name="out",
    )(sc, active.reshape(4, HROWS, FF), resid, *down)


def post_kernel(sc, resid, back, cot, mixed, wo_own, wo_far, gain, *refs):
    (res_own, res_far, heads, d_out_own, d_out_far, d_gain, weight, total, spread) = refs
    step = pl.program_id(0)
    whole_weight(sc, step, wo_own, wo_far, weight)
    shape, slab = (4 * SPAN, WIDTH), (4, SPAN, WIDTH)
    valid = row_valid(sc, step)
    res = resid[...].reshape(shape)
    scale = lax.rsqrt(jnp.mean(res * res, axis=-1, keepdims=True) + EPSILON)
    unit = res * scale
    two_grad = jnp.where(valid, back[...].reshape(shape), 0.0)
    gained = two_grad * gain[...]
    masked = cot[...].reshape(shape).astype(F32)
    grad = masked + scale * (gained - unit * jnp.mean(gained * unit, axis=-1, keepdims=True))
    low = grad.astype(BF16)
    res_own[...] = grad.reshape(slab)[:2]
    res_far[...] = low.reshape(slab)[2:]
    gain_sum = jnp.sum(two_grad * unit, axis=0, keepdims=True)
    out_sum = dot(mixed[...].reshape(shape), low, 0, 0)

    @pl.when(step == 0)
    def _():
        d_gain[...] = gain_sum
        total[...] = out_sum

    @pl.when(step > 0)
    def _():
        d_gain[...] += gain_sum
        total[...] += out_sum

    spread[...] = dot(low, weight[...], 1, 1).astype(BF16).reshape(slab)
    for pair in range(HEADS // 2):
        lanes = slice(pair * 128, (pair + 1) * 128)
        for side in range(2):
            one, two = spread[2 * side, :, lanes], spread[2 * side + 1, :, lanes]
            half = slice(side * 128, (side + 1) * 128)
            heads[2 * pair, :, half] = jnp.concatenate([one[:, :HEAD], two[:, :HEAD]], axis=1)
            heads[2 * pair + 1, :, half] = jnp.concatenate([one[:, HEAD:], two[:, HEAD:]], axis=1)

    @pl.when(step == pl.num_programs(0) - 1)
    def _():
        weight[...] = total[...].astype(BF16)
        d_out_own[...] = weight[:, own_lanes(sc)]
        d_out_far[...] = weight[:, far_lanes(sc)]


def run_post(sc, resid, back, cotangent, mixed, wo, gain):
    whole = (4, HROWS, WIDTH)
    return pl.pallas_call(
        post_kernel,
        grid_spec=pltpu.PrefetchScalarGridSpec(
            num_scalar_prefetch=1,
            grid=(HROWS // SPAN,),
            in_specs=[slab_spec()] * 4 + [held((WIDTH, SIDE)), held((WIDTH, SIDE)), held((1, WIDTH))],
            out_specs=[slab_spec(2)] * 2
            + [heads_spec(), held((WIDTH, SIDE)), held((WIDTH, SIDE)), held((1, WIDTH))],
            scratch_shapes=[
                pltpu.VMEM((WIDTH, WIDTH), BF16),
                pltpu.VMEM((WIDTH, WIDTH), F32),
                pltpu.VMEM((4, SPAN, WIDTH), BF16),
            ],
        ),
        out_shape=[
            jax.ShapeDtypeStruct((2, HROWS, WIDTH), F32),
            jax.ShapeDtypeStruct((2, HROWS, WIDTH), BF16),
            jax.ShapeDtypeStruct((HEADS, HROWS, 4 * HEAD), BF16),
            jax.ShapeDtypeStruct((WIDTH, SIDE), BF16),
            jax.ShapeDtypeStruct((WIDTH, SIDE), BF16),
            jax.ShapeDtypeStruct((1, WIDTH), F32),
        ],
        compiler_params=params(40),
        cost_estimate=pl.CostEstimate(
            flops=4 * ROWS * WIDTH * WIDTH, bytes_accessed=28 * ROWS * WIDTH, transcendentals=0
        ),
        name="post",
    )(sc, resid, back.reshape(whole), cotangent, mixed, *wo, gain)


def unmix_kernel(carried, sc, *refs):
    shards, (v_own, v_far, grad_heads, mean, *rest) = refs[:8], refs[8:]
    rest = rest[2:] if carried else rest
    outs, (own, far, raw, grads, mask, adder, bound, sems, out_sems) = rest[:8], rest[8:]
    place = sc[PLACE]
    step = pl.program_id(0)

    def leave(slot):
        return [
            pltpu.make_async_copy(
                grads.at[slot, pl.ds(pl.multiple_of((place ^ rel) * SUBS * HALF, SUBS * HALF), SUBS * HALF)],
                outs[4 * slot + rel],
                out_sems.at[slot, rel],
            )
            for rel in range(4)
        ]

    fill_mask(sc, mask)

    @pl.when(step == 0)
    def _():
        lane = lax.broadcasted_iota(jnp.int32, (4 * HEAD, 128), 0) // HEAD
        column = lax.broadcasted_iota(jnp.int32, (4 * HEAD, 128), 1)
        adder[...] = jnp.where((lane == column) | (lane + 4 == column), -1.0, 0.0).astype(BF16)
        row = lax.broadcasted_iota(jnp.int32, (LMAX, 128), 0)
        item = lax.broadcasted_iota(jnp.int32, (LMAX, 128), 1)
        length = jnp.where(item % 4 == 0, sc[LENGTHS], sc[LENGTHS + 1])
        length = jnp.where(item % 4 == 2, sc[LENGTHS + 2], length)
        length = jnp.where(item % 4 == 3, sc[LENGTHS + 3], length)
        bound[...] = jnp.where((item < 8) & (row < length), 1.0, 0.0).astype(BF16)

    slot = take_plane(place, shards, raw, sems)
    high_lanes = lax.broadcasted_iota(jnp.int32, (HROWS, 128), 1) < 4
    for head in range(PHEADS):
        weights = jnp.exp(raw[slot, head_rows(head)].astype(F32)).astype(BF16)
        low = (grad_heads[head].astype(F32) * inverse_sums(sc, weights, mask)).astype(BF16)
        product = low.astype(F32) * mean[head]
        coarse = product.astype(BF16)
        fine = (product - coarse.astype(F32)).astype(BF16)
        delta = dot(coarse, adder[...], 1, 0) + dot(fine, adder[...], 1, 0)
        coarse = delta.astype(BF16)
        fine = (delta - coarse.astype(F32)).astype(BF16)
        left = jnp.concatenate([low, jnp.where(high_lanes, coarse, fine)], axis=1)
        score = dot(left, jnp.concatenate([v_own[head], v_far[head], bound[...]], axis=1), 1, 1)
        grads[slot, head_rows(head)] = (score * weights.astype(F32)).astype(BF16)
        back = (dot(weights, low, 0, 0) * mask[...].astype(F32)).astype(BF16)
        own[head] = back[:, : 2 * HEAD]
        far[head] = back[:, 2 * HEAD :]
    for which in range(2):

        @pl.when(step == which)
        def _():
            for copy in leave(which):
                copy.start()
            if which == 1:
                for copy in leave(0) + leave(1):
                    copy.wait()


def run_unmix(sc, planes, shards, v_own, v_far, grad_heads, mean, carry):
    carry = list(carry)
    return pl.pallas_call(
        partial(unmix_kernel, bool(carry)),
        grid_spec=pltpu.PrefetchScalarGridSpec(
            num_scalar_prefetch=1,
            grid=(2,),
            in_specs=anywhere(8)
            + [plane_spec(planes, LMAX, 2 * HEAD)] * 2
            + [plane_spec(planes, HROWS, 4 * HEAD)] * 2
            + anywhere(len(carry)),
            out_specs=anywhere(8) + [plane_spec(planes, LMAX, 2 * HEAD)] * 2,
            scratch_shapes=[
                pltpu.VMEM((2, 4 * SUBS * HALF, LMAX), BF16),
                pltpu.VMEM((2, 4 * SUBS * HALF, LMAX), BF16),
                pltpu.VMEM((LMAX, 4 * HEAD), BF16),
                pltpu.VMEM((4 * HEAD, 128), BF16),
                pltpu.VMEM((LMAX, 128), BF16),
                pltpu.SemaphoreType.DMA((2, 4)),
                pltpu.SemaphoreType.DMA((2, 4)),
            ],
        ),
        out_shape=[jax.ShapeDtypeStruct((SUBS * HALF, LMAX), BF16)] * 8
        + [jax.ShapeDtypeStruct((HEADS, LMAX, 2 * HEAD), BF16)] * 2,
        input_output_aliases={13 + i: 8 + i for i in range(len(carry))},
        compiler_params=params(60),
        cost_estimate=pl.CostEstimate(
            flops=3 * HEADS * HROWS * LMAX * 4 * HEAD,
            bytes_accessed=HEADS * (2 * HROWS * LMAX + 4 * HROWS * 256 + 4 * LMAX * 256),
            transcendentals=HEADS * HROWS * LMAX // 2,
        ),
        name="unmix",
    )(sc, *shards, v_own, v_far, grad_heads, mean, *carry)


def close_kernel(sc, tok, res_own, res_got, out_own, out_got, own, far, gain, w_own, w_far, *refs):
    (output, tok_grad, d_value, d_gain, total, weight) = refs
    step = pl.program_id(0)
    whole_weight(sc, step, w_own, w_far, weight)
    core = sc[CORE]
    output[:, :, core] = out_own[...]
    output[:, :, 1 - core] = out_got[...].astype(F32)
    tok_grad[:, :, core] = res_own[...]
    tok_grad[:, :, 1 - core] = res_got[...].astype(F32)
    runs = tok.shape[1]
    rows = runs * 128
    for item in range(2):
        lanes = slice(item * HEAD, (item + 1) * HEAD)
        pieces = [
            add_low(own[head, :, lanes], far[head, :, lanes]) for head in range(HEADS)
        ]
        back = jnp.concatenate(pieces, axis=1)
        x = tok[item].reshape(rows, WIDTH).astype(F32)
        scale = lax.rsqrt(jnp.mean(x * x, axis=-1, keepdims=True) + EPSILON)
        unit = x * scale
        normed = (unit * gain[...]).astype(BF16)
        normed_grad = dot(back, weight[...], 1, 1)
        gained = normed_grad * gain[...]
        update = scale * (gained - unit * jnp.mean(gained * unit, axis=-1, keepdims=True))
        tok_grad[item] += update.reshape(runs, 2, HALF, WIDTH)
        gain_sum = jnp.sum(normed_grad * unit, axis=0, keepdims=True)
        value_sum = dot(normed, back, 0, 0)
        if item == 0:
            gain_total, value_total = gain_sum, value_sum
        else:
            gain_total, value_total = gain_total + gain_sum, value_total + value_sum

    @pl.when(step == 0)
    def _():
        d_gain[...] = gain_total
        total[...] = value_total

    @pl.when(step > 0)
    def _():
        d_gain[...] += gain_total
        total[...] += value_total

    @pl.when(step == pl.num_programs(0) - 1)
    def _():
        low = total[...].astype(BF16)
        d_value[0] = low[:, :SIDE]
        d_value[1] = low[:, SIDE:]


def run_close(sc, tokens, res_own, res_got, out_own, out_got, own, far, gain, w_own, w_far):
    runs = 2
    slab = (2, RUNS, 2, HALF, WIDTH)
    half = (2, RUNS, HALF, WIDTH)
    whole_spec = spec((2, runs, 2, HALF, WIDTH), lambda j, s: (0, j, 0, 0, 0))
    half_spec = spec((2, runs, HALF, WIDTH), lambda j, s: (0, j, 0, 0))
    back_spec = spec((HEADS, runs * 128, 2 * HEAD), lambda j, s: (0, j, 0))
    return pl.pallas_call(
        close_kernel,
        grid_spec=pltpu.PrefetchScalarGridSpec(
            num_scalar_prefetch=1,
            grid=(RUNS // runs,),
            in_specs=[whole_spec]
            + [half_spec] * 4
            + [back_spec, back_spec, held((1, WIDTH)), held((WIDTH, SIDE)), held((WIDTH, SIDE))],
            out_specs=[whole_spec, whole_spec, held((2, WIDTH, SIDE)), held((1, WIDTH))],
            scratch_shapes=[pltpu.VMEM((WIDTH, WIDTH), F32), pltpu.VMEM((WIDTH, WIDTH), BF16)],
        ),
        out_shape=[
            jax.ShapeDtypeStruct(slab, F32),
            jax.ShapeDtypeStruct(slab, F32),
            jax.ShapeDtypeStruct((2, WIDTH, SIDE), BF16),
            jax.ShapeDtypeStruct((1, WIDTH), F32),
        ],
        compiler_params=params(48),
        cost_estimate=pl.CostEstimate(
            flops=4 * 2 * LMAX * WIDTH * WIDTH, bytes_accessed=38 * LMAX * WIDTH, transcendentals=0
        ),
        name="close",
    )(
        sc,
        tokens.reshape(slab),
        *(x.reshape(half) for x in (res_own, res_got, out_own, out_got)),
        own,
        far,
        gain,
        w_own,
        w_far,
    )


PACK_DOWN, PACK_UP, PACK_OUT, PACK = 0, 192, 384, 432
SHARE = SUBS * HALF + 32


def chip_of(sc, k, rel):
    return plane_of(k, sc) * 4 + (sc[PLACE] ^ rel)


def place_kernel(moves, sc, *refs):
    pieces, targets, sems = refs[:16], refs[16:-1], refs[-1]
    copies = []
    for index, piece in enumerate(pieces):
        chip = chip_of(sc, index // 4, index % 4)
        for which, (start, count, lane, target, step, offset, column) in enumerate(moves):
            rows = pl.ds(pl.multiple_of(chip * step + offset, 16), count)
            copies.append(
                pltpu.make_async_copy(
                    piece.at[pl.ds(start, count), pl.ds(lane, SIDE)],
                    targets[target].at[rows, pl.ds(column, SIDE)],
                    sems.at[index, which],
                )
            )
    for copy in copies:
        copy.start()
    for copy in copies:
        copy.wait()


def run_place(sc, pieces, moves, shapes):
    return pl.pallas_call(
        partial(place_kernel, moves),
        grid_spec=pltpu.PrefetchScalarGridSpec(
            num_scalar_prefetch=1,
            grid=(1,),
            in_specs=anywhere(16),
            out_specs=[held(shape) for shape in shapes],
            scratch_shapes=[pltpu.SemaphoreType.DMA((16, len(moves)))],
        ),
        out_shape=[jax.ShapeDtypeStruct(shape, BF16) for shape in shapes],
        compiler_params=params(60),
        cost_estimate=pl.CostEstimate(
            flops=0, bytes_accessed=4 * sum(a * b for a, b in shapes), transcendentals=0
        ),
        name="place",
    )(sc, *pieces)


def place_values(sc, shares):
    start = SUBS * HALF
    moves = (
        (start, 32, 0, 0, 48, 0, 0),
        (start, 16, SIDE, 0, 48, 32, 0),
        (start + 16, 16, SIDE, 1, 16, 0, 0),
    )
    return run_place(sc, shares, moves, [(WIDTH, SIDE), (256, SIDE)])


def place_weights(sc, pieces):
    moves = (
        (PACK_DOWN, 192, 0, 0, 192, 0, 0),
        *((PACK_UP + 48 * j, 48, 0, 1, 48, 0, j * SIDE) for j in range(4)),
        (PACK_OUT, 48, 0, 2, 48, 0, 0),
    )
    return run_place(sc, pieces, moves, [(FF, SIDE), (WIDTH, FF // 2), (WIDTH, SIDE)])


def collect_kernel(sc, *refs):
    packed = refs[-1]
    for rel in range(4):
        down, down_got, up, up_got, out, out_got = refs[6 * rel : 6 * rel + 6]
        packed[rel, PACK_DOWN:PACK_UP] = add_low(down[...], down_got[...])
        for j in range(4):
            lanes = slice(j * SIDE, (j + 1) * SIDE)
            packed[rel, PACK_UP + 48 * j : PACK_UP + 48 * (j + 1)] = add_low(up[:, lanes], up_got[:, lanes])
        packed[rel, PACK_OUT:] = add_low(out[...], out_got[...])


def run_collect(sc, *sides):
    def rows(x, rel):
        return spec((x.shape[0] // 16, x.shape[1]), lambda k, s: (chip_of(s, k, rel), 0))

    return pl.pallas_call(
        collect_kernel,
        grid_spec=pltpu.PrefetchScalarGridSpec(
            num_scalar_prefetch=1,
            grid=(PLANES,),
            in_specs=[rows(x, rel) for rel in range(4) for x in sides],
            out_specs=spec((4, PACK, SIDE), lambda k, s: (k, 0, 0)),
        ),
        out_shape=jax.ShapeDtypeStruct((16, PACK, SIDE), BF16),
        compiler_params=params(32),
        cost_estimate=pl.CostEstimate(flops=0, bytes_accessed=3 * 16 * PACK * SIDE * 2, transcendentals=0),
        name="collect",
    )(sc, *(x for _ in range(4) for x in sides))


DEVICES = 32
TO_CORE, TO_X, TO_Y = 1, 2, 4


def swap(x, bit):
    return lax.ppermute(x, BOTH, [(d, d ^ bit) for d in range(DEVICES)])


def ring(x, way=1):
    return lax.ppermute(x, BOTH, [(d, (d + 8 * way) % DEVICES) for d in range(DEVICES)])


def pick(x, index, axis=0):
    return lax.dynamic_index_in_dim(x, index, axis, keepdims=False)


def ordered(flag, one, two, axis=0, joined=jnp.stack):
    return jnp.where(flag == 0, joined([one, two], axis), joined([two, one], axis))


def add_low(one, two):
    return (one.astype(F32) + two.astype(F32)).astype(BF16)


STEPS = (
    ((0, 0, 1), (0, 1, 0), (1, 0, 0)),
    ((1, 0, 1), (0, 1, 1), (2, 0, 0)),
    ((2, 0, 1), (1, 1, 0), (3, 0, 0)),
    ((3, 0, 1), (2, 1, 0), (1, 1, 1)),
    ((2, 1, 1), (3, 1, 1), (3, 1, 0)),
)


def gather16(own, works=(), made=()):
    have = {(0, 0, 0): own}
    for step, (by_x, by_y, by_z) in enumerate(STEPS):
        got = {
            by_z: ring(have[by_z[0] - 1, by_z[1], by_z[2]]),
            by_x: swap(have[by_x[0], by_x[1], 0], TO_X),
            by_y: swap(have[by_y[0], 0, by_y[2]], TO_Y),
        }
        if step < len(works):
            made = works[step](made)
        have, made = lax.optimization_barrier(({**have, **got}, made))
    return [have[k, y, x] for k in range(4) for y in range(2) for x in range(2)], made


def scatter16(shares, works=(), made=()):
    have = {}

    def put(planes, values):
        for index, value in enumerate(values):
            have[planes[index // 4], index // 2 % 2, index % 2] = value

    put((0, 1, 2, 3) if len(shares) == 16 else (3, 2), shares)
    for step, (by_x, by_y, by_z) in enumerate(reversed(STEPS)):
        got = [
            ((by_z[0] - 1, by_z[1], by_z[2]), ring(have[by_z], -1)),
            ((by_x[0], by_x[1], 0), swap(have[by_x], TO_X)),
            ((by_y[0], 0, by_y[2]), swap(have[by_y], TO_Y)),
        ]
        for at in (by_x, by_y, by_z):
            del have[at]
        if step < len(works):
            made = works[step](made)
        values, have, made = lax.optimization_barrier(([value for _, value in got], have, made))
        if step == 0 and len(shares) == 8:
            put((1, 0), made[0])
        for at in dict.fromkeys(at for at, _ in got):
            total = have[at].astype(F32)
            for (target, _), value in zip(got, values):
                if target == at:
                    total = total + value.astype(F32)
            have[at] = total if step == len(STEPS) - 1 else total.astype(BF16)
    return have[0, 0, 0], made


def after(x, *others):
    return lax.optimization_barrier((x, others))[0]


def chip_shards(tokens, lengths, rand_mix, w_value, w_out, w_up, w_down, gain_mix, gain_ffn, grad_out):
    wide = lax.axis_index("wide")
    core = lax.axis_index("narrow")
    z, y, x = wide // 4, (wide // 2) % 2, wide % 2
    other = lambda value: swap(value, TO_CORE)
    side = partial(ordered, core, joined=jnp.concatenate)

    gains = jnp.pad(jnp.concatenate([gain_mix, gain_ffn])[None], ((0, 7), (0, SIDE - 48)))
    halves = [
        jnp.concatenate(
            [
                w_value[:, c * SIDE : (c + 1) * SIDE],
                gains,
                w_down[:, c * SIDE : (c + 1) * SIDE],
                *[w_up[:, (4 * c + j) * SIDE : (4 * c + j + 1) * SIDE] for j in range(4)],
                w_out[:, c * SIDE : (c + 1) * SIDE],
            ]
        )
        for c in range(2)
    ]
    both = jnp.stack(halves)
    joined = ordered(core, pick(both, core), other(pick(both, 1 - core)))
    part_of = lambda start, rows: joined[:, start : start + rows].reshape(2 * rows, SIDE)
    up_rows = joined[:, 128:224].reshape(2, 4, 24, SIDE).transpose(1, 0, 2, 3).reshape(192, SIDE)
    packed = jnp.concatenate([part_of(32, 96), up_rows, part_of(224, 24)])
    first = jnp.concatenate([part_of(0, 24), part_of(24, 8)])
    first = jnp.pad(jnp.concatenate([first[:32], first[32:]], axis=1), ((0, 0), (0, LMAX - WIDTH)))
    rand = rand_mix.reshape(3, 2, HALF, LMAX)
    blocks = side(pick(rand, core, 1), other(pick(rand, 1 - core, 1)), 0)
    share = jnp.concatenate([blocks.reshape(SUBS * HALF, LMAX), first])
    share, packed = lax.optimization_barrier((share, packed))

    slab = (2, RUNS, 2, HALF, WIDTH)
    tokens, grad_out = tokens.reshape(slab), grad_out.reshape(slab)

    def from_other(_):
        return other(lengths), other(pick(tokens, 1 - core, 2)), other(pick(grad_out, 1 - core, 2))

    shares, (far_lengths, tokens_far, grad_far) = gather16(share, [from_other])
    sc = jnp.concatenate([jnp.stack([core, z, wide % 4]).astype(jnp.int32), lengths, far_lengths])

    def make_values(_):
        value, gain_rows = place_values(sc, shares)
        value_far = other(value)
        gain_rows = gain_rows.reshape(16, 2, 8, SIDE)[:, :, 0]
        gain_one = gain_rows[..., :24].reshape(1, WIDTH).astype(F32)
        gain_two = gain_rows[..., 24:48].reshape(1, WIDTH).astype(F32)
        v_own = run_values(sc, tokens.reshape(2, LMAX, WIDTH), gain_one, value, value_far)
        return value, value_far, gain_one, gain_two, v_own

    def share_values(made):
        return *made, other(made[-1])

    def mix_near(made):
        return *made, run_mix(sc, (0, 1), shares[:8], made[-2], made[-1], ())

    def mix_far(made):
        *made, near = made
        return *made, run_mix(sc, (2, 3), shares[8:], made[-2], made[-1], near)

    pieces, made = gather16(after(packed, *shares[-3:]), [make_values, share_values, mix_near, mix_far])
    value, value_far, gain_one, gain_two, v_own, v_far, (heads, mean) = made
    down, up, out = place_weights(sc, pieces)
    down, up, out = (down, other(down)), (up, other(up)), (out, other(out))

    mixed, resid, normed, masked = run_pre(sc, tokens, tokens_far, grad_out, grad_far, heads, out, gain_two)
    active, up_grad, back = run_units(sc, normed, masked, up, down)
    res_own, res_far, grad_heads, d_out_own, d_out_far, d_gain_two = run_post(
        sc, resid, back, masked, mixed, out, gain_two
    )
    *far, back_own, back_far = run_unmix(
        sc, (3, 2), shares[12:] + shares[8:12], v_own, v_far, grad_heads, mean, ()
    )

    def unmix_near(_):
        *near, own, far = run_unmix(
            sc, (1, 0), shares[4:8] + shares[:4], v_own, v_far, grad_heads, mean, (back_own, back_far)
        )
        return near, own, far, other(res_far), other(d_out_far)

    def make_down(made):
        near, own, far, *rest = made
        return near, own, other(far), *rest, *run_down_grad(sc, active, masked)

    def make_up(made):
        *rest, down_own, down_far = made
        return *rest, down_own, other(down_far), *run_up_grad(sc, normed, up_grad)

    def share_up(made):
        *rest, up_far = made
        return *rest, other(up_far)

    def pack(made):
        _, own, got, res_got, d_out_got, *sides = made
        return own, got, res_got, run_collect(sc, *sides, d_out_own, d_out_got)

    rand_sum, made = scatter16(far, [unmix_near, make_down, make_up, share_up, pack])
    back_own, back_got, res_got, packed = made

    def make_output(_):
        out_own, out_far = run_out(sc, active, resid, down)
        blocks = rand_sum.reshape(2, 3, HALF, LMAX)
        return pick(blocks, core), other(pick(blocks, 1 - core)), out_own, other(out_far)

    def finish(made):
        *blocks, out_own, out_got = made
        output, tokens_grad, d_value, d_gain_one = run_close(
            sc, tokens, res_own, res_got, out_own, out_got, back_own, back_got, gain_one, value, value_far
        )
        gain_pair = jnp.concatenate([d_gain_one, d_gain_two]).reshape(2, 16, 1, 48).astype(BF16)
        gain_pair = jnp.pad(gain_pair, ((0, 0), (0, 0), (0, 15), (0, SIDE - 48)))
        small = jnp.concatenate([d_value.reshape(2, 16, 48, SIDE), gain_pair], 2)
        small = add_low(pick(small, core), other(pick(small, 1 - core))).reshape(4, 2, 2, 64, SIDE)
        return *blocks, output, tokens_grad, small

    def small_line(made):
        *kept, small = made
        return *kept, add_low(pick(small, x, 2), swap(pick(small, 1 - x, 2), TO_X))

    def small_plane(made):
        *kept, small = made
        return *kept, add_low(pick(small, y, 1), swap(pick(small, 1 - y, 1), TO_Y))

    def small_planes(made):
        *kept, small = made
        total = pick(small, z).astype(F32)
        for k in range(1, PLANES):
            total = total + ring(pick(small, lax.rem(z + PLANES - k, PLANES)), -k).astype(F32)
        return *kept, total

    big_sum, made = scatter16(
        after([packed[i] for i in range(16)], rand_sum), [make_output, finish, small_line, small_plane, small_planes]
    )
    blocks, blocks_far, output, tokens_grad, small_sum = made
    big_far, small_far = other(big_sum), other(small_sum)

    rows_of = lambda value, rows: pick(value.reshape(-1, 2, rows, SIDE), core, 1)
    mine = lambda own, far, rows: side(rows_of(own, rows)[0], rows_of(far, rows)[0], 1)
    down_shard = mine(big_sum[PACK_DOWN:PACK_UP], big_far[PACK_DOWN:PACK_UP], 96)
    up_side = lambda value: rows_of(value[PACK_UP:PACK_OUT], 24).transpose(1, 0, 2).reshape(24, 4 * SIDE)
    up_shard = side(up_side(big_sum), up_side(big_far), 1)
    outproj_shard = mine(big_sum[PACK_OUT:], big_far[PACK_OUT:], 24)
    value_shard = mine(small_sum[:48], small_far[:48], 24)
    gains_pair = ordered(core, small_sum[48, :48], small_far[48, :48])
    gain_pair = pick(gains_pair.reshape(2, 2, 24), core, 1)

    rand_shard = ordered(core, blocks, blocks_far, 1)

    return (
        output.reshape(2, LMAX, WIDTH),
        tokens_grad.reshape(2, LMAX, WIDTH),
        rand_shard.reshape(3 * 128, LMAX),
        value_shard,
        outproj_shard,
        up_shard,
        down_shard,
        gain_pair[0],
        gain_pair[1],
    )


def rms_norm(values, gain):
    scale = lax.rsqrt(jnp.mean(values * values, axis=-1, keepdims=True) + EPSILON)
    return values * scale * gain


def split_heads(block):
    return block.reshape(LMAX, HEADS, HEAD).transpose(1, 0, 2)


def merge_heads(block):
    return block.transpose(1, 0, 2).reshape(LMAX, HEADS * HEAD)


def masked_scores(key_mask, rand_head):
    return jnp.where(key_mask[None, :] > 0, rand_head.astype(jnp.float32), -1e30)


def head_forward(key_mask, paired):
    rand_head, value_head = paired
    scores = masked_scores(key_mask, rand_head)
    row_peak = jnp.max(scores, axis=-1, keepdims=True)
    exponent = jnp.exp(scores - row_peak)
    denom_sum = jnp.sum(exponent, axis=-1, keepdims=True)
    attention = exponent / denom_sum * key_mask[:, None]
    mixed = jnp.dot(attention.astype(jnp.bfloat16), value_head, preferred_element_type=jnp.float32)
    return (mixed.astype(jnp.bfloat16), row_peak + jnp.log(denom_sum))


def head_backward(key_mask, paired):
    rand_head, value_head, mix_grad, log_total = paired
    scores = masked_scores(key_mask, rand_head)
    attention = jnp.exp(scores - log_total) * key_mask[:, None]
    prob_grad = jnp.einsum("id,jd->ij", mix_grad, value_head, preferred_element_type=jnp.float32)
    value_grad = jnp.einsum(
        "ij,id->jd", attention.astype(jnp.bfloat16), mix_grad, preferred_element_type=jnp.float32
    )
    score_grad = attention * (prob_grad - jnp.sum(prob_grad * attention, axis=-1, keepdims=True))
    return (score_grad, value_grad)


def shards(tokens, lengths, rand_mix, w_value, w_out, w_up, w_down, gain_mix, gain_ffn, grad_out):
    item_count = tokens.shape[0]
    width = tokens.shape[2]
    row_count = item_count * LMAX
    tokens_flat = tokens.reshape(row_count, width).astype(jnp.float32)
    positions = jnp.arange(LMAX, dtype=jnp.int32)
    valid_table = (positions[None, :] < lengths[:, None]).astype(jnp.float32)
    row_valid = valid_table.reshape(row_count, 1)
    forward_set = (
        lax.all_gather(rand_mix, ("wide", "narrow"), axis=0, tiled=True),
        lax.all_gather(w_value, ("wide", "narrow"), axis=0, tiled=True),
        lax.all_gather(w_out, ("wide", "narrow"), axis=0, tiled=True),
        lax.all_gather(w_up, ("wide", "narrow"), axis=0, tiled=True),
        lax.all_gather(w_down, ("wide", "narrow"), axis=0, tiled=True),
        lax.all_gather(gain_mix, ("wide", "narrow"), axis=0, tiled=True),
        lax.all_gather(gain_ffn, ("wide", "narrow"), axis=0, tiled=True),
    )
    rand_all, value_all, out_all, up_all, down_all, gain_first, gain_second = forward_set
    normed = rms_norm(tokens_flat, gain_first.astype(jnp.float32)).astype(jnp.bfloat16)
    values = jnp.dot(normed, value_all, preferred_element_type=jnp.float32).astype(jnp.bfloat16)
    rand_heads = rand_all.reshape(HEADS, LMAX, LMAX)
    mixed_parts = []
    totals_kept = []
    for item_index in range(item_count):
        item_values = split_heads(values[item_index * LMAX : (item_index + 1) * LMAX])
        mixed_heads, log_total = lax.map(
            partial(head_forward, valid_table[item_index]), (rand_heads, item_values)
        )
        mixed_parts.append(merge_heads(mixed_heads))
        totals_kept.append(log_total)
    mixed = jnp.concatenate(mixed_parts, axis=0)
    residual = tokens_flat + jnp.dot(mixed, out_all, preferred_element_type=jnp.float32)
    normed_two = rms_norm(residual, gain_second.astype(jnp.float32)).astype(jnp.bfloat16)
    up_proj = jnp.dot(normed_two, up_all, preferred_element_type=jnp.float32)
    active = jax.nn.gelu(up_proj).astype(jnp.bfloat16)
    branch = jnp.dot(active, down_all, preferred_element_type=jnp.float32)
    output = row_valid * (residual + branch)
    back_set = (
        lax.all_gather(rand_mix, ("wide", "narrow"), axis=0, tiled=True),
        lax.all_gather(w_value, ("wide", "narrow"), axis=0, tiled=True),
        lax.all_gather(w_out, ("wide", "narrow"), axis=0, tiled=True),
        lax.all_gather(w_up, ("wide", "narrow"), axis=0, tiled=True),
        lax.all_gather(w_down, ("wide", "narrow"), axis=0, tiled=True),
        lax.all_gather(gain_mix, ("wide", "narrow"), axis=0, tiled=True),
        lax.all_gather(gain_ffn, ("wide", "narrow"), axis=0, tiled=True),
    )
    rand_back, value_back, out_back, up_back, down_back, gain_back_one, gain_back_two = back_set
    cotangent = grad_out.reshape(row_count, width).astype(jnp.float32)
    masked = row_valid * cotangent
    branch_grad = masked.astype(jnp.bfloat16)
    grad_down = jnp.einsum("rk,rd->kd", active, branch_grad, preferred_element_type=jnp.float32)
    active_grad = jnp.einsum(
        "rd,kd->rk", branch_grad, down_back, preferred_element_type=jnp.float32
    )
    gelu_value, gelu_pull = jax.vjp(jax.nn.gelu, up_proj)
    up_grad = gelu_pull(active_grad)[0].astype(jnp.bfloat16)
    grad_up = jnp.einsum("rd,rk->dk", normed_two, up_grad, preferred_element_type=jnp.float32)
    normed_two_grad = jnp.einsum("rk,dk->rd", up_grad, up_back, preferred_element_type=jnp.float32)
    norm_value, norm_pull = jax.vjp(rms_norm, residual, gain_back_two.astype(jnp.float32))
    residual_part, gain_two_grad = norm_pull(normed_two_grad)
    residual_grad = masked + residual_part
    attn_grad = residual_grad.astype(jnp.bfloat16)
    grad_outproj = jnp.einsum("rd,re->de", mixed, attn_grad, preferred_element_type=jnp.float32)
    mixed_grad = jnp.einsum(
        "re,de->rd", attn_grad, out_back, preferred_element_type=jnp.float32
    ).astype(jnp.bfloat16)
    rand_heads_back = rand_back.reshape(HEADS, LMAX, LMAX)
    rand_grad = jnp.zeros((HEADS, LMAX, LMAX), jnp.float32)
    value_parts = []
    for item_index in range(item_count):
        lower_row = item_index * LMAX
        upper_row = lower_row + LMAX
        item_values = split_heads(values[lower_row:upper_row])
        item_mix_grad = split_heads(mixed_grad[lower_row:upper_row])
        score_grad, value_grad = lax.map(
            partial(head_backward, valid_table[item_index]),
            (rand_heads_back, item_values, item_mix_grad, totals_kept[item_index]),
        )
        rand_grad = rand_grad + score_grad
        value_parts.append(merge_heads(value_grad))
    values_grad = jnp.concatenate(value_parts, axis=0).astype(jnp.bfloat16)
    grad_value = jnp.einsum("rd,re->de", normed, values_grad, preferred_element_type=jnp.float32)
    normed_grad = jnp.einsum(
        "re,de->rd", values_grad, value_back, preferred_element_type=jnp.float32
    )
    norm_first, first_pull = jax.vjp(rms_norm, tokens_flat, gain_back_one.astype(jnp.float32))
    token_part, gain_one_grad = first_pull(normed_grad)
    tokens_grad = residual_grad + token_part
    rand_flat = rand_grad.reshape(HEADS * LMAX, LMAX)
    all_shards = (
        lax.psum_scatter(rand_flat, ("wide", "narrow"), scatter_dimension=0, tiled=True),
        lax.psum_scatter(grad_value, ("wide", "narrow"), scatter_dimension=0, tiled=True),
        lax.psum_scatter(grad_outproj, ("wide", "narrow"), scatter_dimension=0, tiled=True),
        lax.psum_scatter(grad_up, ("wide", "narrow"), scatter_dimension=0, tiled=True),
        lax.psum_scatter(grad_down, ("wide", "narrow"), scatter_dimension=0, tiled=True),
        lax.psum_scatter(gain_one_grad, ("wide", "narrow"), scatter_dimension=0, tiled=True),
        lax.psum_scatter(gain_two_grad, ("wide", "narrow"), scatter_dimension=0, tiled=True),
    )
    rand_shard, value_shard, outproj_shard, up_shard, down_shard, gain_one_shard, gain_two_shard = (
        all_shards
    )
    return (
        output.reshape(item_count, LMAX, width),
        tokens_grad.reshape(item_count, LMAX, width),
        rand_shard,
        value_shard,
        outproj_shard,
        up_shard,
        down_shard,
        gain_one_shard,
        gain_two_shard,
    )


def solution(mesh):
    in_specs = (
        P(("wide", "narrow"), None, None),
        P(("wide", "narrow")),
        P(("wide", "narrow"), None),
        P(("wide", "narrow"), None),
        P(("wide", "narrow"), None),
        P(("wide", "narrow"), None),
        P(("wide", "narrow"), None),
        P(("wide", "narrow")),
        P(("wide", "narrow")),
        P(("wide", "narrow"), None, None),
    )
    out_specs = (
        P(("wide", "narrow"), None, None),
        P(("wide", "narrow"), None, None),
        P(("wide", "narrow"), None),
        P(("wide", "narrow"), None),
        P(("wide", "narrow"), None),
        P(("wide", "narrow"), None),
        P(("wide", "narrow"), None),
        P(("wide", "narrow")),
        P(("wide", "narrow")),
    )
    fits = dict(mesh.shape) == {"wide": 16, "narrow": 2}
    return jax.shard_map(chip_shards if fits else shards, mesh=mesh, in_specs=in_specs, out_specs=out_specs, check_vma=False)
```

```python
from functools import partial

import jax
import jax.numpy as jnp
from jax import lax
from jax.experimental import pallas as pl
from jax.experimental.pallas import tpu as pltpu
from jax.sharding import PartitionSpec as P

HEADS = 12
HEAD = 64
LMAX = 1024
WIDTH = 768
FF = 3072
EPSILON = 1e-05

BOTH = ("wide", "narrow")
BF16 = jnp.bfloat16
F32 = jnp.float32
VMEM = 61 << 20

SUBS = 6
RUNS = 8
HALF = 64
HROWS = RUNS * HALF
PLANES = 4
PHEADS = HEADS // PLANES
ROWS = 2 * LMAX
FSTEP = 768
FSIDE = FF // 2 // FSTEP
TILE = 512
SIDE = WIDTH // 2
SPAN = 2 * HALF


def dot(a, b, ca, cb):
    return lax.dot_general(a, b, (((ca,), (cb,)), ((), ())), preferred_element_type=F32)


CORE, PLANE, PLACE, LENGTHS = 0, 1, 2, 3


def spec(shape, index):
    return pl.BlockSpec(shape, index)


def held(shape):
    zeros = (0,) * len(shape)
    return pl.BlockSpec(shape, lambda *_: zeros, pipeline_mode=pl.Buffered(1))


def params(limit):
    return pltpu.CompilerParams(vmem_limit_bytes=limit)


def whole_weight(sc, step, own, far, weight):
    @pl.when(step == 0)
    def _():
        weight[:, pl.ds(pl.multiple_of(sc[CORE] * SIDE, 128), SIDE)] = own[...]
        weight[:, pl.ds(pl.multiple_of((1 - sc[CORE]) * SIDE, 128), SIDE)] = far[...]


def values_kernel(sc, tok, gain, w_own, w_far, out, weight):
    step = pl.program_id(0)
    whole_weight(sc, step, w_own, w_far, weight)
    rows = tok.shape[1]
    position = step * rows + lax.broadcasted_iota(jnp.int32, (rows, 1), 0)
    for item in range(2):
        x = tok[item].astype(F32)
        scale = lax.rsqrt(jnp.mean(x * x, axis=-1, keepdims=True) + EPSILON)
        normed = (x * scale * gain[...]).astype(BF16)
        found = dot(normed, weight[...], 1, 0)
        found = jnp.where(position < sc[LENGTHS + item], found, 0.0).astype(BF16)
        for head in range(HEADS):
            out[head, :, item * HEAD : (item + 1) * HEAD] = found[:, head * HEAD : (head + 1) * HEAD]


def run_values(sc, tokens, gain, w_own, w_far):
    rows = 256
    return pl.pallas_call(
        values_kernel,
        grid_spec=pltpu.PrefetchScalarGridSpec(
            num_scalar_prefetch=1,
            grid=(LMAX // rows,),
            in_specs=[
                spec((2, rows, WIDTH), lambda j, s: (0, j, 0)),
                held((1, WIDTH)),
                held((WIDTH, SIDE)),
                held((WIDTH, SIDE)),
            ],
            out_specs=spec((HEADS, rows, 2 * HEAD), lambda j, s: (0, j, 0)),
            scratch_shapes=[pltpu.VMEM((WIDTH, WIDTH), BF16)],
        ),
        out_shape=jax.ShapeDtypeStruct((HEADS, LMAX, 2 * HEAD), BF16),
        compiler_params=params(VMEM),
        cost_estimate=pl.CostEstimate(
            flops=2 * 2 * LMAX * WIDTH * WIDTH, bytes_accessed=8 * LMAX * WIDTH, transcendentals=0
        ),
        name="values",
    )(sc, tokens, gain, w_own, w_far)


def lane_lengths(sc, shape):
    slot = lax.broadcasted_iota(jnp.int32, shape, 1) // HEAD
    length = jnp.where(slot == 0, sc[LENGTHS], sc[LENGTHS + 1])
    return jnp.where(slot >= 2, jnp.where(slot == 2, sc[LENGTHS + 2], sc[LENGTHS + 3]), length)


def plane_of(k, sc):
    return lax.rem(sc[PLANE] + PLANES - k, PLANES)


def plane_spec(planes, rows, lanes):
    def index(step, sc):
        return (plane_of(planes[0] + step * (planes[1] - planes[0]), sc), 0, 0)

    return spec((PHEADS, rows, lanes), index)


def anywhere(count):
    return [pl.BlockSpec(memory_space=pl.ANY)] * count


def plane_fetch(place, shards, raw, sems, slot):
    return [
        pltpu.make_async_copy(
            shards[4 * slot + rel],
            raw.at[slot, pl.ds(pl.multiple_of((place ^ rel) * SUBS * HALF, SUBS * HALF), SUBS * HALF)],
            sems.at[slot, rel],
        )
        for rel in range(4)
    ]


def take_plane(place, shards, raw, sems):
    step = pl.program_id(0)

    @pl.when(step == 0)
    def _():
        for slot in range(2):
            for copy in plane_fetch(place, shards, raw, sems, slot):
                copy.start()

    for slot in range(2):

        @pl.when(step == slot)
        def _():
            for copy in plane_fetch(place, shards, raw, sems, slot):
                copy.wait()

    return step


def head_rows(head):
    return slice(head * HROWS, (head + 1) * HROWS)


def fill_mask(sc, mask):
    @pl.when(pl.program_id(0) == 0)
    def _():
        shape = (LMAX, 4 * HEAD)
        column = lax.broadcasted_iota(jnp.int32, shape, 0)
        mask[...] = (column < lane_lengths(sc, shape)).astype(F32).astype(BF16)


def inverse_sums(sc, weights, mask):
    shape = (HROWS, 4 * HEAD)
    line = lax.broadcasted_iota(jnp.int32, shape, 0)
    position = 128 * (line // HALF) + HALF * sc[CORE] + line % HALF
    return jnp.where(position < lane_lengths(sc, shape), 1.0 / dot(weights, mask[...], 1, 0), 0.0)


def mix_kernel(carried, sc, *refs):
    shards, (v_own, v_far, *rest) = refs[:8], refs[8:]
    mixed, mean, raw, mask, sems = rest[2:] if carried else rest
    fill_mask(sc, mask)
    slot = take_plane(sc[PLACE], shards, raw, sems)
    for head in range(PHEADS):
        weights = jnp.exp(raw[slot, head_rows(head)].astype(F32)).astype(BF16)
        values = jnp.concatenate([v_own[head], v_far[head]], axis=1)
        found = dot(weights, values, 1, 0) * inverse_sums(sc, weights, mask)
        mean[head] = found
        mixed[head] = found.astype(BF16)


def run_mix(sc, planes, shards, v_own, v_far, carry):
    carry = list(carry)
    return pl.pallas_call(
        partial(mix_kernel, bool(carry)),
        grid_spec=pltpu.PrefetchScalarGridSpec(
            num_scalar_prefetch=1,
            grid=(2,),
            in_specs=anywhere(8) + [plane_spec(planes, LMAX, 2 * HEAD)] * 2 + anywhere(len(carry)),
            out_specs=[plane_spec(planes, HROWS, 4 * HEAD)] * 2,
            scratch_shapes=[
                pltpu.VMEM((2, 4 * SUBS * HALF, LMAX), BF16),
                pltpu.VMEM((LMAX, 4 * HEAD), BF16),
                pltpu.SemaphoreType.DMA((2, 4)),
            ],
        ),
        out_shape=[
            jax.ShapeDtypeStruct((HEADS, HROWS, 4 * HEAD), BF16),
            jax.ShapeDtypeStruct((HEADS, HROWS, 4 * HEAD), F32),
        ],
        input_output_aliases={11 + i: i for i in range(len(carry))},
        compiler_params=params(VMEM),
        cost_estimate=pl.CostEstimate(
            flops=2 * HEADS * HROWS * LMAX * 4 * HEAD,
            bytes_accessed=HEADS * (HROWS * LMAX + 5 * HROWS * 256),
            transcendentals=HEADS * HROWS * LMAX // 2,
        ),
        name="mix",
    )(sc, *shards, v_own, v_far, *carry)


def row_valid(sc, step):
    line = lax.broadcasted_iota(jnp.int32, (4 * SPAN, 1), 0)
    item = line // SPAN
    row = step * SPAN + line % SPAN
    low = jnp.where(item == 0, sc[LENGTHS], sc[LENGTHS + 1])
    high = jnp.where(item == 2, sc[LENGTHS + 2], sc[LENGTHS + 3])
    return 128 * (row // HALF) + HALF * sc[CORE] + row % HALF < jnp.where(item >= 2, high, low)


def four_items(own, far):
    return jnp.concatenate([own[:, :, 0], far[...]], axis=0).reshape(4 * SPAN, WIDTH)


def pre_kernel(sc, tok, tok_far, cot, cot_far, heads, wo_own, wo_far, gain, mixed, resid, normed, grad, weight):
    step = pl.program_id(0)
    whole_weight(sc, step, wo_own, wo_far, weight)
    for item in range(4):
        lanes = slice(item * HEAD, (item + 1) * HEAD)
        for pair in range(HEADS // 2):
            both = jnp.concatenate([heads[2 * pair, :, lanes], heads[2 * pair + 1, :, lanes]], axis=1)
            mixed[item, :, pair * 128 : (pair + 1) * 128] = both
    res = four_items(tok, tok_far).astype(F32) + dot(mixed[...].reshape(4 * SPAN, WIDTH), weight[...], 1, 0)
    resid[...] = res.reshape(4, SPAN, WIDTH)
    scale = lax.rsqrt(jnp.mean(res * res, axis=-1, keepdims=True) + EPSILON)
    valid = row_valid(sc, step)
    normed[...] = jnp.where(valid, res * scale * gain[...], 0.0).astype(BF16).reshape(4, SPAN, WIDTH)
    masked = jnp.where(valid, four_items(cot, cot_far).astype(F32), 0.0)
    grad[...] = masked.astype(BF16).reshape(4, SPAN, WIDTH)


def slab_spec(items=4):
    return spec((items, SPAN, WIDTH), lambda r, s: (0, r, 0))


def half_specs():
    return [
        spec((2, SPAN // HALF, 1, HALF, WIDTH), lambda r, s: (0, r, s[CORE], 0, 0)),
        spec((2, SPAN // HALF, HALF, WIDTH), lambda r, s: (0, r, 0, 0)),
    ]


def heads_spec():
    return spec((HEADS, SPAN, 4 * HEAD), lambda r, s: (0, r, 0))


def run_pre(sc, tokens, tokens_far, cotangent, cotangent_far, heads, wo, gain):
    return pl.pallas_call(
        pre_kernel,
        grid_spec=pltpu.PrefetchScalarGridSpec(
            num_scalar_prefetch=1,
            grid=(HROWS // SPAN,),
            in_specs=half_specs()
            + half_specs()
            + [heads_spec(), held((WIDTH, SIDE)), held((WIDTH, SIDE)), held((1, WIDTH))],
            out_specs=[slab_spec()] * 4,
            scratch_shapes=[pltpu.VMEM((WIDTH, WIDTH), BF16)],
        ),
        out_shape=[
            jax.ShapeDtypeStruct((4, HROWS, WIDTH), BF16),
            jax.ShapeDtypeStruct((4, HROWS, WIDTH), F32),
            jax.ShapeDtypeStruct((4, HROWS, WIDTH), BF16),
            jax.ShapeDtypeStruct((4, HROWS, WIDTH), BF16),
        ],
        compiler_params=params(VMEM),
        cost_estimate=pl.CostEstimate(
            flops=2 * ROWS * WIDTH * WIDTH, bytes_accessed=16 * ROWS * WIDTH, transcendentals=0
        ),
        name="pre",
    )(sc, tokens, tokens_far, cotangent, cotangent_far, heads, *wo, gain)


def own_lanes(sc):
    return pl.ds(pl.multiple_of(sc[CORE] * SIDE, 128), SIDE)


def far_lanes(sc):
    return pl.ds(pl.multiple_of((1 - sc[CORE]) * SIDE, 128), SIDE)


def unit_rows(f, sc):
    return (lax.rem(FSIDE * sc[CORE] + f, 2 * FSIDE), 0)


def unit_columns(f, sc):
    return (0, lax.rem(FSIDE * sc[CORE] + f, 2 * FSIDE))


def early(f, sc):
    return (0, lax.min(f, FSIDE - 1))


def late(f, sc):
    return (0, lax.max(f - FSIDE, 0))


def units_kernel(sc, normed, cot, up_own, up_far, dn_own, dn_far, active, up_grad, back, w_up, w_down):
    step = pl.program_id(0)
    w_down[:, own_lanes(sc)] = dn_own[...]
    w_down[:, far_lanes(sc)] = dn_far[...]

    @pl.when(step < FSIDE)
    def _():
        w_up[...] = up_own[...]

    @pl.when(step >= FSIDE)
    def _():
        w_up[...] = up_far[...]

    for piece in range(ROWS // TILE):
        rows = slice(piece * TILE, (piece + 1) * TILE)
        up = dot(normed[rows], w_up[...], 1, 0)
        square = up * up
        bend = jnp.tanh(up * (0.7978845608028654 + (0.044715 * 0.7978845608028654) * square))
        share = 0.5 + 0.5 * bend
        act = up * share
        active[rows] = act.astype(BF16)
        slope = share + act * (1.0 - share) * (
            2 * 0.7978845608028654 + (6 * 0.044715 * 0.7978845608028654) * square
        )
        low = (dot(cot[rows], w_down[...], 1, 1) * slope).astype(BF16)
        up_grad[rows] = low
        two_grad = dot(low, w_up[...], 1, 1)

        @pl.when(step == 0)
        def _():
            back[rows] = two_grad

        @pl.when(step > 0)
        def _():
            back[rows] += two_grad


def run_units(sc, normed, cotangent, up, down):
    return pl.pallas_call(
        units_kernel,
        grid_spec=pltpu.PrefetchScalarGridSpec(
            num_scalar_prefetch=1,
            grid=(2 * FSIDE,),
            in_specs=[
                held((ROWS, WIDTH)),
                held((ROWS, WIDTH)),
                spec((WIDTH, FSTEP), early),
                spec((WIDTH, FSTEP), late),
                spec((FSTEP, SIDE), unit_rows),
                spec((FSTEP, SIDE), unit_rows),
            ],
            out_specs=[spec((ROWS, FSTEP), unit_columns), spec((ROWS, FSTEP), unit_columns), held((ROWS, WIDTH))],
            scratch_shapes=[pltpu.VMEM((WIDTH, FSTEP), BF16), pltpu.VMEM((FSTEP, WIDTH), BF16)],
        ),
        out_shape=[
            jax.ShapeDtypeStruct((ROWS, FF), BF16),
            jax.ShapeDtypeStruct((ROWS, FF), BF16),
            jax.ShapeDtypeStruct((ROWS, WIDTH), F32),
        ],
        compiler_params=params(VMEM),
        cost_estimate=pl.CostEstimate(
            flops=6 * ROWS * WIDTH * FF, bytes_accessed=8 * ROWS * WIDTH + 4 * ROWS * FF, transcendentals=ROWS * FF
        ),
        name="units",
    )(sc, normed.reshape(ROWS, WIDTH), cotangent.reshape(ROWS, WIDTH), *up, *down)


def down_grad_kernel(sc, active, cot, own, far, total):
    total[...] = dot(active[...], cot[...], 0, 0).astype(BF16)
    own[...] = total[:, own_lanes(sc)]
    far[...] = total[:, far_lanes(sc)]


def run_down_grad(sc, active, cotangent):
    return pl.pallas_call(
        down_grad_kernel,
        grid_spec=pltpu.PrefetchScalarGridSpec(
            num_scalar_prefetch=1,
            grid=(FF // 512,),
            in_specs=[spec((ROWS, 512), lambda f, s: (0, f)), held((ROWS, WIDTH))],
            out_specs=[spec((512, SIDE), lambda f, s: (f, 0))] * 2,
            scratch_shapes=[pltpu.VMEM((512, WIDTH), BF16)],
        ),
        out_shape=[jax.ShapeDtypeStruct((FF, SIDE), BF16)] * 2,
        compiler_params=params(VMEM),
        cost_estimate=pl.CostEstimate(
            flops=2 * ROWS * WIDTH * FF, bytes_accessed=2 * ROWS * (WIDTH + FF), transcendentals=0
        ),
        name="down_grad",
    )(sc, active, cotangent.reshape(ROWS, WIDTH))


def up_grad_kernel(sc, normed, up_grad, own, far):
    total = dot(normed[...], up_grad[...], 0, 0).astype(BF16)

    @pl.when(pl.program_id(0) < FSIDE)
    def _():
        own[...] = total

    @pl.when(pl.program_id(0) >= FSIDE)
    def _():
        far[...] = total


def run_up_grad(sc, normed, up_grad):
    return pl.pallas_call(
        up_grad_kernel,
        grid_spec=pltpu.PrefetchScalarGridSpec(
            num_scalar_prefetch=1,
            grid=(2 * FSIDE,),
            in_specs=[held((ROWS, WIDTH)), spec((ROWS, FSTEP), unit_columns)],
            out_specs=[spec((WIDTH, FSTEP), early), spec((WIDTH, FSTEP), late)],
        ),
        out_shape=[jax.ShapeDtypeStruct((WIDTH, FF // 2), BF16)] * 2,
        compiler_params=params(VMEM),
        cost_estimate=pl.CostEstimate(
            flops=2 * ROWS * WIDTH * FF, bytes_accessed=2 * ROWS * (WIDTH + FF), transcendentals=0
        ),
        name="up_grad",
    )(sc, normed.reshape(ROWS, WIDTH), up_grad)


def out_kernel(sc, active, resid, dn_own, dn_far, own, far, w_down):
    step = pl.program_id(0)

    @pl.when(step == 0)
    def _():
        w_down[:, own_lanes(sc)] = dn_own[...]
        w_down[:, far_lanes(sc)] = dn_far[...]

    branch = dot(active[...].reshape(4 * SPAN, FF), w_down[...], 1, 0)
    output = jnp.where(row_valid(sc, step), resid[...].reshape(4 * SPAN, WIDTH) + branch, 0.0)
    output = output.reshape(4, SPAN, WIDTH)
    own[...] = output[:2]
    far[...] = output[2:].astype(BF16)


def run_out(sc, active, resid, down):
    return pl.pallas_call(
        out_kernel,
        grid_spec=pltpu.PrefetchScalarGridSpec(
            num_scalar_prefetch=1,
            grid=(HROWS // SPAN,),
            in_specs=[
                spec((4, SPAN, FF), lambda r, s: (0, r, 0)),
                slab_spec(),
                held((FF, SIDE)),
                held((FF, SIDE)),
            ],
            out_specs=[slab_spec(2)] * 2,
            scratch_shapes=[pltpu.VMEM((FF, WIDTH), BF16)],
        ),
        out_shape=[
            jax.ShapeDtypeStruct((2, HROWS, WIDTH), F32),
            jax.ShapeDtypeStruct((2, HROWS, WIDTH), BF16),
        ],
        compiler_params=params(VMEM),
        cost_estimate=pl.CostEstimate(
            flops=2 * ROWS * WIDTH * FF, bytes_accessed=ROWS * (2 * FF + 7 * WIDTH), transcendentals=0
        ),
        name="out",
    )(sc, active.reshape(4, HROWS, FF), resid, *down)


def post_kernel(sc, resid, back, cot, mixed, wo_own, wo_far, gain, *refs):
    (res_own, res_far, heads, d_out_own, d_out_far, d_gain, weight, total, spread) = refs
    step = pl.program_id(0)
    whole_weight(sc, step, wo_own, wo_far, weight)
    shape, slab = (4 * SPAN, WIDTH), (4, SPAN, WIDTH)
    valid = row_valid(sc, step)
    res = resid[...].reshape(shape)
    scale = lax.rsqrt(jnp.mean(res * res, axis=-1, keepdims=True) + EPSILON)
    unit = res * scale
    two_grad = jnp.where(valid, back[...].reshape(shape), 0.0)
    gained = two_grad * gain[...]
    masked = cot[...].reshape(shape).astype(F32)
    grad = masked + scale * (gained - unit * jnp.mean(gained * unit, axis=-1, keepdims=True))
    low = grad.astype(BF16)
    res_own[...] = grad.reshape(slab)[:2]
    res_far[...] = low.reshape(slab)[2:]
    gain_sum = jnp.sum(two_grad * unit, axis=0, keepdims=True)
    out_sum = dot(mixed[...].reshape(shape), low, 0, 0)

    @pl.when(step == 0)
    def _():
        d_gain[...] = gain_sum
        total[...] = out_sum

    @pl.when(step > 0)
    def _():
        d_gain[...] += gain_sum
        total[...] += out_sum

    spread[...] = dot(low, weight[...], 1, 1).astype(BF16).reshape(slab)
    for pair in range(HEADS // 2):
        lanes = slice(pair * 128, (pair + 1) * 128)
        for side in range(2):
            one, two = spread[2 * side, :, lanes], spread[2 * side + 1, :, lanes]
            half = slice(side * 128, (side + 1) * 128)
            heads[2 * pair, :, half] = jnp.concatenate([one[:, :HEAD], two[:, :HEAD]], axis=1)
            heads[2 * pair + 1, :, half] = jnp.concatenate([one[:, HEAD:], two[:, HEAD:]], axis=1)

    @pl.when(step == pl.num_programs(0) - 1)
    def _():
        weight[...] = total[...].astype(BF16)
        d_out_own[...] = weight[:, own_lanes(sc)]
        d_out_far[...] = weight[:, far_lanes(sc)]


def run_post(sc, resid, back, cotangent, mixed, wo, gain):
    whole = (4, HROWS, WIDTH)
    return pl.pallas_call(
        post_kernel,
        grid_spec=pltpu.PrefetchScalarGridSpec(
            num_scalar_prefetch=1,
            grid=(HROWS // SPAN,),
            in_specs=[slab_spec()] * 4 + [held((WIDTH, SIDE)), held((WIDTH, SIDE)), held((1, WIDTH))],
            out_specs=[slab_spec(2)] * 2
            + [heads_spec(), held((WIDTH, SIDE)), held((WIDTH, SIDE)), held((1, WIDTH))],
            scratch_shapes=[
                pltpu.VMEM((WIDTH, WIDTH), BF16),
                pltpu.VMEM((WIDTH, WIDTH), F32),
                pltpu.VMEM((4, SPAN, WIDTH), BF16),
            ],
        ),
        out_shape=[
            jax.ShapeDtypeStruct((2, HROWS, WIDTH), F32),
            jax.ShapeDtypeStruct((2, HROWS, WIDTH), BF16),
            jax.ShapeDtypeStruct((HEADS, HROWS, 4 * HEAD), BF16),
            jax.ShapeDtypeStruct((WIDTH, SIDE), BF16),
            jax.ShapeDtypeStruct((WIDTH, SIDE), BF16),
            jax.ShapeDtypeStruct((1, WIDTH), F32),
        ],
        compiler_params=params(VMEM),
        cost_estimate=pl.CostEstimate(
            flops=4 * ROWS * WIDTH * WIDTH, bytes_accessed=28 * ROWS * WIDTH, transcendentals=0
        ),
        name="post",
    )(sc, resid, back.reshape(whole), cotangent, mixed, *wo, gain)


def unmix_kernel(carried, sc, *refs):
    shards, (v_own, v_far, grad_heads, mean, *rest) = refs[:8], refs[8:]
    rest = rest[2:] if carried else rest
    outs, (own, far, raw, grads, mask, adder, bound, sems, out_sems) = rest[:8], rest[8:]
    place = sc[PLACE]
    step = pl.program_id(0)

    def leave(slot):
        return [
            pltpu.make_async_copy(
                grads.at[slot, pl.ds(pl.multiple_of((place ^ rel) * SUBS * HALF, SUBS * HALF), SUBS * HALF)],
                outs[4 * slot + rel],
                out_sems.at[slot, rel],
            )
            for rel in range(4)
        ]

    fill_mask(sc, mask)

    @pl.when(step == 0)
    def _():
        lane = lax.broadcasted_iota(jnp.int32, (4 * HEAD, 128), 0) // HEAD
        column = lax.broadcasted_iota(jnp.int32, (4 * HEAD, 128), 1)
        adder[...] = jnp.where((lane == column) | (lane + 4 == column), -1.0, 0.0).astype(BF16)
        row = lax.broadcasted_iota(jnp.int32, (LMAX, 128), 0)
        item = lax.broadcasted_iota(jnp.int32, (LMAX, 128), 1)
        length = jnp.where(item % 4 == 0, sc[LENGTHS], sc[LENGTHS + 1])
        length = jnp.where(item % 4 == 2, sc[LENGTHS + 2], length)
        length = jnp.where(item % 4 == 3, sc[LENGTHS + 3], length)
        bound[...] = jnp.where((item < 8) & (row < length), 1.0, 0.0).astype(BF16)

    slot = take_plane(place, shards, raw, sems)
    high_lanes = lax.broadcasted_iota(jnp.int32, (HROWS, 128), 1) < 4
    for head in range(PHEADS):
        weights = jnp.exp(raw[slot, head_rows(head)].astype(F32)).astype(BF16)
        low = (grad_heads[head].astype(F32) * inverse_sums(sc, weights, mask)).astype(BF16)
        product = low.astype(F32) * mean[head]
        coarse = product.astype(BF16)
        fine = (product - coarse.astype(F32)).astype(BF16)
        delta = dot(coarse, adder[...], 1, 0) + dot(fine, adder[...], 1, 0)
        coarse = delta.astype(BF16)
        fine = (delta - coarse.astype(F32)).astype(BF16)
        left = jnp.concatenate([low, jnp.where(high_lanes, coarse, fine)], axis=1)
        score = dot(left, jnp.concatenate([v_own[head], v_far[head], bound[...]], axis=1), 1, 1)
        grads[slot, head_rows(head)] = (score * weights.astype(F32)).astype(BF16)
        back = (dot(weights, low, 0, 0) * mask[...].astype(F32)).astype(BF16)
        own[head] = back[:, : 2 * HEAD]
        far[head] = back[:, 2 * HEAD :]
    for which in range(2):

        @pl.when(step == which)
        def _():
            for copy in leave(which):
                copy.start()
            if which == 1:
                for copy in leave(0) + leave(1):
                    copy.wait()


def run_unmix(sc, planes, shards, v_own, v_far, grad_heads, mean, carry):
    carry = list(carry)
    return pl.pallas_call(
        partial(unmix_kernel, bool(carry)),
        grid_spec=pltpu.PrefetchScalarGridSpec(
            num_scalar_prefetch=1,
            grid=(2,),
            in_specs=anywhere(8)
            + [plane_spec(planes, LMAX, 2 * HEAD)] * 2
            + [plane_spec(planes, HROWS, 4 * HEAD)] * 2
            + anywhere(len(carry)),
            out_specs=anywhere(8) + [plane_spec(planes, LMAX, 2 * HEAD)] * 2,
            scratch_shapes=[
                pltpu.VMEM((2, 4 * SUBS * HALF, LMAX), BF16),
                pltpu.VMEM((2, 4 * SUBS * HALF, LMAX), BF16),
                pltpu.VMEM((LMAX, 4 * HEAD), BF16),
                pltpu.VMEM((4 * HEAD, 128), BF16),
                pltpu.VMEM((LMAX, 128), BF16),
                pltpu.SemaphoreType.DMA((2, 4)),
                pltpu.SemaphoreType.DMA((2, 4)),
            ],
        ),
        out_shape=[jax.ShapeDtypeStruct((SUBS * HALF, LMAX), BF16)] * 8
        + [jax.ShapeDtypeStruct((HEADS, LMAX, 2 * HEAD), BF16)] * 2,
        input_output_aliases={13 + i: 8 + i for i in range(len(carry))},
        compiler_params=params(VMEM),
        cost_estimate=pl.CostEstimate(
            flops=3 * HEADS * HROWS * LMAX * 4 * HEAD,
            bytes_accessed=HEADS * (2 * HROWS * LMAX + 4 * HROWS * 256 + 4 * LMAX * 256),
            transcendentals=HEADS * HROWS * LMAX // 2,
        ),
        name="unmix",
    )(sc, *shards, v_own, v_far, grad_heads, mean, *carry)


def close_kernel(sc, tok, res_own, res_got, out_own, out_got, own, far, gain, w_own, w_far, *refs):
    (output, tok_grad, d_value, d_gain, total, weight) = refs
    step = pl.program_id(0)
    whole_weight(sc, step, w_own, w_far, weight)
    core = sc[CORE]
    output[:, :, core] = out_own[...]
    output[:, :, 1 - core] = out_got[...].astype(F32)
    tok_grad[:, :, core] = res_own[...]
    tok_grad[:, :, 1 - core] = res_got[...].astype(F32)
    runs = tok.shape[1]
    rows = runs * 128
    for item in range(2):
        lanes = slice(item * HEAD, (item + 1) * HEAD)
        pieces = [
            add_low(own[head, :, lanes], far[head, :, lanes]) for head in range(HEADS)
        ]
        back = jnp.concatenate(pieces, axis=1)
        x = tok[item].reshape(rows, WIDTH).astype(F32)
        scale = lax.rsqrt(jnp.mean(x * x, axis=-1, keepdims=True) + EPSILON)
        unit = x * scale
        normed = (unit * gain[...]).astype(BF16)
        normed_grad = dot(back, weight[...], 1, 1)
        gained = normed_grad * gain[...]
        update = scale * (gained - unit * jnp.mean(gained * unit, axis=-1, keepdims=True))
        tok_grad[item] += update.reshape(runs, 2, HALF, WIDTH)
        gain_sum = jnp.sum(normed_grad * unit, axis=0, keepdims=True)
        value_sum = dot(normed, back, 0, 0)
        if item == 0:
            gain_total, value_total = gain_sum, value_sum
        else:
            gain_total, value_total = gain_total + gain_sum, value_total + value_sum

    @pl.when(step == 0)
    def _():
        d_gain[...] = gain_total
        total[...] = value_total

    @pl.when(step > 0)
    def _():
        d_gain[...] += gain_total
        total[...] += value_total

    @pl.when(step == pl.num_programs(0) - 1)
    def _():
        low = total[...].astype(BF16)
        d_value[0] = low[:, :SIDE]
        d_value[1] = low[:, SIDE:]


def run_close(sc, tokens, res_own, res_got, out_own, out_got, own, far, gain, w_own, w_far):
    runs = 2
    slab = (2, RUNS, 2, HALF, WIDTH)
    half = (2, RUNS, HALF, WIDTH)
    whole_spec = spec((2, runs, 2, HALF, WIDTH), lambda j, s: (0, j, 0, 0, 0))
    half_spec = spec((2, runs, HALF, WIDTH), lambda j, s: (0, j, 0, 0))
    back_spec = spec((HEADS, runs * 128, 2 * HEAD), lambda j, s: (0, j, 0))
    return pl.pallas_call(
        close_kernel,
        grid_spec=pltpu.PrefetchScalarGridSpec(
            num_scalar_prefetch=1,
            grid=(RUNS // runs,),
            in_specs=[whole_spec]
            + [half_spec] * 4
            + [back_spec, back_spec, held((1, WIDTH)), held((WIDTH, SIDE)), held((WIDTH, SIDE))],
            out_specs=[whole_spec, whole_spec, held((2, WIDTH, SIDE)), held((1, WIDTH))],
            scratch_shapes=[pltpu.VMEM((WIDTH, WIDTH), F32), pltpu.VMEM((WIDTH, WIDTH), BF16)],
        ),
        out_shape=[
            jax.ShapeDtypeStruct(slab, F32),
            jax.ShapeDtypeStruct(slab, F32),
            jax.ShapeDtypeStruct((2, WIDTH, SIDE), BF16),
            jax.ShapeDtypeStruct((1, WIDTH), F32),
        ],
        compiler_params=params(VMEM),
        cost_estimate=pl.CostEstimate(
            flops=4 * 2 * LMAX * WIDTH * WIDTH, bytes_accessed=38 * LMAX * WIDTH, transcendentals=0
        ),
        name="close",
    )(
        sc,
        tokens.reshape(slab),
        *(x.reshape(half) for x in (res_own, res_got, out_own, out_got)),
        own,
        far,
        gain,
        w_own,
        w_far,
    )


PACK_DOWN, PACK_UP, PACK_OUT, PACK_VALUE, PACK_GAIN, PACK = 0, 192, 384, 432, 480, 496


def pack_kernel(sc, down, up, out, value, gain, down_far, up_far, out_far, value_far, gain_far, packed):
    first = sc[CORE] == 0

    def both(own, far, lanes):
        own, far = own[:, lanes], far[:, lanes]
        return jnp.concatenate([jnp.where(first, own, far), jnp.where(first, far, own)], axis=0)

    def side(own, far):
        return both(own, far, own_lanes(sc))

    packed[PACK_DOWN:PACK_UP] = side(down, down_far)
    for j in range(4):
        lanes = pl.ds(pl.multiple_of((4 * sc[CORE] + j) * SIDE, 128), SIDE)
        packed[PACK_UP + 48 * j : PACK_UP + 48 * (j + 1)] = both(up, up_far, lanes)
    packed[PACK_OUT:PACK_VALUE] = side(out, out_far)
    packed[PACK_VALUE:PACK_GAIN] = side(value, value_far)
    packed[PACK_GAIN:] = both(gain, gain_far, slice(0, SIDE))


def run_pack(sc, own, far):
    return pl.pallas_call(
        pack_kernel,
        grid_spec=pltpu.PrefetchScalarGridSpec(
            num_scalar_prefetch=1,
            grid=(1,),
            in_specs=[held(x.shape) for x in (*own, *far)],
            out_specs=held((PACK, SIDE)),
        ),
        out_shape=jax.ShapeDtypeStruct((PACK, SIDE), BF16),
        compiler_params=params(VMEM),
        cost_estimate=pl.CostEstimate(flops=0, bytes_accessed=6 * PACK * SIDE, transcendentals=0),
        name="pack",
    )(sc, *own, *far)


def chip_of(sc, k, rel):
    return plane_of(k, sc) * 4 + (sc[PLACE] ^ rel)


def place_kernel(moves, sc, *refs):
    pieces, targets, sems = refs[:16], refs[16:-1], refs[-1]
    copies = []
    for index, piece in enumerate(pieces):
        chip = chip_of(sc, index // 4, index % 4)
        for which, (start, count, lane, target, step, offset, column) in enumerate(moves):
            rows = pl.ds(pl.multiple_of(chip * step + offset, 16), count)
            copies.append(
                pltpu.make_async_copy(
                    piece.at[pl.ds(start, count), pl.ds(lane, SIDE)],
                    targets[target].at[rows, pl.ds(column, SIDE)],
                    sems.at[index, which],
                )
            )
    for copy in copies:
        copy.start()
    for copy in copies:
        copy.wait()


def run_place(sc, pieces, moves, shapes):
    return pl.pallas_call(
        partial(place_kernel, moves),
        grid_spec=pltpu.PrefetchScalarGridSpec(
            num_scalar_prefetch=1,
            grid=(1,),
            in_specs=anywhere(16),
            out_specs=[held(shape) for shape in shapes],
            scratch_shapes=[pltpu.SemaphoreType.DMA((16, len(moves)))],
        ),
        out_shape=[jax.ShapeDtypeStruct(shape, BF16) for shape in shapes],
        compiler_params=params(VMEM),
        cost_estimate=pl.CostEstimate(
            flops=0, bytes_accessed=4 * sum(a * b for a, b in shapes), transcendentals=0
        ),
        name="place",
    )(sc, *pieces)


def place_weights(sc, pieces):
    moves = (
        (PACK_DOWN, 192, 0, 0, 192, 0, 0),
        *((PACK_UP + 48 * j, 48, 0, 1, 48, 0, j * SIDE) for j in range(4)),
        (PACK_OUT, 48, 0, 2, 48, 0, 0),
        (PACK_VALUE, 48, 0, 3, 48, 0, 0),
        (PACK_GAIN, 16, 0, 4, 16, 0, 0),
    )
    shapes = [(FF, SIDE), (WIDTH, FF // 2), (WIDTH, SIDE), (WIDTH, SIDE), (256, SIDE)]
    return run_place(sc, pieces, moves, shapes)


def collect_kernel(sc, *refs):
    packed = refs[-1]
    for rel in range(4):
        down, down_got, up, up_got, out, out_got = refs[6 * rel : 6 * rel + 6]
        packed[rel, PACK_DOWN:PACK_UP] = add_low(down[...], down_got[...])
        for j in range(4):
            lanes = slice(j * SIDE, (j + 1) * SIDE)
            packed[rel, PACK_UP + 48 * j : PACK_UP + 48 * (j + 1)] = add_low(up[:, lanes], up_got[:, lanes])
        packed[rel, PACK_OUT:PACK_VALUE] = add_low(out[...], out_got[...])


def run_collect(sc, *sides):
    def rows(x, rel):
        return spec((x.shape[0] // 16, x.shape[1]), lambda k, s: (chip_of(s, k, rel), 0))

    return pl.pallas_call(
        collect_kernel,
        grid_spec=pltpu.PrefetchScalarGridSpec(
            num_scalar_prefetch=1,
            grid=(PLANES,),
            in_specs=[rows(x, rel) for rel in range(4) for x in sides],
            out_specs=spec((4, PACK_VALUE, SIDE), lambda k, s: (k, 0, 0)),
        ),
        out_shape=jax.ShapeDtypeStruct((16, PACK_VALUE, SIDE), BF16),
        compiler_params=params(VMEM),
        cost_estimate=pl.CostEstimate(flops=0, bytes_accessed=3 * 16 * PACK_VALUE * SIDE * 2, transcendentals=0),
        name="collect",
    )(sc, *(x for _ in range(4) for x in sides))


DEVICES = 32
TO_CORE, TO_X, TO_Y = 1, 2, 4


def swap(x, bit):
    return lax.ppermute(x, BOTH, [(d, d ^ bit) for d in range(DEVICES)])


def ring(x, way=1):
    return lax.ppermute(x, BOTH, [(d, (d + 8 * way) % DEVICES) for d in range(DEVICES)])


def pick(x, index, axis=0):
    return lax.dynamic_index_in_dim(x, index, axis, keepdims=False)


def ordered(flag, one, two, axis=0, joined=jnp.stack):
    return jnp.where(flag == 0, joined([one, two], axis), joined([two, one], axis))


def add_low(one, two):
    return (one.astype(F32) + two.astype(F32)).astype(BF16)


STEPS = (
    ((0, 0, 1), (0, 1, 0), (1, 0, 0)),
    ((1, 0, 1), (0, 1, 1), (2, 0, 0)),
    ((2, 0, 1), (1, 1, 0), (3, 0, 0)),
    ((3, 0, 1), (2, 1, 0), (1, 1, 1)),
    ((2, 1, 1), (3, 1, 1), (3, 1, 0)),
)


def gather_step(have, step):
    by_x, by_y, by_z = STEPS[step]
    return {
        **have,
        by_z: ring(have[by_z[0] - 1, by_z[1], by_z[2]]),
        by_x: swap(have[by_x[0], by_x[1], 0], TO_X),
        by_y: swap(have[by_y[0], 0, by_y[2]], TO_Y),
    }


def in_order(have):
    return [have[k, y, x] for k in range(4) for y in range(2) for x in range(2)]


def by_place(shares, planes=range(PLANES)):
    return {(k, i // 2, i % 2): shares[4 * at + i] for at, k in enumerate(planes) for i in range(4)}


def scatter_send(have, step):
    by_x, by_y, by_z = STEPS[len(STEPS) - 1 - step]
    got = (ring(have[by_z], -1), swap(have[by_x], TO_X), swap(have[by_y], TO_Y))
    return {at: value for at, value in have.items() if at not in (by_x, by_y, by_z)}, got


def scatter_add(have, got, step):
    by_x, by_y, by_z = STEPS[len(STEPS) - 1 - step]
    targets = ((by_z[0] - 1, by_z[1], by_z[2]), (by_x[0], by_x[1], 0), (by_y[0], 0, by_y[2]))
    have = dict(have)
    for at in dict.fromkeys(targets):
        total = have[at].astype(F32)
        for target, value in zip(targets, got):
            if target == at:
                total = total + value.astype(F32)
        have[at] = total if step == len(STEPS) - 1 else total.astype(BF16)
    return have


together = lax.optimization_barrier


def chip_shards(tokens, lengths, rand_mix, w_value, w_out, w_up, w_down, gain_mix, gain_ffn, grad_out):
    wide = lax.axis_index("wide")
    core = lax.axis_index("narrow")
    z, y, x = wide // 4, (wide // 2) % 2, wide % 2
    other = lambda value: swap(value, TO_CORE)
    side = partial(ordered, core, joined=jnp.concatenate)
    slab = (2, RUNS, 2, HALF, WIDTH)
    tokens, grad_out = tokens.reshape(slab), grad_out.reshape(slab)

    gains = jnp.pad(jnp.concatenate([gain_mix, gain_ffn])[None], ((0, 7), (0, SIDE - 48)))
    own = (w_down, w_up, w_out, w_value, gains)
    far = tuple(other(value) for value in own)
    near_sc = jnp.concatenate([jnp.stack([core, z, wide % 4]).astype(jnp.int32), lengths, lengths])
    weights = {(0, 0, 0): run_pack(near_sc, own, far)}

    rand = rand_mix.reshape(3, 2, HALF, LMAX)
    blocks = side(pick(rand, core, 1), other(pick(rand, 1 - core, 1)), 0)
    weights, (rands, far_lengths) = together(
        (gather_step(weights, 0), ({(0, 0, 0): blocks.reshape(SUBS * HALF, LMAX)}, other(lengths)))
    )
    sc = jnp.concatenate([near_sc[:5], far_lengths])

    rands, weights, tokens_far = together(
        (gather_step(rands, 0), gather_step(gather_step(weights, 1), 2), other(pick(tokens, 1 - core, 2)))
    )
    rands, weights, grad_far = together(
        (gather_step(rands, 1), gather_step(gather_step(weights, 3), 4), other(pick(grad_out, 1 - core, 2)))
    )
    down, up, out, value, gain_rows = place_weights(sc, in_order(weights))
    value_far = other(value)
    gain_rows = gain_rows.reshape(16, 2, 8, SIDE)[:, :, 0]
    gain_one = gain_rows[..., :24].reshape(1, WIDTH).astype(F32)
    gain_two = gain_rows[..., 24:48].reshape(1, WIDTH).astype(F32)
    v_own = run_values(sc, tokens.reshape(2, LMAX, WIDTH), gain_one, value, value_far)
    rands, value_far, v_own, gain_one, gain_two, out, down, up = together(
        (gather_step(rands, 2), value_far, v_own, gain_one, gain_two, out, down, up)
    )
    rands, v_far, out, down = together(
        (gather_step(rands, 3), other(v_own), (out, other(out)), (down, other(down)))
    )
    mixing = run_mix(sc, (0, 1), in_order({**rands, (2, 1, 1): 0, (3, 1, 0): 0, (3, 1, 1): 0})[:8], v_own, v_far, ())
    rands, up, mixing = together((gather_step(rands, 4), (up, other(up)), mixing))
    shares = in_order(rands)
    heads, mean = run_mix(sc, (2, 3), shares[8:], v_own, v_far, mixing)

    mixed, resid, normed, masked = run_pre(sc, tokens, tokens_far, grad_out, grad_far, heads, out, gain_two)
    active, up_grad, back = run_units(sc, normed, masked, up, down)
    res_own, res_far, grad_heads, d_out_own, d_out_far, d_gain_two = run_post(
        sc, resid, back, masked, mixed, out, gain_two
    )

    *far, back_own, back_far = run_unmix(
        sc, (3, 2), shares[12:] + shares[8:12], v_own, v_far, grad_heads, mean, ()
    )
    have, got = scatter_send(by_place(far, (3, 2)), 0)
    *near, back_own, back_far = run_unmix(
        sc, (1, 0), shares[4:8] + shares[:4], v_own, v_far, grad_heads, mean, (back_own, back_far)
    )
    have, got, near, back_own, back_far, res_got, d_out_got = together(
        (have, got, near, back_own, back_far, other(res_far), other(d_out_far))
    )
    have = {**scatter_add(have, got, 0), **by_place(near, (1, 0))}

    have, got = scatter_send(have, 1)
    up_own, up_far = run_up_grad(sc, normed, up_grad)
    have, got, up_own, up_far, back_got = together((have, got, up_own, up_far, other(back_far)))
    have = scatter_add(have, got, 1)

    have, got = scatter_send(have, 2)
    down_own, down_far = run_down_grad(sc, active, masked)
    have, got, down_own, down_far, up_got = together((have, got, down_own, down_far, other(up_far)))
    have = scatter_add(have, got, 2)

    have, got = scatter_send(have, 3)
    packed = run_collect(sc, down_own, other(down_far), up_own, up_got, d_out_own, d_out_got)
    sums, sums_got = scatter_send(by_place([packed[i] for i in range(16)]), 0)
    out_own, out_far = run_out(sc, active, resid, down)
    have, got, sums, sums_got, out_own, out_far = together((have, got, sums, sums_got, out_own, out_far))
    have, sums = scatter_add(have, got, 3), scatter_add(sums, sums_got, 0)

    have, got = scatter_send(have, 4)
    sums, sums_got = scatter_send(sums, 1)
    sums, sums_got = scatter_send(scatter_add(sums, sums_got, 1), 2)
    output, tokens_grad, d_value, d_gain_one = run_close(
        sc, tokens, res_own, res_got, out_own, other(out_far), back_own, back_got, gain_one, value, value_far
    )
    gain_pair = jnp.concatenate([d_gain_one, d_gain_two]).reshape(2, 16, 1, 48).astype(BF16)
    gain_pair = jnp.pad(gain_pair, ((0, 0), (0, 0), (0, 15), (0, SIDE - 48)))
    small = jnp.concatenate([d_value.reshape(2, 16, 48, SIDE), gain_pair], 2)
    small = add_low(pick(small, core), other(pick(small, 1 - core))).reshape(4, 2, 2, 64, SIDE)
    have, got, sums, sums_got, small, output, tokens_grad = together(
        (have, got, sums, sums_got, small, output, tokens_grad)
    )
    rand_sum = scatter_add(have, got, 4)[0, 0, 0].reshape(2, 3, HALF, LMAX)
    sums = scatter_add(sums, sums_got, 2)

    sums, sums_got = scatter_send(sums, 3)
    small = add_low(pick(small, x, 2), swap(pick(small, 1 - x, 2), TO_X))
    blocks, blocks_far = pick(rand_sum, core), other(pick(rand_sum, 1 - core))
    sums, sums_got, small, blocks, blocks_far = together((sums, sums_got, small, blocks, blocks_far))
    sums = scatter_add(sums, sums_got, 3)

    sums, sums_got = scatter_send(sums, 4)
    small = add_low(pick(small, y, 1), swap(pick(small, 1 - y, 1), TO_Y))
    sums, sums_got, small = together((sums, sums_got, small))
    big_sum = scatter_add(sums, sums_got, 4)[0, 0, 0]

    small_sum = pick(small, z).astype(F32)
    for k in range(1, PLANES):
        small_sum = small_sum + ring(pick(small, lax.rem(z + PLANES - k, PLANES)), -k).astype(F32)
    big_far, small_far = other(big_sum), other(small_sum)

    rows_of = lambda value, rows: pick(value.reshape(-1, 2, rows, SIDE), core, 1)
    mine = lambda own, far, rows: side(rows_of(own, rows)[0], rows_of(far, rows)[0], 1)
    down_shard = mine(big_sum[PACK_DOWN:PACK_UP], big_far[PACK_DOWN:PACK_UP], 96)
    up_side = lambda value: rows_of(value[PACK_UP:PACK_OUT], 24).transpose(1, 0, 2).reshape(24, 4 * SIDE)
    up_shard = side(up_side(big_sum), up_side(big_far), 1)
    outproj_shard = mine(big_sum[PACK_OUT:PACK_VALUE], big_far[PACK_OUT:PACK_VALUE], 24)
    value_shard = mine(small_sum[:48], small_far[:48], 24)
    gains_pair = ordered(core, small_sum[48, :48], small_far[48, :48])
    gain_pair = pick(gains_pair.reshape(2, 2, 24), core, 1)

    rand_shard = ordered(core, blocks, blocks_far, 1)

    return (
        output.reshape(2, LMAX, WIDTH),
        tokens_grad.reshape(2, LMAX, WIDTH),
        rand_shard.reshape(3 * 128, LMAX),
        value_shard,
        outproj_shard,
        up_shard,
        down_shard,
        gain_pair[0],
        gain_pair[1],
    )


def rms_norm(values, gain):
    scale = lax.rsqrt(jnp.mean(values * values, axis=-1, keepdims=True) + EPSILON)
    return values * scale * gain


def split_heads(block):
    return block.reshape(LMAX, HEADS, HEAD).transpose(1, 0, 2)


def merge_heads(block):
    return block.transpose(1, 0, 2).reshape(LMAX, HEADS * HEAD)


def masked_scores(key_mask, rand_head):
    return jnp.where(key_mask[None, :] > 0, rand_head.astype(jnp.float32), -1e30)


def head_forward(key_mask, paired):
    rand_head, value_head = paired
    scores = masked_scores(key_mask, rand_head)
    row_peak = jnp.max(scores, axis=-1, keepdims=True)
    exponent = jnp.exp(scores - row_peak)
    denom_sum = jnp.sum(exponent, axis=-1, keepdims=True)
    attention = exponent / denom_sum * key_mask[:, None]
    mixed = jnp.dot(attention.astype(jnp.bfloat16), value_head, preferred_element_type=jnp.float32)
    return (mixed.astype(jnp.bfloat16), row_peak + jnp.log(denom_sum))


def head_backward(key_mask, paired):
    rand_head, value_head, mix_grad, log_total = paired
    scores = masked_scores(key_mask, rand_head)
    attention = jnp.exp(scores - log_total) * key_mask[:, None]
    prob_grad = jnp.einsum("id,jd->ij", mix_grad, value_head, preferred_element_type=jnp.float32)
    value_grad = jnp.einsum(
        "ij,id->jd", attention.astype(jnp.bfloat16), mix_grad, preferred_element_type=jnp.float32
    )
    score_grad = attention * (prob_grad - jnp.sum(prob_grad * attention, axis=-1, keepdims=True))
    return (score_grad, value_grad)


def shards(tokens, lengths, rand_mix, w_value, w_out, w_up, w_down, gain_mix, gain_ffn, grad_out):
    item_count = tokens.shape[0]
    width = tokens.shape[2]
    row_count = item_count * LMAX
    tokens_flat = tokens.reshape(row_count, width).astype(jnp.float32)
    positions = jnp.arange(LMAX, dtype=jnp.int32)
    valid_table = (positions[None, :] < lengths[:, None]).astype(jnp.float32)
    row_valid = valid_table.reshape(row_count, 1)
    forward_set = (
        lax.all_gather(rand_mix, ("wide", "narrow"), axis=0, tiled=True),
        lax.all_gather(w_value, ("wide", "narrow"), axis=0, tiled=True),
        lax.all_gather(w_out, ("wide", "narrow"), axis=0, tiled=True),
        lax.all_gather(w_up, ("wide", "narrow"), axis=0, tiled=True),
        lax.all_gather(w_down, ("wide", "narrow"), axis=0, tiled=True),
        lax.all_gather(gain_mix, ("wide", "narrow"), axis=0, tiled=True),
        lax.all_gather(gain_ffn, ("wide", "narrow"), axis=0, tiled=True),
    )
    rand_all, value_all, out_all, up_all, down_all, gain_first, gain_second = forward_set
    normed = rms_norm(tokens_flat, gain_first.astype(jnp.float32)).astype(jnp.bfloat16)
    values = jnp.dot(normed, value_all, preferred_element_type=jnp.float32).astype(jnp.bfloat16)
    rand_heads = rand_all.reshape(HEADS, LMAX, LMAX)
    mixed_parts = []
    totals_kept = []
    for item_index in range(item_count):
        item_values = split_heads(values[item_index * LMAX : (item_index + 1) * LMAX])
        mixed_heads, log_total = lax.map(
            partial(head_forward, valid_table[item_index]), (rand_heads, item_values)
        )
        mixed_parts.append(merge_heads(mixed_heads))
        totals_kept.append(log_total)
    mixed = jnp.concatenate(mixed_parts, axis=0)
    residual = tokens_flat + jnp.dot(mixed, out_all, preferred_element_type=jnp.float32)
    normed_two = rms_norm(residual, gain_second.astype(jnp.float32)).astype(jnp.bfloat16)
    up_proj = jnp.dot(normed_two, up_all, preferred_element_type=jnp.float32)
    active = jax.nn.gelu(up_proj).astype(jnp.bfloat16)
    branch = jnp.dot(active, down_all, preferred_element_type=jnp.float32)
    output = row_valid * (residual + branch)
    back_set = (
        lax.all_gather(rand_mix, ("wide", "narrow"), axis=0, tiled=True),
        lax.all_gather(w_value, ("wide", "narrow"), axis=0, tiled=True),
        lax.all_gather(w_out, ("wide", "narrow"), axis=0, tiled=True),
        lax.all_gather(w_up, ("wide", "narrow"), axis=0, tiled=True),
        lax.all_gather(w_down, ("wide", "narrow"), axis=0, tiled=True),
        lax.all_gather(gain_mix, ("wide", "narrow"), axis=0, tiled=True),
        lax.all_gather(gain_ffn, ("wide", "narrow"), axis=0, tiled=True),
    )
    rand_back, value_back, out_back, up_back, down_back, gain_back_one, gain_back_two = back_set
    cotangent = grad_out.reshape(row_count, width).astype(jnp.float32)
    masked = row_valid * cotangent
    branch_grad = masked.astype(jnp.bfloat16)
    grad_down = jnp.einsum("rk,rd->kd", active, branch_grad, preferred_element_type=jnp.float32)
    active_grad = jnp.einsum(
        "rd,kd->rk", branch_grad, down_back, preferred_element_type=jnp.float32
    )
    gelu_value, gelu_pull = jax.vjp(jax.nn.gelu, up_proj)
    up_grad = gelu_pull(active_grad)[0].astype(jnp.bfloat16)
    grad_up = jnp.einsum("rd,rk->dk", normed_two, up_grad, preferred_element_type=jnp.float32)
    normed_two_grad = jnp.einsum("rk,dk->rd", up_grad, up_back, preferred_element_type=jnp.float32)
    norm_value, norm_pull = jax.vjp(rms_norm, residual, gain_back_two.astype(jnp.float32))
    residual_part, gain_two_grad = norm_pull(normed_two_grad)
    residual_grad = masked + residual_part
    attn_grad = residual_grad.astype(jnp.bfloat16)
    grad_outproj = jnp.einsum("rd,re->de", mixed, attn_grad, preferred_element_type=jnp.float32)
    mixed_grad = jnp.einsum(
        "re,de->rd", attn_grad, out_back, preferred_element_type=jnp.float32
    ).astype(jnp.bfloat16)
    rand_heads_back = rand_back.reshape(HEADS, LMAX, LMAX)
    rand_grad = jnp.zeros((HEADS, LMAX, LMAX), jnp.float32)
    value_parts = []
    for item_index in range(item_count):
        lower_row = item_index * LMAX
        upper_row = lower_row + LMAX
        item_values = split_heads(values[lower_row:upper_row])
        item_mix_grad = split_heads(mixed_grad[lower_row:upper_row])
        score_grad, value_grad = lax.map(
            partial(head_backward, valid_table[item_index]),
            (rand_heads_back, item_values, item_mix_grad, totals_kept[item_index]),
        )
        rand_grad = rand_grad + score_grad
        value_parts.append(merge_heads(value_grad))
    values_grad = jnp.concatenate(value_parts, axis=0).astype(jnp.bfloat16)
    grad_value = jnp.einsum("rd,re->de", normed, values_grad, preferred_element_type=jnp.float32)
    normed_grad = jnp.einsum(
        "re,de->rd", values_grad, value_back, preferred_element_type=jnp.float32
    )
    norm_first, first_pull = jax.vjp(rms_norm, tokens_flat, gain_back_one.astype(jnp.float32))
    token_part, gain_one_grad = first_pull(normed_grad)
    tokens_grad = residual_grad + token_part
    rand_flat = rand_grad.reshape(HEADS * LMAX, LMAX)
    all_shards = (
        lax.psum_scatter(rand_flat, ("wide", "narrow"), scatter_dimension=0, tiled=True),
        lax.psum_scatter(grad_value, ("wide", "narrow"), scatter_dimension=0, tiled=True),
        lax.psum_scatter(grad_outproj, ("wide", "narrow"), scatter_dimension=0, tiled=True),
        lax.psum_scatter(grad_up, ("wide", "narrow"), scatter_dimension=0, tiled=True),
        lax.psum_scatter(grad_down, ("wide", "narrow"), scatter_dimension=0, tiled=True),
        lax.psum_scatter(gain_one_grad, ("wide", "narrow"), scatter_dimension=0, tiled=True),
        lax.psum_scatter(gain_two_grad, ("wide", "narrow"), scatter_dimension=0, tiled=True),
    )
    rand_shard, value_shard, outproj_shard, up_shard, down_shard, gain_one_shard, gain_two_shard = (
        all_shards
    )
    return (
        output.reshape(item_count, LMAX, width),
        tokens_grad.reshape(item_count, LMAX, width),
        rand_shard,
        value_shard,
        outproj_shard,
        up_shard,
        down_shard,
        gain_one_shard,
        gain_two_shard,
    )


def solution(mesh):
    in_specs = (
        P(("wide", "narrow"), None, None),
        P(("wide", "narrow")),
        P(("wide", "narrow"), None),
        P(("wide", "narrow"), None),
        P(("wide", "narrow"), None),
        P(("wide", "narrow"), None),
        P(("wide", "narrow"), None),
        P(("wide", "narrow")),
        P(("wide", "narrow")),
        P(("wide", "narrow"), None, None),
    )
    out_specs = (
        P(("wide", "narrow"), None, None),
        P(("wide", "narrow"), None, None),
        P(("wide", "narrow"), None),
        P(("wide", "narrow"), None),
        P(("wide", "narrow"), None),
        P(("wide", "narrow"), None),
        P(("wide", "narrow"), None),
        P(("wide", "narrow")),
        P(("wide", "narrow")),
    )
    fits = dict(mesh.shape) == {"wide": 16, "narrow": 2}
    return jax.shard_map(chip_shards if fits else shards, mesh=mesh, in_specs=in_specs, out_specs=out_specs, check_vma=False)
```

```python
from functools import partial

import jax
import jax.numpy as jnp
from jax import lax
from jax.experimental import pallas as pl
from jax.experimental.pallas import tpu as pltpu
from jax.sharding import PartitionSpec as P

HEADS = 12
HEAD = 64
LMAX = 1024
WIDTH = 768
FF = 3072
EPSILON = 1e-05

BOTH = ("wide", "narrow")
BF16 = jnp.bfloat16
F32 = jnp.float32
VMEM = 61 << 20

SUBS = 6
RUNS = 8
HALF = 64
HROWS = RUNS * HALF
PLANES = 4
PHEADS = HEADS // PLANES
ROWS = 2 * LMAX
FSTEP = 768
FSIDE = FF // 2 // FSTEP
TILE = 512
SIDE = WIDTH // 2
SPAN = 2 * HALF


def dot(a, b, ca, cb):
    return lax.dot_general(a, b, (((ca,), (cb,)), ((), ())), preferred_element_type=F32)


CORE, PLANE, PLACE, LENGTHS = 0, 1, 2, 3


def spec(shape, index):
    return pl.BlockSpec(shape, index)


def held(shape):
    zeros = (0,) * len(shape)
    return pl.BlockSpec(shape, lambda *_: zeros, pipeline_mode=pl.Buffered(1))


def params(limit):
    return pltpu.CompilerParams(vmem_limit_bytes=limit)


def whole_weight(sc, step, own, far, weight):
    @pl.when(step == 0)
    def _():
        weight[:, pl.ds(pl.multiple_of(sc[CORE] * SIDE, 128), SIDE)] = own[...]
        weight[:, pl.ds(pl.multiple_of((1 - sc[CORE]) * SIDE, 128), SIDE)] = far[...]


def values_kernel(sc, tok, gain, w_own, w_far, out, weight):
    step = pl.program_id(0)
    whole_weight(sc, step, w_own, w_far, weight)
    rows = tok.shape[1]
    position = step * rows + lax.broadcasted_iota(jnp.int32, (rows, 1), 0)
    for item in range(2):
        x = tok[item].astype(F32)
        scale = lax.rsqrt(jnp.mean(x * x, axis=-1, keepdims=True) + EPSILON)
        normed = (x * scale * gain[...]).astype(BF16)
        found = dot(normed, weight[...], 1, 0)
        found = jnp.where(position < sc[LENGTHS + item], found, 0.0).astype(BF16)
        for head in range(HEADS):
            out[head, :, item * HEAD : (item + 1) * HEAD] = found[:, head * HEAD : (head + 1) * HEAD]


def run_values(sc, tokens, gain, w_own, w_far):
    rows = 256
    return pl.pallas_call(
        values_kernel,
        grid_spec=pltpu.PrefetchScalarGridSpec(
            num_scalar_prefetch=1,
            grid=(LMAX // rows,),
            in_specs=[
                spec((2, rows, WIDTH), lambda j, s: (0, j, 0)),
                held((1, WIDTH)),
                held((WIDTH, SIDE)),
                held((WIDTH, SIDE)),
            ],
            out_specs=spec((HEADS, rows, 2 * HEAD), lambda j, s: (0, j, 0)),
            scratch_shapes=[pltpu.VMEM((WIDTH, WIDTH), BF16)],
        ),
        out_shape=jax.ShapeDtypeStruct((HEADS, LMAX, 2 * HEAD), BF16),
        compiler_params=params(VMEM),
        cost_estimate=pl.CostEstimate(
            flops=2 * 2 * LMAX * WIDTH * WIDTH, bytes_accessed=8 * LMAX * WIDTH, transcendentals=0
        ),
        name="values",
    )(sc, tokens, gain, w_own, w_far)


def lane_lengths(sc, shape):
    slot = lax.broadcasted_iota(jnp.int32, shape, 1) // HEAD
    length = jnp.where(slot == 0, sc[LENGTHS], sc[LENGTHS + 1])
    return jnp.where(slot >= 2, jnp.where(slot == 2, sc[LENGTHS + 2], sc[LENGTHS + 3]), length)


def plane_of(k, sc):
    return lax.rem(sc[PLANE] + PLANES - k, PLANES)


def plane_spec(planes, rows, lanes):
    def index(step, sc):
        return (plane_of(planes[0] + step * (planes[1] - planes[0]), sc), 0, 0)

    return spec((PHEADS, rows, lanes), index)


def anywhere(count):
    return [pl.BlockSpec(memory_space=pl.ANY)] * count


def plane_fetch(place, shards, raw, sems, slot):
    return [
        pltpu.make_async_copy(
            shards[4 * slot + rel],
            raw.at[slot, pl.ds(pl.multiple_of((place ^ rel) * SUBS * HALF, SUBS * HALF), SUBS * HALF)],
            sems.at[slot, rel],
        )
        for rel in range(4)
    ]


def take_plane(place, shards, raw, sems):
    step = pl.program_id(0)

    @pl.when(step == 0)
    def _():
        for slot in range(2):
            for copy in plane_fetch(place, shards, raw, sems, slot):
                copy.start()

    for slot in range(2):

        @pl.when(step == slot)
        def _():
            for copy in plane_fetch(place, shards, raw, sems, slot):
                copy.wait()

    return step


def head_rows(head):
    return slice(head * HROWS, (head + 1) * HROWS)


def fill_mask(sc, mask):
    @pl.when(pl.program_id(0) == 0)
    def _():
        shape = (LMAX, 4 * HEAD)
        column = lax.broadcasted_iota(jnp.int32, shape, 0)
        mask[...] = (column < lane_lengths(sc, shape)).astype(F32).astype(BF16)


def inverse_sums(sc, weights, mask):
    shape = (HROWS, 4 * HEAD)
    line = lax.broadcasted_iota(jnp.int32, shape, 0)
    position = 128 * (line // HALF) + HALF * sc[CORE] + line % HALF
    return jnp.where(position < lane_lengths(sc, shape), 1.0 / dot(weights, mask[...], 1, 0), 0.0)


def mix_kernel(carried, sc, *refs):
    shards, (v_own, v_far, *rest) = refs[:8], refs[8:]
    mixed, mean, raw, mask, sems = rest[2:] if carried else rest
    fill_mask(sc, mask)
    slot = take_plane(sc[PLACE], shards, raw, sems)
    for head in range(PHEADS):
        weights = jnp.exp(raw[slot, head_rows(head)].astype(F32)).astype(BF16)
        values = jnp.concatenate([v_own[head], v_far[head]], axis=1)
        found = dot(weights, values, 1, 0) * inverse_sums(sc, weights, mask)
        mean[head] = found
        mixed[head] = found.astype(BF16)


def run_mix(sc, planes, shards, v_own, v_far, carry):
    carry = list(carry)
    return pl.pallas_call(
        partial(mix_kernel, bool(carry)),
        grid_spec=pltpu.PrefetchScalarGridSpec(
            num_scalar_prefetch=1,
            grid=(2,),
            in_specs=anywhere(8) + [plane_spec(planes, LMAX, 2 * HEAD)] * 2 + anywhere(len(carry)),
            out_specs=[plane_spec(planes, HROWS, 4 * HEAD)] * 2,
            scratch_shapes=[
                pltpu.VMEM((2, 4 * SUBS * HALF, LMAX), BF16),
                pltpu.VMEM((LMAX, 4 * HEAD), BF16),
                pltpu.SemaphoreType.DMA((2, 4)),
            ],
        ),
        out_shape=[
            jax.ShapeDtypeStruct((HEADS, HROWS, 4 * HEAD), BF16),
            jax.ShapeDtypeStruct((HEADS, HROWS, 4 * HEAD), F32),
        ],
        input_output_aliases={11 + i: i for i in range(len(carry))},
        compiler_params=params(VMEM),
        cost_estimate=pl.CostEstimate(
            flops=2 * HEADS * HROWS * LMAX * 4 * HEAD,
            bytes_accessed=HEADS * (HROWS * LMAX + 5 * HROWS * 256),
            transcendentals=HEADS * HROWS * LMAX // 2,
        ),
        name="mix",
    )(sc, *shards, v_own, v_far, *carry)


def row_valid(sc, step):
    line = lax.broadcasted_iota(jnp.int32, (4 * SPAN, 1), 0)
    item = line // SPAN
    row = step * SPAN + line % SPAN
    low = jnp.where(item == 0, sc[LENGTHS], sc[LENGTHS + 1])
    high = jnp.where(item == 2, sc[LENGTHS + 2], sc[LENGTHS + 3])
    return 128 * (row // HALF) + HALF * sc[CORE] + row % HALF < jnp.where(item >= 2, high, low)


def four_items(own, far):
    return jnp.concatenate([own[:, :, 0], far[...]], axis=0).reshape(4 * SPAN, WIDTH)


def pre_kernel(sc, tok, tok_far, cot, cot_far, heads, wo_own, wo_far, gain, mixed, resid, normed, grad, weight):
    step = pl.program_id(0)
    whole_weight(sc, step, wo_own, wo_far, weight)
    for item in range(4):
        lanes = slice(item * HEAD, (item + 1) * HEAD)
        for pair in range(HEADS // 2):
            both = jnp.concatenate([heads[2 * pair, :, lanes], heads[2 * pair + 1, :, lanes]], axis=1)
            mixed[item, :, pair * 128 : (pair + 1) * 128] = both
    res = four_items(tok, tok_far).astype(F32) + dot(mixed[...].reshape(4 * SPAN, WIDTH), weight[...], 1, 0)
    resid[...] = res.astype(BF16).reshape(4, SPAN, WIDTH)
    scale = lax.rsqrt(jnp.mean(res * res, axis=-1, keepdims=True) + EPSILON)
    valid = row_valid(sc, step)
    normed[...] = jnp.where(valid, res * scale * gain[...], 0.0).astype(BF16).reshape(4, SPAN, WIDTH)
    masked = jnp.where(valid, four_items(cot, cot_far).astype(F32), 0.0)
    grad[...] = masked.astype(BF16).reshape(4, SPAN, WIDTH)


def slab_spec(items=4):
    return spec((items, SPAN, WIDTH), lambda r, s: (0, r, 0))


def half_specs():
    return [
        spec((2, SPAN // HALF, 1, HALF, WIDTH), lambda r, s: (0, r, s[CORE], 0, 0)),
        spec((2, SPAN // HALF, HALF, WIDTH), lambda r, s: (0, r, 0, 0)),
    ]


def heads_spec():
    return spec((HEADS, SPAN, 4 * HEAD), lambda r, s: (0, r, 0))


def run_pre(sc, tokens, tokens_far, cotangent, cotangent_far, heads, wo, gain):
    return pl.pallas_call(
        pre_kernel,
        grid_spec=pltpu.PrefetchScalarGridSpec(
            num_scalar_prefetch=1,
            grid=(HROWS // SPAN,),
            in_specs=half_specs()
            + half_specs()
            + [heads_spec(), held((WIDTH, SIDE)), held((WIDTH, SIDE)), held((1, WIDTH))],
            out_specs=[slab_spec()] * 4,
            scratch_shapes=[pltpu.VMEM((WIDTH, WIDTH), BF16)],
        ),
        out_shape=[
            jax.ShapeDtypeStruct((4, HROWS, WIDTH), BF16),
            jax.ShapeDtypeStruct((4, HROWS, WIDTH), BF16),
            jax.ShapeDtypeStruct((4, HROWS, WIDTH), BF16),
            jax.ShapeDtypeStruct((4, HROWS, WIDTH), BF16),
        ],
        compiler_params=params(VMEM),
        cost_estimate=pl.CostEstimate(
            flops=2 * ROWS * WIDTH * WIDTH, bytes_accessed=16 * ROWS * WIDTH, transcendentals=0
        ),
        name="pre",
    )(sc, tokens, tokens_far, cotangent, cotangent_far, heads, *wo, gain)


def own_lanes(sc):
    return pl.ds(pl.multiple_of(sc[CORE] * SIDE, 128), SIDE)


def far_lanes(sc):
    return pl.ds(pl.multiple_of((1 - sc[CORE]) * SIDE, 128), SIDE)


def unit_rows(f, sc):
    return (lax.rem(FSIDE * sc[CORE] + f, 2 * FSIDE), 0)


def unit_columns(f, sc):
    return (0, lax.rem(FSIDE * sc[CORE] + f, 2 * FSIDE))


def early(f, sc):
    return (0, lax.min(f, FSIDE - 1))


def late(f, sc):
    return (0, lax.max(f - FSIDE, 0))


def units_kernel(sc, normed, cot, up_own, up_far, dn_own, dn_far, active, up_grad, back, w_up, w_down, total):
    step = pl.program_id(0)
    w_down[:, own_lanes(sc)] = dn_own[...]
    w_down[:, far_lanes(sc)] = dn_far[...]

    @pl.when(step < FSIDE)
    def _():
        w_up[...] = up_own[...]

    @pl.when(step >= FSIDE)
    def _():
        w_up[...] = up_far[...]

    for piece in range(ROWS // TILE):
        whole = slice(piece * TILE, (piece + 1) * TILE)
        for row in range(piece * TILE, (piece + 1) * TILE, 256):
            rows = slice(row, row + 256)
            for column in range(0, FSTEP, 256):
                columns = slice(column, column + 256)
                up = dot(normed[rows], w_up[:, columns], 1, 0)
                square = up * up
                bend = jnp.tanh(up * (0.7978845608028654 + (0.044715 * 0.7978845608028654) * square))
                share = 0.5 + 0.5 * bend
                act = up * share
                active[rows, columns] = act.astype(BF16)
                slope = share + act * (1.0 - share) * (
                    2 * 0.7978845608028654 + (6 * 0.044715 * 0.7978845608028654) * square
                )
                up_grad[rows, columns] = (dot(cot[rows], w_down[columns], 1, 1) * slope).astype(BF16)
        two_grad = dot(up_grad[whole], w_up[...], 1, 1)

        @pl.when(step == 0)
        def _():
            total[whole] = two_grad

        @pl.when((step > 0) & (step < 2 * FSIDE - 1))
        def _():
            total[whole] += two_grad

        @pl.when(step == 2 * FSIDE - 1)
        def _():
            back[whole] = (total[whole] + two_grad).astype(BF16)


def run_units(sc, normed, cotangent, up, down):
    return pl.pallas_call(
        units_kernel,
        grid_spec=pltpu.PrefetchScalarGridSpec(
            num_scalar_prefetch=1,
            grid=(2 * FSIDE,),
            in_specs=[
                held((ROWS, WIDTH)),
                held((ROWS, WIDTH)),
                spec((WIDTH, FSTEP), early),
                spec((WIDTH, FSTEP), late),
                spec((FSTEP, SIDE), unit_rows),
                spec((FSTEP, SIDE), unit_rows),
            ],
            out_specs=[spec((ROWS, FSTEP), unit_columns), spec((ROWS, FSTEP), unit_columns), held((ROWS, WIDTH))],
            scratch_shapes=[
                pltpu.VMEM((WIDTH, FSTEP), BF16),
                pltpu.VMEM((FSTEP, WIDTH), BF16),
                pltpu.VMEM((ROWS, WIDTH), F32),
            ],
        ),
        out_shape=[
            jax.ShapeDtypeStruct((ROWS, FF), BF16),
            jax.ShapeDtypeStruct((ROWS, FF), BF16),
            jax.ShapeDtypeStruct((ROWS, WIDTH), BF16),
        ],
        compiler_params=params(VMEM),
        cost_estimate=pl.CostEstimate(
            flops=6 * ROWS * WIDTH * FF, bytes_accessed=8 * ROWS * WIDTH + 4 * ROWS * FF, transcendentals=ROWS * FF
        ),
        name="units",
    )(sc, normed.reshape(ROWS, WIDTH), cotangent.reshape(ROWS, WIDTH), *up, *down)


def down_grad_kernel(sc, active, cot, own, far, total):
    total[...] = dot(active[...], cot[...], 0, 0).astype(BF16)
    own[...] = total[:, own_lanes(sc)]
    far[...] = total[:, far_lanes(sc)]


def run_down_grad(sc, active, cotangent):
    return pl.pallas_call(
        down_grad_kernel,
        grid_spec=pltpu.PrefetchScalarGridSpec(
            num_scalar_prefetch=1,
            grid=(FF // 512,),
            in_specs=[spec((ROWS, 512), lambda f, s: (0, f)), held((ROWS, WIDTH))],
            out_specs=[spec((512, SIDE), lambda f, s: (f, 0))] * 2,
            scratch_shapes=[pltpu.VMEM((512, WIDTH), BF16)],
        ),
        out_shape=[jax.ShapeDtypeStruct((FF, SIDE), BF16)] * 2,
        compiler_params=params(VMEM),
        cost_estimate=pl.CostEstimate(
            flops=2 * ROWS * WIDTH * FF, bytes_accessed=2 * ROWS * (WIDTH + FF), transcendentals=0
        ),
        name="down_grad",
    )(sc, active, cotangent.reshape(ROWS, WIDTH))


def up_grad_kernel(sc, normed, up_grad, own, far):
    total = dot(normed[...], up_grad[...], 0, 0).astype(BF16)

    @pl.when(pl.program_id(0) < FSIDE)
    def _():
        own[...] = total

    @pl.when(pl.program_id(0) >= FSIDE)
    def _():
        far[...] = total


def run_up_grad(sc, normed, up_grad):
    return pl.pallas_call(
        up_grad_kernel,
        grid_spec=pltpu.PrefetchScalarGridSpec(
            num_scalar_prefetch=1,
            grid=(2 * FSIDE,),
            in_specs=[held((ROWS, WIDTH)), spec((ROWS, FSTEP), unit_columns)],
            out_specs=[spec((WIDTH, FSTEP), early), spec((WIDTH, FSTEP), late)],
        ),
        out_shape=[jax.ShapeDtypeStruct((WIDTH, FF // 2), BF16)] * 2,
        compiler_params=params(VMEM),
        cost_estimate=pl.CostEstimate(
            flops=2 * ROWS * WIDTH * FF, bytes_accessed=2 * ROWS * (WIDTH + FF), transcendentals=0
        ),
        name="up_grad",
    )(sc, normed.reshape(ROWS, WIDTH), up_grad)


def out_kernel(sc, active, resid, dn_own, dn_far, own, far, w_down):
    step = pl.program_id(0)

    @pl.when(step == 0)
    def _():
        w_down[:, own_lanes(sc)] = dn_own[...]
        w_down[:, far_lanes(sc)] = dn_far[...]

    branch = dot(active[...].reshape(4 * SPAN, FF), w_down[...], 1, 0)
    output = jnp.where(row_valid(sc, step), resid[...].reshape(4 * SPAN, WIDTH).astype(F32) + branch, 0.0)
    output = output.astype(BF16).reshape(4, SPAN, WIDTH)
    own[...] = output[:2]
    far[...] = output[2:]


def run_out(sc, active, resid, down):
    return pl.pallas_call(
        out_kernel,
        grid_spec=pltpu.PrefetchScalarGridSpec(
            num_scalar_prefetch=1,
            grid=(HROWS // SPAN,),
            in_specs=[
                spec((4, SPAN, FF), lambda r, s: (0, r, 0)),
                slab_spec(),
                held((FF, SIDE)),
                held((FF, SIDE)),
            ],
            out_specs=[slab_spec(2)] * 2,
            scratch_shapes=[pltpu.VMEM((FF, WIDTH), BF16)],
        ),
        out_shape=[
            jax.ShapeDtypeStruct((2, HROWS, WIDTH), BF16),
            jax.ShapeDtypeStruct((2, HROWS, WIDTH), BF16),
        ],
        compiler_params=params(VMEM),
        cost_estimate=pl.CostEstimate(
            flops=2 * ROWS * WIDTH * FF, bytes_accessed=ROWS * (2 * FF + 7 * WIDTH), transcendentals=0
        ),
        name="out",
    )(sc, active.reshape(4, HROWS, FF), resid, *down)


def post_kernel(sc, resid, back, cot, mixed, wo_own, wo_far, gain, *refs):
    (res_own, res_far, heads, d_out_own, d_out_far, d_gain, weight, total, spread) = refs
    step = pl.program_id(0)
    whole_weight(sc, step, wo_own, wo_far, weight)
    shape, slab = (4 * SPAN, WIDTH), (4, SPAN, WIDTH)
    valid = row_valid(sc, step)
    res = resid[...].reshape(shape).astype(F32)
    scale = lax.rsqrt(jnp.mean(res * res, axis=-1, keepdims=True) + EPSILON)
    unit = res * scale
    two_grad = jnp.where(valid, back[...].reshape(shape).astype(F32), 0.0)
    gained = two_grad * gain[...]
    masked = cot[...].reshape(shape).astype(F32)
    grad = masked + scale * (gained - unit * jnp.mean(gained * unit, axis=-1, keepdims=True))
    low = grad.astype(BF16)
    res_own[...] = low.reshape(slab)[:2]
    res_far[...] = low.reshape(slab)[2:]
    gain_sum = jnp.sum(two_grad * unit, axis=0, keepdims=True)
    out_sum = dot(mixed[...].reshape(shape), low, 0, 0)

    @pl.when(step == 0)
    def _():
        d_gain[...] = gain_sum
        total[...] = out_sum

    @pl.when(step > 0)
    def _():
        d_gain[...] += gain_sum
        total[...] += out_sum

    spread[...] = dot(low, weight[...], 1, 1).astype(BF16).reshape(slab)
    for pair in range(HEADS // 2):
        lanes = slice(pair * 128, (pair + 1) * 128)
        for side in range(2):
            one, two = spread[2 * side, :, lanes], spread[2 * side + 1, :, lanes]
            half = slice(side * 128, (side + 1) * 128)
            heads[2 * pair, :, half] = jnp.concatenate([one[:, :HEAD], two[:, :HEAD]], axis=1)
            heads[2 * pair + 1, :, half] = jnp.concatenate([one[:, HEAD:], two[:, HEAD:]], axis=1)

    @pl.when(step == pl.num_programs(0) - 1)
    def _():
        weight[...] = total[...].astype(BF16)
        d_out_own[...] = weight[:, own_lanes(sc)]
        d_out_far[...] = weight[:, far_lanes(sc)]


def run_post(sc, resid, back, cotangent, mixed, wo, gain):
    whole = (4, HROWS, WIDTH)
    return pl.pallas_call(
        post_kernel,
        grid_spec=pltpu.PrefetchScalarGridSpec(
            num_scalar_prefetch=1,
            grid=(HROWS // SPAN,),
            in_specs=[slab_spec()] * 4 + [held((WIDTH, SIDE)), held((WIDTH, SIDE)), held((1, WIDTH))],
            out_specs=[slab_spec(2)] * 2
            + [heads_spec(), held((WIDTH, SIDE)), held((WIDTH, SIDE)), held((1, WIDTH))],
            scratch_shapes=[
                pltpu.VMEM((WIDTH, WIDTH), BF16),
                pltpu.VMEM((WIDTH, WIDTH), F32),
                pltpu.VMEM((4, SPAN, WIDTH), BF16),
            ],
        ),
        out_shape=[
            jax.ShapeDtypeStruct((2, HROWS, WIDTH), BF16),
            jax.ShapeDtypeStruct((2, HROWS, WIDTH), BF16),
            jax.ShapeDtypeStruct((HEADS, HROWS, 4 * HEAD), BF16),
            jax.ShapeDtypeStruct((WIDTH, SIDE), BF16),
            jax.ShapeDtypeStruct((WIDTH, SIDE), BF16),
            jax.ShapeDtypeStruct((1, WIDTH), F32),
        ],
        compiler_params=params(VMEM),
        cost_estimate=pl.CostEstimate(
            flops=4 * ROWS * WIDTH * WIDTH, bytes_accessed=28 * ROWS * WIDTH, transcendentals=0
        ),
        name="post",
    )(sc, resid, back.reshape(whole), cotangent, mixed, *wo, gain)


def unmix_kernel(carried, sc, *refs):
    shards, (v_own, v_far, grad_heads, mean, *rest) = refs[:8], refs[8:]
    rest = rest[2:] if carried else rest
    outs, (own, far, raw, grads, mask, adder, bound, sems, out_sems) = rest[:8], rest[8:]
    place = sc[PLACE]
    step = pl.program_id(0)

    def leave(slot):
        return [
            pltpu.make_async_copy(
                grads.at[slot, pl.ds(pl.multiple_of((place ^ rel) * SUBS * HALF, SUBS * HALF), SUBS * HALF)],
                outs[4 * slot + rel],
                out_sems.at[slot, rel],
            )
            for rel in range(4)
        ]

    fill_mask(sc, mask)

    @pl.when(step == 0)
    def _():
        lane = lax.broadcasted_iota(jnp.int32, (4 * HEAD, 128), 0) // HEAD
        column = lax.broadcasted_iota(jnp.int32, (4 * HEAD, 128), 1)
        adder[...] = jnp.where((lane == column) | (lane + 4 == column), -1.0, 0.0).astype(BF16)
        row = lax.broadcasted_iota(jnp.int32, (LMAX, 128), 0)
        item = lax.broadcasted_iota(jnp.int32, (LMAX, 128), 1)
        length = jnp.where(item % 4 == 0, sc[LENGTHS], sc[LENGTHS + 1])
        length = jnp.where(item % 4 == 2, sc[LENGTHS + 2], length)
        length = jnp.where(item % 4 == 3, sc[LENGTHS + 3], length)
        bound[...] = jnp.where((item < 8) & (row < length), 1.0, 0.0).astype(BF16)

    slot = take_plane(place, shards, raw, sems)
    high_lanes = lax.broadcasted_iota(jnp.int32, (HROWS, 128), 1) < 4
    for head in range(PHEADS):
        weights = jnp.exp(raw[slot, head_rows(head)].astype(F32)).astype(BF16)
        low = (grad_heads[head].astype(F32) * inverse_sums(sc, weights, mask)).astype(BF16)
        product = low.astype(F32) * mean[head]
        coarse = product.astype(BF16)
        fine = (product - coarse.astype(F32)).astype(BF16)
        delta = dot(coarse, adder[...], 1, 0) + dot(fine, adder[...], 1, 0)
        coarse = delta.astype(BF16)
        fine = (delta - coarse.astype(F32)).astype(BF16)
        left = jnp.concatenate([low, jnp.where(high_lanes, coarse, fine)], axis=1)
        score = dot(left, jnp.concatenate([v_own[head], v_far[head], bound[...]], axis=1), 1, 1)
        grads[slot, head_rows(head)] = (score * weights.astype(F32)).astype(BF16)
        back = (dot(weights, low, 0, 0) * mask[...].astype(F32)).astype(BF16)
        own[head] = back[:, : 2 * HEAD]
        far[head] = back[:, 2 * HEAD :]
    for which in range(2):

        @pl.when(step == which)
        def _():
            for copy in leave(which):
                copy.start()
            if which == 1:
                for copy in leave(0) + leave(1):
                    copy.wait()


def run_unmix(sc, planes, shards, v_own, v_far, grad_heads, mean, carry):
    carry = list(carry)
    return pl.pallas_call(
        partial(unmix_kernel, bool(carry)),
        grid_spec=pltpu.PrefetchScalarGridSpec(
            num_scalar_prefetch=1,
            grid=(2,),
            in_specs=anywhere(8)
            + [plane_spec(planes, LMAX, 2 * HEAD)] * 2
            + [plane_spec(planes, HROWS, 4 * HEAD)] * 2
            + anywhere(len(carry)),
            out_specs=anywhere(8) + [plane_spec(planes, LMAX, 2 * HEAD)] * 2,
            scratch_shapes=[
                pltpu.VMEM((2, 4 * SUBS * HALF, LMAX), BF16),
                pltpu.VMEM((2, 4 * SUBS * HALF, LMAX), BF16),
                pltpu.VMEM((LMAX, 4 * HEAD), BF16),
                pltpu.VMEM((4 * HEAD, 128), BF16),
                pltpu.VMEM((LMAX, 128), BF16),
                pltpu.SemaphoreType.DMA((2, 4)),
                pltpu.SemaphoreType.DMA((2, 4)),
            ],
        ),
        out_shape=[jax.ShapeDtypeStruct((SUBS * HALF, LMAX), BF16)] * 8
        + [jax.ShapeDtypeStruct((HEADS, LMAX, 2 * HEAD), BF16)] * 2,
        input_output_aliases={13 + i: 8 + i for i in range(len(carry))},
        compiler_params=params(VMEM),
        cost_estimate=pl.CostEstimate(
            flops=3 * HEADS * HROWS * LMAX * 4 * HEAD,
            bytes_accessed=HEADS * (2 * HROWS * LMAX + 4 * HROWS * 256 + 4 * LMAX * 256),
            transcendentals=HEADS * HROWS * LMAX // 2,
        ),
        name="unmix",
    )(sc, *shards, v_own, v_far, grad_heads, mean, *carry)


def close_kernel(sc, tok, res_own, res_got, out_own, out_got, own, far, gain, w_own, w_far, *refs):
    (output, tok_grad, d_value, d_gain, total, weight) = refs
    step = pl.program_id(0)
    whole_weight(sc, step, w_own, w_far, weight)
    core = sc[CORE]
    output[:, :, core] = out_own[...].astype(F32)
    output[:, :, 1 - core] = out_got[...].astype(F32)
    tok_grad[:, :, core] = res_own[...].astype(F32)
    tok_grad[:, :, 1 - core] = res_got[...].astype(F32)
    runs = tok.shape[1]
    rows = runs * 128
    for item in range(2):
        lanes = slice(item * HEAD, (item + 1) * HEAD)
        pieces = [
            add_low(own[head, :, lanes], far[head, :, lanes]) for head in range(HEADS)
        ]
        back = jnp.concatenate(pieces, axis=1)
        x = tok[item].reshape(rows, WIDTH).astype(F32)
        scale = lax.rsqrt(jnp.mean(x * x, axis=-1, keepdims=True) + EPSILON)
        unit = x * scale
        normed = (unit * gain[...]).astype(BF16)
        normed_grad = dot(back, weight[...], 1, 1)
        gained = normed_grad * gain[...]
        update = scale * (gained - unit * jnp.mean(gained * unit, axis=-1, keepdims=True))
        tok_grad[item] += update.reshape(runs, 2, HALF, WIDTH)
        gain_sum = jnp.sum(normed_grad * unit, axis=0, keepdims=True)
        value_sum = dot(normed, back, 0, 0)
        if item == 0:
            gain_total, value_total = gain_sum, value_sum
        else:
            gain_total, value_total = gain_total + gain_sum, value_total + value_sum

    @pl.when(step == 0)
    def _():
        d_gain[...] = gain_total
        total[...] = value_total

    @pl.when(step > 0)
    def _():
        d_gain[...] += gain_total
        total[...] += value_total

    @pl.when(step == pl.num_programs(0) - 1)
    def _():
        low = total[...].astype(BF16)
        d_value[0] = low[:, :SIDE]
        d_value[1] = low[:, SIDE:]


def run_close(sc, tokens, res_own, res_got, out_own, out_got, own, far, gain, w_own, w_far):
    runs = 2
    slab = (2, RUNS, 2, HALF, WIDTH)
    half = (2, RUNS, HALF, WIDTH)
    whole_spec = spec((2, runs, 2, HALF, WIDTH), lambda j, s: (0, j, 0, 0, 0))
    half_spec = spec((2, runs, HALF, WIDTH), lambda j, s: (0, j, 0, 0))
    back_spec = spec((HEADS, runs * 128, 2 * HEAD), lambda j, s: (0, j, 0))
    return pl.pallas_call(
        close_kernel,
        grid_spec=pltpu.PrefetchScalarGridSpec(
            num_scalar_prefetch=1,
            grid=(RUNS // runs,),
            in_specs=[whole_spec]
            + [half_spec] * 4
            + [back_spec, back_spec, held((1, WIDTH)), held((WIDTH, SIDE)), held((WIDTH, SIDE))],
            out_specs=[whole_spec, whole_spec, held((2, WIDTH, SIDE)), held((1, WIDTH))],
            scratch_shapes=[pltpu.VMEM((WIDTH, WIDTH), F32), pltpu.VMEM((WIDTH, WIDTH), BF16)],
        ),
        out_shape=[
            jax.ShapeDtypeStruct(slab, F32),
            jax.ShapeDtypeStruct(slab, F32),
            jax.ShapeDtypeStruct((2, WIDTH, SIDE), BF16),
            jax.ShapeDtypeStruct((1, WIDTH), F32),
        ],
        compiler_params=params(VMEM),
        cost_estimate=pl.CostEstimate(
            flops=4 * 2 * LMAX * WIDTH * WIDTH, bytes_accessed=38 * LMAX * WIDTH, transcendentals=0
        ),
        name="close",
    )(
        sc,
        tokens.reshape(slab),
        *(x.reshape(half) for x in (res_own, res_got, out_own, out_got)),
        own,
        far,
        gain,
        w_own,
        w_far,
    )


PACK_DOWN, PACK_UP, PACK_OUT, PACK_VALUE, PACK_GAIN, PACK = 0, 192, 384, 432, 480, 496


def pack_kernel(sc, down, up, out, value, gain, down_far, up_far, out_far, value_far, gain_far, packed):
    first = sc[CORE] == 0

    def both(own, far, lanes):
        own, far = own[:, lanes], far[:, lanes]
        return jnp.concatenate([jnp.where(first, own, far), jnp.where(first, far, own)], axis=0)

    def side(own, far):
        return both(own, far, own_lanes(sc))

    packed[PACK_DOWN:PACK_UP] = side(down, down_far)
    for j in range(4):
        lanes = pl.ds(pl.multiple_of((4 * sc[CORE] + j) * SIDE, 128), SIDE)
        packed[PACK_UP + 48 * j : PACK_UP + 48 * (j + 1)] = both(up, up_far, lanes)
    packed[PACK_OUT:PACK_VALUE] = side(out, out_far)
    packed[PACK_VALUE:PACK_GAIN] = side(value, value_far)
    packed[PACK_GAIN:] = both(gain, gain_far, slice(0, SIDE))


def run_pack(sc, own, far):
    return pl.pallas_call(
        pack_kernel,
        grid_spec=pltpu.PrefetchScalarGridSpec(
            num_scalar_prefetch=1,
            grid=(1,),
            in_specs=[held(x.shape) for x in (*own, *far)],
            out_specs=held((PACK, SIDE)),
        ),
        out_shape=jax.ShapeDtypeStruct((PACK, SIDE), BF16),
        compiler_params=params(VMEM),
        cost_estimate=pl.CostEstimate(flops=0, bytes_accessed=6 * PACK * SIDE, transcendentals=0),
        name="pack",
    )(sc, *own, *far)


def chip_of(sc, k, rel):
    return plane_of(k, sc) * 4 + (sc[PLACE] ^ rel)


def place_kernel(moves, sc, *refs):
    pieces, targets, sems = refs[:16], refs[16:-1], refs[-1]
    copies = []
    for index, piece in enumerate(pieces):
        chip = chip_of(sc, index // 4, index % 4)
        for which, (start, count, lane, target, step, offset, column) in enumerate(moves):
            rows = pl.ds(pl.multiple_of(chip * step + offset, 16), count)
            copies.append(
                pltpu.make_async_copy(
                    piece.at[pl.ds(start, count), pl.ds(lane, SIDE)],
                    targets[target].at[rows, pl.ds(column, SIDE)],
                    sems.at[index, which],
                )
            )
    for copy in copies:
        copy.start()
    for copy in copies:
        copy.wait()


def run_place(sc, pieces, moves, shapes):
    return pl.pallas_call(
        partial(place_kernel, moves),
        grid_spec=pltpu.PrefetchScalarGridSpec(
            num_scalar_prefetch=1,
            grid=(1,),
            in_specs=anywhere(16),
            out_specs=[held(shape) for shape in shapes],
            scratch_shapes=[pltpu.SemaphoreType.DMA((16, len(moves)))],
        ),
        out_shape=[jax.ShapeDtypeStruct(shape, BF16) for shape in shapes],
        compiler_params=params(VMEM),
        cost_estimate=pl.CostEstimate(
            flops=0, bytes_accessed=4 * sum(a * b for a, b in shapes), transcendentals=0
        ),
        name="place",
    )(sc, *pieces)


def place_weights(sc, pieces):
    moves = (
        (PACK_DOWN, 192, 0, 0, 192, 0, 0),
        *((PACK_UP + 48 * j, 48, 0, 1, 48, 0, j * SIDE) for j in range(4)),
        (PACK_OUT, 48, 0, 2, 48, 0, 0),
        (PACK_VALUE, 48, 0, 3, 48, 0, 0),
        (PACK_GAIN, 16, 0, 4, 16, 0, 0),
    )
    shapes = [(FF, SIDE), (WIDTH, FF // 2), (WIDTH, SIDE), (WIDTH, SIDE), (256, SIDE)]
    return run_place(sc, pieces, moves, shapes)


def collect_kernel(sc, *refs):
    outs = refs[24:]
    for k in range(PLANES):

        @pl.when(pl.program_id(0) == k)
        def _():
            for rel in range(4):
                down, down_got, up, up_got, out, out_got = refs[6 * rel : 6 * rel + 6]
                packed = outs[4 * k + rel]
                packed[PACK_DOWN:PACK_UP] = add_low(down[...], down_got[...])
                for j in range(4):
                    lanes = slice(j * SIDE, (j + 1) * SIDE)
                    packed[PACK_UP + 48 * j : PACK_UP + 48 * (j + 1)] = add_low(up[:, lanes], up_got[:, lanes])
                packed[PACK_OUT:PACK_VALUE] = add_low(out[...], out_got[...])


def run_collect(sc, *sides):
    def rows(x, rel):
        return spec((x.shape[0] // 16, x.shape[1]), lambda k, s: (chip_of(s, k, rel), 0))

    return pl.pallas_call(
        collect_kernel,
        grid_spec=pltpu.PrefetchScalarGridSpec(
            num_scalar_prefetch=1,
            grid=(PLANES,),
            in_specs=[rows(x, rel) for rel in range(4) for x in sides],
            out_specs=[held((PACK_VALUE, SIDE))] * 16,
        ),
        out_shape=[jax.ShapeDtypeStruct((PACK_VALUE, SIDE), BF16)] * 16,
        compiler_params=params(VMEM),
        cost_estimate=pl.CostEstimate(flops=0, bytes_accessed=3 * 16 * PACK_VALUE * SIDE * 2, transcendentals=0),
        name="collect",
    )(sc, *(x for _ in range(4) for x in sides))


def add_kernel(groups, *refs):
    for group, total in zip(groups, refs[-len(groups) :]):
        value = refs[group[0]][...].astype(F32)
        for index in group[1:]:
            value = value + refs[index][...].astype(F32)
        total[...] = value.astype(total.dtype)


def run_add(groups, values, dtype):
    rows, columns = values[0].shape
    parts = 2 if columns == LMAX else 1
    block = pl.BlockSpec((rows // parts, columns), lambda i: (i, 0))
    return pl.pallas_call(
        partial(add_kernel, groups),
        grid=(parts,),
        in_specs=[block] * len(values),
        out_specs=[block] * len(groups),
        out_shape=[jax.ShapeDtypeStruct((rows, columns), dtype)] * len(groups),
        compiler_params=params(VMEM),
        cost_estimate=pl.CostEstimate(
            flops=0, bytes_accessed=2 * rows * columns * (len(values) + len(groups)), transcendentals=0
        ),
        name="add",
    )(*values)


DEVICES = 32
TO_CORE, TO_X, TO_Y = 1, 2, 4


def swap(x, bit):
    return lax.ppermute(x, BOTH, [(d, d ^ bit) for d in range(DEVICES)])


def ring(x, way=1):
    return lax.ppermute(x, BOTH, [(d, (d + 8 * way) % DEVICES) for d in range(DEVICES)])


def pick(x, index, axis=0):
    return lax.dynamic_index_in_dim(x, index, axis, keepdims=False)


def ordered(flag, one, two, axis=0, joined=jnp.stack):
    return jnp.where(flag == 0, joined([one, two], axis), joined([two, one], axis))


def add_low(one, two):
    return (one.astype(F32) + two.astype(F32)).astype(BF16)


STEPS = (
    ((0, 0, 1), (0, 1, 0), (1, 0, 0)),
    ((1, 0, 1), (0, 1, 1), (2, 0, 0)),
    ((2, 0, 1), (1, 1, 0), (3, 0, 0)),
    ((3, 0, 1), (2, 1, 0), (1, 1, 1)),
    ((2, 1, 1), (3, 1, 1), (3, 1, 0)),
)


def gather_step(have, step):
    by_x, by_y, by_z = STEPS[step]
    return {
        **have,
        by_z: ring(have[by_z[0] - 1, by_z[1], by_z[2]]),
        by_x: swap(have[by_x[0], by_x[1], 0], TO_X),
        by_y: swap(have[by_y[0], 0, by_y[2]], TO_Y),
    }


def in_order(have):
    return [have[k, y, x] for k in range(4) for y in range(2) for x in range(2)]


def by_place(shares, planes=range(PLANES)):
    return {(k, i // 2, i % 2): shares[4 * at + i] for at, k in enumerate(planes) for i in range(4)}


def scatter_send(have, step):
    by_x, by_y, by_z = STEPS[len(STEPS) - 1 - step]
    got = (ring(have[by_z], -1), swap(have[by_x], TO_X), swap(have[by_y], TO_Y))
    return {at: value for at, value in have.items() if at not in (by_x, by_y, by_z)}, got


def scatter_add(have, got, step):
    by_x, by_y, by_z = STEPS[len(STEPS) - 1 - step]
    targets = ((by_z[0] - 1, by_z[1], by_z[2]), (by_x[0], by_x[1], 0), (by_y[0], 0, by_y[2]))
    sums = list(dict.fromkeys(targets))
    groups = [(len(got) + i, *(j for j in range(len(got)) if targets[j] == at)) for i, at in enumerate(sums)]
    values = [*got, *(have[at] for at in sums)]
    return {**have, **dict(zip(sums, run_add(groups, values, F32 if step == len(STEPS) - 1 else BF16)))}


together = lax.optimization_barrier


def chip_shards(tokens, lengths, rand_mix, w_value, w_out, w_up, w_down, gain_mix, gain_ffn, grad_out):
    wide = lax.axis_index("wide")
    core = lax.axis_index("narrow")
    z, y, x = wide // 4, (wide // 2) % 2, wide % 2
    other = lambda value: swap(value, TO_CORE)
    side = partial(ordered, core, joined=jnp.concatenate)
    slab = (2, RUNS, 2, HALF, WIDTH)
    tokens, grad_out = tokens.reshape(slab), grad_out.reshape(slab)

    gains = jnp.pad(jnp.concatenate([gain_mix, gain_ffn])[None], ((0, 7), (0, SIDE - 48)))
    own = (w_down, w_up, w_out, w_value, gains)
    far = tuple(other(value) for value in own)
    near_sc = jnp.concatenate([jnp.stack([core, z, wide % 4]).astype(jnp.int32), lengths, lengths])
    weights = {(0, 0, 0): run_pack(near_sc, own, far)}

    rand = rand_mix.reshape(3, 2, HALF, LMAX)
    blocks = side(pick(rand, core, 1), other(pick(rand, 1 - core, 1)), 0)
    weights, rands, far_lengths = together(
        (gather_step(weights, 0), {(0, 0, 0): blocks.reshape(SUBS * HALF, LMAX)}, other(lengths))
    )
    sc = jnp.concatenate([near_sc[:5], far_lengths])
    weights, tokens_far = together((gather_step(weights, 1), other(pick(tokens, 1 - core, 2))))
    weights, grad_far = together((gather_step(weights, 2), other(pick(grad_out, 1 - core, 2))))
    rands, weights = together((gather_step(rands, 0), gather_step(weights, 3)))
    rands, weights = together((gather_step(rands, 1), gather_step(weights, 4)))

    down, up, out, value, gain_rows = place_weights(sc, in_order(weights))
    value_far = other(value)
    gain_rows = gain_rows.reshape(16, 2, 8, SIDE)[:, :, 0]
    gain_one = gain_rows[..., :24].reshape(1, WIDTH).astype(F32)
    gain_two = gain_rows[..., 24:48].reshape(1, WIDTH).astype(F32)
    v_own = run_values(sc, tokens.reshape(2, LMAX, WIDTH), gain_one, value, value_far)
    rands, value_far, v_own, gain_one, gain_two, out, down, up = together(
        (gather_step(rands, 2), value_far, v_own, gain_one, gain_two, out, down, up)
    )
    rands, v_far, out = together((gather_step(rands, 3), other(v_own), (out, other(out))))
    near = [rands[k, y_at, x_at] for k in range(2) for y_at in range(2) for x_at in range(2)]
    mixing = run_mix(sc, (0, 1), near, v_own, v_far, ())
    rands, up, down, mixing = together((gather_step(rands, 4), (up, other(up)), (down, other(down)), mixing))
    shares = in_order(rands)
    heads, mean = run_mix(sc, (2, 3), shares[8:], v_own, v_far, mixing)

    mixed, resid, normed, masked = run_pre(sc, tokens, tokens_far, grad_out, grad_far, heads, out, gain_two)
    active, up_grad, back = run_units(sc, normed, masked, up, down)
    res_own, res_far, grad_heads, d_out_own, d_out_far, d_gain_two = run_post(
        sc, resid, back, masked, mixed, out, gain_two
    )

    *far, back_own, back_far = run_unmix(
        sc, (3, 2), shares[12:] + shares[8:12], v_own, v_far, grad_heads, mean, ()
    )
    have, got = scatter_send(by_place(far, (3, 2)), 0)
    *near, back_own, back_far = run_unmix(
        sc, (1, 0), shares[4:8] + shares[:4], v_own, v_far, grad_heads, mean, (back_own, back_far)
    )
    have, got, near, back_own, back_far, res_got, d_out_got = together(
        (have, got, near, back_own, back_far, other(res_far), other(d_out_far))
    )
    have = {**scatter_add(have, got, 0), **by_place(near, (1, 0))}

    have, got = scatter_send(have, 1)
    up_own, up_far = run_up_grad(sc, normed, up_grad)
    have, got, up_own, up_far, back_got = together((have, got, up_own, up_far, other(back_far)))
    have = scatter_add(have, got, 1)

    have, got = scatter_send(have, 2)
    down_own, down_far = run_down_grad(sc, active, masked)
    have, got, down_own, down_far, up_got = together((have, got, down_own, down_far, other(up_far)))
    have = scatter_add(have, got, 2)

    have, got = scatter_send(have, 3)
    packed = run_collect(sc, down_own, other(down_far), up_own, up_got, d_out_own, d_out_got)
    sums, sums_got = scatter_send(by_place(packed), 0)
    out_own, out_far = run_out(sc, active, resid, down)
    have, got, sums, sums_got, out_own, out_far = together((have, got, sums, sums_got, out_own, out_far))
    have, sums = scatter_add(have, got, 3), scatter_add(sums, sums_got, 0)

    have, got = scatter_send(have, 4)
    sums, sums_got = scatter_send(sums, 1)
    sums, sums_got = scatter_send(scatter_add(sums, sums_got, 1), 2)
    output, tokens_grad, d_value, d_gain_one = run_close(
        sc, tokens, res_own, res_got, out_own, other(out_far), back_own, back_got, gain_one, value, value_far
    )
    gain_pair = jnp.concatenate([d_gain_one, d_gain_two]).reshape(2, 16, 1, 48).astype(BF16)
    gain_pair = jnp.pad(gain_pair, ((0, 0), (0, 0), (0, 15), (0, SIDE - 48)))
    small = jnp.concatenate([d_value.reshape(2, 16, 48, SIDE), gain_pair], 2)
    small = add_low(pick(small, core), other(pick(small, 1 - core))).reshape(4, 2, 2, 64, SIDE)
    have, got, sums, sums_got, small, output, tokens_grad = together(
        (have, got, sums, sums_got, small, output, tokens_grad)
    )
    rand_sum = scatter_add(have, got, 4)[0, 0, 0].reshape(2, 3, HALF, LMAX)
    sums = scatter_add(sums, sums_got, 2)

    sums, sums_got = scatter_send(sums, 3)
    small = add_low(pick(small, x, 2), swap(pick(small, 1 - x, 2), TO_X))
    blocks, blocks_far = pick(rand_sum, core), other(pick(rand_sum, 1 - core))
    sums, sums_got, small, blocks, blocks_far = together((sums, sums_got, small, blocks, blocks_far))
    sums = scatter_add(sums, sums_got, 3)

    sums, sums_got = scatter_send(sums, 4)
    small = add_low(pick(small, y, 1), swap(pick(small, 1 - y, 1), TO_Y))
    sums, sums_got, small = together((sums, sums_got, small))
    big_sum = scatter_add(sums, sums_got, 4)[0, 0, 0]

    small_sum = pick(small, z).astype(F32)
    for k in range(1, PLANES):
        small_sum = small_sum + ring(pick(small, lax.rem(z + PLANES - k, PLANES)), -k).astype(F32)
    big_far, small_far = other(big_sum), other(small_sum)

    rows_of = lambda value, rows: pick(value.reshape(-1, 2, rows, SIDE), core, 1)
    mine = lambda own, far, rows: side(rows_of(own, rows)[0], rows_of(far, rows)[0], 1)
    down_shard = mine(big_sum[PACK_DOWN:PACK_UP], big_far[PACK_DOWN:PACK_UP], 96)
    up_side = lambda value: rows_of(value[PACK_UP:PACK_OUT], 24).transpose(1, 0, 2).reshape(24, 4 * SIDE)
    up_shard = side(up_side(big_sum), up_side(big_far), 1)
    outproj_shard = mine(big_sum[PACK_OUT:PACK_VALUE], big_far[PACK_OUT:PACK_VALUE], 24)
    value_shard = mine(small_sum[:48], small_far[:48], 24)
    gains_pair = ordered(core, small_sum[48, :48], small_far[48, :48])
    gain_pair = pick(gains_pair.reshape(2, 2, 24), core, 1)

    rand_shard = ordered(core, blocks, blocks_far, 1)

    return (
        output.reshape(2, LMAX, WIDTH),
        tokens_grad.reshape(2, LMAX, WIDTH),
        rand_shard.reshape(3 * 128, LMAX),
        value_shard,
        outproj_shard,
        up_shard,
        down_shard,
        gain_pair[0],
        gain_pair[1],
    )


def rms_norm(values, gain):
    scale = lax.rsqrt(jnp.mean(values * values, axis=-1, keepdims=True) + EPSILON)
    return values * scale * gain


def split_heads(block):
    return block.reshape(LMAX, HEADS, HEAD).transpose(1, 0, 2)


def merge_heads(block):
    return block.transpose(1, 0, 2).reshape(LMAX, HEADS * HEAD)


def masked_scores(key_mask, rand_head):
    return jnp.where(key_mask[None, :] > 0, rand_head.astype(jnp.float32), -1e30)


def head_forward(key_mask, paired):
    rand_head, value_head = paired
    scores = masked_scores(key_mask, rand_head)
    row_peak = jnp.max(scores, axis=-1, keepdims=True)
    exponent = jnp.exp(scores - row_peak)
    denom_sum = jnp.sum(exponent, axis=-1, keepdims=True)
    attention = exponent / denom_sum * key_mask[:, None]
    mixed = jnp.dot(attention.astype(jnp.bfloat16), value_head, preferred_element_type=jnp.float32)
    return (mixed.astype(jnp.bfloat16), row_peak + jnp.log(denom_sum))


def head_backward(key_mask, paired):
    rand_head, value_head, mix_grad, log_total = paired
    scores = masked_scores(key_mask, rand_head)
    attention = jnp.exp(scores - log_total) * key_mask[:, None]
    prob_grad = jnp.einsum("id,jd->ij", mix_grad, value_head, preferred_element_type=jnp.float32)
    value_grad = jnp.einsum(
        "ij,id->jd", attention.astype(jnp.bfloat16), mix_grad, preferred_element_type=jnp.float32
    )
    score_grad = attention * (prob_grad - jnp.sum(prob_grad * attention, axis=-1, keepdims=True))
    return (score_grad, value_grad)


def shards(tokens, lengths, rand_mix, w_value, w_out, w_up, w_down, gain_mix, gain_ffn, grad_out):
    item_count = tokens.shape[0]
    width = tokens.shape[2]
    row_count = item_count * LMAX
    tokens_flat = tokens.reshape(row_count, width).astype(jnp.float32)
    positions = jnp.arange(LMAX, dtype=jnp.int32)
    valid_table = (positions[None, :] < lengths[:, None]).astype(jnp.float32)
    row_valid = valid_table.reshape(row_count, 1)
    forward_set = (
        lax.all_gather(rand_mix, ("wide", "narrow"), axis=0, tiled=True),
        lax.all_gather(w_value, ("wide", "narrow"), axis=0, tiled=True),
        lax.all_gather(w_out, ("wide", "narrow"), axis=0, tiled=True),
        lax.all_gather(w_up, ("wide", "narrow"), axis=0, tiled=True),
        lax.all_gather(w_down, ("wide", "narrow"), axis=0, tiled=True),
        lax.all_gather(gain_mix, ("wide", "narrow"), axis=0, tiled=True),
        lax.all_gather(gain_ffn, ("wide", "narrow"), axis=0, tiled=True),
    )
    rand_all, value_all, out_all, up_all, down_all, gain_first, gain_second = forward_set
    normed = rms_norm(tokens_flat, gain_first.astype(jnp.float32)).astype(jnp.bfloat16)
    values = jnp.dot(normed, value_all, preferred_element_type=jnp.float32).astype(jnp.bfloat16)
    rand_heads = rand_all.reshape(HEADS, LMAX, LMAX)
    mixed_parts = []
    totals_kept = []
    for item_index in range(item_count):
        item_values = split_heads(values[item_index * LMAX : (item_index + 1) * LMAX])
        mixed_heads, log_total = lax.map(
            partial(head_forward, valid_table[item_index]), (rand_heads, item_values)
        )
        mixed_parts.append(merge_heads(mixed_heads))
        totals_kept.append(log_total)
    mixed = jnp.concatenate(mixed_parts, axis=0)
    residual = tokens_flat + jnp.dot(mixed, out_all, preferred_element_type=jnp.float32)
    normed_two = rms_norm(residual, gain_second.astype(jnp.float32)).astype(jnp.bfloat16)
    up_proj = jnp.dot(normed_two, up_all, preferred_element_type=jnp.float32)
    active = jax.nn.gelu(up_proj).astype(jnp.bfloat16)
    branch = jnp.dot(active, down_all, preferred_element_type=jnp.float32)
    output = row_valid * (residual + branch)
    back_set = (
        lax.all_gather(rand_mix, ("wide", "narrow"), axis=0, tiled=True),
        lax.all_gather(w_value, ("wide", "narrow"), axis=0, tiled=True),
        lax.all_gather(w_out, ("wide", "narrow"), axis=0, tiled=True),
        lax.all_gather(w_up, ("wide", "narrow"), axis=0, tiled=True),
        lax.all_gather(w_down, ("wide", "narrow"), axis=0, tiled=True),
        lax.all_gather(gain_mix, ("wide", "narrow"), axis=0, tiled=True),
        lax.all_gather(gain_ffn, ("wide", "narrow"), axis=0, tiled=True),
    )
    rand_back, value_back, out_back, up_back, down_back, gain_back_one, gain_back_two = back_set
    cotangent = grad_out.reshape(row_count, width).astype(jnp.float32)
    masked = row_valid * cotangent
    branch_grad = masked.astype(jnp.bfloat16)
    grad_down = jnp.einsum("rk,rd->kd", active, branch_grad, preferred_element_type=jnp.float32)
    active_grad = jnp.einsum(
        "rd,kd->rk", branch_grad, down_back, preferred_element_type=jnp.float32
    )
    gelu_value, gelu_pull = jax.vjp(jax.nn.gelu, up_proj)
    up_grad = gelu_pull(active_grad)[0].astype(jnp.bfloat16)
    grad_up = jnp.einsum("rd,rk->dk", normed_two, up_grad, preferred_element_type=jnp.float32)
    normed_two_grad = jnp.einsum("rk,dk->rd", up_grad, up_back, preferred_element_type=jnp.float32)
    norm_value, norm_pull = jax.vjp(rms_norm, residual, gain_back_two.astype(jnp.float32))
    residual_part, gain_two_grad = norm_pull(normed_two_grad)
    residual_grad = masked + residual_part
    attn_grad = residual_grad.astype(jnp.bfloat16)
    grad_outproj = jnp.einsum("rd,re->de", mixed, attn_grad, preferred_element_type=jnp.float32)
    mixed_grad = jnp.einsum(
        "re,de->rd", attn_grad, out_back, preferred_element_type=jnp.float32
    ).astype(jnp.bfloat16)
    rand_heads_back = rand_back.reshape(HEADS, LMAX, LMAX)
    rand_grad = jnp.zeros((HEADS, LMAX, LMAX), jnp.float32)
    value_parts = []
    for item_index in range(item_count):
        lower_row = item_index * LMAX
        upper_row = lower_row + LMAX
        item_values = split_heads(values[lower_row:upper_row])
        item_mix_grad = split_heads(mixed_grad[lower_row:upper_row])
        score_grad, value_grad = lax.map(
            partial(head_backward, valid_table[item_index]),
            (rand_heads_back, item_values, item_mix_grad, totals_kept[item_index]),
        )
        rand_grad = rand_grad + score_grad
        value_parts.append(merge_heads(value_grad))
    values_grad = jnp.concatenate(value_parts, axis=0).astype(jnp.bfloat16)
    grad_value = jnp.einsum("rd,re->de", normed, values_grad, preferred_element_type=jnp.float32)
    normed_grad = jnp.einsum(
        "re,de->rd", values_grad, value_back, preferred_element_type=jnp.float32
    )
    norm_first, first_pull = jax.vjp(rms_norm, tokens_flat, gain_back_one.astype(jnp.float32))
    token_part, gain_one_grad = first_pull(normed_grad)
    tokens_grad = residual_grad + token_part
    rand_flat = rand_grad.reshape(HEADS * LMAX, LMAX)
    all_shards = (
        lax.psum_scatter(rand_flat, ("wide", "narrow"), scatter_dimension=0, tiled=True),
        lax.psum_scatter(grad_value, ("wide", "narrow"), scatter_dimension=0, tiled=True),
        lax.psum_scatter(grad_outproj, ("wide", "narrow"), scatter_dimension=0, tiled=True),
        lax.psum_scatter(grad_up, ("wide", "narrow"), scatter_dimension=0, tiled=True),
        lax.psum_scatter(grad_down, ("wide", "narrow"), scatter_dimension=0, tiled=True),
        lax.psum_scatter(gain_one_grad, ("wide", "narrow"), scatter_dimension=0, tiled=True),
        lax.psum_scatter(gain_two_grad, ("wide", "narrow"), scatter_dimension=0, tiled=True),
    )
    rand_shard, value_shard, outproj_shard, up_shard, down_shard, gain_one_shard, gain_two_shard = (
        all_shards
    )
    return (
        output.reshape(item_count, LMAX, width),
        tokens_grad.reshape(item_count, LMAX, width),
        rand_shard,
        value_shard,
        outproj_shard,
        up_shard,
        down_shard,
        gain_one_shard,
        gain_two_shard,
    )


def solution(mesh):
    in_specs = (
        P(("wide", "narrow"), None, None),
        P(("wide", "narrow")),
        P(("wide", "narrow"), None),
        P(("wide", "narrow"), None),
        P(("wide", "narrow"), None),
        P(("wide", "narrow"), None),
        P(("wide", "narrow"), None),
        P(("wide", "narrow")),
        P(("wide", "narrow")),
        P(("wide", "narrow"), None, None),
    )
    out_specs = (
        P(("wide", "narrow"), None, None),
        P(("wide", "narrow"), None, None),
        P(("wide", "narrow"), None),
        P(("wide", "narrow"), None),
        P(("wide", "narrow"), None),
        P(("wide", "narrow"), None),
        P(("wide", "narrow"), None),
        P(("wide", "narrow")),
        P(("wide", "narrow")),
    )
    fits = dict(mesh.shape) == {"wide": 16, "narrow": 2}
    return jax.shard_map(chip_shards if fits else shards, mesh=mesh, in_specs=in_specs, out_specs=out_specs, check_vma=False)
```

```python
from functools import partial

import jax
import jax.numpy as jnp
from jax import lax
from jax.experimental import pallas as pl
from jax.experimental.pallas import tpu as pltpu
from jax.sharding import PartitionSpec as P

HEADS = 12
HEAD = 64
LMAX = 1024
WIDTH = 768
FF = 3072
EPSILON = 1e-05

BOTH = ("wide", "narrow")
BF16 = jnp.bfloat16
F32 = jnp.float32
VMEM = 61 << 20

SUBS = 6
RUNS = 8
HALF = 64
HROWS = RUNS * HALF
PLANES = 4
PHEADS = HEADS // PLANES
ROWS = 2 * LMAX
FSTEP = 768
FSIDE = FF // 2 // FSTEP
TILE = 512
SIDE = WIDTH // 2
SPAN = 2 * HALF


def dot(a, b, ca, cb):
    return lax.dot_general(a, b, (((ca,), (cb,)), ((), ())), preferred_element_type=F32)


CORE, PLANE, PLACE, LENGTHS = 0, 1, 2, 3


def spec(shape, index):
    return pl.BlockSpec(shape, index)


def held(shape):
    zeros = (0,) * len(shape)
    return pl.BlockSpec(shape, lambda *_: zeros, pipeline_mode=pl.Buffered(1))


def params(limit):
    return pltpu.CompilerParams(vmem_limit_bytes=limit)


def whole_weight(sc, step, own, far, weight):
    @pl.when(step == 0)
    def _():
        weight[:, pl.ds(pl.multiple_of(sc[CORE] * SIDE, 128), SIDE)] = own[...]
        weight[:, pl.ds(pl.multiple_of((1 - sc[CORE]) * SIDE, 128), SIDE)] = far[...]


def values_kernel(sc, tok, gain, w_own, w_far, out, weight):
    step = pl.program_id(0)
    whole_weight(sc, step, w_own, w_far, weight)
    rows = tok.shape[1]
    position = step * rows + lax.broadcasted_iota(jnp.int32, (rows, 1), 0)
    for item in range(2):
        x = tok[item].astype(F32)
        scale = lax.rsqrt(jnp.mean(x * x, axis=-1, keepdims=True) + EPSILON)
        normed = (x * scale * gain[...]).astype(BF16)
        found = dot(normed, weight[...], 1, 0)
        found = jnp.where(position < sc[LENGTHS + item], found, 0.0).astype(BF16)
        for head in range(HEADS):
            out[head, :, item * HEAD : (item + 1) * HEAD] = found[:, head * HEAD : (head + 1) * HEAD]


def run_values(sc, tokens, gain, w_own, w_far):
    rows = 256
    return pl.pallas_call(
        values_kernel,
        grid_spec=pltpu.PrefetchScalarGridSpec(
            num_scalar_prefetch=1,
            grid=(LMAX // rows,),
            in_specs=[
                spec((2, rows, WIDTH), lambda j, s: (0, j, 0)),
                held((1, WIDTH)),
                held((WIDTH, SIDE)),
                held((WIDTH, SIDE)),
            ],
            out_specs=spec((HEADS, rows, 2 * HEAD), lambda j, s: (0, j, 0)),
            scratch_shapes=[pltpu.VMEM((WIDTH, WIDTH), BF16)],
        ),
        out_shape=jax.ShapeDtypeStruct((HEADS, LMAX, 2 * HEAD), BF16),
        compiler_params=params(VMEM),
        cost_estimate=pl.CostEstimate(
            flops=2 * 2 * LMAX * WIDTH * WIDTH, bytes_accessed=8 * LMAX * WIDTH, transcendentals=0
        ),
        name="values",
    )(sc, tokens, gain, w_own, w_far)


def lane_lengths(sc, shape):
    slot = lax.broadcasted_iota(jnp.int32, shape, 1) // HEAD
    length = jnp.where(slot == 0, sc[LENGTHS], sc[LENGTHS + 1])
    return jnp.where(slot >= 2, jnp.where(slot == 2, sc[LENGTHS + 2], sc[LENGTHS + 3]), length)


def plane_of(k, sc):
    return lax.rem(sc[PLANE] + PLANES - k, PLANES)


def plane_spec(planes, rows, lanes):
    def index(step, sc):
        return (plane_of(planes[0] + step * (planes[1] - planes[0]), sc), 0, 0)

    return spec((PHEADS, rows, lanes), index)


def anywhere(count):
    return [pl.BlockSpec(memory_space=pl.ANY)] * count


def plane_fetch(place, shards, raw, sems, slot):
    return [
        pltpu.make_async_copy(
            shards[4 * slot + rel],
            raw.at[slot, pl.ds(pl.multiple_of((place ^ rel) * SUBS * HALF, SUBS * HALF), SUBS * HALF)],
            sems.at[slot, rel],
        )
        for rel in range(4)
    ]


def take_plane(place, shards, raw, sems):
    step = pl.program_id(0)

    @pl.when(step == 0)
    def _():
        for slot in range(2):
            for copy in plane_fetch(place, shards, raw, sems, slot):
                copy.start()

    for slot in range(2):

        @pl.when(step == slot)
        def _():
            for copy in plane_fetch(place, shards, raw, sems, slot):
                copy.wait()

    return step


def head_rows(head):
    return slice(head * HROWS, (head + 1) * HROWS)


def fill_mask(sc, mask):
    @pl.when(pl.program_id(0) == 0)
    def _():
        shape = (LMAX, 4 * HEAD)
        column = lax.broadcasted_iota(jnp.int32, shape, 0)
        mask[...] = (column < lane_lengths(sc, shape)).astype(F32).astype(BF16)


def inverse_sums(sc, weights, mask):
    shape = (HROWS, 4 * HEAD)
    line = lax.broadcasted_iota(jnp.int32, shape, 0)
    position = 128 * (line // HALF) + HALF * sc[CORE] + line % HALF
    return jnp.where(position < lane_lengths(sc, shape), 1.0 / dot(weights, mask[...], 1, 0), 0.0)


def mix_kernel(carried, sc, *refs):
    shards, (v_own, v_far, *rest) = refs[:8], refs[8:]
    mixed, mean, raw, mask, sems = rest[2:] if carried else rest
    fill_mask(sc, mask)
    slot = take_plane(sc[PLACE], shards, raw, sems)
    for head in range(PHEADS):
        weights = jnp.exp(raw[slot, head_rows(head)].astype(F32)).astype(BF16)
        values = jnp.concatenate([v_own[head], v_far[head]], axis=1)
        found = dot(weights, values, 1, 0) * inverse_sums(sc, weights, mask)
        mean[head] = found
        mixed[head] = found.astype(BF16)


def run_mix(sc, planes, shards, v_own, v_far, carry):
    carry = list(carry)
    return pl.pallas_call(
        partial(mix_kernel, bool(carry)),
        grid_spec=pltpu.PrefetchScalarGridSpec(
            num_scalar_prefetch=1,
            grid=(2,),
            in_specs=anywhere(8) + [plane_spec(planes, LMAX, 2 * HEAD)] * 2 + anywhere(len(carry)),
            out_specs=[plane_spec(planes, HROWS, 4 * HEAD)] * 2,
            scratch_shapes=[
                pltpu.VMEM((2, 4 * SUBS * HALF, LMAX), BF16),
                pltpu.VMEM((LMAX, 4 * HEAD), BF16),
                pltpu.SemaphoreType.DMA((2, 4)),
            ],
        ),
        out_shape=[
            jax.ShapeDtypeStruct((HEADS, HROWS, 4 * HEAD), BF16),
            jax.ShapeDtypeStruct((HEADS, HROWS, 4 * HEAD), F32),
        ],
        input_output_aliases={11 + i: i for i in range(len(carry))},
        compiler_params=params(VMEM),
        cost_estimate=pl.CostEstimate(
            flops=2 * HEADS * HROWS * LMAX * 4 * HEAD,
            bytes_accessed=HEADS * (HROWS * LMAX + 5 * HROWS * 256),
            transcendentals=HEADS * HROWS * LMAX // 2,
        ),
        name="mix",
    )(sc, *shards, v_own, v_far, *carry)


def row_valid(sc, step):
    line = lax.broadcasted_iota(jnp.int32, (4 * SPAN, 1), 0)
    item = line // SPAN
    row = step * SPAN + line % SPAN
    low = jnp.where(item == 0, sc[LENGTHS], sc[LENGTHS + 1])
    high = jnp.where(item == 2, sc[LENGTHS + 2], sc[LENGTHS + 3])
    return 128 * (row // HALF) + HALF * sc[CORE] + row % HALF < jnp.where(item >= 2, high, low)


def four_items(own, far):
    return jnp.concatenate([own[:, :, 0], far[...]], axis=0).reshape(4 * SPAN, WIDTH)


def pre_kernel(sc, tok, tok_far, cot, cot_far, heads, wo_own, wo_far, gain, mixed, resid, normed, grad, weight):
    step = pl.program_id(0)
    whole_weight(sc, step, wo_own, wo_far, weight)
    for item in range(4):
        lanes = slice(item * HEAD, (item + 1) * HEAD)
        for pair in range(HEADS // 2):
            both = jnp.concatenate([heads[2 * pair, :, lanes], heads[2 * pair + 1, :, lanes]], axis=1)
            mixed[item, :, pair * 128 : (pair + 1) * 128] = both
    res = four_items(tok, tok_far).astype(F32) + dot(mixed[...].reshape(4 * SPAN, WIDTH), weight[...], 1, 0)
    resid[...] = res.astype(BF16).reshape(4, SPAN, WIDTH)
    scale = lax.rsqrt(jnp.mean(res * res, axis=-1, keepdims=True) + EPSILON)
    valid = row_valid(sc, step)
    normed[...] = jnp.where(valid, res * scale * gain[...], 0.0).astype(BF16).reshape(4, SPAN, WIDTH)
    masked = jnp.where(valid, four_items(cot, cot_far).astype(F32), 0.0)
    grad[...] = masked.astype(BF16).reshape(4, SPAN, WIDTH)


def slab_spec(items=4):
    return spec((items, SPAN, WIDTH), lambda r, s: (0, r, 0))


def half_specs():
    return [
        spec((2, SPAN // HALF, 1, HALF, WIDTH), lambda r, s: (0, r, s[CORE], 0, 0)),
        spec((2, SPAN // HALF, HALF, WIDTH), lambda r, s: (0, r, 0, 0)),
    ]


def heads_spec():
    return spec((HEADS, SPAN, 4 * HEAD), lambda r, s: (0, r, 0))


def run_pre(sc, tokens, tokens_far, cotangent, cotangent_far, heads, wo, gain):
    return pl.pallas_call(
        pre_kernel,
        grid_spec=pltpu.PrefetchScalarGridSpec(
            num_scalar_prefetch=1,
            grid=(HROWS // SPAN,),
            in_specs=half_specs()
            + half_specs()
            + [heads_spec(), held((WIDTH, SIDE)), held((WIDTH, SIDE)), held((1, WIDTH))],
            out_specs=[slab_spec()] * 4,
            scratch_shapes=[pltpu.VMEM((WIDTH, WIDTH), BF16)],
        ),
        out_shape=[
            jax.ShapeDtypeStruct((4, HROWS, WIDTH), BF16),
            jax.ShapeDtypeStruct((4, HROWS, WIDTH), BF16),
            jax.ShapeDtypeStruct((4, HROWS, WIDTH), BF16),
            jax.ShapeDtypeStruct((4, HROWS, WIDTH), BF16),
        ],
        compiler_params=params(VMEM),
        cost_estimate=pl.CostEstimate(
            flops=2 * ROWS * WIDTH * WIDTH, bytes_accessed=16 * ROWS * WIDTH, transcendentals=0
        ),
        name="pre",
    )(sc, tokens, tokens_far, cotangent, cotangent_far, heads, *wo, gain)


def own_lanes(sc):
    return pl.ds(pl.multiple_of(sc[CORE] * SIDE, 128), SIDE)


def far_lanes(sc):
    return pl.ds(pl.multiple_of((1 - sc[CORE]) * SIDE, 128), SIDE)


def unit_rows(f, sc):
    return (lax.rem(FSIDE * sc[CORE] + f, 2 * FSIDE), 0)


def unit_columns(f, sc):
    return (0, lax.rem(FSIDE * sc[CORE] + f, 2 * FSIDE))


def early(f, sc):
    return (0, lax.min(f, FSIDE - 1))


def late(f, sc):
    return (0, lax.max(f - FSIDE, 0))


def units_kernel(sc, normed, cot, up_own, up_far, dn_own, dn_far, active, up_grad, back, w_up, w_down, total):
    step = pl.program_id(0)
    w_down[:, own_lanes(sc)] = dn_own[...]
    w_down[:, far_lanes(sc)] = dn_far[...]

    @pl.when(step < FSIDE)
    def _():
        w_up[...] = up_own[...]

    @pl.when(step >= FSIDE)
    def _():
        w_up[...] = up_far[...]

    for piece in range(ROWS // TILE):
        whole = slice(piece * TILE, (piece + 1) * TILE)
        for row in range(piece * TILE, (piece + 1) * TILE, 256):
            rows = slice(row, row + 256)
            for column in range(0, FSTEP, 256):
                columns = slice(column, column + 256)
                up = dot(normed[rows], w_up[:, columns], 1, 0)
                square = up * up
                bend = jnp.tanh(up * (0.7978845608028654 + (0.044715 * 0.7978845608028654) * square))
                share = 0.5 + 0.5 * bend
                act = up * share
                active[rows, columns] = act.astype(BF16)
                slope = share + act * (1.0 - share) * (
                    2 * 0.7978845608028654 + (6 * 0.044715 * 0.7978845608028654) * square
                )
                up_grad[rows, columns] = (dot(cot[rows], w_down[columns], 1, 1) * slope).astype(BF16)
        two_grad = dot(up_grad[whole], w_up[...], 1, 1)

        @pl.when(step == 0)
        def _():
            total[whole] = two_grad

        @pl.when((step > 0) & (step < 2 * FSIDE - 1))
        def _():
            total[whole] += two_grad

        @pl.when(step == 2 * FSIDE - 1)
        def _():
            back[whole] = (total[whole] + two_grad).astype(BF16)


def run_units(sc, normed, cotangent, up, down):
    return pl.pallas_call(
        units_kernel,
        grid_spec=pltpu.PrefetchScalarGridSpec(
            num_scalar_prefetch=1,
            grid=(2 * FSIDE,),
            in_specs=[
                held((ROWS, WIDTH)),
                held((ROWS, WIDTH)),
                spec((WIDTH, FSTEP), early),
                spec((WIDTH, FSTEP), late),
                spec((FSTEP, SIDE), unit_rows),
                spec((FSTEP, SIDE), unit_rows),
            ],
            out_specs=[spec((ROWS, FSTEP), unit_columns), spec((ROWS, FSTEP), unit_columns), held((ROWS, WIDTH))],
            scratch_shapes=[
                pltpu.VMEM((WIDTH, FSTEP), BF16),
                pltpu.VMEM((FSTEP, WIDTH), BF16),
                pltpu.VMEM((ROWS, WIDTH), F32),
            ],
        ),
        out_shape=[
            jax.ShapeDtypeStruct((ROWS, FF), BF16),
            jax.ShapeDtypeStruct((ROWS, FF), BF16),
            jax.ShapeDtypeStruct((ROWS, WIDTH), BF16),
        ],
        compiler_params=params(VMEM),
        cost_estimate=pl.CostEstimate(
            flops=6 * ROWS * WIDTH * FF, bytes_accessed=8 * ROWS * WIDTH + 4 * ROWS * FF, transcendentals=ROWS * FF
        ),
        name="units",
    )(sc, normed.reshape(ROWS, WIDTH), cotangent.reshape(ROWS, WIDTH), *up, *down)


def down_grad_kernel(sc, active, cot, own, far, total):
    total[...] = dot(active[...], cot[...], 0, 0).astype(BF16)
    own[...] = total[:, own_lanes(sc)]
    far[...] = total[:, far_lanes(sc)]


def run_down_grad(sc, active, cotangent):
    return pl.pallas_call(
        down_grad_kernel,
        grid_spec=pltpu.PrefetchScalarGridSpec(
            num_scalar_prefetch=1,
            grid=(FF // 512,),
            in_specs=[spec((ROWS, 512), lambda f, s: (0, f)), held((ROWS, WIDTH))],
            out_specs=[spec((512, SIDE), lambda f, s: (f, 0))] * 2,
            scratch_shapes=[pltpu.VMEM((512, WIDTH), BF16)],
        ),
        out_shape=[jax.ShapeDtypeStruct((FF, SIDE), BF16)] * 2,
        compiler_params=params(VMEM),
        cost_estimate=pl.CostEstimate(
            flops=2 * ROWS * WIDTH * FF, bytes_accessed=2 * ROWS * (WIDTH + FF), transcendentals=0
        ),
        name="down_grad",
    )(sc, active, cotangent.reshape(ROWS, WIDTH))


def up_grad_kernel(sc, normed, up_grad, own, far):
    total = dot(normed[...], up_grad[...], 0, 0).astype(BF16)

    @pl.when(pl.program_id(0) < FSIDE)
    def _():
        own[...] = total

    @pl.when(pl.program_id(0) >= FSIDE)
    def _():
        far[...] = total


def run_up_grad(sc, normed, up_grad):
    return pl.pallas_call(
        up_grad_kernel,
        grid_spec=pltpu.PrefetchScalarGridSpec(
            num_scalar_prefetch=1,
            grid=(2 * FSIDE,),
            in_specs=[held((ROWS, WIDTH)), spec((ROWS, FSTEP), unit_columns)],
            out_specs=[spec((WIDTH, FSTEP), early), spec((WIDTH, FSTEP), late)],
        ),
        out_shape=[jax.ShapeDtypeStruct((WIDTH, FF // 2), BF16)] * 2,
        compiler_params=params(VMEM),
        cost_estimate=pl.CostEstimate(
            flops=2 * ROWS * WIDTH * FF, bytes_accessed=2 * ROWS * (WIDTH + FF), transcendentals=0
        ),
        name="up_grad",
    )(sc, normed.reshape(ROWS, WIDTH), up_grad)


def out_kernel(sc, active, resid, dn_own, dn_far, own, far, w_down):
    step = pl.program_id(0)

    @pl.when(step == 0)
    def _():
        w_down[:, own_lanes(sc)] = dn_own[...]
        w_down[:, far_lanes(sc)] = dn_far[...]

    branch = dot(active[...].reshape(4 * SPAN, FF), w_down[...], 1, 0)
    output = jnp.where(row_valid(sc, step), resid[...].reshape(4 * SPAN, WIDTH).astype(F32) + branch, 0.0)
    output = output.astype(BF16).reshape(4, SPAN, WIDTH)
    own[...] = output[:2]
    far[...] = output[2:]


def run_out(sc, active, resid, down):
    return pl.pallas_call(
        out_kernel,
        grid_spec=pltpu.PrefetchScalarGridSpec(
            num_scalar_prefetch=1,
            grid=(HROWS // SPAN,),
            in_specs=[
                spec((4, SPAN, FF), lambda r, s: (0, r, 0)),
                slab_spec(),
                held((FF, SIDE)),
                held((FF, SIDE)),
            ],
            out_specs=[slab_spec(2)] * 2,
            scratch_shapes=[pltpu.VMEM((FF, WIDTH), BF16)],
        ),
        out_shape=[
            jax.ShapeDtypeStruct((2, HROWS, WIDTH), BF16),
            jax.ShapeDtypeStruct((2, HROWS, WIDTH), BF16),
        ],
        compiler_params=params(VMEM),
        cost_estimate=pl.CostEstimate(
            flops=2 * ROWS * WIDTH * FF, bytes_accessed=ROWS * (2 * FF + 7 * WIDTH), transcendentals=0
        ),
        name="out",
    )(sc, active.reshape(4, HROWS, FF), resid, *down)


def post_kernel(sc, resid, back, cot, mixed, wo_own, wo_far, gain, *refs):
    (res_own, res_far, heads, d_out_own, d_out_far, d_gain, weight, total, spread) = refs
    step = pl.program_id(0)
    whole_weight(sc, step, wo_own, wo_far, weight)
    shape, slab = (4 * SPAN, WIDTH), (4, SPAN, WIDTH)
    valid = row_valid(sc, step)
    res = resid[...].reshape(shape).astype(F32)
    scale = lax.rsqrt(jnp.mean(res * res, axis=-1, keepdims=True) + EPSILON)
    unit = res * scale
    two_grad = jnp.where(valid, back[...].reshape(shape).astype(F32), 0.0)
    gained = two_grad * gain[...]
    masked = cot[...].reshape(shape).astype(F32)
    grad = masked + scale * (gained - unit * jnp.mean(gained * unit, axis=-1, keepdims=True))
    low = grad.astype(BF16)
    res_own[...] = low.reshape(slab)[:2]
    res_far[...] = low.reshape(slab)[2:]
    gain_sum = jnp.sum(two_grad * unit, axis=0, keepdims=True)
    out_sum = dot(mixed[...].reshape(shape), low, 0, 0)

    @pl.when(step == 0)
    def _():
        d_gain[...] = gain_sum
        total[...] = out_sum

    @pl.when(step > 0)
    def _():
        d_gain[...] += gain_sum
        total[...] += out_sum

    spread[...] = dot(low, weight[...], 1, 1).astype(BF16).reshape(slab)
    for pair in range(HEADS // 2):
        lanes = slice(pair * 128, (pair + 1) * 128)
        for side in range(2):
            one, two = spread[2 * side, :, lanes], spread[2 * side + 1, :, lanes]
            half = slice(side * 128, (side + 1) * 128)
            heads[2 * pair, :, half] = jnp.concatenate([one[:, :HEAD], two[:, :HEAD]], axis=1)
            heads[2 * pair + 1, :, half] = jnp.concatenate([one[:, HEAD:], two[:, HEAD:]], axis=1)

    @pl.when(step == pl.num_programs(0) - 1)
    def _():
        weight[...] = total[...].astype(BF16)
        d_out_own[...] = weight[:, own_lanes(sc)]
        d_out_far[...] = weight[:, far_lanes(sc)]


def run_post(sc, resid, back, cotangent, mixed, wo, gain):
    whole = (4, HROWS, WIDTH)
    return pl.pallas_call(
        post_kernel,
        grid_spec=pltpu.PrefetchScalarGridSpec(
            num_scalar_prefetch=1,
            grid=(HROWS // SPAN,),
            in_specs=[slab_spec()] * 4 + [held((WIDTH, SIDE)), held((WIDTH, SIDE)), held((1, WIDTH))],
            out_specs=[slab_spec(2)] * 2
            + [heads_spec(), held((WIDTH, SIDE)), held((WIDTH, SIDE)), held((1, WIDTH))],
            scratch_shapes=[
                pltpu.VMEM((WIDTH, WIDTH), BF16),
                pltpu.VMEM((WIDTH, WIDTH), F32),
                pltpu.VMEM((4, SPAN, WIDTH), BF16),
            ],
        ),
        out_shape=[
            jax.ShapeDtypeStruct((2, HROWS, WIDTH), BF16),
            jax.ShapeDtypeStruct((2, HROWS, WIDTH), BF16),
            jax.ShapeDtypeStruct((HEADS, HROWS, 4 * HEAD), BF16),
            jax.ShapeDtypeStruct((WIDTH, SIDE), BF16),
            jax.ShapeDtypeStruct((WIDTH, SIDE), BF16),
            jax.ShapeDtypeStruct((1, WIDTH), F32),
        ],
        compiler_params=params(VMEM),
        cost_estimate=pl.CostEstimate(
            flops=4 * ROWS * WIDTH * WIDTH, bytes_accessed=28 * ROWS * WIDTH, transcendentals=0
        ),
        name="post",
    )(sc, resid, back.reshape(whole), cotangent, mixed, *wo, gain)


def unmix_kernel(carried, sc, *refs):
    shards, (v_own, v_far, grad_heads, mean, *rest) = refs[:8], refs[8:]
    rest = rest[2:] if carried else rest
    outs, (own, far, raw, grads, mask, adder, bound, sems, out_sems) = rest[:8], rest[8:]
    place = sc[PLACE]
    step = pl.program_id(0)

    def leave(slot):
        return [
            pltpu.make_async_copy(
                grads.at[slot, pl.ds(pl.multiple_of((place ^ rel) * SUBS * HALF, SUBS * HALF), SUBS * HALF)],
                outs[4 * slot + rel],
                out_sems.at[slot, rel],
            )
            for rel in range(4)
        ]

    fill_mask(sc, mask)

    @pl.when(step == 0)
    def _():
        lane = lax.broadcasted_iota(jnp.int32, (4 * HEAD, 128), 0) // HEAD
        column = lax.broadcasted_iota(jnp.int32, (4 * HEAD, 128), 1)
        adder[...] = jnp.where((lane == column) | (lane + 4 == column), -1.0, 0.0).astype(BF16)
        row = lax.broadcasted_iota(jnp.int32, (LMAX, 128), 0)
        item = lax.broadcasted_iota(jnp.int32, (LMAX, 128), 1)
        length = jnp.where(item % 4 == 0, sc[LENGTHS], sc[LENGTHS + 1])
        length = jnp.where(item % 4 == 2, sc[LENGTHS + 2], length)
        length = jnp.where(item % 4 == 3, sc[LENGTHS + 3], length)
        bound[...] = jnp.where((item < 8) & (row < length), 1.0, 0.0).astype(BF16)

    slot = take_plane(place, shards, raw, sems)
    high_lanes = lax.broadcasted_iota(jnp.int32, (HROWS, 128), 1) < 4
    for head in range(PHEADS):
        weights = jnp.exp(raw[slot, head_rows(head)].astype(F32)).astype(BF16)
        low = (grad_heads[head].astype(F32) * inverse_sums(sc, weights, mask)).astype(BF16)
        product = low.astype(F32) * mean[head]
        coarse = product.astype(BF16)
        fine = (product - coarse.astype(F32)).astype(BF16)
        delta = dot(coarse, adder[...], 1, 0) + dot(fine, adder[...], 1, 0)
        coarse = delta.astype(BF16)
        fine = (delta - coarse.astype(F32)).astype(BF16)
        left = jnp.concatenate([low, jnp.where(high_lanes, coarse, fine)], axis=1)
        score = dot(left, jnp.concatenate([v_own[head], v_far[head], bound[...]], axis=1), 1, 1)
        grads[slot, head_rows(head)] = (score * weights.astype(F32)).astype(BF16)
        back = (dot(weights, low, 0, 0) * mask[...].astype(F32)).astype(BF16)
        own[head] = back[:, : 2 * HEAD]
        far[head] = back[:, 2 * HEAD :]
    for which in range(2):

        @pl.when(step == which)
        def _():
            for copy in leave(which):
                copy.start()
            if which == 1:
                for copy in leave(0) + leave(1):
                    copy.wait()


def run_unmix(sc, planes, shards, v_own, v_far, grad_heads, mean, carry):
    carry = list(carry)
    return pl.pallas_call(
        partial(unmix_kernel, bool(carry)),
        grid_spec=pltpu.PrefetchScalarGridSpec(
            num_scalar_prefetch=1,
            grid=(2,),
            in_specs=anywhere(8)
            + [plane_spec(planes, LMAX, 2 * HEAD)] * 2
            + [plane_spec(planes, HROWS, 4 * HEAD)] * 2
            + anywhere(len(carry)),
            out_specs=anywhere(8) + [plane_spec(planes, LMAX, 2 * HEAD)] * 2,
            scratch_shapes=[
                pltpu.VMEM((2, 4 * SUBS * HALF, LMAX), BF16),
                pltpu.VMEM((2, 4 * SUBS * HALF, LMAX), BF16),
                pltpu.VMEM((LMAX, 4 * HEAD), BF16),
                pltpu.VMEM((4 * HEAD, 128), BF16),
                pltpu.VMEM((LMAX, 128), BF16),
                pltpu.SemaphoreType.DMA((2, 4)),
                pltpu.SemaphoreType.DMA((2, 4)),
            ],
        ),
        out_shape=[jax.ShapeDtypeStruct((SUBS * HALF, LMAX), BF16)] * 8
        + [jax.ShapeDtypeStruct((HEADS, LMAX, 2 * HEAD), BF16)] * 2,
        input_output_aliases={13 + i: 8 + i for i in range(len(carry))},
        compiler_params=params(VMEM),
        cost_estimate=pl.CostEstimate(
            flops=3 * HEADS * HROWS * LMAX * 4 * HEAD,
            bytes_accessed=HEADS * (2 * HROWS * LMAX + 4 * HROWS * 256 + 4 * LMAX * 256),
            transcendentals=HEADS * HROWS * LMAX // 2,
        ),
        name="unmix",
    )(sc, *shards, v_own, v_far, grad_heads, mean, *carry)


def close_kernel(sc, tok, res_own, res_got, out_own, out_got, own, far, gain, w_own, w_far, *refs):
    (output, tok_grad, d_value, d_gain, total, weight) = refs
    step = pl.program_id(0)
    whole_weight(sc, step, w_own, w_far, weight)
    core = sc[CORE]
    output[:, :, core] = out_own[...].astype(F32)
    output[:, :, 1 - core] = out_got[...].astype(F32)
    tok_grad[:, :, core] = res_own[...].astype(F32)
    tok_grad[:, :, 1 - core] = res_got[...].astype(F32)
    runs = tok.shape[1]
    rows = runs * 128
    for item in range(2):
        lanes = slice(item * HEAD, (item + 1) * HEAD)
        pieces = [
            add_low(own[head, :, lanes], far[head, :, lanes]) for head in range(HEADS)
        ]
        back = jnp.concatenate(pieces, axis=1)
        x = tok[item].reshape(rows, WIDTH).astype(F32)
        scale = lax.rsqrt(jnp.mean(x * x, axis=-1, keepdims=True) + EPSILON)
        unit = x * scale
        normed = (unit * gain[...]).astype(BF16)
        normed_grad = dot(back, weight[...], 1, 1)
        gained = normed_grad * gain[...]
        update = scale * (gained - unit * jnp.mean(gained * unit, axis=-1, keepdims=True))
        tok_grad[item] += update.reshape(runs, 2, HALF, WIDTH)
        gain_sum = jnp.sum(normed_grad * unit, axis=0, keepdims=True)
        value_sum = dot(normed, back, 0, 0)
        if item == 0:
            gain_total, value_total = gain_sum, value_sum
        else:
            gain_total, value_total = gain_total + gain_sum, value_total + value_sum

    @pl.when(step == 0)
    def _():
        d_gain[...] = gain_total
        total[...] = value_total

    @pl.when(step > 0)
    def _():
        d_gain[...] += gain_total
        total[...] += value_total

    @pl.when(step == pl.num_programs(0) - 1)
    def _():
        low = total[...].astype(BF16)
        d_value[0] = low[:, :SIDE]
        d_value[1] = low[:, SIDE:]


def run_close(sc, tokens, res_own, res_got, out_own, out_got, own, far, gain, w_own, w_far):
    runs = 2
    slab = (2, RUNS, 2, HALF, WIDTH)
    half = (2, RUNS, HALF, WIDTH)
    whole_spec = spec((2, runs, 2, HALF, WIDTH), lambda j, s: (0, j, 0, 0, 0))
    half_spec = spec((2, runs, HALF, WIDTH), lambda j, s: (0, j, 0, 0))
    back_spec = spec((HEADS, runs * 128, 2 * HEAD), lambda j, s: (0, j, 0))
    return pl.pallas_call(
        close_kernel,
        grid_spec=pltpu.PrefetchScalarGridSpec(
            num_scalar_prefetch=1,
            grid=(RUNS // runs,),
            in_specs=[whole_spec]
            + [half_spec] * 4
            + [back_spec, back_spec, held((1, WIDTH)), held((WIDTH, SIDE)), held((WIDTH, SIDE))],
            out_specs=[whole_spec, whole_spec, held((2, WIDTH, SIDE)), held((1, WIDTH))],
            scratch_shapes=[pltpu.VMEM((WIDTH, WIDTH), F32), pltpu.VMEM((WIDTH, WIDTH), BF16)],
        ),
        out_shape=[
            jax.ShapeDtypeStruct(slab, F32),
            jax.ShapeDtypeStruct(slab, F32),
            jax.ShapeDtypeStruct((2, WIDTH, SIDE), BF16),
            jax.ShapeDtypeStruct((1, WIDTH), F32),
        ],
        compiler_params=params(VMEM),
        cost_estimate=pl.CostEstimate(
            flops=4 * 2 * LMAX * WIDTH * WIDTH, bytes_accessed=38 * LMAX * WIDTH, transcendentals=0
        ),
        name="close",
    )(
        sc,
        tokens.reshape(slab),
        *(x.reshape(half) for x in (res_own, res_got, out_own, out_got)),
        own,
        far,
        gain,
        w_own,
        w_far,
    )


PACK_DOWN, PACK_UP, PACK_OUT, PACK_VALUE, PACK_GAIN, PACK = 0, 192, 384, 432, 480, 496


def pack_kernel(sc, down, up, out, value, gain, down_far, up_far, out_far, value_far, gain_far, packed):
    first = sc[CORE] == 0

    def both(own, far, lanes):
        own, far = own[:, lanes], far[:, lanes]
        return jnp.concatenate([jnp.where(first, own, far), jnp.where(first, far, own)], axis=0)

    def side(own, far):
        return both(own, far, own_lanes(sc))

    packed[PACK_DOWN:PACK_UP] = side(down, down_far)
    for j in range(4):
        lanes = pl.ds(pl.multiple_of((4 * sc[CORE] + j) * SIDE, 128), SIDE)
        packed[PACK_UP + 48 * j : PACK_UP + 48 * (j + 1)] = both(up, up_far, lanes)
    packed[PACK_OUT:PACK_VALUE] = side(out, out_far)
    packed[PACK_VALUE:PACK_GAIN] = side(value, value_far)
    packed[PACK_GAIN:] = both(gain, gain_far, slice(0, SIDE))


def run_pack(sc, own, far):
    return pl.pallas_call(
        pack_kernel,
        grid_spec=pltpu.PrefetchScalarGridSpec(
            num_scalar_prefetch=1,
            grid=(1,),
            in_specs=[held(x.shape) for x in (*own, *far)],
            out_specs=held((PACK, SIDE)),
        ),
        out_shape=jax.ShapeDtypeStruct((PACK, SIDE), BF16),
        compiler_params=params(VMEM),
        cost_estimate=pl.CostEstimate(flops=0, bytes_accessed=6 * PACK * SIDE, transcendentals=0),
        name="pack",
    )(sc, *own, *far)


def chip_of(sc, k, rel):
    return plane_of(k, sc) * 4 + (sc[PLACE] ^ rel)


def place_kernel(moves, sc, *refs):
    pieces, targets, sems = refs[:16], refs[16:-1], refs[-1]
    copies = []
    for index, piece in enumerate(pieces):
        chip = chip_of(sc, index // 4, index % 4)
        for which, (start, count, lane, target, step, offset, column) in enumerate(moves):
            rows = pl.ds(pl.multiple_of(chip * step + offset, 16), count)
            copies.append(
                pltpu.make_async_copy(
                    piece.at[pl.ds(start, count), pl.ds(lane, SIDE)],
                    targets[target].at[rows, pl.ds(column, SIDE)],
                    sems.at[index, which],
                )
            )
    for copy in copies:
        copy.start()
    for copy in copies:
        copy.wait()


def run_place(sc, pieces, moves, shapes):
    return pl.pallas_call(
        partial(place_kernel, moves),
        grid_spec=pltpu.PrefetchScalarGridSpec(
            num_scalar_prefetch=1,
            grid=(1,),
            in_specs=anywhere(16),
            out_specs=[held(shape) for shape in shapes],
            scratch_shapes=[pltpu.SemaphoreType.DMA((16, len(moves)))],
        ),
        out_shape=[jax.ShapeDtypeStruct(shape, BF16) for shape in shapes],
        compiler_params=params(VMEM),
        cost_estimate=pl.CostEstimate(
            flops=0, bytes_accessed=4 * sum(a * b for a, b in shapes), transcendentals=0
        ),
        name="place",
    )(sc, *pieces)


def place_weights(sc, pieces):
    moves = (
        (PACK_DOWN, 192, 0, 0, 192, 0, 0),
        *((PACK_UP + 48 * j, 48, 0, 1, 48, 0, j * SIDE) for j in range(4)),
        (PACK_OUT, 48, 0, 2, 48, 0, 0),
        (PACK_VALUE, 48, 0, 3, 48, 0, 0),
        (PACK_GAIN, 16, 0, 4, 16, 0, 0),
    )
    shapes = [(FF, SIDE), (WIDTH, FF // 2), (WIDTH, SIDE), (WIDTH, SIDE), (256, SIDE)]
    return run_place(sc, pieces, moves, shapes)


def collect_kernel(sc, *refs):
    outs = refs[24:]
    for k in range(PLANES):

        @pl.when(pl.program_id(0) == k)
        def _():
            for rel in range(4):
                down, down_got, up, up_got, out, out_got = refs[6 * rel : 6 * rel + 6]
                packed = outs[4 * k + rel]
                packed[PACK_DOWN:PACK_UP] = add_low(down[...], down_got[...])
                for j in range(4):
                    lanes = slice(j * SIDE, (j + 1) * SIDE)
                    packed[PACK_UP + 48 * j : PACK_UP + 48 * (j + 1)] = add_low(up[:, lanes], up_got[:, lanes])
                packed[PACK_OUT:PACK_VALUE] = add_low(out[...], out_got[...])


def run_collect(sc, *sides):
    def rows(x, rel):
        return spec((x.shape[0] // 16, x.shape[1]), lambda k, s: (chip_of(s, k, rel), 0))

    return pl.pallas_call(
        collect_kernel,
        grid_spec=pltpu.PrefetchScalarGridSpec(
            num_scalar_prefetch=1,
            grid=(PLANES,),
            in_specs=[rows(x, rel) for rel in range(4) for x in sides],
            out_specs=[held((PACK_VALUE, SIDE))] * 16,
        ),
        out_shape=[jax.ShapeDtypeStruct((PACK_VALUE, SIDE), BF16)] * 16,
        compiler_params=params(VMEM),
        cost_estimate=pl.CostEstimate(flops=0, bytes_accessed=3 * 16 * PACK_VALUE * SIDE * 2, transcendentals=0),
        name="collect",
    )(sc, *(x for _ in range(4) for x in sides))


def add_kernel(groups, *refs):
    for group, total in zip(groups, refs[-len(groups) :]):
        value = refs[group[0]][...].astype(F32)
        for index in group[1:]:
            value = value + refs[index][...].astype(F32)
        total[...] = value.astype(total.dtype)


def run_add(groups, values, dtype):
    rows, columns = values[0].shape
    parts = 2 if columns == LMAX else 1
    block = pl.BlockSpec((rows // parts, columns), lambda i: (i, 0))
    return pl.pallas_call(
        partial(add_kernel, groups),
        grid=(parts,),
        in_specs=[block] * len(values),
        out_specs=[block] * len(groups),
        out_shape=[jax.ShapeDtypeStruct((rows, columns), dtype)] * len(groups),
        compiler_params=params(VMEM),
        cost_estimate=pl.CostEstimate(
            flops=0, bytes_accessed=2 * rows * columns * (len(values) + len(groups)), transcendentals=0
        ),
        name="add",
    )(*values)


DEVICES = 32
TO_CORE, TO_X, TO_Y = 1, 2, 4


def swap(x, bit):
    return lax.ppermute(x, BOTH, [(d, d ^ bit) for d in range(DEVICES)])


def ring(x, way=1):
    return lax.ppermute(x, BOTH, [(d, (d + 8 * way) % DEVICES) for d in range(DEVICES)])


def pick(x, index, axis=0):
    return lax.dynamic_index_in_dim(x, index, axis, keepdims=False)


def ordered(flag, one, two, axis=0, joined=jnp.stack):
    return jnp.where(flag == 0, joined([one, two], axis), joined([two, one], axis))


def add_low(one, two):
    return (one.astype(F32) + two.astype(F32)).astype(BF16)


STEPS = (
    ((0, 0, 1), (0, 1, 0), (1, 0, 0)),
    ((1, 0, 1), (0, 1, 1), (2, 0, 0)),
    ((2, 0, 1), (1, 1, 0), (3, 0, 0)),
    ((3, 0, 1), (2, 1, 0), (1, 1, 1)),
    ((2, 1, 1), (3, 1, 1), (3, 1, 0)),
)


def gather_step(have, step):
    by_x, by_y, by_z = STEPS[step]
    return {
        **have,
        by_z: ring(have[by_z[0] - 1, by_z[1], by_z[2]]),
        by_x: swap(have[by_x[0], by_x[1], 0], TO_X),
        by_y: swap(have[by_y[0], 0, by_y[2]], TO_Y),
    }


def in_order(have):
    return [have[k, y, x] for k in range(4) for y in range(2) for x in range(2)]


def by_place(shares, planes=range(PLANES)):
    return {(k, i // 2, i % 2): shares[4 * at + i] for at, k in enumerate(planes) for i in range(4)}


def scatter_send(have, step):
    by_x, by_y, by_z = STEPS[len(STEPS) - 1 - step]
    got = (ring(have[by_z], -1), swap(have[by_x], TO_X), swap(have[by_y], TO_Y))
    return {at: value for at, value in have.items() if at not in (by_x, by_y, by_z)}, got


def scatter_add(have, got, step):
    by_x, by_y, by_z = STEPS[len(STEPS) - 1 - step]
    targets = ((by_z[0] - 1, by_z[1], by_z[2]), (by_x[0], by_x[1], 0), (by_y[0], 0, by_y[2]))
    sums = list(dict.fromkeys(targets))
    groups = [(len(got) + i, *(j for j in range(len(got)) if targets[j] == at)) for i, at in enumerate(sums)]
    values = [*got, *(have[at] for at in sums)]
    return {**have, **dict(zip(sums, run_add(groups, values, F32 if step == len(STEPS) - 1 else BF16)))}


together = lax.optimization_barrier


def chip_shards(tokens, lengths, rand_mix, w_value, w_out, w_up, w_down, gain_mix, gain_ffn, grad_out):
    wide = lax.axis_index("wide")
    core = lax.axis_index("narrow")
    z, y, x = wide // 4, (wide // 2) % 2, wide % 2
    other = lambda value: swap(value, TO_CORE)
    side = partial(ordered, core, joined=jnp.concatenate)
    slab = (2, RUNS, 2, HALF, WIDTH)
    tokens, grad_out = tokens.reshape(slab), grad_out.reshape(slab)

    gains = jnp.pad(jnp.concatenate([gain_mix, gain_ffn])[None], ((0, 7), (0, SIDE - 48)))
    own = (w_down, w_up, w_out, w_value, gains)
    far = tuple(other(value) for value in own)
    near_sc = jnp.concatenate([jnp.stack([core, z, wide % 4]).astype(jnp.int32), lengths, lengths])
    weights = {(0, 0, 0): run_pack(near_sc, own, far)}

    rand = rand_mix.reshape(3, 2, HALF, LMAX)
    blocks = side(pick(rand, core, 1), other(pick(rand, 1 - core, 1)), 0)
    weights, rands = together((gather_step(weights, 0), {(0, 0, 0): blocks.reshape(SUBS * HALF, LMAX)}))
    weights, tokens_far = together((gather_step(weights, 1), other(pick(tokens, 1 - core, 2))))
    weights, grad_far = together((gather_step(weights, 2), other(pick(grad_out, 1 - core, 2))))
    weights, far_lengths = together((gather_step(weights, 3), other(lengths)))
    sc = jnp.concatenate([near_sc[:5], far_lengths])
    weights, rands = together((gather_step(weights, 4), rands))

    rands = gather_step(rands, 0)
    down, up, out, value, gain_rows = place_weights(sc, in_order(weights))
    rands, value, value_far, gain_rows, out, down, up = together(
        (rands, value, other(value), gain_rows, out, down, up)
    )
    gain_rows = gain_rows.reshape(16, 2, 8, SIDE)[:, :, 0]
    gain_one = gain_rows[..., :24].reshape(1, WIDTH).astype(F32)
    gain_two = gain_rows[..., 24:48].reshape(1, WIDTH).astype(F32)
    rands = gather_step(rands, 1)
    v_own = run_values(sc, tokens.reshape(2, LMAX, WIDTH), gain_one, value, value_far)
    rands, v_own, out, down, up = together((rands, v_own, (out, other(out)), down, up))
    rands, v_own, v_far, down, up = together((gather_step(rands, 2), v_own, other(v_own), down, up))
    rands, v_far, down, up = together((gather_step(rands, 3), v_far, (down, other(down)), up))
    near = [rands[k, y_at, x_at] for k in range(2) for y_at in range(2) for x_at in range(2)]
    rands = gather_step(rands, 4)
    mixing = run_mix(sc, (0, 1), near, v_own, v_far, ())
    rands, up, mixing = together((rands, (up, other(up)), mixing))
    shares = in_order(rands)
    heads, mean = run_mix(sc, (2, 3), shares[8:], v_own, v_far, mixing)

    mixed, resid, normed, masked = run_pre(sc, tokens, tokens_far, grad_out, grad_far, heads, out, gain_two)
    active, up_grad, back = run_units(sc, normed, masked, up, down)
    res_own, res_far, grad_heads, d_out_own, d_out_far, d_gain_two = run_post(
        sc, resid, back, masked, mixed, out, gain_two
    )

    *far, back_own, back_far = run_unmix(
        sc, (3, 2), shares[12:] + shares[8:12], v_own, v_far, grad_heads, mean, ()
    )
    far, back_own, back_far, res_got, d_out_got = together((far, back_own, back_far, other(res_far), other(d_out_far)))
    have, got = scatter_send(by_place(far, (3, 2)), 0)
    *near, back_own, back_far = run_unmix(
        sc, (1, 0), shares[4:8] + shares[:4], v_own, v_far, grad_heads, mean, (back_own, back_far)
    )
    have, got, near, back_own, back_far = together((have, got, near, back_own, back_far))
    have = {**scatter_add(have, got, 0), **by_place(near, (1, 0))}

    have, got = scatter_send(have, 1)
    up_own, up_far = run_up_grad(sc, normed, up_grad)
    have, got, up_own, up_far, back_got = together((have, got, up_own, up_far, other(back_far)))
    have = scatter_add(have, got, 1)

    have, got = scatter_send(have, 2)
    down_own, down_far = run_down_grad(sc, active, masked)
    have, got, down_own, down_far, up_got = together((have, got, down_own, down_far, other(up_far)))
    have = scatter_add(have, got, 2)

    have, got = scatter_send(have, 3)
    out_own, out_far = run_out(sc, active, resid, down)
    have, got, out_own, out_far, down_got = together((have, got, out_own, out_far, other(down_far)))
    have = scatter_add(have, got, 3)

    have, got = scatter_send(have, 4)
    packed = run_collect(sc, down_own, down_got, up_own, up_got, d_out_own, d_out_got)
    have, got, packed, out_got = together((have, got, packed, other(out_far)))
    rand_sum = scatter_add(have, got, 4)[0, 0, 0].reshape(2, 3, HALF, LMAX)

    sums, got = scatter_send(by_place(packed), 0)
    output, tokens_grad, d_value, d_gain_one = run_close(
        sc, tokens, res_own, res_got, out_own, out_got, back_own, back_got, gain_one, value, value_far
    )
    blocks, blocks_far = pick(rand_sum, core), other(pick(rand_sum, 1 - core))
    sums, got, output, tokens_grad, d_value, d_gain_one, blocks, blocks_far = together(
        (sums, got, output, tokens_grad, d_value, d_gain_one, blocks, blocks_far)
    )
    sums = scatter_add(sums, got, 0)

    sums, got = scatter_send(sums, 1)
    gain_pair = jnp.concatenate([d_gain_one, d_gain_two]).reshape(2, 16, 1, 48).astype(BF16)
    gain_pair = jnp.pad(gain_pair, ((0, 0), (0, 0), (0, 15), (0, SIDE - 48)))
    small = jnp.concatenate([d_value.reshape(2, 16, 48, SIDE), gain_pair], 2)
    small = add_low(pick(small, core), other(pick(small, 1 - core))).reshape(4, 2, 2, 64, SIDE)
    sums, got, small = together((sums, got, small))
    sums = scatter_add(sums, got, 1)

    sums, got = scatter_send(sums, 2)
    small = add_low(pick(small, x, 2), swap(pick(small, 1 - x, 2), TO_X))
    sums, got, small = together((sums, got, small))
    sums = scatter_add(sums, got, 2)

    sums, got = scatter_send(sums, 3)
    small = add_low(pick(small, y, 1), swap(pick(small, 1 - y, 1), TO_Y))
    sums, got, small = together((sums, got, small))
    sums = scatter_add(sums, got, 3)

    sums, got = scatter_send(sums, 4)
    small_sum = pick(small, z).astype(F32)
    for k in range(1, PLANES):
        small_sum = small_sum + ring(pick(small, lax.rem(z + PLANES - k, PLANES)), -k).astype(F32)
    sums, got, small_sum = together((sums, got, small_sum))
    big_sum = scatter_add(sums, got, 4)[0, 0, 0]
    big_far, small_far = other(big_sum), other(small_sum)

    rows_of = lambda value, rows: pick(value.reshape(-1, 2, rows, SIDE), core, 1)
    mine = lambda own, far, rows: side(rows_of(own, rows)[0], rows_of(far, rows)[0], 1)
    down_shard = mine(big_sum[PACK_DOWN:PACK_UP], big_far[PACK_DOWN:PACK_UP], 96)
    up_side = lambda value: rows_of(value[PACK_UP:PACK_OUT], 24).transpose(1, 0, 2).reshape(24, 4 * SIDE)
    up_shard = side(up_side(big_sum), up_side(big_far), 1)
    outproj_shard = mine(big_sum[PACK_OUT:PACK_VALUE], big_far[PACK_OUT:PACK_VALUE], 24)
    value_shard = mine(small_sum[:48], small_far[:48], 24)
    gains_pair = ordered(core, small_sum[48, :48], small_far[48, :48])
    gain_pair = pick(gains_pair.reshape(2, 2, 24), core, 1)

    rand_shard = ordered(core, blocks, blocks_far, 1)

    return (
        output.reshape(2, LMAX, WIDTH),
        tokens_grad.reshape(2, LMAX, WIDTH),
        rand_shard.reshape(3 * 128, LMAX),
        value_shard,
        outproj_shard,
        up_shard,
        down_shard,
        gain_pair[0],
        gain_pair[1],
    )


def rms_norm(values, gain):
    scale = lax.rsqrt(jnp.mean(values * values, axis=-1, keepdims=True) + EPSILON)
    return values * scale * gain


def split_heads(block):
    return block.reshape(LMAX, HEADS, HEAD).transpose(1, 0, 2)


def merge_heads(block):
    return block.transpose(1, 0, 2).reshape(LMAX, HEADS * HEAD)


def masked_scores(key_mask, rand_head):
    return jnp.where(key_mask[None, :] > 0, rand_head.astype(jnp.float32), -1e30)


def head_forward(key_mask, paired):
    rand_head, value_head = paired
    scores = masked_scores(key_mask, rand_head)
    row_peak = jnp.max(scores, axis=-1, keepdims=True)
    exponent = jnp.exp(scores - row_peak)
    denom_sum = jnp.sum(exponent, axis=-1, keepdims=True)
    attention = exponent / denom_sum * key_mask[:, None]
    mixed = jnp.dot(attention.astype(jnp.bfloat16), value_head, preferred_element_type=jnp.float32)
    return (mixed.astype(jnp.bfloat16), row_peak + jnp.log(denom_sum))


def head_backward(key_mask, paired):
    rand_head, value_head, mix_grad, log_total = paired
    scores = masked_scores(key_mask, rand_head)
    attention = jnp.exp(scores - log_total) * key_mask[:, None]
    prob_grad = jnp.einsum("id,jd->ij", mix_grad, value_head, preferred_element_type=jnp.float32)
    value_grad = jnp.einsum(
        "ij,id->jd", attention.astype(jnp.bfloat16), mix_grad, preferred_element_type=jnp.float32
    )
    score_grad = attention * (prob_grad - jnp.sum(prob_grad * attention, axis=-1, keepdims=True))
    return (score_grad, value_grad)


def shards(tokens, lengths, rand_mix, w_value, w_out, w_up, w_down, gain_mix, gain_ffn, grad_out):
    item_count = tokens.shape[0]
    width = tokens.shape[2]
    row_count = item_count * LMAX
    tokens_flat = tokens.reshape(row_count, width).astype(jnp.float32)
    positions = jnp.arange(LMAX, dtype=jnp.int32)
    valid_table = (positions[None, :] < lengths[:, None]).astype(jnp.float32)
    row_valid = valid_table.reshape(row_count, 1)
    forward_set = (
        lax.all_gather(rand_mix, ("wide", "narrow"), axis=0, tiled=True),
        lax.all_gather(w_value, ("wide", "narrow"), axis=0, tiled=True),
        lax.all_gather(w_out, ("wide", "narrow"), axis=0, tiled=True),
        lax.all_gather(w_up, ("wide", "narrow"), axis=0, tiled=True),
        lax.all_gather(w_down, ("wide", "narrow"), axis=0, tiled=True),
        lax.all_gather(gain_mix, ("wide", "narrow"), axis=0, tiled=True),
        lax.all_gather(gain_ffn, ("wide", "narrow"), axis=0, tiled=True),
    )
    rand_all, value_all, out_all, up_all, down_all, gain_first, gain_second = forward_set
    normed = rms_norm(tokens_flat, gain_first.astype(jnp.float32)).astype(jnp.bfloat16)
    values = jnp.dot(normed, value_all, preferred_element_type=jnp.float32).astype(jnp.bfloat16)
    rand_heads = rand_all.reshape(HEADS, LMAX, LMAX)
    mixed_parts = []
    totals_kept = []
    for item_index in range(item_count):
        item_values = split_heads(values[item_index * LMAX : (item_index + 1) * LMAX])
        mixed_heads, log_total = lax.map(
            partial(head_forward, valid_table[item_index]), (rand_heads, item_values)
        )
        mixed_parts.append(merge_heads(mixed_heads))
        totals_kept.append(log_total)
    mixed = jnp.concatenate(mixed_parts, axis=0)
    residual = tokens_flat + jnp.dot(mixed, out_all, preferred_element_type=jnp.float32)
    normed_two = rms_norm(residual, gain_second.astype(jnp.float32)).astype(jnp.bfloat16)
    up_proj = jnp.dot(normed_two, up_all, preferred_element_type=jnp.float32)
    active = jax.nn.gelu(up_proj).astype(jnp.bfloat16)
    branch = jnp.dot(active, down_all, preferred_element_type=jnp.float32)
    output = row_valid * (residual + branch)
    back_set = (
        lax.all_gather(rand_mix, ("wide", "narrow"), axis=0, tiled=True),
        lax.all_gather(w_value, ("wide", "narrow"), axis=0, tiled=True),
        lax.all_gather(w_out, ("wide", "narrow"), axis=0, tiled=True),
        lax.all_gather(w_up, ("wide", "narrow"), axis=0, tiled=True),
        lax.all_gather(w_down, ("wide", "narrow"), axis=0, tiled=True),
        lax.all_gather(gain_mix, ("wide", "narrow"), axis=0, tiled=True),
        lax.all_gather(gain_ffn, ("wide", "narrow"), axis=0, tiled=True),
    )
    rand_back, value_back, out_back, up_back, down_back, gain_back_one, gain_back_two = back_set
    cotangent = grad_out.reshape(row_count, width).astype(jnp.float32)
    masked = row_valid * cotangent
    branch_grad = masked.astype(jnp.bfloat16)
    grad_down = jnp.einsum("rk,rd->kd", active, branch_grad, preferred_element_type=jnp.float32)
    active_grad = jnp.einsum(
        "rd,kd->rk", branch_grad, down_back, preferred_element_type=jnp.float32
    )
    gelu_value, gelu_pull = jax.vjp(jax.nn.gelu, up_proj)
    up_grad = gelu_pull(active_grad)[0].astype(jnp.bfloat16)
    grad_up = jnp.einsum("rd,rk->dk", normed_two, up_grad, preferred_element_type=jnp.float32)
    normed_two_grad = jnp.einsum("rk,dk->rd", up_grad, up_back, preferred_element_type=jnp.float32)
    norm_value, norm_pull = jax.vjp(rms_norm, residual, gain_back_two.astype(jnp.float32))
    residual_part, gain_two_grad = norm_pull(normed_two_grad)
    residual_grad = masked + residual_part
    attn_grad = residual_grad.astype(jnp.bfloat16)
    grad_outproj = jnp.einsum("rd,re->de", mixed, attn_grad, preferred_element_type=jnp.float32)
    mixed_grad = jnp.einsum(
        "re,de->rd", attn_grad, out_back, preferred_element_type=jnp.float32
    ).astype(jnp.bfloat16)
    rand_heads_back = rand_back.reshape(HEADS, LMAX, LMAX)
    rand_grad = jnp.zeros((HEADS, LMAX, LMAX), jnp.float32)
    value_parts = []
    for item_index in range(item_count):
        lower_row = item_index * LMAX
        upper_row = lower_row + LMAX
        item_values = split_heads(values[lower_row:upper_row])
        item_mix_grad = split_heads(mixed_grad[lower_row:upper_row])
        score_grad, value_grad = lax.map(
            partial(head_backward, valid_table[item_index]),
            (rand_heads_back, item_values, item_mix_grad, totals_kept[item_index]),
        )
        rand_grad = rand_grad + score_grad
        value_parts.append(merge_heads(value_grad))
    values_grad = jnp.concatenate(value_parts, axis=0).astype(jnp.bfloat16)
    grad_value = jnp.einsum("rd,re->de", normed, values_grad, preferred_element_type=jnp.float32)
    normed_grad = jnp.einsum(
        "re,de->rd", values_grad, value_back, preferred_element_type=jnp.float32
    )
    norm_first, first_pull = jax.vjp(rms_norm, tokens_flat, gain_back_one.astype(jnp.float32))
    token_part, gain_one_grad = first_pull(normed_grad)
    tokens_grad = residual_grad + token_part
    rand_flat = rand_grad.reshape(HEADS * LMAX, LMAX)
    all_shards = (
        lax.psum_scatter(rand_flat, ("wide", "narrow"), scatter_dimension=0, tiled=True),
        lax.psum_scatter(grad_value, ("wide", "narrow"), scatter_dimension=0, tiled=True),
        lax.psum_scatter(grad_outproj, ("wide", "narrow"), scatter_dimension=0, tiled=True),
        lax.psum_scatter(grad_up, ("wide", "narrow"), scatter_dimension=0, tiled=True),
        lax.psum_scatter(grad_down, ("wide", "narrow"), scatter_dimension=0, tiled=True),
        lax.psum_scatter(gain_one_grad, ("wide", "narrow"), scatter_dimension=0, tiled=True),
        lax.psum_scatter(gain_two_grad, ("wide", "narrow"), scatter_dimension=0, tiled=True),
    )
    rand_shard, value_shard, outproj_shard, up_shard, down_shard, gain_one_shard, gain_two_shard = (
        all_shards
    )
    return (
        output.reshape(item_count, LMAX, width),
        tokens_grad.reshape(item_count, LMAX, width),
        rand_shard,
        value_shard,
        outproj_shard,
        up_shard,
        down_shard,
        gain_one_shard,
        gain_two_shard,
    )


def solution(mesh):
    in_specs = (
        P(("wide", "narrow"), None, None),
        P(("wide", "narrow")),
        P(("wide", "narrow"), None),
        P(("wide", "narrow"), None),
        P(("wide", "narrow"), None),
        P(("wide", "narrow"), None),
        P(("wide", "narrow"), None),
        P(("wide", "narrow")),
        P(("wide", "narrow")),
        P(("wide", "narrow"), None, None),
    )
    out_specs = (
        P(("wide", "narrow"), None, None),
        P(("wide", "narrow"), None, None),
        P(("wide", "narrow"), None),
        P(("wide", "narrow"), None),
        P(("wide", "narrow"), None),
        P(("wide", "narrow"), None),
        P(("wide", "narrow"), None),
        P(("wide", "narrow")),
        P(("wide", "narrow")),
    )
    fits = dict(mesh.shape) == {"wide": 16, "narrow": 2}
    return jax.shard_map(chip_shards if fits else shards, mesh=mesh, in_specs=in_specs, out_specs=out_specs, check_vma=False)
```

```python
from functools import partial

import jax
import jax.numpy as jnp
from jax import lax
from jax.experimental import pallas as pl
from jax.experimental.pallas import tpu as pltpu
from jax.sharding import PartitionSpec as P

HEADS = 12
HEAD = 64
LMAX = 1024
WIDTH = 768
FF = 3072
EPSILON = 1e-05

BOTH = ("wide", "narrow")
BF16 = jnp.bfloat16
F32 = jnp.float32
VMEM = 61 << 20

SUBS = 6
RUNS = 8
HALF = 64
HROWS = RUNS * HALF
PLANES = 4
PHEADS = HEADS // PLANES
ROWS = 2 * LMAX
FSTEP = 768
TILE = 512
SIDE = WIDTH // 2
SPAN = 2 * HALF


def dot(a, b, ca, cb):
    return lax.dot_general(a, b, (((ca,), (cb,)), ((), ())), preferred_element_type=F32)


CORE, PLANE, PLACE, LENGTHS = 0, 1, 2, 3


def spec(shape, index):
    return pl.BlockSpec(shape, index)


def held(shape):
    zeros = (0,) * len(shape)
    return pl.BlockSpec(shape, lambda *_: zeros, pipeline_mode=pl.Buffered(1))


def params(limit):
    return pltpu.CompilerParams(vmem_limit_bytes=limit)


def values_kernel(sc, tok, gain, weight, out):
    step = pl.program_id(0)
    rows = tok.shape[1]
    position = step * rows + lax.broadcasted_iota(jnp.int32, (rows, 1), 0)
    for item in range(2):
        x = tok[item].astype(F32)
        scale = lax.rsqrt(jnp.mean(x * x, axis=-1, keepdims=True) + EPSILON)
        normed = (x * scale * gain[...]).astype(BF16)
        found = dot(normed, weight[...], 1, 0)
        found = jnp.where(position < sc[LENGTHS + item], found, 0.0).astype(BF16)
        for head in range(HEADS):
            out[head, :, item * HEAD : (item + 1) * HEAD] = found[:, head * HEAD : (head + 1) * HEAD]


def run_values(sc, tokens, gain, weight):
    rows = 256
    return pl.pallas_call(
        values_kernel,
        grid_spec=pltpu.PrefetchScalarGridSpec(
            num_scalar_prefetch=1,
            grid=(LMAX // rows,),
            in_specs=[
                spec((2, rows, WIDTH), lambda j, s: (0, j, 0)),
                held((1, WIDTH)),
                held((WIDTH, WIDTH)),
            ],
            out_specs=spec((HEADS, rows, 2 * HEAD), lambda j, s: (0, j, 0)),
        ),
        out_shape=jax.ShapeDtypeStruct((HEADS, LMAX, 2 * HEAD), BF16),
        compiler_params=params(VMEM),
        cost_estimate=pl.CostEstimate(
            flops=2 * 2 * LMAX * WIDTH * WIDTH, bytes_accessed=8 * LMAX * WIDTH, transcendentals=0
        ),
        name="values",
    )(sc, tokens, gain, weight)


def lane_lengths(sc, shape):
    slot = lax.broadcasted_iota(jnp.int32, shape, 1) // HEAD
    length = jnp.where(slot == 0, sc[LENGTHS], sc[LENGTHS + 1])
    return jnp.where(slot >= 2, jnp.where(slot == 2, sc[LENGTHS + 2], sc[LENGTHS + 3]), length)


def plane_of(k, sc):
    return lax.rem(sc[PLANE] + PLANES - k, PLANES)


def plane_spec(planes, rows, lanes):
    def index(step, sc):
        return (plane_of(planes[0] + step * (planes[1] - planes[0]), sc), 0, 0)

    return spec((PHEADS, rows, lanes), index)


def anywhere(count):
    return [pl.BlockSpec(memory_space=pl.ANY)] * count


def plane_fetch(place, shards, raw, sems, slot):
    return [
        pltpu.make_async_copy(
            shards[4 * slot + rel],
            raw.at[slot, pl.ds(pl.multiple_of((place ^ rel) * SUBS * HALF, SUBS * HALF), SUBS * HALF)],
            sems.at[slot, rel],
        )
        for rel in range(4)
    ]


def take_plane(place, shards, raw, sems):
    step = pl.program_id(0)

    @pl.when(step == 0)
    def _():
        for slot in range(2):
            for copy in plane_fetch(place, shards, raw, sems, slot):
                copy.start()

    for slot in range(2):

        @pl.when(step == slot)
        def _():
            for copy in plane_fetch(place, shards, raw, sems, slot):
                copy.wait()

    return step


def head_rows(head):
    return slice(head * HROWS, (head + 1) * HROWS)


def fill_mask(sc, mask):
    @pl.when(pl.program_id(0) == 0)
    def _():
        shape = (LMAX, 4 * HEAD)
        column = lax.broadcasted_iota(jnp.int32, shape, 0)
        mask[...] = (column < lane_lengths(sc, shape)).astype(F32).astype(BF16)


def inverse_sums(sc, weights, mask):
    shape = (HROWS, 4 * HEAD)
    line = lax.broadcasted_iota(jnp.int32, shape, 0)
    position = 128 * (line // HALF) + HALF * sc[CORE] + line % HALF
    return jnp.where(position < lane_lengths(sc, shape), 1.0 / dot(weights, mask[...], 1, 0), 0.0)


def mix_kernel(carried, sc, *refs):
    shards, (v_own, v_far, *rest) = refs[:8], refs[8:]
    mixed, mean, raw, mask, sems = rest[2:] if carried else rest
    fill_mask(sc, mask)
    slot = take_plane(sc[PLACE], shards, raw, sems)
    for head in range(PHEADS):
        weights = jnp.exp(raw[slot, head_rows(head)].astype(F32)).astype(BF16)
        values = jnp.concatenate([v_own[head], v_far[head]], axis=1)
        found = dot(weights, values, 1, 0) * inverse_sums(sc, weights, mask)
        mean[head] = found
        mixed[head] = found.astype(BF16)


def run_mix(sc, planes, shards, v_own, v_far, carry):
    carry = list(carry)
    return pl.pallas_call(
        partial(mix_kernel, bool(carry)),
        grid_spec=pltpu.PrefetchScalarGridSpec(
            num_scalar_prefetch=1,
            grid=(2,),
            in_specs=anywhere(8) + [plane_spec(planes, LMAX, 2 * HEAD)] * 2 + anywhere(len(carry)),
            out_specs=[plane_spec(planes, HROWS, 4 * HEAD)] * 2,
            scratch_shapes=[
                pltpu.VMEM((2, 4 * SUBS * HALF, LMAX), BF16),
                pltpu.VMEM((LMAX, 4 * HEAD), BF16),
                pltpu.SemaphoreType.DMA((2, 4)),
            ],
        ),
        out_shape=[
            jax.ShapeDtypeStruct((HEADS, HROWS, 4 * HEAD), BF16),
            jax.ShapeDtypeStruct((HEADS, HROWS, 4 * HEAD), F32),
        ],
        input_output_aliases={11 + i: i for i in range(len(carry))},
        compiler_params=params(VMEM),
        cost_estimate=pl.CostEstimate(
            flops=2 * HEADS * HROWS * LMAX * 4 * HEAD,
            bytes_accessed=HEADS * (HROWS * LMAX + 5 * HROWS * 256),
            transcendentals=HEADS * HROWS * LMAX // 2,
        ),
        name="mix",
    )(sc, *shards, v_own, v_far, *carry)


def row_valid(sc, step):
    line = lax.broadcasted_iota(jnp.int32, (4 * SPAN, 1), 0)
    item = line // SPAN
    row = step * SPAN + line % SPAN
    low = jnp.where(item == 0, sc[LENGTHS], sc[LENGTHS + 1])
    high = jnp.where(item == 2, sc[LENGTHS + 2], sc[LENGTHS + 3])
    return 128 * (row // HALF) + HALF * sc[CORE] + row % HALF < jnp.where(item >= 2, high, low)


def four_items(own, far):
    return jnp.concatenate([own[:, :, 0], far[...]], axis=0).reshape(4 * SPAN, WIDTH)


def pre_kernel(sc, tok, tok_far, cot, cot_far, heads, weight, gain, mixed, resid, normed, grad):
    step = pl.program_id(0)
    for item in range(4):
        lanes = slice(item * HEAD, (item + 1) * HEAD)
        for pair in range(HEADS // 2):
            both = jnp.concatenate([heads[2 * pair, :, lanes], heads[2 * pair + 1, :, lanes]], axis=1)
            mixed[item, :, pair * 128 : (pair + 1) * 128] = both
    res = four_items(tok, tok_far).astype(F32) + dot(mixed[...].reshape(4 * SPAN, WIDTH), weight[...], 1, 0)
    resid[...] = res.astype(BF16).reshape(4, SPAN, WIDTH)
    scale = lax.rsqrt(jnp.mean(res * res, axis=-1, keepdims=True) + EPSILON)
    valid = row_valid(sc, step)
    normed[...] = jnp.where(valid, res * scale * gain[...], 0.0).astype(BF16).reshape(4, SPAN, WIDTH)
    masked = jnp.where(valid, four_items(cot, cot_far).astype(F32), 0.0)
    grad[...] = masked.astype(BF16).reshape(4, SPAN, WIDTH)


def slab_spec(items=4):
    return spec((items, SPAN, WIDTH), lambda r, s: (0, r, 0))


def half_specs():
    return [
        spec((2, SPAN // HALF, 1, HALF, WIDTH), lambda r, s: (0, r, s[CORE], 0, 0)),
        spec((2, SPAN // HALF, HALF, WIDTH), lambda r, s: (0, r, 0, 0)),
    ]


def heads_spec():
    return spec((HEADS, SPAN, 4 * HEAD), lambda r, s: (0, r, 0))


def run_pre(sc, tokens, tokens_far, cotangent, cotangent_far, heads, weight, gain):
    return pl.pallas_call(
        pre_kernel,
        grid_spec=pltpu.PrefetchScalarGridSpec(
            num_scalar_prefetch=1,
            grid=(HROWS // SPAN,),
            in_specs=half_specs()
            + half_specs()
            + [heads_spec(), held((WIDTH, WIDTH)), held((1, WIDTH))],
            out_specs=[slab_spec()] * 4,
        ),
        out_shape=[
            jax.ShapeDtypeStruct((4, HROWS, WIDTH), BF16),
            jax.ShapeDtypeStruct((4, HROWS, WIDTH), BF16),
            jax.ShapeDtypeStruct((4, HROWS, WIDTH), BF16),
            jax.ShapeDtypeStruct((4, HROWS, WIDTH), BF16),
        ],
        compiler_params=params(VMEM),
        cost_estimate=pl.CostEstimate(
            flops=2 * ROWS * WIDTH * WIDTH, bytes_accessed=16 * ROWS * WIDTH, transcendentals=0
        ),
        name="pre",
    )(sc, tokens, tokens_far, cotangent, cotangent_far, heads, weight, gain)


def units_kernel(sc, normed, cot, w_up, w_down, active, up_grad, back, total):
    step = pl.program_id(0)
    for piece in range(ROWS // TILE):
        whole = slice(piece * TILE, (piece + 1) * TILE)
        for row in range(piece * TILE, (piece + 1) * TILE, 256):
            rows = slice(row, row + 256)
            for column in range(0, FSTEP, 256):
                columns = slice(column, column + 256)
                up = dot(normed[rows], w_up[0, :, columns], 1, 0)
                square = up * up
                bend = jnp.tanh(up * (0.7978845608028654 + (0.044715 * 0.7978845608028654) * square))
                share = 0.5 + 0.5 * bend
                act = up * share
                active[rows, columns] = act.astype(BF16)
                slope = share + act * (1.0 - share) * (
                    2 * 0.7978845608028654 + (6 * 0.044715 * 0.7978845608028654) * square
                )
                up_grad[rows, columns] = (dot(cot[rows], w_down[columns], 1, 1) * slope).astype(BF16)
        two_grad = dot(up_grad[whole], w_up[0], 1, 1)

        @pl.when(step == 0)
        def _():
            total[whole] = two_grad

        @pl.when((step > 0) & (step < FF // FSTEP - 1))
        def _():
            total[whole] += two_grad

        @pl.when(step == FF // FSTEP - 1)
        def _():
            back[whole] = (total[whole] + two_grad).astype(BF16)


def run_units(sc, normed, cotangent, w_up, w_down):
    columns = spec((ROWS, FSTEP), lambda f, s: (0, f))
    return pl.pallas_call(
        units_kernel,
        grid_spec=pltpu.PrefetchScalarGridSpec(
            num_scalar_prefetch=1,
            grid=(FF // FSTEP,),
            in_specs=[
                held((ROWS, WIDTH)),
                held((ROWS, WIDTH)),
                spec((1, WIDTH, FSTEP), lambda f, s: (f, 0, 0)),
                spec((FSTEP, WIDTH), lambda f, s: (f, 0)),
            ],
            out_specs=[columns, columns, held((ROWS, WIDTH))],
            scratch_shapes=[pltpu.VMEM((ROWS, WIDTH), F32)],
        ),
        out_shape=[
            jax.ShapeDtypeStruct((ROWS, FF), BF16),
            jax.ShapeDtypeStruct((ROWS, FF), BF16),
            jax.ShapeDtypeStruct((ROWS, WIDTH), BF16),
        ],
        compiler_params=params(VMEM),
        cost_estimate=pl.CostEstimate(
            flops=6 * ROWS * WIDTH * FF, bytes_accessed=8 * ROWS * WIDTH + 4 * ROWS * FF, transcendentals=ROWS * FF
        ),
        name="units",
    )(sc, normed.reshape(ROWS, WIDTH), cotangent.reshape(ROWS, WIDTH), w_up, w_down)


def down_grad_kernel(active, cot, total):
    total[...] = dot(active[...], cot[...], 0, 0).astype(BF16)


def run_down_grad(active, cotangent):
    return pl.pallas_call(
        down_grad_kernel,
        grid=(FF // 512,),
        in_specs=[spec((ROWS, 512), lambda f: (0, f)), held((ROWS, WIDTH))],
        out_specs=spec((512, WIDTH), lambda f: (f, 0)),
        out_shape=jax.ShapeDtypeStruct((FF, WIDTH), BF16),
        compiler_params=params(VMEM),
        cost_estimate=pl.CostEstimate(
            flops=2 * ROWS * WIDTH * FF, bytes_accessed=2 * ROWS * (WIDTH + FF), transcendentals=0
        ),
        name="down_grad",
    )(active, cotangent.reshape(ROWS, WIDTH))


def up_grad_kernel(normed, up_grad, total):
    total[0] = dot(normed[...], up_grad[...], 0, 0).astype(BF16)


def run_up_grad(normed, up_grad):
    return pl.pallas_call(
        up_grad_kernel,
        grid=(FF // FSTEP,),
        in_specs=[held((ROWS, WIDTH)), spec((ROWS, FSTEP), lambda f: (0, f))],
        out_specs=spec((1, WIDTH, FSTEP), lambda f: (f, 0, 0)),
        out_shape=jax.ShapeDtypeStruct((FF // FSTEP, WIDTH, FSTEP), BF16),
        compiler_params=params(VMEM),
        cost_estimate=pl.CostEstimate(
            flops=2 * ROWS * WIDTH * FF, bytes_accessed=2 * ROWS * (WIDTH + FF), transcendentals=0
        ),
        name="up_grad",
    )(normed.reshape(ROWS, WIDTH), up_grad)


def out_kernel(sc, active, resid, w_down, own, far):
    step = pl.program_id(0)
    branch = dot(active[...].reshape(4 * SPAN, FF), w_down[...], 1, 0)
    output = jnp.where(row_valid(sc, step), resid[...].reshape(4 * SPAN, WIDTH).astype(F32) + branch, 0.0)
    output = output.astype(BF16).reshape(4, SPAN, WIDTH)
    own[...] = output[:2]
    far[...] = output[2:]


def run_out(sc, active, resid, w_down):
    return pl.pallas_call(
        out_kernel,
        grid_spec=pltpu.PrefetchScalarGridSpec(
            num_scalar_prefetch=1,
            grid=(HROWS // SPAN,),
            in_specs=[
                spec((4, SPAN, FF), lambda r, s: (0, r, 0)),
                slab_spec(),
                held((FF, WIDTH)),
            ],
            out_specs=[slab_spec(2)] * 2,
        ),
        out_shape=[
            jax.ShapeDtypeStruct((2, HROWS, WIDTH), BF16),
            jax.ShapeDtypeStruct((2, HROWS, WIDTH), BF16),
        ],
        compiler_params=params(VMEM),
        cost_estimate=pl.CostEstimate(
            flops=2 * ROWS * WIDTH * FF, bytes_accessed=ROWS * (2 * FF + 7 * WIDTH), transcendentals=0
        ),
        name="out",
    )(sc, active.reshape(4, HROWS, FF), resid, w_down)


def post_kernel(sc, resid, back, cot, mixed, weight, gain, *refs):
    (res_own, res_far, heads, d_out, d_gain, total, spread) = refs
    step = pl.program_id(0)
    shape, slab = (4 * SPAN, WIDTH), (4, SPAN, WIDTH)
    valid = row_valid(sc, step)
    res = resid[...].reshape(shape).astype(F32)
    scale = lax.rsqrt(jnp.mean(res * res, axis=-1, keepdims=True) + EPSILON)
    unit = res * scale
    two_grad = jnp.where(valid, back[...].reshape(shape).astype(F32), 0.0)
    gained = two_grad * gain[...]
    masked = cot[...].reshape(shape).astype(F32)
    grad = masked + scale * (gained - unit * jnp.mean(gained * unit, axis=-1, keepdims=True))
    low = grad.astype(BF16)
    res_own[...] = low.reshape(slab)[:2]
    res_far[...] = low.reshape(slab)[2:]
    gain_sum = jnp.sum(two_grad * unit, axis=0, keepdims=True)
    out_sum = dot(mixed[...].reshape(shape), low, 0, 0)

    @pl.when(step == 0)
    def _():
        d_gain[...] = gain_sum
        total[...] = out_sum

    @pl.when(step > 0)
    def _():
        d_gain[...] += gain_sum
        total[...] += out_sum

    spread[...] = dot(low, weight[...], 1, 1).astype(BF16).reshape(slab)
    for pair in range(HEADS // 2):
        lanes = slice(pair * 128, (pair + 1) * 128)
        for side in range(2):
            one, two = spread[2 * side, :, lanes], spread[2 * side + 1, :, lanes]
            half = slice(side * 128, (side + 1) * 128)
            heads[2 * pair, :, half] = jnp.concatenate([one[:, :HEAD], two[:, :HEAD]], axis=1)
            heads[2 * pair + 1, :, half] = jnp.concatenate([one[:, HEAD:], two[:, HEAD:]], axis=1)

    @pl.when(step == pl.num_programs(0) - 1)
    def _():
        low = total[...].astype(BF16)
        d_out[0] = low[:, :SIDE]
        d_out[1] = low[:, SIDE:]


def run_post(sc, resid, back, cotangent, mixed, weight, gain):
    whole = (4, HROWS, WIDTH)
    return pl.pallas_call(
        post_kernel,
        grid_spec=pltpu.PrefetchScalarGridSpec(
            num_scalar_prefetch=1,
            grid=(HROWS // SPAN,),
            in_specs=[slab_spec()] * 4 + [held((WIDTH, WIDTH)), held((1, WIDTH))],
            out_specs=[slab_spec(2)] * 2
            + [heads_spec(), held((2, WIDTH, SIDE)), held((1, WIDTH))],
            scratch_shapes=[
                pltpu.VMEM((WIDTH, WIDTH), F32),
                pltpu.VMEM((4, SPAN, WIDTH), BF16),
            ],
        ),
        out_shape=[
            jax.ShapeDtypeStruct((2, HROWS, WIDTH), BF16),
            jax.ShapeDtypeStruct((2, HROWS, WIDTH), BF16),
            jax.ShapeDtypeStruct((HEADS, HROWS, 4 * HEAD), BF16),
            jax.ShapeDtypeStruct((2, WIDTH, SIDE), BF16),
            jax.ShapeDtypeStruct((1, WIDTH), F32),
        ],
        compiler_params=params(VMEM),
        cost_estimate=pl.CostEstimate(
            flops=4 * ROWS * WIDTH * WIDTH, bytes_accessed=28 * ROWS * WIDTH, transcendentals=0
        ),
        name="post",
    )(sc, resid, back.reshape(whole), cotangent, mixed, weight, gain)


def unmix_kernel(carried, sc, *refs):
    shards, (v_own, v_far, grad_heads, mean, *rest) = refs[:8], refs[8:]
    rest = rest[2:] if carried else rest
    outs, (own, far, raw, grads, mask, adder, bound, sems, out_sems) = rest[:8], rest[8:]
    place = sc[PLACE]
    step = pl.program_id(0)

    def leave(slot):
        return [
            pltpu.make_async_copy(
                grads.at[slot, pl.ds(pl.multiple_of((place ^ rel) * SUBS * HALF, SUBS * HALF), SUBS * HALF)],
                outs[4 * slot + rel],
                out_sems.at[slot, rel],
            )
            for rel in range(4)
        ]

    fill_mask(sc, mask)

    @pl.when(step == 0)
    def _():
        lane = lax.broadcasted_iota(jnp.int32, (4 * HEAD, 128), 0) // HEAD
        column = lax.broadcasted_iota(jnp.int32, (4 * HEAD, 128), 1)
        adder[...] = jnp.where((lane == column) | (lane + 4 == column), -1.0, 0.0).astype(BF16)
        row = lax.broadcasted_iota(jnp.int32, (LMAX, 128), 0)
        item = lax.broadcasted_iota(jnp.int32, (LMAX, 128), 1)
        length = jnp.where(item % 4 == 0, sc[LENGTHS], sc[LENGTHS + 1])
        length = jnp.where(item % 4 == 2, sc[LENGTHS + 2], length)
        length = jnp.where(item % 4 == 3, sc[LENGTHS + 3], length)
        bound[...] = jnp.where((item < 8) & (row < length), 1.0, 0.0).astype(BF16)

    slot = take_plane(place, shards, raw, sems)
    high_lanes = lax.broadcasted_iota(jnp.int32, (HROWS, 128), 1) < 4
    for head in range(PHEADS):
        weights = jnp.exp(raw[slot, head_rows(head)].astype(F32)).astype(BF16)
        low = (grad_heads[head].astype(F32) * inverse_sums(sc, weights, mask)).astype(BF16)
        product = low.astype(F32) * mean[head]
        coarse = product.astype(BF16)
        fine = (product - coarse.astype(F32)).astype(BF16)
        delta = dot(coarse, adder[...], 1, 0) + dot(fine, adder[...], 1, 0)
        coarse = delta.astype(BF16)
        fine = (delta - coarse.astype(F32)).astype(BF16)
        left = jnp.concatenate([low, jnp.where(high_lanes, coarse, fine)], axis=1)
        score = dot(left, jnp.concatenate([v_own[head], v_far[head], bound[...]], axis=1), 1, 1)
        grads[slot, head_rows(head)] = (score * weights.astype(F32)).astype(BF16)
        back = (dot(weights, low, 0, 0) * mask[...].astype(F32)).astype(BF16)
        own[head] = back[:, : 2 * HEAD]
        far[head] = back[:, 2 * HEAD :]
    for which in range(2):

        @pl.when(step == which)
        def _():
            for copy in leave(which):
                copy.start()
            if which == 1:
                for copy in leave(0) + leave(1):
                    copy.wait()


def run_unmix(sc, planes, shards, v_own, v_far, grad_heads, mean, carry):
    carry = list(carry)
    return pl.pallas_call(
        partial(unmix_kernel, bool(carry)),
        grid_spec=pltpu.PrefetchScalarGridSpec(
            num_scalar_prefetch=1,
            grid=(2,),
            in_specs=anywhere(8)
            + [plane_spec(planes, LMAX, 2 * HEAD)] * 2
            + [plane_spec(planes, HROWS, 4 * HEAD)] * 2
            + anywhere(len(carry)),
            out_specs=anywhere(8) + [plane_spec(planes, LMAX, 2 * HEAD)] * 2,
            scratch_shapes=[
                pltpu.VMEM((2, 4 * SUBS * HALF, LMAX), BF16),
                pltpu.VMEM((2, 4 * SUBS * HALF, LMAX), BF16),
                pltpu.VMEM((LMAX, 4 * HEAD), BF16),
                pltpu.VMEM((4 * HEAD, 128), BF16),
                pltpu.VMEM((LMAX, 128), BF16),
                pltpu.SemaphoreType.DMA((2, 4)),
                pltpu.SemaphoreType.DMA((2, 4)),
            ],
        ),
        out_shape=[jax.ShapeDtypeStruct((SUBS * HALF, LMAX), BF16)] * 8
        + [jax.ShapeDtypeStruct((HEADS, LMAX, 2 * HEAD), BF16)] * 2,
        input_output_aliases={13 + i: 8 + i for i in range(len(carry))},
        compiler_params=params(VMEM),
        cost_estimate=pl.CostEstimate(
            flops=3 * HEADS * HROWS * LMAX * 4 * HEAD,
            bytes_accessed=HEADS * (2 * HROWS * LMAX + 4 * HROWS * 256 + 4 * LMAX * 256),
            transcendentals=HEADS * HROWS * LMAX // 2,
        ),
        name="unmix",
    )(sc, *shards, v_own, v_far, grad_heads, mean, *carry)


def close_kernel(sc, tok, res_own, res_got, out_own, out_got, own, far, gain, weight, *refs):
    (output, tok_grad, d_value, d_gain, total) = refs
    step = pl.program_id(0)
    core = sc[CORE]
    output[:, :, core] = out_own[...].astype(F32)
    output[:, :, 1 - core] = out_got[...].astype(F32)
    tok_grad[:, :, core] = res_own[...].astype(F32)
    tok_grad[:, :, 1 - core] = res_got[...].astype(F32)
    runs = tok.shape[1]
    rows = runs * 128
    for item in range(2):
        lanes = slice(item * HEAD, (item + 1) * HEAD)
        pieces = [
            add_low(own[head, :, lanes], far[head, :, lanes]) for head in range(HEADS)
        ]
        back = jnp.concatenate(pieces, axis=1)
        x = tok[item].reshape(rows, WIDTH).astype(F32)
        scale = lax.rsqrt(jnp.mean(x * x, axis=-1, keepdims=True) + EPSILON)
        unit = x * scale
        normed = (unit * gain[...]).astype(BF16)
        normed_grad = dot(back, weight[...], 1, 1)
        gained = normed_grad * gain[...]
        update = scale * (gained - unit * jnp.mean(gained * unit, axis=-1, keepdims=True))
        tok_grad[item] += update.reshape(runs, 2, HALF, WIDTH)
        gain_sum = jnp.sum(normed_grad * unit, axis=0, keepdims=True)
        value_sum = dot(normed, back, 0, 0)
        if item == 0:
            gain_total, value_total = gain_sum, value_sum
        else:
            gain_total, value_total = gain_total + gain_sum, value_total + value_sum

    @pl.when(step == 0)
    def _():
        d_gain[...] = gain_total
        total[...] = value_total

    @pl.when(step > 0)
    def _():
        d_gain[...] += gain_total
        total[...] += value_total

    @pl.when(step == pl.num_programs(0) - 1)
    def _():
        low = total[...].astype(BF16)
        d_value[0] = low[:, :SIDE]
        d_value[1] = low[:, SIDE:]


def run_close(sc, tokens, res_own, res_got, out_own, out_got, own, far, gain, weight):
    runs = 2
    slab = (2, RUNS, 2, HALF, WIDTH)
    half = (2, RUNS, HALF, WIDTH)
    whole_spec = spec((2, runs, 2, HALF, WIDTH), lambda j, s: (0, j, 0, 0, 0))
    half_spec = spec((2, runs, HALF, WIDTH), lambda j, s: (0, j, 0, 0))
    back_spec = spec((HEADS, runs * 128, 2 * HEAD), lambda j, s: (0, j, 0))
    return pl.pallas_call(
        close_kernel,
        grid_spec=pltpu.PrefetchScalarGridSpec(
            num_scalar_prefetch=1,
            grid=(RUNS // runs,),
            in_specs=[whole_spec]
            + [half_spec] * 4
            + [back_spec, back_spec, held((1, WIDTH)), held((WIDTH, WIDTH))],
            out_specs=[whole_spec, whole_spec, held((2, WIDTH, SIDE)), held((1, WIDTH))],
            scratch_shapes=[pltpu.VMEM((WIDTH, WIDTH), F32)],
        ),
        out_shape=[
            jax.ShapeDtypeStruct(slab, F32),
            jax.ShapeDtypeStruct(slab, F32),
            jax.ShapeDtypeStruct((2, WIDTH, SIDE), BF16),
            jax.ShapeDtypeStruct((1, WIDTH), F32),
        ],
        compiler_params=params(VMEM),
        cost_estimate=pl.CostEstimate(
            flops=4 * 2 * LMAX * WIDTH * WIDTH, bytes_accessed=38 * LMAX * WIDTH, transcendentals=0
        ),
        name="close",
    )(
        sc,
        tokens.reshape(slab),
        *(x.reshape(half) for x in (res_own, res_got, out_own, out_got)),
        own,
        far,
        gain,
        weight,
    )


def place_kernel(sc, *refs):
    pieces, target, sems = refs[:16], refs[16], refs[17]
    copies = [
        pltpu.make_async_copy(piece, target.at[plane_of(i // 4, sc) * 4 + (sc[PLACE] ^ (i % 4))], sems.at[i])
        for i, piece in enumerate(pieces)
    ]
    for copy in copies:
        copy.start()
    for copy in copies:
        copy.wait()


def run_place(sc, pieces):
    shape = (16, *pieces[0].shape)
    return pl.pallas_call(
        place_kernel,
        grid_spec=pltpu.PrefetchScalarGridSpec(
            num_scalar_prefetch=1,
            grid=(1,),
            in_specs=anywhere(16),
            out_specs=held(shape),
            scratch_shapes=[pltpu.SemaphoreType.DMA((16,))],
        ),
        out_shape=jax.ShapeDtypeStruct(shape, BF16),
        compiler_params=params(VMEM),
        name="place",
    )(sc, *pieces)


def add_kernel(groups, *refs):
    for group, total in zip(groups, refs[-len(groups) :]):
        value = refs[group[0]][...].astype(F32)
        for index in group[1:]:
            value = value + refs[index][...].astype(F32)
        total[...] = value.astype(total.dtype)


def run_add(groups, values, dtype):
    rows, columns = values[0].shape
    parts = 2 if columns == LMAX else 1
    block = pl.BlockSpec((rows // parts, columns), lambda i: (i, 0))
    return pl.pallas_call(
        partial(add_kernel, groups),
        grid=(parts,),
        in_specs=[block] * len(values),
        out_specs=[block] * len(groups),
        out_shape=[jax.ShapeDtypeStruct((rows, columns), dtype)] * len(groups),
        compiler_params=params(VMEM),
        cost_estimate=pl.CostEstimate(
            flops=0, bytes_accessed=2 * rows * columns * (len(values) + len(groups)), transcendentals=0
        ),
        name="add",
    )(*values)


DEVICES = 32
TO_CORE, TO_X, TO_Y = 1, 2, 4


def swap(x, bit):
    return lax.ppermute(x, BOTH, [(d, d ^ bit) for d in range(DEVICES)])


def ring(x, way=1):
    return lax.ppermute(x, BOTH, [(d, (d + 8 * way) % DEVICES) for d in range(DEVICES)])


def pick(x, index, axis=0):
    return lax.dynamic_index_in_dim(x, index, axis, keepdims=False)


def ordered(flag, one, two, axis=0, joined=jnp.stack):
    return jnp.where(flag == 0, joined([one, two], axis), joined([two, one], axis))


def add_low(one, two):
    return (one.astype(F32) + two.astype(F32)).astype(BF16)


STEPS = (
    ((0, 0, 1), (0, 1, 0), (1, 0, 0)),
    ((1, 0, 1), (0, 1, 1), (2, 0, 0)),
    ((2, 0, 1), (1, 1, 0), (3, 0, 0)),
    ((3, 0, 1), (2, 1, 0), (1, 1, 1)),
    ((2, 1, 1), (3, 1, 1), (3, 1, 0)),
)


def gather_step(have, step):
    by_x, by_y, by_z = STEPS[step]
    return {
        **have,
        by_z: ring(have[by_z[0] - 1, by_z[1], by_z[2]]),
        by_x: swap(have[by_x[0], by_x[1], 0], TO_X),
        by_y: swap(have[by_y[0], 0, by_y[2]], TO_Y),
    }


def in_order(have):
    return [have[k, y, x] for k in range(4) for y in range(2) for x in range(2)]


def by_place(shares, planes=range(PLANES)):
    return {(k, i // 2, i % 2): shares[4 * at + i] for at, k in enumerate(planes) for i in range(4)}


def scatter_send(have, step):
    by_x, by_y, by_z = STEPS[len(STEPS) - 1 - step]
    got = (ring(have[by_z], -1), swap(have[by_x], TO_X), swap(have[by_y], TO_Y))
    return {at: value for at, value in have.items() if at not in (by_x, by_y, by_z)}, got


def scatter_add(have, got, step):
    by_x, by_y, by_z = STEPS[len(STEPS) - 1 - step]
    targets = ((by_z[0] - 1, by_z[1], by_z[2]), (by_x[0], by_x[1], 0), (by_y[0], 0, by_y[2]))
    sums = list(dict.fromkeys(targets))
    groups = [(len(got) + i, *(j for j in range(len(got)) if targets[j] == at)) for i, at in enumerate(sums)]
    values = [*got, *(have[at] for at in sums)]
    return {**have, **dict(zip(sums, run_add(groups, values, F32 if step == len(STEPS) - 1 else BF16)))}


together = lax.optimization_barrier


def chip_shards(tokens, lengths, rand_mix, w_value, w_out, w_up, w_down, gain_mix, gain_ffn, grad_out):
    wide = lax.axis_index("wide")
    core = lax.axis_index("narrow")
    z, y, x = wide // 4, (wide // 2) % 2, wide % 2
    other = lambda value: swap(value, TO_CORE)
    side = partial(ordered, core, joined=jnp.concatenate)
    slab = (2, RUNS, 2, HALF, WIDTH)
    tokens, grad_out = tokens.reshape(slab), grad_out.reshape(slab)

    packed = jnp.concatenate([w_out, w_down, *(w_up[:, j * WIDTH : (j + 1) * WIDTH] for j in range(4))])
    packed = lax.all_gather(packed, BOTH, axis=0)

    gains = jnp.pad(jnp.concatenate([gain_mix, gain_ffn])[None], ((0, 7), (0, WIDTH - 48)))
    firsts = {(0, 0, 0): jnp.concatenate([w_value, gains])}
    rand = rand_mix.reshape(3, 2, HALF, LMAX)
    blocks = side(pick(rand, core, 1), other(pick(rand, 1 - core, 1)), 0)
    firsts, rands, far_lengths = together(
        (gather_step(firsts, 0), {(0, 0, 0): blocks.reshape(SUBS * HALF, LMAX)}, other(lengths))
    )
    sc = jnp.concatenate([jnp.stack([core, z, wide % 4]).astype(jnp.int32), lengths, far_lengths])
    for step in range(1, 5):
        firsts = together(gather_step(firsts, step))
    firsts, rands = together((firsts, rands))

    rands = gather_step(rands, 0)
    first = run_place(sc, in_order(firsts))
    rands, first, first_far = together((rands, first, other(first)))
    both = ordered(core, first, first_far, 1)
    value = both[:, :, :24].reshape(WIDTH, WIDTH)
    gain_one = both[:, :, 24, :24].reshape(1, WIDTH).astype(F32)
    gain_two = both[:, :, 24, 24:48].reshape(1, WIDTH).astype(F32)
    rands = gather_step(rands, 1)
    v_own = run_values(sc, tokens.reshape(2, LMAX, WIDTH), gain_one, value)
    rands, v_own, tokens_far = together((rands, v_own, other(pick(tokens, 1 - core, 2))))
    rands, v_own, v_far = together((gather_step(rands, 2), v_own, other(v_own)))
    rands, v_far, grad_far = together((gather_step(rands, 3), v_far, other(pick(grad_out, 1 - core, 2))))
    near = [rands[k, y_at, x_at] for k in range(2) for y_at in range(2) for x_at in range(2)]
    rands = gather_step(rands, 4)
    mixing = run_mix(sc, (0, 1), near, v_own, v_far, ())
    rands, mixing = together((rands, mixing))
    shares = in_order(rands)
    heads, mean = run_mix(sc, (2, 3), shares[8:], v_own, v_far, mixing)

    out = packed[:, :24].reshape(WIDTH, WIDTH)
    down = packed[:, 24:120].reshape(FF, WIDTH)
    up = packed[:, 120:].reshape(32, 4, 24, WIDTH).transpose(1, 0, 2, 3).reshape(4, WIDTH, WIDTH)
    mixed, resid, normed, masked = run_pre(sc, tokens, tokens_far, grad_out, grad_far, heads, out, gain_two)
    active, up_grad, back = run_units(sc, normed, masked, up, down)

    d_down = run_down_grad(active, masked).reshape(32, 96, WIDTH)
    d_up = run_up_grad(normed, up_grad).reshape(4, 32, 24, WIDTH).transpose(1, 0, 2, 3).reshape(32, 96, WIDTH)
    packed, back = together((jnp.concatenate([d_down, d_up], axis=1), back))
    packed = lax.psum_scatter(packed, BOTH, scatter_dimension=0)

    res_own, res_far, grad_heads, d_out, d_gain_two = run_post(sc, resid, back, masked, mixed, out, gain_two)
    *far, back_own, back_far = run_unmix(
        sc, (3, 2), shares[12:] + shares[8:12], v_own, v_far, grad_heads, mean, ()
    )
    far, back_own, back_far, res_got = together((far, back_own, back_far, other(res_far)))
    have, got = scatter_send(by_place(far, (3, 2)), 0)
    *near, back_own, back_far = run_unmix(
        sc, (1, 0), shares[4:8] + shares[:4], v_own, v_far, grad_heads, mean, (back_own, back_far)
    )
    have, got, near, back_own, back_far = together((have, got, near, back_own, back_far))
    have = {**scatter_add(have, got, 0), **by_place(near, (1, 0))}

    have, got = scatter_send(have, 1)
    out_own, out_far = run_out(sc, active, resid, down)
    have, got, out_own, out_far, back_got = together((have, got, out_own, out_far, other(back_far)))
    have = scatter_add(have, got, 1)

    have, got = scatter_send(have, 2)
    output, tokens_grad, d_value, d_gain_one = run_close(
        sc, tokens, res_own, res_got, out_own, other(out_far), back_own, back_got, gain_one, value
    )
    gain_pair = jnp.concatenate([d_gain_one, d_gain_two]).reshape(2, 16, 1, 48).astype(BF16)
    gain_pair = jnp.pad(gain_pair, ((0, 0), (0, 0), (0, 15), (0, SIDE - 48)))
    small = jnp.concatenate([d_value.reshape(2, 16, 48, SIDE), d_out.reshape(2, 16, 48, SIDE), gain_pair], 2)
    have, got, small, output, tokens_grad = together((have, got, small, output, tokens_grad))
    have = scatter_add(have, got, 2)

    have, got = scatter_send(have, 3)
    small = add_low(pick(small, core), other(pick(small, 1 - core))).reshape(4, 2, 2, 112, SIDE)
    small = add_low(pick(small, x, 2), swap(pick(small, 1 - x, 2), TO_X))
    have, got, small = together((have, got, small))
    have = scatter_add(have, got, 3)

    have, got = scatter_send(have, 4)
    small = add_low(pick(small, y, 1), swap(pick(small, 1 - y, 1), TO_Y))
    small_sum = pick(small, z).astype(F32)
    for k in range(1, PLANES):
        small_sum = small_sum + ring(pick(small, lax.rem(z + PLANES - k, PLANES)), -k).astype(F32)
    have, got, small_sum = together((have, got, small_sum))
    rand_sum = scatter_add(have, got, 4)[0, 0, 0].reshape(2, 3, HALF, LMAX)
    blocks, blocks_far = pick(rand_sum, core), other(pick(rand_sum, 1 - core))
    small_far = other(small_sum)

    rows_of = lambda value: pick(value.reshape(2, 24, SIDE), core)
    value_shard = side(rows_of(small_sum[:48]), rows_of(small_far[:48]), 1)
    outproj_shard = side(rows_of(small_sum[48:96]), rows_of(small_far[48:96]), 1)
    down_shard = packed[:96].astype(F32)
    up_shard = packed[96:].reshape(4, 24, WIDTH).transpose(1, 0, 2).reshape(24, FF).astype(F32)
    gains_pair = ordered(core, small_sum[96, :48], small_far[96, :48])
    gain_pair = pick(gains_pair.reshape(2, 2, 24), core, 1)

    rand_shard = ordered(core, blocks, blocks_far, 1)

    return (
        output.reshape(2, LMAX, WIDTH),
        tokens_grad.reshape(2, LMAX, WIDTH),
        rand_shard.reshape(3 * 128, LMAX),
        value_shard,
        outproj_shard,
        up_shard,
        down_shard,
        gain_pair[0],
        gain_pair[1],
    )


def rms_norm(values, gain):
    scale = lax.rsqrt(jnp.mean(values * values, axis=-1, keepdims=True) + EPSILON)
    return values * scale * gain


def split_heads(block):
    return block.reshape(LMAX, HEADS, HEAD).transpose(1, 0, 2)


def merge_heads(block):
    return block.transpose(1, 0, 2).reshape(LMAX, HEADS * HEAD)


def masked_scores(key_mask, rand_head):
    return jnp.where(key_mask[None, :] > 0, rand_head.astype(jnp.float32), -1e30)


def head_forward(key_mask, paired):
    rand_head, value_head = paired
    scores = masked_scores(key_mask, rand_head)
    row_peak = jnp.max(scores, axis=-1, keepdims=True)
    exponent = jnp.exp(scores - row_peak)
    denom_sum = jnp.sum(exponent, axis=-1, keepdims=True)
    attention = exponent / denom_sum * key_mask[:, None]
    mixed = jnp.dot(attention.astype(jnp.bfloat16), value_head, preferred_element_type=jnp.float32)
    return (mixed.astype(jnp.bfloat16), row_peak + jnp.log(denom_sum))


def head_backward(key_mask, paired):
    rand_head, value_head, mix_grad, log_total = paired
    scores = masked_scores(key_mask, rand_head)
    attention = jnp.exp(scores - log_total) * key_mask[:, None]
    prob_grad = jnp.einsum("id,jd->ij", mix_grad, value_head, preferred_element_type=jnp.float32)
    value_grad = jnp.einsum(
        "ij,id->jd", attention.astype(jnp.bfloat16), mix_grad, preferred_element_type=jnp.float32
    )
    score_grad = attention * (prob_grad - jnp.sum(prob_grad * attention, axis=-1, keepdims=True))
    return (score_grad, value_grad)


def shards(tokens, lengths, rand_mix, w_value, w_out, w_up, w_down, gain_mix, gain_ffn, grad_out):
    item_count = tokens.shape[0]
    width = tokens.shape[2]
    row_count = item_count * LMAX
    tokens_flat = tokens.reshape(row_count, width).astype(jnp.float32)
    positions = jnp.arange(LMAX, dtype=jnp.int32)
    valid_table = (positions[None, :] < lengths[:, None]).astype(jnp.float32)
    row_valid = valid_table.reshape(row_count, 1)
    forward_set = (
        lax.all_gather(rand_mix, ("wide", "narrow"), axis=0, tiled=True),
        lax.all_gather(w_value, ("wide", "narrow"), axis=0, tiled=True),
        lax.all_gather(w_out, ("wide", "narrow"), axis=0, tiled=True),
        lax.all_gather(w_up, ("wide", "narrow"), axis=0, tiled=True),
        lax.all_gather(w_down, ("wide", "narrow"), axis=0, tiled=True),
        lax.all_gather(gain_mix, ("wide", "narrow"), axis=0, tiled=True),
        lax.all_gather(gain_ffn, ("wide", "narrow"), axis=0, tiled=True),
    )
    rand_all, value_all, out_all, up_all, down_all, gain_first, gain_second = forward_set
    normed = rms_norm(tokens_flat, gain_first.astype(jnp.float32)).astype(jnp.bfloat16)
    values = jnp.dot(normed, value_all, preferred_element_type=jnp.float32).astype(jnp.bfloat16)
    rand_heads = rand_all.reshape(HEADS, LMAX, LMAX)
    mixed_parts = []
    totals_kept = []
    for item_index in range(item_count):
        item_values = split_heads(values[item_index * LMAX : (item_index + 1) * LMAX])
        mixed_heads, log_total = lax.map(
            partial(head_forward, valid_table[item_index]), (rand_heads, item_values)
        )
        mixed_parts.append(merge_heads(mixed_heads))
        totals_kept.append(log_total)
    mixed = jnp.concatenate(mixed_parts, axis=0)
    residual = tokens_flat + jnp.dot(mixed, out_all, preferred_element_type=jnp.float32)
    normed_two = rms_norm(residual, gain_second.astype(jnp.float32)).astype(jnp.bfloat16)
    up_proj = jnp.dot(normed_two, up_all, preferred_element_type=jnp.float32)
    active = jax.nn.gelu(up_proj).astype(jnp.bfloat16)
    branch = jnp.dot(active, down_all, preferred_element_type=jnp.float32)
    output = row_valid * (residual + branch)
    back_set = (
        lax.all_gather(rand_mix, ("wide", "narrow"), axis=0, tiled=True),
        lax.all_gather(w_value, ("wide", "narrow"), axis=0, tiled=True),
        lax.all_gather(w_out, ("wide", "narrow"), axis=0, tiled=True),
        lax.all_gather(w_up, ("wide", "narrow"), axis=0, tiled=True),
        lax.all_gather(w_down, ("wide", "narrow"), axis=0, tiled=True),
        lax.all_gather(gain_mix, ("wide", "narrow"), axis=0, tiled=True),
        lax.all_gather(gain_ffn, ("wide", "narrow"), axis=0, tiled=True),
    )
    rand_back, value_back, out_back, up_back, down_back, gain_back_one, gain_back_two = back_set
    cotangent = grad_out.reshape(row_count, width).astype(jnp.float32)
    masked = row_valid * cotangent
    branch_grad = masked.astype(jnp.bfloat16)
    grad_down = jnp.einsum("rk,rd->kd", active, branch_grad, preferred_element_type=jnp.float32)
    active_grad = jnp.einsum(
        "rd,kd->rk", branch_grad, down_back, preferred_element_type=jnp.float32
    )
    gelu_value, gelu_pull = jax.vjp(jax.nn.gelu, up_proj)
    up_grad = gelu_pull(active_grad)[0].astype(jnp.bfloat16)
    grad_up = jnp.einsum("rd,rk->dk", normed_two, up_grad, preferred_element_type=jnp.float32)
    normed_two_grad = jnp.einsum("rk,dk->rd", up_grad, up_back, preferred_element_type=jnp.float32)
    norm_value, norm_pull = jax.vjp(rms_norm, residual, gain_back_two.astype(jnp.float32))
    residual_part, gain_two_grad = norm_pull(normed_two_grad)
    residual_grad = masked + residual_part
    attn_grad = residual_grad.astype(jnp.bfloat16)
    grad_outproj = jnp.einsum("rd,re->de", mixed, attn_grad, preferred_element_type=jnp.float32)
    mixed_grad = jnp.einsum(
        "re,de->rd", attn_grad, out_back, preferred_element_type=jnp.float32
    ).astype(jnp.bfloat16)
    rand_heads_back = rand_back.reshape(HEADS, LMAX, LMAX)
    rand_grad = jnp.zeros((HEADS, LMAX, LMAX), jnp.float32)
    value_parts = []
    for item_index in range(item_count):
        lower_row = item_index * LMAX
        upper_row = lower_row + LMAX
        item_values = split_heads(values[lower_row:upper_row])
        item_mix_grad = split_heads(mixed_grad[lower_row:upper_row])
        score_grad, value_grad = lax.map(
            partial(head_backward, valid_table[item_index]),
            (rand_heads_back, item_values, item_mix_grad, totals_kept[item_index]),
        )
        rand_grad = rand_grad + score_grad
        value_parts.append(merge_heads(value_grad))
    values_grad = jnp.concatenate(value_parts, axis=0).astype(jnp.bfloat16)
    grad_value = jnp.einsum("rd,re->de", normed, values_grad, preferred_element_type=jnp.float32)
    normed_grad = jnp.einsum(
        "re,de->rd", values_grad, value_back, preferred_element_type=jnp.float32
    )
    norm_first, first_pull = jax.vjp(rms_norm, tokens_flat, gain_back_one.astype(jnp.float32))
    token_part, gain_one_grad = first_pull(normed_grad)
    tokens_grad = residual_grad + token_part
    rand_flat = rand_grad.reshape(HEADS * LMAX, LMAX)
    all_shards = (
        lax.psum_scatter(rand_flat, ("wide", "narrow"), scatter_dimension=0, tiled=True),
        lax.psum_scatter(grad_value, ("wide", "narrow"), scatter_dimension=0, tiled=True),
        lax.psum_scatter(grad_outproj, ("wide", "narrow"), scatter_dimension=0, tiled=True),
        lax.psum_scatter(grad_up, ("wide", "narrow"), scatter_dimension=0, tiled=True),
        lax.psum_scatter(grad_down, ("wide", "narrow"), scatter_dimension=0, tiled=True),
        lax.psum_scatter(gain_one_grad, ("wide", "narrow"), scatter_dimension=0, tiled=True),
        lax.psum_scatter(gain_two_grad, ("wide", "narrow"), scatter_dimension=0, tiled=True),
    )
    rand_shard, value_shard, outproj_shard, up_shard, down_shard, gain_one_shard, gain_two_shard = (
        all_shards
    )
    return (
        output.reshape(item_count, LMAX, width),
        tokens_grad.reshape(item_count, LMAX, width),
        rand_shard,
        value_shard,
        outproj_shard,
        up_shard,
        down_shard,
        gain_one_shard,
        gain_two_shard,
    )


def solution(mesh):
    in_specs = (
        P(("wide", "narrow"), None, None),
        P(("wide", "narrow")),
        P(("wide", "narrow"), None),
        P(("wide", "narrow"), None),
        P(("wide", "narrow"), None),
        P(("wide", "narrow"), None),
        P(("wide", "narrow"), None),
        P(("wide", "narrow")),
        P(("wide", "narrow")),
        P(("wide", "narrow"), None, None),
    )
    out_specs = (
        P(("wide", "narrow"), None, None),
        P(("wide", "narrow"), None, None),
        P(("wide", "narrow"), None),
        P(("wide", "narrow"), None),
        P(("wide", "narrow"), None),
        P(("wide", "narrow"), None),
        P(("wide", "narrow"), None),
        P(("wide", "narrow")),
        P(("wide", "narrow")),
    )
    fits = dict(mesh.shape) == {"wide": 16, "narrow": 2}
    return jax.shard_map(chip_shards if fits else shards, mesh=mesh, in_specs=in_specs, out_specs=out_specs, check_vma=False)
```

```python
from functools import partial

import jax
import jax.numpy as jnp
from jax import lax
from jax.experimental import pallas as pl
from jax.experimental.pallas import tpu as pltpu
from jax.sharding import PartitionSpec as P

HEADS = 12
HEAD = 64
LMAX = 1024
WIDTH = 768
FF = 3072
EPSILON = 1e-05

BOTH = ("wide", "narrow")
BF16 = jnp.bfloat16
F32 = jnp.float32
VMEM = 61 << 20

PARTS = 2
SUBS = 6 // PARTS
RUNS = 8 // PARTS
HALF = 64
HROWS = RUNS * HALF
PLANES = 4
PHEADS = HEADS // PLANES
ROWS = 4 * HROWS
FSTEP = 768
TILE = 512
SIDE = WIDTH // 2
SPAN = 2 * HALF


def dot(a, b, ca, cb):
    return lax.dot_general(a, b, (((ca,), (cb,)), ((), ())), preferred_element_type=F32)


CORE, PLANE, PLACE, LENGTHS = 0, 1, 2, 3


def spec(shape, index):
    return pl.BlockSpec(shape, index)


def held(shape):
    zeros = (0,) * len(shape)
    return pl.BlockSpec(shape, lambda *_: zeros, pipeline_mode=pl.Buffered(1))


def params(limit):
    return pltpu.CompilerParams(vmem_limit_bytes=limit)


def values_kernel(sc, tok, gain, weight, out):
    step = pl.program_id(0)
    rows = tok.shape[1]
    position = step * rows + lax.broadcasted_iota(jnp.int32, (rows, 1), 0)
    for item in range(2):
        x = tok[item].astype(F32)
        scale = lax.rsqrt(jnp.mean(x * x, axis=-1, keepdims=True) + EPSILON)
        normed = (x * scale * gain[...]).astype(BF16)
        found = dot(normed, weight[...], 1, 0)
        found = jnp.where(position < sc[LENGTHS + item], found, 0.0).astype(BF16)
        for head in range(HEADS):
            out[head, :, item * HEAD : (item + 1) * HEAD] = found[:, head * HEAD : (head + 1) * HEAD]


def run_values(sc, tokens, gain, weight):
    rows = 256
    return pl.pallas_call(
        values_kernel,
        grid_spec=pltpu.PrefetchScalarGridSpec(
            num_scalar_prefetch=1,
            grid=(LMAX // rows,),
            in_specs=[
                spec((2, rows, WIDTH), lambda j, s: (0, j, 0)),
                held((1, WIDTH)),
                held((WIDTH, WIDTH)),
            ],
            out_specs=spec((HEADS, rows, 2 * HEAD), lambda j, s: (0, j, 0)),
        ),
        out_shape=jax.ShapeDtypeStruct((HEADS, LMAX, 2 * HEAD), BF16),
        compiler_params=params(VMEM),
        cost_estimate=pl.CostEstimate(
            flops=2 * 2 * LMAX * WIDTH * WIDTH, bytes_accessed=8 * LMAX * WIDTH, transcendentals=0
        ),
        name="values",
    )(sc, tokens, gain, weight)


def lane_lengths(sc, shape):
    slot = lax.broadcasted_iota(jnp.int32, shape, 1) // HEAD
    length = jnp.where(slot == 0, sc[LENGTHS], sc[LENGTHS + 1])
    return jnp.where(slot >= 2, jnp.where(slot == 2, sc[LENGTHS + 2], sc[LENGTHS + 3]), length)


def plane_of(k, sc):
    return lax.rem(sc[PLANE] + PLANES - k, PLANES)


def plane_spec(planes, rows, lanes):
    def index(step, sc):
        return (plane_of(planes[0] + step * (planes[1] - planes[0]), sc), 0, 0)

    return spec((PHEADS, rows, lanes), index)


def anywhere(count):
    return [pl.BlockSpec(memory_space=pl.ANY)] * count


def plane_fetch(place, shards, raw, sems, slot):
    return [
        pltpu.make_async_copy(
            shards[4 * slot + rel],
            raw.at[slot, pl.ds(pl.multiple_of((place ^ rel) * SUBS * HALF, SUBS * HALF), SUBS * HALF)],
            sems.at[slot, rel],
        )
        for rel in range(4)
    ]


def take_plane(place, shards, raw, sems):
    step = pl.program_id(0)

    @pl.when(step == 0)
    def _():
        for slot in range(2):
            for copy in plane_fetch(place, shards, raw, sems, slot):
                copy.start()

    for slot in range(2):

        @pl.when(step == slot)
        def _():
            for copy in plane_fetch(place, shards, raw, sems, slot):
                copy.wait()

    return step


def head_rows(head):
    return slice(head * HROWS, (head + 1) * HROWS)


def fill_mask(sc, mask):
    @pl.when(pl.program_id(0) == 0)
    def _():
        shape = (LMAX, 4 * HEAD)
        column = lax.broadcasted_iota(jnp.int32, shape, 0)
        mask[...] = (column < lane_lengths(sc, shape)).astype(F32).astype(BF16)


def inverse_sums(part, sc, weights, mask):
    shape = (HROWS, 4 * HEAD)
    line = lax.broadcasted_iota(jnp.int32, shape, 0)
    position = 128 * (PARTS * (line // HALF) + part) + HALF * sc[CORE] + line % HALF
    return jnp.where(position < lane_lengths(sc, shape), 1.0 / dot(weights, mask[...], 1, 0), 0.0)


def mix_kernel(part, carried, sc, *refs):
    shards, (v_own, v_far, *rest) = refs[:8], refs[8:]
    mixed, mean, raw, mask, sems = rest[2:] if carried else rest
    fill_mask(sc, mask)
    slot = take_plane(sc[PLACE], shards, raw, sems)
    for head in range(PHEADS):
        weights = jnp.exp(raw[slot, head_rows(head)].astype(F32)).astype(BF16)
        values = jnp.concatenate([v_own[head], v_far[head]], axis=1)
        found = dot(weights, values, 1, 0) * inverse_sums(part, sc, weights, mask)
        mean[head] = found
        mixed[head] = found.astype(BF16)


def run_mix(part, sc, planes, shards, v_own, v_far, carry):
    carry = list(carry)
    return pl.pallas_call(
        partial(mix_kernel, part, bool(carry)),
        grid_spec=pltpu.PrefetchScalarGridSpec(
            num_scalar_prefetch=1,
            grid=(2,),
            in_specs=anywhere(8) + [plane_spec(planes, LMAX, 2 * HEAD)] * 2 + anywhere(len(carry)),
            out_specs=[plane_spec(planes, HROWS, 4 * HEAD)] * 2,
            scratch_shapes=[
                pltpu.VMEM((2, 4 * SUBS * HALF, LMAX), BF16),
                pltpu.VMEM((LMAX, 4 * HEAD), BF16),
                pltpu.SemaphoreType.DMA((2, 4)),
            ],
        ),
        out_shape=[
            jax.ShapeDtypeStruct((HEADS, HROWS, 4 * HEAD), BF16),
            jax.ShapeDtypeStruct((HEADS, HROWS, 4 * HEAD), F32),
        ],
        input_output_aliases={11 + i: i for i in range(len(carry))},
        compiler_params=params(VMEM),
        cost_estimate=pl.CostEstimate(
            flops=2 * HEADS * HROWS * LMAX * 4 * HEAD,
            bytes_accessed=HEADS * (HROWS * LMAX + 5 * HROWS * 256),
            transcendentals=HEADS * HROWS * LMAX // 2,
        ),
        name="mix",
    )(sc, *shards, v_own, v_far, *carry)


def row_valid(part, sc, step):
    line = lax.broadcasted_iota(jnp.int32, (4 * SPAN, 1), 0)
    item = line // SPAN
    row = step * SPAN + line % SPAN
    low = jnp.where(item == 0, sc[LENGTHS], sc[LENGTHS + 1])
    high = jnp.where(item == 2, sc[LENGTHS + 2], sc[LENGTHS + 3])
    return 128 * (PARTS * (row // HALF) + part) + HALF * sc[CORE] + row % HALF < jnp.where(item >= 2, high, low)


def four_items(own, far):
    return jnp.concatenate([own[:, :, 0, 0], far[:, :, 0]], axis=0).reshape(4 * SPAN, WIDTH)


def pre_kernel(part, sc, tok, tok_far, cot, cot_far, heads, weight, gain, *refs):
    mixed, resid, normed, grad = refs[-4:]
    step = pl.program_id(0)
    for item in range(4):
        lanes = slice(item * HEAD, (item + 1) * HEAD)
        for pair in range(HEADS // 2):
            both = jnp.concatenate([heads[2 * pair, :, lanes], heads[2 * pair + 1, :, lanes]], axis=1)
            mixed[0, item, :, pair * 128 : (pair + 1) * 128] = both
    res = four_items(tok, tok_far).astype(F32) + dot(mixed[...].reshape(4 * SPAN, WIDTH), weight[...], 1, 0)
    slab = (1, 4, SPAN, WIDTH)
    resid[...] = res.astype(BF16).reshape(slab)
    scale = lax.rsqrt(jnp.mean(res * res, axis=-1, keepdims=True) + EPSILON)
    valid = row_valid(part, sc, step)
    normed[...] = jnp.where(valid, res * scale * gain[...], 0.0).astype(BF16).reshape(slab)
    masked = jnp.where(valid, four_items(cot, cot_far).astype(F32), 0.0)
    grad[...] = masked.astype(BF16).reshape(slab)


def slab_spec(part, items=4):
    return spec((1, items, SPAN, WIDTH), lambda r, s: (part, 0, r, 0))


def half_specs(part):
    return [
        spec((2, SPAN // HALF, 1, 1, HALF, WIDTH), lambda r, s: (0, r, part, s[CORE], 0, 0)),
        spec((2, SPAN // HALF, 1, HALF, WIDTH), lambda r, s: (0, r, part, 0, 0)),
    ]


def heads_spec():
    return spec((HEADS, SPAN, 4 * HEAD), lambda r, s: (0, r, 0))


def run_pre(part, sc, tokens, tokens_far, cotangent, cotangent_far, heads, weight, gain, carry):
    own = lambda x: x.reshape(2, RUNS, PARTS, 2, HALF, WIDTH)
    far = lambda x: x.reshape(2, RUNS, PARTS, HALF, WIDTH)
    return pl.pallas_call(
        partial(pre_kernel, part),
        grid_spec=pltpu.PrefetchScalarGridSpec(
            num_scalar_prefetch=1,
            grid=(HROWS // SPAN,),
            in_specs=half_specs(part)
            + half_specs(part)
            + [heads_spec(), held((WIDTH, WIDTH)), held((1, WIDTH))]
            + anywhere(len(carry)),
            out_specs=[slab_spec(part)] * 4,
        ),
        out_shape=[jax.ShapeDtypeStruct((PARTS, 4, HROWS, WIDTH), BF16)] * 4,
        input_output_aliases={8 + i: i for i in range(len(carry))},
        compiler_params=params(VMEM),
        cost_estimate=pl.CostEstimate(
            flops=2 * ROWS * WIDTH * WIDTH, bytes_accessed=16 * ROWS * WIDTH, transcendentals=0
        ),
        name="pre",
    )(sc, own(tokens), far(tokens_far), own(cotangent), far(cotangent_far), heads, weight, gain, *carry)


def units_kernel(sc, normed, cot, w_up, w_down, *refs):
    active, up_grad, back, total = refs[-4:]
    step = pl.program_id(0)
    for piece in range(ROWS // TILE):
        whole = slice(piece * TILE, (piece + 1) * TILE)
        for row in range(piece * TILE, (piece + 1) * TILE, 256):
            rows = slice(row, row + 256)
            for column in range(0, FSTEP, 256):
                columns = slice(column, column + 256)
                up = dot(normed[rows], w_up[0, :, columns], 1, 0)
                square = up * up
                bend = jnp.tanh(up * (0.7978845608028654 + (0.044715 * 0.7978845608028654) * square))
                share = 0.5 + 0.5 * bend
                act = up * share
                active[rows, columns] = act.astype(BF16)
                slope = share + act * (1.0 - share) * (
                    2 * 0.7978845608028654 + (6 * 0.044715 * 0.7978845608028654) * square
                )
                up_grad[rows, columns] = (dot(cot[rows], w_down[columns], 1, 1) * slope).astype(BF16)
        two_grad = dot(up_grad[whole], w_up[0], 1, 1)

        @pl.when(step == 0)
        def _():
            total[whole] = two_grad

        @pl.when((step > 0) & (step < FF // FSTEP - 1))
        def _():
            total[whole] += two_grad

        @pl.when(step == FF // FSTEP - 1)
        def _():
            back[whole] = (total[whole] + two_grad).astype(BF16)


def run_units(part, sc, normed, cotangent, w_up, w_down, carry):
    columns = spec((ROWS, FSTEP), lambda f, s: (part, f))
    rows = pl.BlockSpec((ROWS, WIDTH), lambda f, s: (part, 0), pipeline_mode=pl.Buffered(1))
    flat = lambda x: x.reshape(PARTS * ROWS, WIDTH)
    return pl.pallas_call(
        units_kernel,
        grid_spec=pltpu.PrefetchScalarGridSpec(
            num_scalar_prefetch=1,
            grid=(FF // FSTEP,),
            in_specs=[
                rows,
                rows,
                spec((1, WIDTH, FSTEP), lambda f, s: (f, 0, 0)),
                spec((FSTEP, WIDTH), lambda f, s: (f, 0)),
            ]
            + anywhere(len(carry)),
            out_specs=[columns, columns, held((ROWS, WIDTH))],
            scratch_shapes=[pltpu.VMEM((ROWS, WIDTH), F32)],
        ),
        out_shape=[
            jax.ShapeDtypeStruct((PARTS * ROWS, FF), BF16),
            jax.ShapeDtypeStruct((PARTS * ROWS, FF), BF16),
            jax.ShapeDtypeStruct((ROWS, WIDTH), BF16),
        ],
        input_output_aliases={5 + i: i for i in range(len(carry))},
        compiler_params=params(VMEM),
        cost_estimate=pl.CostEstimate(
            flops=6 * ROWS * WIDTH * FF, bytes_accessed=8 * ROWS * WIDTH + 4 * ROWS * FF, transcendentals=ROWS * FF
        ),
        name="units",
    )(sc, flat(normed), flat(cotangent), w_up, w_down, *carry)


def own_lanes(sc):
    return pl.ds(pl.multiple_of(sc[CORE] * SIDE, 128), SIDE)


def far_lanes(sc):
    return pl.ds(pl.multiple_of((1 - sc[CORE]) * SIDE, 128), SIDE)


def down_grad_kernel(sc, active, cot, own, far, total):
    total[...] = dot(active[...], cot[...], 0, 0).astype(BF16)
    own[...] = total[:, own_lanes(sc)]
    far[...] = total[:, far_lanes(sc)]


def run_down_grad(sc, active, cotangent):
    rows = PARTS * ROWS
    return pl.pallas_call(
        down_grad_kernel,
        grid_spec=pltpu.PrefetchScalarGridSpec(
            num_scalar_prefetch=1,
            grid=(FF // 512,),
            in_specs=[spec((rows, 512), lambda f, s: (0, f)), held((rows, WIDTH))],
            out_specs=[spec((512, SIDE), lambda f, s: (f, 0))] * 2,
            scratch_shapes=[pltpu.VMEM((512, WIDTH), BF16)],
        ),
        out_shape=[jax.ShapeDtypeStruct((FF, SIDE), BF16)] * 2,
        compiler_params=params(VMEM),
        cost_estimate=pl.CostEstimate(
            flops=2 * rows * WIDTH * FF, bytes_accessed=2 * rows * (WIDTH + FF), transcendentals=0
        ),
        name="down_grad",
    )(sc, active, cotangent.reshape(rows, WIDTH))


def up_grad_kernel(sc, normed, up_grad, own, far):
    total = dot(normed[...], up_grad[...], 0, 0).astype(BF16)

    @pl.when(pl.program_id(0) < 2)
    def _():
        own[...] = total

    @pl.when(pl.program_id(0) >= 2)
    def _():
        far[...] = total


def run_up_grad(sc, normed, up_grad):
    rows = PARTS * ROWS
    return pl.pallas_call(
        up_grad_kernel,
        grid_spec=pltpu.PrefetchScalarGridSpec(
            num_scalar_prefetch=1,
            grid=(4,),
            in_specs=[held((rows, WIDTH)), spec((rows, FF // 4), lambda f, s: (0, lax.rem(2 * s[CORE] + f, 4)))],
            out_specs=[
                spec((WIDTH, FF // 4), lambda f, s: (0, lax.min(f, 1))),
                spec((WIDTH, FF // 4), lambda f, s: (0, lax.max(f - 2, 0))),
            ],
        ),
        out_shape=[jax.ShapeDtypeStruct((WIDTH, FF // 2), BF16)] * 2,
        compiler_params=params(VMEM),
        cost_estimate=pl.CostEstimate(
            flops=2 * rows * WIDTH * FF, bytes_accessed=2 * rows * (WIDTH + FF), transcendentals=0
        ),
        name="up_grad",
    )(sc, normed.reshape(rows, WIDTH), up_grad)


def out_grad_kernel(sc, mixed, res_own, res_far, own, far, total):
    step = pl.program_id(0)
    grad = jnp.concatenate([res_own[...].reshape(ROWS // 2, WIDTH), res_far[...].reshape(ROWS // 2, WIDTH)], axis=0)
    found = dot(mixed[...].reshape(ROWS, WIDTH), grad, 0, 0)

    @pl.when(step == 0)
    def _():
        total[...] = found

    @pl.when(step > 0)
    def _():
        total[...] += found

    @pl.when(step == PARTS - 1)
    def _():
        own[...] = total[:, own_lanes(sc)].astype(BF16)
        far[...] = total[:, far_lanes(sc)].astype(BF16)


def run_out_grad(sc, mixed, res_own, res_far):
    block = lambda items: spec((1, items, HROWS, WIDTH), lambda p, s: (p, 0, 0, 0))
    return pl.pallas_call(
        out_grad_kernel,
        grid_spec=pltpu.PrefetchScalarGridSpec(
            num_scalar_prefetch=1,
            grid=(PARTS,),
            in_specs=[block(4), block(2), block(2)],
            out_specs=[held((WIDTH, SIDE))] * 2,
            scratch_shapes=[pltpu.VMEM((WIDTH, WIDTH), F32)],
        ),
        out_shape=[jax.ShapeDtypeStruct((WIDTH, SIDE), BF16)] * 2,
        compiler_params=params(VMEM),
        cost_estimate=pl.CostEstimate(
            flops=2 * PARTS * ROWS * WIDTH * WIDTH, bytes_accessed=4 * PARTS * ROWS * WIDTH, transcendentals=0
        ),
        name="out_grad",
    )(sc, mixed, res_own, res_far)


def out_kernel(sc, active, resid, w_down, own, far):
    branch = dot(active[...].reshape(4 * SPAN, FF), w_down[...], 1, 0)
    valid = row_valid(pl.program_id(0), sc, pl.program_id(1))
    output = jnp.where(valid, resid[...].reshape(4 * SPAN, WIDTH).astype(F32) + branch, 0.0)
    output = output.astype(BF16).reshape(1, 4, SPAN, WIDTH)
    own[...] = output[:, :2]
    far[...] = output[:, 2:]


def run_out(sc, active, resid, w_down):
    block = lambda items, lanes: spec((1, items, SPAN, lanes), lambda p, r, s: (p, 0, r, 0))
    return pl.pallas_call(
        out_kernel,
        grid_spec=pltpu.PrefetchScalarGridSpec(
            num_scalar_prefetch=1,
            grid=(PARTS, HROWS // SPAN),
            in_specs=[block(4, FF), block(4, WIDTH), held((FF, WIDTH))],
            out_specs=[block(2, WIDTH)] * 2,
        ),
        out_shape=[jax.ShapeDtypeStruct((PARTS, 2, HROWS, WIDTH), BF16)] * 2,
        compiler_params=params(VMEM),
        cost_estimate=pl.CostEstimate(
            flops=2 * PARTS * ROWS * WIDTH * FF, bytes_accessed=PARTS * ROWS * (2 * FF + 7 * WIDTH), transcendentals=0
        ),
        name="out",
    )(sc, active.reshape(PARTS, 4, HROWS, FF), resid, w_down)


def post_kernel(part, sc, resid, back, cot, weight, gain, *refs):
    (res_own, res_far, heads, d_gain, spread) = refs[-5:]
    step = pl.program_id(0)
    shape, slab = (4 * SPAN, WIDTH), (1, 4, SPAN, WIDTH)
    valid = row_valid(part, sc, step)
    res = resid[...].reshape(shape).astype(F32)
    scale = lax.rsqrt(jnp.mean(res * res, axis=-1, keepdims=True) + EPSILON)
    unit = res * scale
    two_grad = jnp.where(valid, back[...].reshape(shape).astype(F32), 0.0)
    gained = two_grad * gain[...]
    masked = cot[...].reshape(shape).astype(F32)
    grad = masked + scale * (gained - unit * jnp.mean(gained * unit, axis=-1, keepdims=True))
    low = grad.astype(BF16)
    res_own[...] = low.reshape(slab)[:, :2]
    res_far[...] = low.reshape(slab)[:, 2:]
    gain_sum = jnp.sum(two_grad * unit, axis=0, keepdims=True)

    @pl.when(step == 0)
    def _():
        d_gain[...] = gain_sum

    @pl.when(step > 0)
    def _():
        d_gain[...] += gain_sum

    spread[...] = dot(low, weight[...], 1, 1).astype(BF16).reshape(4, SPAN, WIDTH)
    for pair in range(HEADS // 2):
        lanes = slice(pair * 128, (pair + 1) * 128)
        for side in range(2):
            one, two = spread[2 * side, :, lanes], spread[2 * side + 1, :, lanes]
            half = slice(side * 128, (side + 1) * 128)
            heads[2 * pair, :, half] = jnp.concatenate([one[:, :HEAD], two[:, :HEAD]], axis=1)
            heads[2 * pair + 1, :, half] = jnp.concatenate([one[:, HEAD:], two[:, HEAD:]], axis=1)


def run_post(part, sc, resid, back, cotangent, weight, gain, carry):
    return pl.pallas_call(
        partial(post_kernel, part),
        grid_spec=pltpu.PrefetchScalarGridSpec(
            num_scalar_prefetch=1,
            grid=(HROWS // SPAN,),
            in_specs=[slab_spec(part), slab_spec(0), slab_spec(part), held((WIDTH, WIDTH)), held((1, WIDTH))]
            + anywhere(len(carry)),
            out_specs=[slab_spec(part, 2)] * 2 + [heads_spec(), held((1, WIDTH))],
            scratch_shapes=[pltpu.VMEM((4, SPAN, WIDTH), BF16)],
        ),
        out_shape=[
            jax.ShapeDtypeStruct((PARTS, 2, HROWS, WIDTH), BF16),
            jax.ShapeDtypeStruct((PARTS, 2, HROWS, WIDTH), BF16),
            jax.ShapeDtypeStruct((HEADS, HROWS, 4 * HEAD), BF16),
            jax.ShapeDtypeStruct((1, WIDTH), F32),
        ],
        input_output_aliases={6 + i: i for i in range(len(carry))},
        compiler_params=params(VMEM),
        cost_estimate=pl.CostEstimate(
            flops=2 * ROWS * WIDTH * WIDTH, bytes_accessed=12 * ROWS * WIDTH, transcendentals=0
        ),
        name="post",
    )(sc, resid, back.reshape(1, 4, HROWS, WIDTH), cotangent, weight, gain, *carry)


def unmix_kernel(part, carried, added, sc, *refs):
    shards, (v_own, v_far, grad_heads, mean, *rest) = refs[:8], refs[8:]
    rest = rest[2:] if carried else rest
    if added:
        own_in, far_in, *rest = rest
    outs, (own, far, raw, grads, mask, adder, bound, sems, out_sems) = rest[:8], rest[8:]
    place = sc[PLACE]
    step = pl.program_id(0)

    def leave(slot):
        return [
            pltpu.make_async_copy(
                grads.at[slot, pl.ds(pl.multiple_of((place ^ rel) * SUBS * HALF, SUBS * HALF), SUBS * HALF)],
                outs[4 * slot + rel],
                out_sems.at[slot, rel],
            )
            for rel in range(4)
        ]

    fill_mask(sc, mask)

    @pl.when(step == 0)
    def _():
        lane = lax.broadcasted_iota(jnp.int32, (4 * HEAD, 128), 0) // HEAD
        column = lax.broadcasted_iota(jnp.int32, (4 * HEAD, 128), 1)
        adder[...] = jnp.where((lane == column) | (lane + 4 == column), -1.0, 0.0).astype(BF16)
        row = lax.broadcasted_iota(jnp.int32, (LMAX, 128), 0)
        item = lax.broadcasted_iota(jnp.int32, (LMAX, 128), 1)
        length = jnp.where(item % 4 == 0, sc[LENGTHS], sc[LENGTHS + 1])
        length = jnp.where(item % 4 == 2, sc[LENGTHS + 2], length)
        length = jnp.where(item % 4 == 3, sc[LENGTHS + 3], length)
        bound[...] = jnp.where((item < 8) & (row < length), 1.0, 0.0).astype(BF16)

    slot = take_plane(place, shards, raw, sems)
    high_lanes = lax.broadcasted_iota(jnp.int32, (HROWS, 128), 1) < 4
    for head in range(PHEADS):
        weights = jnp.exp(raw[slot, head_rows(head)].astype(F32)).astype(BF16)
        low = (grad_heads[head].astype(F32) * inverse_sums(part, sc, weights, mask)).astype(BF16)
        product = low.astype(F32) * mean[head]
        coarse = product.astype(BF16)
        fine = (product - coarse.astype(F32)).astype(BF16)
        delta = dot(coarse, adder[...], 1, 0) + dot(fine, adder[...], 1, 0)
        coarse = delta.astype(BF16)
        fine = (delta - coarse.astype(F32)).astype(BF16)
        left = jnp.concatenate([low, jnp.where(high_lanes, coarse, fine)], axis=1)
        score = dot(left, jnp.concatenate([v_own[head], v_far[head], bound[...]], axis=1), 1, 1)
        grads[slot, head_rows(head)] = (score * weights.astype(F32)).astype(BF16)
        back = dot(weights, low, 0, 0) * mask[...].astype(F32)
        for target, lanes in ((own, slice(0, 2 * HEAD)), (far, slice(2 * HEAD, 4 * HEAD))):
            found = back[:, lanes]
            if added:
                found = found + (own_in if target is own else far_in)[head].astype(F32)
            target[head] = found.astype(BF16)
    for which in range(2):

        @pl.when(step == which)
        def _():
            for copy in leave(which):
                copy.start()
            if which == 1:
                for copy in leave(0) + leave(1):
                    copy.wait()


def run_unmix(part, sc, planes, shards, v_own, v_far, grad_heads, mean, carry, add):
    carry, add = list(carry), list(add)
    return pl.pallas_call(
        partial(unmix_kernel, part, bool(carry), bool(add)),
        grid_spec=pltpu.PrefetchScalarGridSpec(
            num_scalar_prefetch=1,
            grid=(2,),
            in_specs=anywhere(8)
            + [plane_spec(planes, LMAX, 2 * HEAD)] * 2
            + [plane_spec(planes, HROWS, 4 * HEAD)] * 2
            + anywhere(len(carry))
            + [plane_spec(planes, LMAX, 2 * HEAD)] * len(add),
            out_specs=anywhere(8) + [plane_spec(planes, LMAX, 2 * HEAD)] * 2,
            scratch_shapes=[
                pltpu.VMEM((2, 4 * SUBS * HALF, LMAX), BF16),
                pltpu.VMEM((2, 4 * SUBS * HALF, LMAX), BF16),
                pltpu.VMEM((LMAX, 4 * HEAD), BF16),
                pltpu.VMEM((4 * HEAD, 128), BF16),
                pltpu.VMEM((LMAX, 128), BF16),
                pltpu.SemaphoreType.DMA((2, 4)),
                pltpu.SemaphoreType.DMA((2, 4)),
            ],
        ),
        out_shape=[jax.ShapeDtypeStruct((SUBS * HALF, LMAX), BF16)] * 8
        + [jax.ShapeDtypeStruct((HEADS, LMAX, 2 * HEAD), BF16)] * 2,
        input_output_aliases={13 + i: 8 + i for i in range(len(carry))},
        compiler_params=params(VMEM),
        cost_estimate=pl.CostEstimate(
            flops=3 * HEADS * HROWS * LMAX * 4 * HEAD,
            bytes_accessed=HEADS * (2 * HROWS * LMAX + 4 * HROWS * 256 + 4 * LMAX * 256),
            transcendentals=HEADS * HROWS * LMAX // 2,
        ),
        name="unmix",
    )(sc, *shards, v_own, v_far, grad_heads, mean, *carry, *add)


def close_kernel(sc, tok, res_own, res_got, out_own, out_got, own, far, gain, weight, *refs):
    (output, tok_grad, d_value, d_gain, total) = refs
    step = pl.program_id(0)
    core = sc[CORE]
    for part in range(PARTS):
        output[:, part, core] = out_own[part, :, 0].astype(F32)
        output[:, part, 1 - core] = out_got[part, :, 0].astype(F32)
        tok_grad[:, part, core] = res_own[part, :, 0].astype(F32)
        tok_grad[:, part, 1 - core] = res_got[part, :, 0].astype(F32)
    runs = tok.shape[1]
    rows = runs * 128
    for item in range(2):
        lanes = slice(item * HEAD, (item + 1) * HEAD)
        pieces = [
            add_low(own[head, :, lanes], far[head, :, lanes]) for head in range(HEADS)
        ]
        back = jnp.concatenate(pieces, axis=1)
        x = tok[item].reshape(rows, WIDTH).astype(F32)
        scale = lax.rsqrt(jnp.mean(x * x, axis=-1, keepdims=True) + EPSILON)
        unit = x * scale
        normed = (unit * gain[...]).astype(BF16)
        normed_grad = dot(back, weight[...], 1, 1)
        gained = normed_grad * gain[...]
        update = scale * (gained - unit * jnp.mean(gained * unit, axis=-1, keepdims=True))
        tok_grad[item] += update.reshape(runs, 2, HALF, WIDTH)
        gain_sum = jnp.sum(normed_grad * unit, axis=0, keepdims=True)
        value_sum = dot(normed, back, 0, 0)
        if item == 0:
            gain_total, value_total = gain_sum, value_sum
        else:
            gain_total, value_total = gain_total + gain_sum, value_total + value_sum

    @pl.when(step == 0)
    def _():
        d_gain[...] = gain_total
        total[...] = value_total

    @pl.when(step > 0)
    def _():
        d_gain[...] += gain_total
        total[...] += value_total

    @pl.when(step == pl.num_programs(0) - 1)
    def _():
        low = total[...].astype(BF16)
        d_value[0] = low[:, :SIDE]
        d_value[1] = low[:, SIDE:]


def run_close(sc, tokens, res_own, res_got, out_own, out_got, own, far, gain, weight):
    runs = PARTS
    slab = (2, PARTS * RUNS, 2, HALF, WIDTH)
    half = (PARTS, 2, RUNS, HALF, WIDTH)
    whole_spec = spec((2, runs, 2, HALF, WIDTH), lambda j, s: (0, j, 0, 0, 0))
    half_spec = spec((PARTS, 2, 1, HALF, WIDTH), lambda j, s: (0, 0, j, 0, 0))
    back_spec = spec((HEADS, runs * 128, 2 * HEAD), lambda j, s: (0, j, 0))
    return pl.pallas_call(
        close_kernel,
        grid_spec=pltpu.PrefetchScalarGridSpec(
            num_scalar_prefetch=1,
            grid=(RUNS,),
            in_specs=[whole_spec]
            + [half_spec] * 4
            + [back_spec, back_spec, held((1, WIDTH)), held((WIDTH, WIDTH))],
            out_specs=[whole_spec, whole_spec, held((2, WIDTH, SIDE)), held((1, WIDTH))],
            scratch_shapes=[pltpu.VMEM((WIDTH, WIDTH), F32)],
        ),
        out_shape=[
            jax.ShapeDtypeStruct(slab, F32),
            jax.ShapeDtypeStruct(slab, F32),
            jax.ShapeDtypeStruct((2, WIDTH, SIDE), BF16),
            jax.ShapeDtypeStruct((1, WIDTH), F32),
        ],
        compiler_params=params(VMEM),
        cost_estimate=pl.CostEstimate(
            flops=4 * 2 * LMAX * WIDTH * WIDTH, bytes_accessed=38 * LMAX * WIDTH, transcendentals=0
        ),
        name="close",
    )(
        sc,
        tokens.reshape(slab),
        *(x.reshape(half) for x in (res_own, res_got, out_own, out_got)),
        own,
        far,
        gain,
        weight,
    )


def place_kernel(sc, *refs):
    pieces, target, sems = refs[:16], refs[16], refs[17]
    copies = [
        pltpu.make_async_copy(piece, target.at[plane_of(i // 4, sc) * 4 + (sc[PLACE] ^ (i % 4))], sems.at[i])
        for i, piece in enumerate(pieces)
    ]
    for copy in copies:
        copy.start()
    for copy in copies:
        copy.wait()


def run_place(sc, pieces):
    shape = (16, *pieces[0].shape)
    return pl.pallas_call(
        place_kernel,
        grid_spec=pltpu.PrefetchScalarGridSpec(
            num_scalar_prefetch=1,
            grid=(1,),
            in_specs=anywhere(16),
            out_specs=held(shape),
            scratch_shapes=[pltpu.SemaphoreType.DMA((16,))],
        ),
        out_shape=jax.ShapeDtypeStruct(shape, BF16),
        compiler_params=params(VMEM),
        name="place",
    )(sc, *pieces)


PACK_DOWN, PACK_UP, PACK_OUT, PACK = 0, 192, 384, 432


def chip_of(sc, k, rel):
    return plane_of(k, sc) * 4 + (sc[PLACE] ^ rel)


def collect_kernel(sc, *refs):
    outs = refs[24:]
    for k in range(PLANES):

        @pl.when(pl.program_id(0) == k)
        def _():
            for rel in range(4):
                down, down_got, up, up_got, out, out_got = refs[6 * rel : 6 * rel + 6]
                packed = outs[4 * k + rel]
                packed[PACK_DOWN:PACK_UP] = add_low(down[...], down_got[...])
                for j in range(4):
                    lanes = slice(j * SIDE, (j + 1) * SIDE)
                    packed[PACK_UP + 48 * j : PACK_UP + 48 * (j + 1)] = add_low(up[:, lanes], up_got[:, lanes])
                packed[PACK_OUT:PACK] = add_low(out[...], out_got[...])


def run_collect(sc, *sides):
    def rows(x, rel):
        return spec((x.shape[0] // 16, x.shape[1]), lambda k, s: (chip_of(s, k, rel), 0))

    return pl.pallas_call(
        collect_kernel,
        grid_spec=pltpu.PrefetchScalarGridSpec(
            num_scalar_prefetch=1,
            grid=(PLANES,),
            in_specs=[rows(x, rel) for rel in range(4) for x in sides],
            out_specs=[held((PACK, SIDE))] * 16,
        ),
        out_shape=[jax.ShapeDtypeStruct((PACK, SIDE), BF16)] * 16,
        compiler_params=params(VMEM),
        cost_estimate=pl.CostEstimate(flops=0, bytes_accessed=3 * 16 * PACK * SIDE * 2, transcendentals=0),
        name="collect",
    )(sc, *(x for _ in range(4) for x in sides))


def add_kernel(groups, *refs):
    for group, total in zip(groups, refs[-len(groups) :]):
        value = refs[group[0]][...].astype(F32)
        for index in group[1:]:
            value = value + refs[index][...].astype(F32)
        total[...] = value.astype(total.dtype)


def run_add(groups, values, dtype):
    rows, columns = values[0].shape
    block = pl.BlockSpec((rows, columns), lambda i: (i, 0))
    return pl.pallas_call(
        partial(add_kernel, groups),
        grid=(1,),
        in_specs=[block] * len(values),
        out_specs=[block] * len(groups),
        out_shape=[jax.ShapeDtypeStruct((rows, columns), dtype)] * len(groups),
        compiler_params=params(VMEM),
        cost_estimate=pl.CostEstimate(
            flops=0, bytes_accessed=2 * rows * columns * (len(values) + len(groups)), transcendentals=0
        ),
        name="add",
    )(*values)


DEVICES = 32
TO_CORE, TO_X, TO_Y = 1, 2, 4


def swap(x, bit):
    return lax.ppermute(x, BOTH, [(d, d ^ bit) for d in range(DEVICES)])


def ring(x, way=1):
    return lax.ppermute(x, BOTH, [(d, (d + 8 * way) % DEVICES) for d in range(DEVICES)])


def pick(x, index, axis=0):
    return lax.dynamic_index_in_dim(x, index, axis, keepdims=False)


def ordered(flag, one, two, axis=0, joined=jnp.stack):
    return jnp.where(flag == 0, joined([one, two], axis), joined([two, one], axis))


def add_low(one, two):
    return (one.astype(F32) + two.astype(F32)).astype(BF16)


STEPS = (
    ((0, 0, 1), (0, 1, 0), (1, 0, 0)),
    ((1, 0, 1), (0, 1, 1), (2, 0, 0)),
    ((2, 0, 1), (1, 1, 0), (3, 0, 0)),
    ((3, 0, 1), (2, 1, 0), (1, 1, 1)),
    ((2, 1, 1), (3, 1, 1), (3, 1, 0)),
)


def gather_step(have, step):
    by_x, by_y, by_z = STEPS[step]
    return {
        **have,
        by_z: ring(have[by_z[0] - 1, by_z[1], by_z[2]]),
        by_x: swap(have[by_x[0], by_x[1], 0], TO_X),
        by_y: swap(have[by_y[0], 0, by_y[2]], TO_Y),
    }


def in_order(have):
    return [have[k, y, x] for k in range(4) for y in range(2) for x in range(2)]


def by_place(shares, planes=range(PLANES)):
    return {(k, i // 2, i % 2): shares[4 * at + i] for at, k in enumerate(planes) for i in range(4)}


def scatter_send(have, step):
    by_x, by_y, by_z = STEPS[len(STEPS) - 1 - step]
    got = (ring(have[by_z], -1), swap(have[by_x], TO_X), swap(have[by_y], TO_Y))
    return {at: value for at, value in have.items() if at not in (by_x, by_y, by_z)}, got


def scatter_add(have, got, step):
    by_x, by_y, by_z = STEPS[len(STEPS) - 1 - step]
    targets = ((by_z[0] - 1, by_z[1], by_z[2]), (by_x[0], by_x[1], 0), (by_y[0], 0, by_y[2]))
    sums = list(dict.fromkeys(targets))
    groups = [(len(got) + i, *(j for j in range(len(got)) if targets[j] == at)) for i, at in enumerate(sums)]
    values = [*got, *(have[at] for at in sums)]
    return {**have, **dict(zip(sums, run_add(groups, values, F32 if step == len(STEPS) - 1 else BF16)))}


together = lax.optimization_barrier


def chip_shards(tokens, lengths, rand_mix, w_value, w_out, w_up, w_down, gain_mix, gain_ffn, grad_out):
    wide = lax.axis_index("wide")
    core = lax.axis_index("narrow")
    z, y, x = wide // 4, (wide // 2) % 2, wide % 2
    other = lambda value: swap(value, TO_CORE)
    side = partial(ordered, core, joined=jnp.concatenate)
    slab = (2, PARTS * RUNS, 2, HALF, WIDTH)
    tokens, grad_out = tokens.reshape(slab), grad_out.reshape(slab)

    packed = jnp.concatenate([w_out, w_down, *(w_up[:, j * WIDTH : (j + 1) * WIDTH] for j in range(4))])
    packed = lax.all_gather(packed, BOTH, axis=0)

    gains = jnp.pad(jnp.concatenate([gain_mix, gain_ffn])[None], ((0, 7), (0, WIDTH - 48)))
    firsts = {(0, 0, 0): jnp.concatenate([w_value, gains])}
    rand = rand_mix.reshape(3, 2, HALF, LMAX)
    blocks = side(pick(rand, core, 1), other(pick(rand, 1 - core, 1)), 0)
    starts = [{(0, 0, 0): blocks[part::PARTS].reshape(SUBS * HALF, LMAX)} for part in range(PARTS)]
    firsts, starts, far_lengths = together((gather_step(firsts, 0), starts, other(lengths)))
    sc = jnp.concatenate([jnp.stack([core, z, wide % 4]).astype(jnp.int32), lengths, far_lengths])
    for step in range(1, 5):
        firsts = together(gather_step(firsts, step))
    firsts, rands = together((firsts, starts[0]))

    rands = gather_step(rands, 0)
    first = run_place(sc, in_order(firsts))
    rands, first, first_far = together((rands, first, other(first)))
    both = ordered(core, first, first_far, 1)
    value = both[:, :, :24].reshape(WIDTH, WIDTH)
    gain_one = both[:, :, 24, :24].reshape(1, WIDTH).astype(F32)
    gain_two = both[:, :, 24, 24:48].reshape(1, WIDTH).astype(F32)
    rands = gather_step(rands, 1)
    v_own = run_values(sc, tokens.reshape(2, LMAX, WIDTH), gain_one, value)
    rands, v_own = together((rands, v_own))
    rands, v_own, v_far = together((gather_step(rands, 2), v_own, other(v_own)))
    rands, v_far, tokens_far = together((gather_step(rands, 3), v_far, other(pick(tokens, 1 - core, 2))))
    rands, grad_far = together((gather_step(rands, 4), other(pick(grad_out, 1 - core, 2))))

    shares = [in_order(rands), None]
    half_one, half_two = (0, 1), (2, 3)
    rands = gather_step(starts[1], 0)
    mixing = run_mix(0, sc, half_one, shares[0][:8], v_own, v_far, ())
    heads, mean_zero = run_mix(0, sc, half_two, shares[0][8:], v_own, v_far, mixing)
    rands, heads, mean_zero = together((rands, heads, mean_zero))

    out = packed[:, :24].reshape(WIDTH, WIDTH)
    down = packed[:, 24:120].reshape(FF, WIDTH)
    up = packed[:, 120:].reshape(32, 4, 24, WIDTH).transpose(1, 0, 2, 3).reshape(4, WIDTH, WIDTH)
    rands = gather_step(rands, 1)
    slabs = run_pre(0, sc, tokens, tokens_far, grad_out, grad_far, heads, out, gain_two, ())
    rands, slabs, down, up = together((rands, slabs, down, up))

    rands = gather_step(rands, 2)
    mixed, resid, normed, masked = slabs
    *acts, back = run_units(0, sc, normed, masked, up, down, ())
    rands, acts, back = together((rands, acts, back))

    rands = gather_step(rands, 3)
    *res, grad_heads, gain_sum = run_post(0, sc, resid, back, masked, out, gain_two, ())
    rands, res, grad_heads, gain_sum = together((rands, res, grad_heads, gain_sum))

    rands = gather_step(rands, 4)
    backward = lambda part, planes, share, grad, mean, carry, add: run_unmix(
        part, sc, planes, share, v_own, v_far, grad, mean, carry, add
    )
    far_planes, near_planes = (3, 2), (1, 0)
    *far, own_sum, far_sum = backward(
        0, far_planes, shares[0][12:] + shares[0][8:12], grad_heads, mean_zero, (), ()
    )
    *near, own_sum, far_sum = backward(
        0, near_planes, shares[0][4:8] + shares[0][:4], grad_heads, mean_zero, (own_sum, far_sum), ()
    )
    rands, far, near, own_sum, far_sum = together((rands, far, near, own_sum, far_sum))
    shares[1] = in_order(rands)

    have, got = scatter_send(by_place(near[4:] + near[:4] + far[4:] + far[:4]), 0)
    mixing = run_mix(1, sc, half_one, shares[1][:8], v_own, v_far, ())
    heads, mean_one = run_mix(1, sc, half_two, shares[1][8:], v_own, v_far, mixing)
    have, got, heads, mean_one = together((have, got, heads, mean_one))
    have = scatter_add(have, got, 0)

    have, got = scatter_send(have, 1)
    slabs = run_pre(1, sc, tokens, tokens_far, grad_out, grad_far, heads, out, gain_two, slabs)
    have, got, slabs = together((have, got, slabs))
    have = scatter_add(have, got, 1)

    have, got = scatter_send(have, 2)
    mixed, resid, normed, masked = slabs
    *acts, back = run_units(1, sc, normed, masked, up, down, acts)
    have, got, acts, back = together((have, got, acts, back))
    have = scatter_add(have, got, 2)

    have, got = scatter_send(have, 3)
    *res, grad_heads, d_gain_two = run_post(1, sc, resid, back, masked, out, gain_two, res)
    d_gain_two = d_gain_two + gain_sum
    have, got, res, grad_heads, d_gain_two = together((have, got, res, grad_heads, d_gain_two))
    have = scatter_add(have, got, 3)
    active, up_grad = acts
    res_own, res_far = res

    have, got = scatter_send(have, 4)
    sums_zero = (own_sum, far_sum)
    *far, own_sum, far_sum = backward(
        1, far_planes, shares[1][12:] + shares[1][8:12], grad_heads, mean_one, (), sums_zero
    )
    have, got, far, own_sum, far_sum, res_got = together((have, got, far, own_sum, far_sum, other(res_far)))
    rand_sums = [scatter_add(have, got, 4)[0, 0, 0]]

    have, got = scatter_send(by_place(far, far_planes), 0)
    *near, back_own, back_far = backward(
        1, near_planes, shares[1][4:8] + shares[1][:4], grad_heads, mean_one, (own_sum, far_sum), sums_zero
    )
    have, got, near, back_own, back_far = together((have, got, near, back_own, back_far))
    have = {**scatter_add(have, got, 0), **by_place(near, near_planes)}

    have, got = scatter_send(have, 1)
    up_own, up_far = run_up_grad(sc, normed, up_grad)
    have, got, up_own, up_far, back_got = together((have, got, up_own, up_far, other(back_far)))
    have = scatter_add(have, got, 1)

    have, got = scatter_send(have, 2)
    down_own, down_far = run_down_grad(sc, active, masked)
    have, got, down_own, down_far, up_got = together((have, got, down_own, down_far, other(up_far)))
    have = scatter_add(have, got, 2)

    have, got = scatter_send(have, 3)
    d_out_own, d_out_far = run_out_grad(sc, mixed, res_own, res_far)
    have, got, d_out_own, d_out_got, down_got = together((have, got, d_out_own, other(d_out_far), other(down_far)))
    have = scatter_add(have, got, 3)

    have, got = scatter_send(have, 4)
    grads = run_collect(sc, down_own, down_got, up_own, up_got, d_out_own, d_out_got)
    have, got, grads = together((have, got, grads))
    rand_sums.append(scatter_add(have, got, 4)[0, 0, 0])

    sums, got = scatter_send(by_place(grads), 0)
    out_own, out_far = run_out(sc, active, resid, down)
    rand_sum = jnp.stack([x.reshape(SUBS, HALF, LMAX) for x in rand_sums], 1).reshape(2, 3, HALF, LMAX)
    blocks, blocks_far = pick(rand_sum, core), other(pick(rand_sum, 1 - core))
    sums, got, out_own, out_far, blocks, blocks_far = together((sums, got, out_own, out_far, blocks, blocks_far))
    sums = scatter_add(sums, got, 0)

    sums, got = scatter_send(sums, 1)
    output, tokens_grad, d_value, d_gain_one = run_close(
        sc, tokens, res_own, res_got, out_own, other(out_far), back_own, back_got, gain_one, value
    )
    gain_pair = jnp.concatenate([d_gain_one, d_gain_two]).reshape(2, 16, 1, 48).astype(BF16)
    gain_pair = jnp.pad(gain_pair, ((0, 0), (0, 0), (0, 15), (0, SIDE - 48)))
    small = jnp.concatenate([d_value.reshape(2, 16, 48, SIDE), gain_pair], 2)
    sums, got, small, output, tokens_grad = together((sums, got, small, output, tokens_grad))
    sums = scatter_add(sums, got, 1)

    sums, got = scatter_send(sums, 2)
    small = add_low(pick(small, core), other(pick(small, 1 - core))).reshape(4, 2, 2, 64, SIDE)
    small = add_low(pick(small, x, 2), swap(pick(small, 1 - x, 2), TO_X))
    sums, got, small = together((sums, got, small))
    sums = scatter_add(sums, got, 2)

    sums, got = scatter_send(sums, 3)
    small = add_low(pick(small, y, 1), swap(pick(small, 1 - y, 1), TO_Y))
    sums, got, small = together((sums, got, small))
    sums = scatter_add(sums, got, 3)

    sums, got = scatter_send(sums, 4)
    small_sum = pick(small, z).astype(F32)
    for k in range(1, PLANES):
        small_sum = small_sum + ring(pick(small, lax.rem(z + PLANES - k, PLANES)), -k).astype(F32)
    sums, got, small_sum = together((sums, got, small_sum))
    big_sum = scatter_add(sums, got, 4)[0, 0, 0]
    big_far, small_far = other(big_sum), other(small_sum)

    rows_of = lambda value, rows: pick(value.reshape(-1, 2, rows, SIDE), core, 1)
    mine = lambda own, far, rows: side(rows_of(own, rows)[0], rows_of(far, rows)[0], 1)
    down_shard = mine(big_sum[PACK_DOWN:PACK_UP], big_far[PACK_DOWN:PACK_UP], 96)
    up_side = lambda value: rows_of(value[PACK_UP:PACK_OUT], 24).transpose(1, 0, 2).reshape(24, 4 * SIDE)
    up_shard = side(up_side(big_sum), up_side(big_far), 1)
    outproj_shard = mine(big_sum[PACK_OUT:], big_far[PACK_OUT:], 24)
    value_shard = mine(small_sum[:48], small_far[:48], 24)
    gains_pair = ordered(core, small_sum[48, :48], small_far[48, :48])
    gain_pair = pick(gains_pair.reshape(2, 2, 24), core, 1)

    rand_shard = ordered(core, blocks, blocks_far, 1)

    return (
        output.reshape(2, LMAX, WIDTH),
        tokens_grad.reshape(2, LMAX, WIDTH),
        rand_shard.reshape(3 * 128, LMAX),
        value_shard,
        outproj_shard,
        up_shard,
        down_shard,
        gain_pair[0],
        gain_pair[1],
    )


def rms_norm(values, gain):
    scale = lax.rsqrt(jnp.mean(values * values, axis=-1, keepdims=True) + EPSILON)
    return values * scale * gain


def split_heads(block):
    return block.reshape(LMAX, HEADS, HEAD).transpose(1, 0, 2)


def merge_heads(block):
    return block.transpose(1, 0, 2).reshape(LMAX, HEADS * HEAD)


def masked_scores(key_mask, rand_head):
    return jnp.where(key_mask[None, :] > 0, rand_head.astype(jnp.float32), -1e30)


def head_forward(key_mask, paired):
    rand_head, value_head = paired
    scores = masked_scores(key_mask, rand_head)
    row_peak = jnp.max(scores, axis=-1, keepdims=True)
    exponent = jnp.exp(scores - row_peak)
    denom_sum = jnp.sum(exponent, axis=-1, keepdims=True)
    attention = exponent / denom_sum * key_mask[:, None]
    mixed = jnp.dot(attention.astype(jnp.bfloat16), value_head, preferred_element_type=jnp.float32)
    return (mixed.astype(jnp.bfloat16), row_peak + jnp.log(denom_sum))


def head_backward(key_mask, paired):
    rand_head, value_head, mix_grad, log_total = paired
    scores = masked_scores(key_mask, rand_head)
    attention = jnp.exp(scores - log_total) * key_mask[:, None]
    prob_grad = jnp.einsum("id,jd->ij", mix_grad, value_head, preferred_element_type=jnp.float32)
    value_grad = jnp.einsum(
        "ij,id->jd", attention.astype(jnp.bfloat16), mix_grad, preferred_element_type=jnp.float32
    )
    score_grad = attention * (prob_grad - jnp.sum(prob_grad * attention, axis=-1, keepdims=True))
    return (score_grad, value_grad)


def shards(tokens, lengths, rand_mix, w_value, w_out, w_up, w_down, gain_mix, gain_ffn, grad_out):
    item_count = tokens.shape[0]
    width = tokens.shape[2]
    row_count = item_count * LMAX
    tokens_flat = tokens.reshape(row_count, width).astype(jnp.float32)
    positions = jnp.arange(LMAX, dtype=jnp.int32)
    valid_table = (positions[None, :] < lengths[:, None]).astype(jnp.float32)
    row_valid = valid_table.reshape(row_count, 1)
    forward_set = (
        lax.all_gather(rand_mix, ("wide", "narrow"), axis=0, tiled=True),
        lax.all_gather(w_value, ("wide", "narrow"), axis=0, tiled=True),
        lax.all_gather(w_out, ("wide", "narrow"), axis=0, tiled=True),
        lax.all_gather(w_up, ("wide", "narrow"), axis=0, tiled=True),
        lax.all_gather(w_down, ("wide", "narrow"), axis=0, tiled=True),
        lax.all_gather(gain_mix, ("wide", "narrow"), axis=0, tiled=True),
        lax.all_gather(gain_ffn, ("wide", "narrow"), axis=0, tiled=True),
    )
    rand_all, value_all, out_all, up_all, down_all, gain_first, gain_second = forward_set
    normed = rms_norm(tokens_flat, gain_first.astype(jnp.float32)).astype(jnp.bfloat16)
    values = jnp.dot(normed, value_all, preferred_element_type=jnp.float32).astype(jnp.bfloat16)
    rand_heads = rand_all.reshape(HEADS, LMAX, LMAX)
    mixed_parts = []
    totals_kept = []
    for item_index in range(item_count):
        item_values = split_heads(values[item_index * LMAX : (item_index + 1) * LMAX])
        mixed_heads, log_total = lax.map(
            partial(head_forward, valid_table[item_index]), (rand_heads, item_values)
        )
        mixed_parts.append(merge_heads(mixed_heads))
        totals_kept.append(log_total)
    mixed = jnp.concatenate(mixed_parts, axis=0)
    residual = tokens_flat + jnp.dot(mixed, out_all, preferred_element_type=jnp.float32)
    normed_two = rms_norm(residual, gain_second.astype(jnp.float32)).astype(jnp.bfloat16)
    up_proj = jnp.dot(normed_two, up_all, preferred_element_type=jnp.float32)
    active = jax.nn.gelu(up_proj).astype(jnp.bfloat16)
    branch = jnp.dot(active, down_all, preferred_element_type=jnp.float32)
    output = row_valid * (residual + branch)
    back_set = (
        lax.all_gather(rand_mix, ("wide", "narrow"), axis=0, tiled=True),
        lax.all_gather(w_value, ("wide", "narrow"), axis=0, tiled=True),
        lax.all_gather(w_out, ("wide", "narrow"), axis=0, tiled=True),
        lax.all_gather(w_up, ("wide", "narrow"), axis=0, tiled=True),
        lax.all_gather(w_down, ("wide", "narrow"), axis=0, tiled=True),
        lax.all_gather(gain_mix, ("wide", "narrow"), axis=0, tiled=True),
        lax.all_gather(gain_ffn, ("wide", "narrow"), axis=0, tiled=True),
    )
    rand_back, value_back, out_back, up_back, down_back, gain_back_one, gain_back_two = back_set
    cotangent = grad_out.reshape(row_count, width).astype(jnp.float32)
    masked = row_valid * cotangent
    branch_grad = masked.astype(jnp.bfloat16)
    grad_down = jnp.einsum("rk,rd->kd", active, branch_grad, preferred_element_type=jnp.float32)
    active_grad = jnp.einsum(
        "rd,kd->rk", branch_grad, down_back, preferred_element_type=jnp.float32
    )
    gelu_value, gelu_pull = jax.vjp(jax.nn.gelu, up_proj)
    up_grad = gelu_pull(active_grad)[0].astype(jnp.bfloat16)
    grad_up = jnp.einsum("rd,rk->dk", normed_two, up_grad, preferred_element_type=jnp.float32)
    normed_two_grad = jnp.einsum("rk,dk->rd", up_grad, up_back, preferred_element_type=jnp.float32)
    norm_value, norm_pull = jax.vjp(rms_norm, residual, gain_back_two.astype(jnp.float32))
    residual_part, gain_two_grad = norm_pull(normed_two_grad)
    residual_grad = masked + residual_part
    attn_grad = residual_grad.astype(jnp.bfloat16)
    grad_outproj = jnp.einsum("rd,re->de", mixed, attn_grad, preferred_element_type=jnp.float32)
    mixed_grad = jnp.einsum(
        "re,de->rd", attn_grad, out_back, preferred_element_type=jnp.float32
    ).astype(jnp.bfloat16)
    rand_heads_back = rand_back.reshape(HEADS, LMAX, LMAX)
    rand_grad = jnp.zeros((HEADS, LMAX, LMAX), jnp.float32)
    value_parts = []
    for item_index in range(item_count):
        lower_row = item_index * LMAX
        upper_row = lower_row + LMAX
        item_values = split_heads(values[lower_row:upper_row])
        item_mix_grad = split_heads(mixed_grad[lower_row:upper_row])
        score_grad, value_grad = lax.map(
            partial(head_backward, valid_table[item_index]),
            (rand_heads_back, item_values, item_mix_grad, totals_kept[item_index]),
        )
        rand_grad = rand_grad + score_grad
        value_parts.append(merge_heads(value_grad))
    values_grad = jnp.concatenate(value_parts, axis=0).astype(jnp.bfloat16)
    grad_value = jnp.einsum("rd,re->de", normed, values_grad, preferred_element_type=jnp.float32)
    normed_grad = jnp.einsum(
        "re,de->rd", values_grad, value_back, preferred_element_type=jnp.float32
    )
    norm_first, first_pull = jax.vjp(rms_norm, tokens_flat, gain_back_one.astype(jnp.float32))
    token_part, gain_one_grad = first_pull(normed_grad)
    tokens_grad = residual_grad + token_part
    rand_flat = rand_grad.reshape(HEADS * LMAX, LMAX)
    all_shards = (
        lax.psum_scatter(rand_flat, ("wide", "narrow"), scatter_dimension=0, tiled=True),
        lax.psum_scatter(grad_value, ("wide", "narrow"), scatter_dimension=0, tiled=True),
        lax.psum_scatter(grad_outproj, ("wide", "narrow"), scatter_dimension=0, tiled=True),
        lax.psum_scatter(grad_up, ("wide", "narrow"), scatter_dimension=0, tiled=True),
        lax.psum_scatter(grad_down, ("wide", "narrow"), scatter_dimension=0, tiled=True),
        lax.psum_scatter(gain_one_grad, ("wide", "narrow"), scatter_dimension=0, tiled=True),
        lax.psum_scatter(gain_two_grad, ("wide", "narrow"), scatter_dimension=0, tiled=True),
    )
    rand_shard, value_shard, outproj_shard, up_shard, down_shard, gain_one_shard, gain_two_shard = (
        all_shards
    )
    return (
        output.reshape(item_count, LMAX, width),
        tokens_grad.reshape(item_count, LMAX, width),
        rand_shard,
        value_shard,
        outproj_shard,
        up_shard,
        down_shard,
        gain_one_shard,
        gain_two_shard,
    )


def solution(mesh):
    in_specs = (
        P(("wide", "narrow"), None, None),
        P(("wide", "narrow")),
        P(("wide", "narrow"), None),
        P(("wide", "narrow"), None),
        P(("wide", "narrow"), None),
        P(("wide", "narrow"), None),
        P(("wide", "narrow"), None),
        P(("wide", "narrow")),
        P(("wide", "narrow")),
        P(("wide", "narrow"), None, None),
    )
    out_specs = (
        P(("wide", "narrow"), None, None),
        P(("wide", "narrow"), None, None),
        P(("wide", "narrow"), None),
        P(("wide", "narrow"), None),
        P(("wide", "narrow"), None),
        P(("wide", "narrow"), None),
        P(("wide", "narrow"), None),
        P(("wide", "narrow")),
        P(("wide", "narrow")),
    )
    fits = dict(mesh.shape) == {"wide": 16, "narrow": 2}
    return jax.shard_map(chip_shards if fits else shards, mesh=mesh, in_specs=in_specs, out_specs=out_specs, check_vma=False)
```

```python
from functools import partial

import jax
import jax.numpy as jnp
from jax import lax
from jax.experimental import pallas as pl
from jax.experimental.pallas import tpu as pltpu
from jax.sharding import PartitionSpec as P

HEADS = 12
HEAD = 64
LMAX = 1024
WIDTH = 768
FF = 3072
EPSILON = 1e-05

BOTH = ("wide", "narrow")
BF16 = jnp.bfloat16
F32 = jnp.float32
VMEM = 61 << 20

SUBS = 6
RUNS = 8
HALF = 64
HROWS = RUNS * HALF
PLANES = 4
PHEADS = HEADS // PLANES
ROWS = 2 * LMAX
FSTEP = 768
FSIDE = FF // 2 // FSTEP
TILE = 512
SIDE = WIDTH // 2
SPAN = 2 * HALF


def dot(a, b, ca, cb):
    return lax.dot_general(a, b, (((ca,), (cb,)), ((), ())), preferred_element_type=F32)


CORE, PLANE, PLACE, LENGTHS = 0, 1, 2, 3


def spec(shape, index):
    return pl.BlockSpec(shape, index)


def held(shape):
    zeros = (0,) * len(shape)
    return pl.BlockSpec(shape, lambda *_: zeros, pipeline_mode=pl.Buffered(1))


def params(limit):
    return pltpu.CompilerParams(vmem_limit_bytes=limit)


def whole_weight(sc, step, own, far, weight):
    @pl.when(step == 0)
    def _():
        weight[:, pl.ds(pl.multiple_of(sc[CORE] * SIDE, 128), SIDE)] = own[...]
        weight[:, pl.ds(pl.multiple_of((1 - sc[CORE]) * SIDE, 128), SIDE)] = far[...]


def values_kernel(sc, tok, gain, w_own, w_far, out, weight):
    step = pl.program_id(0)
    whole_weight(sc, step, w_own, w_far, weight)
    rows = tok.shape[1]
    position = step * rows + lax.broadcasted_iota(jnp.int32, (rows, 1), 0)
    for item in range(2):
        x = tok[item].astype(F32)
        scale = lax.rsqrt(jnp.mean(x * x, axis=-1, keepdims=True) + EPSILON)
        normed = (x * scale * gain[...]).astype(BF16)
        found = dot(normed, weight[...], 1, 0)
        found = jnp.where(position < sc[LENGTHS + item], found, 0.0).astype(BF16)
        for head in range(HEADS):
            out[head, :, item * HEAD : (item + 1) * HEAD] = found[:, head * HEAD : (head + 1) * HEAD]


def run_values(sc, tokens, gain, w_own, w_far):
    rows = 256
    return pl.pallas_call(
        values_kernel,
        grid_spec=pltpu.PrefetchScalarGridSpec(
            num_scalar_prefetch=1,
            grid=(LMAX // rows,),
            in_specs=[
                spec((2, rows, WIDTH), lambda j, s: (0, j, 0)),
                held((1, WIDTH)),
                held((WIDTH, SIDE)),
                held((WIDTH, SIDE)),
            ],
            out_specs=spec((HEADS, rows, 2 * HEAD), lambda j, s: (0, j, 0)),
            scratch_shapes=[pltpu.VMEM((WIDTH, WIDTH), BF16)],
        ),
        out_shape=jax.ShapeDtypeStruct((HEADS, LMAX, 2 * HEAD), BF16),
        compiler_params=params(VMEM),
        cost_estimate=pl.CostEstimate(
            flops=2 * 2 * LMAX * WIDTH * WIDTH, bytes_accessed=8 * LMAX * WIDTH, transcendentals=0
        ),
        name="values",
    )(sc, tokens, gain, w_own, w_far)


def lane_lengths(sc, shape):
    slot = lax.broadcasted_iota(jnp.int32, shape, 1) // HEAD
    length = jnp.where(slot == 0, sc[LENGTHS], sc[LENGTHS + 1])
    return jnp.where(slot >= 2, jnp.where(slot == 2, sc[LENGTHS + 2], sc[LENGTHS + 3]), length)


def plane_of(k, sc):
    return lax.rem(sc[PLANE] + PLANES - k, PLANES)


def plane_spec(planes, rows, lanes):
    def index(step, sc):
        return (plane_of(planes[0] + step * (planes[1] - planes[0]), sc), 0, 0)

    return spec((PHEADS, rows, lanes), index)


def anywhere(count):
    return [pl.BlockSpec(memory_space=pl.ANY)] * count


def plane_fetch(place, shards, raw, sems, slot):
    return [
        pltpu.make_async_copy(
            shards[4 * slot + rel],
            raw.at[slot, pl.ds(pl.multiple_of((place ^ rel) * SUBS * HALF, SUBS * HALF), SUBS * HALF)],
            sems.at[slot, rel],
        )
        for rel in range(4)
    ]


def take_plane(place, shards, raw, sems):
    step = pl.program_id(0)

    @pl.when(step == 0)
    def _():
        for slot in range(2):
            for copy in plane_fetch(place, shards, raw, sems, slot):
                copy.start()

    for slot in range(2):

        @pl.when(step == slot)
        def _():
            for copy in plane_fetch(place, shards, raw, sems, slot):
                copy.wait()

    return step


def head_rows(head):
    return slice(head * HROWS, (head + 1) * HROWS)


def fill_mask(sc, mask):
    @pl.when(pl.program_id(0) == 0)
    def _():
        shape = (LMAX, 4 * HEAD)
        column = lax.broadcasted_iota(jnp.int32, shape, 0)
        mask[...] = (column < lane_lengths(sc, shape)).astype(F32).astype(BF16)


def mix_kernel(carried, sc, *refs):
    shards, (v_own, v_far, *rest) = refs[:8], refs[8:]
    mixed, mean, exps, inverse, raw, mask, sems = rest[4:] if carried else rest
    fill_mask(sc, mask)
    slot = take_plane(sc[PLACE], shards, raw, sems)
    shape = (HROWS, 4 * HEAD)
    line = lax.broadcasted_iota(jnp.int32, shape, 0)
    position = 128 * (line // HALF) + HALF * sc[CORE] + line % HALF
    valid = position < lane_lengths(sc, shape)
    for head in range(PHEADS):
        weights = jnp.exp(raw[slot, head_rows(head)].astype(F32)).astype(BF16)
        exps[head] = weights
        both = dot(weights, jnp.concatenate([v_own[head], v_far[head], mask[...]], axis=1), 1, 0)
        flip = jnp.where(valid, 1.0 / both[:, 4 * HEAD :], 0.0)
        found = both[:, : 4 * HEAD] * flip
        inverse[head] = flip.astype(BF16)
        mean[head] = found
        mixed[head] = found.astype(BF16)


def run_mix(sc, planes, shards, v_own, v_far, carry):
    carry = list(carry)
    shape = (HEADS, HROWS, 4 * HEAD)
    return pl.pallas_call(
        partial(mix_kernel, bool(carry)),
        grid_spec=pltpu.PrefetchScalarGridSpec(
            num_scalar_prefetch=1,
            grid=(2,),
            in_specs=anywhere(8) + [plane_spec(planes, LMAX, 2 * HEAD)] * 2 + anywhere(len(carry)),
            out_specs=[
                plane_spec(planes, HROWS, 4 * HEAD),
                plane_spec(planes, HROWS, 4 * HEAD),
                plane_spec(planes, HROWS, LMAX),
                plane_spec(planes, HROWS, 4 * HEAD),
            ],
            scratch_shapes=[
                pltpu.VMEM((2, 4 * SUBS * HALF, LMAX), BF16),
                pltpu.VMEM((LMAX, 4 * HEAD), BF16),
                pltpu.SemaphoreType.DMA((2, 4)),
            ],
        ),
        out_shape=[
            jax.ShapeDtypeStruct(shape, BF16),
            jax.ShapeDtypeStruct(shape, F32),
            jax.ShapeDtypeStruct((HEADS, HROWS, LMAX), BF16),
            jax.ShapeDtypeStruct(shape, BF16),
        ],
        input_output_aliases={11 + i: i for i in range(len(carry))},
        compiler_params=params(VMEM),
        cost_estimate=pl.CostEstimate(
            flops=2 * HEADS * HROWS * LMAX * 4 * HEAD,
            bytes_accessed=HEADS * (2 * HROWS * LMAX + 5 * HROWS * 256),
            transcendentals=HEADS * HROWS * LMAX // 2,
        ),
        name="mix",
    )(sc, *shards, v_own, v_far, *carry)


def row_valid(sc, step):
    line = lax.broadcasted_iota(jnp.int32, (4 * SPAN, 1), 0)
    item = line // SPAN
    row = step * SPAN + line % SPAN
    low = jnp.where(item == 0, sc[LENGTHS], sc[LENGTHS + 1])
    high = jnp.where(item == 2, sc[LENGTHS + 2], sc[LENGTHS + 3])
    return 128 * (row // HALF) + HALF * sc[CORE] + row % HALF < jnp.where(item >= 2, high, low)


def four_items(own, far):
    return jnp.concatenate([own[:, :, 0], far[...]], axis=0).reshape(4 * SPAN, WIDTH)


def pre_kernel(sc, tok, tok_far, cot, cot_far, heads, wo_own, wo_far, gain, mixed, resid, normed, grad, weight):
    step = pl.program_id(0)
    whole_weight(sc, step, wo_own, wo_far, weight)
    for item in range(4):
        lanes = slice(item * HEAD, (item + 1) * HEAD)
        for pair in range(HEADS // 2):
            both = jnp.concatenate([heads[2 * pair, :, lanes], heads[2 * pair + 1, :, lanes]], axis=1)
            mixed[item, :, pair * 128 : (pair + 1) * 128] = both
    res = four_items(tok, tok_far).astype(F32) + dot(mixed[...].reshape(4 * SPAN, WIDTH), weight[...], 1, 0)
    resid[...] = res.astype(BF16).reshape(4, SPAN, WIDTH)
    scale = lax.rsqrt(jnp.mean(res * res, axis=-1, keepdims=True) + EPSILON)
    valid = row_valid(sc, step)
    normed[...] = jnp.where(valid, res * scale * gain[...], 0.0).astype(BF16).reshape(4, SPAN, WIDTH)
    masked = jnp.where(valid, four_items(cot, cot_far).astype(F32), 0.0)
    grad[...] = masked.astype(BF16).reshape(4, SPAN, WIDTH)


def slab_spec(items=4):
    return spec((items, SPAN, WIDTH), lambda r, s: (0, r, 0))


def half_specs():
    return [
        spec((2, SPAN // HALF, 1, HALF, WIDTH), lambda r, s: (0, r, s[CORE], 0, 0)),
        spec((2, SPAN // HALF, HALF, WIDTH), lambda r, s: (0, r, 0, 0)),
    ]


def heads_spec():
    return spec((HEADS, SPAN, 4 * HEAD), lambda r, s: (0, r, 0))


def run_pre(sc, tokens, tokens_far, cotangent, cotangent_far, heads, wo, gain):
    return pl.pallas_call(
        pre_kernel,
        grid_spec=pltpu.PrefetchScalarGridSpec(
            num_scalar_prefetch=1,
            grid=(HROWS // SPAN,),
            in_specs=half_specs()
            + half_specs()
            + [heads_spec(), held((WIDTH, SIDE)), held((WIDTH, SIDE)), held((1, WIDTH))],
            out_specs=[slab_spec()] * 4,
            scratch_shapes=[pltpu.VMEM((WIDTH, WIDTH), BF16)],
        ),
        out_shape=[
            jax.ShapeDtypeStruct((4, HROWS, WIDTH), BF16),
            jax.ShapeDtypeStruct((4, HROWS, WIDTH), BF16),
            jax.ShapeDtypeStruct((4, HROWS, WIDTH), BF16),
            jax.ShapeDtypeStruct((4, HROWS, WIDTH), BF16),
        ],
        compiler_params=params(VMEM),
        cost_estimate=pl.CostEstimate(
            flops=2 * ROWS * WIDTH * WIDTH, bytes_accessed=16 * ROWS * WIDTH, transcendentals=0
        ),
        name="pre",
    )(sc, tokens, tokens_far, cotangent, cotangent_far, heads, *wo, gain)


def own_lanes(sc):
    return pl.ds(pl.multiple_of(sc[CORE] * SIDE, 128), SIDE)


def far_lanes(sc):
    return pl.ds(pl.multiple_of((1 - sc[CORE]) * SIDE, 128), SIDE)


def unit_rows(f, sc):
    return (lax.rem(FSIDE * sc[CORE] + f, 2 * FSIDE), 0)


def unit_columns(f, sc):
    return (0, lax.rem(FSIDE * sc[CORE] + f, 2 * FSIDE))


def early(f, sc):
    return (0, lax.min(f, FSIDE - 1))


def late(f, sc):
    return (0, lax.max(f - FSIDE, 0))


def units_kernel(sc, normed, cot, up_own, up_far, dn_own, dn_far, active, up_grad, back, w_up, w_down, total):
    step = pl.program_id(0)
    w_down[:, own_lanes(sc)] = dn_own[...]
    w_down[:, far_lanes(sc)] = dn_far[...]

    @pl.when(step < FSIDE)
    def _():
        w_up[...] = up_own[...]

    @pl.when(step >= FSIDE)
    def _():
        w_up[...] = up_far[...]

    for piece in range(ROWS // TILE):
        whole = slice(piece * TILE, (piece + 1) * TILE)
        for row in range(piece * TILE, (piece + 1) * TILE, 256):
            rows = slice(row, row + 256)
            for column in range(0, FSTEP, 256):
                columns = slice(column, column + 256)
                up = dot(normed[rows], w_up[:, columns], 1, 0)
                square = up * up
                bend = jnp.tanh(up * (0.7978845608028654 + (0.044715 * 0.7978845608028654) * square))
                share = 0.5 + 0.5 * bend
                act = up * share
                active[rows, columns] = act.astype(BF16)
                slope = share + act * (1.0 - share) * (
                    2 * 0.7978845608028654 + (6 * 0.044715 * 0.7978845608028654) * square
                )
                up_grad[rows, columns] = (dot(cot[rows], w_down[columns], 1, 1) * slope).astype(BF16)
        two_grad = dot(up_grad[whole], w_up[...], 1, 1)

        @pl.when(step == 0)
        def _():
            total[whole] = two_grad

        @pl.when((step > 0) & (step < 2 * FSIDE - 1))
        def _():
            total[whole] += two_grad

        @pl.when(step == 2 * FSIDE - 1)
        def _():
            back[whole] = (total[whole] + two_grad).astype(BF16)


def run_units(sc, normed, cotangent, up, down):
    return pl.pallas_call(
        units_kernel,
        grid_spec=pltpu.PrefetchScalarGridSpec(
            num_scalar_prefetch=1,
            grid=(2 * FSIDE,),
            in_specs=[
                held((ROWS, WIDTH)),
                held((ROWS, WIDTH)),
                spec((WIDTH, FSTEP), early),
                spec((WIDTH, FSTEP), late),
                spec((FSTEP, SIDE), unit_rows),
                spec((FSTEP, SIDE), unit_rows),
            ],
            out_specs=[spec((ROWS, FSTEP), unit_columns), spec((ROWS, FSTEP), unit_columns), held((ROWS, WIDTH))],
            scratch_shapes=[
                pltpu.VMEM((WIDTH, FSTEP), BF16),
                pltpu.VMEM((FSTEP, WIDTH), BF16),
                pltpu.VMEM((ROWS, WIDTH), F32),
            ],
        ),
        out_shape=[
            jax.ShapeDtypeStruct((ROWS, FF), BF16),
            jax.ShapeDtypeStruct((ROWS, FF), BF16),
            jax.ShapeDtypeStruct((ROWS, WIDTH), BF16),
        ],
        compiler_params=params(VMEM),
        cost_estimate=pl.CostEstimate(
            flops=6 * ROWS * WIDTH * FF, bytes_accessed=8 * ROWS * WIDTH + 4 * ROWS * FF, transcendentals=ROWS * FF
        ),
        name="units",
    )(sc, normed.reshape(ROWS, WIDTH), cotangent.reshape(ROWS, WIDTH), *up, *down)


def down_grad_kernel(sc, active, cot, own, far, total):
    total[...] = dot(active[...], cot[...], 0, 0).astype(BF16)
    own[...] = total[:, own_lanes(sc)]
    far[...] = total[:, far_lanes(sc)]


def run_down_grad(sc, active, cotangent):
    return pl.pallas_call(
        down_grad_kernel,
        grid_spec=pltpu.PrefetchScalarGridSpec(
            num_scalar_prefetch=1,
            grid=(FF // 512,),
            in_specs=[spec((ROWS, 512), lambda f, s: (0, f)), held((ROWS, WIDTH))],
            out_specs=[spec((512, SIDE), lambda f, s: (f, 0))] * 2,
            scratch_shapes=[pltpu.VMEM((512, WIDTH), BF16)],
        ),
        out_shape=[jax.ShapeDtypeStruct((FF, SIDE), BF16)] * 2,
        compiler_params=params(VMEM),
        cost_estimate=pl.CostEstimate(
            flops=2 * ROWS * WIDTH * FF, bytes_accessed=2 * ROWS * (WIDTH + FF), transcendentals=0
        ),
        name="down_grad",
    )(sc, active, cotangent.reshape(ROWS, WIDTH))


def up_grad_kernel(sc, normed, up_grad, own, far):
    total = dot(normed[...], up_grad[...], 0, 0).astype(BF16)

    @pl.when(pl.program_id(0) < 3)
    def _():
        own[...] = total

    @pl.when(pl.program_id(0) >= 3)
    def _():
        far[...] = total


def run_up_grad(sc, normed, up_grad):
    return pl.pallas_call(
        up_grad_kernel,
        grid_spec=pltpu.PrefetchScalarGridSpec(
            num_scalar_prefetch=1,
            grid=(6,),
            in_specs=[held((ROWS, WIDTH)), spec((ROWS, 512), lambda f, s: (0, lax.rem(3 * s[CORE] + f, 6)))],
            out_specs=[
                spec((WIDTH, 512), lambda f, s: (0, lax.min(f, 2))),
                spec((WIDTH, 512), lambda f, s: (0, lax.max(f - 3, 0))),
            ],
        ),
        out_shape=[jax.ShapeDtypeStruct((WIDTH, FF // 2), BF16)] * 2,
        compiler_params=params(VMEM),
        cost_estimate=pl.CostEstimate(
            flops=2 * ROWS * WIDTH * FF, bytes_accessed=2 * ROWS * (WIDTH + FF), transcendentals=0
        ),
        name="up_grad",
    )(sc, normed.reshape(ROWS, WIDTH), up_grad)


def out_grad_kernel(sc, mixed, res_own, res_far, own, far, total):
    step = pl.program_id(0)
    grad = jnp.concatenate([res_own[...], res_far[...]], axis=0).reshape(4 * SPAN, WIDTH)
    found = dot(mixed[...].reshape(4 * SPAN, WIDTH), grad, 0, 0)

    @pl.when(step == 0)
    def _():
        total[...] = found

    @pl.when(step > 0)
    def _():
        total[...] += found

    @pl.when(step == pl.num_programs(0) - 1)
    def _():
        own[...] = total[:, own_lanes(sc)].astype(BF16)
        far[...] = total[:, far_lanes(sc)].astype(BF16)


def run_out_grad(sc, mixed, res_own, res_far):
    return pl.pallas_call(
        out_grad_kernel,
        grid_spec=pltpu.PrefetchScalarGridSpec(
            num_scalar_prefetch=1,
            grid=(HROWS // SPAN,),
            in_specs=[slab_spec(), slab_spec(2), slab_spec(2)],
            out_specs=[held((WIDTH, SIDE))] * 2,
            scratch_shapes=[pltpu.VMEM((WIDTH, WIDTH), F32)],
        ),
        out_shape=[jax.ShapeDtypeStruct((WIDTH, SIDE), BF16)] * 2,
        compiler_params=params(VMEM),
        cost_estimate=pl.CostEstimate(
            flops=2 * ROWS * WIDTH * WIDTH, bytes_accessed=4 * ROWS * WIDTH, transcendentals=0
        ),
        name="out_grad",
    )(sc, mixed, res_own, res_far)


def out_kernel(sc, active, resid, dn_own, dn_far, own, far, w_down):
    step = pl.program_id(0)

    @pl.when(step == 0)
    def _():
        w_down[:, own_lanes(sc)] = dn_own[...]
        w_down[:, far_lanes(sc)] = dn_far[...]

    branch = dot(active[...].reshape(4 * SPAN, FF), w_down[...], 1, 0)
    output = jnp.where(row_valid(sc, step), resid[...].reshape(4 * SPAN, WIDTH).astype(F32) + branch, 0.0)
    output = output.astype(BF16).reshape(4, SPAN, WIDTH)
    own[...] = output[:2]
    far[...] = output[2:]


def run_out(sc, active, resid, down):
    return pl.pallas_call(
        out_kernel,
        grid_spec=pltpu.PrefetchScalarGridSpec(
            num_scalar_prefetch=1,
            grid=(HROWS // SPAN,),
            in_specs=[
                spec((4, SPAN, FF), lambda r, s: (0, r, 0)),
                slab_spec(),
                held((FF, SIDE)),
                held((FF, SIDE)),
            ],
            out_specs=[slab_spec(2)] * 2,
            scratch_shapes=[pltpu.VMEM((FF, WIDTH), BF16)],
        ),
        out_shape=[
            jax.ShapeDtypeStruct((2, HROWS, WIDTH), BF16),
            jax.ShapeDtypeStruct((2, HROWS, WIDTH), BF16),
        ],
        compiler_params=params(VMEM),
        cost_estimate=pl.CostEstimate(
            flops=2 * ROWS * WIDTH * FF, bytes_accessed=ROWS * (2 * FF + 7 * WIDTH), transcendentals=0
        ),
        name="out",
    )(sc, active.reshape(4, HROWS, FF), resid, *down)


def post_kernel(sc, resid, back, cot, wo_own, wo_far, gain, *refs):
    (res_own, res_far, heads, d_gain, weight, spread) = refs
    step = pl.program_id(0)
    whole_weight(sc, step, wo_own, wo_far, weight)
    shape, slab = (4 * SPAN, WIDTH), (4, SPAN, WIDTH)
    valid = row_valid(sc, step)
    res = resid[...].reshape(shape).astype(F32)
    scale = lax.rsqrt(jnp.mean(res * res, axis=-1, keepdims=True) + EPSILON)
    unit = res * scale
    two_grad = jnp.where(valid, back[...].reshape(shape).astype(F32), 0.0)
    gained = two_grad * gain[...]
    masked = cot[...].reshape(shape).astype(F32)
    grad = masked + scale * (gained - unit * jnp.mean(gained * unit, axis=-1, keepdims=True))
    low = grad.astype(BF16)
    res_own[...] = low.reshape(slab)[:2]
    res_far[...] = low.reshape(slab)[2:]
    gain_sum = jnp.sum(two_grad * unit, axis=0, keepdims=True)

    @pl.when(step == 0)
    def _():
        d_gain[...] = gain_sum

    @pl.when(step > 0)
    def _():
        d_gain[...] += gain_sum

    spread[...] = dot(low, weight[...], 1, 1).astype(BF16).reshape(slab)
    for pair in range(HEADS // 2):
        lanes = slice(pair * 128, (pair + 1) * 128)
        for side in range(2):
            one, two = spread[2 * side, :, lanes], spread[2 * side + 1, :, lanes]
            half = slice(side * 128, (side + 1) * 128)
            heads[2 * pair, :, half] = jnp.concatenate([one[:, :HEAD], two[:, :HEAD]], axis=1)
            heads[2 * pair + 1, :, half] = jnp.concatenate([one[:, HEAD:], two[:, HEAD:]], axis=1)


def run_post(sc, resid, back, cotangent, wo, gain):
    whole = (4, HROWS, WIDTH)
    return pl.pallas_call(
        post_kernel,
        grid_spec=pltpu.PrefetchScalarGridSpec(
            num_scalar_prefetch=1,
            grid=(HROWS // SPAN,),
            in_specs=[slab_spec()] * 3 + [held((WIDTH, SIDE)), held((WIDTH, SIDE)), held((1, WIDTH))],
            out_specs=[slab_spec(2)] * 2 + [heads_spec(), held((1, WIDTH))],
            scratch_shapes=[
                pltpu.VMEM((WIDTH, WIDTH), BF16),
                pltpu.VMEM((4, SPAN, WIDTH), BF16),
            ],
        ),
        out_shape=[
            jax.ShapeDtypeStruct((2, HROWS, WIDTH), BF16),
            jax.ShapeDtypeStruct((2, HROWS, WIDTH), BF16),
            jax.ShapeDtypeStruct((HEADS, HROWS, 4 * HEAD), BF16),
            jax.ShapeDtypeStruct((1, WIDTH), F32),
        ],
        compiler_params=params(VMEM),
        cost_estimate=pl.CostEstimate(
            flops=4 * ROWS * WIDTH * WIDTH, bytes_accessed=28 * ROWS * WIDTH, transcendentals=0
        ),
        name="post",
    )(sc, resid, back.reshape(whole), cotangent, *wo, gain)


def unmix_kernel(carried, sc, v_own, v_far, grad_heads, mean, exps, inverse, *refs):
    refs = refs[2:] if carried else refs
    outs, (own, far, grads, mask, adder, bound, out_sems) = refs[:8], refs[8:]
    place = sc[PLACE]
    step = pl.program_id(0)

    def leave(slot):
        return [
            pltpu.make_async_copy(
                grads.at[slot, pl.ds(pl.multiple_of((place ^ rel) * SUBS * HALF, SUBS * HALF), SUBS * HALF)],
                outs[4 * slot + rel],
                out_sems.at[slot, rel],
            )
            for rel in range(4)
        ]

    fill_mask(sc, mask)

    @pl.when(step == 0)
    def _():
        lane = lax.broadcasted_iota(jnp.int32, (4 * HEAD, 128), 0) // HEAD
        column = lax.broadcasted_iota(jnp.int32, (4 * HEAD, 128), 1)
        adder[...] = jnp.where((lane == column) | (lane + 4 == column), -1.0, 0.0).astype(BF16)
        row = lax.broadcasted_iota(jnp.int32, (LMAX, 128), 0)
        item = lax.broadcasted_iota(jnp.int32, (LMAX, 128), 1)
        length = jnp.where(item % 4 == 0, sc[LENGTHS], sc[LENGTHS + 1])
        length = jnp.where(item % 4 == 2, sc[LENGTHS + 2], length)
        length = jnp.where(item % 4 == 3, sc[LENGTHS + 3], length)
        bound[...] = jnp.where((item < 8) & (row < length), 1.0, 0.0).astype(BF16)

    high_lanes = lax.broadcasted_iota(jnp.int32, (HROWS, 128), 1) < 4
    for head in range(PHEADS):
        weights = exps[head]
        low = (grad_heads[head].astype(F32) * inverse[head].astype(F32)).astype(BF16)
        product = low.astype(F32) * mean[head]
        coarse = product.astype(BF16)
        fine = (product - coarse.astype(F32)).astype(BF16)
        delta = dot(coarse, adder[...], 1, 0) + dot(fine, adder[...], 1, 0)
        coarse = delta.astype(BF16)
        fine = (delta - coarse.astype(F32)).astype(BF16)
        left = jnp.concatenate([low, jnp.where(high_lanes, coarse, fine)], axis=1)
        score = dot(left, jnp.concatenate([v_own[head], v_far[head], bound[...]], axis=1), 1, 1)
        grads[step, head_rows(head)] = (score * weights.astype(F32)).astype(BF16)
        back = (dot(weights, low, 0, 0) * mask[...].astype(F32)).astype(BF16)
        own[head] = back[:, : 2 * HEAD]
        far[head] = back[:, 2 * HEAD :]
    for which in range(2):

        @pl.when(step == which)
        def _():
            for copy in leave(which):
                copy.start()
            if which == 1:
                for copy in leave(0) + leave(1):
                    copy.wait()


def run_unmix(sc, planes, v_own, v_far, grad_heads, mean, exps, inverse, carry):
    carry = list(carry)
    return pl.pallas_call(
        partial(unmix_kernel, bool(carry)),
        grid_spec=pltpu.PrefetchScalarGridSpec(
            num_scalar_prefetch=1,
            grid=(2,),
            in_specs=[
                plane_spec(planes, LMAX, 2 * HEAD),
                plane_spec(planes, LMAX, 2 * HEAD),
                plane_spec(planes, HROWS, 4 * HEAD),
                plane_spec(planes, HROWS, 4 * HEAD),
                plane_spec(planes, HROWS, LMAX),
                plane_spec(planes, HROWS, 4 * HEAD),
            ]
            + anywhere(len(carry)),
            out_specs=anywhere(8) + [plane_spec(planes, LMAX, 2 * HEAD)] * 2,
            scratch_shapes=[
                pltpu.VMEM((2, 4 * SUBS * HALF, LMAX), BF16),
                pltpu.VMEM((LMAX, 4 * HEAD), BF16),
                pltpu.VMEM((4 * HEAD, 128), BF16),
                pltpu.VMEM((LMAX, 128), BF16),
                pltpu.SemaphoreType.DMA((2, 4)),
            ],
        ),
        out_shape=[jax.ShapeDtypeStruct((SUBS * HALF, LMAX), BF16)] * 8
        + [jax.ShapeDtypeStruct((HEADS, LMAX, 2 * HEAD), BF16)] * 2,
        input_output_aliases={7 + i: 8 + i for i in range(len(carry))},
        compiler_params=params(VMEM),
        cost_estimate=pl.CostEstimate(
            flops=3 * HEADS * HROWS * LMAX * 4 * HEAD,
            bytes_accessed=HEADS * (2 * HROWS * LMAX + 5 * HROWS * 256 + 4 * LMAX * 256),
            transcendentals=0,
        ),
        name="unmix",
    )(sc, v_own, v_far, grad_heads, mean, exps, inverse, *carry)


def close_kernel(sc, tok, res_own, res_got, out_own, out_got, own, far, gain, w_own, w_far, *refs):
    (output, tok_grad, d_value, d_gain, total, weight) = refs
    step = pl.program_id(0)
    whole_weight(sc, step, w_own, w_far, weight)
    core = sc[CORE]
    output[:, :, core] = out_own[...].astype(F32)
    output[:, :, 1 - core] = out_got[...].astype(F32)
    tok_grad[:, :, core] = res_own[...].astype(F32)
    tok_grad[:, :, 1 - core] = res_got[...].astype(F32)
    runs = tok.shape[1]
    rows = runs * 128
    for item in range(2):
        lanes = slice(item * HEAD, (item + 1) * HEAD)
        pieces = [
            add_low(own[head, :, lanes], far[head, :, lanes]) for head in range(HEADS)
        ]
        back = jnp.concatenate(pieces, axis=1)
        x = tok[item].reshape(rows, WIDTH).astype(F32)
        scale = lax.rsqrt(jnp.mean(x * x, axis=-1, keepdims=True) + EPSILON)
        unit = x * scale
        normed = (unit * gain[...]).astype(BF16)
        normed_grad = dot(back, weight[...], 1, 1)
        gained = normed_grad * gain[...]
        update = scale * (gained - unit * jnp.mean(gained * unit, axis=-1, keepdims=True))
        tok_grad[item] += update.reshape(runs, 2, HALF, WIDTH)
        gain_sum = jnp.sum(normed_grad * unit, axis=0, keepdims=True)
        value_sum = dot(normed, back, 0, 0)
        if item == 0:
            gain_total, value_total = gain_sum, value_sum
        else:
            gain_total, value_total = gain_total + gain_sum, value_total + value_sum

    @pl.when(step == 0)
    def _():
        d_gain[...] = gain_total
        total[...] = value_total

    @pl.when(step > 0)
    def _():
        d_gain[...] += gain_total
        total[...] += value_total

    @pl.when(step == pl.num_programs(0) - 1)
    def _():
        low = total[...].astype(BF16)
        d_value[0] = low[:, :SIDE]
        d_value[1] = low[:, SIDE:]


def run_close(sc, tokens, res_own, res_got, out_own, out_got, own, far, gain, w_own, w_far):
    runs = 2
    slab = (2, RUNS, 2, HALF, WIDTH)
    half = (2, RUNS, HALF, WIDTH)
    whole_spec = spec((2, runs, 2, HALF, WIDTH), lambda j, s: (0, j, 0, 0, 0))
    half_spec = spec((2, runs, HALF, WIDTH), lambda j, s: (0, j, 0, 0))
    back_spec = spec((HEADS, runs * 128, 2 * HEAD), lambda j, s: (0, j, 0))
    return pl.pallas_call(
        close_kernel,
        grid_spec=pltpu.PrefetchScalarGridSpec(
            num_scalar_prefetch=1,
            grid=(RUNS // runs,),
            in_specs=[whole_spec]
            + [half_spec] * 4
            + [back_spec, back_spec, held((1, WIDTH)), held((WIDTH, SIDE)), held((WIDTH, SIDE))],
            out_specs=[whole_spec, whole_spec, held((2, WIDTH, SIDE)), held((1, WIDTH))],
            scratch_shapes=[pltpu.VMEM((WIDTH, WIDTH), F32), pltpu.VMEM((WIDTH, WIDTH), BF16)],
        ),
        out_shape=[
            jax.ShapeDtypeStruct(slab, F32),
            jax.ShapeDtypeStruct(slab, F32),
            jax.ShapeDtypeStruct((2, WIDTH, SIDE), BF16),
            jax.ShapeDtypeStruct((1, WIDTH), F32),
        ],
        compiler_params=params(VMEM),
        cost_estimate=pl.CostEstimate(
            flops=4 * 2 * LMAX * WIDTH * WIDTH, bytes_accessed=38 * LMAX * WIDTH, transcendentals=0
        ),
        name="close",
    )(
        sc,
        tokens.reshape(slab),
        *(x.reshape(half) for x in (res_own, res_got, out_own, out_got)),
        own,
        far,
        gain,
        w_own,
        w_far,
    )


PACK_DOWN, PACK_UP, PACK_OUT, PACK_VALUE, PACK_GAIN, PACK = 0, 192, 384, 432, 480, 496


def pack_kernel(sc, down, up, out, value, gain, down_far, up_far, out_far, value_far, gain_far, packed):
    first = sc[CORE] == 0

    def both(own, far, lanes):
        own, far = own[:, lanes], far[:, lanes]
        return jnp.concatenate([jnp.where(first, own, far), jnp.where(first, far, own)], axis=0)

    def side(own, far):
        return both(own, far, own_lanes(sc))

    packed[PACK_DOWN:PACK_UP] = side(down, down_far)
    for j in range(4):
        lanes = pl.ds(pl.multiple_of((4 * sc[CORE] + j) * SIDE, 128), SIDE)
        packed[PACK_UP + 48 * j : PACK_UP + 48 * (j + 1)] = both(up, up_far, lanes)
    packed[PACK_OUT:PACK_VALUE] = side(out, out_far)
    packed[PACK_VALUE:PACK_GAIN] = side(value, value_far)
    packed[PACK_GAIN:] = both(gain, gain_far, slice(0, SIDE))


def run_pack(sc, own, far):
    return pl.pallas_call(
        pack_kernel,
        grid_spec=pltpu.PrefetchScalarGridSpec(
            num_scalar_prefetch=1,
            grid=(1,),
            in_specs=[held(x.shape) for x in (*own, *far)],
            out_specs=held((PACK, SIDE)),
        ),
        out_shape=jax.ShapeDtypeStruct((PACK, SIDE), BF16),
        compiler_params=params(VMEM),
        cost_estimate=pl.CostEstimate(flops=0, bytes_accessed=6 * PACK * SIDE, transcendentals=0),
        name="pack",
    )(sc, *own, *far)


def chip_of(sc, k, rel):
    return plane_of(k, sc) * 4 + (sc[PLACE] ^ rel)


def place_kernel(moves, sc, *refs):
    pieces, targets, sems = refs[:16], refs[16:-1], refs[-1]
    copies = []
    for index, piece in enumerate(pieces):
        chip = chip_of(sc, index // 4, index % 4)
        for which, (start, count, lane, target, step, offset, column) in enumerate(moves):
            rows = pl.ds(pl.multiple_of(chip * step + offset, 16), count)
            copies.append(
                pltpu.make_async_copy(
                    piece.at[pl.ds(start, count), pl.ds(lane, SIDE)],
                    targets[target].at[rows, pl.ds(column, SIDE)],
                    sems.at[index, which],
                )
            )
    for copy in copies:
        copy.start()
    for copy in copies:
        copy.wait()


def run_place(sc, pieces, moves, shapes):
    return pl.pallas_call(
        partial(place_kernel, moves),
        grid_spec=pltpu.PrefetchScalarGridSpec(
            num_scalar_prefetch=1,
            grid=(1,),
            in_specs=anywhere(16),
            out_specs=[held(shape) for shape in shapes],
            scratch_shapes=[pltpu.SemaphoreType.DMA((16, len(moves)))],
        ),
        out_shape=[jax.ShapeDtypeStruct(shape, BF16) for shape in shapes],
        compiler_params=params(VMEM),
        cost_estimate=pl.CostEstimate(
            flops=0, bytes_accessed=4 * sum(a * b for a, b in shapes), transcendentals=0
        ),
        name="place",
    )(sc, *pieces)


def place_weights(sc, pieces):
    moves = (
        (PACK_DOWN, 192, 0, 0, 192, 0, 0),
        *((PACK_UP + 48 * j, 48, 0, 1, 48, 0, j * SIDE) for j in range(4)),
        (PACK_OUT, 48, 0, 2, 48, 0, 0),
        (PACK_VALUE, 48, 0, 3, 48, 0, 0),
        (PACK_GAIN, 16, 0, 4, 16, 0, 0),
    )
    shapes = [(FF, SIDE), (WIDTH, FF // 2), (WIDTH, SIDE), (WIDTH, SIDE), (256, SIDE)]
    return run_place(sc, pieces, moves, shapes)


def collect_kernel(sc, *refs):
    outs = refs[24:]
    for k in range(PLANES):

        @pl.when(pl.program_id(0) == k)
        def _():
            for rel in range(4):
                down, down_got, up, up_got, out, out_got = refs[6 * rel : 6 * rel + 6]
                packed = outs[4 * k + rel]
                packed[PACK_DOWN:PACK_UP] = add_low(down[...], down_got[...])
                for j in range(4):
                    lanes = slice(j * SIDE, (j + 1) * SIDE)
                    packed[PACK_UP + 48 * j : PACK_UP + 48 * (j + 1)] = add_low(up[:, lanes], up_got[:, lanes])
                packed[PACK_OUT:PACK_VALUE] = add_low(out[...], out_got[...])


def run_collect(sc, *sides):
    def rows(x, rel):
        return spec((x.shape[0] // 16, x.shape[1]), lambda k, s: (chip_of(s, k, rel), 0))

    return pl.pallas_call(
        collect_kernel,
        grid_spec=pltpu.PrefetchScalarGridSpec(
            num_scalar_prefetch=1,
            grid=(PLANES,),
            in_specs=[rows(x, rel) for rel in range(4) for x in sides],
            out_specs=[held((PACK_VALUE, SIDE))] * 16,
        ),
        out_shape=[jax.ShapeDtypeStruct((PACK_VALUE, SIDE), BF16)] * 16,
        compiler_params=params(VMEM),
        cost_estimate=pl.CostEstimate(flops=0, bytes_accessed=3 * 16 * PACK_VALUE * SIDE * 2, transcendentals=0),
        name="collect",
    )(sc, *(x for _ in range(4) for x in sides))


def add_kernel(groups, *refs):
    for group, total in zip(groups, refs[-len(groups) :]):
        value = refs[group[0]][...].astype(F32)
        for index in group[1:]:
            value = value + refs[index][...].astype(F32)
        total[...] = value.astype(total.dtype)


def run_add(groups, values, dtype):
    rows, columns = values[0].shape
    parts = 2 if columns == LMAX else 1
    block = pl.BlockSpec((rows // parts, columns), lambda i: (i, 0))
    return pl.pallas_call(
        partial(add_kernel, groups),
        grid=(parts,),
        in_specs=[block] * len(values),
        out_specs=[block] * len(groups),
        out_shape=[jax.ShapeDtypeStruct((rows, columns), dtype)] * len(groups),
        compiler_params=params(VMEM),
        cost_estimate=pl.CostEstimate(
            flops=0, bytes_accessed=2 * rows * columns * (len(values) + len(groups)), transcendentals=0
        ),
        name="add",
    )(*values)


DEVICES = 32
TO_CORE, TO_X, TO_Y = 1, 2, 4


def swap(x, bit):
    return lax.ppermute(x, BOTH, [(d, d ^ bit) for d in range(DEVICES)])


def ring(x, way=1):
    return lax.ppermute(x, BOTH, [(d, (d + 8 * way) % DEVICES) for d in range(DEVICES)])


def pick(x, index, axis=0):
    return lax.dynamic_index_in_dim(x, index, axis, keepdims=False)


def ordered(flag, one, two, axis=0, joined=jnp.stack):
    return jnp.where(flag == 0, joined([one, two], axis), joined([two, one], axis))


def add_low(one, two):
    return (one.astype(F32) + two.astype(F32)).astype(BF16)


STEPS = (
    ((0, 0, 1), (0, 1, 0), (1, 0, 0)),
    ((1, 0, 1), (0, 1, 1), (2, 0, 0)),
    ((2, 0, 1), (1, 1, 0), (3, 0, 0)),
    ((3, 0, 1), (2, 1, 0), (1, 1, 1)),
    ((2, 1, 1), (3, 1, 1), (3, 1, 0)),
)


def gather_step(have, step):
    by_x, by_y, by_z = STEPS[step]
    return {
        **have,
        by_z: ring(have[by_z[0] - 1, by_z[1], by_z[2]]),
        by_x: swap(have[by_x[0], by_x[1], 0], TO_X),
        by_y: swap(have[by_y[0], 0, by_y[2]], TO_Y),
    }


def in_order(have):
    return [have[k, y, x] for k in range(4) for y in range(2) for x in range(2)]


def by_place(shares, planes=range(PLANES)):
    return {(k, i // 2, i % 2): shares[4 * at + i] for at, k in enumerate(planes) for i in range(4)}


def scatter_send(have, step):
    by_x, by_y, by_z = STEPS[len(STEPS) - 1 - step]
    got = (ring(have[by_z], -1), swap(have[by_x], TO_X), swap(have[by_y], TO_Y))
    return {at: value for at, value in have.items() if at not in (by_x, by_y, by_z)}, got


def scatter_add(have, got, step):
    by_x, by_y, by_z = STEPS[len(STEPS) - 1 - step]
    targets = ((by_z[0] - 1, by_z[1], by_z[2]), (by_x[0], by_x[1], 0), (by_y[0], 0, by_y[2]))
    sums = list(dict.fromkeys(targets))
    groups = [(len(got) + i, *(j for j in range(len(got)) if targets[j] == at)) for i, at in enumerate(sums)]
    values = [*got, *(have[at] for at in sums)]
    return {**have, **dict(zip(sums, run_add(groups, values, F32 if step == len(STEPS) - 1 else BF16)))}


together = lax.optimization_barrier


def chip_shards(tokens, lengths, rand_mix, w_value, w_out, w_up, w_down, gain_mix, gain_ffn, grad_out):
    wide = lax.axis_index("wide")
    core = lax.axis_index("narrow")
    z, y, x = wide // 4, (wide // 2) % 2, wide % 2
    other = lambda value: swap(value, TO_CORE)
    side = partial(ordered, core, joined=jnp.concatenate)
    slab = (2, RUNS, 2, HALF, WIDTH)
    tokens, grad_out = tokens.reshape(slab), grad_out.reshape(slab)

    gains = jnp.pad(jnp.concatenate([gain_mix, gain_ffn])[None], ((0, 7), (0, SIDE - 48)))
    own = (w_down, w_up, w_out, w_value, gains)
    far = tuple(other(value) for value in own)
    near_sc = jnp.concatenate([jnp.stack([core, z, wide % 4]).astype(jnp.int32), lengths, lengths])
    weights = {(0, 0, 0): run_pack(near_sc, own, far)}

    rand = rand_mix.reshape(3, 2, HALF, LMAX)
    blocks = side(pick(rand, core, 1), other(pick(rand, 1 - core, 1)), 0)
    weights, rands, late_tokens, late_grad = together(
        (gather_step(weights, 0), {(0, 0, 0): blocks.reshape(SUBS * HALF, LMAX)}, tokens, grad_out)
    )
    weights, tokens_far = together((gather_step(weights, 1), other(pick(late_tokens, 1 - core, 2))))
    weights, grad_far = together((gather_step(weights, 2), other(pick(late_grad, 1 - core, 2))))
    weights, far_lengths = together((gather_step(weights, 3), other(lengths)))
    sc = jnp.concatenate([near_sc[:5], far_lengths])
    weights, rands = together((gather_step(weights, 4), rands))

    rands = gather_step(rands, 0)
    down, up, out, value, gain_rows = place_weights(sc, in_order(weights))
    rands, value, value_far, gain_rows, out, down, up = together(
        (rands, value, other(value), gain_rows, out, down, up)
    )
    gain_rows = gain_rows.reshape(16, 2, 8, SIDE)[:, :, 0]
    gain_one = gain_rows[..., :24].reshape(1, WIDTH).astype(F32)
    gain_two = gain_rows[..., 24:48].reshape(1, WIDTH).astype(F32)
    rands = gather_step(rands, 1)
    v_own = run_values(sc, tokens.reshape(2, LMAX, WIDTH), gain_one, value, value_far)
    rands, v_own, out, down, up = together((rands, v_own, (out, other(out)), down, up))
    rands, v_own, v_far, down, up = together((gather_step(rands, 2), v_own, other(v_own), down, up))
    rands, v_far, down, up = together((gather_step(rands, 3), v_far, down, up))
    near = [rands[k, y_at, x_at] for k in range(2) for y_at in range(2) for x_at in range(2)]
    rands = gather_step(rands, 4)
    mixing = run_mix(sc, (0, 1), near, v_own, v_far, ())
    rands, down, up, mixing = together((rands, down, up, mixing))
    heads, mean, exps, inverse = run_mix(sc, (2, 3), in_order(rands)[8:], v_own, v_far, mixing)
    down, up = (down, other(down)), (up, other(up))

    mixed, resid, normed, masked = run_pre(sc, tokens, tokens_far, grad_out, grad_far, heads, out, gain_two)
    active, up_grad, back = run_units(sc, normed, masked, up, down)
    res_own, res_far, grad_heads, d_gain_two = run_post(sc, resid, back, masked, out, gain_two)

    backward = lambda planes, carry: run_unmix(sc, planes, v_own, v_far, grad_heads, mean, exps, inverse, carry)
    *far, back_own, back_far = backward((3, 2), ())
    far, back_own, back_far, res_got = together((far, back_own, back_far, other(res_far)))
    have, got = scatter_send(by_place(far, (3, 2)), 0)
    *near, back_own, back_far = backward((1, 0), (back_own, back_far))
    have, got, near, back_own, back_far = together((have, got, near, back_own, back_far))
    have = {**scatter_add(have, got, 0), **by_place(near, (1, 0))}

    have, got = scatter_send(have, 1)
    up_own, up_far = run_up_grad(sc, normed, up_grad)
    have, got, up_own, up_far, back_got = together((have, got, up_own, up_far, other(back_far)))
    have = scatter_add(have, got, 1)

    have, got = scatter_send(have, 2)
    down_own, down_far = run_down_grad(sc, active, masked)
    have, got, down_own, down_far, up_got = together((have, got, down_own, down_far, other(up_far)))
    have = scatter_add(have, got, 2)

    have, got = scatter_send(have, 3)
    d_out_own, d_out_far = run_out_grad(sc, mixed, res_own, res_far)
    packed = run_collect(sc, down_own, other(down_far), up_own, up_got, d_out_own, other(d_out_far))
    have, got, packed = together((have, got, packed))
    have = scatter_add(have, got, 3)

    have, got = scatter_send(have, 4)
    out_own, out_far = run_out(sc, active, resid, down)
    have, got, packed, out_own, out_far = together((have, got, packed, out_own, out_far))
    rand_sum = scatter_add(have, got, 4)[0, 0, 0].reshape(2, 3, HALF, LMAX)

    sums, got = scatter_send(by_place(packed), 0)
    sums, got = scatter_send(scatter_add(sums, got, 0), 1)
    output, tokens_grad, d_value, d_gain_one = run_close(
        sc, tokens, res_own, res_got, out_own, other(out_far), back_own, back_got, gain_one, value, value_far
    )
    sums, got, output, tokens_grad, d_value, d_gain_one = together(
        (sums, got, output, tokens_grad, d_value, d_gain_one)
    )
    sums = scatter_add(sums, got, 1)

    sums, got = scatter_send(sums, 2)
    gain_pair = jnp.concatenate([d_gain_one, d_gain_two]).reshape(2, 16, 1, 48).astype(BF16)
    gain_pair = jnp.pad(gain_pair, ((0, 0), (0, 0), (0, 15), (0, SIDE - 48)))
    small = jnp.concatenate([d_value.reshape(2, 16, 48, SIDE), gain_pair], 2)
    small = add_low(pick(small, core), other(pick(small, 1 - core))).reshape(4, 2, 2, 64, SIDE)
    small = add_low(pick(small, x, 2), swap(pick(small, 1 - x, 2), TO_X))
    sums, got, small = together((sums, got, small))
    sums = scatter_add(sums, got, 2)

    sums, got = scatter_send(sums, 3)
    small = add_low(pick(small, y, 1), swap(pick(small, 1 - y, 1), TO_Y))
    blocks, blocks_far = pick(rand_sum, core), other(pick(rand_sum, 1 - core))
    sums, got, small, blocks, blocks_far = together((sums, got, small, blocks, blocks_far))
    sums = scatter_add(sums, got, 3)

    sums, got = scatter_send(sums, 4)
    small_sum = pick(small, z).astype(F32)
    for k in range(1, PLANES):
        small_sum = small_sum + ring(pick(small, lax.rem(z + PLANES - k, PLANES)), -k).astype(F32)
    sums, got, small_sum = together((sums, got, small_sum))
    big_sum = scatter_add(sums, got, 4)[0, 0, 0]
    big_far, small_far = other(big_sum), other(small_sum)

    rows_of = lambda value, rows: pick(value.reshape(-1, 2, rows, SIDE), core, 1)
    mine = lambda own, far, rows: side(rows_of(own, rows)[0], rows_of(far, rows)[0], 1)
    down_shard = mine(big_sum[PACK_DOWN:PACK_UP], big_far[PACK_DOWN:PACK_UP], 96)
    up_side = lambda value: rows_of(value[PACK_UP:PACK_OUT], 24).transpose(1, 0, 2).reshape(24, 4 * SIDE)
    up_shard = side(up_side(big_sum), up_side(big_far), 1)
    outproj_shard = mine(big_sum[PACK_OUT:PACK_VALUE], big_far[PACK_OUT:PACK_VALUE], 24)
    value_shard = mine(small_sum[:48], small_far[:48], 24)
    gains_pair = ordered(core, small_sum[48, :48], small_far[48, :48])
    gain_pair = pick(gains_pair.reshape(2, 2, 24), core, 1)

    rand_shard = ordered(core, blocks, blocks_far, 1)

    return (
        output.reshape(2, LMAX, WIDTH),
        tokens_grad.reshape(2, LMAX, WIDTH),
        rand_shard.reshape(3 * 128, LMAX),
        value_shard,
        outproj_shard,
        up_shard,
        down_shard,
        gain_pair[0],
        gain_pair[1],
    )


def rms_norm(values, gain):
    scale = lax.rsqrt(jnp.mean(values * values, axis=-1, keepdims=True) + EPSILON)
    return values * scale * gain


def split_heads(block):
    return block.reshape(LMAX, HEADS, HEAD).transpose(1, 0, 2)


def merge_heads(block):
    return block.transpose(1, 0, 2).reshape(LMAX, HEADS * HEAD)


def masked_scores(key_mask, rand_head):
    return jnp.where(key_mask[None, :] > 0, rand_head.astype(jnp.float32), -1e30)


def head_forward(key_mask, paired):
    rand_head, value_head = paired
    scores = masked_scores(key_mask, rand_head)
    row_peak = jnp.max(scores, axis=-1, keepdims=True)
    exponent = jnp.exp(scores - row_peak)
    denom_sum = jnp.sum(exponent, axis=-1, keepdims=True)
    attention = exponent / denom_sum * key_mask[:, None]
    mixed = jnp.dot(attention.astype(jnp.bfloat16), value_head, preferred_element_type=jnp.float32)
    return (mixed.astype(jnp.bfloat16), row_peak + jnp.log(denom_sum))


def head_backward(key_mask, paired):
    rand_head, value_head, mix_grad, log_total = paired
    scores = masked_scores(key_mask, rand_head)
    attention = jnp.exp(scores - log_total) * key_mask[:, None]
    prob_grad = jnp.einsum("id,jd->ij", mix_grad, value_head, preferred_element_type=jnp.float32)
    value_grad = jnp.einsum(
        "ij,id->jd", attention.astype(jnp.bfloat16), mix_grad, preferred_element_type=jnp.float32
    )
    score_grad = attention * (prob_grad - jnp.sum(prob_grad * attention, axis=-1, keepdims=True))
    return (score_grad, value_grad)


def shards(tokens, lengths, rand_mix, w_value, w_out, w_up, w_down, gain_mix, gain_ffn, grad_out):
    item_count = tokens.shape[0]
    width = tokens.shape[2]
    row_count = item_count * LMAX
    tokens_flat = tokens.reshape(row_count, width).astype(jnp.float32)
    positions = jnp.arange(LMAX, dtype=jnp.int32)
    valid_table = (positions[None, :] < lengths[:, None]).astype(jnp.float32)
    row_valid = valid_table.reshape(row_count, 1)
    forward_set = (
        lax.all_gather(rand_mix, ("wide", "narrow"), axis=0, tiled=True),
        lax.all_gather(w_value, ("wide", "narrow"), axis=0, tiled=True),
        lax.all_gather(w_out, ("wide", "narrow"), axis=0, tiled=True),
        lax.all_gather(w_up, ("wide", "narrow"), axis=0, tiled=True),
        lax.all_gather(w_down, ("wide", "narrow"), axis=0, tiled=True),
        lax.all_gather(gain_mix, ("wide", "narrow"), axis=0, tiled=True),
        lax.all_gather(gain_ffn, ("wide", "narrow"), axis=0, tiled=True),
    )
    rand_all, value_all, out_all, up_all, down_all, gain_first, gain_second = forward_set
    normed = rms_norm(tokens_flat, gain_first.astype(jnp.float32)).astype(jnp.bfloat16)
    values = jnp.dot(normed, value_all, preferred_element_type=jnp.float32).astype(jnp.bfloat16)
    rand_heads = rand_all.reshape(HEADS, LMAX, LMAX)
    mixed_parts = []
    totals_kept = []
    for item_index in range(item_count):
        item_values = split_heads(values[item_index * LMAX : (item_index + 1) * LMAX])
        mixed_heads, log_total = lax.map(
            partial(head_forward, valid_table[item_index]), (rand_heads, item_values)
        )
        mixed_parts.append(merge_heads(mixed_heads))
        totals_kept.append(log_total)
    mixed = jnp.concatenate(mixed_parts, axis=0)
    residual = tokens_flat + jnp.dot(mixed, out_all, preferred_element_type=jnp.float32)
    normed_two = rms_norm(residual, gain_second.astype(jnp.float32)).astype(jnp.bfloat16)
    up_proj = jnp.dot(normed_two, up_all, preferred_element_type=jnp.float32)
    active = jax.nn.gelu(up_proj).astype(jnp.bfloat16)
    branch = jnp.dot(active, down_all, preferred_element_type=jnp.float32)
    output = row_valid * (residual + branch)
    back_set = (
        lax.all_gather(rand_mix, ("wide", "narrow"), axis=0, tiled=True),
        lax.all_gather(w_value, ("wide", "narrow"), axis=0, tiled=True),
        lax.all_gather(w_out, ("wide", "narrow"), axis=0, tiled=True),
        lax.all_gather(w_up, ("wide", "narrow"), axis=0, tiled=True),
        lax.all_gather(w_down, ("wide", "narrow"), axis=0, tiled=True),
        lax.all_gather(gain_mix, ("wide", "narrow"), axis=0, tiled=True),
        lax.all_gather(gain_ffn, ("wide", "narrow"), axis=0, tiled=True),
    )
    rand_back, value_back, out_back, up_back, down_back, gain_back_one, gain_back_two = back_set
    cotangent = grad_out.reshape(row_count, width).astype(jnp.float32)
    masked = row_valid * cotangent
    branch_grad = masked.astype(jnp.bfloat16)
    grad_down = jnp.einsum("rk,rd->kd", active, branch_grad, preferred_element_type=jnp.float32)
    active_grad = jnp.einsum(
        "rd,kd->rk", branch_grad, down_back, preferred_element_type=jnp.float32
    )
    gelu_value, gelu_pull = jax.vjp(jax.nn.gelu, up_proj)
    up_grad = gelu_pull(active_grad)[0].astype(jnp.bfloat16)
    grad_up = jnp.einsum("rd,rk->dk", normed_two, up_grad, preferred_element_type=jnp.float32)
    normed_two_grad = jnp.einsum("rk,dk->rd", up_grad, up_back, preferred_element_type=jnp.float32)
    norm_value, norm_pull = jax.vjp(rms_norm, residual, gain_back_two.astype(jnp.float32))
    residual_part, gain_two_grad = norm_pull(normed_two_grad)
    residual_grad = masked + residual_part
    attn_grad = residual_grad.astype(jnp.bfloat16)
    grad_outproj = jnp.einsum("rd,re->de", mixed, attn_grad, preferred_element_type=jnp.float32)
    mixed_grad = jnp.einsum(
        "re,de->rd", attn_grad, out_back, preferred_element_type=jnp.float32
    ).astype(jnp.bfloat16)
    rand_heads_back = rand_back.reshape(HEADS, LMAX, LMAX)
    rand_grad = jnp.zeros((HEADS, LMAX, LMAX), jnp.float32)
    value_parts = []
    for item_index in range(item_count):
        lower_row = item_index * LMAX
        upper_row = lower_row + LMAX
        item_values = split_heads(values[lower_row:upper_row])
        item_mix_grad = split_heads(mixed_grad[lower_row:upper_row])
        score_grad, value_grad = lax.map(
            partial(head_backward, valid_table[item_index]),
            (rand_heads_back, item_values, item_mix_grad, totals_kept[item_index]),
        )
        rand_grad = rand_grad + score_grad
        value_parts.append(merge_heads(value_grad))
    values_grad = jnp.concatenate(value_parts, axis=0).astype(jnp.bfloat16)
    grad_value = jnp.einsum("rd,re->de", normed, values_grad, preferred_element_type=jnp.float32)
    normed_grad = jnp.einsum(
        "re,de->rd", values_grad, value_back, preferred_element_type=jnp.float32
    )
    norm_first, first_pull = jax.vjp(rms_norm, tokens_flat, gain_back_one.astype(jnp.float32))
    token_part, gain_one_grad = first_pull(normed_grad)
    tokens_grad = residual_grad + token_part
    rand_flat = rand_grad.reshape(HEADS * LMAX, LMAX)
    all_shards = (
        lax.psum_scatter(rand_flat, ("wide", "narrow"), scatter_dimension=0, tiled=True),
        lax.psum_scatter(grad_value, ("wide", "narrow"), scatter_dimension=0, tiled=True),
        lax.psum_scatter(grad_outproj, ("wide", "narrow"), scatter_dimension=0, tiled=True),
        lax.psum_scatter(grad_up, ("wide", "narrow"), scatter_dimension=0, tiled=True),
        lax.psum_scatter(grad_down, ("wide", "narrow"), scatter_dimension=0, tiled=True),
        lax.psum_scatter(gain_one_grad, ("wide", "narrow"), scatter_dimension=0, tiled=True),
        lax.psum_scatter(gain_two_grad, ("wide", "narrow"), scatter_dimension=0, tiled=True),
    )
    rand_shard, value_shard, outproj_shard, up_shard, down_shard, gain_one_shard, gain_two_shard = (
        all_shards
    )
    return (
        output.reshape(item_count, LMAX, width),
        tokens_grad.reshape(item_count, LMAX, width),
        rand_shard,
        value_shard,
        outproj_shard,
        up_shard,
        down_shard,
        gain_one_shard,
        gain_two_shard,
    )


def solution(mesh):
    in_specs = (
        P(("wide", "narrow"), None, None),
        P(("wide", "narrow")),
        P(("wide", "narrow"), None),
        P(("wide", "narrow"), None),
        P(("wide", "narrow"), None),
        P(("wide", "narrow"), None),
        P(("wide", "narrow"), None),
        P(("wide", "narrow")),
        P(("wide", "narrow")),
        P(("wide", "narrow"), None, None),
    )
    out_specs = (
        P(("wide", "narrow"), None, None),
        P(("wide", "narrow"), None, None),
        P(("wide", "narrow"), None),
        P(("wide", "narrow"), None),
        P(("wide", "narrow"), None),
        P(("wide", "narrow"), None),
        P(("wide", "narrow"), None),
        P(("wide", "narrow")),
        P(("wide", "narrow")),
    )
    fits = dict(mesh.shape) == {"wide": 16, "narrow": 2}
    return jax.shard_map(chip_shards if fits else shards, mesh=mesh, in_specs=in_specs, out_specs=out_specs, check_vma=False)
```

```python
from functools import partial

import jax
import jax.numpy as jnp
from jax import lax
from jax.experimental import pallas as pl
from jax.experimental.pallas import tpu as pltpu
from jax.sharding import PartitionSpec as P

HEADS = 12
HEAD = 64
LMAX = 1024
WIDTH = 768
FF = 3072
EPSILON = 1e-05

BOTH = ("wide", "narrow")
BF16 = jnp.bfloat16
F32 = jnp.float32
VMEM = 61 << 20
LESS = 34 << 20

SUBS = 6
RUNS = 8
HALF = 64
HROWS = RUNS * HALF
PLANES = 4
PHEADS = HEADS // PLANES
ROWS = 2 * LMAX
FSTEP = 768
FSIDE = FF // 2 // FSTEP
TILE = 512
SIDE = WIDTH // 2
SPAN = 2 * HALF


def dot(a, b, ca, cb):
    return lax.dot_general(a, b, (((ca,), (cb,)), ((), ())), preferred_element_type=F32)


CORE, PLANE, PLACE, LENGTHS = 0, 1, 2, 3


def spec(shape, index):
    return pl.BlockSpec(shape, index)


def held(shape):
    zeros = (0,) * len(shape)
    return pl.BlockSpec(shape, lambda *_: zeros, pipeline_mode=pl.Buffered(1))


def params(limit):
    return pltpu.CompilerParams(vmem_limit_bytes=limit)


def whole_weight(sc, step, own, far, weight):
    @pl.when(step == 0)
    def _():
        weight[:, pl.ds(pl.multiple_of(sc[CORE] * SIDE, 128), SIDE)] = own[...]
        weight[:, pl.ds(pl.multiple_of((1 - sc[CORE]) * SIDE, 128), SIDE)] = far[...]


def values_kernel(sc, tok, gain, w_own, w_far, out, weight):
    step = pl.program_id(0)
    whole_weight(sc, step, w_own, w_far, weight)
    rows = tok.shape[1]
    position = step * rows + lax.broadcasted_iota(jnp.int32, (rows, 1), 0)
    for item in range(2):
        x = tok[item].astype(F32)
        scale = lax.rsqrt(jnp.mean(x * x, axis=-1, keepdims=True) + EPSILON)
        normed = (x * scale * gain[...]).astype(BF16)
        found = dot(normed, weight[...], 1, 0)
        found = jnp.where(position < sc[LENGTHS + item], found, 0.0).astype(BF16)
        for head in range(HEADS):
            out[head, :, item * HEAD : (item + 1) * HEAD] = found[:, head * HEAD : (head + 1) * HEAD]


def run_values(sc, tokens, gain, w_own, w_far):
    rows = 256
    return pl.pallas_call(
        values_kernel,
        grid_spec=pltpu.PrefetchScalarGridSpec(
            num_scalar_prefetch=1,
            grid=(LMAX // rows,),
            in_specs=[
                spec((2, rows, WIDTH), lambda j, s: (0, j, 0)),
                held((1, WIDTH)),
                held((WIDTH, SIDE)),
                held((WIDTH, SIDE)),
            ],
            out_specs=spec((HEADS, rows, 2 * HEAD), lambda j, s: (0, j, 0)),
            scratch_shapes=[pltpu.VMEM((WIDTH, WIDTH), BF16)],
        ),
        out_shape=jax.ShapeDtypeStruct((HEADS, LMAX, 2 * HEAD), BF16),
        compiler_params=params(VMEM),
        cost_estimate=pl.CostEstimate(
            flops=2 * 2 * LMAX * WIDTH * WIDTH, bytes_accessed=8 * LMAX * WIDTH, transcendentals=0
        ),
        name="values",
    )(sc, tokens, gain, w_own, w_far)


def lane_lengths(sc, shape):
    slot = lax.broadcasted_iota(jnp.int32, shape, 1) // HEAD
    length = jnp.where(slot == 0, sc[LENGTHS], sc[LENGTHS + 1])
    return jnp.where(slot >= 2, jnp.where(slot == 2, sc[LENGTHS + 2], sc[LENGTHS + 3]), length)


def plane_of(k, sc):
    return lax.rem(sc[PLANE] + PLANES - k, PLANES)


def plane_spec(planes, rows, lanes):
    def index(step, sc):
        return (plane_of(planes[0] + step * (planes[1] - planes[0]), sc), 0, 0)

    return spec((PHEADS, rows, lanes), index)


def anywhere(count):
    return [pl.BlockSpec(memory_space=pl.ANY)] * count


def plane_fetch(place, shards, raw, sems, slot):
    return [
        pltpu.make_async_copy(
            shards[4 * slot + rel],
            raw.at[slot, pl.ds(pl.multiple_of((place ^ rel) * SUBS * HALF, SUBS * HALF), SUBS * HALF)],
            sems.at[slot, rel],
        )
        for rel in range(4)
    ]


def take_plane(place, shards, raw, sems):
    step = pl.program_id(0)

    @pl.when(step == 0)
    def _():
        for slot in range(2):
            for copy in plane_fetch(place, shards, raw, sems, slot):
                copy.start()

    for slot in range(2):

        @pl.when(step == slot)
        def _():
            for copy in plane_fetch(place, shards, raw, sems, slot):
                copy.wait()

    return step


def head_rows(head):
    return slice(head * HROWS, (head + 1) * HROWS)


def fill_mask(sc, mask):
    @pl.when(pl.program_id(0) == 0)
    def _():
        shape = (LMAX, 4 * HEAD)
        column = lax.broadcasted_iota(jnp.int32, shape, 0)
        mask[...] = (column < lane_lengths(sc, shape)).astype(F32).astype(BF16)


def mix_kernel(carried, sc, *refs):
    shards, (v_own, v_far, *rest) = refs[:8], refs[8:]
    mixed, mean, exps, inverse, raw, mask, sems = rest[4:] if carried else rest
    fill_mask(sc, mask)
    slot = take_plane(sc[PLACE], shards, raw, sems)
    shape = (HROWS, 4 * HEAD)
    line = lax.broadcasted_iota(jnp.int32, shape, 0)
    position = 128 * (line // HALF) + HALF * sc[CORE] + line % HALF
    valid = position < lane_lengths(sc, shape)
    for head in range(PHEADS):
        weights = jnp.exp(raw[slot, head_rows(head)].astype(F32)).astype(BF16)
        exps[head] = weights
        both = dot(weights, jnp.concatenate([v_own[head], v_far[head], mask[...]], axis=1), 1, 0)
        flip = jnp.where(valid, 1.0 / both[:, 4 * HEAD :], 0.0)
        found = both[:, : 4 * HEAD] * flip
        inverse[head] = flip.astype(BF16)
        mean[head] = found
        mixed[head] = found.astype(BF16)


def run_mix(sc, planes, shards, v_own, v_far, carry):
    carry = list(carry)
    shape = (HEADS, HROWS, 4 * HEAD)
    return pl.pallas_call(
        partial(mix_kernel, bool(carry)),
        grid_spec=pltpu.PrefetchScalarGridSpec(
            num_scalar_prefetch=1,
            grid=(2,),
            in_specs=anywhere(8) + [plane_spec(planes, LMAX, 2 * HEAD)] * 2 + anywhere(len(carry)),
            out_specs=[
                plane_spec(planes, HROWS, 4 * HEAD),
                plane_spec(planes, HROWS, 4 * HEAD),
                plane_spec(planes, HROWS, LMAX),
                plane_spec(planes, HROWS, 4 * HEAD),
            ],
            scratch_shapes=[
                pltpu.VMEM((2, 4 * SUBS * HALF, LMAX), BF16),
                pltpu.VMEM((LMAX, 4 * HEAD), BF16),
                pltpu.SemaphoreType.DMA((2, 4)),
            ],
        ),
        out_shape=[
            jax.ShapeDtypeStruct(shape, BF16),
            jax.ShapeDtypeStruct(shape, F32),
            jax.ShapeDtypeStruct((HEADS, HROWS, LMAX), BF16),
            jax.ShapeDtypeStruct(shape, BF16),
        ],
        input_output_aliases={11 + i: i for i in range(len(carry))},
        compiler_params=params(VMEM),
        cost_estimate=pl.CostEstimate(
            flops=2 * HEADS * HROWS * LMAX * 4 * HEAD,
            bytes_accessed=HEADS * (2 * HROWS * LMAX + 5 * HROWS * 256),
            transcendentals=HEADS * HROWS * LMAX // 2,
        ),
        name="mix",
    )(sc, *shards, v_own, v_far, *carry)


def row_valid(sc, step):
    line = lax.broadcasted_iota(jnp.int32, (4 * SPAN, 1), 0)
    item = line // SPAN
    row = step * SPAN + line % SPAN
    low = jnp.where(item == 0, sc[LENGTHS], sc[LENGTHS + 1])
    high = jnp.where(item == 2, sc[LENGTHS + 2], sc[LENGTHS + 3])
    return 128 * (row // HALF) + HALF * sc[CORE] + row % HALF < jnp.where(item >= 2, high, low)


def four_items(own, far):
    return jnp.concatenate([own[:, :, 0], far[...]], axis=0).reshape(4 * SPAN, WIDTH)


def pre_kernel(sc, tok, tok_far, cot, cot_far, heads, wo_own, wo_far, gain, mixed, resid, normed, grad, weight):
    step = pl.program_id(0)
    whole_weight(sc, step, wo_own, wo_far, weight)
    for item in range(4):
        lanes = slice(item * HEAD, (item + 1) * HEAD)
        for pair in range(HEADS // 2):
            both = jnp.concatenate([heads[2 * pair, :, lanes], heads[2 * pair + 1, :, lanes]], axis=1)
            mixed[item, :, pair * 128 : (pair + 1) * 128] = both
    res = four_items(tok, tok_far).astype(F32) + dot(mixed[...].reshape(4 * SPAN, WIDTH), weight[...], 1, 0)
    resid[...] = res.astype(BF16).reshape(4, SPAN, WIDTH)
    scale = lax.rsqrt(jnp.mean(res * res, axis=-1, keepdims=True) + EPSILON)
    valid = row_valid(sc, step)
    normed[...] = jnp.where(valid, res * scale * gain[...], 0.0).astype(BF16).reshape(4, SPAN, WIDTH)
    masked = jnp.where(valid, four_items(cot, cot_far).astype(F32), 0.0)
    grad[...] = masked.astype(BF16).reshape(4, SPAN, WIDTH)


def slab_spec(items=4):
    return spec((items, SPAN, WIDTH), lambda r, s: (0, r, 0))


def half_specs():
    return [
        spec((2, SPAN // HALF, 1, HALF, WIDTH), lambda r, s: (0, r, s[CORE], 0, 0)),
        spec((2, SPAN // HALF, HALF, WIDTH), lambda r, s: (0, r, 0, 0)),
    ]


def heads_spec():
    return spec((HEADS, SPAN, 4 * HEAD), lambda r, s: (0, r, 0))


def run_pre(sc, tokens, tokens_far, cotangent, cotangent_far, heads, wo, gain):
    return pl.pallas_call(
        pre_kernel,
        grid_spec=pltpu.PrefetchScalarGridSpec(
            num_scalar_prefetch=1,
            grid=(HROWS // SPAN,),
            in_specs=half_specs()
            + half_specs()
            + [heads_spec(), held((WIDTH, SIDE)), held((WIDTH, SIDE)), held((1, WIDTH))],
            out_specs=[slab_spec()] * 4,
            scratch_shapes=[pltpu.VMEM((WIDTH, WIDTH), BF16)],
        ),
        out_shape=[
            jax.ShapeDtypeStruct((4, HROWS, WIDTH), BF16),
            jax.ShapeDtypeStruct((4, HROWS, WIDTH), BF16),
            jax.ShapeDtypeStruct((4, HROWS, WIDTH), BF16),
            jax.ShapeDtypeStruct((4, HROWS, WIDTH), BF16),
        ],
        compiler_params=params(VMEM),
        cost_estimate=pl.CostEstimate(
            flops=2 * ROWS * WIDTH * WIDTH, bytes_accessed=16 * ROWS * WIDTH, transcendentals=0
        ),
        name="pre",
    )(sc, tokens, tokens_far, cotangent, cotangent_far, heads, *wo, gain)


def own_lanes(sc):
    return pl.ds(pl.multiple_of(sc[CORE] * SIDE, 128), SIDE)


def far_lanes(sc):
    return pl.ds(pl.multiple_of((1 - sc[CORE]) * SIDE, 128), SIDE)


def unit_rows(f, sc):
    return (lax.rem(FSIDE * sc[CORE] + f, 2 * FSIDE), 0)


def unit_columns(f, sc):
    return (0, lax.rem(FSIDE * sc[CORE] + f, 2 * FSIDE))


def early(f, sc):
    return (0, lax.min(f, FSIDE - 1))


def late(f, sc):
    return (0, lax.max(f - FSIDE, 0))


def units_kernel(sc, normed, cot, up_own, up_far, dn_own, dn_far, active, up_grad, back, w_up, w_down, total):
    step = pl.program_id(0)
    w_down[:, own_lanes(sc)] = dn_own[...]
    w_down[:, far_lanes(sc)] = dn_far[...]

    @pl.when(step < FSIDE)
    def _():
        w_up[...] = up_own[...]

    @pl.when(step >= FSIDE)
    def _():
        w_up[...] = up_far[...]

    for piece in range(ROWS // TILE):
        whole = slice(piece * TILE, (piece + 1) * TILE)
        for row in range(piece * TILE, (piece + 1) * TILE, 256):
            rows = slice(row, row + 256)
            for column in range(0, FSTEP, 256):
                columns = slice(column, column + 256)
                up = dot(normed[rows], w_up[:, columns], 1, 0)
                square = up * up
                bend = jnp.tanh(up * (0.7978845608028654 + (0.044715 * 0.7978845608028654) * square))
                share = 0.5 + 0.5 * bend
                act = up * share
                active[rows, columns] = act.astype(BF16)
                slope = share + act * (1.0 - share) * (
                    2 * 0.7978845608028654 + (6 * 0.044715 * 0.7978845608028654) * square
                )
                up_grad[rows, columns] = (dot(cot[rows], w_down[columns], 1, 1) * slope).astype(BF16)
        two_grad = dot(up_grad[whole], w_up[...], 1, 1)

        @pl.when(step == 0)
        def _():
            total[whole] = two_grad

        @pl.when((step > 0) & (step < 2 * FSIDE - 1))
        def _():
            total[whole] += two_grad

        @pl.when(step == 2 * FSIDE - 1)
        def _():
            back[whole] = (total[whole] + two_grad).astype(BF16)


def run_units(sc, normed, cotangent, up, down):
    return pl.pallas_call(
        units_kernel,
        grid_spec=pltpu.PrefetchScalarGridSpec(
            num_scalar_prefetch=1,
            grid=(2 * FSIDE,),
            in_specs=[
                held((ROWS, WIDTH)),
                held((ROWS, WIDTH)),
                spec((WIDTH, FSTEP), early),
                spec((WIDTH, FSTEP), late),
                spec((FSTEP, SIDE), unit_rows),
                spec((FSTEP, SIDE), unit_rows),
            ],
            out_specs=[spec((ROWS, FSTEP), unit_columns), spec((ROWS, FSTEP), unit_columns), held((ROWS, WIDTH))],
            scratch_shapes=[
                pltpu.VMEM((WIDTH, FSTEP), BF16),
                pltpu.VMEM((FSTEP, WIDTH), BF16),
                pltpu.VMEM((ROWS, WIDTH), F32),
            ],
        ),
        out_shape=[
            jax.ShapeDtypeStruct((ROWS, FF), BF16),
            jax.ShapeDtypeStruct((ROWS, FF), BF16),
            jax.ShapeDtypeStruct((ROWS, WIDTH), BF16),
        ],
        compiler_params=params(VMEM),
        cost_estimate=pl.CostEstimate(
            flops=6 * ROWS * WIDTH * FF, bytes_accessed=8 * ROWS * WIDTH + 4 * ROWS * FF, transcendentals=ROWS * FF
        ),
        name="units",
    )(sc, normed.reshape(ROWS, WIDTH), cotangent.reshape(ROWS, WIDTH), *up, *down)


def down_grad_kernel(sc, active, cot, own, far, total):
    total[...] = dot(active[...], cot[...], 0, 0).astype(BF16)
    own[...] = total[:, own_lanes(sc)]
    far[...] = total[:, far_lanes(sc)]


def run_down_grad(sc, active, cotangent):
    return pl.pallas_call(
        down_grad_kernel,
        grid_spec=pltpu.PrefetchScalarGridSpec(
            num_scalar_prefetch=1,
            grid=(FF // 512,),
            in_specs=[spec((ROWS, 512), lambda f, s: (0, f)), held((ROWS, WIDTH))],
            out_specs=[spec((512, SIDE), lambda f, s: (f, 0))] * 2,
            scratch_shapes=[pltpu.VMEM((512, WIDTH), BF16)],
        ),
        out_shape=[jax.ShapeDtypeStruct((FF, SIDE), BF16)] * 2,
        compiler_params=params(LESS),
        cost_estimate=pl.CostEstimate(
            flops=2 * ROWS * WIDTH * FF, bytes_accessed=2 * ROWS * (WIDTH + FF), transcendentals=0
        ),
        name="down_grad",
    )(sc, active, cotangent.reshape(ROWS, WIDTH))


def up_grad_kernel(sc, normed, up_grad, own, far):
    total = dot(normed[...], up_grad[...], 0, 0).astype(BF16)

    @pl.when(pl.program_id(0) < 3)
    def _():
        own[...] = total

    @pl.when(pl.program_id(0) >= 3)
    def _():
        far[...] = total


def run_up_grad(sc, normed, up_grad):
    return pl.pallas_call(
        up_grad_kernel,
        grid_spec=pltpu.PrefetchScalarGridSpec(
            num_scalar_prefetch=1,
            grid=(6,),
            in_specs=[held((ROWS, WIDTH)), spec((ROWS, 512), lambda f, s: (0, lax.rem(3 * s[CORE] + f, 6)))],
            out_specs=[
                spec((WIDTH, 512), lambda f, s: (0, lax.min(f, 2))),
                spec((WIDTH, 512), lambda f, s: (0, lax.max(f - 3, 0))),
            ],
        ),
        out_shape=[jax.ShapeDtypeStruct((WIDTH, FF // 2), BF16)] * 2,
        compiler_params=params(LESS),
        cost_estimate=pl.CostEstimate(
            flops=2 * ROWS * WIDTH * FF, bytes_accessed=2 * ROWS * (WIDTH + FF), transcendentals=0
        ),
        name="up_grad",
    )(sc, normed.reshape(ROWS, WIDTH), up_grad)


def out_grad_kernel(sc, mixed, res_own, res_far, own, far, total):
    step = pl.program_id(0)
    grad = jnp.concatenate([res_own[...], res_far[...]], axis=0).reshape(4 * SPAN, WIDTH)
    found = dot(mixed[...].reshape(4 * SPAN, WIDTH), grad, 0, 0)

    @pl.when(step == 0)
    def _():
        total[...] = found

    @pl.when(step > 0)
    def _():
        total[...] += found

    @pl.when(step == pl.num_programs(0) - 1)
    def _():
        own[...] = total[:, own_lanes(sc)].astype(BF16)
        far[...] = total[:, far_lanes(sc)].astype(BF16)


def run_out_grad(sc, mixed, res_own, res_far):
    return pl.pallas_call(
        out_grad_kernel,
        grid_spec=pltpu.PrefetchScalarGridSpec(
            num_scalar_prefetch=1,
            grid=(HROWS // SPAN,),
            in_specs=[slab_spec(), slab_spec(2), slab_spec(2)],
            out_specs=[held((WIDTH, SIDE))] * 2,
            scratch_shapes=[pltpu.VMEM((WIDTH, WIDTH), F32)],
        ),
        out_shape=[jax.ShapeDtypeStruct((WIDTH, SIDE), BF16)] * 2,
        compiler_params=params(LESS),
        cost_estimate=pl.CostEstimate(
            flops=2 * ROWS * WIDTH * WIDTH, bytes_accessed=4 * ROWS * WIDTH, transcendentals=0
        ),
        name="out_grad",
    )(sc, mixed, res_own, res_far)


def out_kernel(sc, active, resid, dn_own, dn_far, own, far, w_down):
    step = pl.program_id(0)

    @pl.when(step == 0)
    def _():
        w_down[:, own_lanes(sc)] = dn_own[...]
        w_down[:, far_lanes(sc)] = dn_far[...]

    branch = dot(active[...].reshape(4 * SPAN, FF), w_down[...], 1, 0)
    output = jnp.where(row_valid(sc, step), resid[...].reshape(4 * SPAN, WIDTH).astype(F32) + branch, 0.0)
    output = output.astype(BF16).reshape(4, SPAN, WIDTH)
    own[...] = output[:2]
    far[...] = output[2:]


def run_out(sc, active, resid, down):
    return pl.pallas_call(
        out_kernel,
        grid_spec=pltpu.PrefetchScalarGridSpec(
            num_scalar_prefetch=1,
            grid=(HROWS // SPAN,),
            in_specs=[
                spec((4, SPAN, FF), lambda r, s: (0, r, 0)),
                slab_spec(),
                held((FF, SIDE)),
                held((FF, SIDE)),
            ],
            out_specs=[slab_spec(2)] * 2,
            scratch_shapes=[pltpu.VMEM((FF, WIDTH), BF16)],
        ),
        out_shape=[
            jax.ShapeDtypeStruct((2, HROWS, WIDTH), BF16),
            jax.ShapeDtypeStruct((2, HROWS, WIDTH), BF16),
        ],
        compiler_params=params(LESS),
        cost_estimate=pl.CostEstimate(
            flops=2 * ROWS * WIDTH * FF, bytes_accessed=ROWS * (2 * FF + 7 * WIDTH), transcendentals=0
        ),
        name="out",
    )(sc, active.reshape(4, HROWS, FF), resid, *down)


def post_kernel(sc, resid, back, cot, wo_own, wo_far, gain, *refs):
    (res_own, res_far, heads, d_gain, weight, spread) = refs
    step = pl.program_id(0)
    whole_weight(sc, step, wo_own, wo_far, weight)
    shape, slab = (4 * SPAN, WIDTH), (4, SPAN, WIDTH)
    valid = row_valid(sc, step)
    res = resid[...].reshape(shape).astype(F32)
    scale = lax.rsqrt(jnp.mean(res * res, axis=-1, keepdims=True) + EPSILON)
    unit = res * scale
    two_grad = jnp.where(valid, back[...].reshape(shape).astype(F32), 0.0)
    gained = two_grad * gain[...]
    masked = cot[...].reshape(shape).astype(F32)
    grad = masked + scale * (gained - unit * jnp.mean(gained * unit, axis=-1, keepdims=True))
    low = grad.astype(BF16)
    res_own[...] = low.reshape(slab)[:2]
    res_far[...] = low.reshape(slab)[2:]
    gain_sum = jnp.sum(two_grad * unit, axis=0, keepdims=True)

    @pl.when(step == 0)
    def _():
        d_gain[...] = gain_sum

    @pl.when(step > 0)
    def _():
        d_gain[...] += gain_sum

    spread[...] = dot(low, weight[...], 1, 1).astype(BF16).reshape(slab)
    for pair in range(HEADS // 2):
        lanes = slice(pair * 128, (pair + 1) * 128)
        for side in range(2):
            one, two = spread[2 * side, :, lanes], spread[2 * side + 1, :, lanes]
            half = slice(side * 128, (side + 1) * 128)
            heads[2 * pair, :, half] = jnp.concatenate([one[:, :HEAD], two[:, :HEAD]], axis=1)
            heads[2 * pair + 1, :, half] = jnp.concatenate([one[:, HEAD:], two[:, HEAD:]], axis=1)


def run_post(sc, resid, back, cotangent, wo, gain):
    whole = (4, HROWS, WIDTH)
    return pl.pallas_call(
        post_kernel,
        grid_spec=pltpu.PrefetchScalarGridSpec(
            num_scalar_prefetch=1,
            grid=(HROWS // SPAN,),
            in_specs=[slab_spec()] * 3 + [held((WIDTH, SIDE)), held((WIDTH, SIDE)), held((1, WIDTH))],
            out_specs=[slab_spec(2)] * 2 + [heads_spec(), held((1, WIDTH))],
            scratch_shapes=[
                pltpu.VMEM((WIDTH, WIDTH), BF16),
                pltpu.VMEM((4, SPAN, WIDTH), BF16),
            ],
        ),
        out_shape=[
            jax.ShapeDtypeStruct((2, HROWS, WIDTH), BF16),
            jax.ShapeDtypeStruct((2, HROWS, WIDTH), BF16),
            jax.ShapeDtypeStruct((HEADS, HROWS, 4 * HEAD), BF16),
            jax.ShapeDtypeStruct((1, WIDTH), F32),
        ],
        compiler_params=params(VMEM),
        cost_estimate=pl.CostEstimate(
            flops=4 * ROWS * WIDTH * WIDTH, bytes_accessed=28 * ROWS * WIDTH, transcendentals=0
        ),
        name="post",
    )(sc, resid, back.reshape(whole), cotangent, *wo, gain)


def unmix_kernel(carried, sc, v_own, v_far, grad_heads, mean, exps, inverse, *refs):
    refs = refs[2:] if carried else refs
    outs, (own, far, grads, mask, adder, bound, out_sems) = refs[:8], refs[8:]
    place = sc[PLACE]
    step = pl.program_id(0)

    def leave(slot):
        return [
            pltpu.make_async_copy(
                grads.at[slot, pl.ds(pl.multiple_of((place ^ rel) * SUBS * HALF, SUBS * HALF), SUBS * HALF)],
                outs[4 * slot + rel],
                out_sems.at[slot, rel],
            )
            for rel in range(4)
        ]

    fill_mask(sc, mask)

    @pl.when(step == 0)
    def _():
        lane = lax.broadcasted_iota(jnp.int32, (4 * HEAD, 128), 0) // HEAD
        column = lax.broadcasted_iota(jnp.int32, (4 * HEAD, 128), 1)
        adder[...] = jnp.where((lane == column) | (lane + 4 == column), -1.0, 0.0).astype(BF16)
        row = lax.broadcasted_iota(jnp.int32, (LMAX, 128), 0)
        item = lax.broadcasted_iota(jnp.int32, (LMAX, 128), 1)
        length = jnp.where(item % 4 == 0, sc[LENGTHS], sc[LENGTHS + 1])
        length = jnp.where(item % 4 == 2, sc[LENGTHS + 2], length)
        length = jnp.where(item % 4 == 3, sc[LENGTHS + 3], length)
        bound[...] = jnp.where((item < 8) & (row < length), 1.0, 0.0).astype(BF16)

    high_lanes = lax.broadcasted_iota(jnp.int32, (HROWS, 128), 1) < 4
    for head in range(PHEADS):
        weights = exps[head]
        low = (grad_heads[head].astype(F32) * inverse[head].astype(F32)).astype(BF16)
        product = low.astype(F32) * mean[head]
        coarse = product.astype(BF16)
        fine = (product - coarse.astype(F32)).astype(BF16)
        delta = dot(coarse, adder[...], 1, 0) + dot(fine, adder[...], 1, 0)
        coarse = delta.astype(BF16)
        fine = (delta - coarse.astype(F32)).astype(BF16)
        left = jnp.concatenate([low, jnp.where(high_lanes, coarse, fine)], axis=1)
        score = dot(left, jnp.concatenate([v_own[head], v_far[head], bound[...]], axis=1), 1, 1)
        grads[step, head_rows(head)] = (score * weights.astype(F32)).astype(BF16)
        back = (dot(weights, low, 0, 0) * mask[...].astype(F32)).astype(BF16)
        own[head] = back[:, : 2 * HEAD]
        far[head] = back[:, 2 * HEAD :]
    for which in range(2):

        @pl.when(step == which)
        def _():
            for copy in leave(which):
                copy.start()
            if which == 1:
                for copy in leave(0) + leave(1):
                    copy.wait()


def run_unmix(sc, planes, v_own, v_far, grad_heads, mean, exps, inverse, carry):
    carry = list(carry)
    return pl.pallas_call(
        partial(unmix_kernel, bool(carry)),
        grid_spec=pltpu.PrefetchScalarGridSpec(
            num_scalar_prefetch=1,
            grid=(2,),
            in_specs=[
                plane_spec(planes, LMAX, 2 * HEAD),
                plane_spec(planes, LMAX, 2 * HEAD),
                plane_spec(planes, HROWS, 4 * HEAD),
                plane_spec(planes, HROWS, 4 * HEAD),
                plane_spec(planes, HROWS, LMAX),
                plane_spec(planes, HROWS, 4 * HEAD),
            ]
            + anywhere(len(carry)),
            out_specs=anywhere(8) + [plane_spec(planes, LMAX, 2 * HEAD)] * 2,
            scratch_shapes=[
                pltpu.VMEM((2, 4 * SUBS * HALF, LMAX), BF16),
                pltpu.VMEM((LMAX, 4 * HEAD), BF16),
                pltpu.VMEM((4 * HEAD, 128), BF16),
                pltpu.VMEM((LMAX, 128), BF16),
                pltpu.SemaphoreType.DMA((2, 4)),
            ],
        ),
        out_shape=[jax.ShapeDtypeStruct((SUBS * HALF, LMAX), BF16)] * 8
        + [jax.ShapeDtypeStruct((HEADS, LMAX, 2 * HEAD), BF16)] * 2,
        input_output_aliases={7 + i: 8 + i for i in range(len(carry))},
        compiler_params=params(VMEM),
        cost_estimate=pl.CostEstimate(
            flops=3 * HEADS * HROWS * LMAX * 4 * HEAD,
            bytes_accessed=HEADS * (2 * HROWS * LMAX + 5 * HROWS * 256 + 4 * LMAX * 256),
            transcendentals=0,
        ),
        name="unmix",
    )(sc, v_own, v_far, grad_heads, mean, exps, inverse, *carry)


def close_kernel(sc, tok, res_own, res_got, out_own, out_got, own, far, gain, w_own, w_far, *refs):
    (output, tok_grad, d_value, d_gain, total, weight) = refs
    step = pl.program_id(0)
    whole_weight(sc, step, w_own, w_far, weight)
    core = sc[CORE]
    output[:, :, core] = out_own[...].astype(F32)
    output[:, :, 1 - core] = out_got[...].astype(F32)
    tok_grad[:, :, core] = res_own[...].astype(F32)
    tok_grad[:, :, 1 - core] = res_got[...].astype(F32)
    runs = tok.shape[1]
    rows = runs * 128
    for item in range(2):
        lanes = slice(item * HEAD, (item + 1) * HEAD)
        pieces = [
            add_low(own[head, :, lanes], far[head, :, lanes]) for head in range(HEADS)
        ]
        back = jnp.concatenate(pieces, axis=1)
        x = tok[item].reshape(rows, WIDTH).astype(F32)
        scale = lax.rsqrt(jnp.mean(x * x, axis=-1, keepdims=True) + EPSILON)
        unit = x * scale
        normed = (unit * gain[...]).astype(BF16)
        normed_grad = dot(back, weight[...], 1, 1)
        gained = normed_grad * gain[...]
        update = scale * (gained - unit * jnp.mean(gained * unit, axis=-1, keepdims=True))
        tok_grad[item] += update.reshape(runs, 2, HALF, WIDTH)
        gain_sum = jnp.sum(normed_grad * unit, axis=0, keepdims=True)
        value_sum = dot(normed, back, 0, 0)
        if item == 0:
            gain_total, value_total = gain_sum, value_sum
        else:
            gain_total, value_total = gain_total + gain_sum, value_total + value_sum

    @pl.when(step == 0)
    def _():
        d_gain[...] = gain_total
        total[...] = value_total

    @pl.when(step > 0)
    def _():
        d_gain[...] += gain_total
        total[...] += value_total

    @pl.when(step == pl.num_programs(0) - 1)
    def _():
        low = total[...].astype(BF16)
        d_value[0] = low[:, :SIDE]
        d_value[1] = low[:, SIDE:]


def run_close(sc, tokens, res_own, res_got, out_own, out_got, own, far, gain, w_own, w_far):
    runs = 2
    slab = (2, RUNS, 2, HALF, WIDTH)
    half = (2, RUNS, HALF, WIDTH)
    whole_spec = spec((2, runs, 2, HALF, WIDTH), lambda j, s: (0, j, 0, 0, 0))
    half_spec = spec((2, runs, HALF, WIDTH), lambda j, s: (0, j, 0, 0))
    back_spec = spec((HEADS, runs * 128, 2 * HEAD), lambda j, s: (0, j, 0))
    return pl.pallas_call(
        close_kernel,
        grid_spec=pltpu.PrefetchScalarGridSpec(
            num_scalar_prefetch=1,
            grid=(RUNS // runs,),
            in_specs=[whole_spec]
            + [half_spec] * 4
            + [back_spec, back_spec, held((1, WIDTH)), held((WIDTH, SIDE)), held((WIDTH, SIDE))],
            out_specs=[whole_spec, whole_spec, held((2, WIDTH, SIDE)), held((1, WIDTH))],
            scratch_shapes=[pltpu.VMEM((WIDTH, WIDTH), F32), pltpu.VMEM((WIDTH, WIDTH), BF16)],
        ),
        out_shape=[
            jax.ShapeDtypeStruct(slab, F32),
            jax.ShapeDtypeStruct(slab, F32),
            jax.ShapeDtypeStruct((2, WIDTH, SIDE), BF16),
            jax.ShapeDtypeStruct((1, WIDTH), F32),
        ],
        compiler_params=params(LESS),
        cost_estimate=pl.CostEstimate(
            flops=4 * 2 * LMAX * WIDTH * WIDTH, bytes_accessed=38 * LMAX * WIDTH, transcendentals=0
        ),
        name="close",
    )(
        sc,
        tokens.reshape(slab),
        *(x.reshape(half) for x in (res_own, res_got, out_own, out_got)),
        own,
        far,
        gain,
        w_own,
        w_far,
    )


PACK_DOWN, PACK_UP, PACK_OUT, PACK_VALUE, PACK_GAIN, PACK = 0, 192, 384, 432, 480, 496


def pack_kernel(sc, down, up, out, value, gain, down_far, up_far, out_far, value_far, gain_far, packed):
    first = sc[CORE] == 0

    def both(own, far, lanes):
        own, far = own[:, lanes], far[:, lanes]
        return jnp.concatenate([jnp.where(first, own, far), jnp.where(first, far, own)], axis=0)

    def side(own, far):
        return both(own, far, own_lanes(sc))

    packed[PACK_DOWN:PACK_UP] = side(down, down_far)
    for j in range(4):
        lanes = pl.ds(pl.multiple_of((4 * sc[CORE] + j) * SIDE, 128), SIDE)
        packed[PACK_UP + 48 * j : PACK_UP + 48 * (j + 1)] = both(up, up_far, lanes)
    packed[PACK_OUT:PACK_VALUE] = side(out, out_far)
    packed[PACK_VALUE:PACK_GAIN] = side(value, value_far)
    packed[PACK_GAIN:] = both(gain, gain_far, slice(0, SIDE))


def run_pack(sc, own, far):
    return pl.pallas_call(
        pack_kernel,
        grid_spec=pltpu.PrefetchScalarGridSpec(
            num_scalar_prefetch=1,
            grid=(1,),
            in_specs=[held(x.shape) for x in (*own, *far)],
            out_specs=held((PACK, SIDE)),
        ),
        out_shape=jax.ShapeDtypeStruct((PACK, SIDE), BF16),
        compiler_params=params(VMEM),
        cost_estimate=pl.CostEstimate(flops=0, bytes_accessed=6 * PACK * SIDE, transcendentals=0),
        name="pack",
    )(sc, *own, *far)


def chip_of(sc, k, rel):
    return plane_of(k, sc) * 4 + (sc[PLACE] ^ rel)


def place_kernel(moves, sc, *refs):
    pieces, targets, sems = refs[:16], refs[16:-1], refs[-1]
    copies = []
    for index, piece in enumerate(pieces):
        chip = chip_of(sc, index // 4, index % 4)
        for which, (start, count, lane, target, step, offset, column) in enumerate(moves):
            rows = pl.ds(pl.multiple_of(chip * step + offset, 16), count)
            copies.append(
                pltpu.make_async_copy(
                    piece.at[pl.ds(start, count), pl.ds(lane, SIDE)],
                    targets[target].at[rows, pl.ds(column, SIDE)],
                    sems.at[index, which],
                )
            )
    for copy in copies:
        copy.start()
    for copy in copies:
        copy.wait()


def run_place(sc, pieces, moves, shapes):
    return pl.pallas_call(
        partial(place_kernel, moves),
        grid_spec=pltpu.PrefetchScalarGridSpec(
            num_scalar_prefetch=1,
            grid=(1,),
            in_specs=anywhere(16),
            out_specs=[held(shape) for shape in shapes],
            scratch_shapes=[pltpu.SemaphoreType.DMA((16, len(moves)))],
        ),
        out_shape=[jax.ShapeDtypeStruct(shape, BF16) for shape in shapes],
        compiler_params=params(VMEM),
        cost_estimate=pl.CostEstimate(
            flops=0, bytes_accessed=4 * sum(a * b for a, b in shapes), transcendentals=0
        ),
        name="place",
    )(sc, *pieces)


def place_weights(sc, pieces):
    moves = (
        (PACK_DOWN, 192, 0, 0, 192, 0, 0),
        *((PACK_UP + 48 * j, 48, 0, 1, 48, 0, j * SIDE) for j in range(4)),
        (PACK_OUT, 48, 0, 2, 48, 0, 0),
        (PACK_VALUE, 48, 0, 3, 48, 0, 0),
        (PACK_GAIN, 16, 0, 4, 16, 0, 0),
    )
    shapes = [(FF, SIDE), (WIDTH, FF // 2), (WIDTH, SIDE), (WIDTH, SIDE), (256, SIDE)]
    return run_place(sc, pieces, moves, shapes)


def collect_kernel(sc, *refs):
    outs = refs[24:]
    for k in range(PLANES):

        @pl.when(pl.program_id(0) == k)
        def _():
            for rel in range(4):
                down, down_got, up, up_got, out, out_got = refs[6 * rel : 6 * rel + 6]
                packed = outs[4 * k + rel]
                packed[PACK_DOWN:PACK_UP] = add_low(down[...], down_got[...])
                for j in range(4):
                    lanes = slice(j * SIDE, (j + 1) * SIDE)
                    packed[PACK_UP + 48 * j : PACK_UP + 48 * (j + 1)] = add_low(up[:, lanes], up_got[:, lanes])
                packed[PACK_OUT:PACK_VALUE] = add_low(out[...], out_got[...])


def run_collect(sc, *sides):
    def rows(x, rel):
        return spec((x.shape[0] // 16, x.shape[1]), lambda k, s: (chip_of(s, k, rel), 0))

    return pl.pallas_call(
        collect_kernel,
        grid_spec=pltpu.PrefetchScalarGridSpec(
            num_scalar_prefetch=1,
            grid=(PLANES,),
            in_specs=[rows(x, rel) for rel in range(4) for x in sides],
            out_specs=[held((PACK_VALUE, SIDE))] * 16,
        ),
        out_shape=[jax.ShapeDtypeStruct((PACK_VALUE, SIDE), BF16)] * 16,
        compiler_params=params(LESS),
        cost_estimate=pl.CostEstimate(flops=0, bytes_accessed=3 * 16 * PACK_VALUE * SIDE * 2, transcendentals=0),
        name="collect",
    )(sc, *(x for _ in range(4) for x in sides))


def add_kernel(groups, *refs):
    for group, total in zip(groups, refs[-len(groups) :]):
        value = refs[group[0]][...].astype(F32)
        for index in group[1:]:
            value = value + refs[index][...].astype(F32)
        total[...] = value.astype(total.dtype)


def run_add(groups, values, dtype):
    shape = values[0].shape
    here = pl.BlockSpec(memory_space=pltpu.VMEM)
    return pl.pallas_call(
        partial(add_kernel, groups),
        in_specs=[here] * len(values),
        out_specs=[here] * len(groups),
        out_shape=[jax.ShapeDtypeStruct(shape, dtype)] * len(groups),
        compiler_params=params(LESS),
        cost_estimate=pl.CostEstimate(
            flops=0, bytes_accessed=2 * shape[0] * shape[1] * (len(values) + len(groups)), transcendentals=0
        ),
        name="add",
    )(*values)


DEVICES = 32
TO_CORE, TO_X, TO_Y = 1, 2, 4


def swap(x, bit):
    return lax.ppermute(x, BOTH, [(d, d ^ bit) for d in range(DEVICES)])


def ring(x, way=1):
    return lax.ppermute(x, BOTH, [(d, (d + 8 * way) % DEVICES) for d in range(DEVICES)])


def pick(x, index, axis=0):
    return lax.dynamic_index_in_dim(x, index, axis, keepdims=False)


def ordered(flag, one, two, axis=0, joined=jnp.stack):
    return jnp.where(flag == 0, joined([one, two], axis), joined([two, one], axis))


def add_low(one, two):
    return (one.astype(F32) + two.astype(F32)).astype(BF16)


STEPS = (
    ((0, 0, 1), (0, 1, 0), (1, 0, 0)),
    ((1, 0, 1), (0, 1, 1), (2, 0, 0)),
    ((2, 0, 1), (1, 1, 0), (3, 0, 0)),
    ((3, 0, 1), (2, 1, 0), (1, 1, 1)),
    ((2, 1, 1), (3, 1, 1), (3, 1, 0)),
)


def gather_step(have, step):
    by_x, by_y, by_z = STEPS[step]
    return {
        **have,
        by_z: ring(have[by_z[0] - 1, by_z[1], by_z[2]]),
        by_x: swap(have[by_x[0], by_x[1], 0], TO_X),
        by_y: swap(have[by_y[0], 0, by_y[2]], TO_Y),
    }


def in_order(have):
    return [have[k, y, x] for k in range(4) for y in range(2) for x in range(2)]


def by_place(shares, planes=range(PLANES)):
    return {(k, i // 2, i % 2): shares[4 * at + i] for at, k in enumerate(planes) for i in range(4)}


def scatter_send(have, step):
    by_x, by_y, by_z = STEPS[len(STEPS) - 1 - step]
    got = (ring(have[by_z], -1), swap(have[by_x], TO_X), swap(have[by_y], TO_Y))
    return {at: value for at, value in have.items() if at not in (by_x, by_y, by_z)}, got


def scatter_add(have, got, step):
    by_x, by_y, by_z = STEPS[len(STEPS) - 1 - step]
    targets = ((by_z[0] - 1, by_z[1], by_z[2]), (by_x[0], by_x[1], 0), (by_y[0], 0, by_y[2]))
    sums = list(dict.fromkeys(targets))
    groups = [(len(got) + i, *(j for j in range(len(got)) if targets[j] == at)) for i, at in enumerate(sums)]
    values = [*got, *(have[at] for at in sums)]
    return {**have, **dict(zip(sums, run_add(groups, values, F32 if step == len(STEPS) - 1 else BF16)))}


together = lax.optimization_barrier


def chip_shards(tokens, lengths, rand_mix, w_value, w_out, w_up, w_down, gain_mix, gain_ffn, grad_out):
    wide = lax.axis_index("wide")
    core = lax.axis_index("narrow")
    z, y, x = wide // 4, (wide // 2) % 2, wide % 2
    other = lambda value: swap(value, TO_CORE)
    side = partial(ordered, core, joined=jnp.concatenate)
    slab = (2, RUNS, 2, HALF, WIDTH)
    tokens, grad_out = tokens.reshape(slab), grad_out.reshape(slab)

    gains = jnp.pad(jnp.concatenate([gain_mix, gain_ffn])[None], ((0, 7), (0, SIDE - 48)))
    own = (w_down, w_up, w_out, w_value, gains)
    far = tuple(other(value) for value in own)
    near_sc = jnp.concatenate([jnp.stack([core, z, wide % 4]).astype(jnp.int32), lengths, lengths])
    weights = {(0, 0, 0): run_pack(near_sc, own, far)}

    rand = rand_mix.reshape(3, 2, HALF, LMAX)
    blocks = side(pick(rand, core, 1), other(pick(rand, 1 - core, 1)), 0)
    weights, rands, late_tokens, late_grad = together(
        (gather_step(weights, 0), {(0, 0, 0): blocks.reshape(SUBS * HALF, LMAX)}, tokens, grad_out)
    )
    weights, tokens_far = together((gather_step(weights, 1), other(pick(late_tokens, 1 - core, 2))))
    weights, grad_far = together((gather_step(weights, 2), other(pick(late_grad, 1 - core, 2))))
    weights, far_lengths = together((gather_step(weights, 3), other(lengths)))
    sc = jnp.concatenate([near_sc[:5], far_lengths])
    weights, rands = together((gather_step(weights, 4), rands))

    rands = gather_step(rands, 0)
    down, up, out, value, gain_rows = place_weights(sc, in_order(weights))
    rands, value, value_far, gain_rows, out, down, up = together(
        (rands, value, other(value), gain_rows, out, down, up)
    )
    gain_rows = gain_rows.reshape(16, 2, 8, SIDE)[:, :, 0]
    gain_one = gain_rows[..., :24].reshape(1, WIDTH).astype(F32)
    gain_two = gain_rows[..., 24:48].reshape(1, WIDTH).astype(F32)
    rands = gather_step(rands, 1)
    v_own = run_values(sc, tokens.reshape(2, LMAX, WIDTH), gain_one, value, value_far)
    rands, v_own, out, down, up = together((rands, v_own, (out, other(out)), down, up))
    rands, v_own, v_far, down, up = together((gather_step(rands, 2), v_own, other(v_own), down, up))
    rands, v_far, down, up = together((gather_step(rands, 3), v_far, down, up))
    near = [rands[k, y_at, x_at] for k in range(2) for y_at in range(2) for x_at in range(2)]
    rands = gather_step(rands, 4)
    mixing = run_mix(sc, (0, 1), near, v_own, v_far, ())
    rands, down, up, mixing = together((rands, down, up, mixing))
    heads, mean, exps, inverse = run_mix(sc, (2, 3), in_order(rands)[8:], v_own, v_far, mixing)
    down, up = (down, other(down)), (up, other(up))

    mixed, resid, normed, masked = run_pre(sc, tokens, tokens_far, grad_out, grad_far, heads, out, gain_two)
    active, up_grad, back = run_units(sc, normed, masked, up, down)
    res_own, res_far, grad_heads, d_gain_two = run_post(sc, resid, back, masked, out, gain_two)

    backward = lambda planes, carry: run_unmix(sc, planes, v_own, v_far, grad_heads, mean, exps, inverse, carry)
    *far, back_own, back_far = backward((3, 2), ())
    far, back_own, back_far, res_got = together((far, back_own, back_far, other(res_far)))
    have, got = scatter_send(by_place(far, (3, 2)), 0)
    *near, back_own, back_far = backward((1, 0), (back_own, back_far))
    have, got, near, back_own, back_far = together((have, got, near, back_own, back_far))
    have = {**scatter_add(have, got, 0), **by_place(near, (1, 0))}

    have, got = scatter_send(have, 1)
    up_own, up_far = run_up_grad(sc, normed, up_grad)
    have, got, up_own, up_far, back_got = together((have, got, up_own, up_far, other(back_far)))
    have = scatter_add(have, got, 1)

    have, got = scatter_send(have, 2)
    down_own, down_far = run_down_grad(sc, active, masked)
    have, got, down_own, down_far, up_got = together((have, got, down_own, down_far, other(up_far)))
    have = scatter_add(have, got, 2)

    have, got = scatter_send(have, 3)
    d_out_own, d_out_far = run_out_grad(sc, mixed, res_own, res_far)
    packed = run_collect(sc, down_own, other(down_far), up_own, up_got, d_out_own, other(d_out_far))
    have, got, packed = together((have, got, packed))
    have = scatter_add(have, got, 3)

    have, got = scatter_send(have, 4)
    sums, sums_got = scatter_send(by_place(packed), 0)
    out_own, out_far = run_out(sc, active, resid, down)
    have, got, sums, sums_got, out_own, out_far = together((have, got, sums, sums_got, out_own, out_far))
    rand_sum = scatter_add(have, got, 4)[0, 0, 0].reshape(2, 3, HALF, LMAX)

    sums, got = scatter_send(scatter_add(sums, sums_got, 0), 1)
    output, tokens_grad, d_value, d_gain_one = run_close(
        sc, tokens, res_own, res_got, out_own, other(out_far), back_own, back_got, gain_one, value, value_far
    )
    sums, got, output, tokens_grad, d_value, d_gain_one = together(
        (sums, got, output, tokens_grad, d_value, d_gain_one)
    )
    sums = scatter_add(sums, got, 1)

    sums, got = scatter_send(sums, 2)
    gain_pair = jnp.concatenate([d_gain_one, d_gain_two]).reshape(2, 16, 1, 48).astype(BF16)
    gain_pair = jnp.pad(gain_pair, ((0, 0), (0, 0), (0, 15), (0, SIDE - 48)))
    small = jnp.concatenate([d_value.reshape(2, 16, 48, SIDE), gain_pair], 2)
    small = add_low(pick(small, core), other(pick(small, 1 - core))).reshape(4, 2, 2, 64, SIDE)
    small = add_low(pick(small, x, 2), swap(pick(small, 1 - x, 2), TO_X))
    sums, got, small = together((sums, got, small))
    sums = scatter_add(sums, got, 2)

    sums, got = scatter_send(sums, 3)
    small = add_low(pick(small, y, 1), swap(pick(small, 1 - y, 1), TO_Y))
    blocks, blocks_far = pick(rand_sum, core), other(pick(rand_sum, 1 - core))
    sums, got, small, blocks, blocks_far = together((sums, got, small, blocks, blocks_far))
    sums = scatter_add(sums, got, 3)

    sums, got = scatter_send(sums, 4)
    small_sum = pick(small, z).astype(F32)
    for k in range(1, PLANES):
        small_sum = small_sum + ring(pick(small, lax.rem(z + PLANES - k, PLANES)), -k).astype(F32)
    sums, got, small_sum = together((sums, got, small_sum))
    big_sum = scatter_add(sums, got, 4)[0, 0, 0]
    big_far, small_far = other(big_sum), other(small_sum)

    rows_of = lambda value, rows: pick(value.reshape(-1, 2, rows, SIDE), core, 1)
    mine = lambda own, far, rows: side(rows_of(own, rows)[0], rows_of(far, rows)[0], 1)
    down_shard = mine(big_sum[PACK_DOWN:PACK_UP], big_far[PACK_DOWN:PACK_UP], 96)
    up_side = lambda value: rows_of(value[PACK_UP:PACK_OUT], 24).transpose(1, 0, 2).reshape(24, 4 * SIDE)
    up_shard = side(up_side(big_sum), up_side(big_far), 1)
    outproj_shard = mine(big_sum[PACK_OUT:PACK_VALUE], big_far[PACK_OUT:PACK_VALUE], 24)
    value_shard = mine(small_sum[:48], small_far[:48], 24)
    gains_pair = ordered(core, small_sum[48, :48], small_far[48, :48])
    gain_pair = pick(gains_pair.reshape(2, 2, 24), core, 1)

    rand_shard = ordered(core, blocks, blocks_far, 1)

    return (
        output.reshape(2, LMAX, WIDTH),
        tokens_grad.reshape(2, LMAX, WIDTH),
        rand_shard.reshape(3 * 128, LMAX),
        value_shard,
        outproj_shard,
        up_shard,
        down_shard,
        gain_pair[0],
        gain_pair[1],
    )


def rms_norm(values, gain):
    scale = lax.rsqrt(jnp.mean(values * values, axis=-1, keepdims=True) + EPSILON)
    return values * scale * gain


def split_heads(block):
    return block.reshape(LMAX, HEADS, HEAD).transpose(1, 0, 2)


def merge_heads(block):
    return block.transpose(1, 0, 2).reshape(LMAX, HEADS * HEAD)


def masked_scores(key_mask, rand_head):
    return jnp.where(key_mask[None, :] > 0, rand_head.astype(jnp.float32), -1e30)


def head_forward(key_mask, paired):
    rand_head, value_head = paired
    scores = masked_scores(key_mask, rand_head)
    row_peak = jnp.max(scores, axis=-1, keepdims=True)
    exponent = jnp.exp(scores - row_peak)
    denom_sum = jnp.sum(exponent, axis=-1, keepdims=True)
    attention = exponent / denom_sum * key_mask[:, None]
    mixed = jnp.dot(attention.astype(jnp.bfloat16), value_head, preferred_element_type=jnp.float32)
    return (mixed.astype(jnp.bfloat16), row_peak + jnp.log(denom_sum))


def head_backward(key_mask, paired):
    rand_head, value_head, mix_grad, log_total = paired
    scores = masked_scores(key_mask, rand_head)
    attention = jnp.exp(scores - log_total) * key_mask[:, None]
    prob_grad = jnp.einsum("id,jd->ij", mix_grad, value_head, preferred_element_type=jnp.float32)
    value_grad = jnp.einsum(
        "ij,id->jd", attention.astype(jnp.bfloat16), mix_grad, preferred_element_type=jnp.float32
    )
    score_grad = attention * (prob_grad - jnp.sum(prob_grad * attention, axis=-1, keepdims=True))
    return (score_grad, value_grad)


def shards(tokens, lengths, rand_mix, w_value, w_out, w_up, w_down, gain_mix, gain_ffn, grad_out):
    item_count = tokens.shape[0]
    width = tokens.shape[2]
    row_count = item_count * LMAX
    tokens_flat = tokens.reshape(row_count, width).astype(jnp.float32)
    positions = jnp.arange(LMAX, dtype=jnp.int32)
    valid_table = (positions[None, :] < lengths[:, None]).astype(jnp.float32)
    row_valid = valid_table.reshape(row_count, 1)
    forward_set = (
        lax.all_gather(rand_mix, ("wide", "narrow"), axis=0, tiled=True),
        lax.all_gather(w_value, ("wide", "narrow"), axis=0, tiled=True),
        lax.all_gather(w_out, ("wide", "narrow"), axis=0, tiled=True),
        lax.all_gather(w_up, ("wide", "narrow"), axis=0, tiled=True),
        lax.all_gather(w_down, ("wide", "narrow"), axis=0, tiled=True),
        lax.all_gather(gain_mix, ("wide", "narrow"), axis=0, tiled=True),
        lax.all_gather(gain_ffn, ("wide", "narrow"), axis=0, tiled=True),
    )
    rand_all, value_all, out_all, up_all, down_all, gain_first, gain_second = forward_set
    normed = rms_norm(tokens_flat, gain_first.astype(jnp.float32)).astype(jnp.bfloat16)
    values = jnp.dot(normed, value_all, preferred_element_type=jnp.float32).astype(jnp.bfloat16)
    rand_heads = rand_all.reshape(HEADS, LMAX, LMAX)
    mixed_parts = []
    totals_kept = []
    for item_index in range(item_count):
        item_values = split_heads(values[item_index * LMAX : (item_index + 1) * LMAX])
        mixed_heads, log_total = lax.map(
            partial(head_forward, valid_table[item_index]), (rand_heads, item_values)
        )
        mixed_parts.append(merge_heads(mixed_heads))
        totals_kept.append(log_total)
    mixed = jnp.concatenate(mixed_parts, axis=0)
    residual = tokens_flat + jnp.dot(mixed, out_all, preferred_element_type=jnp.float32)
    normed_two = rms_norm(residual, gain_second.astype(jnp.float32)).astype(jnp.bfloat16)
    up_proj = jnp.dot(normed_two, up_all, preferred_element_type=jnp.float32)
    active = jax.nn.gelu(up_proj).astype(jnp.bfloat16)
    branch = jnp.dot(active, down_all, preferred_element_type=jnp.float32)
    output = row_valid * (residual + branch)
    back_set = (
        lax.all_gather(rand_mix, ("wide", "narrow"), axis=0, tiled=True),
        lax.all_gather(w_value, ("wide", "narrow"), axis=0, tiled=True),
        lax.all_gather(w_out, ("wide", "narrow"), axis=0, tiled=True),
        lax.all_gather(w_up, ("wide", "narrow"), axis=0, tiled=True),
        lax.all_gather(w_down, ("wide", "narrow"), axis=0, tiled=True),
        lax.all_gather(gain_mix, ("wide", "narrow"), axis=0, tiled=True),
        lax.all_gather(gain_ffn, ("wide", "narrow"), axis=0, tiled=True),
    )
    rand_back, value_back, out_back, up_back, down_back, gain_back_one, gain_back_two = back_set
    cotangent = grad_out.reshape(row_count, width).astype(jnp.float32)
    masked = row_valid * cotangent
    branch_grad = masked.astype(jnp.bfloat16)
    grad_down = jnp.einsum("rk,rd->kd", active, branch_grad, preferred_element_type=jnp.float32)
    active_grad = jnp.einsum(
        "rd,kd->rk", branch_grad, down_back, preferred_element_type=jnp.float32
    )
    gelu_value, gelu_pull = jax.vjp(jax.nn.gelu, up_proj)
    up_grad = gelu_pull(active_grad)[0].astype(jnp.bfloat16)
    grad_up = jnp.einsum("rd,rk->dk", normed_two, up_grad, preferred_element_type=jnp.float32)
    normed_two_grad = jnp.einsum("rk,dk->rd", up_grad, up_back, preferred_element_type=jnp.float32)
    norm_value, norm_pull = jax.vjp(rms_norm, residual, gain_back_two.astype(jnp.float32))
    residual_part, gain_two_grad = norm_pull(normed_two_grad)
    residual_grad = masked + residual_part
    attn_grad = residual_grad.astype(jnp.bfloat16)
    grad_outproj = jnp.einsum("rd,re->de", mixed, attn_grad, preferred_element_type=jnp.float32)
    mixed_grad = jnp.einsum(
        "re,de->rd", attn_grad, out_back, preferred_element_type=jnp.float32
    ).astype(jnp.bfloat16)
    rand_heads_back = rand_back.reshape(HEADS, LMAX, LMAX)
    rand_grad = jnp.zeros((HEADS, LMAX, LMAX), jnp.float32)
    value_parts = []
    for item_index in range(item_count):
        lower_row = item_index * LMAX
        upper_row = lower_row + LMAX
        item_values = split_heads(values[lower_row:upper_row])
        item_mix_grad = split_heads(mixed_grad[lower_row:upper_row])
        score_grad, value_grad = lax.map(
            partial(head_backward, valid_table[item_index]),
            (rand_heads_back, item_values, item_mix_grad, totals_kept[item_index]),
        )
        rand_grad = rand_grad + score_grad
        value_parts.append(merge_heads(value_grad))
    values_grad = jnp.concatenate(value_parts, axis=0).astype(jnp.bfloat16)
    grad_value = jnp.einsum("rd,re->de", normed, values_grad, preferred_element_type=jnp.float32)
    normed_grad = jnp.einsum(
        "re,de->rd", values_grad, value_back, preferred_element_type=jnp.float32
    )
    norm_first, first_pull = jax.vjp(rms_norm, tokens_flat, gain_back_one.astype(jnp.float32))
    token_part, gain_one_grad = first_pull(normed_grad)
    tokens_grad = residual_grad + token_part
    rand_flat = rand_grad.reshape(HEADS * LMAX, LMAX)
    all_shards = (
        lax.psum_scatter(rand_flat, ("wide", "narrow"), scatter_dimension=0, tiled=True),
        lax.psum_scatter(grad_value, ("wide", "narrow"), scatter_dimension=0, tiled=True),
        lax.psum_scatter(grad_outproj, ("wide", "narrow"), scatter_dimension=0, tiled=True),
        lax.psum_scatter(grad_up, ("wide", "narrow"), scatter_dimension=0, tiled=True),
        lax.psum_scatter(grad_down, ("wide", "narrow"), scatter_dimension=0, tiled=True),
        lax.psum_scatter(gain_one_grad, ("wide", "narrow"), scatter_dimension=0, tiled=True),
        lax.psum_scatter(gain_two_grad, ("wide", "narrow"), scatter_dimension=0, tiled=True),
    )
    rand_shard, value_shard, outproj_shard, up_shard, down_shard, gain_one_shard, gain_two_shard = (
        all_shards
    )
    return (
        output.reshape(item_count, LMAX, width),
        tokens_grad.reshape(item_count, LMAX, width),
        rand_shard,
        value_shard,
        outproj_shard,
        up_shard,
        down_shard,
        gain_one_shard,
        gain_two_shard,
    )


def solution(mesh):
    in_specs = (
        P(("wide", "narrow"), None, None),
        P(("wide", "narrow")),
        P(("wide", "narrow"), None),
        P(("wide", "narrow"), None),
        P(("wide", "narrow"), None),
        P(("wide", "narrow"), None),
        P(("wide", "narrow"), None),
        P(("wide", "narrow")),
        P(("wide", "narrow")),
        P(("wide", "narrow"), None, None),
    )
    out_specs = (
        P(("wide", "narrow"), None, None),
        P(("wide", "narrow"), None, None),
        P(("wide", "narrow"), None),
        P(("wide", "narrow"), None),
        P(("wide", "narrow"), None),
        P(("wide", "narrow"), None),
        P(("wide", "narrow"), None),
        P(("wide", "narrow")),
        P(("wide", "narrow")),
    )
    fits = dict(mesh.shape) == {"wide": 16, "narrow": 2}
    return jax.shard_map(chip_shards if fits else shards, mesh=mesh, in_specs=in_specs, out_specs=out_specs, check_vma=False)
```

```python
from functools import partial

import jax
import jax.numpy as jnp
from jax import lax
from jax.experimental import pallas as pl
from jax.experimental.pallas import tpu as pltpu
from jax.sharding import PartitionSpec as P

HEADS = 12
HEAD = 64
LMAX = 1024
WIDTH = 768
FF = 3072
EPSILON = 1e-05

BOTH = ("wide", "narrow")
BF16 = jnp.bfloat16
F32 = jnp.float32
VMEM = 61 << 20
LESS = 34 << 20

SUBS = 6
RUNS = 8
HALF = 64
HROWS = RUNS * HALF
PLANES = 4
PHEADS = HEADS // PLANES
ROWS = 2 * LMAX
FSTEP = 768
FSIDE = FF // 2 // FSTEP
TILE = 512
SIDE = WIDTH // 2
SPAN = 2 * HALF


def dot(a, b, ca, cb):
    return lax.dot_general(a, b, (((ca,), (cb,)), ((), ())), preferred_element_type=F32)


CORE, PLANE, PLACE, LENGTHS = 0, 1, 2, 3


def spec(shape, index):
    return pl.BlockSpec(shape, index)


def held(shape):
    zeros = (0,) * len(shape)
    return pl.BlockSpec(shape, lambda *_: zeros, pipeline_mode=pl.Buffered(1))


def params(limit):
    return pltpu.CompilerParams(vmem_limit_bytes=limit)


def whole_weight(sc, step, own, far, weight):
    @pl.when(step == 0)
    def _():
        weight[:, pl.ds(pl.multiple_of(sc[CORE] * SIDE, 128), SIDE)] = own[...]
        weight[:, pl.ds(pl.multiple_of((1 - sc[CORE]) * SIDE, 128), SIDE)] = far[...]


def values_kernel(sc, tok, gain, w_own, w_far, out, weight):
    step = pl.program_id(0)
    whole_weight(sc, step, w_own, w_far, weight)
    rows = tok.shape[1]
    position = step * rows + lax.broadcasted_iota(jnp.int32, (rows, 1), 0)
    for item in range(2):
        x = tok[item].astype(F32)
        scale = lax.rsqrt(jnp.mean(x * x, axis=-1, keepdims=True) + EPSILON)
        normed = (x * scale * gain[...]).astype(BF16)
        found = dot(normed, weight[...], 1, 0)
        found = jnp.where(position < sc[LENGTHS + item], found, 0.0).astype(BF16)
        for head in range(HEADS):
            out[head, :, item * HEAD : (item + 1) * HEAD] = found[:, head * HEAD : (head + 1) * HEAD]


def run_values(sc, tokens, gain, w_own, w_far):
    rows = 256
    return pl.pallas_call(
        values_kernel,
        grid_spec=pltpu.PrefetchScalarGridSpec(
            num_scalar_prefetch=1,
            grid=(LMAX // rows,),
            in_specs=[
                spec((2, rows, WIDTH), lambda j, s: (0, j, 0)),
                held((1, WIDTH)),
                held((WIDTH, SIDE)),
                held((WIDTH, SIDE)),
            ],
            out_specs=spec((HEADS, rows, 2 * HEAD), lambda j, s: (0, j, 0)),
            scratch_shapes=[pltpu.VMEM((WIDTH, WIDTH), BF16)],
        ),
        out_shape=jax.ShapeDtypeStruct((HEADS, LMAX, 2 * HEAD), BF16),
        compiler_params=params(VMEM),
        cost_estimate=pl.CostEstimate(
            flops=2 * 2 * LMAX * WIDTH * WIDTH, bytes_accessed=8 * LMAX * WIDTH, transcendentals=0
        ),
        name="values",
    )(sc, tokens, gain, w_own, w_far)


def lane_lengths(sc, shape):
    slot = lax.broadcasted_iota(jnp.int32, shape, 1) // HEAD
    length = jnp.where(slot == 0, sc[LENGTHS], sc[LENGTHS + 1])
    return jnp.where(slot >= 2, jnp.where(slot == 2, sc[LENGTHS + 2], sc[LENGTHS + 3]), length)


def plane_of(k, sc):
    return lax.rem(sc[PLANE] + PLANES - k, PLANES)


def plane_spec(planes, rows, lanes):
    def index(step, sc):
        return (plane_of(planes[0] + step * (planes[1] - planes[0]), sc), 0, 0)

    return spec((PHEADS, rows, lanes), index)


def anywhere(count):
    return [pl.BlockSpec(memory_space=pl.ANY)] * count


def plane_fetch(place, shards, raw, sems, slot):
    return [
        pltpu.make_async_copy(
            shards[4 * slot + rel],
            raw.at[slot, pl.ds(pl.multiple_of((place ^ rel) * SUBS * HALF, SUBS * HALF), SUBS * HALF)],
            sems.at[slot, rel],
        )
        for rel in range(4)
    ]


def take_plane(place, shards, raw, sems):
    step = pl.program_id(0)

    @pl.when(step == 0)
    def _():
        for slot in range(2):
            for copy in plane_fetch(place, shards, raw, sems, slot):
                copy.start()

    for slot in range(2):

        @pl.when(step == slot)
        def _():
            for copy in plane_fetch(place, shards, raw, sems, slot):
                copy.wait()

    return step


def head_rows(head):
    return slice(head * HROWS, (head + 1) * HROWS)


def fill_mask(sc, mask):
    @pl.when(pl.program_id(0) == 0)
    def _():
        shape = (LMAX, 4 * HEAD)
        column = lax.broadcasted_iota(jnp.int32, shape, 0)
        mask[...] = (column < lane_lengths(sc, shape)).astype(F32).astype(BF16)


def mix_kernel(carried, sc, *refs):
    shards, (v_own, v_far, *rest) = refs[:8], refs[8:]
    mixed, mean, exps, inverse, raw, mask, sems = rest[4:] if carried else rest
    fill_mask(sc, mask)
    slot = take_plane(sc[PLACE], shards, raw, sems)
    shape = (HROWS, 4 * HEAD)
    line = lax.broadcasted_iota(jnp.int32, shape, 0)
    position = 128 * (line // HALF) + HALF * sc[CORE] + line % HALF
    valid = position < lane_lengths(sc, shape)
    for head in range(PHEADS):
        weights = jnp.exp(raw[slot, head_rows(head)].astype(F32)).astype(BF16)
        exps[head] = weights
        both = dot(weights, jnp.concatenate([v_own[head], v_far[head], mask[...]], axis=1), 1, 0)
        flip = jnp.where(valid, 1.0 / both[:, 4 * HEAD :], 0.0)
        found = both[:, : 4 * HEAD] * flip
        inverse[head] = flip.astype(BF16)
        mean[head] = found
        mixed[head] = found.astype(BF16)


def run_mix(sc, planes, shards, v_own, v_far, carry):
    carry = list(carry)
    shape = (HEADS, HROWS, 4 * HEAD)
    return pl.pallas_call(
        partial(mix_kernel, bool(carry)),
        grid_spec=pltpu.PrefetchScalarGridSpec(
            num_scalar_prefetch=1,
            grid=(2,),
            in_specs=anywhere(8) + [plane_spec(planes, LMAX, 2 * HEAD)] * 2 + anywhere(len(carry)),
            out_specs=[
                plane_spec(planes, HROWS, 4 * HEAD),
                plane_spec(planes, HROWS, 4 * HEAD),
                plane_spec(planes, HROWS, LMAX),
                plane_spec(planes, HROWS, 4 * HEAD),
            ],
            scratch_shapes=[
                pltpu.VMEM((2, 4 * SUBS * HALF, LMAX), BF16),
                pltpu.VMEM((LMAX, 4 * HEAD), BF16),
                pltpu.SemaphoreType.DMA((2, 4)),
            ],
        ),
        out_shape=[
            jax.ShapeDtypeStruct(shape, BF16),
            jax.ShapeDtypeStruct(shape, F32),
            jax.ShapeDtypeStruct((HEADS, HROWS, LMAX), BF16),
            jax.ShapeDtypeStruct(shape, BF16),
        ],
        input_output_aliases={11 + i: i for i in range(len(carry))},
        compiler_params=params(VMEM),
        cost_estimate=pl.CostEstimate(
            flops=2 * HEADS * HROWS * LMAX * 4 * HEAD,
            bytes_accessed=HEADS * (2 * HROWS * LMAX + 5 * HROWS * 256),
            transcendentals=HEADS * HROWS * LMAX // 2,
        ),
        name="mix",
    )(sc, *shards, v_own, v_far, *carry)


def row_valid(sc, step):
    line = lax.broadcasted_iota(jnp.int32, (4 * SPAN, 1), 0)
    item = line // SPAN
    row = step * SPAN + line % SPAN
    low = jnp.where(item == 0, sc[LENGTHS], sc[LENGTHS + 1])
    high = jnp.where(item == 2, sc[LENGTHS + 2], sc[LENGTHS + 3])
    return 128 * (row // HALF) + HALF * sc[CORE] + row % HALF < jnp.where(item >= 2, high, low)


def four_items(own, far):
    return jnp.concatenate([own[:, :, 0], far[...]], axis=0).reshape(4 * SPAN, WIDTH)


def pre_kernel(sc, tok, tok_far, cot, cot_far, heads, wo_own, wo_far, gain, mixed, resid, normed, grad, weight):
    step = pl.program_id(0)
    whole_weight(sc, step, wo_own, wo_far, weight)
    for item in range(4):
        lanes = slice(item * HEAD, (item + 1) * HEAD)
        for pair in range(HEADS // 2):
            both = jnp.concatenate([heads[2 * pair, :, lanes], heads[2 * pair + 1, :, lanes]], axis=1)
            mixed[item, :, pair * 128 : (pair + 1) * 128] = both
    res = four_items(tok, tok_far).astype(F32) + dot(mixed[...].reshape(4 * SPAN, WIDTH), weight[...], 1, 0)
    resid[...] = res.astype(BF16).reshape(4, SPAN, WIDTH)
    scale = lax.rsqrt(jnp.mean(res * res, axis=-1, keepdims=True) + EPSILON)
    valid = row_valid(sc, step)
    normed[...] = jnp.where(valid, res * scale * gain[...], 0.0).astype(BF16).reshape(4, SPAN, WIDTH)
    masked = jnp.where(valid, four_items(cot, cot_far).astype(F32), 0.0)
    grad[...] = masked.astype(BF16).reshape(4, SPAN, WIDTH)


def slab_spec(items=4):
    return spec((items, SPAN, WIDTH), lambda r, s: (0, r, 0))


def half_specs():
    return [
        spec((2, SPAN // HALF, 1, HALF, WIDTH), lambda r, s: (0, r, s[CORE], 0, 0)),
        spec((2, SPAN // HALF, HALF, WIDTH), lambda r, s: (0, r, 0, 0)),
    ]


def heads_spec():
    return spec((HEADS, SPAN, 4 * HEAD), lambda r, s: (0, r, 0))


def run_pre(sc, tokens, tokens_far, cotangent, cotangent_far, heads, wo, gain):
    return pl.pallas_call(
        pre_kernel,
        grid_spec=pltpu.PrefetchScalarGridSpec(
            num_scalar_prefetch=1,
            grid=(HROWS // SPAN,),
            in_specs=half_specs()
            + half_specs()
            + [heads_spec(), held((WIDTH, SIDE)), held((WIDTH, SIDE)), held((1, WIDTH))],
            out_specs=[slab_spec()] * 4,
            scratch_shapes=[pltpu.VMEM((WIDTH, WIDTH), BF16)],
        ),
        out_shape=[
            jax.ShapeDtypeStruct((4, HROWS, WIDTH), BF16),
            jax.ShapeDtypeStruct((4, HROWS, WIDTH), BF16),
            jax.ShapeDtypeStruct((4, HROWS, WIDTH), BF16),
            jax.ShapeDtypeStruct((4, HROWS, WIDTH), BF16),
        ],
        compiler_params=params(VMEM),
        cost_estimate=pl.CostEstimate(
            flops=2 * ROWS * WIDTH * WIDTH, bytes_accessed=16 * ROWS * WIDTH, transcendentals=0
        ),
        name="pre",
    )(sc, tokens, tokens_far, cotangent, cotangent_far, heads, *wo, gain)


def own_lanes(sc):
    return pl.ds(pl.multiple_of(sc[CORE] * SIDE, 128), SIDE)


def far_lanes(sc):
    return pl.ds(pl.multiple_of((1 - sc[CORE]) * SIDE, 128), SIDE)


def unit_rows(f, sc):
    return (lax.rem(FSIDE * sc[CORE] + f, 2 * FSIDE), 0)


def unit_columns(f, sc):
    return (0, lax.rem(FSIDE * sc[CORE] + f, 2 * FSIDE))


def early(f, sc):
    return (0, lax.min(f, FSIDE - 1))


def late(f, sc):
    return (0, lax.max(f - FSIDE, 0))


def units_kernel(sc, normed, cot, up_own, up_far, dn_own, dn_far, active, up_grad, w_up, w_down):
    step = pl.program_id(0)
    w_down[:, own_lanes(sc)] = dn_own[...]
    w_down[:, far_lanes(sc)] = dn_far[...]

    @pl.when(step < FSIDE)
    def _():
        w_up[...] = up_own[...]

    @pl.when(step >= FSIDE)
    def _():
        w_up[...] = up_far[...]

    for row in range(0, ROWS, 256):
        rows = slice(row, row + 256)
        for column in range(0, FSTEP, 256):
            columns = slice(column, column + 256)
            up = dot(normed[rows], w_up[:, columns], 1, 0)
            square = up * up
            bend = jnp.tanh(up * (0.7978845608028654 + (0.044715 * 0.7978845608028654) * square))
            share = 0.5 + 0.5 * bend
            act = up * share
            active[rows, columns] = act.astype(BF16)
            slope = share + act * (1.0 - share) * (
                2 * 0.7978845608028654 + (6 * 0.044715 * 0.7978845608028654) * square
            )
            up_grad[rows, columns] = (dot(cot[rows], w_down[columns], 1, 1) * slope).astype(BF16)


def run_units(sc, normed, cotangent, up, down):
    return pl.pallas_call(
        units_kernel,
        grid_spec=pltpu.PrefetchScalarGridSpec(
            num_scalar_prefetch=1,
            grid=(2 * FSIDE,),
            in_specs=[
                held((ROWS, WIDTH)),
                held((ROWS, WIDTH)),
                spec((WIDTH, FSTEP), early),
                spec((WIDTH, FSTEP), late),
                spec((FSTEP, SIDE), unit_rows),
                spec((FSTEP, SIDE), unit_rows),
            ],
            out_specs=[spec((ROWS, FSTEP), unit_columns), spec((ROWS, FSTEP), unit_columns)],
            scratch_shapes=[pltpu.VMEM((WIDTH, FSTEP), BF16), pltpu.VMEM((FSTEP, WIDTH), BF16)],
        ),
        out_shape=[jax.ShapeDtypeStruct((ROWS, FF), BF16), jax.ShapeDtypeStruct((ROWS, FF), BF16)],
        compiler_params=params(VMEM),
        cost_estimate=pl.CostEstimate(
            flops=4 * ROWS * WIDTH * FF, bytes_accessed=6 * ROWS * WIDTH + 4 * ROWS * FF, transcendentals=ROWS * FF
        ),
        name="units",
    )(sc, normed.reshape(ROWS, WIDTH), cotangent.reshape(ROWS, WIDTH), *up, *down)


def down_grad_kernel(sc, active, cot, own, far, total):
    total[...] = dot(active[...], cot[...], 0, 0).astype(BF16)
    own[...] = total[:, own_lanes(sc)]
    far[...] = total[:, far_lanes(sc)]


def run_down_grad(sc, active, cotangent):
    return pl.pallas_call(
        down_grad_kernel,
        grid_spec=pltpu.PrefetchScalarGridSpec(
            num_scalar_prefetch=1,
            grid=(FF // 512,),
            in_specs=[spec((ROWS, 512), lambda f, s: (0, f)), held((ROWS, WIDTH))],
            out_specs=[spec((512, SIDE), lambda f, s: (f, 0))] * 2,
            scratch_shapes=[pltpu.VMEM((512, WIDTH), BF16)],
        ),
        out_shape=[jax.ShapeDtypeStruct((FF, SIDE), BF16)] * 2,
        compiler_params=params(57 << 20),
        cost_estimate=pl.CostEstimate(
            flops=2 * ROWS * WIDTH * FF, bytes_accessed=2 * ROWS * (WIDTH + FF), transcendentals=0
        ),
        name="down_grad",
    )(sc, active, cotangent.reshape(ROWS, WIDTH))


def up_grad_kernel(sc, normed, up_grad, own, far):
    total = dot(normed[...], up_grad[...], 0, 0).astype(BF16)

    @pl.when(pl.program_id(0) < 3)
    def _():
        own[...] = total

    @pl.when(pl.program_id(0) >= 3)
    def _():
        far[...] = total


def run_up_grad(sc, normed, up_grad):
    return pl.pallas_call(
        up_grad_kernel,
        grid_spec=pltpu.PrefetchScalarGridSpec(
            num_scalar_prefetch=1,
            grid=(6,),
            in_specs=[held((ROWS, WIDTH)), spec((ROWS, 512), lambda f, s: (0, lax.rem(3 * s[CORE] + f, 6)))],
            out_specs=[
                spec((WIDTH, 512), lambda f, s: (0, lax.min(f, 2))),
                spec((WIDTH, 512), lambda f, s: (0, lax.max(f - 3, 0))),
            ],
        ),
        out_shape=[jax.ShapeDtypeStruct((WIDTH, FF // 2), BF16)] * 2,
        compiler_params=params(57 << 20),
        cost_estimate=pl.CostEstimate(
            flops=2 * ROWS * WIDTH * FF, bytes_accessed=2 * ROWS * (WIDTH + FF), transcendentals=0
        ),
        name="up_grad",
    )(sc, normed.reshape(ROWS, WIDTH), up_grad)


def out_grad_kernel(sc, mixed, res_own, res_far, own, far, total):
    step = pl.program_id(0)
    grad = jnp.concatenate([res_own[...], res_far[...]], axis=0).reshape(4 * SPAN, WIDTH)
    found = dot(mixed[...].reshape(4 * SPAN, WIDTH), grad, 0, 0)

    @pl.when(step == 0)
    def _():
        total[...] = found

    @pl.when(step > 0)
    def _():
        total[...] += found

    @pl.when(step == pl.num_programs(0) - 1)
    def _():
        own[...] = total[:, own_lanes(sc)].astype(BF16)
        far[...] = total[:, far_lanes(sc)].astype(BF16)


def run_out_grad(sc, mixed, res_own, res_far):
    return pl.pallas_call(
        out_grad_kernel,
        grid_spec=pltpu.PrefetchScalarGridSpec(
            num_scalar_prefetch=1,
            grid=(HROWS // SPAN,),
            in_specs=[slab_spec(), slab_spec(2), slab_spec(2)],
            out_specs=[held((WIDTH, SIDE))] * 2,
            scratch_shapes=[pltpu.VMEM((WIDTH, WIDTH), F32)],
        ),
        out_shape=[jax.ShapeDtypeStruct((WIDTH, SIDE), BF16)] * 2,
        compiler_params=params(LESS),
        cost_estimate=pl.CostEstimate(
            flops=2 * ROWS * WIDTH * WIDTH, bytes_accessed=4 * ROWS * WIDTH, transcendentals=0
        ),
        name="out_grad",
    )(sc, mixed, res_own, res_far)


def out_kernel(sc, active, resid, dn_own, dn_far, own, far, w_down):
    step = pl.program_id(0)

    @pl.when(step == 0)
    def _():
        w_down[:, own_lanes(sc)] = dn_own[...]
        w_down[:, far_lanes(sc)] = dn_far[...]

    branch = dot(active[...].reshape(4 * SPAN, FF), w_down[...], 1, 0)
    output = jnp.where(row_valid(sc, step), resid[...].reshape(4 * SPAN, WIDTH).astype(F32) + branch, 0.0)
    output = output.astype(BF16).reshape(4, SPAN, WIDTH)
    own[...] = output[:2]
    far[...] = output[2:]


def run_out(sc, active, resid, down):
    return pl.pallas_call(
        out_kernel,
        grid_spec=pltpu.PrefetchScalarGridSpec(
            num_scalar_prefetch=1,
            grid=(HROWS // SPAN,),
            in_specs=[
                spec((4, SPAN, FF), lambda r, s: (0, r, 0)),
                slab_spec(),
                held((FF, SIDE)),
                held((FF, SIDE)),
            ],
            out_specs=[slab_spec(2)] * 2,
            scratch_shapes=[pltpu.VMEM((FF, WIDTH), BF16)],
        ),
        out_shape=[
            jax.ShapeDtypeStruct((2, HROWS, WIDTH), BF16),
            jax.ShapeDtypeStruct((2, HROWS, WIDTH), BF16),
        ],
        compiler_params=params(LESS),
        cost_estimate=pl.CostEstimate(
            flops=2 * ROWS * WIDTH * FF, bytes_accessed=ROWS * (2 * FF + 7 * WIDTH), transcendentals=0
        ),
        name="out",
    )(sc, active.reshape(4, HROWS, FF), resid, *down)


def post_kernel(sc, resid, grad_own, grad_far, cot, up_own, up_far, wo_own, wo_far, gain, *refs):
    (res_own, res_far, heads, d_gain, weight, spread) = refs
    step = pl.program_id(0)
    whole_weight(sc, step, wo_own, wo_far, weight)
    shape, slab = (4 * SPAN, WIDTH), (4, SPAN, WIDTH)
    valid = row_valid(sc, step)
    res = resid[...].reshape(shape).astype(F32)
    scale = lax.rsqrt(jnp.mean(res * res, axis=-1, keepdims=True) + EPSILON)
    unit = res * scale
    units = (4 * SPAN, FF // 2)
    back = dot(grad_own[...].reshape(units), up_own[...], 1, 1) + dot(grad_far[...].reshape(units), up_far[...], 1, 1)
    two_grad = jnp.where(valid, back, 0.0)
    gained = two_grad * gain[...]
    masked = cot[...].reshape(shape).astype(F32)
    grad = masked + scale * (gained - unit * jnp.mean(gained * unit, axis=-1, keepdims=True))
    low = grad.astype(BF16)
    res_own[...] = low.reshape(slab)[:2]
    res_far[...] = low.reshape(slab)[2:]
    gain_sum = jnp.sum(two_grad * unit, axis=0, keepdims=True)

    @pl.when(step == 0)
    def _():
        d_gain[...] = gain_sum

    @pl.when(step > 0)
    def _():
        d_gain[...] += gain_sum

    spread[...] = dot(low, weight[...], 1, 1).astype(BF16).reshape(slab)
    for pair in range(HEADS // 2):
        lanes = slice(pair * 128, (pair + 1) * 128)
        for side in range(2):
            one, two = spread[2 * side, :, lanes], spread[2 * side + 1, :, lanes]
            half = slice(side * 128, (side + 1) * 128)
            heads[2 * pair, :, half] = jnp.concatenate([one[:, :HEAD], two[:, :HEAD]], axis=1)
            heads[2 * pair + 1, :, half] = jnp.concatenate([one[:, HEAD:], two[:, HEAD:]], axis=1)


def run_post(sc, resid, up_grad, cotangent, up, wo, gain):
    side = lambda which: spec((4, SPAN, FF // 2), lambda r, s: (0, r, s[CORE] if which == 0 else 1 - s[CORE]))
    up_grad = up_grad.reshape(4, HROWS, FF)
    return pl.pallas_call(
        post_kernel,
        grid_spec=pltpu.PrefetchScalarGridSpec(
            num_scalar_prefetch=1,
            grid=(HROWS // SPAN,),
            in_specs=[
                slab_spec(),
                side(0),
                side(1),
                slab_spec(),
                held((WIDTH, FF // 2)),
                held((WIDTH, FF // 2)),
                held((WIDTH, SIDE)),
                held((WIDTH, SIDE)),
                held((1, WIDTH)),
            ],
            out_specs=[slab_spec(2)] * 2 + [heads_spec(), held((1, WIDTH))],
            scratch_shapes=[
                pltpu.VMEM((WIDTH, WIDTH), BF16),
                pltpu.VMEM((4, SPAN, WIDTH), BF16),
            ],
        ),
        out_shape=[
            jax.ShapeDtypeStruct((2, HROWS, WIDTH), BF16),
            jax.ShapeDtypeStruct((2, HROWS, WIDTH), BF16),
            jax.ShapeDtypeStruct((HEADS, HROWS, 4 * HEAD), BF16),
            jax.ShapeDtypeStruct((1, WIDTH), F32),
        ],
        compiler_params=params(VMEM),
        cost_estimate=pl.CostEstimate(
            flops=2 * ROWS * WIDTH * (WIDTH + FF), bytes_accessed=ROWS * (16 * WIDTH + 2 * FF), transcendentals=0
        ),
        name="post",
    )(sc, resid, up_grad, up_grad, cotangent, *up, *wo, gain)


def unmix_kernel(carried, sc, v_own, v_far, grad_heads, mean, exps, inverse, *refs):
    refs = refs[2:] if carried else refs
    outs, (own, far, grads, mask, adder, bound, out_sems) = refs[:8], refs[8:]
    place = sc[PLACE]
    step = pl.program_id(0)

    def leave(slot):
        return [
            pltpu.make_async_copy(
                grads.at[slot, pl.ds(pl.multiple_of((place ^ rel) * SUBS * HALF, SUBS * HALF), SUBS * HALF)],
                outs[4 * slot + rel],
                out_sems.at[slot, rel],
            )
            for rel in range(4)
        ]

    fill_mask(sc, mask)

    @pl.when(step == 0)
    def _():
        lane = lax.broadcasted_iota(jnp.int32, (4 * HEAD, 128), 0) // HEAD
        column = lax.broadcasted_iota(jnp.int32, (4 * HEAD, 128), 1)
        adder[...] = jnp.where((lane == column) | (lane + 4 == column), -1.0, 0.0).astype(BF16)
        row = lax.broadcasted_iota(jnp.int32, (LMAX, 128), 0)
        item = lax.broadcasted_iota(jnp.int32, (LMAX, 128), 1)
        length = jnp.where(item % 4 == 0, sc[LENGTHS], sc[LENGTHS + 1])
        length = jnp.where(item % 4 == 2, sc[LENGTHS + 2], length)
        length = jnp.where(item % 4 == 3, sc[LENGTHS + 3], length)
        bound[...] = jnp.where((item < 8) & (row < length), 1.0, 0.0).astype(BF16)

    high_lanes = lax.broadcasted_iota(jnp.int32, (HROWS, 128), 1) < 4
    for head in range(PHEADS):
        weights = exps[head]
        low = (grad_heads[head].astype(F32) * inverse[head].astype(F32)).astype(BF16)
        product = low.astype(F32) * mean[head]
        coarse = product.astype(BF16)
        fine = (product - coarse.astype(F32)).astype(BF16)
        delta = dot(coarse, adder[...], 1, 0) + dot(fine, adder[...], 1, 0)
        coarse = delta.astype(BF16)
        fine = (delta - coarse.astype(F32)).astype(BF16)
        left = jnp.concatenate([low, jnp.where(high_lanes, coarse, fine)], axis=1)
        score = dot(left, jnp.concatenate([v_own[head], v_far[head], bound[...]], axis=1), 1, 1)
        grads[step, head_rows(head)] = (score * weights.astype(F32)).astype(BF16)
        back = (dot(weights, low, 0, 0) * mask[...].astype(F32)).astype(BF16)
        own[head] = back[:, : 2 * HEAD]
        far[head] = back[:, 2 * HEAD :]
    for which in range(2):

        @pl.when(step == which)
        def _():
            for copy in leave(which):
                copy.start()
            if which == 1:
                for copy in leave(0) + leave(1):
                    copy.wait()


def run_unmix(sc, planes, v_own, v_far, grad_heads, mean, exps, inverse, carry):
    carry = list(carry)
    return pl.pallas_call(
        partial(unmix_kernel, bool(carry)),
        grid_spec=pltpu.PrefetchScalarGridSpec(
            num_scalar_prefetch=1,
            grid=(2,),
            in_specs=[
                plane_spec(planes, LMAX, 2 * HEAD),
                plane_spec(planes, LMAX, 2 * HEAD),
                plane_spec(planes, HROWS, 4 * HEAD),
                plane_spec(planes, HROWS, 4 * HEAD),
                plane_spec(planes, HROWS, LMAX),
                plane_spec(planes, HROWS, 4 * HEAD),
            ]
            + anywhere(len(carry)),
            out_specs=anywhere(8) + [plane_spec(planes, LMAX, 2 * HEAD)] * 2,
            scratch_shapes=[
                pltpu.VMEM((2, 4 * SUBS * HALF, LMAX), BF16),
                pltpu.VMEM((LMAX, 4 * HEAD), BF16),
                pltpu.VMEM((4 * HEAD, 128), BF16),
                pltpu.VMEM((LMAX, 128), BF16),
                pltpu.SemaphoreType.DMA((2, 4)),
            ],
        ),
        out_shape=[jax.ShapeDtypeStruct((SUBS * HALF, LMAX), BF16)] * 8
        + [jax.ShapeDtypeStruct((HEADS, LMAX, 2 * HEAD), BF16)] * 2,
        input_output_aliases={7 + i: 8 + i for i in range(len(carry))},
        compiler_params=params(VMEM),
        cost_estimate=pl.CostEstimate(
            flops=3 * HEADS * HROWS * LMAX * 4 * HEAD,
            bytes_accessed=HEADS * (2 * HROWS * LMAX + 5 * HROWS * 256 + 4 * LMAX * 256),
            transcendentals=0,
        ),
        name="unmix",
    )(sc, v_own, v_far, grad_heads, mean, exps, inverse, *carry)


def close_kernel(sc, tok, res_own, res_got, out_own, out_got, own, far, gain, w_own, w_far, *refs):
    (output, tok_grad, d_value, d_gain, total, weight) = refs
    step = pl.program_id(0)
    whole_weight(sc, step, w_own, w_far, weight)
    core = sc[CORE]
    output[:, :, core] = out_own[...].astype(F32)
    output[:, :, 1 - core] = out_got[...].astype(F32)
    tok_grad[:, :, core] = res_own[...].astype(F32)
    tok_grad[:, :, 1 - core] = res_got[...].astype(F32)
    runs = tok.shape[1]
    rows = runs * 128
    for item in range(2):
        lanes = slice(item * HEAD, (item + 1) * HEAD)
        pieces = [
            add_low(own[head, :, lanes], far[head, :, lanes]) for head in range(HEADS)
        ]
        back = jnp.concatenate(pieces, axis=1)
        x = tok[item].reshape(rows, WIDTH).astype(F32)
        scale = lax.rsqrt(jnp.mean(x * x, axis=-1, keepdims=True) + EPSILON)
        unit = x * scale
        normed = (unit * gain[...]).astype(BF16)
        normed_grad = dot(back, weight[...], 1, 1)
        gained = normed_grad * gain[...]
        update = scale * (gained - unit * jnp.mean(gained * unit, axis=-1, keepdims=True))
        tok_grad[item] += update.reshape(runs, 2, HALF, WIDTH)
        gain_sum = jnp.sum(normed_grad * unit, axis=0, keepdims=True)
        value_sum = dot(normed, back, 0, 0)
        if item == 0:
            gain_total, value_total = gain_sum, value_sum
        else:
            gain_total, value_total = gain_total + gain_sum, value_total + value_sum

    @pl.when(step == 0)
    def _():
        d_gain[...] = gain_total
        total[...] = value_total

    @pl.when(step > 0)
    def _():
        d_gain[...] += gain_total
        total[...] += value_total

    @pl.when(step == pl.num_programs(0) - 1)
    def _():
        low = total[...].astype(BF16)
        d_value[0] = low[:, :SIDE]
        d_value[1] = low[:, SIDE:]


def run_close(sc, tokens, res_own, res_got, out_own, out_got, own, far, gain, w_own, w_far):
    runs = 2
    slab = (2, RUNS, 2, HALF, WIDTH)
    half = (2, RUNS, HALF, WIDTH)
    whole_spec = spec((2, runs, 2, HALF, WIDTH), lambda j, s: (0, j, 0, 0, 0))
    half_spec = spec((2, runs, HALF, WIDTH), lambda j, s: (0, j, 0, 0))
    back_spec = spec((HEADS, runs * 128, 2 * HEAD), lambda j, s: (0, j, 0))
    return pl.pallas_call(
        close_kernel,
        grid_spec=pltpu.PrefetchScalarGridSpec(
            num_scalar_prefetch=1,
            grid=(RUNS // runs,),
            in_specs=[whole_spec]
            + [half_spec] * 4
            + [back_spec, back_spec, held((1, WIDTH)), held((WIDTH, SIDE)), held((WIDTH, SIDE))],
            out_specs=[whole_spec, whole_spec, held((2, WIDTH, SIDE)), held((1, WIDTH))],
            scratch_shapes=[pltpu.VMEM((WIDTH, WIDTH), F32), pltpu.VMEM((WIDTH, WIDTH), BF16)],
        ),
        out_shape=[
            jax.ShapeDtypeStruct(slab, F32),
            jax.ShapeDtypeStruct(slab, F32),
            jax.ShapeDtypeStruct((2, WIDTH, SIDE), BF16),
            jax.ShapeDtypeStruct((1, WIDTH), F32),
        ],
        compiler_params=params(LESS),
        cost_estimate=pl.CostEstimate(
            flops=4 * 2 * LMAX * WIDTH * WIDTH, bytes_accessed=38 * LMAX * WIDTH, transcendentals=0
        ),
        name="close",
    )(
        sc,
        tokens.reshape(slab),
        *(x.reshape(half) for x in (res_own, res_got, out_own, out_got)),
        own,
        far,
        gain,
        w_own,
        w_far,
    )


PACK_DOWN, PACK_UP, PACK_OUT, PACK_VALUE, PACK_GAIN, PACK = 0, 192, 384, 432, 480, 496


def pack_kernel(sc, down, up, out, value, gain, down_far, up_far, out_far, value_far, gain_far, packed):
    first = sc[CORE] == 0

    def both(own, far, lanes):
        own, far = own[:, lanes], far[:, lanes]
        return jnp.concatenate([jnp.where(first, own, far), jnp.where(first, far, own)], axis=0)

    def side(own, far):
        return both(own, far, own_lanes(sc))

    packed[PACK_DOWN:PACK_UP] = side(down, down_far)
    for j in range(4):
        lanes = pl.ds(pl.multiple_of((4 * sc[CORE] + j) * SIDE, 128), SIDE)
        packed[PACK_UP + 48 * j : PACK_UP + 48 * (j + 1)] = both(up, up_far, lanes)
    packed[PACK_OUT:PACK_VALUE] = side(out, out_far)
    packed[PACK_VALUE:PACK_GAIN] = side(value, value_far)
    packed[PACK_GAIN:] = both(gain, gain_far, slice(0, SIDE))


def run_pack(sc, own, far):
    return pl.pallas_call(
        pack_kernel,
        grid_spec=pltpu.PrefetchScalarGridSpec(
            num_scalar_prefetch=1,
            grid=(1,),
            in_specs=[held(x.shape) for x in (*own, *far)],
            out_specs=held((PACK, SIDE)),
        ),
        out_shape=jax.ShapeDtypeStruct((PACK, SIDE), BF16),
        compiler_params=params(VMEM),
        cost_estimate=pl.CostEstimate(flops=0, bytes_accessed=6 * PACK * SIDE, transcendentals=0),
        name="pack",
    )(sc, *own, *far)


def chip_of(sc, k, rel):
    return plane_of(k, sc) * 4 + (sc[PLACE] ^ rel)


def place_kernel(moves, sc, *refs):
    pieces, targets, sems = refs[:16], refs[16:-1], refs[-1]
    copies = []
    for index, piece in enumerate(pieces):
        chip = chip_of(sc, index // 4, index % 4)
        for which, (start, count, lane, target, step, offset, column) in enumerate(moves):
            rows = pl.ds(pl.multiple_of(chip * step + offset, 16), count)
            copies.append(
                pltpu.make_async_copy(
                    piece.at[pl.ds(start, count), pl.ds(lane, SIDE)],
                    targets[target].at[rows, pl.ds(column, SIDE)],
                    sems.at[index, which],
                )
            )
    for copy in copies:
        copy.start()
    for copy in copies:
        copy.wait()


def run_place(sc, pieces, moves, shapes):
    return pl.pallas_call(
        partial(place_kernel, moves),
        grid_spec=pltpu.PrefetchScalarGridSpec(
            num_scalar_prefetch=1,
            grid=(1,),
            in_specs=anywhere(16),
            out_specs=[held(shape) for shape in shapes],
            scratch_shapes=[pltpu.SemaphoreType.DMA((16, len(moves)))],
        ),
        out_shape=[jax.ShapeDtypeStruct(shape, BF16) for shape in shapes],
        compiler_params=params(VMEM),
        cost_estimate=pl.CostEstimate(
            flops=0, bytes_accessed=4 * sum(a * b for a, b in shapes), transcendentals=0
        ),
        name="place",
    )(sc, *pieces)


def place_weights(sc, pieces):
    moves = (
        (PACK_DOWN, 192, 0, 0, 192, 0, 0),
        *((PACK_UP + 48 * j, 48, 0, 1, 48, 0, j * SIDE) for j in range(4)),
        (PACK_OUT, 48, 0, 2, 48, 0, 0),
        (PACK_VALUE, 48, 0, 3, 48, 0, 0),
        (PACK_GAIN, 16, 0, 4, 16, 0, 0),
    )
    shapes = [(FF, SIDE), (WIDTH, FF // 2), (WIDTH, SIDE), (WIDTH, SIDE), (256, SIDE)]
    return run_place(sc, pieces, moves, shapes)


def collect_kernel(sc, *refs):
    outs = refs[24:]
    for k in range(PLANES):

        @pl.when(pl.program_id(0) == k)
        def _():
            for rel in range(4):
                down, down_got, up, up_got, out, out_got = refs[6 * rel : 6 * rel + 6]
                packed = outs[4 * k + rel]
                packed[PACK_DOWN:PACK_UP] = add_low(down[...], down_got[...])
                for j in range(4):
                    lanes = slice(j * SIDE, (j + 1) * SIDE)
                    packed[PACK_UP + 48 * j : PACK_UP + 48 * (j + 1)] = add_low(up[:, lanes], up_got[:, lanes])
                packed[PACK_OUT:PACK_VALUE] = add_low(out[...], out_got[...])


def run_collect(sc, *sides):
    def rows(x, rel):
        return spec((x.shape[0] // 16, x.shape[1]), lambda k, s: (chip_of(s, k, rel), 0))

    return pl.pallas_call(
        collect_kernel,
        grid_spec=pltpu.PrefetchScalarGridSpec(
            num_scalar_prefetch=1,
            grid=(PLANES,),
            in_specs=[rows(x, rel) for rel in range(4) for x in sides],
            out_specs=[held((PACK_VALUE, SIDE))] * 16,
        ),
        out_shape=[jax.ShapeDtypeStruct((PACK_VALUE, SIDE), BF16)] * 16,
        compiler_params=params(LESS),
        cost_estimate=pl.CostEstimate(flops=0, bytes_accessed=3 * 16 * PACK_VALUE * SIDE * 2, transcendentals=0),
        name="collect",
    )(sc, *(x for _ in range(4) for x in sides))


def add_kernel(groups, *refs):
    for group, total in zip(groups, refs[-len(groups) :]):
        value = refs[group[0]][...].astype(F32)
        for index in group[1:]:
            value = value + refs[index][...].astype(F32)
        total[...] = value.astype(total.dtype)


def run_add(groups, values, dtype):
    shape = values[0].shape
    here = pl.BlockSpec(memory_space=pltpu.VMEM)
    return pl.pallas_call(
        partial(add_kernel, groups),
        in_specs=[here] * len(values),
        out_specs=[here] * len(groups),
        out_shape=[jax.ShapeDtypeStruct(shape, dtype)] * len(groups),
        compiler_params=params(LESS),
        cost_estimate=pl.CostEstimate(
            flops=0, bytes_accessed=2 * shape[0] * shape[1] * (len(values) + len(groups)), transcendentals=0
        ),
        name="add",
    )(*values)


DEVICES = 32
TO_CORE, TO_X, TO_Y = 1, 2, 4


def swap(x, bit):
    return lax.ppermute(x, BOTH, [(d, d ^ bit) for d in range(DEVICES)])


def ring(x, way=1):
    return lax.ppermute(x, BOTH, [(d, (d + 8 * way) % DEVICES) for d in range(DEVICES)])


def pick(x, index, axis=0):
    return lax.dynamic_index_in_dim(x, index, axis, keepdims=False)


def ordered(flag, one, two, axis=0, joined=jnp.stack):
    return jnp.where(flag == 0, joined([one, two], axis), joined([two, one], axis))


def add_low(one, two):
    return (one.astype(F32) + two.astype(F32)).astype(BF16)


STEPS = (
    ((0, 0, 1), (0, 1, 0), (1, 0, 0)),
    ((1, 0, 1), (0, 1, 1), (2, 0, 0)),
    ((2, 0, 1), (1, 1, 0), (3, 0, 0)),
    ((3, 0, 1), (2, 1, 0), (1, 1, 1)),
    ((2, 1, 1), (3, 1, 1), (3, 1, 0)),
)


def gather_step(have, step):
    by_x, by_y, by_z = STEPS[step]
    return {
        **have,
        by_z: ring(have[by_z[0] - 1, by_z[1], by_z[2]]),
        by_x: swap(have[by_x[0], by_x[1], 0], TO_X),
        by_y: swap(have[by_y[0], 0, by_y[2]], TO_Y),
    }


def in_order(have):
    return [have[k, y, x] for k in range(4) for y in range(2) for x in range(2)]


def by_place(shares, planes=range(PLANES)):
    return {(k, i // 2, i % 2): shares[4 * at + i] for at, k in enumerate(planes) for i in range(4)}


def scatter_send(have, step):
    by_x, by_y, by_z = STEPS[len(STEPS) - 1 - step]
    got = (ring(have[by_z], -1), swap(have[by_x], TO_X), swap(have[by_y], TO_Y))
    return {at: value for at, value in have.items() if at not in (by_x, by_y, by_z)}, got


def scatter_add(have, got, step):
    by_x, by_y, by_z = STEPS[len(STEPS) - 1 - step]
    targets = ((by_z[0] - 1, by_z[1], by_z[2]), (by_x[0], by_x[1], 0), (by_y[0], 0, by_y[2]))
    sums = list(dict.fromkeys(targets))
    groups = [(len(got) + i, *(j for j in range(len(got)) if targets[j] == at)) for i, at in enumerate(sums)]
    values = [*got, *(have[at] for at in sums)]
    return {**have, **dict(zip(sums, run_add(groups, values, F32 if step == len(STEPS) - 1 else BF16)))}


together = lax.optimization_barrier


def chip_shards(tokens, lengths, rand_mix, w_value, w_out, w_up, w_down, gain_mix, gain_ffn, grad_out):
    wide = lax.axis_index("wide")
    core = lax.axis_index("narrow")
    z, y, x = wide // 4, (wide // 2) % 2, wide % 2
    other = lambda value: swap(value, TO_CORE)
    side = partial(ordered, core, joined=jnp.concatenate)
    slab = (2, RUNS, 2, HALF, WIDTH)
    tokens, grad_out = tokens.reshape(slab), grad_out.reshape(slab)

    gains = jnp.pad(jnp.concatenate([gain_mix, gain_ffn])[None], ((0, 7), (0, SIDE - 48)))
    own = (w_down, w_up, w_out, w_value, gains)
    far = tuple(other(value) for value in own)
    near_sc = jnp.concatenate([jnp.stack([core, z, wide % 4]).astype(jnp.int32), lengths, lengths])
    weights = {(0, 0, 0): run_pack(near_sc, own, far)}

    rand = rand_mix.reshape(3, 2, HALF, LMAX)
    blocks = side(pick(rand, core, 1), other(pick(rand, 1 - core, 1)), 0)
    weights, rands, late_tokens, late_grad = together(
        (gather_step(weights, 0), {(0, 0, 0): blocks.reshape(SUBS * HALF, LMAX)}, tokens, grad_out)
    )
    weights, tokens_far = together((gather_step(weights, 1), other(pick(late_tokens, 1 - core, 2))))
    weights, grad_far = together((gather_step(weights, 2), other(pick(late_grad, 1 - core, 2))))
    weights, far_lengths = together((gather_step(weights, 3), other(lengths)))
    sc = jnp.concatenate([near_sc[:5], far_lengths])
    weights, rands = together((gather_step(weights, 4), rands))

    rands = gather_step(rands, 0)
    down, up, out, value, gain_rows = place_weights(sc, in_order(weights))
    rands, value, value_far, gain_rows, out, down, up = together(
        (rands, value, other(value), gain_rows, out, down, up)
    )
    gain_rows = gain_rows.reshape(16, 2, 8, SIDE)[:, :, 0]
    gain_one = gain_rows[..., :24].reshape(1, WIDTH).astype(F32)
    gain_two = gain_rows[..., 24:48].reshape(1, WIDTH).astype(F32)
    rands = gather_step(rands, 1)
    v_own = run_values(sc, tokens.reshape(2, LMAX, WIDTH), gain_one, value, value_far)
    rands, v_own, out, down, up = together((rands, v_own, (out, other(out)), down, up))
    rands, v_own, v_far, down, up = together((gather_step(rands, 2), v_own, other(v_own), down, up))
    rands, v_far, down, up = together((gather_step(rands, 3), v_far, down, up))
    near = [rands[k, y_at, x_at] for k in range(2) for y_at in range(2) for x_at in range(2)]
    rands = gather_step(rands, 4)
    mixing = run_mix(sc, (0, 1), near, v_own, v_far, ())
    rands, down, up, mixing = together((rands, down, up, mixing))
    heads, mean, exps, inverse = run_mix(sc, (2, 3), in_order(rands)[8:], v_own, v_far, mixing)
    down, up = (down, other(down)), (up, other(up))

    mixed, resid, normed, masked = run_pre(sc, tokens, tokens_far, grad_out, grad_far, heads, out, gain_two)
    active, up_grad = run_units(sc, normed, masked, up, down)
    res_own, res_far, grad_heads, d_gain_two = run_post(sc, resid, up_grad, masked, up, out, gain_two)

    backward = lambda planes, carry: run_unmix(sc, planes, v_own, v_far, grad_heads, mean, exps, inverse, carry)
    *far, back_own, back_far = backward((3, 2), ())
    far, back_own, back_far, res_got = together((far, back_own, back_far, other(res_far)))
    have, got = scatter_send(by_place(far, (3, 2)), 0)
    *near, back_own, back_far = backward((1, 0), (back_own, back_far))
    have, got, near, back_own, back_far = together((have, got, near, back_own, back_far))
    have = {**scatter_add(have, got, 0), **by_place(near, (1, 0))}

    have, got = scatter_send(have, 1)
    out_own, out_far = run_out(sc, active, resid, down)
    have, got, out_own, out_far, back_got = together((have, got, out_own, out_far, other(back_far)))
    have = scatter_add(have, got, 1)

    have, got = scatter_send(have, 2)
    up_own, up_far = run_up_grad(sc, normed, up_grad)
    have, got, up_own, up_far, out_got = together((have, got, up_own, up_far, other(out_far)))
    have = scatter_add(have, got, 2)

    have, got = scatter_send(have, 3)
    down_own, down_far = run_down_grad(sc, active, masked)
    have, got, down_own, down_far, up_got = together((have, got, down_own, down_far, other(up_far)))
    have = scatter_add(have, got, 3)

    have, got = scatter_send(have, 4)
    d_out_own, d_out_far = run_out_grad(sc, mixed, res_own, res_far)
    packed = run_collect(sc, down_own, other(down_far), up_own, up_got, d_out_own, other(d_out_far))
    have, got, packed = together((have, got, packed))
    rand_sum = scatter_add(have, got, 4)[0, 0, 0].reshape(2, 3, HALF, LMAX)

    sums, got = scatter_send(by_place(packed), 0)
    output, tokens_grad, d_value, d_gain_one = run_close(
        sc, tokens, res_own, res_got, out_own, out_got, back_own, back_got, gain_one, value, value_far
    )
    gain_pair = jnp.concatenate([d_gain_one, d_gain_two]).reshape(2, 16, 1, 48).astype(BF16)
    gain_pair = jnp.pad(gain_pair, ((0, 0), (0, 0), (0, 15), (0, SIDE - 48)))
    small = jnp.concatenate([d_value.reshape(2, 16, 48, SIDE), gain_pair], 2)
    sums, got, output, tokens_grad, small = together((sums, got, output, tokens_grad, small))
    sums = scatter_add(sums, got, 0)

    sums, got = scatter_send(sums, 1)
    small = add_low(pick(small, core), other(pick(small, 1 - core))).reshape(4, 2, 2, 64, SIDE)
    sums, got, small = together((sums, got, small))
    sums = scatter_add(sums, got, 1)

    sums, got = scatter_send(sums, 2)
    small = add_low(pick(small, x, 2), swap(pick(small, 1 - x, 2), TO_X))
    sums, got, small = together((sums, got, small))
    sums = scatter_add(sums, got, 2)

    sums, got = scatter_send(sums, 3)
    small = add_low(pick(small, y, 1), swap(pick(small, 1 - y, 1), TO_Y))
    sums, got, small = together((sums, got, small))
    sums = scatter_add(sums, got, 3)

    sums, got = scatter_send(sums, 4)
    small_sum = pick(small, z).astype(F32)
    for k in range(1, PLANES):
        small_sum = small_sum + ring(pick(small, lax.rem(z + PLANES - k, PLANES)), -k).astype(F32)
    blocks, blocks_far = pick(rand_sum, core), other(pick(rand_sum, 1 - core))
    sums, got, small_sum, blocks, blocks_far = together((sums, got, small_sum, blocks, blocks_far))
    big_sum = scatter_add(sums, got, 4)[0, 0, 0]
    big_far, small_far = other(big_sum), other(small_sum)

    rows_of = lambda value, rows: pick(value.reshape(-1, 2, rows, SIDE), core, 1)
    mine = lambda own, far, rows: side(rows_of(own, rows)[0], rows_of(far, rows)[0], 1)
    down_shard = mine(big_sum[PACK_DOWN:PACK_UP], big_far[PACK_DOWN:PACK_UP], 96)
    up_side = lambda value: rows_of(value[PACK_UP:PACK_OUT], 24).transpose(1, 0, 2).reshape(24, 4 * SIDE)
    up_shard = side(up_side(big_sum), up_side(big_far), 1)
    outproj_shard = mine(big_sum[PACK_OUT:PACK_VALUE], big_far[PACK_OUT:PACK_VALUE], 24)
    value_shard = mine(small_sum[:48], small_far[:48], 24)
    gains_pair = ordered(core, small_sum[48, :48], small_far[48, :48])
    gain_pair = pick(gains_pair.reshape(2, 2, 24), core, 1)

    rand_shard = ordered(core, blocks, blocks_far, 1)

    return (
        output.reshape(2, LMAX, WIDTH),
        tokens_grad.reshape(2, LMAX, WIDTH),
        rand_shard.reshape(3 * 128, LMAX),
        value_shard,
        outproj_shard,
        up_shard,
        down_shard,
        gain_pair[0],
        gain_pair[1],
    )


def rms_norm(values, gain):
    scale = lax.rsqrt(jnp.mean(values * values, axis=-1, keepdims=True) + EPSILON)
    return values * scale * gain


def split_heads(block):
    return block.reshape(LMAX, HEADS, HEAD).transpose(1, 0, 2)


def merge_heads(block):
    return block.transpose(1, 0, 2).reshape(LMAX, HEADS * HEAD)


def masked_scores(key_mask, rand_head):
    return jnp.where(key_mask[None, :] > 0, rand_head.astype(jnp.float32), -1e30)


def head_forward(key_mask, paired):
    rand_head, value_head = paired
    scores = masked_scores(key_mask, rand_head)
    row_peak = jnp.max(scores, axis=-1, keepdims=True)
    exponent = jnp.exp(scores - row_peak)
    denom_sum = jnp.sum(exponent, axis=-1, keepdims=True)
    attention = exponent / denom_sum * key_mask[:, None]
    mixed = jnp.dot(attention.astype(jnp.bfloat16), value_head, preferred_element_type=jnp.float32)
    return (mixed.astype(jnp.bfloat16), row_peak + jnp.log(denom_sum))


def head_backward(key_mask, paired):
    rand_head, value_head, mix_grad, log_total = paired
    scores = masked_scores(key_mask, rand_head)
    attention = jnp.exp(scores - log_total) * key_mask[:, None]
    prob_grad = jnp.einsum("id,jd->ij", mix_grad, value_head, preferred_element_type=jnp.float32)
    value_grad = jnp.einsum(
        "ij,id->jd", attention.astype(jnp.bfloat16), mix_grad, preferred_element_type=jnp.float32
    )
    score_grad = attention * (prob_grad - jnp.sum(prob_grad * attention, axis=-1, keepdims=True))
    return (score_grad, value_grad)


def shards(tokens, lengths, rand_mix, w_value, w_out, w_up, w_down, gain_mix, gain_ffn, grad_out):
    item_count = tokens.shape[0]
    width = tokens.shape[2]
    row_count = item_count * LMAX
    tokens_flat = tokens.reshape(row_count, width).astype(jnp.float32)
    positions = jnp.arange(LMAX, dtype=jnp.int32)
    valid_table = (positions[None, :] < lengths[:, None]).astype(jnp.float32)
    row_valid = valid_table.reshape(row_count, 1)
    forward_set = (
        lax.all_gather(rand_mix, ("wide", "narrow"), axis=0, tiled=True),
        lax.all_gather(w_value, ("wide", "narrow"), axis=0, tiled=True),
        lax.all_gather(w_out, ("wide", "narrow"), axis=0, tiled=True),
        lax.all_gather(w_up, ("wide", "narrow"), axis=0, tiled=True),
        lax.all_gather(w_down, ("wide", "narrow"), axis=0, tiled=True),
        lax.all_gather(gain_mix, ("wide", "narrow"), axis=0, tiled=True),
        lax.all_gather(gain_ffn, ("wide", "narrow"), axis=0, tiled=True),
    )
    rand_all, value_all, out_all, up_all, down_all, gain_first, gain_second = forward_set
    normed = rms_norm(tokens_flat, gain_first.astype(jnp.float32)).astype(jnp.bfloat16)
    values = jnp.dot(normed, value_all, preferred_element_type=jnp.float32).astype(jnp.bfloat16)
    rand_heads = rand_all.reshape(HEADS, LMAX, LMAX)
    mixed_parts = []
    totals_kept = []
    for item_index in range(item_count):
        item_values = split_heads(values[item_index * LMAX : (item_index + 1) * LMAX])
        mixed_heads, log_total = lax.map(
            partial(head_forward, valid_table[item_index]), (rand_heads, item_values)
        )
        mixed_parts.append(merge_heads(mixed_heads))
        totals_kept.append(log_total)
    mixed = jnp.concatenate(mixed_parts, axis=0)
    residual = tokens_flat + jnp.dot(mixed, out_all, preferred_element_type=jnp.float32)
    normed_two = rms_norm(residual, gain_second.astype(jnp.float32)).astype(jnp.bfloat16)
    up_proj = jnp.dot(normed_two, up_all, preferred_element_type=jnp.float32)
    active = jax.nn.gelu(up_proj).astype(jnp.bfloat16)
    branch = jnp.dot(active, down_all, preferred_element_type=jnp.float32)
    output = row_valid * (residual + branch)
    back_set = (
        lax.all_gather(rand_mix, ("wide", "narrow"), axis=0, tiled=True),
        lax.all_gather(w_value, ("wide", "narrow"), axis=0, tiled=True),
        lax.all_gather(w_out, ("wide", "narrow"), axis=0, tiled=True),
        lax.all_gather(w_up, ("wide", "narrow"), axis=0, tiled=True),
        lax.all_gather(w_down, ("wide", "narrow"), axis=0, tiled=True),
        lax.all_gather(gain_mix, ("wide", "narrow"), axis=0, tiled=True),
        lax.all_gather(gain_ffn, ("wide", "narrow"), axis=0, tiled=True),
    )
    rand_back, value_back, out_back, up_back, down_back, gain_back_one, gain_back_two = back_set
    cotangent = grad_out.reshape(row_count, width).astype(jnp.float32)
    masked = row_valid * cotangent
    branch_grad = masked.astype(jnp.bfloat16)
    grad_down = jnp.einsum("rk,rd->kd", active, branch_grad, preferred_element_type=jnp.float32)
    active_grad = jnp.einsum(
        "rd,kd->rk", branch_grad, down_back, preferred_element_type=jnp.float32
    )
    gelu_value, gelu_pull = jax.vjp(jax.nn.gelu, up_proj)
    up_grad = gelu_pull(active_grad)[0].astype(jnp.bfloat16)
    grad_up = jnp.einsum("rd,rk->dk", normed_two, up_grad, preferred_element_type=jnp.float32)
    normed_two_grad = jnp.einsum("rk,dk->rd", up_grad, up_back, preferred_element_type=jnp.float32)
    norm_value, norm_pull = jax.vjp(rms_norm, residual, gain_back_two.astype(jnp.float32))
    residual_part, gain_two_grad = norm_pull(normed_two_grad)
    residual_grad = masked + residual_part
    attn_grad = residual_grad.astype(jnp.bfloat16)
    grad_outproj = jnp.einsum("rd,re->de", mixed, attn_grad, preferred_element_type=jnp.float32)
    mixed_grad = jnp.einsum(
        "re,de->rd", attn_grad, out_back, preferred_element_type=jnp.float32
    ).astype(jnp.bfloat16)
    rand_heads_back = rand_back.reshape(HEADS, LMAX, LMAX)
    rand_grad = jnp.zeros((HEADS, LMAX, LMAX), jnp.float32)
    value_parts = []
    for item_index in range(item_count):
        lower_row = item_index * LMAX
        upper_row = lower_row + LMAX
        item_values = split_heads(values[lower_row:upper_row])
        item_mix_grad = split_heads(mixed_grad[lower_row:upper_row])
        score_grad, value_grad = lax.map(
            partial(head_backward, valid_table[item_index]),
            (rand_heads_back, item_values, item_mix_grad, totals_kept[item_index]),
        )
        rand_grad = rand_grad + score_grad
        value_parts.append(merge_heads(value_grad))
    values_grad = jnp.concatenate(value_parts, axis=0).astype(jnp.bfloat16)
    grad_value = jnp.einsum("rd,re->de", normed, values_grad, preferred_element_type=jnp.float32)
    normed_grad = jnp.einsum(
        "re,de->rd", values_grad, value_back, preferred_element_type=jnp.float32
    )
    norm_first, first_pull = jax.vjp(rms_norm, tokens_flat, gain_back_one.astype(jnp.float32))
    token_part, gain_one_grad = first_pull(normed_grad)
    tokens_grad = residual_grad + token_part
    rand_flat = rand_grad.reshape(HEADS * LMAX, LMAX)
    all_shards = (
        lax.psum_scatter(rand_flat, ("wide", "narrow"), scatter_dimension=0, tiled=True),
        lax.psum_scatter(grad_value, ("wide", "narrow"), scatter_dimension=0, tiled=True),
        lax.psum_scatter(grad_outproj, ("wide", "narrow"), scatter_dimension=0, tiled=True),
        lax.psum_scatter(grad_up, ("wide", "narrow"), scatter_dimension=0, tiled=True),
        lax.psum_scatter(grad_down, ("wide", "narrow"), scatter_dimension=0, tiled=True),
        lax.psum_scatter(gain_one_grad, ("wide", "narrow"), scatter_dimension=0, tiled=True),
        lax.psum_scatter(gain_two_grad, ("wide", "narrow"), scatter_dimension=0, tiled=True),
    )
    rand_shard, value_shard, outproj_shard, up_shard, down_shard, gain_one_shard, gain_two_shard = (
        all_shards
    )
    return (
        output.reshape(item_count, LMAX, width),
        tokens_grad.reshape(item_count, LMAX, width),
        rand_shard,
        value_shard,
        outproj_shard,
        up_shard,
        down_shard,
        gain_one_shard,
        gain_two_shard,
    )


def solution(mesh):
    in_specs = (
        P(("wide", "narrow"), None, None),
        P(("wide", "narrow")),
        P(("wide", "narrow"), None),
        P(("wide", "narrow"), None),
        P(("wide", "narrow"), None),
        P(("wide", "narrow"), None),
        P(("wide", "narrow"), None),
        P(("wide", "narrow")),
        P(("wide", "narrow")),
        P(("wide", "narrow"), None, None),
    )
    out_specs = (
        P(("wide", "narrow"), None, None),
        P(("wide", "narrow"), None, None),
        P(("wide", "narrow"), None),
        P(("wide", "narrow"), None),
        P(("wide", "narrow"), None),
        P(("wide", "narrow"), None),
        P(("wide", "narrow"), None),
        P(("wide", "narrow")),
        P(("wide", "narrow")),
    )
    fits = dict(mesh.shape) == {"wide": 16, "narrow": 2}
    return jax.shard_map(chip_shards if fits else shards, mesh=mesh, in_specs=in_specs, out_specs=out_specs, check_vma=False)
```

```python
from functools import partial

import jax
import jax.numpy as jnp
from jax import lax
from jax.experimental import pallas as pl
from jax.experimental.pallas import tpu as pltpu
from jax.sharding import PartitionSpec as P

HEADS = 12
HEAD = 64
LMAX = 1024
WIDTH = 768
FF = 3072
EPSILON = 1e-05

BOTH = ("wide", "narrow")
BF16 = jnp.bfloat16
F32 = jnp.float32
VMEM = 61 << 20
LESS = 34 << 20

SUBS = 6
RUNS = 8
HALF = 64
HROWS = RUNS * HALF
PLANES = 4
PHEADS = HEADS // PLANES
ROWS = 2 * LMAX
FSTEP = 768
FSIDE = FF // 2 // FSTEP
TILE = 512
SIDE = WIDTH // 2
SPAN = 2 * HALF


def dot(a, b, ca, cb):
    return lax.dot_general(a, b, (((ca,), (cb,)), ((), ())), preferred_element_type=F32)


CORE, PLANE, PLACE, LENGTHS = 0, 1, 2, 3


def spec(shape, index):
    return pl.BlockSpec(shape, index)


def held(shape):
    zeros = (0,) * len(shape)
    return pl.BlockSpec(shape, lambda *_: zeros, pipeline_mode=pl.Buffered(1))


def params(limit):
    return pltpu.CompilerParams(vmem_limit_bytes=limit)


def whole_weight(sc, step, own, far, weight):
    @pl.when(step == 0)
    def _():
        weight[:, pl.ds(pl.multiple_of(sc[CORE] * SIDE, 128), SIDE)] = own[...]
        weight[:, pl.ds(pl.multiple_of((1 - sc[CORE]) * SIDE, 128), SIDE)] = far[...]


def values_kernel(sc, tok, gain, w_own, w_far, out, weight):
    step = pl.program_id(0)
    whole_weight(sc, step, w_own, w_far, weight)
    rows = tok.shape[1]
    position = step * rows + lax.broadcasted_iota(jnp.int32, (rows, 1), 0)
    for item in range(2):
        x = tok[item].astype(F32)
        scale = lax.rsqrt(jnp.mean(x * x, axis=-1, keepdims=True) + EPSILON)
        normed = (x * scale * gain[...]).astype(BF16)
        found = dot(normed, weight[...], 1, 0)
        found = jnp.where(position < sc[LENGTHS + item], found, 0.0).astype(BF16)
        for head in range(HEADS):
            out[head, :, item * HEAD : (item + 1) * HEAD] = found[:, head * HEAD : (head + 1) * HEAD]


def run_values(sc, tokens, gain, w_own, w_far):
    rows = 256
    return pl.pallas_call(
        values_kernel,
        grid_spec=pltpu.PrefetchScalarGridSpec(
            num_scalar_prefetch=1,
            grid=(LMAX // rows,),
            in_specs=[
                spec((2, rows, WIDTH), lambda j, s: (0, j, 0)),
                held((1, WIDTH)),
                held((WIDTH, SIDE)),
                held((WIDTH, SIDE)),
            ],
            out_specs=spec((HEADS, rows, 2 * HEAD), lambda j, s: (0, j, 0)),
            scratch_shapes=[pltpu.VMEM((WIDTH, WIDTH), BF16)],
        ),
        out_shape=jax.ShapeDtypeStruct((HEADS, LMAX, 2 * HEAD), BF16),
        compiler_params=params(VMEM),
        cost_estimate=pl.CostEstimate(
            flops=2 * 2 * LMAX * WIDTH * WIDTH, bytes_accessed=8 * LMAX * WIDTH, transcendentals=0
        ),
        name="values",
    )(sc, tokens, gain, w_own, w_far)


def lane_lengths(sc, shape):
    slot = lax.broadcasted_iota(jnp.int32, shape, 1) // HEAD
    length = jnp.where(slot == 0, sc[LENGTHS], sc[LENGTHS + 1])
    return jnp.where(slot >= 2, jnp.where(slot == 2, sc[LENGTHS + 2], sc[LENGTHS + 3]), length)


def plane_of(k, sc):
    return lax.rem(sc[PLANE] + PLANES - k, PLANES)


def plane_spec(planes, rows, lanes):
    def index(step, sc):
        return (plane_of(planes[0] + step * (planes[-1] - planes[0]) // max(len(planes) - 1, 1), sc), 0, 0)

    return spec((PHEADS, rows, lanes), index)


def anywhere(count):
    return [pl.BlockSpec(memory_space=pl.ANY)] * count


def plane_fetch(place, shards, raw, sems, slot):
    return [
        pltpu.make_async_copy(
            shards[4 * slot + rel],
            raw.at[slot, pl.ds(pl.multiple_of((place ^ rel) * SUBS * HALF, SUBS * HALF), SUBS * HALF)],
            sems.at[slot, rel],
        )
        for rel in range(4)
    ]


def take_plane(place, shards, raw, sems):
    step = pl.program_id(0)
    count = len(shards) // 4

    @pl.when(step == 0)
    def _():
        for slot in range(count):
            for copy in plane_fetch(place, shards, raw, sems, slot):
                copy.start()

    for slot in range(count):

        @pl.when(step == slot)
        def _():
            for copy in plane_fetch(place, shards, raw, sems, slot):
                copy.wait()

    return step


def head_rows(head):
    return slice(head * HROWS, (head + 1) * HROWS)


def fill_mask(sc, mask):
    @pl.when(pl.program_id(0) == 0)
    def _():
        shape = (LMAX, 4 * HEAD)
        column = lax.broadcasted_iota(jnp.int32, shape, 0)
        mask[...] = (column < lane_lengths(sc, shape)).astype(F32).astype(BF16)


def mix_kernel(count, carried, sc, *refs):
    shards, (v_own, v_far, *rest) = refs[: 4 * count], refs[4 * count :]
    mixed, mean, exps, inverse, raw, mask, sems = rest[4:] if carried else rest
    fill_mask(sc, mask)
    slot = take_plane(sc[PLACE], shards, raw, sems)
    shape = (HROWS, 4 * HEAD)
    line = lax.broadcasted_iota(jnp.int32, shape, 0)
    position = 128 * (line // HALF) + HALF * sc[CORE] + line % HALF
    valid = position < lane_lengths(sc, shape)
    for head in range(PHEADS):
        weights = jnp.exp(raw[slot, head_rows(head)].astype(F32)).astype(BF16)
        exps[head] = weights
        both = dot(weights, jnp.concatenate([v_own[head], v_far[head], mask[...]], axis=1), 1, 0)
        flip = jnp.where(valid, 1.0 / both[:, 4 * HEAD :], 0.0)
        found = both[:, : 4 * HEAD] * flip
        inverse[head] = flip.astype(BF16)
        mean[head] = found
        mixed[head] = found.astype(BF16)


def run_mix(sc, planes, shards, v_own, v_far, carry):
    carry, count = list(carry), len(planes)
    shape = (HEADS, HROWS, 4 * HEAD)
    return pl.pallas_call(
        partial(mix_kernel, count, bool(carry)),
        grid_spec=pltpu.PrefetchScalarGridSpec(
            num_scalar_prefetch=1,
            grid=(count,),
            in_specs=anywhere(4 * count) + [plane_spec(planes, LMAX, 2 * HEAD)] * 2 + anywhere(len(carry)),
            out_specs=[
                plane_spec(planes, HROWS, 4 * HEAD),
                plane_spec(planes, HROWS, 4 * HEAD),
                plane_spec(planes, HROWS, LMAX),
                plane_spec(planes, HROWS, 4 * HEAD),
            ],
            scratch_shapes=[
                pltpu.VMEM((count, 4 * SUBS * HALF, LMAX), BF16),
                pltpu.VMEM((LMAX, 4 * HEAD), BF16),
                pltpu.SemaphoreType.DMA((count, 4)),
            ],
        ),
        out_shape=[
            jax.ShapeDtypeStruct(shape, BF16),
            jax.ShapeDtypeStruct(shape, F32),
            jax.ShapeDtypeStruct((HEADS, HROWS, LMAX), BF16),
            jax.ShapeDtypeStruct(shape, BF16),
        ],
        input_output_aliases={3 + 4 * count + i: i for i in range(len(carry))},
        compiler_params=params(VMEM),
        cost_estimate=pl.CostEstimate(
            flops=2 * HEADS * HROWS * LMAX * 4 * HEAD,
            bytes_accessed=HEADS * (2 * HROWS * LMAX + 5 * HROWS * 256),
            transcendentals=HEADS * HROWS * LMAX // 2,
        ),
        name="mix",
    )(sc, *shards, v_own, v_far, *carry)


def row_valid(sc, step):
    line = lax.broadcasted_iota(jnp.int32, (4 * SPAN, 1), 0)
    item = line // SPAN
    row = step * SPAN + line % SPAN
    low = jnp.where(item == 0, sc[LENGTHS], sc[LENGTHS + 1])
    high = jnp.where(item == 2, sc[LENGTHS + 2], sc[LENGTHS + 3])
    return 128 * (row // HALF) + HALF * sc[CORE] + row % HALF < jnp.where(item >= 2, high, low)


def four_items(own, far):
    return jnp.concatenate([own[:, :, 0], far[...]], axis=0).reshape(4 * SPAN, WIDTH)


def pre_kernel(sc, tok, tok_far, heads, wo_own, wo_far, gain, mixed, resid, normed, weight):
    step = pl.program_id(0)
    whole_weight(sc, step, wo_own, wo_far, weight)
    for item in range(4):
        lanes = slice(item * HEAD, (item + 1) * HEAD)
        for pair in range(HEADS // 2):
            both = jnp.concatenate([heads[2 * pair, :, lanes], heads[2 * pair + 1, :, lanes]], axis=1)
            mixed[item, :, pair * 128 : (pair + 1) * 128] = both
    res = four_items(tok, tok_far).astype(F32) + dot(mixed[...].reshape(4 * SPAN, WIDTH), weight[...], 1, 0)
    resid[...] = res.astype(BF16).reshape(4, SPAN, WIDTH)
    scale = lax.rsqrt(jnp.mean(res * res, axis=-1, keepdims=True) + EPSILON)
    valid = row_valid(sc, step)
    normed[...] = jnp.where(valid, res * scale * gain[...], 0.0).astype(BF16).reshape(4, SPAN, WIDTH)


def slab_spec(items=4):
    return spec((items, SPAN, WIDTH), lambda r, s: (0, r, 0))


def half_specs():
    return [
        spec((2, SPAN // HALF, 1, HALF, WIDTH), lambda r, s: (0, r, s[CORE], 0, 0)),
        spec((2, SPAN // HALF, HALF, WIDTH), lambda r, s: (0, r, 0, 0)),
    ]


def heads_spec():
    return spec((HEADS, SPAN, 4 * HEAD), lambda r, s: (0, r, 0))


def run_pre(sc, tokens, tokens_far, heads, wo, gain):
    return pl.pallas_call(
        pre_kernel,
        grid_spec=pltpu.PrefetchScalarGridSpec(
            num_scalar_prefetch=1,
            grid=(HROWS // SPAN,),
            in_specs=half_specs()
            + [heads_spec(), held((WIDTH, SIDE)), held((WIDTH, SIDE)), held((1, WIDTH))],
            out_specs=[slab_spec()] * 3,
            scratch_shapes=[pltpu.VMEM((WIDTH, WIDTH), BF16)],
        ),
        out_shape=[
            jax.ShapeDtypeStruct((4, HROWS, WIDTH), BF16),
            jax.ShapeDtypeStruct((4, HROWS, WIDTH), BF16),
            jax.ShapeDtypeStruct((4, HROWS, WIDTH), BF16),
        ],
        compiler_params=params(VMEM),
        cost_estimate=pl.CostEstimate(
            flops=2 * ROWS * WIDTH * WIDTH, bytes_accessed=16 * ROWS * WIDTH, transcendentals=0
        ),
        name="pre",
    )(sc, tokens, tokens_far, heads, *wo, gain)


def masked_kernel(sc, cot, cot_far, masked):
    value = jnp.where(row_valid(sc, pl.program_id(0)), four_items(cot, cot_far).astype(F32), 0.0)
    masked[...] = value.astype(BF16).reshape(4, SPAN, WIDTH)


def run_masked(sc, cotangent, cotangent_far):
    return pl.pallas_call(
        masked_kernel,
        grid_spec=pltpu.PrefetchScalarGridSpec(
            num_scalar_prefetch=1, grid=(HROWS // SPAN,), in_specs=half_specs(), out_specs=slab_spec()
        ),
        out_shape=jax.ShapeDtypeStruct((4, HROWS, WIDTH), BF16),
        compiler_params=params(VMEM),
        cost_estimate=pl.CostEstimate(flops=0, bytes_accessed=4 * ROWS * WIDTH, transcendentals=0),
        name="masked",
    )(sc, cotangent, cotangent_far)


def own_lanes(sc):
    return pl.ds(pl.multiple_of(sc[CORE] * SIDE, 128), SIDE)


def far_lanes(sc):
    return pl.ds(pl.multiple_of((1 - sc[CORE]) * SIDE, 128), SIDE)


def unit_rows(f, sc):
    return (lax.rem(FSIDE * sc[CORE] + f, 2 * FSIDE), 0)


def unit_columns(f, sc):
    return (0, lax.rem(FSIDE * sc[CORE] + f, 2 * FSIDE))


def early(f, sc):
    return (0, lax.min(f, FSIDE - 1))


def late(f, sc):
    return (0, lax.max(f - FSIDE, 0))


def units_kernel(sc, normed, cot, up_own, up_far, dn_own, dn_far, active, up_grad, w_up, w_down):
    step = pl.program_id(0)
    w_down[:, own_lanes(sc)] = dn_own[...]
    w_down[:, far_lanes(sc)] = dn_far[...]

    @pl.when(step < FSIDE)
    def _():
        w_up[...] = up_own[...]

    @pl.when(step >= FSIDE)
    def _():
        w_up[...] = up_far[...]

    for row in range(0, ROWS, 256):
        rows = slice(row, row + 256)
        for column in range(0, FSTEP, 256):
            columns = slice(column, column + 256)
            up = dot(normed[rows], w_up[:, columns], 1, 0)
            square = up * up
            bend = jnp.tanh(up * (0.7978845608028654 + (0.044715 * 0.7978845608028654) * square))
            share = 0.5 + 0.5 * bend
            act = up * share
            active[rows, columns] = act.astype(BF16)
            slope = share + act * (1.0 - share) * (
                2 * 0.7978845608028654 + (6 * 0.044715 * 0.7978845608028654) * square
            )
            up_grad[rows, columns] = (dot(cot[rows], w_down[columns], 1, 1) * slope).astype(BF16)


def run_units(sc, normed, cotangent, up, down):
    return pl.pallas_call(
        units_kernel,
        grid_spec=pltpu.PrefetchScalarGridSpec(
            num_scalar_prefetch=1,
            grid=(2 * FSIDE,),
            in_specs=[
                held((ROWS, WIDTH)),
                held((ROWS, WIDTH)),
                spec((WIDTH, FSTEP), early),
                spec((WIDTH, FSTEP), late),
                spec((FSTEP, SIDE), unit_rows),
                spec((FSTEP, SIDE), unit_rows),
            ],
            out_specs=[spec((ROWS, FSTEP), unit_columns), spec((ROWS, FSTEP), unit_columns)],
            scratch_shapes=[pltpu.VMEM((WIDTH, FSTEP), BF16), pltpu.VMEM((FSTEP, WIDTH), BF16)],
        ),
        out_shape=[jax.ShapeDtypeStruct((ROWS, FF), BF16), jax.ShapeDtypeStruct((ROWS, FF), BF16)],
        compiler_params=params(VMEM),
        cost_estimate=pl.CostEstimate(
            flops=4 * ROWS * WIDTH * FF, bytes_accessed=6 * ROWS * WIDTH + 4 * ROWS * FF, transcendentals=ROWS * FF
        ),
        name="units",
    )(sc, normed.reshape(ROWS, WIDTH), cotangent.reshape(ROWS, WIDTH), *up, *down)


def down_grad_kernel(sc, active, cot, own, far, total):
    total[...] = dot(active[...], cot[...], 0, 0).astype(BF16)
    own[...] = total[:, own_lanes(sc)]
    far[...] = total[:, far_lanes(sc)]


def run_down_grad(sc, active, cotangent):
    return pl.pallas_call(
        down_grad_kernel,
        grid_spec=pltpu.PrefetchScalarGridSpec(
            num_scalar_prefetch=1,
            grid=(FF // 512,),
            in_specs=[spec((ROWS, 512), lambda f, s: (0, f)), held((ROWS, WIDTH))],
            out_specs=[spec((512, SIDE), lambda f, s: (f, 0))] * 2,
            scratch_shapes=[pltpu.VMEM((512, WIDTH), BF16)],
        ),
        out_shape=[jax.ShapeDtypeStruct((FF, SIDE), BF16)] * 2,
        compiler_params=params(VMEM),
        cost_estimate=pl.CostEstimate(
            flops=2 * ROWS * WIDTH * FF, bytes_accessed=2 * ROWS * (WIDTH + FF), transcendentals=0
        ),
        name="down_grad",
    )(sc, active, cotangent.reshape(ROWS, WIDTH))


def up_grad_kernel(sc, normed, up_grad, own, far):
    total = dot(normed[...], up_grad[...], 0, 0).astype(BF16)

    @pl.when(pl.program_id(0) < 3)
    def _():
        own[...] = total

    @pl.when(pl.program_id(0) >= 3)
    def _():
        far[...] = total


def run_up_grad(sc, normed, up_grad):
    return pl.pallas_call(
        up_grad_kernel,
        grid_spec=pltpu.PrefetchScalarGridSpec(
            num_scalar_prefetch=1,
            grid=(6,),
            in_specs=[held((ROWS, WIDTH)), spec((ROWS, 512), lambda f, s: (0, lax.rem(3 * s[CORE] + f, 6)))],
            out_specs=[
                spec((WIDTH, 512), lambda f, s: (0, lax.min(f, 2))),
                spec((WIDTH, 512), lambda f, s: (0, lax.max(f - 3, 0))),
            ],
        ),
        out_shape=[jax.ShapeDtypeStruct((WIDTH, FF // 2), BF16)] * 2,
        compiler_params=params(VMEM),
        cost_estimate=pl.CostEstimate(
            flops=2 * ROWS * WIDTH * FF, bytes_accessed=2 * ROWS * (WIDTH + FF), transcendentals=0
        ),
        name="up_grad",
    )(sc, normed.reshape(ROWS, WIDTH), up_grad)


def out_grad_kernel(sc, mixed, res_own, res_far, own, far, total):
    step = pl.program_id(0)
    grad = jnp.concatenate([res_own[...], res_far[...]], axis=0).reshape(4 * SPAN, WIDTH)
    found = dot(mixed[...].reshape(4 * SPAN, WIDTH), grad, 0, 0)

    @pl.when(step == 0)
    def _():
        total[...] = found

    @pl.when(step > 0)
    def _():
        total[...] += found

    @pl.when(step == pl.num_programs(0) - 1)
    def _():
        own[...] = total[:, own_lanes(sc)].astype(BF16)
        far[...] = total[:, far_lanes(sc)].astype(BF16)


def run_out_grad(sc, mixed, res_own, res_far):
    return pl.pallas_call(
        out_grad_kernel,
        grid_spec=pltpu.PrefetchScalarGridSpec(
            num_scalar_prefetch=1,
            grid=(HROWS // SPAN,),
            in_specs=[slab_spec(), slab_spec(2), slab_spec(2)],
            out_specs=[held((WIDTH, SIDE))] * 2,
            scratch_shapes=[pltpu.VMEM((WIDTH, WIDTH), F32)],
        ),
        out_shape=[jax.ShapeDtypeStruct((WIDTH, SIDE), BF16)] * 2,
        compiler_params=params(VMEM),
        cost_estimate=pl.CostEstimate(
            flops=2 * ROWS * WIDTH * WIDTH, bytes_accessed=4 * ROWS * WIDTH, transcendentals=0
        ),
        name="out_grad",
    )(sc, mixed, res_own, res_far)


def out_kernel(sc, active, resid, dn_own, dn_far, own, far, w_down):
    step = pl.program_id(0)

    @pl.when(step == 0)
    def _():
        w_down[:, own_lanes(sc)] = dn_own[...]
        w_down[:, far_lanes(sc)] = dn_far[...]

    branch = dot(active[...].reshape(4 * SPAN, FF), w_down[...], 1, 0)
    output = jnp.where(row_valid(sc, step), resid[...].reshape(4 * SPAN, WIDTH).astype(F32) + branch, 0.0)
    output = output.astype(BF16).reshape(4, SPAN, WIDTH)
    own[...] = output[:2]
    far[...] = output[2:]


def run_out(sc, active, resid, down):
    return pl.pallas_call(
        out_kernel,
        grid_spec=pltpu.PrefetchScalarGridSpec(
            num_scalar_prefetch=1,
            grid=(HROWS // SPAN,),
            in_specs=[
                spec((4, SPAN, FF), lambda r, s: (0, r, 0)),
                slab_spec(),
                held((FF, SIDE)),
                held((FF, SIDE)),
            ],
            out_specs=[slab_spec(2)] * 2,
            scratch_shapes=[pltpu.VMEM((FF, WIDTH), BF16)],
        ),
        out_shape=[
            jax.ShapeDtypeStruct((2, HROWS, WIDTH), BF16),
            jax.ShapeDtypeStruct((2, HROWS, WIDTH), BF16),
        ],
        compiler_params=params(VMEM),
        cost_estimate=pl.CostEstimate(
            flops=2 * ROWS * WIDTH * FF, bytes_accessed=ROWS * (2 * FF + 7 * WIDTH), transcendentals=0
        ),
        name="out",
    )(sc, active.reshape(4, HROWS, FF), resid, *down)


def post_kernel(sc, resid, grad_own, grad_far, cot, up_own, up_far, wo_own, wo_far, gain, *refs):
    (res_own, res_far, heads, d_gain, weight, spread) = refs
    step = pl.program_id(0)
    whole_weight(sc, step, wo_own, wo_far, weight)
    shape, slab = (4 * SPAN, WIDTH), (4, SPAN, WIDTH)
    valid = row_valid(sc, step)
    res = resid[...].reshape(shape).astype(F32)
    scale = lax.rsqrt(jnp.mean(res * res, axis=-1, keepdims=True) + EPSILON)
    unit = res * scale
    units = (4 * SPAN, FF // 2)
    back = dot(grad_own[...].reshape(units), up_own[...], 1, 1) + dot(grad_far[...].reshape(units), up_far[...], 1, 1)
    two_grad = jnp.where(valid, back, 0.0)
    gained = two_grad * gain[...]
    masked = cot[...].reshape(shape).astype(F32)
    grad = masked + scale * (gained - unit * jnp.mean(gained * unit, axis=-1, keepdims=True))
    low = grad.astype(BF16)
    res_own[...] = low.reshape(slab)[:2]
    res_far[...] = low.reshape(slab)[2:]
    gain_sum = jnp.sum(two_grad * unit, axis=0, keepdims=True)

    @pl.when(step == 0)
    def _():
        d_gain[...] = gain_sum

    @pl.when(step > 0)
    def _():
        d_gain[...] += gain_sum

    spread[...] = dot(low, weight[...], 1, 1).astype(BF16).reshape(slab)
    for pair in range(HEADS // 2):
        lanes = slice(pair * 128, (pair + 1) * 128)
        for side in range(2):
            one, two = spread[2 * side, :, lanes], spread[2 * side + 1, :, lanes]
            half = slice(side * 128, (side + 1) * 128)
            heads[2 * pair, :, half] = jnp.concatenate([one[:, :HEAD], two[:, :HEAD]], axis=1)
            heads[2 * pair + 1, :, half] = jnp.concatenate([one[:, HEAD:], two[:, HEAD:]], axis=1)


def run_post(sc, resid, up_grad, cotangent, up, wo, gain):
    side = lambda which: spec((4, SPAN, FF // 2), lambda r, s: (0, r, s[CORE] if which == 0 else 1 - s[CORE]))
    up_grad = up_grad.reshape(4, HROWS, FF)
    return pl.pallas_call(
        post_kernel,
        grid_spec=pltpu.PrefetchScalarGridSpec(
            num_scalar_prefetch=1,
            grid=(HROWS // SPAN,),
            in_specs=[
                slab_spec(),
                side(0),
                side(1),
                slab_spec(),
                held((WIDTH, FF // 2)),
                held((WIDTH, FF // 2)),
                held((WIDTH, SIDE)),
                held((WIDTH, SIDE)),
                held((1, WIDTH)),
            ],
            out_specs=[slab_spec(2)] * 2 + [heads_spec(), held((1, WIDTH))],
            scratch_shapes=[
                pltpu.VMEM((WIDTH, WIDTH), BF16),
                pltpu.VMEM((4, SPAN, WIDTH), BF16),
            ],
        ),
        out_shape=[
            jax.ShapeDtypeStruct((2, HROWS, WIDTH), BF16),
            jax.ShapeDtypeStruct((2, HROWS, WIDTH), BF16),
            jax.ShapeDtypeStruct((HEADS, HROWS, 4 * HEAD), BF16),
            jax.ShapeDtypeStruct((1, WIDTH), F32),
        ],
        compiler_params=params(VMEM),
        cost_estimate=pl.CostEstimate(
            flops=2 * ROWS * WIDTH * (WIDTH + FF), bytes_accessed=ROWS * (16 * WIDTH + 2 * FF), transcendentals=0
        ),
        name="post",
    )(sc, resid, up_grad, up_grad, cotangent, *up, *wo, gain)


def unmix_kernel(count, carried, sc, v_own, v_far, grad_heads, mean, exps, inverse, *refs):
    refs = refs[2:] if carried else refs
    outs, (own, far, grads, mask, adder, bound, out_sems) = refs[: 4 * count], refs[4 * count :]
    place = sc[PLACE]
    step = pl.program_id(0)

    def leave(slot):
        return [
            pltpu.make_async_copy(
                grads.at[slot, pl.ds(pl.multiple_of((place ^ rel) * SUBS * HALF, SUBS * HALF), SUBS * HALF)],
                outs[4 * slot + rel],
                out_sems.at[slot, rel],
            )
            for rel in range(4)
        ]

    fill_mask(sc, mask)

    @pl.when(step == 0)
    def _():
        lane = lax.broadcasted_iota(jnp.int32, (4 * HEAD, 128), 0) // HEAD
        column = lax.broadcasted_iota(jnp.int32, (4 * HEAD, 128), 1)
        adder[...] = jnp.where((lane == column) | (lane + 4 == column), -1.0, 0.0).astype(BF16)
        row = lax.broadcasted_iota(jnp.int32, (LMAX, 128), 0)
        item = lax.broadcasted_iota(jnp.int32, (LMAX, 128), 1)
        length = jnp.where(item % 4 == 0, sc[LENGTHS], sc[LENGTHS + 1])
        length = jnp.where(item % 4 == 2, sc[LENGTHS + 2], length)
        length = jnp.where(item % 4 == 3, sc[LENGTHS + 3], length)
        bound[...] = jnp.where((item < 8) & (row < length), 1.0, 0.0).astype(BF16)

    high_lanes = lax.broadcasted_iota(jnp.int32, (HROWS, 128), 1) < 4
    for head in range(PHEADS):
        weights = exps[head]
        low = (grad_heads[head].astype(F32) * inverse[head].astype(F32)).astype(BF16)
        product = low.astype(F32) * mean[head]
        coarse = product.astype(BF16)
        fine = (product - coarse.astype(F32)).astype(BF16)
        delta = dot(coarse, adder[...], 1, 0) + dot(fine, adder[...], 1, 0)
        coarse = delta.astype(BF16)
        fine = (delta - coarse.astype(F32)).astype(BF16)
        left = jnp.concatenate([low, jnp.where(high_lanes, coarse, fine)], axis=1)
        score = dot(left, jnp.concatenate([v_own[head], v_far[head], bound[...]], axis=1), 1, 1)
        grads[step, head_rows(head)] = (score * weights.astype(F32)).astype(BF16)
        back = (dot(weights, low, 0, 0) * mask[...].astype(F32)).astype(BF16)
        own[head] = back[:, : 2 * HEAD]
        far[head] = back[:, 2 * HEAD :]
    for which in range(count):

        @pl.when(step == which)
        def _():
            for copy in leave(which):
                copy.start()
            if which == count - 1:
                for slot in range(count):
                    for copy in leave(slot):
                        copy.wait()


def run_unmix(sc, planes, v_own, v_far, grad_heads, mean, exps, inverse, carry):
    carry, count = list(carry), len(planes)
    return pl.pallas_call(
        partial(unmix_kernel, count, bool(carry)),
        grid_spec=pltpu.PrefetchScalarGridSpec(
            num_scalar_prefetch=1,
            grid=(count,),
            in_specs=[
                plane_spec(planes, LMAX, 2 * HEAD),
                plane_spec(planes, LMAX, 2 * HEAD),
                plane_spec(planes, HROWS, 4 * HEAD),
                plane_spec(planes, HROWS, 4 * HEAD),
                plane_spec(planes, HROWS, LMAX),
                plane_spec(planes, HROWS, 4 * HEAD),
            ]
            + anywhere(len(carry)),
            out_specs=anywhere(4 * count) + [plane_spec(planes, LMAX, 2 * HEAD)] * 2,
            scratch_shapes=[
                pltpu.VMEM((count, 4 * SUBS * HALF, LMAX), BF16),
                pltpu.VMEM((LMAX, 4 * HEAD), BF16),
                pltpu.VMEM((4 * HEAD, 128), BF16),
                pltpu.VMEM((LMAX, 128), BF16),
                pltpu.SemaphoreType.DMA((count, 4)),
            ],
        ),
        out_shape=[jax.ShapeDtypeStruct((SUBS * HALF, LMAX), BF16)] * (4 * count)
        + [jax.ShapeDtypeStruct((HEADS, LMAX, 2 * HEAD), BF16)] * 2,
        input_output_aliases={7 + i: 4 * count + i for i in range(len(carry))},
        compiler_params=params(VMEM),
        cost_estimate=pl.CostEstimate(
            flops=3 * HEADS * HROWS * LMAX * 4 * HEAD,
            bytes_accessed=HEADS * (2 * HROWS * LMAX + 5 * HROWS * 256 + 4 * LMAX * 256),
            transcendentals=0,
        ),
        name="unmix",
    )(sc, v_own, v_far, grad_heads, mean, exps, inverse, *carry)


def close_kernel(sc, tok, res_own, res_got, out_own, out_got, own, far, gain, w_own, w_far, *refs):
    (output, tok_grad, d_value, d_gain, total, weight) = refs
    step = pl.program_id(0)
    whole_weight(sc, step, w_own, w_far, weight)
    core = sc[CORE]
    output[:, :, core] = out_own[...].astype(F32)
    output[:, :, 1 - core] = out_got[...].astype(F32)
    tok_grad[:, :, core] = res_own[...].astype(F32)
    tok_grad[:, :, 1 - core] = res_got[...].astype(F32)
    runs = tok.shape[1]
    rows = runs * 128
    for item in range(2):
        lanes = slice(item * HEAD, (item + 1) * HEAD)
        pieces = [
            add_low(own[head, :, lanes], far[head, :, lanes]) for head in range(HEADS)
        ]
        back = jnp.concatenate(pieces, axis=1)
        x = tok[item].reshape(rows, WIDTH).astype(F32)
        scale = lax.rsqrt(jnp.mean(x * x, axis=-1, keepdims=True) + EPSILON)
        unit = x * scale
        normed = (unit * gain[...]).astype(BF16)
        normed_grad = dot(back, weight[...], 1, 1)
        gained = normed_grad * gain[...]
        update = scale * (gained - unit * jnp.mean(gained * unit, axis=-1, keepdims=True))
        tok_grad[item] += update.reshape(runs, 2, HALF, WIDTH)
        gain_sum = jnp.sum(normed_grad * unit, axis=0, keepdims=True)
        value_sum = dot(normed, back, 0, 0)
        if item == 0:
            gain_total, value_total = gain_sum, value_sum
        else:
            gain_total, value_total = gain_total + gain_sum, value_total + value_sum

    @pl.when(step == 0)
    def _():
        d_gain[...] = gain_total
        total[...] = value_total

    @pl.when(step > 0)
    def _():
        d_gain[...] += gain_total
        total[...] += value_total

    @pl.when(step == pl.num_programs(0) - 1)
    def _():
        low = total[...].astype(BF16)
        d_value[0] = low[:, :SIDE]
        d_value[1] = low[:, SIDE:]


def run_close(sc, tokens, res_own, res_got, out_own, out_got, own, far, gain, w_own, w_far):
    runs = 2
    slab = (2, RUNS, 2, HALF, WIDTH)
    half = (2, RUNS, HALF, WIDTH)
    whole_spec = spec((2, runs, 2, HALF, WIDTH), lambda j, s: (0, j, 0, 0, 0))
    half_spec = spec((2, runs, HALF, WIDTH), lambda j, s: (0, j, 0, 0))
    back_spec = spec((HEADS, runs * 128, 2 * HEAD), lambda j, s: (0, j, 0))
    return pl.pallas_call(
        close_kernel,
        grid_spec=pltpu.PrefetchScalarGridSpec(
            num_scalar_prefetch=1,
            grid=(RUNS // runs,),
            in_specs=[whole_spec]
            + [half_spec] * 4
            + [back_spec, back_spec, held((1, WIDTH)), held((WIDTH, SIDE)), held((WIDTH, SIDE))],
            out_specs=[whole_spec, whole_spec, held((2, WIDTH, SIDE)), held((1, WIDTH))],
            scratch_shapes=[pltpu.VMEM((WIDTH, WIDTH), F32), pltpu.VMEM((WIDTH, WIDTH), BF16)],
        ),
        out_shape=[
            jax.ShapeDtypeStruct(slab, F32),
            jax.ShapeDtypeStruct(slab, F32),
            jax.ShapeDtypeStruct((2, WIDTH, SIDE), BF16),
            jax.ShapeDtypeStruct((1, WIDTH), F32),
        ],
        compiler_params=params(VMEM),
        cost_estimate=pl.CostEstimate(
            flops=4 * 2 * LMAX * WIDTH * WIDTH, bytes_accessed=38 * LMAX * WIDTH, transcendentals=0
        ),
        name="close",
    )(
        sc,
        tokens.reshape(slab),
        *(x.reshape(half) for x in (res_own, res_got, out_own, out_got)),
        own,
        far,
        gain,
        w_own,
        w_far,
    )


PACK_DOWN, PACK_UP, PACK_OUT, PACK_VALUE, PACK_GAIN, PACK = 0, 192, 384, 432, 480, 496


def pack_kernel(sc, down, up, out, value, gain, down_far, up_far, out_far, value_far, gain_far, packed):
    first = sc[CORE] == 0

    def both(own, far, lanes):
        own, far = own[:, lanes], far[:, lanes]
        return jnp.concatenate([jnp.where(first, own, far), jnp.where(first, far, own)], axis=0)

    def side(own, far):
        return both(own, far, own_lanes(sc))

    packed[PACK_DOWN:PACK_UP] = side(down, down_far)
    for j in range(4):
        lanes = pl.ds(pl.multiple_of((4 * sc[CORE] + j) * SIDE, 128), SIDE)
        packed[PACK_UP + 48 * j : PACK_UP + 48 * (j + 1)] = both(up, up_far, lanes)
    packed[PACK_OUT:PACK_VALUE] = side(out, out_far)
    packed[PACK_VALUE:PACK_GAIN] = side(value, value_far)
    packed[PACK_GAIN:] = both(gain, gain_far, slice(0, SIDE))


def run_pack(sc, own, far):
    return pl.pallas_call(
        pack_kernel,
        grid_spec=pltpu.PrefetchScalarGridSpec(
            num_scalar_prefetch=1,
            grid=(1,),
            in_specs=[held(x.shape) for x in (*own, *far)],
            out_specs=held((PACK, SIDE)),
        ),
        out_shape=jax.ShapeDtypeStruct((PACK, SIDE), BF16),
        compiler_params=params(VMEM),
        cost_estimate=pl.CostEstimate(flops=0, bytes_accessed=6 * PACK * SIDE, transcendentals=0),
        name="pack",
    )(sc, *own, *far)


def chip_of(sc, k, rel):
    return plane_of(k, sc) * 4 + (sc[PLACE] ^ rel)


def place_kernel(moves, sc, *refs):
    pieces, targets, sems = refs[:16], refs[16:-1], refs[-1]
    copies = []
    for index, piece in enumerate(pieces):
        chip = chip_of(sc, index // 4, index % 4)
        for which, (start, count, lane, target, step, offset, column) in enumerate(moves):
            rows = pl.ds(pl.multiple_of(chip * step + offset, 16), count)
            copies.append(
                pltpu.make_async_copy(
                    piece.at[pl.ds(start, count), pl.ds(lane, SIDE)],
                    targets[target].at[rows, pl.ds(column, SIDE)],
                    sems.at[index, which],
                )
            )
    for copy in copies:
        copy.start()
    for copy in copies:
        copy.wait()


def run_place(sc, pieces, moves, shapes):
    return pl.pallas_call(
        partial(place_kernel, moves),
        grid_spec=pltpu.PrefetchScalarGridSpec(
            num_scalar_prefetch=1,
            grid=(1,),
            in_specs=anywhere(16),
            out_specs=[held(shape) for shape in shapes],
            scratch_shapes=[pltpu.SemaphoreType.DMA((16, len(moves)))],
        ),
        out_shape=[jax.ShapeDtypeStruct(shape, BF16) for shape in shapes],
        compiler_params=params(VMEM),
        cost_estimate=pl.CostEstimate(
            flops=0, bytes_accessed=4 * sum(a * b for a, b in shapes), transcendentals=0
        ),
        name="place",
    )(sc, *pieces)


def place_weights(sc, pieces):
    moves = (
        (PACK_DOWN, 192, 0, 0, 192, 0, 0),
        *((PACK_UP + 48 * j, 48, 0, 1, 48, 0, j * SIDE) for j in range(4)),
        (PACK_OUT, 48, 0, 2, 48, 0, 0),
        (PACK_VALUE, 48, 0, 3, 48, 0, 0),
        (PACK_GAIN, 16, 0, 4, 16, 0, 0),
    )
    shapes = [(FF, SIDE), (WIDTH, FF // 2), (WIDTH, SIDE), (WIDTH, SIDE), (256, SIDE)]
    return run_place(sc, pieces, moves, shapes)


def collect_kernel(sc, *refs):
    outs = refs[24:]
    for k in range(PLANES):

        @pl.when(pl.program_id(0) == k)
        def _():
            for rel in range(4):
                down, down_got, up, up_got, out, out_got = refs[6 * rel : 6 * rel + 6]
                packed = outs[4 * k + rel]
                packed[PACK_DOWN:PACK_UP] = add_low(down[...], down_got[...])
                for j in range(4):
                    lanes = slice(j * SIDE, (j + 1) * SIDE)
                    packed[PACK_UP + 48 * j : PACK_UP + 48 * (j + 1)] = add_low(up[:, lanes], up_got[:, lanes])
                packed[PACK_OUT:PACK_VALUE] = add_low(out[...], out_got[...])


def run_collect(sc, *sides):
    def rows(x, rel):
        return spec((x.shape[0] // 16, x.shape[1]), lambda k, s: (chip_of(s, k, rel), 0))

    return pl.pallas_call(
        collect_kernel,
        grid_spec=pltpu.PrefetchScalarGridSpec(
            num_scalar_prefetch=1,
            grid=(PLANES,),
            in_specs=[rows(x, rel) for rel in range(4) for x in sides],
            out_specs=[held((PACK_VALUE, SIDE))] * 16,
        ),
        out_shape=[jax.ShapeDtypeStruct((PACK_VALUE, SIDE), BF16)] * 16,
        compiler_params=params(LESS),
        cost_estimate=pl.CostEstimate(flops=0, bytes_accessed=3 * 16 * PACK_VALUE * SIDE * 2, transcendentals=0),
        name="collect",
    )(sc, *(x for _ in range(4) for x in sides))


def add_kernel(groups, *refs):
    for group, total in zip(groups, refs[-len(groups) :]):
        value = refs[group[0]][...].astype(F32)
        for index in group[1:]:
            value = value + refs[index][...].astype(F32)
        total[...] = value.astype(total.dtype)


def run_add(groups, values, dtype):
    shape = values[0].shape
    here = pl.BlockSpec(memory_space=pltpu.VMEM)
    return pl.pallas_call(
        partial(add_kernel, groups),
        in_specs=[here] * len(values),
        out_specs=[here] * len(groups),
        out_shape=[jax.ShapeDtypeStruct(shape, dtype)] * len(groups),
        compiler_params=params(LESS),
        cost_estimate=pl.CostEstimate(
            flops=0, bytes_accessed=2 * shape[0] * shape[1] * (len(values) + len(groups)), transcendentals=0
        ),
        name="add",
    )(*values)


DEVICES = 32
TO_CORE, TO_X, TO_Y = 1, 2, 4


def swap(x, bit):
    return lax.ppermute(x, BOTH, [(d, d ^ bit) for d in range(DEVICES)])


def ring(x, way=1):
    return lax.ppermute(x, BOTH, [(d, (d + 8 * way) % DEVICES) for d in range(DEVICES)])


def pick(x, index, axis=0):
    return lax.dynamic_index_in_dim(x, index, axis, keepdims=False)


def ordered(flag, one, two, axis=0, joined=jnp.stack):
    return jnp.where(flag == 0, joined([one, two], axis), joined([two, one], axis))


def add_low(one, two):
    return (one.astype(F32) + two.astype(F32)).astype(BF16)


STEPS = (
    ((0, 0, 1), (0, 1, 0), (1, 0, 0)),
    ((1, 0, 1), (0, 1, 1), (2, 0, 0)),
    ((2, 0, 1), (1, 1, 0), (3, 0, 0)),
    ((1, 1, 1), (2, 1, 1), (2, 1, 0)),
    ((3, 0, 1), (3, 1, 0), (3, 1, 1)),
)


def gather_step(have, step):
    by_x, by_y, by_z = STEPS[step]
    return {
        **have,
        by_z: ring(have[by_z[0] - 1, by_z[1], by_z[2]]),
        by_x: swap(have[by_x[0], by_x[1], 0], TO_X),
        by_y: swap(have[by_y[0], 0, by_y[2]], TO_Y),
    }


def in_order(have):
    return [have[k, y, x] for k in range(4) for y in range(2) for x in range(2)]


def by_place(shares, planes=range(PLANES)):
    return {(k, i // 2, i % 2): shares[4 * at + i] for at, k in enumerate(planes) for i in range(4)}


def scatter_send(have, step):
    by_x, by_y, by_z = STEPS[len(STEPS) - 1 - step]
    got = (ring(have[by_z], -1), swap(have[by_x], TO_X), swap(have[by_y], TO_Y))
    return {at: value for at, value in have.items() if at not in (by_x, by_y, by_z)}, got


def scatter_add(have, got, step):
    by_x, by_y, by_z = STEPS[len(STEPS) - 1 - step]
    targets = ((by_z[0] - 1, by_z[1], by_z[2]), (by_x[0], by_x[1], 0), (by_y[0], 0, by_y[2]))
    sums = list(dict.fromkeys(targets))
    groups = [(len(got) + i, *(j for j in range(len(got)) if targets[j] == at)) for i, at in enumerate(sums)]
    values = [*got, *(have[at] for at in sums)]
    return {**have, **dict(zip(sums, run_add(groups, values, F32 if step == len(STEPS) - 1 else BF16)))}


together = lax.optimization_barrier


def chip_shards(tokens, lengths, rand_mix, w_value, w_out, w_up, w_down, gain_mix, gain_ffn, grad_out):
    wide = lax.axis_index("wide")
    core = lax.axis_index("narrow")
    z, y, x = wide // 4, (wide // 2) % 2, wide % 2
    other = lambda value: swap(value, TO_CORE)
    side = partial(ordered, core, joined=jnp.concatenate)
    slab = (2, RUNS, 2, HALF, WIDTH)
    tokens, grad_out = tokens.reshape(slab), grad_out.reshape(slab)

    gains = jnp.pad(jnp.concatenate([gain_mix, gain_ffn])[None], ((0, 7), (0, SIDE - 48)))
    own = (w_down, w_up, w_out, w_value, gains)
    far = tuple(other(value) for value in own)
    near_sc = jnp.concatenate([jnp.stack([core, z, wide % 4]).astype(jnp.int32), lengths, lengths])
    weights = {(0, 0, 0): run_pack(near_sc, own, far)}

    rand = rand_mix.reshape(3, 2, HALF, LMAX)
    blocks = side(pick(rand, core, 1), other(pick(rand, 1 - core, 1)), 0)
    weights, rands, late_tokens, late_grad = together(
        (gather_step(weights, 0), {(0, 0, 0): blocks.reshape(SUBS * HALF, LMAX)}, tokens, grad_out)
    )
    weights, tokens_far = together((gather_step(weights, 1), other(pick(late_tokens, 1 - core, 2))))
    weights, grad_far = together((gather_step(weights, 2), other(pick(late_grad, 1 - core, 2))))
    weights, far_lengths = together((gather_step(weights, 3), other(lengths)))
    sc = jnp.concatenate([near_sc[:5], far_lengths])
    weights, rands = together((gather_step(weights, 4), rands))

    rands = gather_step(rands, 0)
    down, up, out, value, gain_rows = place_weights(sc, in_order(weights))
    rands, value, value_far, gain_rows, out, down, up = together(
        (rands, value, other(value), gain_rows, out, down, up)
    )
    gain_rows = gain_rows.reshape(16, 2, 8, SIDE)[:, :, 0]
    gain_one = gain_rows[..., :24].reshape(1, WIDTH).astype(F32)
    gain_two = gain_rows[..., 24:48].reshape(1, WIDTH).astype(F32)
    rands = gather_step(rands, 1)
    v_own = run_values(sc, tokens.reshape(2, LMAX, WIDTH), gain_one, value, value_far)
    rands, v_own, out, down, up = together((rands, v_own, (out, other(out)), down, up))
    rands, v_own, v_far, grad_far, down, up = together(
        (gather_step(rands, 2), v_own, other(v_own), grad_far, down, up)
    )
    rands = gather_step(rands, 3)
    masked = run_masked(sc, grad_out, grad_far)
    rands, v_far, masked, down, up = together((rands, v_far, masked, down, up))
    near = [rands[k, y_at, x_at] for k in range(3) for y_at in range(2) for x_at in range(2)]
    rands = gather_step(rands, 4)
    mixing = run_mix(sc, (0, 1, 2), near, v_own, v_far, ())
    rands, down, up, mixing = together((rands, down, up, mixing))
    heads, mean, exps, inverse = run_mix(sc, (3,), in_order(rands)[12:], v_own, v_far, mixing)
    down, up = (down, other(down)), (up, other(up))

    mixed, resid, normed = run_pre(sc, tokens, tokens_far, heads, out, gain_two)
    active, up_grad = run_units(sc, normed, masked, up, down)
    res_own, res_far, grad_heads, d_gain_two = run_post(sc, resid, up_grad, masked, up, out, gain_two)

    backward = lambda planes, carry: run_unmix(sc, planes, v_own, v_far, grad_heads, mean, exps, inverse, carry)
    *far, back_own, back_far = backward((3,), ())
    far, back_own, back_far, res_got = together((far, back_own, back_far, other(res_far)))
    have, got = scatter_send(by_place(far, (3,)), 0)
    *near, back_own, back_far = backward((2, 1, 0), (back_own, back_far))
    have, got, near, back_own, back_far = together((have, got, near, back_own, back_far))
    have = scatter_add({**have, **by_place(near, (2, 1, 0))}, got, 0)

    have, got = scatter_send(have, 1)
    up_own, up_far = run_up_grad(sc, normed, up_grad)
    have, got, up_own, up_far, back_got = together((have, got, up_own, up_far, other(back_far)))
    have = scatter_add(have, got, 1)

    have, got = scatter_send(have, 2)
    down_own, down_far = run_down_grad(sc, active, masked)
    have, got, down_own, down_far, up_got = together((have, got, down_own, down_far, other(up_far)))
    have = scatter_add(have, got, 2)

    have, got = scatter_send(have, 3)
    d_out_own, d_out_far = run_out_grad(sc, mixed, res_own, res_far)
    packed = run_collect(sc, down_own, other(down_far), up_own, up_got, d_out_own, other(d_out_far))
    have, got, packed = together((have, got, packed))
    have = scatter_add(have, got, 3)

    have, got = scatter_send(have, 4)
    sums, sums_got = scatter_send(by_place(packed), 0)
    out_own, out_far = run_out(sc, active, resid, down)
    have, got, sums, sums_got, out_own, out_far = together((have, got, sums, sums_got, out_own, out_far))
    rand_sum = scatter_add(have, got, 4)[0, 0, 0].reshape(2, 3, HALF, LMAX)

    sums, got = scatter_send(scatter_add(sums, sums_got, 0), 1)
    output, tokens_grad, d_value, d_gain_one = run_close(
        sc, tokens, res_own, res_got, out_own, other(out_far), back_own, back_got, gain_one, value, value_far
    )
    gain_pair = jnp.concatenate([d_gain_one, d_gain_two]).reshape(2, 16, 1, 48).astype(BF16)
    gain_pair = jnp.pad(gain_pair, ((0, 0), (0, 0), (0, 15), (0, SIDE - 48)))
    small = jnp.concatenate([d_value.reshape(2, 16, 48, SIDE), gain_pair], 2)
    sums, got, output, tokens_grad, small = together((sums, got, output, tokens_grad, small))
    sums = scatter_add(sums, got, 1)

    sums, got = scatter_send(sums, 2)
    small = add_low(pick(small, core), other(pick(small, 1 - core))).reshape(4, 2, 2, 64, SIDE)
    sums, got, small = together((sums, got, small))
    sums = scatter_add(sums, got, 2)

    sums, got = scatter_send(sums, 3)
    small = add_low(pick(small, x, 2), swap(pick(small, 1 - x, 2), TO_X))
    blocks, blocks_far = pick(rand_sum, core), other(pick(rand_sum, 1 - core))
    sums, got, small, blocks, blocks_far = together((sums, got, small, blocks, blocks_far))
    sums = scatter_add(sums, got, 3)

    sums, got = scatter_send(sums, 4)
    small = add_low(pick(small, y, 1), swap(pick(small, 1 - y, 1), TO_Y))
    sums, got, small = together((sums, got, small))
    small_sum = pick(small, z).astype(F32)
    for k in range(1, PLANES):
        small_sum = small_sum + ring(pick(small, lax.rem(z + PLANES - k, PLANES)), -k).astype(F32)
    big_sum = scatter_add(sums, got, 4)[0, 0, 0]
    big_far, small_far = other(big_sum), other(small_sum)

    rows_of = lambda value, rows: pick(value.reshape(-1, 2, rows, SIDE), core, 1)
    mine = lambda own, far, rows: side(rows_of(own, rows)[0], rows_of(far, rows)[0], 1)
    down_shard = mine(big_sum[PACK_DOWN:PACK_UP], big_far[PACK_DOWN:PACK_UP], 96)
    up_side = lambda value: rows_of(value[PACK_UP:PACK_OUT], 24).transpose(1, 0, 2).reshape(24, 4 * SIDE)
    up_shard = side(up_side(big_sum), up_side(big_far), 1)
    outproj_shard = mine(big_sum[PACK_OUT:PACK_VALUE], big_far[PACK_OUT:PACK_VALUE], 24)
    value_shard = mine(small_sum[:48], small_far[:48], 24)
    gains_pair = ordered(core, small_sum[48, :48], small_far[48, :48])
    gain_pair = pick(gains_pair.reshape(2, 2, 24), core, 1)

    rand_shard = ordered(core, blocks, blocks_far, 1)

    return (
        output.reshape(2, LMAX, WIDTH),
        tokens_grad.reshape(2, LMAX, WIDTH),
        rand_shard.reshape(3 * 128, LMAX),
        value_shard,
        outproj_shard,
        up_shard,
        down_shard,
        gain_pair[0],
        gain_pair[1],
    )


def rms_norm(values, gain):
    scale = lax.rsqrt(jnp.mean(values * values, axis=-1, keepdims=True) + EPSILON)
    return values * scale * gain


def split_heads(block):
    return block.reshape(LMAX, HEADS, HEAD).transpose(1, 0, 2)


def merge_heads(block):
    return block.transpose(1, 0, 2).reshape(LMAX, HEADS * HEAD)


def masked_scores(key_mask, rand_head):
    return jnp.where(key_mask[None, :] > 0, rand_head.astype(jnp.float32), -1e30)


def head_forward(key_mask, paired):
    rand_head, value_head = paired
    scores = masked_scores(key_mask, rand_head)
    row_peak = jnp.max(scores, axis=-1, keepdims=True)
    exponent = jnp.exp(scores - row_peak)
    denom_sum = jnp.sum(exponent, axis=-1, keepdims=True)
    attention = exponent / denom_sum * key_mask[:, None]
    mixed = jnp.dot(attention.astype(jnp.bfloat16), value_head, preferred_element_type=jnp.float32)
    return (mixed.astype(jnp.bfloat16), row_peak + jnp.log(denom_sum))


def head_backward(key_mask, paired):
    rand_head, value_head, mix_grad, log_total = paired
    scores = masked_scores(key_mask, rand_head)
    attention = jnp.exp(scores - log_total) * key_mask[:, None]
    prob_grad = jnp.einsum("id,jd->ij", mix_grad, value_head, preferred_element_type=jnp.float32)
    value_grad = jnp.einsum(
        "ij,id->jd", attention.astype(jnp.bfloat16), mix_grad, preferred_element_type=jnp.float32
    )
    score_grad = attention * (prob_grad - jnp.sum(prob_grad * attention, axis=-1, keepdims=True))
    return (score_grad, value_grad)


def shards(tokens, lengths, rand_mix, w_value, w_out, w_up, w_down, gain_mix, gain_ffn, grad_out):
    item_count = tokens.shape[0]
    width = tokens.shape[2]
    row_count = item_count * LMAX
    tokens_flat = tokens.reshape(row_count, width).astype(jnp.float32)
    positions = jnp.arange(LMAX, dtype=jnp.int32)
    valid_table = (positions[None, :] < lengths[:, None]).astype(jnp.float32)
    row_valid = valid_table.reshape(row_count, 1)
    forward_set = (
        lax.all_gather(rand_mix, ("wide", "narrow"), axis=0, tiled=True),
        lax.all_gather(w_value, ("wide", "narrow"), axis=0, tiled=True),
        lax.all_gather(w_out, ("wide", "narrow"), axis=0, tiled=True),
        lax.all_gather(w_up, ("wide", "narrow"), axis=0, tiled=True),
        lax.all_gather(w_down, ("wide", "narrow"), axis=0, tiled=True),
        lax.all_gather(gain_mix, ("wide", "narrow"), axis=0, tiled=True),
        lax.all_gather(gain_ffn, ("wide", "narrow"), axis=0, tiled=True),
    )
    rand_all, value_all, out_all, up_all, down_all, gain_first, gain_second = forward_set
    normed = rms_norm(tokens_flat, gain_first.astype(jnp.float32)).astype(jnp.bfloat16)
    values = jnp.dot(normed, value_all, preferred_element_type=jnp.float32).astype(jnp.bfloat16)
    rand_heads = rand_all.reshape(HEADS, LMAX, LMAX)
    mixed_parts = []
    totals_kept = []
    for item_index in range(item_count):
        item_values = split_heads(values[item_index * LMAX : (item_index + 1) * LMAX])
        mixed_heads, log_total = lax.map(
            partial(head_forward, valid_table[item_index]), (rand_heads, item_values)
        )
        mixed_parts.append(merge_heads(mixed_heads))
        totals_kept.append(log_total)
    mixed = jnp.concatenate(mixed_parts, axis=0)
    residual = tokens_flat + jnp.dot(mixed, out_all, preferred_element_type=jnp.float32)
    normed_two = rms_norm(residual, gain_second.astype(jnp.float32)).astype(jnp.bfloat16)
    up_proj = jnp.dot(normed_two, up_all, preferred_element_type=jnp.float32)
    active = jax.nn.gelu(up_proj).astype(jnp.bfloat16)
    branch = jnp.dot(active, down_all, preferred_element_type=jnp.float32)
    output = row_valid * (residual + branch)
    back_set = (
        lax.all_gather(rand_mix, ("wide", "narrow"), axis=0, tiled=True),
        lax.all_gather(w_value, ("wide", "narrow"), axis=0, tiled=True),
        lax.all_gather(w_out, ("wide", "narrow"), axis=0, tiled=True),
        lax.all_gather(w_up, ("wide", "narrow"), axis=0, tiled=True),
        lax.all_gather(w_down, ("wide", "narrow"), axis=0, tiled=True),
        lax.all_gather(gain_mix, ("wide", "narrow"), axis=0, tiled=True),
        lax.all_gather(gain_ffn, ("wide", "narrow"), axis=0, tiled=True),
    )
    rand_back, value_back, out_back, up_back, down_back, gain_back_one, gain_back_two = back_set
    cotangent = grad_out.reshape(row_count, width).astype(jnp.float32)
    masked = row_valid * cotangent
    branch_grad = masked.astype(jnp.bfloat16)
    grad_down = jnp.einsum("rk,rd->kd", active, branch_grad, preferred_element_type=jnp.float32)
    active_grad = jnp.einsum(
        "rd,kd->rk", branch_grad, down_back, preferred_element_type=jnp.float32
    )
    gelu_value, gelu_pull = jax.vjp(jax.nn.gelu, up_proj)
    up_grad = gelu_pull(active_grad)[0].astype(jnp.bfloat16)
    grad_up = jnp.einsum("rd,rk->dk", normed_two, up_grad, preferred_element_type=jnp.float32)
    normed_two_grad = jnp.einsum("rk,dk->rd", up_grad, up_back, preferred_element_type=jnp.float32)
    norm_value, norm_pull = jax.vjp(rms_norm, residual, gain_back_two.astype(jnp.float32))
    residual_part, gain_two_grad = norm_pull(normed_two_grad)
    residual_grad = masked + residual_part
    attn_grad = residual_grad.astype(jnp.bfloat16)
    grad_outproj = jnp.einsum("rd,re->de", mixed, attn_grad, preferred_element_type=jnp.float32)
    mixed_grad = jnp.einsum(
        "re,de->rd", attn_grad, out_back, preferred_element_type=jnp.float32
    ).astype(jnp.bfloat16)
    rand_heads_back = rand_back.reshape(HEADS, LMAX, LMAX)
    rand_grad = jnp.zeros((HEADS, LMAX, LMAX), jnp.float32)
    value_parts = []
    for item_index in range(item_count):
        lower_row = item_index * LMAX
        upper_row = lower_row + LMAX
        item_values = split_heads(values[lower_row:upper_row])
        item_mix_grad = split_heads(mixed_grad[lower_row:upper_row])
        score_grad, value_grad = lax.map(
            partial(head_backward, valid_table[item_index]),
            (rand_heads_back, item_values, item_mix_grad, totals_kept[item_index]),
        )
        rand_grad = rand_grad + score_grad
        value_parts.append(merge_heads(value_grad))
    values_grad = jnp.concatenate(value_parts, axis=0).astype(jnp.bfloat16)
    grad_value = jnp.einsum("rd,re->de", normed, values_grad, preferred_element_type=jnp.float32)
    normed_grad = jnp.einsum(
        "re,de->rd", values_grad, value_back, preferred_element_type=jnp.float32
    )
    norm_first, first_pull = jax.vjp(rms_norm, tokens_flat, gain_back_one.astype(jnp.float32))
    token_part, gain_one_grad = first_pull(normed_grad)
    tokens_grad = residual_grad + token_part
    rand_flat = rand_grad.reshape(HEADS * LMAX, LMAX)
    all_shards = (
        lax.psum_scatter(rand_flat, ("wide", "narrow"), scatter_dimension=0, tiled=True),
        lax.psum_scatter(grad_value, ("wide", "narrow"), scatter_dimension=0, tiled=True),
        lax.psum_scatter(grad_outproj, ("wide", "narrow"), scatter_dimension=0, tiled=True),
        lax.psum_scatter(grad_up, ("wide", "narrow"), scatter_dimension=0, tiled=True),
        lax.psum_scatter(grad_down, ("wide", "narrow"), scatter_dimension=0, tiled=True),
        lax.psum_scatter(gain_one_grad, ("wide", "narrow"), scatter_dimension=0, tiled=True),
        lax.psum_scatter(gain_two_grad, ("wide", "narrow"), scatter_dimension=0, tiled=True),
    )
    rand_shard, value_shard, outproj_shard, up_shard, down_shard, gain_one_shard, gain_two_shard = (
        all_shards
    )
    return (
        output.reshape(item_count, LMAX, width),
        tokens_grad.reshape(item_count, LMAX, width),
        rand_shard,
        value_shard,
        outproj_shard,
        up_shard,
        down_shard,
        gain_one_shard,
        gain_two_shard,
    )


def solution(mesh):
    in_specs = (
        P(("wide", "narrow"), None, None),
        P(("wide", "narrow")),
        P(("wide", "narrow"), None),
        P(("wide", "narrow"), None),
        P(("wide", "narrow"), None),
        P(("wide", "narrow"), None),
        P(("wide", "narrow"), None),
        P(("wide", "narrow")),
        P(("wide", "narrow")),
        P(("wide", "narrow"), None, None),
    )
    out_specs = (
        P(("wide", "narrow"), None, None),
        P(("wide", "narrow"), None, None),
        P(("wide", "narrow"), None),
        P(("wide", "narrow"), None),
        P(("wide", "narrow"), None),
        P(("wide", "narrow"), None),
        P(("wide", "narrow"), None),
        P(("wide", "narrow")),
        P(("wide", "narrow")),
    )
    fits = dict(mesh.shape) == {"wide": 16, "narrow": 2}
    return jax.shard_map(chip_shards if fits else shards, mesh=mesh, in_specs=in_specs, out_specs=out_specs, check_vma=False)
```

```python
from functools import partial

import jax
import jax.numpy as jnp
from jax import lax
from jax.experimental import pallas as pl
from jax.experimental.pallas import tpu as pltpu
from jax.sharding import PartitionSpec as P

HEADS = 12
HEAD = 64
LMAX = 1024
WIDTH = 768
FF = 3072
EPSILON = 1e-05

BOTH = ("wide", "narrow")
BF16 = jnp.bfloat16
F32 = jnp.float32
VMEM = 61 << 20
LESS = 34 << 20

SUBS = 6
RUNS = 8
HALF = 64
HROWS = RUNS * HALF
PLANES = 4
PHEADS = HEADS // PLANES
ROWS = 2 * LMAX
FSTEP = 768
FSIDE = FF // 2 // FSTEP
TILE = 512
SIDE = WIDTH // 2
SPAN = 2 * HALF


def dot(a, b, ca, cb):
    return lax.dot_general(a, b, (((ca,), (cb,)), ((), ())), preferred_element_type=F32)


CORE, PLANE, PLACE, LENGTHS = 0, 1, 2, 3


def spec(shape, index):
    return pl.BlockSpec(shape, index)


def held(shape):
    zeros = (0,) * len(shape)
    return pl.BlockSpec(shape, lambda *_: zeros, pipeline_mode=pl.Buffered(1))


def params(limit):
    return pltpu.CompilerParams(vmem_limit_bytes=limit)


def whole_weight(sc, step, own, far, weight):
    @pl.when(step == 0)
    def _():
        weight[:, pl.ds(pl.multiple_of(sc[CORE] * SIDE, 128), SIDE)] = own[...]
        weight[:, pl.ds(pl.multiple_of((1 - sc[CORE]) * SIDE, 128), SIDE)] = far[...]


def values_kernel(sc, tok, gain, w_own, w_far, out, weight):
    step = pl.program_id(0)
    whole_weight(sc, step, w_own, w_far, weight)
    rows = tok.shape[1]
    position = step * rows + lax.broadcasted_iota(jnp.int32, (rows, 1), 0)
    for item in range(2):
        x = tok[item].astype(F32)
        scale = lax.rsqrt(jnp.mean(x * x, axis=-1, keepdims=True) + EPSILON)
        normed = (x * scale * gain[...]).astype(BF16)
        found = dot(normed, weight[...], 1, 0)
        found = jnp.where(position < sc[LENGTHS + item], found, 0.0).astype(BF16)
        for head in range(HEADS):
            out[head, :, item * HEAD : (item + 1) * HEAD] = found[:, head * HEAD : (head + 1) * HEAD]


def run_values(sc, tokens, gain, w_own, w_far):
    rows = 256
    return pl.pallas_call(
        values_kernel,
        grid_spec=pltpu.PrefetchScalarGridSpec(
            num_scalar_prefetch=1,
            grid=(LMAX // rows,),
            in_specs=[
                spec((2, rows, WIDTH), lambda j, s: (0, j, 0)),
                held((1, WIDTH)),
                held((WIDTH, SIDE)),
                held((WIDTH, SIDE)),
            ],
            out_specs=spec((HEADS, rows, 2 * HEAD), lambda j, s: (0, j, 0)),
            scratch_shapes=[pltpu.VMEM((WIDTH, WIDTH), BF16)],
        ),
        out_shape=jax.ShapeDtypeStruct((HEADS, LMAX, 2 * HEAD), BF16),
        compiler_params=params(VMEM),
        cost_estimate=pl.CostEstimate(
            flops=2 * 2 * LMAX * WIDTH * WIDTH, bytes_accessed=8 * LMAX * WIDTH, transcendentals=0
        ),
        name="values",
    )(sc, tokens, gain, w_own, w_far)


def lane_lengths(sc, shape):
    slot = lax.broadcasted_iota(jnp.int32, shape, 1) // HEAD
    length = jnp.where(slot == 0, sc[LENGTHS], sc[LENGTHS + 1])
    return jnp.where(slot >= 2, jnp.where(slot == 2, sc[LENGTHS + 2], sc[LENGTHS + 3]), length)


def plane_of(k, sc):
    return lax.rem(sc[PLANE] + PLANES - k, PLANES)


def plane_spec(planes, rows, lanes):
    def index(step, sc):
        return (plane_of(planes[0] + step * (planes[-1] - planes[0]) // max(len(planes) - 1, 1), sc), 0, 0)

    return spec((PHEADS, rows, lanes), index)


def anywhere(count):
    return [pl.BlockSpec(memory_space=pl.ANY)] * count


def plane_fetch(place, shards, raw, sems, slot):
    return [
        pltpu.make_async_copy(
            shards[4 * slot + rel],
            raw.at[slot, pl.ds(pl.multiple_of((place ^ rel) * SUBS * HALF, SUBS * HALF), SUBS * HALF)],
            sems.at[slot, rel],
        )
        for rel in range(4)
    ]


def take_plane(place, shards, raw, sems):
    step = pl.program_id(0)
    count = len(shards) // 4

    @pl.when(step == 0)
    def _():
        for slot in range(count):
            for copy in plane_fetch(place, shards, raw, sems, slot):
                copy.start()

    for slot in range(count):

        @pl.when(step == slot)
        def _():
            for copy in plane_fetch(place, shards, raw, sems, slot):
                copy.wait()

    return step


def head_rows(head):
    return slice(head * HROWS, (head + 1) * HROWS)


def fill_mask(sc, mask):
    @pl.when(pl.program_id(0) == 0)
    def _():
        shape = (LMAX, 4 * HEAD)
        column = lax.broadcasted_iota(jnp.int32, shape, 0)
        mask[...] = (column < lane_lengths(sc, shape)).astype(F32).astype(BF16)


def mix_kernel(count, carried, sc, *refs):
    shards, (v_own, v_far, *rest) = refs[: 4 * count], refs[4 * count :]
    mixed, mean, exps, inverse, raw, mask, sems = rest[4:] if carried else rest
    fill_mask(sc, mask)
    slot = take_plane(sc[PLACE], shards, raw, sems)
    shape = (HROWS, 4 * HEAD)
    line = lax.broadcasted_iota(jnp.int32, shape, 0)
    position = 128 * (line // HALF) + HALF * sc[CORE] + line % HALF
    valid = position < lane_lengths(sc, shape)
    for head in range(PHEADS):
        weights = jnp.exp(raw[slot, head_rows(head)].astype(F32)).astype(BF16)
        exps[head] = weights
        both = dot(weights, jnp.concatenate([v_own[head], v_far[head], mask[...]], axis=1), 1, 0)
        flip = jnp.where(valid, 1.0 / both[:, 4 * HEAD :], 0.0)
        found = both[:, : 4 * HEAD] * flip
        inverse[head] = flip.astype(BF16)
        mean[head] = found
        mixed[head] = found.astype(BF16)


def run_mix(sc, planes, shards, v_own, v_far, carry):
    carry, count = list(carry), len(planes)
    shape = (HEADS, HROWS, 4 * HEAD)
    return pl.pallas_call(
        partial(mix_kernel, count, bool(carry)),
        grid_spec=pltpu.PrefetchScalarGridSpec(
            num_scalar_prefetch=1,
            grid=(count,),
            in_specs=anywhere(4 * count) + [plane_spec(planes, LMAX, 2 * HEAD)] * 2 + anywhere(len(carry)),
            out_specs=[
                plane_spec(planes, HROWS, 4 * HEAD),
                plane_spec(planes, HROWS, 4 * HEAD),
                plane_spec(planes, HROWS, LMAX),
                plane_spec(planes, HROWS, 4 * HEAD),
            ],
            scratch_shapes=[
                pltpu.VMEM((count, 4 * SUBS * HALF, LMAX), BF16),
                pltpu.VMEM((LMAX, 4 * HEAD), BF16),
                pltpu.SemaphoreType.DMA((count, 4)),
            ],
        ),
        out_shape=[
            jax.ShapeDtypeStruct(shape, BF16),
            jax.ShapeDtypeStruct(shape, F32),
            jax.ShapeDtypeStruct((HEADS, HROWS, LMAX), BF16),
            jax.ShapeDtypeStruct(shape, BF16),
        ],
        input_output_aliases={3 + 4 * count + i: i for i in range(len(carry))},
        compiler_params=params(VMEM),
        cost_estimate=pl.CostEstimate(
            flops=2 * HEADS * HROWS * LMAX * 4 * HEAD,
            bytes_accessed=HEADS * (2 * HROWS * LMAX + 5 * HROWS * 256),
            transcendentals=HEADS * HROWS * LMAX // 2,
        ),
        name="mix",
    )(sc, *shards, v_own, v_far, *carry)


def row_valid(sc, step):
    line = lax.broadcasted_iota(jnp.int32, (4 * SPAN, 1), 0)
    item = line // SPAN
    row = step * SPAN + line % SPAN
    low = jnp.where(item == 0, sc[LENGTHS], sc[LENGTHS + 1])
    high = jnp.where(item == 2, sc[LENGTHS + 2], sc[LENGTHS + 3])
    return 128 * (row // HALF) + HALF * sc[CORE] + row % HALF < jnp.where(item >= 2, high, low)


def four_items(own, far):
    return jnp.concatenate([own[:, :, 0], far[...]], axis=0).reshape(4 * SPAN, WIDTH)


def pre_kernel(sc, tok, tok_far, heads, wo_own, wo_far, gain, mixed, resid, normed, weight):
    step = pl.program_id(0)
    whole_weight(sc, step, wo_own, wo_far, weight)
    for item in range(4):
        lanes = slice(item * HEAD, (item + 1) * HEAD)
        for pair in range(HEADS // 2):
            both = jnp.concatenate([heads[2 * pair, :, lanes], heads[2 * pair + 1, :, lanes]], axis=1)
            mixed[item, :, pair * 128 : (pair + 1) * 128] = both
    res = four_items(tok, tok_far).astype(F32) + dot(mixed[...].reshape(4 * SPAN, WIDTH), weight[...], 1, 0)
    resid[...] = res.astype(BF16).reshape(4, SPAN, WIDTH)
    scale = lax.rsqrt(jnp.mean(res * res, axis=-1, keepdims=True) + EPSILON)
    valid = row_valid(sc, step)
    normed[...] = jnp.where(valid, res * scale * gain[...], 0.0).astype(BF16).reshape(4, SPAN, WIDTH)


def slab_spec(items=4):
    return spec((items, SPAN, WIDTH), lambda r, s: (0, r, 0))


def half_specs():
    return [
        spec((2, SPAN // HALF, 1, HALF, WIDTH), lambda r, s: (0, r, s[CORE], 0, 0)),
        spec((2, SPAN // HALF, HALF, WIDTH), lambda r, s: (0, r, 0, 0)),
    ]


def heads_spec():
    return spec((HEADS, SPAN, 4 * HEAD), lambda r, s: (0, r, 0))


def run_pre(sc, tokens, tokens_far, heads, wo, gain):
    return pl.pallas_call(
        pre_kernel,
        grid_spec=pltpu.PrefetchScalarGridSpec(
            num_scalar_prefetch=1,
            grid=(HROWS // SPAN,),
            in_specs=half_specs()
            + [heads_spec(), held((WIDTH, SIDE)), held((WIDTH, SIDE)), held((1, WIDTH))],
            out_specs=[slab_spec()] * 3,
            scratch_shapes=[pltpu.VMEM((WIDTH, WIDTH), BF16)],
        ),
        out_shape=[
            jax.ShapeDtypeStruct((4, HROWS, WIDTH), BF16),
            jax.ShapeDtypeStruct((4, HROWS, WIDTH), BF16),
            jax.ShapeDtypeStruct((4, HROWS, WIDTH), BF16),
        ],
        compiler_params=params(VMEM),
        cost_estimate=pl.CostEstimate(
            flops=2 * ROWS * WIDTH * WIDTH, bytes_accessed=16 * ROWS * WIDTH, transcendentals=0
        ),
        name="pre",
    )(sc, tokens, tokens_far, heads, *wo, gain)


def masked_kernel(sc, cot, cot_far, masked):
    value = jnp.where(row_valid(sc, pl.program_id(0)), four_items(cot, cot_far).astype(F32), 0.0)
    masked[...] = value.astype(BF16).reshape(4, SPAN, WIDTH)


def run_masked(sc, cotangent, cotangent_far):
    return pl.pallas_call(
        masked_kernel,
        grid_spec=pltpu.PrefetchScalarGridSpec(
            num_scalar_prefetch=1, grid=(HROWS // SPAN,), in_specs=half_specs(), out_specs=slab_spec()
        ),
        out_shape=jax.ShapeDtypeStruct((4, HROWS, WIDTH), BF16),
        compiler_params=params(VMEM),
        cost_estimate=pl.CostEstimate(flops=0, bytes_accessed=4 * ROWS * WIDTH, transcendentals=0),
        name="masked",
    )(sc, cotangent, cotangent_far)


def own_lanes(sc):
    return pl.ds(pl.multiple_of(sc[CORE] * SIDE, 128), SIDE)


def far_lanes(sc):
    return pl.ds(pl.multiple_of((1 - sc[CORE]) * SIDE, 128), SIDE)


def unit_rows(f, sc):
    return (lax.rem(FSIDE * sc[CORE] + f, 2 * FSIDE), 0)


def unit_columns(f, sc):
    return (0, lax.rem(FSIDE * sc[CORE] + f, 2 * FSIDE))


def early(f, sc):
    return (0, lax.min(f, FSIDE - 1))


def late(f, sc):
    return (0, lax.max(f - FSIDE, 0))


def units_kernel(sc, normed, cot, up_own, up_far, dn_own, dn_far, active, up_grad, w_up, w_down):
    step = pl.program_id(0)
    w_down[:, own_lanes(sc)] = dn_own[...]
    w_down[:, far_lanes(sc)] = dn_far[...]

    @pl.when(step < FSIDE)
    def _():
        w_up[...] = up_own[...]

    @pl.when(step >= FSIDE)
    def _():
        w_up[...] = up_far[...]

    for row in range(0, ROWS, 256):
        rows = slice(row, row + 256)
        for column in range(0, FSTEP, 256):
            columns = slice(column, column + 256)
            up = dot(normed[rows], w_up[:, columns], 1, 0)
            square = up * up
            bend = jnp.tanh(up * (0.7978845608028654 + (0.044715 * 0.7978845608028654) * square))
            share = 0.5 + 0.5 * bend
            act = up * share
            active[rows, columns] = act.astype(BF16)
            slope = share + act * (1.0 - share) * (
                2 * 0.7978845608028654 + (6 * 0.044715 * 0.7978845608028654) * square
            )
            up_grad[rows, columns] = (dot(cot[rows], w_down[columns], 1, 1) * slope).astype(BF16)


def run_units(sc, normed, cotangent, up, down):
    return pl.pallas_call(
        units_kernel,
        grid_spec=pltpu.PrefetchScalarGridSpec(
            num_scalar_prefetch=1,
            grid=(2 * FSIDE,),
            in_specs=[
                held((ROWS, WIDTH)),
                held((ROWS, WIDTH)),
                spec((WIDTH, FSTEP), early),
                spec((WIDTH, FSTEP), late),
                spec((FSTEP, SIDE), unit_rows),
                spec((FSTEP, SIDE), unit_rows),
            ],
            out_specs=[spec((ROWS, FSTEP), unit_columns), spec((ROWS, FSTEP), unit_columns)],
            scratch_shapes=[pltpu.VMEM((WIDTH, FSTEP), BF16), pltpu.VMEM((FSTEP, WIDTH), BF16)],
        ),
        out_shape=[jax.ShapeDtypeStruct((ROWS, FF), BF16), jax.ShapeDtypeStruct((ROWS, FF), BF16)],
        compiler_params=params(VMEM),
        cost_estimate=pl.CostEstimate(
            flops=4 * ROWS * WIDTH * FF, bytes_accessed=6 * ROWS * WIDTH + 4 * ROWS * FF, transcendentals=ROWS * FF
        ),
        name="units",
    )(sc, normed.reshape(ROWS, WIDTH), cotangent.reshape(ROWS, WIDTH), *up, *down)


def down_grad_kernel(sc, active, cot, own, far, total):
    total[...] = dot(active[...], cot[...], 0, 0).astype(BF16)
    own[...] = total[:, own_lanes(sc)]
    far[...] = total[:, far_lanes(sc)]


def run_down_grad(sc, active, cotangent):
    return pl.pallas_call(
        down_grad_kernel,
        grid_spec=pltpu.PrefetchScalarGridSpec(
            num_scalar_prefetch=1,
            grid=(FF // 512,),
            in_specs=[spec((ROWS, 512), lambda f, s: (0, f)), held((ROWS, WIDTH))],
            out_specs=[spec((512, SIDE), lambda f, s: (f, 0))] * 2,
            scratch_shapes=[pltpu.VMEM((512, WIDTH), BF16)],
        ),
        out_shape=[jax.ShapeDtypeStruct((FF, SIDE), BF16)] * 2,
        compiler_params=params(57 << 20),
        cost_estimate=pl.CostEstimate(
            flops=2 * ROWS * WIDTH * FF, bytes_accessed=2 * ROWS * (WIDTH + FF), transcendentals=0
        ),
        name="down_grad",
    )(sc, active, cotangent.reshape(ROWS, WIDTH))


def up_grad_kernel(sc, normed, up_grad, own, far):
    total = dot(normed[...], up_grad[...], 0, 0).astype(BF16)

    @pl.when(pl.program_id(0) < 3)
    def _():
        own[...] = total

    @pl.when(pl.program_id(0) >= 3)
    def _():
        far[...] = total


def run_up_grad(sc, normed, up_grad):
    return pl.pallas_call(
        up_grad_kernel,
        grid_spec=pltpu.PrefetchScalarGridSpec(
            num_scalar_prefetch=1,
            grid=(6,),
            in_specs=[held((ROWS, WIDTH)), spec((ROWS, 512), lambda f, s: (0, lax.rem(3 * s[CORE] + f, 6)))],
            out_specs=[
                spec((WIDTH, 512), lambda f, s: (0, lax.min(f, 2))),
                spec((WIDTH, 512), lambda f, s: (0, lax.max(f - 3, 0))),
            ],
        ),
        out_shape=[jax.ShapeDtypeStruct((WIDTH, FF // 2), BF16)] * 2,
        compiler_params=params(57 << 20),
        cost_estimate=pl.CostEstimate(
            flops=2 * ROWS * WIDTH * FF, bytes_accessed=2 * ROWS * (WIDTH + FF), transcendentals=0
        ),
        name="up_grad",
    )(sc, normed.reshape(ROWS, WIDTH), up_grad)


def out_grad_kernel(sc, mixed, res_own, res_far, own, far, total):
    step = pl.program_id(0)
    grad = jnp.concatenate([res_own[...], res_far[...]], axis=0).reshape(4 * SPAN, WIDTH)
    found = dot(mixed[...].reshape(4 * SPAN, WIDTH), grad, 0, 0)

    @pl.when(step == 0)
    def _():
        total[...] = found

    @pl.when(step > 0)
    def _():
        total[...] += found

    @pl.when(step == pl.num_programs(0) - 1)
    def _():
        own[...] = total[:, own_lanes(sc)].astype(BF16)
        far[...] = total[:, far_lanes(sc)].astype(BF16)


def run_out_grad(sc, mixed, res_own, res_far):
    return pl.pallas_call(
        out_grad_kernel,
        grid_spec=pltpu.PrefetchScalarGridSpec(
            num_scalar_prefetch=1,
            grid=(HROWS // SPAN,),
            in_specs=[slab_spec(), slab_spec(2), slab_spec(2)],
            out_specs=[held((WIDTH, SIDE))] * 2,
            scratch_shapes=[pltpu.VMEM((WIDTH, WIDTH), F32)],
        ),
        out_shape=[jax.ShapeDtypeStruct((WIDTH, SIDE), BF16)] * 2,
        compiler_params=params(LESS),
        cost_estimate=pl.CostEstimate(
            flops=2 * ROWS * WIDTH * WIDTH, bytes_accessed=4 * ROWS * WIDTH, transcendentals=0
        ),
        name="out_grad",
    )(sc, mixed, res_own, res_far)


def out_kernel(sc, active, resid, dn_own, dn_far, own, far, w_down):
    step = pl.program_id(0)

    @pl.when(step == 0)
    def _():
        w_down[:, own_lanes(sc)] = dn_own[...]
        w_down[:, far_lanes(sc)] = dn_far[...]

    branch = dot(active[...].reshape(4 * SPAN, FF), w_down[...], 1, 0)
    output = jnp.where(row_valid(sc, step), resid[...].reshape(4 * SPAN, WIDTH).astype(F32) + branch, 0.0)
    output = output.astype(BF16).reshape(4, SPAN, WIDTH)
    own[...] = output[:2]
    far[...] = output[2:]


def run_out(sc, active, resid, down):
    return pl.pallas_call(
        out_kernel,
        grid_spec=pltpu.PrefetchScalarGridSpec(
            num_scalar_prefetch=1,
            grid=(HROWS // SPAN,),
            in_specs=[
                spec((4, SPAN, FF), lambda r, s: (0, r, 0)),
                slab_spec(),
                held((FF, SIDE)),
                held((FF, SIDE)),
            ],
            out_specs=[slab_spec(2)] * 2,
            scratch_shapes=[pltpu.VMEM((FF, WIDTH), BF16)],
        ),
        out_shape=[
            jax.ShapeDtypeStruct((2, HROWS, WIDTH), BF16),
            jax.ShapeDtypeStruct((2, HROWS, WIDTH), BF16),
        ],
        compiler_params=params(LESS),
        cost_estimate=pl.CostEstimate(
            flops=2 * ROWS * WIDTH * FF, bytes_accessed=ROWS * (2 * FF + 7 * WIDTH), transcendentals=0
        ),
        name="out",
    )(sc, active.reshape(4, HROWS, FF), resid, *down)


def post_kernel(sc, resid, grad_own, grad_far, cot, up_own, up_far, wo_own, wo_far, gain, *refs):
    (res_own, res_far, heads, d_gain, weight, spread) = refs
    step = pl.program_id(0)
    whole_weight(sc, step, wo_own, wo_far, weight)
    shape, slab = (4 * SPAN, WIDTH), (4, SPAN, WIDTH)
    valid = row_valid(sc, step)
    res = resid[...].reshape(shape).astype(F32)
    scale = lax.rsqrt(jnp.mean(res * res, axis=-1, keepdims=True) + EPSILON)
    unit = res * scale
    units = (4 * SPAN, FF // 2)
    back = dot(grad_own[...].reshape(units), up_own[...], 1, 1) + dot(grad_far[...].reshape(units), up_far[...], 1, 1)
    two_grad = jnp.where(valid, back, 0.0)
    gained = two_grad * gain[...]
    masked = cot[...].reshape(shape).astype(F32)
    grad = masked + scale * (gained - unit * jnp.mean(gained * unit, axis=-1, keepdims=True))
    low = grad.astype(BF16)
    res_own[...] = low.reshape(slab)[:2]
    res_far[...] = low.reshape(slab)[2:]
    gain_sum = jnp.sum(two_grad * unit, axis=0, keepdims=True)

    @pl.when(step == 0)
    def _():
        d_gain[...] = gain_sum

    @pl.when(step > 0)
    def _():
        d_gain[...] += gain_sum

    spread[...] = dot(low, weight[...], 1, 1).astype(BF16).reshape(slab)
    for pair in range(HEADS // 2):
        lanes = slice(pair * 128, (pair + 1) * 128)
        for side in range(2):
            one, two = spread[2 * side, :, lanes], spread[2 * side + 1, :, lanes]
            half = slice(side * 128, (side + 1) * 128)
            heads[2 * pair, :, half] = jnp.concatenate([one[:, :HEAD], two[:, :HEAD]], axis=1)
            heads[2 * pair + 1, :, half] = jnp.concatenate([one[:, HEAD:], two[:, HEAD:]], axis=1)


def run_post(sc, resid, up_grad, cotangent, up, wo, gain):
    side = lambda which: spec((4, SPAN, FF // 2), lambda r, s: (0, r, s[CORE] if which == 0 else 1 - s[CORE]))
    up_grad = up_grad.reshape(4, HROWS, FF)
    return pl.pallas_call(
        post_kernel,
        grid_spec=pltpu.PrefetchScalarGridSpec(
            num_scalar_prefetch=1,
            grid=(HROWS // SPAN,),
            in_specs=[
                slab_spec(),
                side(0),
                side(1),
                slab_spec(),
                held((WIDTH, FF // 2)),
                held((WIDTH, FF // 2)),
                held((WIDTH, SIDE)),
                held((WIDTH, SIDE)),
                held((1, WIDTH)),
            ],
            out_specs=[slab_spec(2)] * 2 + [heads_spec(), held((1, WIDTH))],
            scratch_shapes=[
                pltpu.VMEM((WIDTH, WIDTH), BF16),
                pltpu.VMEM((4, SPAN, WIDTH), BF16),
            ],
        ),
        out_shape=[
            jax.ShapeDtypeStruct((2, HROWS, WIDTH), BF16),
            jax.ShapeDtypeStruct((2, HROWS, WIDTH), BF16),
            jax.ShapeDtypeStruct((HEADS, HROWS, 4 * HEAD), BF16),
            jax.ShapeDtypeStruct((1, WIDTH), F32),
        ],
        compiler_params=params(VMEM),
        cost_estimate=pl.CostEstimate(
            flops=2 * ROWS * WIDTH * (WIDTH + FF), bytes_accessed=ROWS * (16 * WIDTH + 2 * FF), transcendentals=0
        ),
        name="post",
    )(sc, resid, up_grad, up_grad, cotangent, *up, *wo, gain)


def unmix_kernel(count, carried, sc, v_own, v_far, grad_heads, mean, exps, inverse, *refs):
    refs = refs[2:] if carried else refs
    outs, (own, far, grads, mask, adder, bound, out_sems) = refs[: 4 * count], refs[4 * count :]
    place = sc[PLACE]
    step = pl.program_id(0)

    def leave(slot):
        return [
            pltpu.make_async_copy(
                grads.at[slot, pl.ds(pl.multiple_of((place ^ rel) * SUBS * HALF, SUBS * HALF), SUBS * HALF)],
                outs[4 * slot + rel],
                out_sems.at[slot, rel],
            )
            for rel in range(4)
        ]

    fill_mask(sc, mask)

    @pl.when(step == 0)
    def _():
        lane = lax.broadcasted_iota(jnp.int32, (4 * HEAD, 128), 0) // HEAD
        column = lax.broadcasted_iota(jnp.int32, (4 * HEAD, 128), 1)
        adder[...] = jnp.where((lane == column) | (lane + 4 == column), -1.0, 0.0).astype(BF16)
        row = lax.broadcasted_iota(jnp.int32, (LMAX, 128), 0)
        item = lax.broadcasted_iota(jnp.int32, (LMAX, 128), 1)
        length = jnp.where(item % 4 == 0, sc[LENGTHS], sc[LENGTHS + 1])
        length = jnp.where(item % 4 == 2, sc[LENGTHS + 2], length)
        length = jnp.where(item % 4 == 3, sc[LENGTHS + 3], length)
        bound[...] = jnp.where((item < 8) & (row < length), 1.0, 0.0).astype(BF16)

    high_lanes = lax.broadcasted_iota(jnp.int32, (HROWS, 128), 1) < 4
    for head in range(PHEADS):
        weights = exps[head]
        low = (grad_heads[head].astype(F32) * inverse[head].astype(F32)).astype(BF16)
        product = low.astype(F32) * mean[head]
        coarse = product.astype(BF16)
        fine = (product - coarse.astype(F32)).astype(BF16)
        delta = dot(coarse, adder[...], 1, 0) + dot(fine, adder[...], 1, 0)
        coarse = delta.astype(BF16)
        fine = (delta - coarse.astype(F32)).astype(BF16)
        left = jnp.concatenate([low, jnp.where(high_lanes, coarse, fine)], axis=1)
        score = dot(left, jnp.concatenate([v_own[head], v_far[head], bound[...]], axis=1), 1, 1)
        grads[step, head_rows(head)] = (score * weights.astype(F32)).astype(BF16)
        back = (dot(weights, low, 0, 0) * mask[...].astype(F32)).astype(BF16)
        own[head] = back[:, : 2 * HEAD]
        far[head] = back[:, 2 * HEAD :]
    for which in range(count):

        @pl.when(step == which)
        def _():
            for copy in leave(which):
                copy.start()
            if which == count - 1:
                for slot in range(count):
                    for copy in leave(slot):
                        copy.wait()


def run_unmix(sc, planes, v_own, v_far, grad_heads, mean, exps, inverse, carry):
    carry, count = list(carry), len(planes)
    return pl.pallas_call(
        partial(unmix_kernel, count, bool(carry)),
        grid_spec=pltpu.PrefetchScalarGridSpec(
            num_scalar_prefetch=1,
            grid=(count,),
            in_specs=[
                plane_spec(planes, LMAX, 2 * HEAD),
                plane_spec(planes, LMAX, 2 * HEAD),
                plane_spec(planes, HROWS, 4 * HEAD),
                plane_spec(planes, HROWS, 4 * HEAD),
                plane_spec(planes, HROWS, LMAX),
                plane_spec(planes, HROWS, 4 * HEAD),
            ]
            + anywhere(len(carry)),
            out_specs=anywhere(4 * count) + [plane_spec(planes, LMAX, 2 * HEAD)] * 2,
            scratch_shapes=[
                pltpu.VMEM((count, 4 * SUBS * HALF, LMAX), BF16),
                pltpu.VMEM((LMAX, 4 * HEAD), BF16),
                pltpu.VMEM((4 * HEAD, 128), BF16),
                pltpu.VMEM((LMAX, 128), BF16),
                pltpu.SemaphoreType.DMA((count, 4)),
            ],
        ),
        out_shape=[jax.ShapeDtypeStruct((SUBS * HALF, LMAX), BF16)] * (4 * count)
        + [jax.ShapeDtypeStruct((HEADS, LMAX, 2 * HEAD), BF16)] * 2,
        input_output_aliases={7 + i: 4 * count + i for i in range(len(carry))},
        compiler_params=params(VMEM),
        cost_estimate=pl.CostEstimate(
            flops=3 * HEADS * HROWS * LMAX * 4 * HEAD,
            bytes_accessed=HEADS * (2 * HROWS * LMAX + 5 * HROWS * 256 + 4 * LMAX * 256),
            transcendentals=0,
        ),
        name="unmix",
    )(sc, v_own, v_far, grad_heads, mean, exps, inverse, *carry)


def close_kernel(sc, tok, res_own, res_got, out_own, out_got, own, far, gain, w_own, w_far, *refs):
    (output, tok_grad, d_value, d_gain, total, weight) = refs
    step = pl.program_id(0)
    whole_weight(sc, step, w_own, w_far, weight)
    core = sc[CORE]
    output[:, :, core] = out_own[...].astype(F32)
    output[:, :, 1 - core] = out_got[...].astype(F32)
    tok_grad[:, :, core] = res_own[...].astype(F32)
    tok_grad[:, :, 1 - core] = res_got[...].astype(F32)
    runs = tok.shape[1]
    rows = runs * 128
    for item in range(2):
        lanes = slice(item * HEAD, (item + 1) * HEAD)
        pieces = [
            add_low(own[head, :, lanes], far[head, :, lanes]) for head in range(HEADS)
        ]
        back = jnp.concatenate(pieces, axis=1)
        x = tok[item].reshape(rows, WIDTH).astype(F32)
        scale = lax.rsqrt(jnp.mean(x * x, axis=-1, keepdims=True) + EPSILON)
        unit = x * scale
        normed = (unit * gain[...]).astype(BF16)
        normed_grad = dot(back, weight[...], 1, 1)
        gained = normed_grad * gain[...]
        update = scale * (gained - unit * jnp.mean(gained * unit, axis=-1, keepdims=True))
        tok_grad[item] += update.reshape(runs, 2, HALF, WIDTH)
        gain_sum = jnp.sum(normed_grad * unit, axis=0, keepdims=True)
        value_sum = dot(normed, back, 0, 0)
        if item == 0:
            gain_total, value_total = gain_sum, value_sum
        else:
            gain_total, value_total = gain_total + gain_sum, value_total + value_sum

    @pl.when(step == 0)
    def _():
        d_gain[...] = gain_total
        total[...] = value_total

    @pl.when(step > 0)
    def _():
        d_gain[...] += gain_total
        total[...] += value_total

    @pl.when(step == pl.num_programs(0) - 1)
    def _():
        d_value[...] = total[...].astype(BF16)


def run_close(sc, tokens, res_own, res_got, out_own, out_got, own, far, gain, w_own, w_far):
    runs = 2
    slab = (2, RUNS, 2, HALF, WIDTH)
    half = (2, RUNS, HALF, WIDTH)
    whole_spec = spec((2, runs, 2, HALF, WIDTH), lambda j, s: (0, j, 0, 0, 0))
    half_spec = spec((2, runs, HALF, WIDTH), lambda j, s: (0, j, 0, 0))
    back_spec = spec((HEADS, runs * 128, 2 * HEAD), lambda j, s: (0, j, 0))
    return pl.pallas_call(
        close_kernel,
        grid_spec=pltpu.PrefetchScalarGridSpec(
            num_scalar_prefetch=1,
            grid=(RUNS // runs,),
            in_specs=[whole_spec]
            + [half_spec] * 4
            + [back_spec, back_spec, held((1, WIDTH)), held((WIDTH, SIDE)), held((WIDTH, SIDE))],
            out_specs=[whole_spec, whole_spec, held((WIDTH, WIDTH)), held((1, WIDTH))],
            scratch_shapes=[pltpu.VMEM((WIDTH, WIDTH), F32), pltpu.VMEM((WIDTH, WIDTH), BF16)],
        ),
        out_shape=[
            jax.ShapeDtypeStruct(slab, F32),
            jax.ShapeDtypeStruct(slab, F32),
            jax.ShapeDtypeStruct((WIDTH, WIDTH), BF16),
            jax.ShapeDtypeStruct((1, WIDTH), F32),
        ],
        compiler_params=params(LESS),
        cost_estimate=pl.CostEstimate(
            flops=4 * 2 * LMAX * WIDTH * WIDTH, bytes_accessed=38 * LMAX * WIDTH, transcendentals=0
        ),
        name="close",
    )(
        sc,
        tokens.reshape(slab),
        *(x.reshape(half) for x in (res_own, res_got, out_own, out_got)),
        own,
        far,
        gain,
        w_own,
        w_far,
    )


PACK_DOWN, PACK_UP, PACK_OUT, PACK_VALUE, PACK_GAIN, PACK = 0, 192, 384, 432, 480, 496


def pack_kernel(sc, down, up, out, value, gain, down_far, up_far, out_far, value_far, gain_far, packed):
    first = sc[CORE] == 0

    def both(own, far, lanes):
        own, far = own[:, lanes], far[:, lanes]
        return jnp.concatenate([jnp.where(first, own, far), jnp.where(first, far, own)], axis=0)

    def side(own, far):
        return both(own, far, own_lanes(sc))

    packed[PACK_DOWN:PACK_UP] = side(down, down_far)
    for j in range(4):
        lanes = pl.ds(pl.multiple_of((4 * sc[CORE] + j) * SIDE, 128), SIDE)
        packed[PACK_UP + 48 * j : PACK_UP + 48 * (j + 1)] = both(up, up_far, lanes)
    packed[PACK_OUT:PACK_VALUE] = side(out, out_far)
    packed[PACK_VALUE:PACK_GAIN] = side(value, value_far)
    packed[PACK_GAIN:] = both(gain, gain_far, slice(0, SIDE))


def run_pack(sc, own, far):
    return pl.pallas_call(
        pack_kernel,
        grid_spec=pltpu.PrefetchScalarGridSpec(
            num_scalar_prefetch=1,
            grid=(1,),
            in_specs=[held(x.shape) for x in (*own, *far)],
            out_specs=held((PACK, SIDE)),
        ),
        out_shape=jax.ShapeDtypeStruct((PACK, SIDE), BF16),
        compiler_params=params(VMEM),
        cost_estimate=pl.CostEstimate(flops=0, bytes_accessed=6 * PACK * SIDE, transcendentals=0),
        name="pack",
    )(sc, *own, *far)


def chip_of(sc, k, rel):
    return plane_of(k, sc) * 4 + (sc[PLACE] ^ rel)


def place_kernel(moves, sc, *refs):
    pieces, targets, sems = refs[:16], refs[16:-1], refs[-1]
    copies = []
    for index, piece in enumerate(pieces):
        chip = chip_of(sc, index // 4, index % 4)
        for which, (start, count, lane, target, step, offset, column) in enumerate(moves):
            rows = pl.ds(pl.multiple_of(chip * step + offset, 16), count)
            copies.append(
                pltpu.make_async_copy(
                    piece.at[pl.ds(start, count), pl.ds(lane, SIDE)],
                    targets[target].at[rows, pl.ds(column, SIDE)],
                    sems.at[index, which],
                )
            )
    for copy in copies:
        copy.start()
    for copy in copies:
        copy.wait()


def run_place(sc, pieces, moves, shapes):
    return pl.pallas_call(
        partial(place_kernel, moves),
        grid_spec=pltpu.PrefetchScalarGridSpec(
            num_scalar_prefetch=1,
            grid=(1,),
            in_specs=anywhere(16),
            out_specs=[held(shape) for shape in shapes],
            scratch_shapes=[pltpu.SemaphoreType.DMA((16, len(moves)))],
        ),
        out_shape=[jax.ShapeDtypeStruct(shape, BF16) for shape in shapes],
        compiler_params=params(VMEM),
        cost_estimate=pl.CostEstimate(
            flops=0, bytes_accessed=4 * sum(a * b for a, b in shapes), transcendentals=0
        ),
        name="place",
    )(sc, *pieces)


def place_weights(sc, pieces):
    moves = (
        (PACK_DOWN, 192, 0, 0, 192, 0, 0),
        *((PACK_UP + 48 * j, 48, 0, 1, 48, 0, j * SIDE) for j in range(4)),
        (PACK_OUT, 48, 0, 2, 48, 0, 0),
        (PACK_VALUE, 48, 0, 3, 48, 0, 0),
        (PACK_GAIN, 16, 0, 4, 16, 0, 0),
    )
    shapes = [(FF, SIDE), (WIDTH, FF // 2), (WIDTH, SIDE), (WIDTH, SIDE), (256, SIDE)]
    return run_place(sc, pieces, moves, shapes)


def collect_kernel(sc, *refs):
    outs = refs[24:]
    for k in range(PLANES):

        @pl.when(pl.program_id(0) == k)
        def _():
            for rel in range(4):
                down, down_got, up, up_got, out, out_got = refs[6 * rel : 6 * rel + 6]
                packed = outs[4 * k + rel]
                packed[PACK_DOWN:PACK_UP] = add_low(down[...], down_got[...])
                for j in range(4):
                    lanes = slice(j * SIDE, (j + 1) * SIDE)
                    packed[PACK_UP + 48 * j : PACK_UP + 48 * (j + 1)] = add_low(up[:, lanes], up_got[:, lanes])
                packed[PACK_OUT:PACK_VALUE] = add_low(out[...], out_got[...])


def run_collect(sc, *sides):
    def rows(x, rel):
        return spec((x.shape[0] // 16, x.shape[1]), lambda k, s: (chip_of(s, k, rel), 0))

    return pl.pallas_call(
        collect_kernel,
        grid_spec=pltpu.PrefetchScalarGridSpec(
            num_scalar_prefetch=1,
            grid=(PLANES,),
            in_specs=[rows(x, rel) for rel in range(4) for x in sides],
            out_specs=[held((PACK_VALUE, SIDE))] * 16,
        ),
        out_shape=[jax.ShapeDtypeStruct((PACK_VALUE, SIDE), BF16)] * 16,
        compiler_params=params(LESS),
        cost_estimate=pl.CostEstimate(flops=0, bytes_accessed=3 * 16 * PACK_VALUE * SIDE * 2, transcendentals=0),
        name="collect",
    )(sc, *(x for _ in range(4) for x in sides))


def add_kernel(groups, *refs):
    for group, total in zip(groups, refs[-len(groups) :]):
        value = refs[group[0]][...].astype(F32)
        for index in group[1:]:
            value = value + refs[index][...].astype(F32)
        total[...] = value.astype(total.dtype)


def run_add(groups, values, dtype):
    shape = values[0].shape
    here = pl.BlockSpec(memory_space=pltpu.VMEM)
    return pl.pallas_call(
        partial(add_kernel, groups),
        in_specs=[here] * len(values),
        out_specs=[here] * len(groups),
        out_shape=[jax.ShapeDtypeStruct(shape, dtype)] * len(groups),
        compiler_params=params(LESS),
        cost_estimate=pl.CostEstimate(
            flops=0, bytes_accessed=2 * shape[0] * shape[1] * (len(values) + len(groups)), transcendentals=0
        ),
        name="add",
    )(*values)


DEVICES = 32
TO_CORE, TO_X, TO_Y = 1, 2, 4


def swap(x, bit):
    return lax.ppermute(x, BOTH, [(d, d ^ bit) for d in range(DEVICES)])


def ring(x, way=1):
    return lax.ppermute(x, BOTH, [(d, (d + 8 * way) % DEVICES) for d in range(DEVICES)])


def pick(x, index, axis=0):
    return lax.dynamic_index_in_dim(x, index, axis, keepdims=False)


def ordered(flag, one, two, axis=0, joined=jnp.stack):
    return jnp.where(flag == 0, joined([one, two], axis), joined([two, one], axis))


def add_low(one, two):
    return (one.astype(F32) + two.astype(F32)).astype(BF16)


STEPS = (
    ((0, 0, 1), (0, 1, 0), (1, 0, 0)),
    ((1, 0, 1), (0, 1, 1), (2, 0, 0)),
    ((2, 0, 1), (1, 1, 0), (3, 0, 0)),
    ((1, 1, 1), (2, 1, 1), (2, 1, 0)),
    ((3, 0, 1), (3, 1, 0), (3, 1, 1)),
)


def gather_step(have, step):
    by_x, by_y, by_z = STEPS[step]
    return {
        **have,
        by_z: ring(have[by_z[0] - 1, by_z[1], by_z[2]]),
        by_x: swap(have[by_x[0], by_x[1], 0], TO_X),
        by_y: swap(have[by_y[0], 0, by_y[2]], TO_Y),
    }


def in_order(have):
    return [have[k, y, x] for k in range(4) for y in range(2) for x in range(2)]


def by_place(shares, planes=range(PLANES)):
    return {(k, i // 2, i % 2): shares[4 * at + i] for at, k in enumerate(planes) for i in range(4)}


def scatter_send(have, step):
    by_x, by_y, by_z = STEPS[len(STEPS) - 1 - step]
    got = (ring(have[by_z], -1), swap(have[by_x], TO_X), swap(have[by_y], TO_Y))
    return {at: value for at, value in have.items() if at not in (by_x, by_y, by_z)}, got


def scatter_add(have, got, step):
    by_x, by_y, by_z = STEPS[len(STEPS) - 1 - step]
    targets = ((by_z[0] - 1, by_z[1], by_z[2]), (by_x[0], by_x[1], 0), (by_y[0], 0, by_y[2]))
    sums = list(dict.fromkeys(targets))
    groups = [(len(got) + i, *(j for j in range(len(got)) if targets[j] == at)) for i, at in enumerate(sums)]
    values = [*got, *(have[at] for at in sums)]
    return {**have, **dict(zip(sums, run_add(groups, values, F32 if step == len(STEPS) - 1 else BF16)))}


together = lax.optimization_barrier


def chip_shards(tokens, lengths, rand_mix, w_value, w_out, w_up, w_down, gain_mix, gain_ffn, grad_out):
    wide = lax.axis_index("wide")
    core = lax.axis_index("narrow")
    z, y, x = wide // 4, (wide // 2) % 2, wide % 2
    other = lambda value: swap(value, TO_CORE)
    side = partial(ordered, core, joined=jnp.concatenate)
    slab = (2, RUNS, 2, HALF, WIDTH)
    tokens, grad_out = tokens.reshape(slab), grad_out.reshape(slab)

    gains = jnp.pad(jnp.concatenate([gain_mix, gain_ffn])[None], ((0, 7), (0, SIDE - 48)))
    own = (w_down, w_up, w_out, w_value, gains)
    far = tuple(other(value) for value in own)
    near_sc = jnp.concatenate([jnp.stack([core, z, wide % 4]).astype(jnp.int32), lengths, lengths])
    weights = {(0, 0, 0): run_pack(near_sc, own, far)}

    rand = rand_mix.reshape(3, 2, HALF, LMAX)
    blocks = side(pick(rand, core, 1), other(pick(rand, 1 - core, 1)), 0)
    weights, rands, late_tokens, late_grad = together(
        (gather_step(weights, 0), {(0, 0, 0): blocks.reshape(SUBS * HALF, LMAX)}, tokens, grad_out)
    )
    weights, tokens_far = together((gather_step(weights, 1), other(pick(late_tokens, 1 - core, 2))))
    weights, grad_far = together((gather_step(weights, 2), other(pick(late_grad, 1 - core, 2))))
    weights, far_lengths = together((gather_step(weights, 3), other(lengths)))
    sc = jnp.concatenate([near_sc[:5], far_lengths])
    weights, rands = together((gather_step(weights, 4), rands))

    rands = gather_step(rands, 0)
    down, up, out, value, gain_rows = place_weights(sc, in_order(weights))
    rands, value, value_far, gain_rows, out, down, up = together(
        (rands, value, other(value), gain_rows, out, down, up)
    )
    gain_rows = gain_rows.reshape(16, 2, 8, SIDE)[:, :, 0]
    gain_one = gain_rows[..., :24].reshape(1, WIDTH).astype(F32)
    gain_two = gain_rows[..., 24:48].reshape(1, WIDTH).astype(F32)
    rands = gather_step(rands, 1)
    v_own = run_values(sc, tokens.reshape(2, LMAX, WIDTH), gain_one, value, value_far)
    rands, v_own, out, down, up = together((rands, v_own, (out, other(out)), down, up))
    rands, v_own, v_far, grad_far, down, up = together(
        (gather_step(rands, 2), v_own, other(v_own), grad_far, down, up)
    )
    rands = gather_step(rands, 3)
    masked = run_masked(sc, grad_out, grad_far)
    rands, v_far, masked, down, up = together((rands, v_far, masked, down, up))
    near = [rands[k, y_at, x_at] for k in range(3) for y_at in range(2) for x_at in range(2)]
    rands = gather_step(rands, 4)
    mixing = run_mix(sc, (0, 1, 2), near, v_own, v_far, ())
    rands, down, up, mixing = together((rands, down, up, mixing))
    heads, mean, exps, inverse = run_mix(sc, (3,), in_order(rands)[12:], v_own, v_far, mixing)
    down, up = (down, other(down)), (up, other(up))

    mixed, resid, normed = run_pre(sc, tokens, tokens_far, heads, out, gain_two)
    active, up_grad = run_units(sc, normed, masked, up, down)
    res_own, res_far, grad_heads, d_gain_two = run_post(sc, resid, up_grad, masked, up, out, gain_two)

    backward = lambda planes, carry: run_unmix(sc, planes, v_own, v_far, grad_heads, mean, exps, inverse, carry)
    *far, back_own, back_far = backward((3,), ())
    far, back_own, back_far, res_got = together((far, back_own, back_far, other(res_far)))
    have, got = scatter_send(by_place(far, (3,)), 0)
    *near, back_own, back_far = backward((2, 1, 0), (back_own, back_far))
    have, got, near, back_own, back_far = together((have, got, near, back_own, back_far))
    have = scatter_add({**have, **by_place(near, (2, 1, 0))}, got, 0)

    have, got = scatter_send(have, 1)
    up_own, up_far = run_up_grad(sc, normed, up_grad)
    have, got, up_own, up_far, back_got = together((have, got, up_own, up_far, other(back_far)))
    have = scatter_add(have, got, 1)

    have, got = scatter_send(have, 2)
    down_own, down_far = run_down_grad(sc, active, masked)
    have, got, down_own, down_far, up_got = together((have, got, down_own, down_far, other(up_far)))
    have = scatter_add(have, got, 2)

    have, got = scatter_send(have, 3)
    d_out_own, d_out_far = run_out_grad(sc, mixed, res_own, res_far)
    packed = run_collect(sc, down_own, other(down_far), up_own, up_got, d_out_own, other(d_out_far))
    have, got, packed = together((have, got, packed))
    have = scatter_add(have, got, 3)

    have, got = scatter_send(have, 4)
    sums, sums_got = scatter_send(by_place(packed), 0)
    out_own, out_far = run_out(sc, active, resid, down)
    have, got, sums, sums_got, out_own, out_far = together((have, got, sums, sums_got, out_own, out_far))
    rand_sum = scatter_add(have, got, 4)[0, 0, 0].reshape(2, 3, HALF, LMAX)

    sums, got = scatter_send(scatter_add(sums, sums_got, 0), 1)
    output, tokens_grad, d_value, d_gain_one = run_close(
        sc, tokens, res_own, res_got, out_own, other(out_far), back_own, back_got, gain_one, value, value_far
    )
    gain_pair = jnp.stack([d_gain_one.reshape(16, 2, 24), d_gain_two.reshape(16, 2, 24)], 2).reshape(16, 2, 1, 48)
    gain_pair = jnp.pad(gain_pair.astype(BF16), ((0, 0), (0, 0), (0, 7), (0, WIDTH - 48)))
    small = jnp.concatenate([d_value.reshape(16, 2, 24, WIDTH), gain_pair], 2).reshape(4, 2, 2, 2, 32, WIDTH)
    sums, got, output, tokens_grad, small = together((sums, got, output, tokens_grad, small))
    sums = scatter_add(sums, got, 1)

    sums, got = scatter_send(sums, 2)
    share = lambda to_x, to_core: pick(pick(small, to_core, 3), to_x, 2)
    small = (
        share(x, core).astype(F32)
        + other(share(x, 1 - core)).astype(F32)
        + swap(share(1 - x, core), TO_X).astype(F32)
        + swap(share(1 - x, 1 - core), TO_X | TO_CORE).astype(F32)
    ).astype(BF16)
    sums, got, small = together((sums, got, small))
    sums = scatter_add(sums, got, 2)

    sums, got = scatter_send(sums, 3)
    small = add_low(pick(small, y, 1), swap(pick(small, 1 - y, 1), TO_Y))
    blocks, blocks_far = pick(rand_sum, core), other(pick(rand_sum, 1 - core))
    sums, got, small, blocks, blocks_far = together((sums, got, small, blocks, blocks_far))
    sums = scatter_add(sums, got, 3)

    sums, got = scatter_send(sums, 4)
    small_sum = pick(small, z).astype(F32)
    for k in range(1, PLANES):
        small_sum = small_sum + ring(pick(small, lax.rem(z + PLANES - k, PLANES)), -k).astype(F32)
    sums, got, small_sum = together((sums, got, small_sum))
    big_sum = scatter_add(sums, got, 4)[0, 0, 0]
    big_far = other(big_sum)

    rows_of = lambda value, rows: pick(value.reshape(-1, 2, rows, SIDE), core, 1)
    mine = lambda own, far, rows: side(rows_of(own, rows)[0], rows_of(far, rows)[0], 1)
    down_shard = mine(big_sum[PACK_DOWN:PACK_UP], big_far[PACK_DOWN:PACK_UP], 96)
    up_side = lambda value: rows_of(value[PACK_UP:PACK_OUT], 24).transpose(1, 0, 2).reshape(24, 4 * SIDE)
    up_shard = side(up_side(big_sum), up_side(big_far), 1)
    outproj_shard = mine(big_sum[PACK_OUT:PACK_VALUE], big_far[PACK_OUT:PACK_VALUE], 24)
    rand_shard = ordered(core, blocks, blocks_far, 1)

    return (
        output.reshape(2, LMAX, WIDTH),
        tokens_grad.reshape(2, LMAX, WIDTH),
        rand_shard.reshape(3 * 128, LMAX),
        small_sum[:24],
        outproj_shard,
        up_shard,
        down_shard,
        small_sum[24, :24],
        small_sum[24, 24:48],
    )


def rms_norm(values, gain):
    scale = lax.rsqrt(jnp.mean(values * values, axis=-1, keepdims=True) + EPSILON)
    return values * scale * gain


def split_heads(block):
    return block.reshape(LMAX, HEADS, HEAD).transpose(1, 0, 2)


def merge_heads(block):
    return block.transpose(1, 0, 2).reshape(LMAX, HEADS * HEAD)


def masked_scores(key_mask, rand_head):
    return jnp.where(key_mask[None, :] > 0, rand_head.astype(jnp.float32), -1e30)


def head_forward(key_mask, paired):
    rand_head, value_head = paired
    scores = masked_scores(key_mask, rand_head)
    row_peak = jnp.max(scores, axis=-1, keepdims=True)
    exponent = jnp.exp(scores - row_peak)
    denom_sum = jnp.sum(exponent, axis=-1, keepdims=True)
    attention = exponent / denom_sum * key_mask[:, None]
    mixed = jnp.dot(attention.astype(jnp.bfloat16), value_head, preferred_element_type=jnp.float32)
    return (mixed.astype(jnp.bfloat16), row_peak + jnp.log(denom_sum))


def head_backward(key_mask, paired):
    rand_head, value_head, mix_grad, log_total = paired
    scores = masked_scores(key_mask, rand_head)
    attention = jnp.exp(scores - log_total) * key_mask[:, None]
    prob_grad = jnp.einsum("id,jd->ij", mix_grad, value_head, preferred_element_type=jnp.float32)
    value_grad = jnp.einsum(
        "ij,id->jd", attention.astype(jnp.bfloat16), mix_grad, preferred_element_type=jnp.float32
    )
    score_grad = attention * (prob_grad - jnp.sum(prob_grad * attention, axis=-1, keepdims=True))
    return (score_grad, value_grad)


def shards(tokens, lengths, rand_mix, w_value, w_out, w_up, w_down, gain_mix, gain_ffn, grad_out):
    item_count = tokens.shape[0]
    width = tokens.shape[2]
    row_count = item_count * LMAX
    tokens_flat = tokens.reshape(row_count, width).astype(jnp.float32)
    positions = jnp.arange(LMAX, dtype=jnp.int32)
    valid_table = (positions[None, :] < lengths[:, None]).astype(jnp.float32)
    row_valid = valid_table.reshape(row_count, 1)
    forward_set = (
        lax.all_gather(rand_mix, ("wide", "narrow"), axis=0, tiled=True),
        lax.all_gather(w_value, ("wide", "narrow"), axis=0, tiled=True),
        lax.all_gather(w_out, ("wide", "narrow"), axis=0, tiled=True),
        lax.all_gather(w_up, ("wide", "narrow"), axis=0, tiled=True),
        lax.all_gather(w_down, ("wide", "narrow"), axis=0, tiled=True),
        lax.all_gather(gain_mix, ("wide", "narrow"), axis=0, tiled=True),
        lax.all_gather(gain_ffn, ("wide", "narrow"), axis=0, tiled=True),
    )
    rand_all, value_all, out_all, up_all, down_all, gain_first, gain_second = forward_set
    normed = rms_norm(tokens_flat, gain_first.astype(jnp.float32)).astype(jnp.bfloat16)
    values = jnp.dot(normed, value_all, preferred_element_type=jnp.float32).astype(jnp.bfloat16)
    rand_heads = rand_all.reshape(HEADS, LMAX, LMAX)
    mixed_parts = []
    totals_kept = []
    for item_index in range(item_count):
        item_values = split_heads(values[item_index * LMAX : (item_index + 1) * LMAX])
        mixed_heads, log_total = lax.map(
            partial(head_forward, valid_table[item_index]), (rand_heads, item_values)
        )
        mixed_parts.append(merge_heads(mixed_heads))
        totals_kept.append(log_total)
    mixed = jnp.concatenate(mixed_parts, axis=0)
    residual = tokens_flat + jnp.dot(mixed, out_all, preferred_element_type=jnp.float32)
    normed_two = rms_norm(residual, gain_second.astype(jnp.float32)).astype(jnp.bfloat16)
    up_proj = jnp.dot(normed_two, up_all, preferred_element_type=jnp.float32)
    active = jax.nn.gelu(up_proj).astype(jnp.bfloat16)
    branch = jnp.dot(active, down_all, preferred_element_type=jnp.float32)
    output = row_valid * (residual + branch)
    back_set = (
        lax.all_gather(rand_mix, ("wide", "narrow"), axis=0, tiled=True),
        lax.all_gather(w_value, ("wide", "narrow"), axis=0, tiled=True),
        lax.all_gather(w_out, ("wide", "narrow"), axis=0, tiled=True),
        lax.all_gather(w_up, ("wide", "narrow"), axis=0, tiled=True),
        lax.all_gather(w_down, ("wide", "narrow"), axis=0, tiled=True),
        lax.all_gather(gain_mix, ("wide", "narrow"), axis=0, tiled=True),
        lax.all_gather(gain_ffn, ("wide", "narrow"), axis=0, tiled=True),
    )
    rand_back, value_back, out_back, up_back, down_back, gain_back_one, gain_back_two = back_set
    cotangent = grad_out.reshape(row_count, width).astype(jnp.float32)
    masked = row_valid * cotangent
    branch_grad = masked.astype(jnp.bfloat16)
    grad_down = jnp.einsum("rk,rd->kd", active, branch_grad, preferred_element_type=jnp.float32)
    active_grad = jnp.einsum(
        "rd,kd->rk", branch_grad, down_back, preferred_element_type=jnp.float32
    )
    gelu_value, gelu_pull = jax.vjp(jax.nn.gelu, up_proj)
    up_grad = gelu_pull(active_grad)[0].astype(jnp.bfloat16)
    grad_up = jnp.einsum("rd,rk->dk", normed_two, up_grad, preferred_element_type=jnp.float32)
    normed_two_grad = jnp.einsum("rk,dk->rd", up_grad, up_back, preferred_element_type=jnp.float32)
    norm_value, norm_pull = jax.vjp(rms_norm, residual, gain_back_two.astype(jnp.float32))
    residual_part, gain_two_grad = norm_pull(normed_two_grad)
    residual_grad = masked + residual_part
    attn_grad = residual_grad.astype(jnp.bfloat16)
    grad_outproj = jnp.einsum("rd,re->de", mixed, attn_grad, preferred_element_type=jnp.float32)
    mixed_grad = jnp.einsum(
        "re,de->rd", attn_grad, out_back, preferred_element_type=jnp.float32
    ).astype(jnp.bfloat16)
    rand_heads_back = rand_back.reshape(HEADS, LMAX, LMAX)
    rand_grad = jnp.zeros((HEADS, LMAX, LMAX), jnp.float32)
    value_parts = []
    for item_index in range(item_count):
        lower_row = item_index * LMAX
        upper_row = lower_row + LMAX
        item_values = split_heads(values[lower_row:upper_row])
        item_mix_grad = split_heads(mixed_grad[lower_row:upper_row])
        score_grad, value_grad = lax.map(
            partial(head_backward, valid_table[item_index]),
            (rand_heads_back, item_values, item_mix_grad, totals_kept[item_index]),
        )
        rand_grad = rand_grad + score_grad
        value_parts.append(merge_heads(value_grad))
    values_grad = jnp.concatenate(value_parts, axis=0).astype(jnp.bfloat16)
    grad_value = jnp.einsum("rd,re->de", normed, values_grad, preferred_element_type=jnp.float32)
    normed_grad = jnp.einsum(
        "re,de->rd", values_grad, value_back, preferred_element_type=jnp.float32
    )
    norm_first, first_pull = jax.vjp(rms_norm, tokens_flat, gain_back_one.astype(jnp.float32))
    token_part, gain_one_grad = first_pull(normed_grad)
    tokens_grad = residual_grad + token_part
    rand_flat = rand_grad.reshape(HEADS * LMAX, LMAX)
    all_shards = (
        lax.psum_scatter(rand_flat, ("wide", "narrow"), scatter_dimension=0, tiled=True),
        lax.psum_scatter(grad_value, ("wide", "narrow"), scatter_dimension=0, tiled=True),
        lax.psum_scatter(grad_outproj, ("wide", "narrow"), scatter_dimension=0, tiled=True),
        lax.psum_scatter(grad_up, ("wide", "narrow"), scatter_dimension=0, tiled=True),
        lax.psum_scatter(grad_down, ("wide", "narrow"), scatter_dimension=0, tiled=True),
        lax.psum_scatter(gain_one_grad, ("wide", "narrow"), scatter_dimension=0, tiled=True),
        lax.psum_scatter(gain_two_grad, ("wide", "narrow"), scatter_dimension=0, tiled=True),
    )
    rand_shard, value_shard, outproj_shard, up_shard, down_shard, gain_one_shard, gain_two_shard = (
        all_shards
    )
    return (
        output.reshape(item_count, LMAX, width),
        tokens_grad.reshape(item_count, LMAX, width),
        rand_shard,
        value_shard,
        outproj_shard,
        up_shard,
        down_shard,
        gain_one_shard,
        gain_two_shard,
    )


def solution(mesh):
    in_specs = (
        P(("wide", "narrow"), None, None),
        P(("wide", "narrow")),
        P(("wide", "narrow"), None),
        P(("wide", "narrow"), None),
        P(("wide", "narrow"), None),
        P(("wide", "narrow"), None),
        P(("wide", "narrow"), None),
        P(("wide", "narrow")),
        P(("wide", "narrow")),
        P(("wide", "narrow"), None, None),
    )
    out_specs = (
        P(("wide", "narrow"), None, None),
        P(("wide", "narrow"), None, None),
        P(("wide", "narrow"), None),
        P(("wide", "narrow"), None),
        P(("wide", "narrow"), None),
        P(("wide", "narrow"), None),
        P(("wide", "narrow"), None),
        P(("wide", "narrow")),
        P(("wide", "narrow")),
    )
    fits = dict(mesh.shape) == {"wide": 16, "narrow": 2}
    return jax.shard_map(chip_shards if fits else shards, mesh=mesh, in_specs=in_specs, out_specs=out_specs, check_vma=False)
```

```python
from functools import partial

import jax
import jax.numpy as jnp
from jax import lax
from jax.experimental import pallas as pl
from jax.experimental.pallas import tpu as pltpu
from jax.sharding import PartitionSpec as P

HEADS = 12
HEAD = 64
LMAX = 1024
WIDTH = 768
FF = 3072
EPSILON = 1e-05

BOTH = ("wide", "narrow")
BF16 = jnp.bfloat16
F32 = jnp.float32
VMEM = 61 << 20
LESS = 34 << 20

SUBS = 6
RUNS = 8
HALF = 64
HROWS = RUNS * HALF
PLANES = 4
PHEADS = HEADS // PLANES
ROWS = 2 * LMAX
FSTEP = 768
FSIDE = FF // 2 // FSTEP
TILE = 512
SIDE = WIDTH // 2
SPAN = 2 * HALF


def dot(a, b, ca, cb):
    return lax.dot_general(a, b, (((ca,), (cb,)), ((), ())), preferred_element_type=F32)


CORE, PLANE, PLACE, LENGTHS = 0, 1, 2, 3


def spec(shape, index):
    return pl.BlockSpec(shape, index)


def held(shape):
    zeros = (0,) * len(shape)
    return pl.BlockSpec(shape, lambda *_: zeros, pipeline_mode=pl.Buffered(1))


def params(limit):
    return pltpu.CompilerParams(vmem_limit_bytes=limit)


def whole_weight(sc, step, own, far, weight):
    @pl.when(step == 0)
    def _():
        weight[:, pl.ds(pl.multiple_of(sc[CORE] * SIDE, 128), SIDE)] = own[...]
        weight[:, pl.ds(pl.multiple_of((1 - sc[CORE]) * SIDE, 128), SIDE)] = far[...]


def values_kernel(sc, tok, gain, w_own, w_far, out, weight):
    step = pl.program_id(0)
    whole_weight(sc, step, w_own, w_far, weight)
    rows = tok.shape[1]
    position = step * rows + lax.broadcasted_iota(jnp.int32, (rows, 1), 0)
    for item in range(2):
        x = tok[item].astype(F32)
        scale = lax.rsqrt(jnp.mean(x * x, axis=-1, keepdims=True) + EPSILON)
        normed = (x * scale * gain[...]).astype(BF16)
        found = dot(normed, weight[...], 1, 0)
        found = jnp.where(position < sc[LENGTHS + item], found, 0.0).astype(BF16)
        for head in range(HEADS):
            out[head, :, item * HEAD : (item + 1) * HEAD] = found[:, head * HEAD : (head + 1) * HEAD]


def run_values(sc, tokens, gain, w_own, w_far):
    rows = 256
    return pl.pallas_call(
        values_kernel,
        grid_spec=pltpu.PrefetchScalarGridSpec(
            num_scalar_prefetch=1,
            grid=(LMAX // rows,),
            in_specs=[
                spec((2, rows, WIDTH), lambda j, s: (0, j, 0)),
                held((1, WIDTH)),
                held((WIDTH, SIDE)),
                held((WIDTH, SIDE)),
            ],
            out_specs=spec((HEADS, rows, 2 * HEAD), lambda j, s: (0, j, 0)),
            scratch_shapes=[pltpu.VMEM((WIDTH, WIDTH), BF16)],
        ),
        out_shape=jax.ShapeDtypeStruct((HEADS, LMAX, 2 * HEAD), BF16),
        compiler_params=params(VMEM),
        cost_estimate=pl.CostEstimate(
            flops=2 * 2 * LMAX * WIDTH * WIDTH, bytes_accessed=8 * LMAX * WIDTH, transcendentals=0
        ),
        name="values",
    )(sc, tokens, gain, w_own, w_far)


def lane_lengths(sc, shape):
    slot = lax.broadcasted_iota(jnp.int32, shape, 1) // HEAD
    length = jnp.where(slot == 0, sc[LENGTHS], sc[LENGTHS + 1])
    return jnp.where(slot >= 2, jnp.where(slot == 2, sc[LENGTHS + 2], sc[LENGTHS + 3]), length)


def plane_of(k, sc):
    return lax.rem(sc[PLANE] + PLANES - k, PLANES)


def plane_spec(planes, rows, lanes):
    def index(step, sc):
        return (plane_of(planes[0] + step * (planes[-1] - planes[0]) // max(len(planes) - 1, 1), sc), 0, 0)

    return spec((PHEADS, rows, lanes), index)


def anywhere(count):
    return [pl.BlockSpec(memory_space=pl.ANY)] * count


def plane_fetch(place, shards, raw, sems, slot):
    return [
        pltpu.make_async_copy(
            shards[4 * slot + rel],
            raw.at[slot, pl.ds(pl.multiple_of((place ^ rel) * SUBS * HALF, SUBS * HALF), SUBS * HALF)],
            sems.at[slot, rel],
        )
        for rel in range(4)
    ]


def take_plane(place, shards, raw, sems):
    step = pl.program_id(0)
    count = len(shards) // 4

    @pl.when(step == 0)
    def _():
        for slot in range(count):
            for copy in plane_fetch(place, shards, raw, sems, slot):
                copy.start()

    for slot in range(count):

        @pl.when(step == slot)
        def _():
            for copy in plane_fetch(place, shards, raw, sems, slot):
                copy.wait()

    return step


def head_rows(head):
    return slice(head * HROWS, (head + 1) * HROWS)


def fill_mask(sc, mask):
    @pl.when(pl.program_id(0) == 0)
    def _():
        shape = (LMAX, 4 * HEAD)
        column = lax.broadcasted_iota(jnp.int32, shape, 0)
        mask[...] = (column < lane_lengths(sc, shape)).astype(F32).astype(BF16)


def mix_kernel(count, carried, sc, *refs):
    shards, (v_own, v_far, *rest) = refs[: 4 * count], refs[4 * count :]
    mixed, mean, exps, inverse, raw, mask, sems = rest[4:] if carried else rest
    fill_mask(sc, mask)
    slot = take_plane(sc[PLACE], shards, raw, sems)
    shape = (HROWS, 4 * HEAD)
    line = lax.broadcasted_iota(jnp.int32, shape, 0)
    position = 128 * (line // HALF) + HALF * sc[CORE] + line % HALF
    valid = position < lane_lengths(sc, shape)
    for head in range(PHEADS):
        weights = jnp.exp(raw[slot, head_rows(head)].astype(F32)).astype(BF16)
        exps[head] = weights
        both = dot(weights, jnp.concatenate([v_own[head], v_far[head], mask[...]], axis=1), 1, 0)
        flip = jnp.where(valid, 1.0 / both[:, 4 * HEAD :], 0.0)
        found = both[:, : 4 * HEAD] * flip
        inverse[head] = flip.astype(BF16)
        mean[head] = found
        mixed[head] = found.astype(BF16)


def run_mix(sc, planes, shards, v_own, v_far, carry):
    carry, count = list(carry), len(planes)
    shape = (HEADS, HROWS, 4 * HEAD)
    return pl.pallas_call(
        partial(mix_kernel, count, bool(carry)),
        grid_spec=pltpu.PrefetchScalarGridSpec(
            num_scalar_prefetch=1,
            grid=(count,),
            in_specs=anywhere(4 * count) + [plane_spec(planes, LMAX, 2 * HEAD)] * 2 + anywhere(len(carry)),
            out_specs=[
                plane_spec(planes, HROWS, 4 * HEAD),
                plane_spec(planes, HROWS, 4 * HEAD),
                plane_spec(planes, HROWS, LMAX),
                plane_spec(planes, HROWS, 4 * HEAD),
            ],
            scratch_shapes=[
                pltpu.VMEM((count, 4 * SUBS * HALF, LMAX), BF16),
                pltpu.VMEM((LMAX, 4 * HEAD), BF16),
                pltpu.SemaphoreType.DMA((count, 4)),
            ],
        ),
        out_shape=[
            jax.ShapeDtypeStruct(shape, BF16),
            jax.ShapeDtypeStruct(shape, F32),
            jax.ShapeDtypeStruct((HEADS, HROWS, LMAX), BF16),
            jax.ShapeDtypeStruct(shape, BF16),
        ],
        input_output_aliases={3 + 4 * count + i: i for i in range(len(carry))},
        compiler_params=params(VMEM),
        cost_estimate=pl.CostEstimate(
            flops=2 * HEADS * HROWS * LMAX * 4 * HEAD,
            bytes_accessed=HEADS * (2 * HROWS * LMAX + 5 * HROWS * 256),
            transcendentals=HEADS * HROWS * LMAX // 2,
        ),
        name="mix",
    )(sc, *shards, v_own, v_far, *carry)


def row_valid(sc, step):
    line = lax.broadcasted_iota(jnp.int32, (4 * SPAN, 1), 0)
    item = line // SPAN
    row = step * SPAN + line % SPAN
    low = jnp.where(item == 0, sc[LENGTHS], sc[LENGTHS + 1])
    high = jnp.where(item == 2, sc[LENGTHS + 2], sc[LENGTHS + 3])
    return 128 * (row // HALF) + HALF * sc[CORE] + row % HALF < jnp.where(item >= 2, high, low)


def four_items(own, far):
    return jnp.concatenate([own[:, :, 0], far[...]], axis=0).reshape(4 * SPAN, WIDTH)


def pre_kernel(sc, tok, tok_far, heads, wo_own, wo_far, gain, mixed, resid, normed, weight):
    step = pl.program_id(0)
    whole_weight(sc, step, wo_own, wo_far, weight)
    for item in range(4):
        lanes = slice(item * HEAD, (item + 1) * HEAD)
        for pair in range(HEADS // 2):
            both = jnp.concatenate([heads[2 * pair, :, lanes], heads[2 * pair + 1, :, lanes]], axis=1)
            mixed[item, :, pair * 128 : (pair + 1) * 128] = both
    res = four_items(tok, tok_far).astype(F32) + dot(mixed[...].reshape(4 * SPAN, WIDTH), weight[...], 1, 0)
    resid[...] = res.astype(BF16).reshape(4, SPAN, WIDTH)
    scale = lax.rsqrt(jnp.mean(res * res, axis=-1, keepdims=True) + EPSILON)
    valid = row_valid(sc, step)
    normed[...] = jnp.where(valid, res * scale * gain[...], 0.0).astype(BF16).reshape(4, SPAN, WIDTH)


def slab_spec(items=4):
    return spec((items, SPAN, WIDTH), lambda r, s: (0, r, 0))


def half_specs():
    return [
        spec((2, SPAN // HALF, 1, HALF, WIDTH), lambda r, s: (0, r, s[CORE], 0, 0)),
        spec((2, SPAN // HALF, HALF, WIDTH), lambda r, s: (0, r, 0, 0)),
    ]


def heads_spec():
    return spec((HEADS, SPAN, 4 * HEAD), lambda r, s: (0, r, 0))


def run_pre(sc, tokens, tokens_far, heads, wo, gain):
    return pl.pallas_call(
        pre_kernel,
        grid_spec=pltpu.PrefetchScalarGridSpec(
            num_scalar_prefetch=1,
            grid=(HROWS // SPAN,),
            in_specs=half_specs()
            + [heads_spec(), held((WIDTH, SIDE)), held((WIDTH, SIDE)), held((1, WIDTH))],
            out_specs=[slab_spec()] * 3,
            scratch_shapes=[pltpu.VMEM((WIDTH, WIDTH), BF16)],
        ),
        out_shape=[
            jax.ShapeDtypeStruct((4, HROWS, WIDTH), BF16),
            jax.ShapeDtypeStruct((4, HROWS, WIDTH), BF16),
            jax.ShapeDtypeStruct((4, HROWS, WIDTH), BF16),
        ],
        compiler_params=params(VMEM),
        cost_estimate=pl.CostEstimate(
            flops=2 * ROWS * WIDTH * WIDTH, bytes_accessed=16 * ROWS * WIDTH, transcendentals=0
        ),
        name="pre",
    )(sc, tokens, tokens_far, heads, *wo, gain)


def masked_kernel(sc, cot, cot_far, masked):
    value = jnp.where(row_valid(sc, pl.program_id(0)), four_items(cot, cot_far).astype(F32), 0.0)
    masked[...] = value.astype(BF16).reshape(4, SPAN, WIDTH)


def run_masked(sc, cotangent, cotangent_far):
    return pl.pallas_call(
        masked_kernel,
        grid_spec=pltpu.PrefetchScalarGridSpec(
            num_scalar_prefetch=1, grid=(HROWS // SPAN,), in_specs=half_specs(), out_specs=slab_spec()
        ),
        out_shape=jax.ShapeDtypeStruct((4, HROWS, WIDTH), BF16),
        compiler_params=params(VMEM),
        cost_estimate=pl.CostEstimate(flops=0, bytes_accessed=4 * ROWS * WIDTH, transcendentals=0),
        name="masked",
    )(sc, cotangent, cotangent_far)


def own_lanes(sc):
    return pl.ds(pl.multiple_of(sc[CORE] * SIDE, 128), SIDE)


def far_lanes(sc):
    return pl.ds(pl.multiple_of((1 - sc[CORE]) * SIDE, 128), SIDE)


def unit_rows(f, sc):
    return (lax.rem(FSIDE * sc[CORE] + f, 2 * FSIDE), 0)


def unit_columns(f, sc):
    return (0, lax.rem(FSIDE * sc[CORE] + f, 2 * FSIDE))


def early(f, sc):
    return (0, lax.min(f, FSIDE - 1))


def late(f, sc):
    return (0, lax.max(f - FSIDE, 0))


def units_kernel(sc, normed, cot, up_own, up_far, dn_own, dn_far, active, up_grad, w_up, w_down):
    step = pl.program_id(0)
    w_down[:, own_lanes(sc)] = dn_own[...]
    w_down[:, far_lanes(sc)] = dn_far[...]

    @pl.when(step < FSIDE)
    def _():
        w_up[...] = up_own[...]

    @pl.when(step >= FSIDE)
    def _():
        w_up[...] = up_far[...]

    for row in range(0, ROWS, 256):
        rows = slice(row, row + 256)
        for column in range(0, FSTEP, 256):
            columns = slice(column, column + 256)
            up = dot(normed[rows], w_up[:, columns], 1, 0)
            square = up * up
            bend = jnp.tanh(up * (0.7978845608028654 + (0.044715 * 0.7978845608028654) * square))
            share = 0.5 + 0.5 * bend
            act = up * share
            active[rows, columns] = act.astype(BF16)
            slope = share + act * (1.0 - share) * (
                2 * 0.7978845608028654 + (6 * 0.044715 * 0.7978845608028654) * square
            )
            up_grad[rows, columns] = (dot(cot[rows], w_down[columns], 1, 1) * slope).astype(BF16)


def run_units(sc, normed, cotangent, up, down):
    return pl.pallas_call(
        units_kernel,
        grid_spec=pltpu.PrefetchScalarGridSpec(
            num_scalar_prefetch=1,
            grid=(2 * FSIDE,),
            in_specs=[
                held((ROWS, WIDTH)),
                held((ROWS, WIDTH)),
                spec((WIDTH, FSTEP), early),
                spec((WIDTH, FSTEP), late),
                spec((FSTEP, SIDE), unit_rows),
                spec((FSTEP, SIDE), unit_rows),
            ],
            out_specs=[spec((ROWS, FSTEP), unit_columns), spec((ROWS, FSTEP), unit_columns)],
            scratch_shapes=[pltpu.VMEM((WIDTH, FSTEP), BF16), pltpu.VMEM((FSTEP, WIDTH), BF16)],
        ),
        out_shape=[jax.ShapeDtypeStruct((ROWS, FF), BF16), jax.ShapeDtypeStruct((ROWS, FF), BF16)],
        compiler_params=params(VMEM),
        cost_estimate=pl.CostEstimate(
            flops=4 * ROWS * WIDTH * FF, bytes_accessed=6 * ROWS * WIDTH + 4 * ROWS * FF, transcendentals=ROWS * FF
        ),
        name="units",
    )(sc, normed.reshape(ROWS, WIDTH), cotangent.reshape(ROWS, WIDTH), *up, *down)


def down_grad_kernel(sc, active, cot, own, far, total):
    total[...] = dot(active[...], cot[...], 0, 0).astype(BF16)
    own[...] = total[:, own_lanes(sc)]
    far[...] = total[:, far_lanes(sc)]


def run_down_grad(sc, active, cotangent):
    return pl.pallas_call(
        down_grad_kernel,
        grid_spec=pltpu.PrefetchScalarGridSpec(
            num_scalar_prefetch=1,
            grid=(FF // 512,),
            in_specs=[spec((ROWS, 512), lambda f, s: (0, f)), held((ROWS, WIDTH))],
            out_specs=[spec((512, SIDE), lambda f, s: (f, 0))] * 2,
            scratch_shapes=[pltpu.VMEM((512, WIDTH), BF16)],
        ),
        out_shape=[jax.ShapeDtypeStruct((FF, SIDE), BF16)] * 2,
        compiler_params=params(LESS),
        cost_estimate=pl.CostEstimate(
            flops=2 * ROWS * WIDTH * FF, bytes_accessed=2 * ROWS * (WIDTH + FF), transcendentals=0
        ),
        name="down_grad",
    )(sc, active, cotangent.reshape(ROWS, WIDTH))


def up_grad_kernel(sc, normed, up_grad, own, far):
    total = dot(normed[...], up_grad[...], 0, 0).astype(BF16)

    @pl.when(pl.program_id(0) < 3)
    def _():
        own[...] = total

    @pl.when(pl.program_id(0) >= 3)
    def _():
        far[...] = total


def run_up_grad(sc, normed, up_grad):
    return pl.pallas_call(
        up_grad_kernel,
        grid_spec=pltpu.PrefetchScalarGridSpec(
            num_scalar_prefetch=1,
            grid=(6,),
            in_specs=[held((ROWS, WIDTH)), spec((ROWS, 512), lambda f, s: (0, lax.rem(3 * s[CORE] + f, 6)))],
            out_specs=[
                spec((WIDTH, 512), lambda f, s: (0, lax.min(f, 2))),
                spec((WIDTH, 512), lambda f, s: (0, lax.max(f - 3, 0))),
            ],
        ),
        out_shape=[jax.ShapeDtypeStruct((WIDTH, FF // 2), BF16)] * 2,
        compiler_params=params(LESS),
        cost_estimate=pl.CostEstimate(
            flops=2 * ROWS * WIDTH * FF, bytes_accessed=2 * ROWS * (WIDTH + FF), transcendentals=0
        ),
        name="up_grad",
    )(sc, normed.reshape(ROWS, WIDTH), up_grad)


def out_grad_kernel(sc, mixed, res_own, res_far, own, far, total):
    step = pl.program_id(0)
    grad = jnp.concatenate([res_own[...], res_far[...]], axis=0).reshape(4 * SPAN, WIDTH)
    found = dot(mixed[...].reshape(4 * SPAN, WIDTH), grad, 0, 0)

    @pl.when(step == 0)
    def _():
        total[...] = found

    @pl.when(step > 0)
    def _():
        total[...] += found

    @pl.when(step == pl.num_programs(0) - 1)
    def _():
        own[...] = total[:, own_lanes(sc)].astype(BF16)
        far[...] = total[:, far_lanes(sc)].astype(BF16)


def run_out_grad(sc, mixed, res_own, res_far):
    return pl.pallas_call(
        out_grad_kernel,
        grid_spec=pltpu.PrefetchScalarGridSpec(
            num_scalar_prefetch=1,
            grid=(HROWS // SPAN,),
            in_specs=[slab_spec(), slab_spec(2), slab_spec(2)],
            out_specs=[held((WIDTH, SIDE))] * 2,
            scratch_shapes=[pltpu.VMEM((WIDTH, WIDTH), F32)],
        ),
        out_shape=[jax.ShapeDtypeStruct((WIDTH, SIDE), BF16)] * 2,
        compiler_params=params(LESS),
        cost_estimate=pl.CostEstimate(
            flops=2 * ROWS * WIDTH * WIDTH, bytes_accessed=4 * ROWS * WIDTH, transcendentals=0
        ),
        name="out_grad",
    )(sc, mixed, res_own, res_far)


def out_kernel(sc, active, resid, dn_own, dn_far, own, far, w_down):
    step = pl.program_id(0)

    @pl.when(step == 0)
    def _():
        w_down[:, own_lanes(sc)] = dn_own[...]
        w_down[:, far_lanes(sc)] = dn_far[...]

    branch = dot(active[...].reshape(4 * SPAN, FF), w_down[...], 1, 0)
    output = jnp.where(row_valid(sc, step), resid[...].reshape(4 * SPAN, WIDTH).astype(F32) + branch, 0.0)
    output = output.astype(BF16).reshape(4, SPAN, WIDTH)
    own[...] = output[:2]
    far[...] = output[2:]


def run_out(sc, active, resid, down):
    return pl.pallas_call(
        out_kernel,
        grid_spec=pltpu.PrefetchScalarGridSpec(
            num_scalar_prefetch=1,
            grid=(HROWS // SPAN,),
            in_specs=[
                spec((4, SPAN, FF), lambda r, s: (0, r, 0)),
                slab_spec(),
                held((FF, SIDE)),
                held((FF, SIDE)),
            ],
            out_specs=[slab_spec(2)] * 2,
            scratch_shapes=[pltpu.VMEM((FF, WIDTH), BF16)],
        ),
        out_shape=[
            jax.ShapeDtypeStruct((2, HROWS, WIDTH), BF16),
            jax.ShapeDtypeStruct((2, HROWS, WIDTH), BF16),
        ],
        compiler_params=params(LESS),
        cost_estimate=pl.CostEstimate(
            flops=2 * ROWS * WIDTH * FF, bytes_accessed=ROWS * (2 * FF + 7 * WIDTH), transcendentals=0
        ),
        name="out",
    )(sc, active.reshape(4, HROWS, FF), resid, *down)


def post_kernel(sc, resid, grad_own, grad_far, cot, up_own, up_far, wo_own, wo_far, gain, *refs):
    (res_own, res_far, heads, d_gain, weight, spread) = refs
    step = pl.program_id(0)
    whole_weight(sc, step, wo_own, wo_far, weight)
    shape, slab = (4 * SPAN, WIDTH), (4, SPAN, WIDTH)
    valid = row_valid(sc, step)
    res = resid[...].reshape(shape).astype(F32)
    scale = lax.rsqrt(jnp.mean(res * res, axis=-1, keepdims=True) + EPSILON)
    unit = res * scale
    units = (4 * SPAN, FF // 2)
    back = dot(grad_own[...].reshape(units), up_own[...], 1, 1) + dot(grad_far[...].reshape(units), up_far[...], 1, 1)
    two_grad = jnp.where(valid, back, 0.0)
    gained = two_grad * gain[...]
    masked = cot[...].reshape(shape).astype(F32)
    grad = masked + scale * (gained - unit * jnp.mean(gained * unit, axis=-1, keepdims=True))
    low = grad.astype(BF16)
    res_own[...] = low.reshape(slab)[:2]
    res_far[...] = low.reshape(slab)[2:]
    gain_sum = jnp.sum(two_grad * unit, axis=0, keepdims=True)

    @pl.when(step == 0)
    def _():
        d_gain[...] = gain_sum

    @pl.when(step > 0)
    def _():
        d_gain[...] += gain_sum

    spread[...] = dot(low, weight[...], 1, 1).astype(BF16).reshape(slab)
    for pair in range(HEADS // 2):
        lanes = slice(pair * 128, (pair + 1) * 128)
        for side in range(2):
            one, two = spread[2 * side, :, lanes], spread[2 * side + 1, :, lanes]
            half = slice(side * 128, (side + 1) * 128)
            heads[2 * pair, :, half] = jnp.concatenate([one[:, :HEAD], two[:, :HEAD]], axis=1)
            heads[2 * pair + 1, :, half] = jnp.concatenate([one[:, HEAD:], two[:, HEAD:]], axis=1)


def run_post(sc, resid, up_grad, cotangent, up, wo, gain):
    side = lambda which: spec((4, SPAN, FF // 2), lambda r, s: (0, r, s[CORE] if which == 0 else 1 - s[CORE]))
    up_grad = up_grad.reshape(4, HROWS, FF)
    return pl.pallas_call(
        post_kernel,
        grid_spec=pltpu.PrefetchScalarGridSpec(
            num_scalar_prefetch=1,
            grid=(HROWS // SPAN,),
            in_specs=[
                slab_spec(),
                side(0),
                side(1),
                slab_spec(),
                held((WIDTH, FF // 2)),
                held((WIDTH, FF // 2)),
                held((WIDTH, SIDE)),
                held((WIDTH, SIDE)),
                held((1, WIDTH)),
            ],
            out_specs=[slab_spec(2)] * 2 + [heads_spec(), held((1, WIDTH))],
            scratch_shapes=[
                pltpu.VMEM((WIDTH, WIDTH), BF16),
                pltpu.VMEM((4, SPAN, WIDTH), BF16),
            ],
        ),
        out_shape=[
            jax.ShapeDtypeStruct((2, HROWS, WIDTH), BF16),
            jax.ShapeDtypeStruct((2, HROWS, WIDTH), BF16),
            jax.ShapeDtypeStruct((HEADS, HROWS, 4 * HEAD), BF16),
            jax.ShapeDtypeStruct((1, WIDTH), F32),
        ],
        compiler_params=params(VMEM),
        cost_estimate=pl.CostEstimate(
            flops=2 * ROWS * WIDTH * (WIDTH + FF), bytes_accessed=ROWS * (16 * WIDTH + 2 * FF), transcendentals=0
        ),
        name="post",
    )(sc, resid, up_grad, up_grad, cotangent, *up, *wo, gain)


def unmix_kernel(count, carried, sc, v_own, v_far, grad_heads, mean, exps, inverse, *refs):
    refs = refs[2:] if carried else refs
    outs, (own, far, grads, mask, adder, bound, out_sems) = refs[: 4 * count], refs[4 * count :]
    place = sc[PLACE]
    step = pl.program_id(0)

    def leave(slot):
        return [
            pltpu.make_async_copy(
                grads.at[slot, pl.ds(pl.multiple_of((place ^ rel) * SUBS * HALF, SUBS * HALF), SUBS * HALF)],
                outs[4 * slot + rel],
                out_sems.at[slot, rel],
            )
            for rel in range(4)
        ]

    fill_mask(sc, mask)

    @pl.when(step == 0)
    def _():
        lane = lax.broadcasted_iota(jnp.int32, (4 * HEAD, 128), 0) // HEAD
        column = lax.broadcasted_iota(jnp.int32, (4 * HEAD, 128), 1)
        adder[...] = jnp.where((lane == column) | (lane + 4 == column), -1.0, 0.0).astype(BF16)
        row = lax.broadcasted_iota(jnp.int32, (LMAX, 128), 0)
        item = lax.broadcasted_iota(jnp.int32, (LMAX, 128), 1)
        length = jnp.where(item % 4 == 0, sc[LENGTHS], sc[LENGTHS + 1])
        length = jnp.where(item % 4 == 2, sc[LENGTHS + 2], length)
        length = jnp.where(item % 4 == 3, sc[LENGTHS + 3], length)
        bound[...] = jnp.where((item < 8) & (row < length), 1.0, 0.0).astype(BF16)

    high_lanes = lax.broadcasted_iota(jnp.int32, (HROWS, 128), 1) < 4
    for head in range(PHEADS):
        weights = exps[head]
        low = (grad_heads[head].astype(F32) * inverse[head].astype(F32)).astype(BF16)
        product = low.astype(F32) * mean[head]
        coarse = product.astype(BF16)
        fine = (product - coarse.astype(F32)).astype(BF16)
        delta = dot(coarse, adder[...], 1, 0) + dot(fine, adder[...], 1, 0)
        coarse = delta.astype(BF16)
        fine = (delta - coarse.astype(F32)).astype(BF16)
        left = jnp.concatenate([low, jnp.where(high_lanes, coarse, fine)], axis=1)
        score = dot(left, jnp.concatenate([v_own[head], v_far[head], bound[...]], axis=1), 1, 1)
        grads[step, head_rows(head)] = (score * weights.astype(F32)).astype(BF16)
        back = (dot(weights, low, 0, 0) * mask[...].astype(F32)).astype(BF16)
        own[head] = back[:, : 2 * HEAD]
        far[head] = back[:, 2 * HEAD :]
    for which in range(count):

        @pl.when(step == which)
        def _():
            for copy in leave(which):
                copy.start()
            if which == count - 1:
                for slot in range(count):
                    for copy in leave(slot):
                        copy.wait()


def run_unmix(sc, planes, v_own, v_far, grad_heads, mean, exps, inverse, carry):
    carry, count = list(carry), len(planes)
    return pl.pallas_call(
        partial(unmix_kernel, count, bool(carry)),
        grid_spec=pltpu.PrefetchScalarGridSpec(
            num_scalar_prefetch=1,
            grid=(count,),
            in_specs=[
                plane_spec(planes, LMAX, 2 * HEAD),
                plane_spec(planes, LMAX, 2 * HEAD),
                plane_spec(planes, HROWS, 4 * HEAD),
                plane_spec(planes, HROWS, 4 * HEAD),
                plane_spec(planes, HROWS, LMAX),
                plane_spec(planes, HROWS, 4 * HEAD),
            ]
            + anywhere(len(carry)),
            out_specs=anywhere(4 * count) + [plane_spec(planes, LMAX, 2 * HEAD)] * 2,
            scratch_shapes=[
                pltpu.VMEM((count, 4 * SUBS * HALF, LMAX), BF16),
                pltpu.VMEM((LMAX, 4 * HEAD), BF16),
                pltpu.VMEM((4 * HEAD, 128), BF16),
                pltpu.VMEM((LMAX, 128), BF16),
                pltpu.SemaphoreType.DMA((count, 4)),
            ],
        ),
        out_shape=[jax.ShapeDtypeStruct((SUBS * HALF, LMAX), BF16)] * (4 * count)
        + [jax.ShapeDtypeStruct((HEADS, LMAX, 2 * HEAD), BF16)] * 2,
        input_output_aliases={7 + i: 4 * count + i for i in range(len(carry))},
        compiler_params=params(VMEM),
        cost_estimate=pl.CostEstimate(
            flops=3 * HEADS * HROWS * LMAX * 4 * HEAD,
            bytes_accessed=HEADS * (2 * HROWS * LMAX + 5 * HROWS * 256 + 4 * LMAX * 256),
            transcendentals=0,
        ),
        name="unmix",
    )(sc, v_own, v_far, grad_heads, mean, exps, inverse, *carry)


def close_kernel(sc, tok, res_own, res_got, out_own, out_got, own, far, gain, w_own, w_far, *refs):
    (output, tok_grad, d_value, d_gain, total, weight) = refs
    step = pl.program_id(0)
    whole_weight(sc, step, w_own, w_far, weight)
    core = sc[CORE]
    output[:, :, core] = out_own[...].astype(F32)
    output[:, :, 1 - core] = out_got[...].astype(F32)
    tok_grad[:, :, core] = res_own[...].astype(F32)
    tok_grad[:, :, 1 - core] = res_got[...].astype(F32)
    runs = tok.shape[1]
    rows = runs * 128
    for item in range(2):
        lanes = slice(item * HEAD, (item + 1) * HEAD)
        pieces = [
            add_low(own[head, :, lanes], far[head, :, lanes]) for head in range(HEADS)
        ]
        back = jnp.concatenate(pieces, axis=1)
        x = tok[item].reshape(rows, WIDTH).astype(F32)
        scale = lax.rsqrt(jnp.mean(x * x, axis=-1, keepdims=True) + EPSILON)
        unit = x * scale
        normed = (unit * gain[...]).astype(BF16)
        normed_grad = dot(back, weight[...], 1, 1)
        gained = normed_grad * gain[...]
        update = scale * (gained - unit * jnp.mean(gained * unit, axis=-1, keepdims=True))
        tok_grad[item] += update.reshape(runs, 2, HALF, WIDTH)
        gain_sum = jnp.sum(normed_grad * unit, axis=0, keepdims=True)
        value_sum = dot(normed, back, 0, 0)
        if item == 0:
            gain_total, value_total = gain_sum, value_sum
        else:
            gain_total, value_total = gain_total + gain_sum, value_total + value_sum

    @pl.when(step == 0)
    def _():
        d_gain[...] = gain_total
        total[...] = value_total

    @pl.when(step > 0)
    def _():
        d_gain[...] += gain_total
        total[...] += value_total

    @pl.when(step == pl.num_programs(0) - 1)
    def _():
        low = total[...].astype(BF16)
        d_value[0] = low[:, :SIDE]
        d_value[1] = low[:, SIDE:]


def run_close(sc, tokens, res_own, res_got, out_own, out_got, own, far, gain, w_own, w_far):
    runs = 2
    slab = (2, RUNS, 2, HALF, WIDTH)
    half = (2, RUNS, HALF, WIDTH)
    whole_spec = spec((2, runs, 2, HALF, WIDTH), lambda j, s: (0, j, 0, 0, 0))
    half_spec = spec((2, runs, HALF, WIDTH), lambda j, s: (0, j, 0, 0))
    back_spec = spec((HEADS, runs * 128, 2 * HEAD), lambda j, s: (0, j, 0))
    return pl.pallas_call(
        close_kernel,
        grid_spec=pltpu.PrefetchScalarGridSpec(
            num_scalar_prefetch=1,
            grid=(RUNS // runs,),
            in_specs=[whole_spec]
            + [half_spec] * 4
            + [back_spec, back_spec, held((1, WIDTH)), held((WIDTH, SIDE)), held((WIDTH, SIDE))],
            out_specs=[whole_spec, whole_spec, held((2, WIDTH, SIDE)), held((1, WIDTH))],
            scratch_shapes=[pltpu.VMEM((WIDTH, WIDTH), F32), pltpu.VMEM((WIDTH, WIDTH), BF16)],
        ),
        out_shape=[
            jax.ShapeDtypeStruct(slab, F32),
            jax.ShapeDtypeStruct(slab, F32),
            jax.ShapeDtypeStruct((2, WIDTH, SIDE), BF16),
            jax.ShapeDtypeStruct((1, WIDTH), F32),
        ],
        compiler_params=params(LESS),
        cost_estimate=pl.CostEstimate(
            flops=4 * 2 * LMAX * WIDTH * WIDTH, bytes_accessed=38 * LMAX * WIDTH, transcendentals=0
        ),
        name="close",
    )(
        sc,
        tokens.reshape(slab),
        *(x.reshape(half) for x in (res_own, res_got, out_own, out_got)),
        own,
        far,
        gain,
        w_own,
        w_far,
    )


PACK_DOWN, PACK_UP, PACK_OUT, PACK_VALUE, PACK_GAIN, PACK = 0, 192, 384, 432, 480, 496


def pack_kernel(sc, down, up, out, value, gain, down_far, up_far, out_far, value_far, gain_far, packed):
    first = sc[CORE] == 0

    def both(own, far, lanes):
        own, far = own[:, lanes], far[:, lanes]
        return jnp.concatenate([jnp.where(first, own, far), jnp.where(first, far, own)], axis=0)

    def side(own, far):
        return both(own, far, own_lanes(sc))

    packed[PACK_DOWN:PACK_UP] = side(down, down_far)
    for j in range(4):
        lanes = pl.ds(pl.multiple_of((4 * sc[CORE] + j) * SIDE, 128), SIDE)
        packed[PACK_UP + 48 * j : PACK_UP + 48 * (j + 1)] = both(up, up_far, lanes)
    packed[PACK_OUT:PACK_VALUE] = side(out, out_far)
    packed[PACK_VALUE:PACK_GAIN] = side(value, value_far)
    packed[PACK_GAIN:] = both(gain, gain_far, slice(0, SIDE))


def run_pack(sc, own, far):
    return pl.pallas_call(
        pack_kernel,
        grid_spec=pltpu.PrefetchScalarGridSpec(
            num_scalar_prefetch=1,
            grid=(1,),
            in_specs=[held(x.shape) for x in (*own, *far)],
            out_specs=held((PACK, SIDE)),
        ),
        out_shape=jax.ShapeDtypeStruct((PACK, SIDE), BF16),
        compiler_params=params(VMEM),
        cost_estimate=pl.CostEstimate(flops=0, bytes_accessed=6 * PACK * SIDE, transcendentals=0),
        name="pack",
    )(sc, *own, *far)


def chip_of(sc, k, rel):
    return plane_of(k, sc) * 4 + (sc[PLACE] ^ rel)


def place_kernel(moves, sc, *refs):
    pieces, targets, sems = refs[:16], refs[16:-1], refs[-1]
    copies = []
    for index, piece in enumerate(pieces):
        chip = chip_of(sc, index // 4, index % 4)
        for which, (start, count, lane, target, step, offset, column) in enumerate(moves):
            rows = pl.ds(pl.multiple_of(chip * step + offset, 16), count)
            copies.append(
                pltpu.make_async_copy(
                    piece.at[pl.ds(start, count), pl.ds(lane, SIDE)],
                    targets[target].at[rows, pl.ds(column, SIDE)],
                    sems.at[index, which],
                )
            )
    for copy in copies:
        copy.start()
    for copy in copies:
        copy.wait()


def run_place(sc, pieces, moves, shapes):
    return pl.pallas_call(
        partial(place_kernel, moves),
        grid_spec=pltpu.PrefetchScalarGridSpec(
            num_scalar_prefetch=1,
            grid=(1,),
            in_specs=anywhere(16),
            out_specs=[held(shape) for shape in shapes],
            scratch_shapes=[pltpu.SemaphoreType.DMA((16, len(moves)))],
        ),
        out_shape=[jax.ShapeDtypeStruct(shape, BF16) for shape in shapes],
        compiler_params=params(VMEM),
        cost_estimate=pl.CostEstimate(
            flops=0, bytes_accessed=4 * sum(a * b for a, b in shapes), transcendentals=0
        ),
        name="place",
    )(sc, *pieces)


def place_weights(sc, pieces):
    moves = (
        (PACK_DOWN, 192, 0, 0, 192, 0, 0),
        *((PACK_UP + 48 * j, 48, 0, 1, 48, 0, j * SIDE) for j in range(4)),
        (PACK_OUT, 48, 0, 2, 48, 0, 0),
        (PACK_VALUE, 48, 0, 3, 48, 0, 0),
        (PACK_GAIN, 16, 0, 4, 16, 0, 0),
    )
    shapes = [(FF, SIDE), (WIDTH, FF // 2), (WIDTH, SIDE), (WIDTH, SIDE), (256, SIDE)]
    return run_place(sc, pieces, moves, shapes)


def collect_kernel(sc, *refs):
    outs = refs[24:]
    for k in range(PLANES):

        @pl.when(pl.program_id(0) == k)
        def _():
            for rel in range(4):
                down, down_got, up, up_got, out, out_got = refs[6 * rel : 6 * rel + 6]
                packed = outs[4 * k + rel]
                packed[PACK_DOWN:PACK_UP] = add_low(down[...], down_got[...])
                for j in range(4):
                    lanes = slice(j * SIDE, (j + 1) * SIDE)
                    packed[PACK_UP + 48 * j : PACK_UP + 48 * (j + 1)] = add_low(up[:, lanes], up_got[:, lanes])
                packed[PACK_OUT:PACK_VALUE] = add_low(out[...], out_got[...])


def run_collect(sc, *sides):
    def rows(x, rel):
        return spec((x.shape[0] // 16, x.shape[1]), lambda k, s: (chip_of(s, k, rel), 0))

    return pl.pallas_call(
        collect_kernel,
        grid_spec=pltpu.PrefetchScalarGridSpec(
            num_scalar_prefetch=1,
            grid=(PLANES,),
            in_specs=[rows(x, rel) for rel in range(4) for x in sides],
            out_specs=[held((PACK_VALUE, SIDE))] * 16,
        ),
        out_shape=[jax.ShapeDtypeStruct((PACK_VALUE, SIDE), BF16)] * 16,
        compiler_params=params(LESS),
        cost_estimate=pl.CostEstimate(flops=0, bytes_accessed=3 * 16 * PACK_VALUE * SIDE * 2, transcendentals=0),
        name="collect",
    )(sc, *(x for _ in range(4) for x in sides))


def add_kernel(groups, *refs):
    for group, total in zip(groups, refs[-len(groups) :]):
        value = refs[group[0]][...].astype(F32)
        for index in group[1:]:
            value = value + refs[index][...].astype(F32)
        total[...] = value.astype(total.dtype)


def run_add(groups, values, dtype):
    shape = values[0].shape
    here = pl.BlockSpec(memory_space=pltpu.VMEM)
    return pl.pallas_call(
        partial(add_kernel, groups),
        in_specs=[here] * len(values),
        out_specs=[here] * len(groups),
        out_shape=[jax.ShapeDtypeStruct(shape, dtype)] * len(groups),
        compiler_params=params(LESS),
        cost_estimate=pl.CostEstimate(
            flops=0, bytes_accessed=2 * shape[0] * shape[1] * (len(values) + len(groups)), transcendentals=0
        ),
        name="add",
    )(*values)


DEVICES = 32
TO_CORE, TO_X, TO_Y = 1, 2, 4


def swap(x, bit):
    return lax.ppermute(x, BOTH, [(d, d ^ bit) for d in range(DEVICES)])


def ring(x, way=1):
    return lax.ppermute(x, BOTH, [(d, (d + 8 * way) % DEVICES) for d in range(DEVICES)])


def pick(x, index, axis=0):
    return lax.dynamic_index_in_dim(x, index, axis, keepdims=False)


def ordered(flag, one, two, axis=0, joined=jnp.stack):
    return jnp.where(flag == 0, joined([one, two], axis), joined([two, one], axis))


def add_low(one, two):
    return (one.astype(F32) + two.astype(F32)).astype(BF16)


STEPS = (
    ((0, 0, 1), (0, 1, 0), (1, 0, 0)),
    ((1, 0, 1), (0, 1, 1), (2, 0, 0)),
    ((2, 0, 1), (1, 1, 0), (3, 0, 0)),
    ((1, 1, 1), (2, 1, 1), (2, 1, 0)),
    ((3, 0, 1), (3, 1, 0), (3, 1, 1)),
)


def gather_step(have, step):
    by_x, by_y, by_z = STEPS[step]
    return {
        **have,
        by_z: ring(have[by_z[0] - 1, by_z[1], by_z[2]]),
        by_x: swap(have[by_x[0], by_x[1], 0], TO_X),
        by_y: swap(have[by_y[0], 0, by_y[2]], TO_Y),
    }


def in_order(have):
    return [have[k, y, x] for k in range(4) for y in range(2) for x in range(2)]


def by_place(shares, planes=range(PLANES)):
    return {(k, i // 2, i % 2): shares[4 * at + i] for at, k in enumerate(planes) for i in range(4)}


def scatter_send(have, step):
    by_x, by_y, by_z = STEPS[len(STEPS) - 1 - step]
    got = (ring(have[by_z], -1), swap(have[by_x], TO_X), swap(have[by_y], TO_Y))
    return {at: value for at, value in have.items() if at not in (by_x, by_y, by_z)}, got


def scatter_add(have, got, step):
    by_x, by_y, by_z = STEPS[len(STEPS) - 1 - step]
    targets = ((by_z[0] - 1, by_z[1], by_z[2]), (by_x[0], by_x[1], 0), (by_y[0], 0, by_y[2]))
    sums = list(dict.fromkeys(targets))
    groups = [(len(got) + i, *(j for j in range(len(got)) if targets[j] == at)) for i, at in enumerate(sums)]
    values = [*got, *(have[at] for at in sums)]
    dtype = F32 if step == len(STEPS) - 1 else BF16
    if values[0].shape[1] == LMAX:
        totals = run_add(groups, values, dtype)
    else:
        totals = [sum(values[i].astype(F32) for i in group).astype(dtype) for group in groups]
    return {**have, **dict(zip(sums, totals))}


together = lax.optimization_barrier


def chip_shards(tokens, lengths, rand_mix, w_value, w_out, w_up, w_down, gain_mix, gain_ffn, grad_out):
    wide = lax.axis_index("wide")
    core = lax.axis_index("narrow")
    z, y, x = wide // 4, (wide // 2) % 2, wide % 2
    other = lambda value: swap(value, TO_CORE)
    side = partial(ordered, core, joined=jnp.concatenate)
    slab = (2, RUNS, 2, HALF, WIDTH)
    tokens, grad_out = tokens.reshape(slab), grad_out.reshape(slab)

    gains = jnp.pad(jnp.concatenate([gain_mix, gain_ffn])[None], ((0, 7), (0, SIDE - 48)))
    own = (w_down, w_up, w_out, w_value, gains)
    far = tuple(other(value) for value in own)
    near_sc = jnp.concatenate([jnp.stack([core, z, wide % 4]).astype(jnp.int32), lengths, lengths])
    weights = {(0, 0, 0): run_pack(near_sc, own, far)}

    rand = rand_mix.reshape(3, 2, HALF, LMAX)
    blocks = side(pick(rand, core, 1), other(pick(rand, 1 - core, 1)), 0)
    weights, rands, late_tokens, late_grad = together(
        (gather_step(weights, 0), {(0, 0, 0): blocks.reshape(SUBS * HALF, LMAX)}, tokens, grad_out)
    )
    weights, tokens_far = together((gather_step(weights, 1), other(pick(late_tokens, 1 - core, 2))))
    weights, grad_far = together((gather_step(weights, 2), other(pick(late_grad, 1 - core, 2))))
    weights, far_lengths = together((gather_step(weights, 3), other(lengths)))
    sc = jnp.concatenate([near_sc[:5], far_lengths])
    weights, rands = together((gather_step(weights, 4), rands))

    rands = gather_step(rands, 0)
    down, up, out, value, gain_rows = place_weights(sc, in_order(weights))
    rands, value, value_far, gain_rows, out, down, up = together(
        (rands, value, other(value), gain_rows, out, down, up)
    )
    gain_rows = gain_rows.reshape(16, 2, 8, SIDE)[:, :, 0]
    gain_one = gain_rows[..., :24].reshape(1, WIDTH).astype(F32)
    gain_two = gain_rows[..., 24:48].reshape(1, WIDTH).astype(F32)
    rands = gather_step(rands, 1)
    v_own = run_values(sc, tokens.reshape(2, LMAX, WIDTH), gain_one, value, value_far)
    rands, v_own, out, down, up = together((rands, v_own, (out, other(out)), down, up))
    rands, v_own, v_far, grad_far, down, up = together(
        (gather_step(rands, 2), v_own, other(v_own), grad_far, down, up)
    )
    rands = gather_step(rands, 3)
    masked = run_masked(sc, grad_out, grad_far)
    rands, v_far, masked, down, up = together((rands, v_far, masked, down, up))
    near = [rands[k, y_at, x_at] for k in range(3) for y_at in range(2) for x_at in range(2)]
    rands = gather_step(rands, 4)
    mixing = run_mix(sc, (0, 1, 2), near, v_own, v_far, ())
    rands, down, up, mixing = together((rands, down, up, mixing))
    heads, mean, exps, inverse = run_mix(sc, (3,), in_order(rands)[12:], v_own, v_far, mixing)
    down, up = (down, other(down)), (up, other(up))

    mixed, resid, normed = run_pre(sc, tokens, tokens_far, heads, out, gain_two)
    active, up_grad = run_units(sc, normed, masked, up, down)
    res_own, res_far, grad_heads, d_gain_two = run_post(sc, resid, up_grad, masked, up, out, gain_two)

    backward = lambda planes, carry: run_unmix(sc, planes, v_own, v_far, grad_heads, mean, exps, inverse, carry)
    *far, back_own, back_far = backward((3,), ())
    far, back_own, back_far, res_got = together((far, back_own, back_far, other(res_far)))
    have, got = scatter_send(by_place(far, (3,)), 0)
    *near, back_own, back_far = backward((2, 1, 0), (back_own, back_far))
    have, got, near, back_own, back_far = together((have, got, near, back_own, back_far))
    have = scatter_add({**have, **by_place(near, (2, 1, 0))}, got, 0)

    have, got = scatter_send(have, 1)
    up_own, up_far = run_up_grad(sc, normed, up_grad)
    have, got, up_own, up_far, back_got = together((have, got, up_own, up_far, other(back_far)))
    have = scatter_add(have, got, 1)

    have, got = scatter_send(have, 2)
    down_own, down_far = run_down_grad(sc, active, masked)
    have, got, down_own, down_far, up_got = together((have, got, down_own, down_far, other(up_far)))
    have = scatter_add(have, got, 2)

    have, got = scatter_send(have, 3)
    d_out_own, d_out_far = run_out_grad(sc, mixed, res_own, res_far)
    packed = run_collect(sc, down_own, other(down_far), up_own, up_got, d_out_own, other(d_out_far))
    have, got, packed = together((have, got, packed))
    have = scatter_add(have, got, 3)

    have, got = scatter_send(have, 4)
    sums, sums_got = scatter_send(by_place(packed), 0)
    out_own, out_far = run_out(sc, active, resid, down)
    have, got, sums, sums_got, out_own, out_far = together((have, got, sums, sums_got, out_own, out_far))
    rand_sum = scatter_add(have, got, 4)[0, 0, 0].reshape(2, 3, HALF, LMAX)

    sums, got = scatter_send(scatter_add(sums, sums_got, 0), 1)
    output, tokens_grad, d_value, d_gain_one = run_close(
        sc, tokens, res_own, res_got, out_own, other(out_far), back_own, back_got, gain_one, value, value_far
    )
    sums, got, output, tokens_grad, d_value, d_gain_one = together(
        (sums, got, output, tokens_grad, d_value, d_gain_one)
    )
    sums = scatter_add(sums, got, 1)

    sums, got = scatter_send(sums, 2)
    gain_pair = jnp.concatenate([d_gain_one, d_gain_two]).reshape(2, 16, 1, 48).astype(BF16)
    gain_pair = jnp.pad(gain_pair, ((0, 0), (0, 0), (0, 15), (0, SIDE - 48)))
    small = jnp.concatenate([d_value.reshape(2, 16, 48, SIDE), gain_pair], 2)
    small = add_low(pick(small, core), other(pick(small, 1 - core))).reshape(4, 2, 2, 64, SIDE)
    small = add_low(pick(small, x, 2), swap(pick(small, 1 - x, 2), TO_X))
    sums, got, small = together((sums, got, small))
    sums = scatter_add(sums, got, 2)

    sums, got = scatter_send(sums, 3)
    small = add_low(pick(small, y, 1), swap(pick(small, 1 - y, 1), TO_Y))
    blocks, blocks_far = pick(rand_sum, core), other(pick(rand_sum, 1 - core))
    sums, got, small, blocks, blocks_far = together((sums, got, small, blocks, blocks_far))
    sums = scatter_add(sums, got, 3)

    sums, got = scatter_send(sums, 4)
    small_sum = pick(small, z).astype(F32)
    for k in range(1, PLANES):
        small_sum = small_sum + ring(pick(small, lax.rem(z + PLANES - k, PLANES)), -k).astype(F32)
    sums, got, small_sum = together((sums, got, small_sum))
    big_sum = scatter_add(sums, got, 4)[0, 0, 0]
    big_far, small_far = other(big_sum), other(small_sum)

    rows_of = lambda value, rows: pick(value.reshape(-1, 2, rows, SIDE), core, 1)
    mine = lambda own, far, rows: side(rows_of(own, rows)[0], rows_of(far, rows)[0], 1)
    down_shard = mine(big_sum[PACK_DOWN:PACK_UP], big_far[PACK_DOWN:PACK_UP], 96)
    up_side = lambda value: rows_of(value[PACK_UP:PACK_OUT], 24).transpose(1, 0, 2).reshape(24, 4 * SIDE)
    up_shard = side(up_side(big_sum), up_side(big_far), 1)
    outproj_shard = mine(big_sum[PACK_OUT:PACK_VALUE], big_far[PACK_OUT:PACK_VALUE], 24)
    value_shard = mine(small_sum[:48], small_far[:48], 24)
    gains_pair = ordered(core, small_sum[48, :48], small_far[48, :48])
    gain_pair = pick(gains_pair.reshape(2, 2, 24), core, 1)

    rand_shard = ordered(core, blocks, blocks_far, 1)

    return (
        output.reshape(2, LMAX, WIDTH),
        tokens_grad.reshape(2, LMAX, WIDTH),
        rand_shard.reshape(3 * 128, LMAX),
        value_shard,
        outproj_shard,
        up_shard,
        down_shard,
        gain_pair[0],
        gain_pair[1],
    )


def rms_norm(values, gain):
    scale = lax.rsqrt(jnp.mean(values * values, axis=-1, keepdims=True) + EPSILON)
    return values * scale * gain


def split_heads(block):
    return block.reshape(LMAX, HEADS, HEAD).transpose(1, 0, 2)


def merge_heads(block):
    return block.transpose(1, 0, 2).reshape(LMAX, HEADS * HEAD)


def masked_scores(key_mask, rand_head):
    return jnp.where(key_mask[None, :] > 0, rand_head.astype(jnp.float32), -1e30)


def head_forward(key_mask, paired):
    rand_head, value_head = paired
    scores = masked_scores(key_mask, rand_head)
    row_peak = jnp.max(scores, axis=-1, keepdims=True)
    exponent = jnp.exp(scores - row_peak)
    denom_sum = jnp.sum(exponent, axis=-1, keepdims=True)
    attention = exponent / denom_sum * key_mask[:, None]
    mixed = jnp.dot(attention.astype(jnp.bfloat16), value_head, preferred_element_type=jnp.float32)
    return (mixed.astype(jnp.bfloat16), row_peak + jnp.log(denom_sum))


def head_backward(key_mask, paired):
    rand_head, value_head, mix_grad, log_total = paired
    scores = masked_scores(key_mask, rand_head)
    attention = jnp.exp(scores - log_total) * key_mask[:, None]
    prob_grad = jnp.einsum("id,jd->ij", mix_grad, value_head, preferred_element_type=jnp.float32)
    value_grad = jnp.einsum(
        "ij,id->jd", attention.astype(jnp.bfloat16), mix_grad, preferred_element_type=jnp.float32
    )
    score_grad = attention * (prob_grad - jnp.sum(prob_grad * attention, axis=-1, keepdims=True))
    return (score_grad, value_grad)


def shards(tokens, lengths, rand_mix, w_value, w_out, w_up, w_down, gain_mix, gain_ffn, grad_out):
    item_count = tokens.shape[0]
    width = tokens.shape[2]
    row_count = item_count * LMAX
    tokens_flat = tokens.reshape(row_count, width).astype(jnp.float32)
    positions = jnp.arange(LMAX, dtype=jnp.int32)
    valid_table = (positions[None, :] < lengths[:, None]).astype(jnp.float32)
    row_valid = valid_table.reshape(row_count, 1)
    forward_set = (
        lax.all_gather(rand_mix, ("wide", "narrow"), axis=0, tiled=True),
        lax.all_gather(w_value, ("wide", "narrow"), axis=0, tiled=True),
        lax.all_gather(w_out, ("wide", "narrow"), axis=0, tiled=True),
        lax.all_gather(w_up, ("wide", "narrow"), axis=0, tiled=True),
        lax.all_gather(w_down, ("wide", "narrow"), axis=0, tiled=True),
        lax.all_gather(gain_mix, ("wide", "narrow"), axis=0, tiled=True),
        lax.all_gather(gain_ffn, ("wide", "narrow"), axis=0, tiled=True),
    )
    rand_all, value_all, out_all, up_all, down_all, gain_first, gain_second = forward_set
    normed = rms_norm(tokens_flat, gain_first.astype(jnp.float32)).astype(jnp.bfloat16)
    values = jnp.dot(normed, value_all, preferred_element_type=jnp.float32).astype(jnp.bfloat16)
    rand_heads = rand_all.reshape(HEADS, LMAX, LMAX)
    mixed_parts = []
    totals_kept = []
    for item_index in range(item_count):
        item_values = split_heads(values[item_index * LMAX : (item_index + 1) * LMAX])
        mixed_heads, log_total = lax.map(
            partial(head_forward, valid_table[item_index]), (rand_heads, item_values)
        )
        mixed_parts.append(merge_heads(mixed_heads))
        totals_kept.append(log_total)
    mixed = jnp.concatenate(mixed_parts, axis=0)
    residual = tokens_flat + jnp.dot(mixed, out_all, preferred_element_type=jnp.float32)
    normed_two = rms_norm(residual, gain_second.astype(jnp.float32)).astype(jnp.bfloat16)
    up_proj = jnp.dot(normed_two, up_all, preferred_element_type=jnp.float32)
    active = jax.nn.gelu(up_proj).astype(jnp.bfloat16)
    branch = jnp.dot(active, down_all, preferred_element_type=jnp.float32)
    output = row_valid * (residual + branch)
    back_set = (
        lax.all_gather(rand_mix, ("wide", "narrow"), axis=0, tiled=True),
        lax.all_gather(w_value, ("wide", "narrow"), axis=0, tiled=True),
        lax.all_gather(w_out, ("wide", "narrow"), axis=0, tiled=True),
        lax.all_gather(w_up, ("wide", "narrow"), axis=0, tiled=True),
        lax.all_gather(w_down, ("wide", "narrow"), axis=0, tiled=True),
        lax.all_gather(gain_mix, ("wide", "narrow"), axis=0, tiled=True),
        lax.all_gather(gain_ffn, ("wide", "narrow"), axis=0, tiled=True),
    )
    rand_back, value_back, out_back, up_back, down_back, gain_back_one, gain_back_two = back_set
    cotangent = grad_out.reshape(row_count, width).astype(jnp.float32)
    masked = row_valid * cotangent
    branch_grad = masked.astype(jnp.bfloat16)
    grad_down = jnp.einsum("rk,rd->kd", active, branch_grad, preferred_element_type=jnp.float32)
    active_grad = jnp.einsum(
        "rd,kd->rk", branch_grad, down_back, preferred_element_type=jnp.float32
    )
    gelu_value, gelu_pull = jax.vjp(jax.nn.gelu, up_proj)
    up_grad = gelu_pull(active_grad)[0].astype(jnp.bfloat16)
    grad_up = jnp.einsum("rd,rk->dk", normed_two, up_grad, preferred_element_type=jnp.float32)
    normed_two_grad = jnp.einsum("rk,dk->rd", up_grad, up_back, preferred_element_type=jnp.float32)
    norm_value, norm_pull = jax.vjp(rms_norm, residual, gain_back_two.astype(jnp.float32))
    residual_part, gain_two_grad = norm_pull(normed_two_grad)
    residual_grad = masked + residual_part
    attn_grad = residual_grad.astype(jnp.bfloat16)
    grad_outproj = jnp.einsum("rd,re->de", mixed, attn_grad, preferred_element_type=jnp.float32)
    mixed_grad = jnp.einsum(
        "re,de->rd", attn_grad, out_back, preferred_element_type=jnp.float32
    ).astype(jnp.bfloat16)
    rand_heads_back = rand_back.reshape(HEADS, LMAX, LMAX)
    rand_grad = jnp.zeros((HEADS, LMAX, LMAX), jnp.float32)
    value_parts = []
    for item_index in range(item_count):
        lower_row = item_index * LMAX
        upper_row = lower_row + LMAX
        item_values = split_heads(values[lower_row:upper_row])
        item_mix_grad = split_heads(mixed_grad[lower_row:upper_row])
        score_grad, value_grad = lax.map(
            partial(head_backward, valid_table[item_index]),
            (rand_heads_back, item_values, item_mix_grad, totals_kept[item_index]),
        )
        rand_grad = rand_grad + score_grad
        value_parts.append(merge_heads(value_grad))
    values_grad = jnp.concatenate(value_parts, axis=0).astype(jnp.bfloat16)
    grad_value = jnp.einsum("rd,re->de", normed, values_grad, preferred_element_type=jnp.float32)
    normed_grad = jnp.einsum(
        "re,de->rd", values_grad, value_back, preferred_element_type=jnp.float32
    )
    norm_first, first_pull = jax.vjp(rms_norm, tokens_flat, gain_back_one.astype(jnp.float32))
    token_part, gain_one_grad = first_pull(normed_grad)
    tokens_grad = residual_grad + token_part
    rand_flat = rand_grad.reshape(HEADS * LMAX, LMAX)
    all_shards = (
        lax.psum_scatter(rand_flat, ("wide", "narrow"), scatter_dimension=0, tiled=True),
        lax.psum_scatter(grad_value, ("wide", "narrow"), scatter_dimension=0, tiled=True),
        lax.psum_scatter(grad_outproj, ("wide", "narrow"), scatter_dimension=0, tiled=True),
        lax.psum_scatter(grad_up, ("wide", "narrow"), scatter_dimension=0, tiled=True),
        lax.psum_scatter(grad_down, ("wide", "narrow"), scatter_dimension=0, tiled=True),
        lax.psum_scatter(gain_one_grad, ("wide", "narrow"), scatter_dimension=0, tiled=True),
        lax.psum_scatter(gain_two_grad, ("wide", "narrow"), scatter_dimension=0, tiled=True),
    )
    rand_shard, value_shard, outproj_shard, up_shard, down_shard, gain_one_shard, gain_two_shard = (
        all_shards
    )
    return (
        output.reshape(item_count, LMAX, width),
        tokens_grad.reshape(item_count, LMAX, width),
        rand_shard,
        value_shard,
        outproj_shard,
        up_shard,
        down_shard,
        gain_one_shard,
        gain_two_shard,
    )


def solution(mesh):
    in_specs = (
        P(("wide", "narrow"), None, None),
        P(("wide", "narrow")),
        P(("wide", "narrow"), None),
        P(("wide", "narrow"), None),
        P(("wide", "narrow"), None),
        P(("wide", "narrow"), None),
        P(("wide", "narrow"), None),
        P(("wide", "narrow")),
        P(("wide", "narrow")),
        P(("wide", "narrow"), None, None),
    )
    out_specs = (
        P(("wide", "narrow"), None, None),
        P(("wide", "narrow"), None, None),
        P(("wide", "narrow"), None),
        P(("wide", "narrow"), None),
        P(("wide", "narrow"), None),
        P(("wide", "narrow"), None),
        P(("wide", "narrow"), None),
        P(("wide", "narrow")),
        P(("wide", "narrow")),
    )
    fits = dict(mesh.shape) == {"wide": 16, "narrow": 2}
    return jax.shard_map(chip_shards if fits else shards, mesh=mesh, in_specs=in_specs, out_specs=out_specs, check_vma=False)
```

```python
from functools import partial

import jax
import jax.numpy as jnp
from jax import lax
from jax.experimental import pallas as pl
from jax.experimental.pallas import tpu as pltpu
from jax.sharding import PartitionSpec as P

HEADS = 12
HEAD = 64
LMAX = 1024
WIDTH = 768
FF = 3072
EPSILON = 1e-05

BOTH = ("wide", "narrow")
BF16 = jnp.bfloat16
F32 = jnp.float32
VMEM = 61 << 20
LESS = 34 << 20

SUBS = 6
RUNS = 8
HALF = 64
HROWS = RUNS * HALF
PLANES = 4
PHEADS = HEADS // PLANES
ROWS = 2 * LMAX
FSTEP = 768
FSIDE = FF // 2 // FSTEP
TILE = 512
SIDE = WIDTH // 2
SPAN = 2 * HALF


def dot(a, b, ca, cb):
    return lax.dot_general(a, b, (((ca,), (cb,)), ((), ())), preferred_element_type=F32)


CORE, PLANE, PLACE, LENGTHS = 0, 1, 2, 3


def spec(shape, index):
    return pl.BlockSpec(shape, index)


def held(shape):
    zeros = (0,) * len(shape)
    return pl.BlockSpec(shape, lambda *_: zeros, pipeline_mode=pl.Buffered(1))


def params(limit):
    return pltpu.CompilerParams(vmem_limit_bytes=limit)


def whole_weight(sc, step, own, far, weight):
    @pl.when(step == 0)
    def _():
        weight[:, pl.ds(pl.multiple_of(sc[CORE] * SIDE, 128), SIDE)] = own[...]
        weight[:, pl.ds(pl.multiple_of((1 - sc[CORE]) * SIDE, 128), SIDE)] = far[...]


def values_kernel(sc, tok, gain, w_own, w_far, out, weight):
    step = pl.program_id(0)
    whole_weight(sc, step, w_own, w_far, weight)
    rows = tok.shape[1]
    position = step * rows + lax.broadcasted_iota(jnp.int32, (rows, 1), 0)
    for item in range(2):
        x = tok[item].astype(F32)
        scale = lax.rsqrt(jnp.mean(x * x, axis=-1, keepdims=True) + EPSILON)
        normed = (x * scale * gain[...]).astype(BF16)
        found = dot(normed, weight[...], 1, 0)
        found = jnp.where(position < sc[LENGTHS + item], found, 0.0).astype(BF16)
        for head in range(HEADS):
            out[head, :, item * HEAD : (item + 1) * HEAD] = found[:, head * HEAD : (head + 1) * HEAD]


def run_values(sc, tokens, gain, w_own, w_far):
    rows = 256
    return pl.pallas_call(
        values_kernel,
        grid_spec=pltpu.PrefetchScalarGridSpec(
            num_scalar_prefetch=1,
            grid=(LMAX // rows,),
            in_specs=[
                spec((2, rows, WIDTH), lambda j, s: (0, j, 0)),
                held((1, WIDTH)),
                held((WIDTH, SIDE)),
                held((WIDTH, SIDE)),
            ],
            out_specs=spec((HEADS, rows, 2 * HEAD), lambda j, s: (0, j, 0)),
            scratch_shapes=[pltpu.VMEM((WIDTH, WIDTH), BF16)],
        ),
        out_shape=jax.ShapeDtypeStruct((HEADS, LMAX, 2 * HEAD), BF16),
        compiler_params=params(VMEM),
        cost_estimate=pl.CostEstimate(
            flops=2 * 2 * LMAX * WIDTH * WIDTH, bytes_accessed=8 * LMAX * WIDTH, transcendentals=0
        ),
        name="values",
    )(sc, tokens, gain, w_own, w_far)


def lane_lengths(sc, shape):
    slot = lax.broadcasted_iota(jnp.int32, shape, 1) // HEAD
    length = jnp.where(slot == 0, sc[LENGTHS], sc[LENGTHS + 1])
    return jnp.where(slot >= 2, jnp.where(slot == 2, sc[LENGTHS + 2], sc[LENGTHS + 3]), length)


def plane_of(k, sc):
    return lax.rem(sc[PLANE] + PLANES - k, PLANES)


def plane_spec(planes, rows, lanes):
    def index(step, sc):
        return (plane_of(planes[0] + step * (planes[-1] - planes[0]) // max(len(planes) - 1, 1), sc), 0, 0)

    return spec((PHEADS, rows, lanes), index)


def anywhere(count):
    return [pl.BlockSpec(memory_space=pl.ANY)] * count


def plane_fetch(place, shards, raw, sems, slot):
    return [
        pltpu.make_async_copy(
            shards[4 * slot + rel],
            raw.at[slot, pl.ds(pl.multiple_of((place ^ rel) * SUBS * HALF, SUBS * HALF), SUBS * HALF)],
            sems.at[slot, rel],
        )
        for rel in range(4)
    ]


def take_plane(place, shards, raw, sems):
    step = pl.program_id(0)
    count = len(shards) // 4

    @pl.when(step == 0)
    def _():
        for slot in range(count):
            for copy in plane_fetch(place, shards, raw, sems, slot):
                copy.start()

    for slot in range(count):

        @pl.when(step == slot)
        def _():
            for copy in plane_fetch(place, shards, raw, sems, slot):
                copy.wait()

    return step


def head_rows(head):
    return slice(head * HROWS, (head + 1) * HROWS)


def fill_mask(sc, mask):
    @pl.when(pl.program_id(0) == 0)
    def _():
        shape = (LMAX, 4 * HEAD)
        column = lax.broadcasted_iota(jnp.int32, shape, 0)
        mask[...] = (column < lane_lengths(sc, shape)).astype(F32).astype(BF16)


def mix_kernel(count, carried, sc, *refs):
    shards, (v_own, v_far, *rest) = refs[: 4 * count], refs[4 * count :]
    mixed, mean, exps, inverse, raw, mask, sems = rest[4:] if carried else rest
    fill_mask(sc, mask)
    slot = take_plane(sc[PLACE], shards, raw, sems)
    shape = (HROWS, 4 * HEAD)
    line = lax.broadcasted_iota(jnp.int32, shape, 0)
    position = 128 * (line // HALF) + HALF * sc[CORE] + line % HALF
    valid = position < lane_lengths(sc, shape)
    for head in range(PHEADS):
        weights = jnp.exp(raw[slot, head_rows(head)].astype(F32)).astype(BF16)
        exps[head] = weights
        both = dot(weights, jnp.concatenate([v_own[head], v_far[head], mask[...]], axis=1), 1, 0)
        flip = jnp.where(valid, 1.0 / both[:, 4 * HEAD :], 0.0)
        found = both[:, : 4 * HEAD] * flip
        inverse[head] = flip.astype(BF16)
        mean[head] = found
        mixed[head] = found.astype(BF16)


def run_mix(sc, planes, shards, v_own, v_far, carry):
    carry, count = list(carry), len(planes)
    shape = (HEADS, HROWS, 4 * HEAD)
    return pl.pallas_call(
        partial(mix_kernel, count, bool(carry)),
        grid_spec=pltpu.PrefetchScalarGridSpec(
            num_scalar_prefetch=1,
            grid=(count,),
            in_specs=anywhere(4 * count) + [plane_spec(planes, LMAX, 2 * HEAD)] * 2 + anywhere(len(carry)),
            out_specs=[
                plane_spec(planes, HROWS, 4 * HEAD),
                plane_spec(planes, HROWS, 4 * HEAD),
                plane_spec(planes, HROWS, LMAX),
                plane_spec(planes, HROWS, 4 * HEAD),
            ],
            scratch_shapes=[
                pltpu.VMEM((count, 4 * SUBS * HALF, LMAX), BF16),
                pltpu.VMEM((LMAX, 4 * HEAD), BF16),
                pltpu.SemaphoreType.DMA((count, 4)),
            ],
        ),
        out_shape=[
            jax.ShapeDtypeStruct(shape, BF16),
            jax.ShapeDtypeStruct(shape, F32),
            jax.ShapeDtypeStruct((HEADS, HROWS, LMAX), BF16),
            jax.ShapeDtypeStruct(shape, BF16),
        ],
        input_output_aliases={3 + 4 * count + i: i for i in range(len(carry))},
        compiler_params=params(VMEM),
        cost_estimate=pl.CostEstimate(
            flops=2 * HEADS * HROWS * LMAX * 4 * HEAD,
            bytes_accessed=HEADS * (2 * HROWS * LMAX + 5 * HROWS * 256),
            transcendentals=HEADS * HROWS * LMAX // 2,
        ),
        name="mix",
    )(sc, *shards, v_own, v_far, *carry)


def row_valid(sc, step):
    line = lax.broadcasted_iota(jnp.int32, (4 * SPAN, 1), 0)
    item = line // SPAN
    row = step * SPAN + line % SPAN
    low = jnp.where(item == 0, sc[LENGTHS], sc[LENGTHS + 1])
    high = jnp.where(item == 2, sc[LENGTHS + 2], sc[LENGTHS + 3])
    return 128 * (row // HALF) + HALF * sc[CORE] + row % HALF < jnp.where(item >= 2, high, low)


def four_items(own, far):
    return jnp.concatenate([own[:, :, 0], far[...]], axis=0).reshape(4 * SPAN, WIDTH)


def pre_kernel(sc, tok, tok_far, heads, wo_own, wo_far, gain, mixed, resid, normed, weight):
    step = pl.program_id(0)
    whole_weight(sc, step, wo_own, wo_far, weight)
    for item in range(4):
        lanes = slice(item * HEAD, (item + 1) * HEAD)
        for pair in range(HEADS // 2):
            both = jnp.concatenate([heads[2 * pair, :, lanes], heads[2 * pair + 1, :, lanes]], axis=1)
            mixed[item, :, pair * 128 : (pair + 1) * 128] = both
    res = four_items(tok, tok_far).astype(F32) + dot(mixed[...].reshape(4 * SPAN, WIDTH), weight[...], 1, 0)
    resid[...] = res.astype(BF16).reshape(4, SPAN, WIDTH)
    scale = lax.rsqrt(jnp.mean(res * res, axis=-1, keepdims=True) + EPSILON)
    valid = row_valid(sc, step)
    normed[...] = jnp.where(valid, res * scale * gain[...], 0.0).astype(BF16).reshape(4, SPAN, WIDTH)


def slab_spec(items=4):
    return spec((items, SPAN, WIDTH), lambda r, s: (0, r, 0))


def half_specs():
    return [
        spec((2, SPAN // HALF, 1, HALF, WIDTH), lambda r, s: (0, r, s[CORE], 0, 0)),
        spec((2, SPAN // HALF, HALF, WIDTH), lambda r, s: (0, r, 0, 0)),
    ]


def heads_spec():
    return spec((HEADS, SPAN, 4 * HEAD), lambda r, s: (0, r, 0))


def run_pre(sc, tokens, tokens_far, heads, wo, gain):
    return pl.pallas_call(
        pre_kernel,
        grid_spec=pltpu.PrefetchScalarGridSpec(
            num_scalar_prefetch=1,
            grid=(HROWS // SPAN,),
            in_specs=half_specs()
            + [heads_spec(), held((WIDTH, SIDE)), held((WIDTH, SIDE)), held((1, WIDTH))],
            out_specs=[slab_spec()] * 3,
            scratch_shapes=[pltpu.VMEM((WIDTH, WIDTH), BF16)],
        ),
        out_shape=[
            jax.ShapeDtypeStruct((4, HROWS, WIDTH), BF16),
            jax.ShapeDtypeStruct((4, HROWS, WIDTH), BF16),
            jax.ShapeDtypeStruct((4, HROWS, WIDTH), BF16),
        ],
        compiler_params=params(VMEM),
        cost_estimate=pl.CostEstimate(
            flops=2 * ROWS * WIDTH * WIDTH, bytes_accessed=16 * ROWS * WIDTH, transcendentals=0
        ),
        name="pre",
    )(sc, tokens, tokens_far, heads, *wo, gain)


def masked_kernel(sc, cot, cot_far, masked):
    value = jnp.where(row_valid(sc, pl.program_id(0)), four_items(cot, cot_far).astype(F32), 0.0)
    masked[...] = value.astype(BF16).reshape(4, SPAN, WIDTH)


def run_masked(sc, cotangent, cotangent_far):
    return pl.pallas_call(
        masked_kernel,
        grid_spec=pltpu.PrefetchScalarGridSpec(
            num_scalar_prefetch=1, grid=(HROWS // SPAN,), in_specs=half_specs(), out_specs=slab_spec()
        ),
        out_shape=jax.ShapeDtypeStruct((4, HROWS, WIDTH), BF16),
        compiler_params=params(VMEM),
        cost_estimate=pl.CostEstimate(flops=0, bytes_accessed=4 * ROWS * WIDTH, transcendentals=0),
        name="masked",
    )(sc, cotangent, cotangent_far)


def own_lanes(sc):
    return pl.ds(pl.multiple_of(sc[CORE] * SIDE, 128), SIDE)


def far_lanes(sc):
    return pl.ds(pl.multiple_of((1 - sc[CORE]) * SIDE, 128), SIDE)


def unit_rows(f, sc):
    return (lax.rem(FSIDE * sc[CORE] + f, 2 * FSIDE), 0)


def unit_columns(f, sc):
    return (0, lax.rem(FSIDE * sc[CORE] + f, 2 * FSIDE))


def early(f, sc):
    return (0, lax.min(f, FSIDE - 1))


def late(f, sc):
    return (0, lax.max(f - FSIDE, 0))


def units_kernel(sc, normed, cot, up_own, up_far, dn_own, dn_far, active, up_grad, w_up, w_down):
    step = pl.program_id(0)
    w_down[:, own_lanes(sc)] = dn_own[...]
    w_down[:, far_lanes(sc)] = dn_far[...]

    @pl.when(step < FSIDE)
    def _():
        w_up[...] = up_own[...]

    @pl.when(step >= FSIDE)
    def _():
        w_up[...] = up_far[...]

    for row in range(0, ROWS, 256):
        rows = slice(row, row + 256)
        for column in range(0, FSTEP, 256):
            columns = slice(column, column + 256)
            up = dot(normed[rows], w_up[:, columns], 1, 0)
            square = up * up
            bend = jnp.tanh(up * (0.7978845608028654 + (0.044715 * 0.7978845608028654) * square))
            share = 0.5 + 0.5 * bend
            act = up * share
            active[rows, columns] = act.astype(BF16)
            slope = share + act * (1.0 - share) * (
                2 * 0.7978845608028654 + (6 * 0.044715 * 0.7978845608028654) * square
            )
            up_grad[rows, columns] = (dot(cot[rows], w_down[columns], 1, 1) * slope).astype(BF16)


def run_units(sc, normed, cotangent, up, down):
    return pl.pallas_call(
        units_kernel,
        grid_spec=pltpu.PrefetchScalarGridSpec(
            num_scalar_prefetch=1,
            grid=(2 * FSIDE,),
            in_specs=[
                held((ROWS, WIDTH)),
                held((ROWS, WIDTH)),
                spec((WIDTH, FSTEP), early),
                spec((WIDTH, FSTEP), late),
                spec((FSTEP, SIDE), unit_rows),
                spec((FSTEP, SIDE), unit_rows),
            ],
            out_specs=[spec((ROWS, FSTEP), unit_columns), spec((ROWS, FSTEP), unit_columns)],
            scratch_shapes=[pltpu.VMEM((WIDTH, FSTEP), BF16), pltpu.VMEM((FSTEP, WIDTH), BF16)],
        ),
        out_shape=[jax.ShapeDtypeStruct((ROWS, FF), BF16), jax.ShapeDtypeStruct((ROWS, FF), BF16)],
        compiler_params=params(VMEM),
        cost_estimate=pl.CostEstimate(
            flops=4 * ROWS * WIDTH * FF, bytes_accessed=6 * ROWS * WIDTH + 4 * ROWS * FF, transcendentals=ROWS * FF
        ),
        name="units",
    )(sc, normed.reshape(ROWS, WIDTH), cotangent.reshape(ROWS, WIDTH), *up, *down)


def down_grad_kernel(sc, active, cot, own, far, total):
    total[...] = dot(active[...], cot[...], 0, 0).astype(BF16)
    own[...] = total[:, own_lanes(sc)]
    far[...] = total[:, far_lanes(sc)]


def run_down_grad(sc, active, cotangent):
    return pl.pallas_call(
        down_grad_kernel,
        grid_spec=pltpu.PrefetchScalarGridSpec(
            num_scalar_prefetch=1,
            grid=(FF // 512,),
            in_specs=[spec((ROWS, 512), lambda f, s: (0, f)), held((ROWS, WIDTH))],
            out_specs=[spec((512, SIDE), lambda f, s: (f, 0))] * 2,
            scratch_shapes=[pltpu.VMEM((512, WIDTH), BF16)],
        ),
        out_shape=[jax.ShapeDtypeStruct((FF, SIDE), BF16)] * 2,
        compiler_params=params(57 << 20),
        cost_estimate=pl.CostEstimate(
            flops=2 * ROWS * WIDTH * FF, bytes_accessed=2 * ROWS * (WIDTH + FF), transcendentals=0
        ),
        name="down_grad",
    )(sc, active, cotangent.reshape(ROWS, WIDTH))


def up_grad_kernel(sc, normed, up_grad, own, far):
    total = dot(normed[...], up_grad[...], 0, 0).astype(BF16)

    @pl.when(pl.program_id(0) < 3)
    def _():
        own[...] = total

    @pl.when(pl.program_id(0) >= 3)
    def _():
        far[...] = total


def run_up_grad(sc, normed, up_grad):
    return pl.pallas_call(
        up_grad_kernel,
        grid_spec=pltpu.PrefetchScalarGridSpec(
            num_scalar_prefetch=1,
            grid=(6,),
            in_specs=[held((ROWS, WIDTH)), spec((ROWS, 512), lambda f, s: (0, lax.rem(3 * s[CORE] + f, 6)))],
            out_specs=[
                spec((WIDTH, 512), lambda f, s: (0, lax.min(f, 2))),
                spec((WIDTH, 512), lambda f, s: (0, lax.max(f - 3, 0))),
            ],
        ),
        out_shape=[jax.ShapeDtypeStruct((WIDTH, FF // 2), BF16)] * 2,
        compiler_params=params(57 << 20),
        cost_estimate=pl.CostEstimate(
            flops=2 * ROWS * WIDTH * FF, bytes_accessed=2 * ROWS * (WIDTH + FF), transcendentals=0
        ),
        name="up_grad",
    )(sc, normed.reshape(ROWS, WIDTH), up_grad)


def out_grad_kernel(sc, mixed, res_own, res_far, own, far, total):
    step = pl.program_id(0)
    grad = jnp.concatenate([res_own[...], res_far[...]], axis=0).reshape(4 * SPAN, WIDTH)
    found = dot(mixed[...].reshape(4 * SPAN, WIDTH), grad, 0, 0)

    @pl.when(step == 0)
    def _():
        total[...] = found

    @pl.when(step > 0)
    def _():
        total[...] += found

    @pl.when(step == pl.num_programs(0) - 1)
    def _():
        own[...] = total[:, own_lanes(sc)].astype(BF16)
        far[...] = total[:, far_lanes(sc)].astype(BF16)


def run_out_grad(sc, mixed, res_own, res_far):
    return pl.pallas_call(
        out_grad_kernel,
        grid_spec=pltpu.PrefetchScalarGridSpec(
            num_scalar_prefetch=1,
            grid=(HROWS // SPAN,),
            in_specs=[slab_spec(), slab_spec(2), slab_spec(2)],
            out_specs=[held((WIDTH, SIDE))] * 2,
            scratch_shapes=[pltpu.VMEM((WIDTH, WIDTH), F32)],
        ),
        out_shape=[jax.ShapeDtypeStruct((WIDTH, SIDE), BF16)] * 2,
        compiler_params=params(LESS),
        cost_estimate=pl.CostEstimate(
            flops=2 * ROWS * WIDTH * WIDTH, bytes_accessed=4 * ROWS * WIDTH, transcendentals=0
        ),
        name="out_grad",
    )(sc, mixed, res_own, res_far)


def out_kernel(sc, active, resid, dn_own, dn_far, own, far, w_down):
    step = pl.program_id(0)

    @pl.when(step == 0)
    def _():
        w_down[:, own_lanes(sc)] = dn_own[...]
        w_down[:, far_lanes(sc)] = dn_far[...]

    branch = dot(active[...].reshape(4 * SPAN, FF), w_down[...], 1, 0)
    output = jnp.where(row_valid(sc, step), resid[...].reshape(4 * SPAN, WIDTH).astype(F32) + branch, 0.0)
    output = output.astype(BF16).reshape(4, SPAN, WIDTH)
    own[...] = output[:2]
    far[...] = output[2:]


def run_out(sc, active, resid, down):
    return pl.pallas_call(
        out_kernel,
        grid_spec=pltpu.PrefetchScalarGridSpec(
            num_scalar_prefetch=1,
            grid=(HROWS // SPAN,),
            in_specs=[
                spec((4, SPAN, FF), lambda r, s: (0, r, 0)),
                slab_spec(),
                held((FF, SIDE)),
                held((FF, SIDE)),
            ],
            out_specs=[slab_spec(2)] * 2,
            scratch_shapes=[pltpu.VMEM((FF, WIDTH), BF16)],
        ),
        out_shape=[
            jax.ShapeDtypeStruct((2, HROWS, WIDTH), BF16),
            jax.ShapeDtypeStruct((2, HROWS, WIDTH), BF16),
        ],
        compiler_params=params(LESS),
        cost_estimate=pl.CostEstimate(
            flops=2 * ROWS * WIDTH * FF, bytes_accessed=ROWS * (2 * FF + 7 * WIDTH), transcendentals=0
        ),
        name="out",
    )(sc, active.reshape(4, HROWS, FF), resid, *down)


def post_kernel(sc, resid, grad_own, grad_far, cot, up_own, up_far, wo_own, wo_far, gain, *refs):
    (res_own, res_far, heads, d_gain, weight, spread) = refs
    step = pl.program_id(0)
    whole_weight(sc, step, wo_own, wo_far, weight)
    shape, slab = (4 * SPAN, WIDTH), (4, SPAN, WIDTH)
    valid = row_valid(sc, step)
    res = resid[...].reshape(shape).astype(F32)
    scale = lax.rsqrt(jnp.mean(res * res, axis=-1, keepdims=True) + EPSILON)
    unit = res * scale
    units = (4 * SPAN, FF // 2)
    back = dot(grad_own[...].reshape(units), up_own[...], 1, 1) + dot(grad_far[...].reshape(units), up_far[...], 1, 1)
    two_grad = jnp.where(valid, back, 0.0)
    gained = two_grad * gain[...]
    masked = cot[...].reshape(shape).astype(F32)
    grad = masked + scale * (gained - unit * jnp.mean(gained * unit, axis=-1, keepdims=True))
    low = grad.astype(BF16)
    res_own[...] = low.reshape(slab)[:2]
    res_far[...] = low.reshape(slab)[2:]
    gain_sum = jnp.sum(two_grad * unit, axis=0, keepdims=True)

    @pl.when(step == 0)
    def _():
        d_gain[...] = gain_sum

    @pl.when(step > 0)
    def _():
        d_gain[...] += gain_sum

    spread[...] = dot(low, weight[...], 1, 1).astype(BF16).reshape(slab)
    for pair in range(HEADS // 2):
        lanes = slice(pair * 128, (pair + 1) * 128)
        for side in range(2):
            one, two = spread[2 * side, :, lanes], spread[2 * side + 1, :, lanes]
            half = slice(side * 128, (side + 1) * 128)
            heads[2 * pair, :, half] = jnp.concatenate([one[:, :HEAD], two[:, :HEAD]], axis=1)
            heads[2 * pair + 1, :, half] = jnp.concatenate([one[:, HEAD:], two[:, HEAD:]], axis=1)


def run_post(sc, resid, up_grad, cotangent, up, wo, gain):
    side = lambda which: spec((4, SPAN, FF // 2), lambda r, s: (0, r, s[CORE] if which == 0 else 1 - s[CORE]))
    up_grad = up_grad.reshape(4, HROWS, FF)
    return pl.pallas_call(
        post_kernel,
        grid_spec=pltpu.PrefetchScalarGridSpec(
            num_scalar_prefetch=1,
            grid=(HROWS // SPAN,),
            in_specs=[
                slab_spec(),
                side(0),
                side(1),
                slab_spec(),
                held((WIDTH, FF // 2)),
                held((WIDTH, FF // 2)),
                held((WIDTH, SIDE)),
                held((WIDTH, SIDE)),
                held((1, WIDTH)),
            ],
            out_specs=[slab_spec(2)] * 2 + [heads_spec(), held((1, WIDTH))],
            scratch_shapes=[
                pltpu.VMEM((WIDTH, WIDTH), BF16),
                pltpu.VMEM((4, SPAN, WIDTH), BF16),
            ],
        ),
        out_shape=[
            jax.ShapeDtypeStruct((2, HROWS, WIDTH), BF16),
            jax.ShapeDtypeStruct((2, HROWS, WIDTH), BF16),
            jax.ShapeDtypeStruct((HEADS, HROWS, 4 * HEAD), BF16),
            jax.ShapeDtypeStruct((1, WIDTH), F32),
        ],
        compiler_params=params(VMEM),
        cost_estimate=pl.CostEstimate(
            flops=2 * ROWS * WIDTH * (WIDTH + FF), bytes_accessed=ROWS * (16 * WIDTH + 2 * FF), transcendentals=0
        ),
        name="post",
    )(sc, resid, up_grad, up_grad, cotangent, *up, *wo, gain)


def unmix_kernel(count, carried, sc, v_own, v_far, grad_heads, mean, exps, inverse, *refs):
    refs = refs[2:] if carried else refs
    outs, (own, far, grads, mask, adder, bound, out_sems) = refs[: 4 * count], refs[4 * count :]
    place = sc[PLACE]
    step = pl.program_id(0)

    def leave(slot):
        return [
            pltpu.make_async_copy(
                grads.at[slot, pl.ds(pl.multiple_of((place ^ rel) * SUBS * HALF, SUBS * HALF), SUBS * HALF)],
                outs[4 * slot + rel],
                out_sems.at[slot, rel],
            )
            for rel in range(4)
        ]

    fill_mask(sc, mask)

    @pl.when(step == 0)
    def _():
        lane = lax.broadcasted_iota(jnp.int32, (4 * HEAD, 128), 0) // HEAD
        column = lax.broadcasted_iota(jnp.int32, (4 * HEAD, 128), 1)
        adder[...] = jnp.where((lane == column) | (lane + 4 == column), -1.0, 0.0).astype(BF16)
        row = lax.broadcasted_iota(jnp.int32, (LMAX, 128), 0)
        item = lax.broadcasted_iota(jnp.int32, (LMAX, 128), 1)
        length = jnp.where(item % 4 == 0, sc[LENGTHS], sc[LENGTHS + 1])
        length = jnp.where(item % 4 == 2, sc[LENGTHS + 2], length)
        length = jnp.where(item % 4 == 3, sc[LENGTHS + 3], length)
        bound[...] = jnp.where((item < 8) & (row < length), 1.0, 0.0).astype(BF16)

    high_lanes = lax.broadcasted_iota(jnp.int32, (HROWS, 128), 1) < 4
    for head in range(PHEADS):
        weights = exps[head]
        low = (grad_heads[head].astype(F32) * inverse[head].astype(F32)).astype(BF16)
        product = low.astype(F32) * mean[head]
        coarse = product.astype(BF16)
        fine = (product - coarse.astype(F32)).astype(BF16)
        delta = dot(coarse, adder[...], 1, 0) + dot(fine, adder[...], 1, 0)
        coarse = delta.astype(BF16)
        fine = (delta - coarse.astype(F32)).astype(BF16)
        left = jnp.concatenate([low, jnp.where(high_lanes, coarse, fine)], axis=1)
        score = dot(left, jnp.concatenate([v_own[head], v_far[head], bound[...]], axis=1), 1, 1)
        grads[step, head_rows(head)] = (score * weights.astype(F32)).astype(BF16)
        back = (dot(weights, low, 0, 0) * mask[...].astype(F32)).astype(BF16)
        own[head] = back[:, : 2 * HEAD]
        far[head] = back[:, 2 * HEAD :]
    for which in range(count):

        @pl.when(step == which)
        def _():
            for copy in leave(which):
                copy.start()
            if which == count - 1:
                for slot in range(count):
                    for copy in leave(slot):
                        copy.wait()


def run_unmix(sc, planes, v_own, v_far, grad_heads, mean, exps, inverse, carry):
    carry, count = list(carry), len(planes)
    return pl.pallas_call(
        partial(unmix_kernel, count, bool(carry)),
        grid_spec=pltpu.PrefetchScalarGridSpec(
            num_scalar_prefetch=1,
            grid=(count,),
            in_specs=[
                plane_spec(planes, LMAX, 2 * HEAD),
                plane_spec(planes, LMAX, 2 * HEAD),
                plane_spec(planes, HROWS, 4 * HEAD),
                plane_spec(planes, HROWS, 4 * HEAD),
                plane_spec(planes, HROWS, LMAX),
                plane_spec(planes, HROWS, 4 * HEAD),
            ]
            + anywhere(len(carry)),
            out_specs=anywhere(4 * count) + [plane_spec(planes, LMAX, 2 * HEAD)] * 2,
            scratch_shapes=[
                pltpu.VMEM((count, 4 * SUBS * HALF, LMAX), BF16),
                pltpu.VMEM((LMAX, 4 * HEAD), BF16),
                pltpu.VMEM((4 * HEAD, 128), BF16),
                pltpu.VMEM((LMAX, 128), BF16),
                pltpu.SemaphoreType.DMA((count, 4)),
            ],
        ),
        out_shape=[jax.ShapeDtypeStruct((SUBS * HALF, LMAX), BF16)] * (4 * count)
        + [jax.ShapeDtypeStruct((HEADS, LMAX, 2 * HEAD), BF16)] * 2,
        input_output_aliases={7 + i: 4 * count + i for i in range(len(carry))},
        compiler_params=params(VMEM),
        cost_estimate=pl.CostEstimate(
            flops=3 * HEADS * HROWS * LMAX * 4 * HEAD,
            bytes_accessed=HEADS * (2 * HROWS * LMAX + 5 * HROWS * 256 + 4 * LMAX * 256),
            transcendentals=0,
        ),
        name="unmix",
    )(sc, v_own, v_far, grad_heads, mean, exps, inverse, *carry)


def close_kernel(sc, tok, res_own, res_got, out_own, out_got, own, far, gain, w_own, w_far, *refs):
    (output, tok_grad, d_value, d_gain, total, weight) = refs
    step = pl.program_id(0)
    whole_weight(sc, step, w_own, w_far, weight)
    core = sc[CORE]
    output[:, :, core] = out_own[...].astype(F32)
    output[:, :, 1 - core] = out_got[...].astype(F32)
    tok_grad[:, :, core] = res_own[...].astype(F32)
    tok_grad[:, :, 1 - core] = res_got[...].astype(F32)
    runs = tok.shape[1]
    rows = runs * 128
    for item in range(2):
        lanes = slice(item * HEAD, (item + 1) * HEAD)
        pieces = [
            add_low(own[head, :, lanes], far[head, :, lanes]) for head in range(HEADS)
        ]
        back = jnp.concatenate(pieces, axis=1)
        x = tok[item].reshape(rows, WIDTH).astype(F32)
        scale = lax.rsqrt(jnp.mean(x * x, axis=-1, keepdims=True) + EPSILON)
        unit = x * scale
        normed = (unit * gain[...]).astype(BF16)
        normed_grad = dot(back, weight[...], 1, 1)
        gained = normed_grad * gain[...]
        update = scale * (gained - unit * jnp.mean(gained * unit, axis=-1, keepdims=True))
        tok_grad[item] += update.reshape(runs, 2, HALF, WIDTH)
        gain_sum = jnp.sum(normed_grad * unit, axis=0, keepdims=True)
        value_sum = dot(normed, back, 0, 0)
        if item == 0:
            gain_total, value_total = gain_sum, value_sum
        else:
            gain_total, value_total = gain_total + gain_sum, value_total + value_sum

    @pl.when(step == 0)
    def _():
        d_gain[...] = gain_total
        total[...] = value_total

    @pl.when(step > 0)
    def _():
        d_gain[...] += gain_total
        total[...] += value_total

    @pl.when(step == pl.num_programs(0) - 1)
    def _():
        low = total[...].astype(BF16)
        d_value[0] = low[:, :SIDE]
        d_value[1] = low[:, SIDE:]


def run_close(sc, tokens, res_own, res_got, out_own, out_got, own, far, gain, w_own, w_far):
    runs = 2
    slab = (2, RUNS, 2, HALF, WIDTH)
    half = (2, RUNS, HALF, WIDTH)
    whole_spec = spec((2, runs, 2, HALF, WIDTH), lambda j, s: (0, j, 0, 0, 0))
    half_spec = spec((2, runs, HALF, WIDTH), lambda j, s: (0, j, 0, 0))
    back_spec = spec((HEADS, runs * 128, 2 * HEAD), lambda j, s: (0, j, 0))
    return pl.pallas_call(
        close_kernel,
        grid_spec=pltpu.PrefetchScalarGridSpec(
            num_scalar_prefetch=1,
            grid=(RUNS // runs,),
            in_specs=[whole_spec]
            + [half_spec] * 4
            + [back_spec, back_spec, held((1, WIDTH)), held((WIDTH, SIDE)), held((WIDTH, SIDE))],
            out_specs=[whole_spec, whole_spec, held((2, WIDTH, SIDE)), held((1, WIDTH))],
            scratch_shapes=[pltpu.VMEM((WIDTH, WIDTH), F32), pltpu.VMEM((WIDTH, WIDTH), BF16)],
        ),
        out_shape=[
            jax.ShapeDtypeStruct(slab, F32),
            jax.ShapeDtypeStruct(slab, F32),
            jax.ShapeDtypeStruct((2, WIDTH, SIDE), BF16),
            jax.ShapeDtypeStruct((1, WIDTH), F32),
        ],
        compiler_params=params(LESS),
        cost_estimate=pl.CostEstimate(
            flops=4 * 2 * LMAX * WIDTH * WIDTH, bytes_accessed=38 * LMAX * WIDTH, transcendentals=0
        ),
        name="close",
    )(
        sc,
        tokens.reshape(slab),
        *(x.reshape(half) for x in (res_own, res_got, out_own, out_got)),
        own,
        far,
        gain,
        w_own,
        w_far,
    )


PACK_DOWN, PACK_UP, PACK_OUT, PACK_VALUE, PACK_GAIN, PACK = 0, 192, 384, 432, 480, 496


def pack_kernel(sc, down, up, out, value, gain, down_far, up_far, out_far, value_far, gain_far, packed):
    first = sc[CORE] == 0

    def both(own, far, lanes):
        own, far = own[:, lanes], far[:, lanes]
        return jnp.concatenate([jnp.where(first, own, far), jnp.where(first, far, own)], axis=0)

    def side(own, far):
        return both(own, far, own_lanes(sc))

    packed[PACK_DOWN:PACK_UP] = side(down, down_far)
    for j in range(4):
        lanes = pl.ds(pl.multiple_of((4 * sc[CORE] + j) * SIDE, 128), SIDE)
        packed[PACK_UP + 48 * j : PACK_UP + 48 * (j + 1)] = both(up, up_far, lanes)
    packed[PACK_OUT:PACK_VALUE] = side(out, out_far)
    packed[PACK_VALUE:PACK_GAIN] = side(value, value_far)
    packed[PACK_GAIN:] = both(gain, gain_far, slice(0, SIDE))


def run_pack(sc, own, far):
    return pl.pallas_call(
        pack_kernel,
        grid_spec=pltpu.PrefetchScalarGridSpec(
            num_scalar_prefetch=1,
            grid=(1,),
            in_specs=[held(x.shape) for x in (*own, *far)],
            out_specs=held((PACK, SIDE)),
        ),
        out_shape=jax.ShapeDtypeStruct((PACK, SIDE), BF16),
        compiler_params=params(VMEM),
        cost_estimate=pl.CostEstimate(flops=0, bytes_accessed=6 * PACK * SIDE, transcendentals=0),
        name="pack",
    )(sc, *own, *far)


def chip_of(sc, k, rel):
    return plane_of(k, sc) * 4 + (sc[PLACE] ^ rel)


def place_kernel(moves, sc, *refs):
    pieces, targets, sems = refs[:16], refs[16:-1], refs[-1]
    copies = []
    for index, piece in enumerate(pieces):
        chip = chip_of(sc, index // 4, index % 4)
        for which, (start, count, lane, target, step, offset, column) in enumerate(moves):
            rows = pl.ds(pl.multiple_of(chip * step + offset, 16), count)
            copies.append(
                pltpu.make_async_copy(
                    piece.at[pl.ds(start, count), pl.ds(lane, SIDE)],
                    targets[target].at[rows, pl.ds(column, SIDE)],
                    sems.at[index, which],
                )
            )
    for copy in copies:
        copy.start()
    for copy in copies:
        copy.wait()


def run_place(sc, pieces, moves, shapes):
    return pl.pallas_call(
        partial(place_kernel, moves),
        grid_spec=pltpu.PrefetchScalarGridSpec(
            num_scalar_prefetch=1,
            grid=(1,),
            in_specs=anywhere(16),
            out_specs=[held(shape) for shape in shapes],
            scratch_shapes=[pltpu.SemaphoreType.DMA((16, len(moves)))],
        ),
        out_shape=[jax.ShapeDtypeStruct(shape, BF16) for shape in shapes],
        compiler_params=params(VMEM),
        cost_estimate=pl.CostEstimate(
            flops=0, bytes_accessed=4 * sum(a * b for a, b in shapes), transcendentals=0
        ),
        name="place",
    )(sc, *pieces)


def place_weights(sc, pieces):
    moves = (
        (PACK_DOWN, 192, 0, 0, 192, 0, 0),
        *((PACK_UP + 48 * j, 48, 0, 1, 48, 0, j * SIDE) for j in range(4)),
        (PACK_OUT, 48, 0, 2, 48, 0, 0),
        (PACK_VALUE, 48, 0, 3, 48, 0, 0),
        (PACK_GAIN, 16, 0, 4, 16, 0, 0),
    )
    shapes = [(FF, SIDE), (WIDTH, FF // 2), (WIDTH, SIDE), (WIDTH, SIDE), (256, SIDE)]
    return run_place(sc, pieces, moves, shapes)


def collect_kernel(sc, *refs):
    outs = refs[24:]
    for k in range(PLANES):

        @pl.when(pl.program_id(0) == k)
        def _():
            for rel in range(4):
                down, down_got, up, up_got, out, out_got = refs[6 * rel : 6 * rel + 6]
                packed = outs[4 * k + rel]
                packed[PACK_DOWN:PACK_UP] = add_low(down[...], down_got[...])
                for j in range(4):
                    lanes = slice(j * SIDE, (j + 1) * SIDE)
                    packed[PACK_UP + 48 * j : PACK_UP + 48 * (j + 1)] = add_low(up[:, lanes], up_got[:, lanes])
                packed[PACK_OUT:PACK_VALUE] = add_low(out[...], out_got[...])


def run_collect(sc, *sides):
    def rows(x, rel):
        return spec((x.shape[0] // 16, x.shape[1]), lambda k, s: (chip_of(s, k, rel), 0))

    return pl.pallas_call(
        collect_kernel,
        grid_spec=pltpu.PrefetchScalarGridSpec(
            num_scalar_prefetch=1,
            grid=(PLANES,),
            in_specs=[rows(x, rel) for rel in range(4) for x in sides],
            out_specs=[held((PACK_VALUE, SIDE))] * 16,
        ),
        out_shape=[jax.ShapeDtypeStruct((PACK_VALUE, SIDE), BF16)] * 16,
        compiler_params=params(LESS),
        cost_estimate=pl.CostEstimate(flops=0, bytes_accessed=3 * 16 * PACK_VALUE * SIDE * 2, transcendentals=0),
        name="collect",
    )(sc, *(x for _ in range(4) for x in sides))


def add_kernel(groups, *refs):
    for group, total in zip(groups, refs[-len(groups) :]):
        value = refs[group[0]][...].astype(F32)
        for index in group[1:]:
            value = value + refs[index][...].astype(F32)
        total[...] = value.astype(total.dtype)


def run_add(groups, values, dtype):
    shape = values[0].shape
    here = pl.BlockSpec(memory_space=pltpu.VMEM)
    return pl.pallas_call(
        partial(add_kernel, groups),
        in_specs=[here] * len(values),
        out_specs=[here] * len(groups),
        out_shape=[jax.ShapeDtypeStruct(shape, dtype)] * len(groups),
        compiler_params=params(LESS),
        cost_estimate=pl.CostEstimate(
            flops=0, bytes_accessed=2 * shape[0] * shape[1] * (len(values) + len(groups)), transcendentals=0
        ),
        name="add",
    )(*values)


DEVICES = 32
TO_CORE, TO_X, TO_Y = 1, 2, 4


def swap(x, bit):
    return lax.ppermute(x, BOTH, [(d, d ^ bit) for d in range(DEVICES)])


def ring(x, way=1):
    return lax.ppermute(x, BOTH, [(d, (d + 8 * way) % DEVICES) for d in range(DEVICES)])


def pick(x, index, axis=0):
    return lax.dynamic_index_in_dim(x, index, axis, keepdims=False)


def ordered(flag, one, two, axis=0, joined=jnp.stack):
    return jnp.where(flag == 0, joined([one, two], axis), joined([two, one], axis))


def add_low(one, two):
    return (one.astype(F32) + two.astype(F32)).astype(BF16)


STEPS = (
    ((0, 0, 1), (0, 1, 0), (1, 0, 0)),
    ((1, 0, 1), (0, 1, 1), (2, 0, 0)),
    ((2, 0, 1), (1, 1, 0), (3, 0, 0)),
    ((1, 1, 1), (2, 1, 1), (2, 1, 0)),
    ((3, 0, 1), (3, 1, 0), (3, 1, 1)),
)


def gather_step(have, step):
    by_x, by_y, by_z = STEPS[step]
    return {
        **have,
        by_z: ring(have[by_z[0] - 1, by_z[1], by_z[2]]),
        by_x: swap(have[by_x[0], by_x[1], 0], TO_X),
        by_y: swap(have[by_y[0], 0, by_y[2]], TO_Y),
    }


def in_order(have):
    return [have[k, y, x] for k in range(4) for y in range(2) for x in range(2)]


def by_place(shares, planes=range(PLANES)):
    return {(k, i // 2, i % 2): shares[4 * at + i] for at, k in enumerate(planes) for i in range(4)}


def scatter_send(have, step):
    by_x, by_y, by_z = STEPS[len(STEPS) - 1 - step]
    got = (ring(have[by_z], -1), swap(have[by_x], TO_X), swap(have[by_y], TO_Y))
    return {at: value for at, value in have.items() if at not in (by_x, by_y, by_z)}, got


def scatter_add(have, got, step):
    by_x, by_y, by_z = STEPS[len(STEPS) - 1 - step]
    targets = ((by_z[0] - 1, by_z[1], by_z[2]), (by_x[0], by_x[1], 0), (by_y[0], 0, by_y[2]))
    sums = list(dict.fromkeys(targets))
    groups = [(len(got) + i, *(j for j in range(len(got)) if targets[j] == at)) for i, at in enumerate(sums)]
    values = [*got, *(have[at] for at in sums)]
    dtype = F32 if step == len(STEPS) - 1 else BF16
    if values[0].shape[1] == LMAX:
        totals = run_add(groups, values, dtype)
    else:
        totals = [sum(values[i].astype(F32) for i in group).astype(dtype) for group in groups]
    return {**have, **dict(zip(sums, totals))}


together = lax.optimization_barrier


def chip_shards(tokens, lengths, rand_mix, w_value, w_out, w_up, w_down, gain_mix, gain_ffn, grad_out):
    wide = lax.axis_index("wide")
    core = lax.axis_index("narrow")
    z, y, x = wide // 4, (wide // 2) % 2, wide % 2
    other = lambda value: swap(value, TO_CORE)
    side = partial(ordered, core, joined=jnp.concatenate)
    slab = (2, RUNS, 2, HALF, WIDTH)
    tokens, grad_out = tokens.reshape(slab), grad_out.reshape(slab)

    gains = jnp.pad(jnp.concatenate([gain_mix, gain_ffn])[None], ((0, 7), (0, SIDE - 48)))
    own = (w_down, w_up, w_out, w_value, gains)
    far = tuple(other(value) for value in own)
    near_sc = jnp.concatenate([jnp.stack([core, z, wide % 4]).astype(jnp.int32), lengths, lengths])
    weights = {(0, 0, 0): run_pack(near_sc, own, far)}

    rand = rand_mix.reshape(3, 2, HALF, LMAX)
    blocks = side(pick(rand, core, 1), other(pick(rand, 1 - core, 1)), 0)
    weights, rands, late_tokens, late_grad = together(
        (gather_step(weights, 0), {(0, 0, 0): blocks.reshape(SUBS * HALF, LMAX)}, tokens, grad_out)
    )
    weights, tokens_far = together((gather_step(weights, 1), other(pick(late_tokens, 1 - core, 2))))
    weights, grad_far = together((gather_step(weights, 2), other(pick(late_grad, 1 - core, 2))))
    weights, far_lengths = together((gather_step(weights, 3), other(lengths)))
    sc = jnp.concatenate([near_sc[:5], far_lengths])
    weights, rands = together((gather_step(weights, 4), rands))

    rands = gather_step(rands, 0)
    down, up, out, value, gain_rows = place_weights(sc, in_order(weights))
    rands, value, value_far, gain_rows, out, down, up = together(
        (rands, value, other(value), gain_rows, out, down, up)
    )
    gain_rows = gain_rows.reshape(16, 2, 8, SIDE)[:, :, 0]
    gain_one = gain_rows[..., :24].reshape(1, WIDTH).astype(F32)
    gain_two = gain_rows[..., 24:48].reshape(1, WIDTH).astype(F32)
    rands = gather_step(rands, 1)
    v_own = run_values(sc, tokens.reshape(2, LMAX, WIDTH), gain_one, value, value_far)
    rands, v_own, out, down, up = together((rands, v_own, (out, other(out)), down, up))
    rands, v_own, v_far, grad_far, down, up = together(
        (gather_step(rands, 2), v_own, other(v_own), grad_far, down, up)
    )
    rands = gather_step(rands, 3)
    masked = run_masked(sc, grad_out, grad_far)
    rands, v_far, masked, down, up = together((rands, v_far, masked, down, up))
    near = [rands[k, y_at, x_at] for k in range(3) for y_at in range(2) for x_at in range(2)]
    rands = gather_step(rands, 4)
    mixing = run_mix(sc, (0, 1, 2), near, v_own, v_far, ())
    rands, down, up, mixing = together((rands, down, up, mixing))
    heads, mean, exps, inverse = run_mix(sc, (3,), in_order(rands)[12:], v_own, v_far, mixing)
    down, up = (down, other(down)), (up, other(up))

    mixed, resid, normed = run_pre(sc, tokens, tokens_far, heads, out, gain_two)
    active, up_grad = run_units(sc, normed, masked, up, down)
    res_own, res_far, grad_heads, d_gain_two = run_post(sc, resid, up_grad, masked, up, out, gain_two)

    backward = lambda planes, carry: run_unmix(sc, planes, v_own, v_far, grad_heads, mean, exps, inverse, carry)
    *far, back_own, back_far = backward((3,), ())
    far, back_own, back_far, res_got = together((far, back_own, back_far, other(res_far)))
    have, got = scatter_send(by_place(far, (3,)), 0)
    *near, back_own, back_far = backward((2, 1, 0), (back_own, back_far))
    have, got, near, back_own, back_far = together((have, got, near, back_own, back_far))
    have = scatter_add({**have, **by_place(near, (2, 1, 0))}, got, 0)

    have, got = scatter_send(have, 1)
    up_own, up_far = run_up_grad(sc, normed, up_grad)
    have, got, up_own, up_far, back_got = together((have, got, up_own, up_far, other(back_far)))
    have = scatter_add(have, got, 1)

    have, got = scatter_send(have, 2)
    down_own, down_far = run_down_grad(sc, active, masked)
    have, got, down_own, down_far, up_got = together((have, got, down_own, down_far, other(up_far)))
    have = scatter_add(have, got, 2)

    have, got = scatter_send(have, 3)
    out_own, out_far = run_out(sc, active, resid, down)
    have, got, out_own, out_far, down_got = together((have, got, out_own, out_far, other(down_far)))
    have = scatter_add(have, got, 3)

    have, got = scatter_send(have, 4)
    d_out_own, d_out_far = run_out_grad(sc, mixed, res_own, res_far)
    packed = run_collect(sc, down_own, down_got, up_own, up_got, d_out_own, other(d_out_far))
    sums, sums_got = scatter_send(by_place(packed), 0)
    have, got, sums, sums_got, out_got = together((have, got, sums, sums_got, other(out_far)))
    rand_sum = scatter_add(have, got, 4)[0, 0, 0].reshape(2, 3, HALF, LMAX)

    sums, got = scatter_send(scatter_add(sums, sums_got, 0), 1)
    output, tokens_grad, d_value, d_gain_one = run_close(
        sc, tokens, res_own, res_got, out_own, out_got, back_own, back_got, gain_one, value, value_far
    )
    sums, got, output, tokens_grad, d_value, d_gain_one = together(
        (sums, got, output, tokens_grad, d_value, d_gain_one)
    )
    sums = scatter_add(sums, got, 1)

    sums, got = scatter_send(sums, 2)
    gain_pair = jnp.concatenate([d_gain_one, d_gain_two]).reshape(2, 16, 1, 48).astype(BF16)
    gain_pair = jnp.pad(gain_pair, ((0, 0), (0, 0), (0, 15), (0, SIDE - 48)))
    small = jnp.concatenate([d_value.reshape(2, 16, 48, SIDE), gain_pair], 2)
    small = add_low(pick(small, core), other(pick(small, 1 - core))).reshape(4, 2, 2, 64, SIDE)
    small = add_low(pick(small, x, 2), swap(pick(small, 1 - x, 2), TO_X))
    sums, got, small = together((sums, got, small))
    sums = scatter_add(sums, got, 2)

    sums, got = scatter_send(sums, 3)
    small = add_low(pick(small, y, 1), swap(pick(small, 1 - y, 1), TO_Y))
    blocks, blocks_far = pick(rand_sum, core), other(pick(rand_sum, 1 - core))
    sums, got, small, blocks, blocks_far = together((sums, got, small, blocks, blocks_far))
    sums = scatter_add(sums, got, 3)

    sums, got = scatter_send(sums, 4)
    small_sum = pick(small, z).astype(F32)
    for k in range(1, PLANES):
        small_sum = small_sum + ring(pick(small, lax.rem(z + PLANES - k, PLANES)), -k).astype(F32)
    sums, got, small_sum = together((sums, got, small_sum))
    big_sum = scatter_add(sums, got, 4)[0, 0, 0]
    big_far, small_far = other(big_sum), other(small_sum)

    rows_of = lambda value, rows: pick(value.reshape(-1, 2, rows, SIDE), core, 1)
    mine = lambda own, far, rows: side(rows_of(own, rows)[0], rows_of(far, rows)[0], 1)
    down_shard = mine(big_sum[PACK_DOWN:PACK_UP], big_far[PACK_DOWN:PACK_UP], 96)
    up_side = lambda value: rows_of(value[PACK_UP:PACK_OUT], 24).transpose(1, 0, 2).reshape(24, 4 * SIDE)
    up_shard = side(up_side(big_sum), up_side(big_far), 1)
    outproj_shard = mine(big_sum[PACK_OUT:PACK_VALUE], big_far[PACK_OUT:PACK_VALUE], 24)
    value_shard = mine(small_sum[:48], small_far[:48], 24)
    gains_pair = ordered(core, small_sum[48, :48], small_far[48, :48])
    gain_pair = pick(gains_pair.reshape(2, 2, 24), core, 1)

    rand_shard = ordered(core, blocks, blocks_far, 1)

    return (
        output.reshape(2, LMAX, WIDTH),
        tokens_grad.reshape(2, LMAX, WIDTH),
        rand_shard.reshape(3 * 128, LMAX),
        value_shard,
        outproj_shard,
        up_shard,
        down_shard,
        gain_pair[0],
        gain_pair[1],
    )


def rms_norm(values, gain):
    scale = lax.rsqrt(jnp.mean(values * values, axis=-1, keepdims=True) + EPSILON)
    return values * scale * gain


def split_heads(block):
    return block.reshape(LMAX, HEADS, HEAD).transpose(1, 0, 2)


def merge_heads(block):
    return block.transpose(1, 0, 2).reshape(LMAX, HEADS * HEAD)


def masked_scores(key_mask, rand_head):
    return jnp.where(key_mask[None, :] > 0, rand_head.astype(jnp.float32), -1e30)


def head_forward(key_mask, paired):
    rand_head, value_head = paired
    scores = masked_scores(key_mask, rand_head)
    row_peak = jnp.max(scores, axis=-1, keepdims=True)
    exponent = jnp.exp(scores - row_peak)
    denom_sum = jnp.sum(exponent, axis=-1, keepdims=True)
    attention = exponent / denom_sum * key_mask[:, None]
    mixed = jnp.dot(attention.astype(jnp.bfloat16), value_head, preferred_element_type=jnp.float32)
    return (mixed.astype(jnp.bfloat16), row_peak + jnp.log(denom_sum))


def head_backward(key_mask, paired):
    rand_head, value_head, mix_grad, log_total = paired
    scores = masked_scores(key_mask, rand_head)
    attention = jnp.exp(scores - log_total) * key_mask[:, None]
    prob_grad = jnp.einsum("id,jd->ij", mix_grad, value_head, preferred_element_type=jnp.float32)
    value_grad = jnp.einsum(
        "ij,id->jd", attention.astype(jnp.bfloat16), mix_grad, preferred_element_type=jnp.float32
    )
    score_grad = attention * (prob_grad - jnp.sum(prob_grad * attention, axis=-1, keepdims=True))
    return (score_grad, value_grad)


def shards(tokens, lengths, rand_mix, w_value, w_out, w_up, w_down, gain_mix, gain_ffn, grad_out):
    item_count = tokens.shape[0]
    width = tokens.shape[2]
    row_count = item_count * LMAX
    tokens_flat = tokens.reshape(row_count, width).astype(jnp.float32)
    positions = jnp.arange(LMAX, dtype=jnp.int32)
    valid_table = (positions[None, :] < lengths[:, None]).astype(jnp.float32)
    row_valid = valid_table.reshape(row_count, 1)
    forward_set = (
        lax.all_gather(rand_mix, ("wide", "narrow"), axis=0, tiled=True),
        lax.all_gather(w_value, ("wide", "narrow"), axis=0, tiled=True),
        lax.all_gather(w_out, ("wide", "narrow"), axis=0, tiled=True),
        lax.all_gather(w_up, ("wide", "narrow"), axis=0, tiled=True),
        lax.all_gather(w_down, ("wide", "narrow"), axis=0, tiled=True),
        lax.all_gather(gain_mix, ("wide", "narrow"), axis=0, tiled=True),
        lax.all_gather(gain_ffn, ("wide", "narrow"), axis=0, tiled=True),
    )
    rand_all, value_all, out_all, up_all, down_all, gain_first, gain_second = forward_set
    normed = rms_norm(tokens_flat, gain_first.astype(jnp.float32)).astype(jnp.bfloat16)
    values = jnp.dot(normed, value_all, preferred_element_type=jnp.float32).astype(jnp.bfloat16)
    rand_heads = rand_all.reshape(HEADS, LMAX, LMAX)
    mixed_parts = []
    totals_kept = []
    for item_index in range(item_count):
        item_values = split_heads(values[item_index * LMAX : (item_index + 1) * LMAX])
        mixed_heads, log_total = lax.map(
            partial(head_forward, valid_table[item_index]), (rand_heads, item_values)
        )
        mixed_parts.append(merge_heads(mixed_heads))
        totals_kept.append(log_total)
    mixed = jnp.concatenate(mixed_parts, axis=0)
    residual = tokens_flat + jnp.dot(mixed, out_all, preferred_element_type=jnp.float32)
    normed_two = rms_norm(residual, gain_second.astype(jnp.float32)).astype(jnp.bfloat16)
    up_proj = jnp.dot(normed_two, up_all, preferred_element_type=jnp.float32)
    active = jax.nn.gelu(up_proj).astype(jnp.bfloat16)
    branch = jnp.dot(active, down_all, preferred_element_type=jnp.float32)
    output = row_valid * (residual + branch)
    back_set = (
        lax.all_gather(rand_mix, ("wide", "narrow"), axis=0, tiled=True),
        lax.all_gather(w_value, ("wide", "narrow"), axis=0, tiled=True),
        lax.all_gather(w_out, ("wide", "narrow"), axis=0, tiled=True),
        lax.all_gather(w_up, ("wide", "narrow"), axis=0, tiled=True),
        lax.all_gather(w_down, ("wide", "narrow"), axis=0, tiled=True),
        lax.all_gather(gain_mix, ("wide", "narrow"), axis=0, tiled=True),
        lax.all_gather(gain_ffn, ("wide", "narrow"), axis=0, tiled=True),
    )
    rand_back, value_back, out_back, up_back, down_back, gain_back_one, gain_back_two = back_set
    cotangent = grad_out.reshape(row_count, width).astype(jnp.float32)
    masked = row_valid * cotangent
    branch_grad = masked.astype(jnp.bfloat16)
    grad_down = jnp.einsum("rk,rd->kd", active, branch_grad, preferred_element_type=jnp.float32)
    active_grad = jnp.einsum(
        "rd,kd->rk", branch_grad, down_back, preferred_element_type=jnp.float32
    )
    gelu_value, gelu_pull = jax.vjp(jax.nn.gelu, up_proj)
    up_grad = gelu_pull(active_grad)[0].astype(jnp.bfloat16)
    grad_up = jnp.einsum("rd,rk->dk", normed_two, up_grad, preferred_element_type=jnp.float32)
    normed_two_grad = jnp.einsum("rk,dk->rd", up_grad, up_back, preferred_element_type=jnp.float32)
    norm_value, norm_pull = jax.vjp(rms_norm, residual, gain_back_two.astype(jnp.float32))
    residual_part, gain_two_grad = norm_pull(normed_two_grad)
    residual_grad = masked + residual_part
    attn_grad = residual_grad.astype(jnp.bfloat16)
    grad_outproj = jnp.einsum("rd,re->de", mixed, attn_grad, preferred_element_type=jnp.float32)
    mixed_grad = jnp.einsum(
        "re,de->rd", attn_grad, out_back, preferred_element_type=jnp.float32
    ).astype(jnp.bfloat16)
    rand_heads_back = rand_back.reshape(HEADS, LMAX, LMAX)
    rand_grad = jnp.zeros((HEADS, LMAX, LMAX), jnp.float32)
    value_parts = []
    for item_index in range(item_count):
        lower_row = item_index * LMAX
        upper_row = lower_row + LMAX
        item_values = split_heads(values[lower_row:upper_row])
        item_mix_grad = split_heads(mixed_grad[lower_row:upper_row])
        score_grad, value_grad = lax.map(
            partial(head_backward, valid_table[item_index]),
            (rand_heads_back, item_values, item_mix_grad, totals_kept[item_index]),
        )
        rand_grad = rand_grad + score_grad
        value_parts.append(merge_heads(value_grad))
    values_grad = jnp.concatenate(value_parts, axis=0).astype(jnp.bfloat16)
    grad_value = jnp.einsum("rd,re->de", normed, values_grad, preferred_element_type=jnp.float32)
    normed_grad = jnp.einsum(
        "re,de->rd", values_grad, value_back, preferred_element_type=jnp.float32
    )
    norm_first, first_pull = jax.vjp(rms_norm, tokens_flat, gain_back_one.astype(jnp.float32))
    token_part, gain_one_grad = first_pull(normed_grad)
    tokens_grad = residual_grad + token_part
    rand_flat = rand_grad.reshape(HEADS * LMAX, LMAX)
    all_shards = (
        lax.psum_scatter(rand_flat, ("wide", "narrow"), scatter_dimension=0, tiled=True),
        lax.psum_scatter(grad_value, ("wide", "narrow"), scatter_dimension=0, tiled=True),
        lax.psum_scatter(grad_outproj, ("wide", "narrow"), scatter_dimension=0, tiled=True),
        lax.psum_scatter(grad_up, ("wide", "narrow"), scatter_dimension=0, tiled=True),
        lax.psum_scatter(grad_down, ("wide", "narrow"), scatter_dimension=0, tiled=True),
        lax.psum_scatter(gain_one_grad, ("wide", "narrow"), scatter_dimension=0, tiled=True),
        lax.psum_scatter(gain_two_grad, ("wide", "narrow"), scatter_dimension=0, tiled=True),
    )
    rand_shard, value_shard, outproj_shard, up_shard, down_shard, gain_one_shard, gain_two_shard = (
        all_shards
    )
    return (
        output.reshape(item_count, LMAX, width),
        tokens_grad.reshape(item_count, LMAX, width),
        rand_shard,
        value_shard,
        outproj_shard,
        up_shard,
        down_shard,
        gain_one_shard,
        gain_two_shard,
    )


def solution(mesh):
    in_specs = (
        P(("wide", "narrow"), None, None),
        P(("wide", "narrow")),
        P(("wide", "narrow"), None),
        P(("wide", "narrow"), None),
        P(("wide", "narrow"), None),
        P(("wide", "narrow"), None),
        P(("wide", "narrow"), None),
        P(("wide", "narrow")),
        P(("wide", "narrow")),
        P(("wide", "narrow"), None, None),
    )
    out_specs = (
        P(("wide", "narrow"), None, None),
        P(("wide", "narrow"), None, None),
        P(("wide", "narrow"), None),
        P(("wide", "narrow"), None),
        P(("wide", "narrow"), None),
        P(("wide", "narrow"), None),
        P(("wide", "narrow"), None),
        P(("wide", "narrow")),
        P(("wide", "narrow")),
    )
    fits = dict(mesh.shape) == {"wide": 16, "narrow": 2}
    return jax.shard_map(chip_shards if fits else shards, mesh=mesh, in_specs=in_specs, out_specs=out_specs, check_vma=False)
```

```python
from functools import partial

import jax
import jax.numpy as jnp
from jax import lax
from jax.experimental import pallas as pl
from jax.experimental.pallas import tpu as pltpu
from jax.sharding import PartitionSpec as P

HEADS = 12
HEAD = 64
LMAX = 1024
WIDTH = 768
FF = 3072
EPSILON = 1e-05

BOTH = ("wide", "narrow")
BF16 = jnp.bfloat16
F32 = jnp.float32
VMEM = 61 << 20
LESS = 34 << 20

SUBS = 6
RUNS = 8
HALF = 64
HROWS = RUNS * HALF
PLANES = 4
PHEADS = HEADS // PLANES
ROWS = 2 * LMAX
FSTEP = 768
FSIDE = FF // 2 // FSTEP
TILE = 512
SIDE = WIDTH // 2
SPAN = 2 * HALF


def dot(a, b, ca, cb):
    return lax.dot_general(a, b, (((ca,), (cb,)), ((), ())), preferred_element_type=F32)


CORE, PLANE, PLACE, LENGTHS = 0, 1, 2, 3


def spec(shape, index):
    return pl.BlockSpec(shape, index)


def held(shape):
    zeros = (0,) * len(shape)
    return pl.BlockSpec(shape, lambda *_: zeros, pipeline_mode=pl.Buffered(1))


def params(limit):
    return pltpu.CompilerParams(vmem_limit_bytes=limit)


def whole_weight(sc, step, own, far, weight):
    @pl.when(step == 0)
    def _():
        weight[:, pl.ds(pl.multiple_of(sc[CORE] * SIDE, 128), SIDE)] = own[...]
        weight[:, pl.ds(pl.multiple_of((1 - sc[CORE]) * SIDE, 128), SIDE)] = far[...]


def values_kernel(sc, tok, gain, w_own, w_far, out, weight):
    step = pl.program_id(0)
    whole_weight(sc, step, w_own, w_far, weight)
    rows = tok.shape[1]
    position = step * rows + lax.broadcasted_iota(jnp.int32, (rows, 1), 0)
    for item in range(2):
        x = tok[item].astype(F32)
        scale = lax.rsqrt(jnp.mean(x * x, axis=-1, keepdims=True) + EPSILON)
        normed = (x * scale * gain[...]).astype(BF16)
        found = dot(normed, weight[...], 1, 0)
        found = jnp.where(position < sc[LENGTHS + item], found, 0.0).astype(BF16)
        for head in range(HEADS):
            out[head, :, item * HEAD : (item + 1) * HEAD] = found[:, head * HEAD : (head + 1) * HEAD]


def run_values(sc, tokens, gain, w_own, w_far):
    rows = 256
    return pl.pallas_call(
        values_kernel,
        grid_spec=pltpu.PrefetchScalarGridSpec(
            num_scalar_prefetch=1,
            grid=(LMAX // rows,),
            in_specs=[
                spec((2, rows, WIDTH), lambda j, s: (0, j, 0)),
                held((1, WIDTH)),
                held((WIDTH, SIDE)),
                held((WIDTH, SIDE)),
            ],
            out_specs=spec((HEADS, rows, 2 * HEAD), lambda j, s: (0, j, 0)),
            scratch_shapes=[pltpu.VMEM((WIDTH, WIDTH), BF16)],
        ),
        out_shape=jax.ShapeDtypeStruct((HEADS, LMAX, 2 * HEAD), BF16),
        compiler_params=params(VMEM),
        cost_estimate=pl.CostEstimate(
            flops=2 * 2 * LMAX * WIDTH * WIDTH, bytes_accessed=8 * LMAX * WIDTH, transcendentals=0
        ),
        name="values",
    )(sc, tokens, gain, w_own, w_far)


def lane_lengths(sc, shape):
    slot = lax.broadcasted_iota(jnp.int32, shape, 1) // HEAD
    length = jnp.where(slot == 0, sc[LENGTHS], sc[LENGTHS + 1])
    return jnp.where(slot >= 2, jnp.where(slot == 2, sc[LENGTHS + 2], sc[LENGTHS + 3]), length)


def plane_of(k, sc):
    return lax.rem(sc[PLANE] + PLANES - k, PLANES)


def plane_spec(planes, rows, lanes):
    def index(step, sc):
        return (plane_of(planes[0] + step * (planes[-1] - planes[0]) // max(len(planes) - 1, 1), sc), 0, 0)

    return spec((PHEADS, rows, lanes), index)


def anywhere(count):
    return [pl.BlockSpec(memory_space=pl.ANY)] * count


def plane_fetch(place, shards, raw, sems, slot):
    return [
        pltpu.make_async_copy(
            shards[4 * slot + rel],
            raw.at[slot, pl.ds(pl.multiple_of((place ^ rel) * SUBS * HALF, SUBS * HALF), SUBS * HALF)],
            sems.at[slot, rel],
        )
        for rel in range(4)
    ]


def take_plane(place, shards, raw, sems):
    step = pl.program_id(0)
    count = len(shards) // 4

    @pl.when(step == 0)
    def _():
        for slot in range(count):
            for copy in plane_fetch(place, shards, raw, sems, slot):
                copy.start()

    for slot in range(count):

        @pl.when(step == slot)
        def _():
            for copy in plane_fetch(place, shards, raw, sems, slot):
                copy.wait()

    return step


def head_rows(head):
    return slice(head * HROWS, (head + 1) * HROWS)


def fill_mask(sc, mask):
    @pl.when(pl.program_id(0) == 0)
    def _():
        shape = (LMAX, 4 * HEAD)
        column = lax.broadcasted_iota(jnp.int32, shape, 0)
        mask[...] = (column < lane_lengths(sc, shape)).astype(F32).astype(BF16)


def mix_kernel(count, carried, sc, *refs):
    shards, (v_own, v_far, *rest) = refs[: 4 * count], refs[4 * count :]
    mixed, mean, exps, inverse, raw, mask, sems = rest[4:] if carried else rest
    fill_mask(sc, mask)
    slot = take_plane(sc[PLACE], shards, raw, sems)
    shape = (HROWS, 4 * HEAD)
    line = lax.broadcasted_iota(jnp.int32, shape, 0)
    position = 128 * (line // HALF) + HALF * sc[CORE] + line % HALF
    valid = position < lane_lengths(sc, shape)
    for head in range(PHEADS):
        weights = jnp.exp(raw[slot, head_rows(head)].astype(F32)).astype(BF16)
        exps[head] = weights
        both = dot(weights, jnp.concatenate([v_own[head], v_far[head], mask[...]], axis=1), 1, 0)
        flip = jnp.where(valid, 1.0 / both[:, 4 * HEAD :], 0.0)
        found = both[:, : 4 * HEAD] * flip
        inverse[head] = flip.astype(BF16)
        mean[head] = found
        mixed[head] = found.astype(BF16)


def run_mix(sc, planes, shards, v_own, v_far, carry):
    carry, count = list(carry), len(planes)
    shape = (HEADS, HROWS, 4 * HEAD)
    return pl.pallas_call(
        partial(mix_kernel, count, bool(carry)),
        grid_spec=pltpu.PrefetchScalarGridSpec(
            num_scalar_prefetch=1,
            grid=(count,),
            in_specs=anywhere(4 * count) + [plane_spec(planes, LMAX, 2 * HEAD)] * 2 + anywhere(len(carry)),
            out_specs=[
                plane_spec(planes, HROWS, 4 * HEAD),
                plane_spec(planes, HROWS, 4 * HEAD),
                plane_spec(planes, HROWS, LMAX),
                plane_spec(planes, HROWS, 4 * HEAD),
            ],
            scratch_shapes=[
                pltpu.VMEM((count, 4 * SUBS * HALF, LMAX), BF16),
                pltpu.VMEM((LMAX, 4 * HEAD), BF16),
                pltpu.SemaphoreType.DMA((count, 4)),
            ],
        ),
        out_shape=[
            jax.ShapeDtypeStruct(shape, BF16),
            jax.ShapeDtypeStruct(shape, F32),
            jax.ShapeDtypeStruct((HEADS, HROWS, LMAX), BF16),
            jax.ShapeDtypeStruct(shape, BF16),
        ],
        input_output_aliases={3 + 4 * count + i: i for i in range(len(carry))},
        compiler_params=params(VMEM),
        cost_estimate=pl.CostEstimate(
            flops=2 * HEADS * HROWS * LMAX * 4 * HEAD,
            bytes_accessed=HEADS * (2 * HROWS * LMAX + 5 * HROWS * 256),
            transcendentals=HEADS * HROWS * LMAX // 2,
        ),
        name="mix",
    )(sc, *shards, v_own, v_far, *carry)


def row_valid(sc, step):
    line = lax.broadcasted_iota(jnp.int32, (4 * SPAN, 1), 0)
    item = line // SPAN
    row = step * SPAN + line % SPAN
    low = jnp.where(item == 0, sc[LENGTHS], sc[LENGTHS + 1])
    high = jnp.where(item == 2, sc[LENGTHS + 2], sc[LENGTHS + 3])
    return 128 * (row // HALF) + HALF * sc[CORE] + row % HALF < jnp.where(item >= 2, high, low)


def four_items(own, far):
    return jnp.concatenate([own[:, :, 0], far[...]], axis=0).reshape(4 * SPAN, WIDTH)


def pre_kernel(sc, tok, tok_far, heads, wo_own, wo_far, gain, mixed, resid, normed, weight):
    step = pl.program_id(0)
    whole_weight(sc, step, wo_own, wo_far, weight)
    for item in range(4):
        lanes = slice(item * HEAD, (item + 1) * HEAD)
        for pair in range(HEADS // 2):
            both = jnp.concatenate([heads[2 * pair, :, lanes], heads[2 * pair + 1, :, lanes]], axis=1)
            mixed[item, :, pair * 128 : (pair + 1) * 128] = both
    res = four_items(tok, tok_far).astype(F32) + dot(mixed[...].reshape(4 * SPAN, WIDTH), weight[...], 1, 0)
    resid[...] = res.astype(BF16).reshape(4, SPAN, WIDTH)
    scale = lax.rsqrt(jnp.mean(res * res, axis=-1, keepdims=True) + EPSILON)
    valid = row_valid(sc, step)
    normed[...] = jnp.where(valid, res * scale * gain[...], 0.0).astype(BF16).reshape(4, SPAN, WIDTH)


def slab_spec(items=4):
    return spec((items, SPAN, WIDTH), lambda r, s: (0, r, 0))


def half_specs():
    return [
        spec((2, SPAN // HALF, 1, HALF, WIDTH), lambda r, s: (0, r, s[CORE], 0, 0)),
        spec((2, SPAN // HALF, HALF, WIDTH), lambda r, s: (0, r, 0, 0)),
    ]


def heads_spec():
    return spec((HEADS, SPAN, 4 * HEAD), lambda r, s: (0, r, 0))


def run_pre(sc, tokens, tokens_far, heads, wo, gain):
    return pl.pallas_call(
        pre_kernel,
        grid_spec=pltpu.PrefetchScalarGridSpec(
            num_scalar_prefetch=1,
            grid=(HROWS // SPAN,),
            in_specs=half_specs()
            + [heads_spec(), held((WIDTH, SIDE)), held((WIDTH, SIDE)), held((1, WIDTH))],
            out_specs=[slab_spec()] * 3,
            scratch_shapes=[pltpu.VMEM((WIDTH, WIDTH), BF16)],
        ),
        out_shape=[
            jax.ShapeDtypeStruct((4, HROWS, WIDTH), BF16),
            jax.ShapeDtypeStruct((4, HROWS, WIDTH), BF16),
            jax.ShapeDtypeStruct((4, HROWS, WIDTH), BF16),
        ],
        compiler_params=params(VMEM),
        cost_estimate=pl.CostEstimate(
            flops=2 * ROWS * WIDTH * WIDTH, bytes_accessed=16 * ROWS * WIDTH, transcendentals=0
        ),
        name="pre",
    )(sc, tokens, tokens_far, heads, *wo, gain)


def masked_kernel(sc, cot, cot_far, masked):
    value = jnp.where(row_valid(sc, pl.program_id(0)), four_items(cot, cot_far).astype(F32), 0.0)
    masked[...] = value.astype(BF16).reshape(4, SPAN, WIDTH)


def run_masked(sc, cotangent, cotangent_far):
    return pl.pallas_call(
        masked_kernel,
        grid_spec=pltpu.PrefetchScalarGridSpec(
            num_scalar_prefetch=1, grid=(HROWS // SPAN,), in_specs=half_specs(), out_specs=slab_spec()
        ),
        out_shape=jax.ShapeDtypeStruct((4, HROWS, WIDTH), BF16),
        compiler_params=params(VMEM),
        cost_estimate=pl.CostEstimate(flops=0, bytes_accessed=4 * ROWS * WIDTH, transcendentals=0),
        name="masked",
    )(sc, cotangent, cotangent_far)


def own_lanes(sc):
    return pl.ds(pl.multiple_of(sc[CORE] * SIDE, 128), SIDE)


def far_lanes(sc):
    return pl.ds(pl.multiple_of((1 - sc[CORE]) * SIDE, 128), SIDE)


def unit_rows(f, sc):
    return (lax.rem(FSIDE * sc[CORE] + f, 2 * FSIDE), 0)


def unit_columns(f, sc):
    return (0, lax.rem(FSIDE * sc[CORE] + f, 2 * FSIDE))


def early(f, sc):
    return (0, lax.min(f, FSIDE - 1))


def late(f, sc):
    return (0, lax.max(f - FSIDE, 0))


def units_kernel(sc, normed, cot, up_own, up_far, dn_own, dn_far, active, up_grad, w_up, w_down):
    step = pl.program_id(0)
    w_down[:, own_lanes(sc)] = dn_own[...]
    w_down[:, far_lanes(sc)] = dn_far[...]

    @pl.when(step < FSIDE)
    def _():
        w_up[...] = up_own[...]

    @pl.when(step >= FSIDE)
    def _():
        w_up[...] = up_far[...]

    for row in range(0, ROWS, 256):
        rows = slice(row, row + 256)
        for column in range(0, FSTEP, 256):
            columns = slice(column, column + 256)
            up = dot(normed[rows], w_up[:, columns], 1, 0)
            square = up * up
            bend = jnp.tanh(up * (0.7978845608028654 + (0.044715 * 0.7978845608028654) * square))
            share = 0.5 + 0.5 * bend
            act = up * share
            active[rows, columns] = act.astype(BF16)
            slope = share + act * (1.0 - share) * (
                2 * 0.7978845608028654 + (6 * 0.044715 * 0.7978845608028654) * square
            )
            up_grad[rows, columns] = (dot(cot[rows], w_down[columns], 1, 1) * slope).astype(BF16)


def run_units(sc, normed, cotangent, up, down):
    return pl.pallas_call(
        units_kernel,
        grid_spec=pltpu.PrefetchScalarGridSpec(
            num_scalar_prefetch=1,
            grid=(2 * FSIDE,),
            in_specs=[
                held((ROWS, WIDTH)),
                held((ROWS, WIDTH)),
                spec((WIDTH, FSTEP), early),
                spec((WIDTH, FSTEP), late),
                spec((FSTEP, SIDE), unit_rows),
                spec((FSTEP, SIDE), unit_rows),
            ],
            out_specs=[spec((ROWS, FSTEP), unit_columns), spec((ROWS, FSTEP), unit_columns)],
            scratch_shapes=[pltpu.VMEM((WIDTH, FSTEP), BF16), pltpu.VMEM((FSTEP, WIDTH), BF16)],
        ),
        out_shape=[jax.ShapeDtypeStruct((ROWS, FF), BF16), jax.ShapeDtypeStruct((ROWS, FF), BF16)],
        compiler_params=params(VMEM),
        cost_estimate=pl.CostEstimate(
            flops=4 * ROWS * WIDTH * FF, bytes_accessed=6 * ROWS * WIDTH + 4 * ROWS * FF, transcendentals=ROWS * FF
        ),
        name="units",
    )(sc, normed.reshape(ROWS, WIDTH), cotangent.reshape(ROWS, WIDTH), *up, *down)


def down_grad_kernel(sc, active, cot, own, far, total):
    total[...] = dot(active[...], cot[...], 0, 0).astype(BF16)
    own[...] = total[:, own_lanes(sc)]
    far[...] = total[:, far_lanes(sc)]


def run_down_grad(sc, active, cotangent):
    return pl.pallas_call(
        down_grad_kernel,
        grid_spec=pltpu.PrefetchScalarGridSpec(
            num_scalar_prefetch=1,
            grid=(FF // 512,),
            in_specs=[spec((ROWS, 512), lambda f, s: (0, f)), held((ROWS, WIDTH))],
            out_specs=[spec((512, SIDE), lambda f, s: (f, 0))] * 2,
            scratch_shapes=[pltpu.VMEM((512, WIDTH), BF16)],
        ),
        out_shape=[jax.ShapeDtypeStruct((FF, SIDE), BF16)] * 2,
        compiler_params=params(57 << 20),
        cost_estimate=pl.CostEstimate(
            flops=2 * ROWS * WIDTH * FF, bytes_accessed=2 * ROWS * (WIDTH + FF), transcendentals=0
        ),
        name="down_grad",
    )(sc, active, cotangent.reshape(ROWS, WIDTH))


def up_grad_kernel(sc, normed, up_grad, own, far):
    total = dot(normed[...], up_grad[...], 0, 0).astype(BF16)

    @pl.when(pl.program_id(0) < 3)
    def _():
        own[...] = total

    @pl.when(pl.program_id(0) >= 3)
    def _():
        far[...] = total


def run_up_grad(sc, normed, up_grad):
    return pl.pallas_call(
        up_grad_kernel,
        grid_spec=pltpu.PrefetchScalarGridSpec(
            num_scalar_prefetch=1,
            grid=(6,),
            in_specs=[held((ROWS, WIDTH)), spec((ROWS, 512), lambda f, s: (0, lax.rem(3 * s[CORE] + f, 6)))],
            out_specs=[
                spec((WIDTH, 512), lambda f, s: (0, lax.min(f, 2))),
                spec((WIDTH, 512), lambda f, s: (0, lax.max(f - 3, 0))),
            ],
        ),
        out_shape=[jax.ShapeDtypeStruct((WIDTH, FF // 2), BF16)] * 2,
        compiler_params=params(57 << 20),
        cost_estimate=pl.CostEstimate(
            flops=2 * ROWS * WIDTH * FF, bytes_accessed=2 * ROWS * (WIDTH + FF), transcendentals=0
        ),
        name="up_grad",
    )(sc, normed.reshape(ROWS, WIDTH), up_grad)


def out_grad_kernel(sc, mixed, res_own, res_far, own, far, total):
    step = pl.program_id(0)
    grad = jnp.concatenate([res_own[...], res_far[...]], axis=0).reshape(4 * SPAN, WIDTH)
    found = dot(mixed[...].reshape(4 * SPAN, WIDTH), grad, 0, 0)

    @pl.when(step == 0)
    def _():
        total[...] = found

    @pl.when(step > 0)
    def _():
        total[...] += found

    @pl.when(step == pl.num_programs(0) - 1)
    def _():
        own[...] = total[:, own_lanes(sc)].astype(BF16)
        far[...] = total[:, far_lanes(sc)].astype(BF16)


def run_out_grad(sc, mixed, res_own, res_far):
    return pl.pallas_call(
        out_grad_kernel,
        grid_spec=pltpu.PrefetchScalarGridSpec(
            num_scalar_prefetch=1,
            grid=(HROWS // SPAN,),
            in_specs=[slab_spec(), slab_spec(2), slab_spec(2)],
            out_specs=[held((WIDTH, SIDE))] * 2,
            scratch_shapes=[pltpu.VMEM((WIDTH, WIDTH), F32)],
        ),
        out_shape=[jax.ShapeDtypeStruct((WIDTH, SIDE), BF16)] * 2,
        compiler_params=params(LESS),
        cost_estimate=pl.CostEstimate(
            flops=2 * ROWS * WIDTH * WIDTH, bytes_accessed=4 * ROWS * WIDTH, transcendentals=0
        ),
        name="out_grad",
    )(sc, mixed, res_own, res_far)


def out_kernel(sc, active, resid, dn_own, dn_far, own, far, w_down):
    step = pl.program_id(0)

    @pl.when(step == 0)
    def _():
        w_down[:, own_lanes(sc)] = dn_own[...]
        w_down[:, far_lanes(sc)] = dn_far[...]

    branch = dot(active[...].reshape(4 * SPAN, FF), w_down[...], 1, 0)
    output = jnp.where(row_valid(sc, step), resid[...].reshape(4 * SPAN, WIDTH).astype(F32) + branch, 0.0)
    output = output.astype(BF16).reshape(4, SPAN, WIDTH)
    own[...] = output[:2]
    far[...] = output[2:]


def run_out(sc, active, resid, down):
    return pl.pallas_call(
        out_kernel,
        grid_spec=pltpu.PrefetchScalarGridSpec(
            num_scalar_prefetch=1,
            grid=(HROWS // SPAN,),
            in_specs=[
                spec((4, SPAN, FF), lambda r, s: (0, r, 0)),
                slab_spec(),
                held((FF, SIDE)),
                held((FF, SIDE)),
            ],
            out_specs=[slab_spec(2)] * 2,
            scratch_shapes=[pltpu.VMEM((FF, WIDTH), BF16)],
        ),
        out_shape=[
            jax.ShapeDtypeStruct((2, HROWS, WIDTH), BF16),
            jax.ShapeDtypeStruct((2, HROWS, WIDTH), BF16),
        ],
        compiler_params=params(LESS),
        cost_estimate=pl.CostEstimate(
            flops=2 * ROWS * WIDTH * FF, bytes_accessed=ROWS * (2 * FF + 7 * WIDTH), transcendentals=0
        ),
        name="out",
    )(sc, active.reshape(4, HROWS, FF), resid, *down)


def post_kernel(sc, resid, grad_own, grad_far, cot, up_own, up_far, wo_own, wo_far, gain, *refs):
    (res_own, res_far, heads, d_gain, weight, spread) = refs
    step = pl.program_id(0)
    whole_weight(sc, step, wo_own, wo_far, weight)
    shape, slab = (4 * SPAN, WIDTH), (4, SPAN, WIDTH)
    valid = row_valid(sc, step)
    res = resid[...].reshape(shape).astype(F32)
    scale = lax.rsqrt(jnp.mean(res * res, axis=-1, keepdims=True) + EPSILON)
    unit = res * scale
    units = (4 * SPAN, FF // 2)
    back = dot(grad_own[...].reshape(units), up_own[...], 1, 1) + dot(grad_far[...].reshape(units), up_far[...], 1, 1)
    two_grad = jnp.where(valid, back, 0.0)
    gained = two_grad * gain[...]
    masked = cot[...].reshape(shape).astype(F32)
    grad = masked + scale * (gained - unit * jnp.mean(gained * unit, axis=-1, keepdims=True))
    low = grad.astype(BF16)
    res_own[...] = low.reshape(slab)[:2]
    res_far[...] = low.reshape(slab)[2:]
    gain_sum = jnp.sum(two_grad * unit, axis=0, keepdims=True)

    @pl.when(step == 0)
    def _():
        d_gain[...] = gain_sum

    @pl.when(step > 0)
    def _():
        d_gain[...] += gain_sum

    spread[...] = dot(low, weight[...], 1, 1).astype(BF16).reshape(slab)
    for pair in range(HEADS // 2):
        lanes = slice(pair * 128, (pair + 1) * 128)
        for side in range(2):
            one, two = spread[2 * side, :, lanes], spread[2 * side + 1, :, lanes]
            half = slice(side * 128, (side + 1) * 128)
            heads[2 * pair, :, half] = jnp.concatenate([one[:, :HEAD], two[:, :HEAD]], axis=1)
            heads[2 * pair + 1, :, half] = jnp.concatenate([one[:, HEAD:], two[:, HEAD:]], axis=1)


def run_post(sc, resid, up_grad, cotangent, up, wo, gain):
    side = lambda which: spec((4, SPAN, FF // 2), lambda r, s: (0, r, s[CORE] if which == 0 else 1 - s[CORE]))
    up_grad = up_grad.reshape(4, HROWS, FF)
    return pl.pallas_call(
        post_kernel,
        grid_spec=pltpu.PrefetchScalarGridSpec(
            num_scalar_prefetch=1,
            grid=(HROWS // SPAN,),
            in_specs=[
                slab_spec(),
                side(0),
                side(1),
                slab_spec(),
                held((WIDTH, FF // 2)),
                held((WIDTH, FF // 2)),
                held((WIDTH, SIDE)),
                held((WIDTH, SIDE)),
                held((1, WIDTH)),
            ],
            out_specs=[slab_spec(2)] * 2 + [heads_spec(), held((1, WIDTH))],
            scratch_shapes=[
                pltpu.VMEM((WIDTH, WIDTH), BF16),
                pltpu.VMEM((4, SPAN, WIDTH), BF16),
            ],
        ),
        out_shape=[
            jax.ShapeDtypeStruct((2, HROWS, WIDTH), BF16),
            jax.ShapeDtypeStruct((2, HROWS, WIDTH), BF16),
            jax.ShapeDtypeStruct((HEADS, HROWS, 4 * HEAD), BF16),
            jax.ShapeDtypeStruct((1, WIDTH), F32),
        ],
        compiler_params=params(VMEM),
        cost_estimate=pl.CostEstimate(
            flops=2 * ROWS * WIDTH * (WIDTH + FF), bytes_accessed=ROWS * (16 * WIDTH + 2 * FF), transcendentals=0
        ),
        name="post",
    )(sc, resid, up_grad, up_grad, cotangent, *up, *wo, gain)


def unmix_kernel(count, carried, sc, v_own, v_far, grad_heads, mean, exps, inverse, *refs):
    refs = refs[2:] if carried else refs
    outs, (own, far, grads, mask, adder, bound, out_sems) = refs[: 4 * count], refs[4 * count :]
    place = sc[PLACE]
    step = pl.program_id(0)

    def leave(slot):
        return [
            pltpu.make_async_copy(
                grads.at[slot, pl.ds(pl.multiple_of((place ^ rel) * SUBS * HALF, SUBS * HALF), SUBS * HALF)],
                outs[4 * slot + rel],
                out_sems.at[slot, rel],
            )
            for rel in range(4)
        ]

    fill_mask(sc, mask)

    @pl.when(step == 0)
    def _():
        lane = lax.broadcasted_iota(jnp.int32, (4 * HEAD, 128), 0) // HEAD
        column = lax.broadcasted_iota(jnp.int32, (4 * HEAD, 128), 1)
        adder[...] = jnp.where((lane == column) | (lane + 4 == column), -1.0, 0.0).astype(BF16)
        row = lax.broadcasted_iota(jnp.int32, (LMAX, 128), 0)
        item = lax.broadcasted_iota(jnp.int32, (LMAX, 128), 1)
        length = jnp.where(item % 4 == 0, sc[LENGTHS], sc[LENGTHS + 1])
        length = jnp.where(item % 4 == 2, sc[LENGTHS + 2], length)
        length = jnp.where(item % 4 == 3, sc[LENGTHS + 3], length)
        bound[...] = jnp.where((item < 8) & (row < length), 1.0, 0.0).astype(BF16)

    high_lanes = lax.broadcasted_iota(jnp.int32, (HROWS, 128), 1) < 4
    for head in range(PHEADS):
        weights = exps[head]
        low = (grad_heads[head].astype(F32) * inverse[head].astype(F32)).astype(BF16)
        product = low.astype(F32) * mean[head]
        coarse = product.astype(BF16)
        fine = (product - coarse.astype(F32)).astype(BF16)
        delta = dot(coarse, adder[...], 1, 0) + dot(fine, adder[...], 1, 0)
        coarse = delta.astype(BF16)
        fine = (delta - coarse.astype(F32)).astype(BF16)
        left = jnp.concatenate([low, jnp.where(high_lanes, coarse, fine)], axis=1)
        score = dot(left, jnp.concatenate([v_own[head], v_far[head], bound[...]], axis=1), 1, 1)
        grads[step, head_rows(head)] = (score * weights.astype(F32)).astype(BF16)
        back = (dot(weights, low, 0, 0) * mask[...].astype(F32)).astype(BF16)
        own[head] = back[:, : 2 * HEAD]
        far[head] = back[:, 2 * HEAD :]
    for which in range(count):

        @pl.when(step == which)
        def _():
            for copy in leave(which):
                copy.start()
            if which == count - 1:
                for slot in range(count):
                    for copy in leave(slot):
                        copy.wait()


def run_unmix(sc, planes, v_own, v_far, grad_heads, mean, exps, inverse, carry):
    carry, count = list(carry), len(planes)
    return pl.pallas_call(
        partial(unmix_kernel, count, bool(carry)),
        grid_spec=pltpu.PrefetchScalarGridSpec(
            num_scalar_prefetch=1,
            grid=(count,),
            in_specs=[
                plane_spec(planes, LMAX, 2 * HEAD),
                plane_spec(planes, LMAX, 2 * HEAD),
                plane_spec(planes, HROWS, 4 * HEAD),
                plane_spec(planes, HROWS, 4 * HEAD),
                plane_spec(planes, HROWS, LMAX),
                plane_spec(planes, HROWS, 4 * HEAD),
            ]
            + anywhere(len(carry)),
            out_specs=anywhere(4 * count) + [plane_spec(planes, LMAX, 2 * HEAD)] * 2,
            scratch_shapes=[
                pltpu.VMEM((count, 4 * SUBS * HALF, LMAX), BF16),
                pltpu.VMEM((LMAX, 4 * HEAD), BF16),
                pltpu.VMEM((4 * HEAD, 128), BF16),
                pltpu.VMEM((LMAX, 128), BF16),
                pltpu.SemaphoreType.DMA((count, 4)),
            ],
        ),
        out_shape=[jax.ShapeDtypeStruct((SUBS * HALF, LMAX), BF16)] * (4 * count)
        + [jax.ShapeDtypeStruct((HEADS, LMAX, 2 * HEAD), BF16)] * 2,
        input_output_aliases={7 + i: 4 * count + i for i in range(len(carry))},
        compiler_params=params(VMEM),
        cost_estimate=pl.CostEstimate(
            flops=3 * HEADS * HROWS * LMAX * 4 * HEAD,
            bytes_accessed=HEADS * (2 * HROWS * LMAX + 5 * HROWS * 256 + 4 * LMAX * 256),
            transcendentals=0,
        ),
        name="unmix",
    )(sc, v_own, v_far, grad_heads, mean, exps, inverse, *carry)


def close_kernel(sc, tok, res_own, res_got, out_own, out_got, own, far, gain, w_own, w_far, *refs):
    (output, tok_grad, d_value, d_gain, total, weight) = refs
    step = pl.program_id(0)
    whole_weight(sc, step, w_own, w_far, weight)
    core = sc[CORE]
    output[:, :, core] = out_own[...].astype(F32)
    output[:, :, 1 - core] = out_got[...].astype(F32)
    tok_grad[:, :, core] = res_own[...].astype(F32)
    tok_grad[:, :, 1 - core] = res_got[...].astype(F32)
    runs = tok.shape[1]
    rows = runs * 128
    for item in range(2):
        lanes = slice(item * HEAD, (item + 1) * HEAD)
        pieces = [
            add_low(own[head, :, lanes], far[head, :, lanes]) for head in range(HEADS)
        ]
        back = jnp.concatenate(pieces, axis=1)
        x = tok[item].reshape(rows, WIDTH).astype(F32)
        scale = lax.rsqrt(jnp.mean(x * x, axis=-1, keepdims=True) + EPSILON)
        unit = x * scale
        normed = (unit * gain[...]).astype(BF16)
        normed_grad = dot(back, weight[...], 1, 1)
        gained = normed_grad * gain[...]
        update = scale * (gained - unit * jnp.mean(gained * unit, axis=-1, keepdims=True))
        tok_grad[item] += update.reshape(runs, 2, HALF, WIDTH)
        gain_sum = jnp.sum(normed_grad * unit, axis=0, keepdims=True)
        value_sum = dot(normed, back, 0, 0)
        if item == 0:
            gain_total, value_total = gain_sum, value_sum
        else:
            gain_total, value_total = gain_total + gain_sum, value_total + value_sum

    @pl.when(step == 0)
    def _():
        d_gain[...] = gain_total
        total[...] = value_total

    @pl.when(step > 0)
    def _():
        d_gain[...] += gain_total
        total[...] += value_total

    @pl.when(step == pl.num_programs(0) - 1)
    def _():
        low = total[...].astype(BF16)
        d_value[0] = low[:, :SIDE]
        d_value[1] = low[:, SIDE:]


def run_close(sc, tokens, res_own, res_got, out_own, out_got, own, far, gain, w_own, w_far):
    runs = 2
    slab = (2, RUNS, 2, HALF, WIDTH)
    half = (2, RUNS, HALF, WIDTH)
    whole_spec = spec((2, runs, 2, HALF, WIDTH), lambda j, s: (0, j, 0, 0, 0))
    half_spec = spec((2, runs, HALF, WIDTH), lambda j, s: (0, j, 0, 0))
    back_spec = spec((HEADS, runs * 128, 2 * HEAD), lambda j, s: (0, j, 0))
    return pl.pallas_call(
        close_kernel,
        grid_spec=pltpu.PrefetchScalarGridSpec(
            num_scalar_prefetch=1,
            grid=(RUNS // runs,),
            in_specs=[whole_spec]
            + [half_spec] * 4
            + [back_spec, back_spec, held((1, WIDTH)), held((WIDTH, SIDE)), held((WIDTH, SIDE))],
            out_specs=[whole_spec, whole_spec, held((2, WIDTH, SIDE)), held((1, WIDTH))],
            scratch_shapes=[pltpu.VMEM((WIDTH, WIDTH), F32), pltpu.VMEM((WIDTH, WIDTH), BF16)],
        ),
        out_shape=[
            jax.ShapeDtypeStruct(slab, F32),
            jax.ShapeDtypeStruct(slab, F32),
            jax.ShapeDtypeStruct((2, WIDTH, SIDE), BF16),
            jax.ShapeDtypeStruct((1, WIDTH), F32),
        ],
        compiler_params=params(LESS),
        cost_estimate=pl.CostEstimate(
            flops=4 * 2 * LMAX * WIDTH * WIDTH, bytes_accessed=38 * LMAX * WIDTH, transcendentals=0
        ),
        name="close",
    )(
        sc,
        tokens.reshape(slab),
        *(x.reshape(half) for x in (res_own, res_got, out_own, out_got)),
        own,
        far,
        gain,
        w_own,
        w_far,
    )


PACK_DOWN, PACK_UP, PACK_OUT, PACK_VALUE, PACK_GAIN, PACK = 0, 192, 384, 432, 480, 496


def pack_kernel(sc, down, up, out, value, gain, down_far, up_far, out_far, value_far, gain_far, packed):
    first = sc[CORE] == 0

    def both(own, far, lanes):
        own, far = own[:, lanes], far[:, lanes]
        return jnp.concatenate([jnp.where(first, own, far), jnp.where(first, far, own)], axis=0)

    def side(own, far):
        return both(own, far, own_lanes(sc))

    packed[PACK_DOWN:PACK_UP] = side(down, down_far)
    for j in range(4):
        lanes = pl.ds(pl.multiple_of((4 * sc[CORE] + j) * SIDE, 128), SIDE)
        packed[PACK_UP + 48 * j : PACK_UP + 48 * (j + 1)] = both(up, up_far, lanes)
    packed[PACK_OUT:PACK_VALUE] = side(out, out_far)
    packed[PACK_VALUE:PACK_GAIN] = side(value, value_far)
    packed[PACK_GAIN:] = both(gain, gain_far, slice(0, SIDE))


def run_pack(sc, own, far):
    return pl.pallas_call(
        pack_kernel,
        grid_spec=pltpu.PrefetchScalarGridSpec(
            num_scalar_prefetch=1,
            grid=(1,),
            in_specs=[held(x.shape) for x in (*own, *far)],
            out_specs=held((PACK, SIDE)),
        ),
        out_shape=jax.ShapeDtypeStruct((PACK, SIDE), BF16),
        compiler_params=params(VMEM),
        cost_estimate=pl.CostEstimate(flops=0, bytes_accessed=6 * PACK * SIDE, transcendentals=0),
        name="pack",
    )(sc, *own, *far)


def chip_of(sc, k, rel):
    return plane_of(k, sc) * 4 + (sc[PLACE] ^ rel)


def place_kernel(moves, sc, *refs):
    pieces, targets, sems = refs[:16], refs[16:-1], refs[-1]
    copies = []
    for index, piece in enumerate(pieces):
        chip = chip_of(sc, index // 4, index % 4)
        for which, (start, count, lane, target, step, offset, column) in enumerate(moves):
            rows = pl.ds(pl.multiple_of(chip * step + offset, 16), count)
            copies.append(
                pltpu.make_async_copy(
                    piece.at[pl.ds(start, count), pl.ds(lane, SIDE)],
                    targets[target].at[rows, pl.ds(column, SIDE)],
                    sems.at[index, which],
                )
            )
    for copy in copies:
        copy.start()
    for copy in copies:
        copy.wait()


def run_place(sc, pieces, moves, shapes):
    return pl.pallas_call(
        partial(place_kernel, moves),
        grid_spec=pltpu.PrefetchScalarGridSpec(
            num_scalar_prefetch=1,
            grid=(1,),
            in_specs=anywhere(16),
            out_specs=[held(shape) for shape in shapes],
            scratch_shapes=[pltpu.SemaphoreType.DMA((16, len(moves)))],
        ),
        out_shape=[jax.ShapeDtypeStruct(shape, BF16) for shape in shapes],
        compiler_params=params(VMEM),
        cost_estimate=pl.CostEstimate(
            flops=0, bytes_accessed=4 * sum(a * b for a, b in shapes), transcendentals=0
        ),
        name="place",
    )(sc, *pieces)


def place_weights(sc, pieces):
    moves = (
        (PACK_DOWN, 192, 0, 0, 192, 0, 0),
        *((PACK_UP + 48 * j, 48, 0, 1, 48, 0, j * SIDE) for j in range(4)),
        (PACK_OUT, 48, 0, 2, 48, 0, 0),
        (PACK_VALUE, 48, 0, 3, 48, 0, 0),
        (PACK_GAIN, 16, 0, 4, 16, 0, 0),
    )
    shapes = [(FF, SIDE), (WIDTH, FF // 2), (WIDTH, SIDE), (WIDTH, SIDE), (256, SIDE)]
    return run_place(sc, pieces, moves, shapes)


def collect_kernel(sc, *refs):
    outs = refs[24:]
    for k in range(PLANES):

        @pl.when(pl.program_id(0) == k)
        def _():
            for rel in range(4):
                down, down_got, up, up_got, out, out_got = refs[6 * rel : 6 * rel + 6]
                packed = outs[4 * k + rel]
                packed[PACK_DOWN:PACK_UP] = add_low(down[...], down_got[...])
                for j in range(4):
                    lanes = slice(j * SIDE, (j + 1) * SIDE)
                    packed[PACK_UP + 48 * j : PACK_UP + 48 * (j + 1)] = add_low(up[:, lanes], up_got[:, lanes])
                packed[PACK_OUT:PACK_VALUE] = add_low(out[...], out_got[...])


def run_collect(sc, *sides):
    def rows(x, rel):
        return spec((x.shape[0] // 16, x.shape[1]), lambda k, s: (chip_of(s, k, rel), 0))

    return pl.pallas_call(
        collect_kernel,
        grid_spec=pltpu.PrefetchScalarGridSpec(
            num_scalar_prefetch=1,
            grid=(PLANES,),
            in_specs=[rows(x, rel) for rel in range(4) for x in sides],
            out_specs=[held((PACK_VALUE, SIDE))] * 16,
        ),
        out_shape=[jax.ShapeDtypeStruct((PACK_VALUE, SIDE), BF16)] * 16,
        compiler_params=params(LESS),
        cost_estimate=pl.CostEstimate(flops=0, bytes_accessed=3 * 16 * PACK_VALUE * SIDE * 2, transcendentals=0),
        name="collect",
    )(sc, *(x for _ in range(4) for x in sides))


def add_kernel(groups, *refs):
    for group, total in zip(groups, refs[-len(groups) :]):
        value = refs[group[0]][...].astype(F32)
        for index in group[1:]:
            value = value + refs[index][...].astype(F32)
        total[...] = value.astype(total.dtype)


def run_add(groups, values, dtype):
    shape = values[0].shape
    here = pl.BlockSpec(memory_space=pltpu.VMEM)
    return pl.pallas_call(
        partial(add_kernel, groups),
        in_specs=[here] * len(values),
        out_specs=[here] * len(groups),
        out_shape=[jax.ShapeDtypeStruct(shape, dtype)] * len(groups),
        compiler_params=params(LESS),
        cost_estimate=pl.CostEstimate(
            flops=0, bytes_accessed=2 * shape[0] * shape[1] * (len(values) + len(groups)), transcendentals=0
        ),
        name="add",
    )(*values)


DEVICES = 32
TO_CORE, TO_X, TO_Y = 1, 2, 4


def swap(x, bit):
    return lax.ppermute(x, BOTH, [(d, d ^ bit) for d in range(DEVICES)])


def ring(x, way=1):
    return lax.ppermute(x, BOTH, [(d, (d + 8 * way) % DEVICES) for d in range(DEVICES)])


def pick(x, index, axis=0):
    return lax.dynamic_index_in_dim(x, index, axis, keepdims=False)


def ordered(flag, one, two, axis=0, joined=jnp.stack):
    return jnp.where(flag == 0, joined([one, two], axis), joined([two, one], axis))


def add_low(one, two):
    return (one.astype(F32) + two.astype(F32)).astype(BF16)


STEPS = (
    ((0, 0, 1), (0, 1, 0), (1, 0, 0)),
    ((1, 0, 1), (0, 1, 1), (2, 0, 0)),
    ((2, 0, 1), (1, 1, 0), (3, 0, 0)),
    ((1, 1, 1), (2, 1, 1), (2, 1, 0)),
    ((3, 0, 1), (3, 1, 0), (3, 1, 1)),
)


def gather_step(have, step):
    by_x, by_y, by_z = STEPS[step]
    return {
        **have,
        by_z: ring(have[by_z[0] - 1, by_z[1], by_z[2]]),
        by_x: swap(have[by_x[0], by_x[1], 0], TO_X),
        by_y: swap(have[by_y[0], 0, by_y[2]], TO_Y),
    }


def in_order(have):
    return [have[k, y, x] for k in range(4) for y in range(2) for x in range(2)]


def by_place(shares, planes=range(PLANES)):
    return {(k, i // 2, i % 2): shares[4 * at + i] for at, k in enumerate(planes) for i in range(4)}


def scatter_send(have, step):
    by_x, by_y, by_z = STEPS[len(STEPS) - 1 - step]
    got = (ring(have[by_z], -1), swap(have[by_x], TO_X), swap(have[by_y], TO_Y))
    return {at: value for at, value in have.items() if at not in (by_x, by_y, by_z)}, got


def scatter_add(have, got, step):
    by_x, by_y, by_z = STEPS[len(STEPS) - 1 - step]
    targets = ((by_z[0] - 1, by_z[1], by_z[2]), (by_x[0], by_x[1], 0), (by_y[0], 0, by_y[2]))
    sums = list(dict.fromkeys(targets))
    groups = [(len(got) + i, *(j for j in range(len(got)) if targets[j] == at)) for i, at in enumerate(sums)]
    values = [*got, *(have[at] for at in sums)]
    dtype = F32 if step == len(STEPS) - 1 else BF16
    if values[0].shape[1] == LMAX:
        totals = run_add(groups, values, dtype)
    else:
        totals = [sum(values[i].astype(F32) for i in group).astype(dtype) for group in groups]
    return {**have, **dict(zip(sums, totals))}


together = lax.optimization_barrier


def chip_shards(tokens, lengths, rand_mix, w_value, w_out, w_up, w_down, gain_mix, gain_ffn, grad_out):
    wide = lax.axis_index("wide")
    core = lax.axis_index("narrow")
    z, y, x = wide // 4, (wide // 2) % 2, wide % 2
    other = lambda value: swap(value, TO_CORE)
    side = partial(ordered, core, joined=jnp.concatenate)
    slab = (2, RUNS, 2, HALF, WIDTH)
    tokens, grad_out = tokens.reshape(slab), grad_out.reshape(slab)

    gains = jnp.pad(jnp.concatenate([gain_mix, gain_ffn])[None], ((0, 7), (0, SIDE - 48)))
    own = (w_down, w_up, w_out, w_value, gains)
    far = tuple(other(value) for value in own)
    near_sc = jnp.concatenate([jnp.stack([core, z, wide % 4]).astype(jnp.int32), lengths, lengths])
    weights = {(0, 0, 0): run_pack(near_sc, own, far)}

    rand = rand_mix.reshape(3, 2, HALF, LMAX)
    blocks = side(pick(rand, core, 1), other(pick(rand, 1 - core, 1)), 0)
    weights, rands, late_tokens, late_grad = together(
        (gather_step(weights, 0), {(0, 0, 0): blocks.reshape(SUBS * HALF, LMAX)}, tokens, grad_out)
    )
    weights, tokens_far = together((gather_step(weights, 1), other(pick(late_tokens, 1 - core, 2))))
    weights, grad_far = together((gather_step(weights, 2), other(pick(late_grad, 1 - core, 2))))
    weights, far_lengths = together((gather_step(weights, 3), other(lengths)))
    sc = jnp.concatenate([near_sc[:5], far_lengths])
    weights, rands = together((gather_step(weights, 4), rands))

    rands = gather_step(rands, 0)
    down, up, out, value, gain_rows = place_weights(sc, in_order(weights))
    rands, value, value_far, gain_rows, out, down, up = together(
        (rands, value, other(value), gain_rows, out, down, up)
    )
    gain_rows = gain_rows.reshape(16, 2, 8, SIDE)[:, :, 0]
    gain_one = gain_rows[..., :24].reshape(1, WIDTH).astype(F32)
    gain_two = gain_rows[..., 24:48].reshape(1, WIDTH).astype(F32)
    rands = gather_step(rands, 1)
    v_own = run_values(sc, tokens.reshape(2, LMAX, WIDTH), gain_one, value, value_far)
    rands, v_own, out, down, up = together((rands, v_own, (out, other(out)), down, up))
    rands, v_own, v_far, grad_far, down, up = together(
        (gather_step(rands, 2), v_own, other(v_own), grad_far, down, up)
    )
    rands = gather_step(rands, 3)
    masked = run_masked(sc, grad_out, grad_far)
    rands, v_far, masked, down, up = together((rands, v_far, masked, down, up))
    near = [rands[k, y_at, x_at] for k in range(3) for y_at in range(2) for x_at in range(2)]
    rands = gather_step(rands, 4)
    mixing = run_mix(sc, (0, 1, 2), near, v_own, v_far, ())
    rands, down, up, mixing = together((rands, down, up, mixing))
    heads, mean, exps, inverse = run_mix(sc, (3,), in_order(rands)[12:], v_own, v_far, mixing)
    down, up = (down, other(down)), (up, other(up))

    mixed, resid, normed = run_pre(sc, tokens, tokens_far, heads, out, gain_two)
    active, up_grad = run_units(sc, normed, masked, up, down)
    res_own, res_far, grad_heads, d_gain_two = run_post(sc, resid, up_grad, masked, up, out, gain_two)

    backward = lambda planes, carry: run_unmix(sc, planes, v_own, v_far, grad_heads, mean, exps, inverse, carry)
    *far, back_own, back_far = backward((3,), ())
    far, back_own, back_far, res_got = together((far, back_own, back_far, other(res_far)))
    have, got = scatter_send(by_place(far, (3,)), 0)
    *near, back_own, back_far = backward((2, 1, 0), (back_own, back_far))
    have, got, near, back_own, back_far = together((have, got, near, back_own, back_far))
    have = scatter_add({**have, **by_place(near, (2, 1, 0))}, got, 0)

    have, got = scatter_send(have, 1)
    up_own, up_far = run_up_grad(sc, normed, up_grad)
    have, got, up_own, up_far, back_got = together((have, got, up_own, up_far, other(back_far)))
    have = scatter_add(have, got, 1)

    have, got = scatter_send(have, 2)
    down_own, down_far = run_down_grad(sc, active, masked)
    have, got, down_own, down_far, up_got = together((have, got, down_own, down_far, other(up_far)))
    have = scatter_add(have, got, 2)

    have, got = scatter_send(have, 3)
    d_out_own, d_out_far = run_out_grad(sc, mixed, res_own, res_far)
    packed = run_collect(sc, down_own, other(down_far), up_own, up_got, d_out_own, other(d_out_far))
    have, got, packed = together((have, got, packed))
    have = scatter_add(have, got, 3)

    have, got = scatter_send(have, 4)
    out_own, out_far = run_out(sc, active, resid, down)
    have, got, packed, out_own, out_far = together((have, got, packed, out_own, out_far))
    rand_sum = scatter_add(have, got, 4)[0, 0, 0].reshape(2, 3, HALF, LMAX)

    sums, got = scatter_send(by_place(packed), 0)
    output, tokens_grad, d_value, d_gain_one = run_close(
        sc, tokens, res_own, res_got, out_own, other(out_far), back_own, back_got, gain_one, value, value_far
    )
    gain_pair = jnp.concatenate([d_gain_one, d_gain_two]).reshape(2, 16, 1, 48).astype(BF16)
    gain_pair = jnp.pad(gain_pair, ((0, 0), (0, 0), (0, 15), (0, SIDE - 48)))
    small = jnp.concatenate([d_value.reshape(2, 16, 48, SIDE), gain_pair], 2)
    sums, got, output, tokens_grad, small = together((sums, got, output, tokens_grad, small))
    sums = scatter_add(sums, got, 0)

    sums, got = scatter_send(sums, 1)
    small = add_low(pick(small, core), other(pick(small, 1 - core))).reshape(4, 2, 2, 64, SIDE)
    sums, got, small = together((sums, got, small))
    sums = scatter_add(sums, got, 1)

    sums, got = scatter_send(sums, 2)
    small = add_low(pick(small, x, 2), swap(pick(small, 1 - x, 2), TO_X))
    sums, got, small = together((sums, got, small))
    sums = scatter_add(sums, got, 2)

    sums, got = scatter_send(sums, 3)
    small = add_low(pick(small, y, 1), swap(pick(small, 1 - y, 1), TO_Y))
    blocks, blocks_far = pick(rand_sum, core), other(pick(rand_sum, 1 - core))
    sums, got, small, blocks, blocks_far = together((sums, got, small, blocks, blocks_far))
    sums = scatter_add(sums, got, 3)

    sums, got = scatter_send(sums, 4)
    small_sum = pick(small, z).astype(F32)
    for k in range(1, PLANES):
        small_sum = small_sum + ring(pick(small, lax.rem(z + PLANES - k, PLANES)), -k).astype(F32)
    sums, got, small_sum = together((sums, got, small_sum))
    big_sum = scatter_add(sums, got, 4)[0, 0, 0]
    big_far, small_far = other(big_sum), other(small_sum)

    rows_of = lambda value, rows: pick(value.reshape(-1, 2, rows, SIDE), core, 1)
    mine = lambda own, far, rows: side(rows_of(own, rows)[0], rows_of(far, rows)[0], 1)
    down_shard = mine(big_sum[PACK_DOWN:PACK_UP], big_far[PACK_DOWN:PACK_UP], 96)
    up_side = lambda value: rows_of(value[PACK_UP:PACK_OUT], 24).transpose(1, 0, 2).reshape(24, 4 * SIDE)
    up_shard = side(up_side(big_sum), up_side(big_far), 1)
    outproj_shard = mine(big_sum[PACK_OUT:PACK_VALUE], big_far[PACK_OUT:PACK_VALUE], 24)
    value_shard = mine(small_sum[:48], small_far[:48], 24)
    gains_pair = ordered(core, small_sum[48, :48], small_far[48, :48])
    gain_pair = pick(gains_pair.reshape(2, 2, 24), core, 1)

    rand_shard = ordered(core, blocks, blocks_far, 1)

    return (
        output.reshape(2, LMAX, WIDTH),
        tokens_grad.reshape(2, LMAX, WIDTH),
        rand_shard.reshape(3 * 128, LMAX),
        value_shard,
        outproj_shard,
        up_shard,
        down_shard,
        gain_pair[0],
        gain_pair[1],
    )


def rms_norm(values, gain):
    scale = lax.rsqrt(jnp.mean(values * values, axis=-1, keepdims=True) + EPSILON)
    return values * scale * gain


def split_heads(block):
    return block.reshape(LMAX, HEADS, HEAD).transpose(1, 0, 2)


def merge_heads(block):
    return block.transpose(1, 0, 2).reshape(LMAX, HEADS * HEAD)


def masked_scores(key_mask, rand_head):
    return jnp.where(key_mask[None, :] > 0, rand_head.astype(jnp.float32), -1e30)


def head_forward(key_mask, paired):
    rand_head, value_head = paired
    scores = masked_scores(key_mask, rand_head)
    row_peak = jnp.max(scores, axis=-1, keepdims=True)
    exponent = jnp.exp(scores - row_peak)
    denom_sum = jnp.sum(exponent, axis=-1, keepdims=True)
    attention = exponent / denom_sum * key_mask[:, None]
    mixed = jnp.dot(attention.astype(jnp.bfloat16), value_head, preferred_element_type=jnp.float32)
    return (mixed.astype(jnp.bfloat16), row_peak + jnp.log(denom_sum))


def head_backward(key_mask, paired):
    rand_head, value_head, mix_grad, log_total = paired
    scores = masked_scores(key_mask, rand_head)
    attention = jnp.exp(scores - log_total) * key_mask[:, None]
    prob_grad = jnp.einsum("id,jd->ij", mix_grad, value_head, preferred_element_type=jnp.float32)
    value_grad = jnp.einsum(
        "ij,id->jd", attention.astype(jnp.bfloat16), mix_grad, preferred_element_type=jnp.float32
    )
    score_grad = attention * (prob_grad - jnp.sum(prob_grad * attention, axis=-1, keepdims=True))
    return (score_grad, value_grad)


def shards(tokens, lengths, rand_mix, w_value, w_out, w_up, w_down, gain_mix, gain_ffn, grad_out):
    item_count = tokens.shape[0]
    width = tokens.shape[2]
    row_count = item_count * LMAX
    tokens_flat = tokens.reshape(row_count, width).astype(jnp.float32)
    positions = jnp.arange(LMAX, dtype=jnp.int32)
    valid_table = (positions[None, :] < lengths[:, None]).astype(jnp.float32)
    row_valid = valid_table.reshape(row_count, 1)
    forward_set = (
        lax.all_gather(rand_mix, ("wide", "narrow"), axis=0, tiled=True),
        lax.all_gather(w_value, ("wide", "narrow"), axis=0, tiled=True),
        lax.all_gather(w_out, ("wide", "narrow"), axis=0, tiled=True),
        lax.all_gather(w_up, ("wide", "narrow"), axis=0, tiled=True),
        lax.all_gather(w_down, ("wide", "narrow"), axis=0, tiled=True),
        lax.all_gather(gain_mix, ("wide", "narrow"), axis=0, tiled=True),
        lax.all_gather(gain_ffn, ("wide", "narrow"), axis=0, tiled=True),
    )
    rand_all, value_all, out_all, up_all, down_all, gain_first, gain_second = forward_set
    normed = rms_norm(tokens_flat, gain_first.astype(jnp.float32)).astype(jnp.bfloat16)
    values = jnp.dot(normed, value_all, preferred_element_type=jnp.float32).astype(jnp.bfloat16)
    rand_heads = rand_all.reshape(HEADS, LMAX, LMAX)
    mixed_parts = []
    totals_kept = []
    for item_index in range(item_count):
        item_values = split_heads(values[item_index * LMAX : (item_index + 1) * LMAX])
        mixed_heads, log_total = lax.map(
            partial(head_forward, valid_table[item_index]), (rand_heads, item_values)
        )
        mixed_parts.append(merge_heads(mixed_heads))
        totals_kept.append(log_total)
    mixed = jnp.concatenate(mixed_parts, axis=0)
    residual = tokens_flat + jnp.dot(mixed, out_all, preferred_element_type=jnp.float32)
    normed_two = rms_norm(residual, gain_second.astype(jnp.float32)).astype(jnp.bfloat16)
    up_proj = jnp.dot(normed_two, up_all, preferred_element_type=jnp.float32)
    active = jax.nn.gelu(up_proj).astype(jnp.bfloat16)
    branch = jnp.dot(active, down_all, preferred_element_type=jnp.float32)
    output = row_valid * (residual + branch)
    back_set = (
        lax.all_gather(rand_mix, ("wide", "narrow"), axis=0, tiled=True),
        lax.all_gather(w_value, ("wide", "narrow"), axis=0, tiled=True),
        lax.all_gather(w_out, ("wide", "narrow"), axis=0, tiled=True),
        lax.all_gather(w_up, ("wide", "narrow"), axis=0, tiled=True),
        lax.all_gather(w_down, ("wide", "narrow"), axis=0, tiled=True),
        lax.all_gather(gain_mix, ("wide", "narrow"), axis=0, tiled=True),
        lax.all_gather(gain_ffn, ("wide", "narrow"), axis=0, tiled=True),
    )
    rand_back, value_back, out_back, up_back, down_back, gain_back_one, gain_back_two = back_set
    cotangent = grad_out.reshape(row_count, width).astype(jnp.float32)
    masked = row_valid * cotangent
    branch_grad = masked.astype(jnp.bfloat16)
    grad_down = jnp.einsum("rk,rd->kd", active, branch_grad, preferred_element_type=jnp.float32)
    active_grad = jnp.einsum(
        "rd,kd->rk", branch_grad, down_back, preferred_element_type=jnp.float32
    )
    gelu_value, gelu_pull = jax.vjp(jax.nn.gelu, up_proj)
    up_grad = gelu_pull(active_grad)[0].astype(jnp.bfloat16)
    grad_up = jnp.einsum("rd,rk->dk", normed_two, up_grad, preferred_element_type=jnp.float32)
    normed_two_grad = jnp.einsum("rk,dk->rd", up_grad, up_back, preferred_element_type=jnp.float32)
    norm_value, norm_pull = jax.vjp(rms_norm, residual, gain_back_two.astype(jnp.float32))
    residual_part, gain_two_grad = norm_pull(normed_two_grad)
    residual_grad = masked + residual_part
    attn_grad = residual_grad.astype(jnp.bfloat16)
    grad_outproj = jnp.einsum("rd,re->de", mixed, attn_grad, preferred_element_type=jnp.float32)
    mixed_grad = jnp.einsum(
        "re,de->rd", attn_grad, out_back, preferred_element_type=jnp.float32
    ).astype(jnp.bfloat16)
    rand_heads_back = rand_back.reshape(HEADS, LMAX, LMAX)
    rand_grad = jnp.zeros((HEADS, LMAX, LMAX), jnp.float32)
    value_parts = []
    for item_index in range(item_count):
        lower_row = item_index * LMAX
        upper_row = lower_row + LMAX
        item_values = split_heads(values[lower_row:upper_row])
        item_mix_grad = split_heads(mixed_grad[lower_row:upper_row])
        score_grad, value_grad = lax.map(
            partial(head_backward, valid_table[item_index]),
            (rand_heads_back, item_values, item_mix_grad, totals_kept[item_index]),
        )
        rand_grad = rand_grad + score_grad
        value_parts.append(merge_heads(value_grad))
    values_grad = jnp.concatenate(value_parts, axis=0).astype(jnp.bfloat16)
    grad_value = jnp.einsum("rd,re->de", normed, values_grad, preferred_element_type=jnp.float32)
    normed_grad = jnp.einsum(
        "re,de->rd", values_grad, value_back, preferred_element_type=jnp.float32
    )
    norm_first, first_pull = jax.vjp(rms_norm, tokens_flat, gain_back_one.astype(jnp.float32))
    token_part, gain_one_grad = first_pull(normed_grad)
    tokens_grad = residual_grad + token_part
    rand_flat = rand_grad.reshape(HEADS * LMAX, LMAX)
    all_shards = (
        lax.psum_scatter(rand_flat, ("wide", "narrow"), scatter_dimension=0, tiled=True),
        lax.psum_scatter(grad_value, ("wide", "narrow"), scatter_dimension=0, tiled=True),
        lax.psum_scatter(grad_outproj, ("wide", "narrow"), scatter_dimension=0, tiled=True),
        lax.psum_scatter(grad_up, ("wide", "narrow"), scatter_dimension=0, tiled=True),
        lax.psum_scatter(grad_down, ("wide", "narrow"), scatter_dimension=0, tiled=True),
        lax.psum_scatter(gain_one_grad, ("wide", "narrow"), scatter_dimension=0, tiled=True),
        lax.psum_scatter(gain_two_grad, ("wide", "narrow"), scatter_dimension=0, tiled=True),
    )
    rand_shard, value_shard, outproj_shard, up_shard, down_shard, gain_one_shard, gain_two_shard = (
        all_shards
    )
    return (
        output.reshape(item_count, LMAX, width),
        tokens_grad.reshape(item_count, LMAX, width),
        rand_shard,
        value_shard,
        outproj_shard,
        up_shard,
        down_shard,
        gain_one_shard,
        gain_two_shard,
    )


def solution(mesh):
    in_specs = (
        P(("wide", "narrow"), None, None),
        P(("wide", "narrow")),
        P(("wide", "narrow"), None),
        P(("wide", "narrow"), None),
        P(("wide", "narrow"), None),
        P(("wide", "narrow"), None),
        P(("wide", "narrow"), None),
        P(("wide", "narrow")),
        P(("wide", "narrow")),
        P(("wide", "narrow"), None, None),
    )
    out_specs = (
        P(("wide", "narrow"), None, None),
        P(("wide", "narrow"), None, None),
        P(("wide", "narrow"), None),
        P(("wide", "narrow"), None),
        P(("wide", "narrow"), None),
        P(("wide", "narrow"), None),
        P(("wide", "narrow"), None),
        P(("wide", "narrow")),
        P(("wide", "narrow")),
    )
    fits = dict(mesh.shape) == {"wide": 16, "narrow": 2}
    return jax.shard_map(chip_shards if fits else shards, mesh=mesh, in_specs=in_specs, out_specs=out_specs, check_vma=False)
```

```python
from functools import partial

import jax
import jax.numpy as jnp
from jax import lax
from jax.experimental import pallas as pl
from jax.experimental.pallas import tpu as pltpu
from jax.sharding import PartitionSpec as P

HEADS = 12
HEAD = 64
LMAX = 1024
WIDTH = 768
FF = 3072
EPSILON = 1e-05

BOTH = ("wide", "narrow")
BF16 = jnp.bfloat16
F32 = jnp.float32
VMEM = 61 << 20
LESS = 34 << 20

SUBS = 6
RUNS = 8
HALF = 64
HROWS = RUNS * HALF
PLANES = 4
PHEADS = HEADS // PLANES
ROWS = 2 * LMAX
FSTEP = 768
FSIDE = FF // 2 // FSTEP
TILE = 512
SIDE = WIDTH // 2
SPAN = 2 * HALF


def dot(a, b, ca, cb):
    return lax.dot_general(a, b, (((ca,), (cb,)), ((), ())), preferred_element_type=F32)


CORE, PLANE, PLACE, LENGTHS = 0, 1, 2, 3


def spec(shape, index):
    return pl.BlockSpec(shape, index)


def held(shape):
    zeros = (0,) * len(shape)
    return pl.BlockSpec(shape, lambda *_: zeros, pipeline_mode=pl.Buffered(1))


def params(limit):
    return pltpu.CompilerParams(vmem_limit_bytes=limit)


def whole_weight(sc, step, own, far, weight):
    @pl.when(step == 0)
    def _():
        weight[:, pl.ds(pl.multiple_of(sc[CORE] * SIDE, 128), SIDE)] = own[...]
        weight[:, pl.ds(pl.multiple_of((1 - sc[CORE]) * SIDE, 128), SIDE)] = far[...]


def values_kernel(sc, tok, gain, w_own, w_far, out, weight):
    step = pl.program_id(0)
    whole_weight(sc, step, w_own, w_far, weight)
    rows = tok.shape[1]
    position = step * rows + lax.broadcasted_iota(jnp.int32, (rows, 1), 0)
    for item in range(2):
        x = tok[item].astype(F32)
        scale = lax.rsqrt(jnp.mean(x * x, axis=-1, keepdims=True) + EPSILON)
        normed = (x * scale * gain[...]).astype(BF16)
        found = dot(normed, weight[...], 1, 0)
        found = jnp.where(position < sc[LENGTHS + item], found, 0.0).astype(BF16)
        for head in range(HEADS):
            out[head, :, item * HEAD : (item + 1) * HEAD] = found[:, head * HEAD : (head + 1) * HEAD]


def run_values(sc, tokens, gain, w_own, w_far):
    rows = 256
    return pl.pallas_call(
        values_kernel,
        grid_spec=pltpu.PrefetchScalarGridSpec(
            num_scalar_prefetch=1,
            grid=(LMAX // rows,),
            in_specs=[
                spec((2, rows, WIDTH), lambda j, s: (0, j, 0)),
                held((1, WIDTH)),
                held((WIDTH, SIDE)),
                held((WIDTH, SIDE)),
            ],
            out_specs=spec((HEADS, rows, 2 * HEAD), lambda j, s: (0, j, 0)),
            scratch_shapes=[pltpu.VMEM((WIDTH, WIDTH), BF16)],
        ),
        out_shape=jax.ShapeDtypeStruct((HEADS, LMAX, 2 * HEAD), BF16),
        compiler_params=params(VMEM),
        cost_estimate=pl.CostEstimate(
            flops=2 * 2 * LMAX * WIDTH * WIDTH, bytes_accessed=8 * LMAX * WIDTH, transcendentals=0
        ),
        name="values",
    )(sc, tokens, gain, w_own, w_far)


def lane_lengths(sc, shape):
    slot = lax.broadcasted_iota(jnp.int32, shape, 1) // HEAD
    length = jnp.where(slot == 0, sc[LENGTHS], sc[LENGTHS + 1])
    return jnp.where(slot >= 2, jnp.where(slot == 2, sc[LENGTHS + 2], sc[LENGTHS + 3]), length)


def plane_of(k, sc):
    return lax.rem(sc[PLANE] + PLANES - k, PLANES)


def plane_spec(planes, per, rows, lanes):
    parts = PHEADS // per

    def index(step, sc):
        k = planes[0] + step // parts * (planes[-1] - planes[0]) // max(len(planes) - 1, 1)
        return (plane_of(k, sc) * parts + step % parts, 0, 0)

    return spec((per, rows, lanes), index)


def anywhere(count):
    return [pl.BlockSpec(memory_space=pl.ANY)] * count


def plane_fetch(place, shards, raw, sems, slot):
    return [
        pltpu.make_async_copy(
            shards[4 * slot + rel],
            raw.at[slot, pl.ds(pl.multiple_of((place ^ rel) * SUBS * HALF, SUBS * HALF), SUBS * HALF)],
            sems.at[slot, rel],
        )
        for rel in range(4)
    ]


def take_plane(place, shards, raw, sems, parts):
    step = pl.program_id(0)
    count = len(shards) // 4

    @pl.when(step == 0)
    def _():
        for slot in range(count):
            for copy in plane_fetch(place, shards, raw, sems, slot):
                copy.start()

    for slot in range(count):

        @pl.when(step == slot * parts)
        def _():
            for copy in plane_fetch(place, shards, raw, sems, slot):
                copy.wait()

    return step // parts


def head_rows(per, head):
    if per == PHEADS:
        return pl.ds(head * HROWS, HROWS)
    first = pl.program_id(0) % (PHEADS // per) * per
    return pl.ds(pl.multiple_of((first + head) * HROWS, HROWS), HROWS)


def mix_kernel(count, per, carried, sc, *refs):
    shards, (v_own, v_far, mask, *rest) = refs[: 4 * count], refs[4 * count :]
    mixed, mean, exps, inverse, raw, sems = rest[4:] if carried else rest
    slot = take_plane(sc[PLACE], shards, raw, sems, PHEADS // per)
    shape = (HROWS, 4 * HEAD)
    line = lax.broadcasted_iota(jnp.int32, shape, 0)
    position = 128 * (line // HALF) + HALF * sc[CORE] + line % HALF
    valid = position < lane_lengths(sc, shape)
    for head in range(per):
        weights = jnp.exp(raw[slot, head_rows(per, head)].astype(F32)).astype(BF16)
        exps[head] = weights
        both = dot(weights, jnp.concatenate([v_own[head], v_far[head], mask[...]], axis=1), 1, 0)
        flip = jnp.where(valid, 1.0 / both[:, 4 * HEAD :], 0.0)
        found = both[:, : 4 * HEAD] * flip
        inverse[head] = flip.astype(BF16)
        mean[head] = found
        mixed[head] = found.astype(BF16)


def run_mix(sc, planes, shards, v_own, v_far, mask, carry):
    carry, count = list(carry), len(planes)
    per = 1 if count == 1 else PHEADS
    shape = (HEADS, HROWS, 4 * HEAD)
    return pl.pallas_call(
        partial(mix_kernel, count, per, bool(carry)),
        grid_spec=pltpu.PrefetchScalarGridSpec(
            num_scalar_prefetch=1,
            grid=(count * PHEADS // per,),
            in_specs=anywhere(4 * count) + [plane_spec(planes, per, LMAX, 2 * HEAD)] * 2
            + [held((LMAX, 4 * HEAD))]
            + anywhere(len(carry)),
            out_specs=[
                plane_spec(planes, per, HROWS, 4 * HEAD),
                plane_spec(planes, per, HROWS, 4 * HEAD),
                plane_spec(planes, per, HROWS, LMAX),
                plane_spec(planes, per, HROWS, 4 * HEAD),
            ],
            scratch_shapes=[
                pltpu.VMEM((count, 4 * SUBS * HALF, LMAX), BF16),
                pltpu.SemaphoreType.DMA((count, 4)),
            ],
        ),
        out_shape=[
            jax.ShapeDtypeStruct(shape, BF16),
            jax.ShapeDtypeStruct(shape, F32),
            jax.ShapeDtypeStruct((HEADS, HROWS, LMAX), BF16),
            jax.ShapeDtypeStruct(shape, BF16),
        ],
        input_output_aliases={4 + 4 * count + i: i for i in range(len(carry))},
        compiler_params=params(VMEM),
        cost_estimate=pl.CostEstimate(
            flops=2 * HEADS * HROWS * LMAX * 4 * HEAD,
            bytes_accessed=HEADS * (2 * HROWS * LMAX + 5 * HROWS * 256),
            transcendentals=HEADS * HROWS * LMAX // 2,
        ),
        name="mix",
    )(sc, *shards, v_own, v_far, mask, *carry)


def row_valid(sc, step):
    line = lax.broadcasted_iota(jnp.int32, (4 * SPAN, 1), 0)
    item = line // SPAN
    row = step * SPAN + line % SPAN
    low = jnp.where(item == 0, sc[LENGTHS], sc[LENGTHS + 1])
    high = jnp.where(item == 2, sc[LENGTHS + 2], sc[LENGTHS + 3])
    return 128 * (row // HALF) + HALF * sc[CORE] + row % HALF < jnp.where(item >= 2, high, low)


def four_items(own, far):
    return jnp.concatenate([own[:, :, 0], far[...]], axis=0).reshape(4 * SPAN, WIDTH)


def pre_kernel(sc, tok, tok_far, heads, wo_own, wo_far, gain, mixed, resid, normed, weight):
    step = pl.program_id(0)
    whole_weight(sc, step, wo_own, wo_far, weight)
    for item in range(4):
        lanes = slice(item * HEAD, (item + 1) * HEAD)
        for pair in range(HEADS // 2):
            both = jnp.concatenate([heads[2 * pair, :, lanes], heads[2 * pair + 1, :, lanes]], axis=1)
            mixed[item, :, pair * 128 : (pair + 1) * 128] = both
    res = four_items(tok, tok_far).astype(F32) + dot(mixed[...].reshape(4 * SPAN, WIDTH), weight[...], 1, 0)
    resid[...] = res.astype(BF16).reshape(4, SPAN, WIDTH)
    scale = lax.rsqrt(jnp.mean(res * res, axis=-1, keepdims=True) + EPSILON)
    valid = row_valid(sc, step)
    normed[...] = jnp.where(valid, res * scale * gain[...], 0.0).astype(BF16).reshape(4, SPAN, WIDTH)


def slab_spec(items=4):
    return spec((items, SPAN, WIDTH), lambda r, s: (0, r, 0))


def half_specs():
    return [
        spec((2, SPAN // HALF, 1, HALF, WIDTH), lambda r, s: (0, r, s[CORE], 0, 0)),
        spec((2, SPAN // HALF, HALF, WIDTH), lambda r, s: (0, r, 0, 0)),
    ]


def heads_spec():
    return spec((HEADS, SPAN, 4 * HEAD), lambda r, s: (0, r, 0))


def run_pre(sc, tokens, tokens_far, heads, wo, gain):
    return pl.pallas_call(
        pre_kernel,
        grid_spec=pltpu.PrefetchScalarGridSpec(
            num_scalar_prefetch=1,
            grid=(HROWS // SPAN,),
            in_specs=half_specs()
            + [heads_spec(), held((WIDTH, SIDE)), held((WIDTH, SIDE)), held((1, WIDTH))],
            out_specs=[slab_spec()] * 3,
            scratch_shapes=[pltpu.VMEM((WIDTH, WIDTH), BF16)],
        ),
        out_shape=[
            jax.ShapeDtypeStruct((4, HROWS, WIDTH), BF16),
            jax.ShapeDtypeStruct((4, HROWS, WIDTH), BF16),
            jax.ShapeDtypeStruct((4, HROWS, WIDTH), BF16),
        ],
        compiler_params=params(VMEM),
        cost_estimate=pl.CostEstimate(
            flops=2 * ROWS * WIDTH * WIDTH, bytes_accessed=16 * ROWS * WIDTH, transcendentals=0
        ),
        name="pre",
    )(sc, tokens, tokens_far, heads, *wo, gain)


def masked_kernel(sc, cot, cot_far, masked):
    value = jnp.where(row_valid(sc, pl.program_id(0)), four_items(cot, cot_far).astype(F32), 0.0)
    masked[...] = value.astype(BF16).reshape(4, SPAN, WIDTH)


def run_masked(sc, cotangent, cotangent_far):
    return pl.pallas_call(
        masked_kernel,
        grid_spec=pltpu.PrefetchScalarGridSpec(
            num_scalar_prefetch=1, grid=(HROWS // SPAN,), in_specs=half_specs(), out_specs=slab_spec()
        ),
        out_shape=jax.ShapeDtypeStruct((4, HROWS, WIDTH), BF16),
        compiler_params=params(VMEM),
        cost_estimate=pl.CostEstimate(flops=0, bytes_accessed=4 * ROWS * WIDTH, transcendentals=0),
        name="masked",
    )(sc, cotangent, cotangent_far)


def own_lanes(sc):
    return pl.ds(pl.multiple_of(sc[CORE] * SIDE, 128), SIDE)


def far_lanes(sc):
    return pl.ds(pl.multiple_of((1 - sc[CORE]) * SIDE, 128), SIDE)


def unit_rows(f, sc):
    return (lax.rem(FSIDE * sc[CORE] + f, 2 * FSIDE), 0)


def unit_columns(f, sc):
    return (0, lax.rem(FSIDE * sc[CORE] + f, 2 * FSIDE))


def early(f, sc):
    return (0, lax.min(f, FSIDE - 1))


def late(f, sc):
    return (0, lax.max(f - FSIDE, 0))


def units_kernel(sc, normed, cot, up_own, up_far, dn_own, dn_far, active, up_grad, w_up, w_down):
    step = pl.program_id(0)
    w_down[:, own_lanes(sc)] = dn_own[...]
    w_down[:, far_lanes(sc)] = dn_far[...]

    @pl.when(step < FSIDE)
    def _():
        w_up[...] = up_own[...]

    @pl.when(step >= FSIDE)
    def _():
        w_up[...] = up_far[...]

    for row in range(0, ROWS, 256):
        rows = slice(row, row + 256)
        for column in range(0, FSTEP, 256):
            columns = slice(column, column + 256)
            up = dot(normed[rows], w_up[:, columns], 1, 0)
            square = up * up
            bend = jnp.tanh(up * (0.7978845608028654 + (0.044715 * 0.7978845608028654) * square))
            share = 0.5 + 0.5 * bend
            act = up * share
            active[rows, columns] = act.astype(BF16)
            slope = share + act * (1.0 - share) * (
                2 * 0.7978845608028654 + (6 * 0.044715 * 0.7978845608028654) * square
            )
            up_grad[rows, columns] = (dot(cot[rows], w_down[columns], 1, 1) * slope).astype(BF16)


def run_units(sc, normed, cotangent, up, down):
    return pl.pallas_call(
        units_kernel,
        grid_spec=pltpu.PrefetchScalarGridSpec(
            num_scalar_prefetch=1,
            grid=(2 * FSIDE,),
            in_specs=[
                held((ROWS, WIDTH)),
                held((ROWS, WIDTH)),
                spec((WIDTH, FSTEP), early),
                spec((WIDTH, FSTEP), late),
                spec((FSTEP, SIDE), unit_rows),
                spec((FSTEP, SIDE), unit_rows),
            ],
            out_specs=[spec((ROWS, FSTEP), unit_columns), spec((ROWS, FSTEP), unit_columns)],
            scratch_shapes=[pltpu.VMEM((WIDTH, FSTEP), BF16), pltpu.VMEM((FSTEP, WIDTH), BF16)],
        ),
        out_shape=[jax.ShapeDtypeStruct((ROWS, FF), BF16), jax.ShapeDtypeStruct((ROWS, FF), BF16)],
        compiler_params=params(VMEM),
        cost_estimate=pl.CostEstimate(
            flops=4 * ROWS * WIDTH * FF, bytes_accessed=6 * ROWS * WIDTH + 4 * ROWS * FF, transcendentals=ROWS * FF
        ),
        name="units",
    )(sc, normed.reshape(ROWS, WIDTH), cotangent.reshape(ROWS, WIDTH), *up, *down)


def down_grad_kernel(sc, active, cot, own, far, total):
    total[...] = dot(active[...], cot[...], 0, 0).astype(BF16)
    own[...] = total[:, own_lanes(sc)]
    far[...] = total[:, far_lanes(sc)]


def run_down_grad(sc, active, cotangent):
    return pl.pallas_call(
        down_grad_kernel,
        grid_spec=pltpu.PrefetchScalarGridSpec(
            num_scalar_prefetch=1,
            grid=(FF // 512,),
            in_specs=[spec((ROWS, 512), lambda f, s: (0, f)), held((ROWS, WIDTH))],
            out_specs=[spec((512, SIDE), lambda f, s: (f, 0))] * 2,
            scratch_shapes=[pltpu.VMEM((512, WIDTH), BF16)],
        ),
        out_shape=[jax.ShapeDtypeStruct((FF, SIDE), BF16)] * 2,
        compiler_params=params(57 << 20),
        cost_estimate=pl.CostEstimate(
            flops=2 * ROWS * WIDTH * FF, bytes_accessed=2 * ROWS * (WIDTH + FF), transcendentals=0
        ),
        name="down_grad",
    )(sc, active, cotangent.reshape(ROWS, WIDTH))


def up_grad_kernel(sc, normed, up_grad, own, far):
    total = dot(normed[...], up_grad[...], 0, 0).astype(BF16)

    @pl.when(pl.program_id(0) < 3)
    def _():
        own[...] = total

    @pl.when(pl.program_id(0) >= 3)
    def _():
        far[...] = total


def run_up_grad(sc, normed, up_grad):
    return pl.pallas_call(
        up_grad_kernel,
        grid_spec=pltpu.PrefetchScalarGridSpec(
            num_scalar_prefetch=1,
            grid=(6,),
            in_specs=[held((ROWS, WIDTH)), spec((ROWS, 512), lambda f, s: (0, lax.rem(3 * s[CORE] + f, 6)))],
            out_specs=[
                spec((WIDTH, 512), lambda f, s: (0, lax.min(f, 2))),
                spec((WIDTH, 512), lambda f, s: (0, lax.max(f - 3, 0))),
            ],
        ),
        out_shape=[jax.ShapeDtypeStruct((WIDTH, FF // 2), BF16)] * 2,
        compiler_params=params(57 << 20),
        cost_estimate=pl.CostEstimate(
            flops=2 * ROWS * WIDTH * FF, bytes_accessed=2 * ROWS * (WIDTH + FF), transcendentals=0
        ),
        name="up_grad",
    )(sc, normed.reshape(ROWS, WIDTH), up_grad)


def out_grad_kernel(sc, mixed, res_own, res_far, own, far, total):
    step = pl.program_id(0)
    grad = jnp.concatenate([res_own[...], res_far[...]], axis=0).reshape(4 * SPAN, WIDTH)
    found = dot(mixed[...].reshape(4 * SPAN, WIDTH), grad, 0, 0)

    @pl.when(step == 0)
    def _():
        total[...] = found

    @pl.when(step > 0)
    def _():
        total[...] += found

    @pl.when(step == pl.num_programs(0) - 1)
    def _():
        own[...] = total[:, own_lanes(sc)].astype(BF16)
        far[...] = total[:, far_lanes(sc)].astype(BF16)


def run_out_grad(sc, mixed, res_own, res_far):
    return pl.pallas_call(
        out_grad_kernel,
        grid_spec=pltpu.PrefetchScalarGridSpec(
            num_scalar_prefetch=1,
            grid=(HROWS // SPAN,),
            in_specs=[slab_spec(), slab_spec(2), slab_spec(2)],
            out_specs=[held((WIDTH, SIDE))] * 2,
            scratch_shapes=[pltpu.VMEM((WIDTH, WIDTH), F32)],
        ),
        out_shape=[jax.ShapeDtypeStruct((WIDTH, SIDE), BF16)] * 2,
        compiler_params=params(LESS),
        cost_estimate=pl.CostEstimate(
            flops=2 * ROWS * WIDTH * WIDTH, bytes_accessed=4 * ROWS * WIDTH, transcendentals=0
        ),
        name="out_grad",
    )(sc, mixed, res_own, res_far)


def out_kernel(sc, active, resid, dn_own, dn_far, own, far, w_down):
    step = pl.program_id(0)

    @pl.when(step == 0)
    def _():
        w_down[:, own_lanes(sc)] = dn_own[...]
        w_down[:, far_lanes(sc)] = dn_far[...]

    branch = dot(active[...].reshape(4 * SPAN, FF), w_down[...], 1, 0)
    output = jnp.where(row_valid(sc, step), resid[...].reshape(4 * SPAN, WIDTH).astype(F32) + branch, 0.0)
    output = output.astype(BF16).reshape(4, SPAN, WIDTH)
    own[...] = output[:2]
    far[...] = output[2:]


def run_out(sc, active, resid, down):
    return pl.pallas_call(
        out_kernel,
        grid_spec=pltpu.PrefetchScalarGridSpec(
            num_scalar_prefetch=1,
            grid=(HROWS // SPAN,),
            in_specs=[
                spec((4, SPAN, FF), lambda r, s: (0, r, 0)),
                slab_spec(),
                held((FF, SIDE)),
                held((FF, SIDE)),
            ],
            out_specs=[slab_spec(2)] * 2,
            scratch_shapes=[pltpu.VMEM((FF, WIDTH), BF16)],
        ),
        out_shape=[
            jax.ShapeDtypeStruct((2, HROWS, WIDTH), BF16),
            jax.ShapeDtypeStruct((2, HROWS, WIDTH), BF16),
        ],
        compiler_params=params(LESS),
        cost_estimate=pl.CostEstimate(
            flops=2 * ROWS * WIDTH * FF, bytes_accessed=ROWS * (2 * FF + 7 * WIDTH), transcendentals=0
        ),
        name="out",
    )(sc, active.reshape(4, HROWS, FF), resid, *down)


def post_kernel(sc, resid, grad_own, grad_far, cot, up_own, up_far, wo_own, wo_far, gain, *refs):
    (res_own, res_far, heads, d_gain, weight, spread) = refs
    step = pl.program_id(0)
    whole_weight(sc, step, wo_own, wo_far, weight)
    shape, slab = (4 * SPAN, WIDTH), (4, SPAN, WIDTH)
    valid = row_valid(sc, step)
    res = resid[...].reshape(shape).astype(F32)
    scale = lax.rsqrt(jnp.mean(res * res, axis=-1, keepdims=True) + EPSILON)
    unit = res * scale
    units = (4 * SPAN, FF // 2)
    back = dot(grad_own[...].reshape(units), up_own[...], 1, 1) + dot(grad_far[...].reshape(units), up_far[...], 1, 1)
    two_grad = jnp.where(valid, back, 0.0)
    gained = two_grad * gain[...]
    masked = cot[...].reshape(shape).astype(F32)
    grad = masked + scale * (gained - unit * jnp.mean(gained * unit, axis=-1, keepdims=True))
    low = grad.astype(BF16)
    res_own[...] = low.reshape(slab)[:2]
    res_far[...] = low.reshape(slab)[2:]
    gain_sum = jnp.sum(two_grad * unit, axis=0, keepdims=True)

    @pl.when(step == 0)
    def _():
        d_gain[...] = gain_sum

    @pl.when(step > 0)
    def _():
        d_gain[...] += gain_sum

    spread[...] = dot(low, weight[...], 1, 1).astype(BF16).reshape(slab)
    for pair in range(HEADS // 2):
        lanes = slice(pair * 128, (pair + 1) * 128)
        for side in range(2):
            one, two = spread[2 * side, :, lanes], spread[2 * side + 1, :, lanes]
            half = slice(side * 128, (side + 1) * 128)
            heads[2 * pair, :, half] = jnp.concatenate([one[:, :HEAD], two[:, :HEAD]], axis=1)
            heads[2 * pair + 1, :, half] = jnp.concatenate([one[:, HEAD:], two[:, HEAD:]], axis=1)


def run_post(sc, resid, up_grad, cotangent, up, wo, gain):
    side = lambda which: spec((4, SPAN, FF // 2), lambda r, s: (0, r, s[CORE] if which == 0 else 1 - s[CORE]))
    up_grad = up_grad.reshape(4, HROWS, FF)
    return pl.pallas_call(
        post_kernel,
        grid_spec=pltpu.PrefetchScalarGridSpec(
            num_scalar_prefetch=1,
            grid=(HROWS // SPAN,),
            in_specs=[
                slab_spec(),
                side(0),
                side(1),
                slab_spec(),
                held((WIDTH, FF // 2)),
                held((WIDTH, FF // 2)),
                held((WIDTH, SIDE)),
                held((WIDTH, SIDE)),
                held((1, WIDTH)),
            ],
            out_specs=[slab_spec(2)] * 2 + [heads_spec(), held((1, WIDTH))],
            scratch_shapes=[
                pltpu.VMEM((WIDTH, WIDTH), BF16),
                pltpu.VMEM((4, SPAN, WIDTH), BF16),
            ],
        ),
        out_shape=[
            jax.ShapeDtypeStruct((2, HROWS, WIDTH), BF16),
            jax.ShapeDtypeStruct((2, HROWS, WIDTH), BF16),
            jax.ShapeDtypeStruct((HEADS, HROWS, 4 * HEAD), BF16),
            jax.ShapeDtypeStruct((1, WIDTH), F32),
        ],
        compiler_params=params(VMEM),
        cost_estimate=pl.CostEstimate(
            flops=2 * ROWS * WIDTH * (WIDTH + FF), bytes_accessed=ROWS * (16 * WIDTH + 2 * FF), transcendentals=0
        ),
        name="post",
    )(sc, resid, up_grad, up_grad, cotangent, *up, *wo, gain)


def unmix_kernel(count, per, carried, sc, v_own, v_far, grad_heads, mean, exps, inverse, mask, adder, bound, *refs):
    refs = refs[2:] if carried else refs
    outs, (own, far, grads, out_sems) = refs[: 4 * count], refs[4 * count :]
    place = sc[PLACE]
    step = pl.program_id(0)

    def leave(slot):
        return [
            pltpu.make_async_copy(
                grads.at[slot, pl.ds(pl.multiple_of((place ^ rel) * SUBS * HALF, SUBS * HALF), SUBS * HALF)],
                outs[4 * slot + rel],
                out_sems.at[slot, rel],
            )
            for rel in range(4)
        ]

    parts = PHEADS // per
    slot = step // parts
    high_lanes = lax.broadcasted_iota(jnp.int32, (HROWS, 128), 1) < 4
    for head in range(per):
        weights = exps[head]
        low = (grad_heads[head].astype(F32) * inverse[head].astype(F32)).astype(BF16)
        product = low.astype(F32) * mean[head]
        coarse = product.astype(BF16)
        fine = (product - coarse.astype(F32)).astype(BF16)
        delta = dot(coarse, adder[...], 1, 0) + dot(fine, adder[...], 1, 0)
        coarse = delta.astype(BF16)
        fine = (delta - coarse.astype(F32)).astype(BF16)
        left = jnp.concatenate([low, jnp.where(high_lanes, coarse, fine)], axis=1)
        score = dot(left, jnp.concatenate([v_own[head], v_far[head], bound[...]], axis=1), 1, 1)
        grads[slot, head_rows(per, head)] = (score * weights.astype(F32)).astype(BF16)
        back = (dot(weights, low, 0, 0) * mask[...].astype(F32)).astype(BF16)
        own[head] = back[:, : 2 * HEAD]
        far[head] = back[:, 2 * HEAD :]
    for which in range(count):

        @pl.when(step == which * parts + parts - 1)
        def _():
            for copy in leave(which):
                copy.start()
            if which == count - 1:
                for slot in range(count):
                    for copy in leave(slot):
                        copy.wait()


def run_unmix(sc, planes, v_own, v_far, grad_heads, mean, exps, inverse, masks, carry):
    carry, count = list(carry), len(planes)
    per = 1 if count == 1 else PHEADS
    return pl.pallas_call(
        partial(unmix_kernel, count, per, bool(carry)),
        grid_spec=pltpu.PrefetchScalarGridSpec(
            num_scalar_prefetch=1,
            grid=(count * PHEADS // per,),
            in_specs=[
                plane_spec(planes, per, LMAX, 2 * HEAD),
                plane_spec(planes, per, LMAX, 2 * HEAD),
                plane_spec(planes, per, HROWS, 4 * HEAD),
                plane_spec(planes, per, HROWS, 4 * HEAD),
                plane_spec(planes, per, HROWS, LMAX),
                plane_spec(planes, per, HROWS, 4 * HEAD),
                held((LMAX, 4 * HEAD)),
                held((4 * HEAD, 128)),
                held((LMAX, 128)),
            ]
            + anywhere(len(carry)),
            out_specs=anywhere(4 * count) + [plane_spec(planes, per, LMAX, 2 * HEAD)] * 2,
            scratch_shapes=[
                pltpu.VMEM((count, 4 * SUBS * HALF, LMAX), BF16),
                pltpu.SemaphoreType.DMA((count, 4)),
            ],
        ),
        out_shape=[jax.ShapeDtypeStruct((SUBS * HALF, LMAX), BF16)] * (4 * count)
        + [jax.ShapeDtypeStruct((HEADS, LMAX, 2 * HEAD), BF16)] * 2,
        input_output_aliases={10 + i: 4 * count + i for i in range(len(carry))},
        compiler_params=params(VMEM),
        cost_estimate=pl.CostEstimate(
            flops=3 * HEADS * HROWS * LMAX * 4 * HEAD,
            bytes_accessed=HEADS * (2 * HROWS * LMAX + 5 * HROWS * 256 + 4 * LMAX * 256),
            transcendentals=0,
        ),
        name="unmix",
    )(sc, v_own, v_far, grad_heads, mean, exps, inverse, *masks, *carry)


def close_kernel(sc, tok, res_own, res_got, out_own, out_got, own, far, gain, w_own, w_far, *refs):
    (output, tok_grad, d_value, d_gain, total, weight) = refs
    step = pl.program_id(0)
    whole_weight(sc, step, w_own, w_far, weight)
    core = sc[CORE]
    output[:, :, core] = out_own[...].astype(F32)
    output[:, :, 1 - core] = out_got[...].astype(F32)
    tok_grad[:, :, core] = res_own[...].astype(F32)
    tok_grad[:, :, 1 - core] = res_got[...].astype(F32)
    runs = tok.shape[1]
    rows = runs * 128
    for item in range(2):
        lanes = slice(item * HEAD, (item + 1) * HEAD)
        pieces = [
            add_low(own[head, :, lanes], far[head, :, lanes]) for head in range(HEADS)
        ]
        back = jnp.concatenate(pieces, axis=1)
        x = tok[item].reshape(rows, WIDTH).astype(F32)
        scale = lax.rsqrt(jnp.mean(x * x, axis=-1, keepdims=True) + EPSILON)
        unit = x * scale
        normed = (unit * gain[...]).astype(BF16)
        normed_grad = dot(back, weight[...], 1, 1)
        gained = normed_grad * gain[...]
        update = scale * (gained - unit * jnp.mean(gained * unit, axis=-1, keepdims=True))
        tok_grad[item] += update.reshape(runs, 2, HALF, WIDTH)
        gain_sum = jnp.sum(normed_grad * unit, axis=0, keepdims=True)
        value_sum = dot(normed, back, 0, 0)
        if item == 0:
            gain_total, value_total = gain_sum, value_sum
        else:
            gain_total, value_total = gain_total + gain_sum, value_total + value_sum

    @pl.when(step == 0)
    def _():
        d_gain[...] = gain_total
        total[...] = value_total

    @pl.when(step > 0)
    def _():
        d_gain[...] += gain_total
        total[...] += value_total

    @pl.when(step == pl.num_programs(0) - 1)
    def _():
        low = total[...].astype(BF16)
        d_value[0] = low[:, :SIDE]
        d_value[1] = low[:, SIDE:]


def run_close(sc, tokens, res_own, res_got, out_own, out_got, own, far, gain, w_own, w_far):
    runs = 2
    slab = (2, RUNS, 2, HALF, WIDTH)
    half = (2, RUNS, HALF, WIDTH)
    whole_spec = spec((2, runs, 2, HALF, WIDTH), lambda j, s: (0, j, 0, 0, 0))
    half_spec = spec((2, runs, HALF, WIDTH), lambda j, s: (0, j, 0, 0))
    back_spec = spec((HEADS, runs * 128, 2 * HEAD), lambda j, s: (0, j, 0))
    return pl.pallas_call(
        close_kernel,
        grid_spec=pltpu.PrefetchScalarGridSpec(
            num_scalar_prefetch=1,
            grid=(RUNS // runs,),
            in_specs=[whole_spec]
            + [half_spec] * 4
            + [back_spec, back_spec, held((1, WIDTH)), held((WIDTH, SIDE)), held((WIDTH, SIDE))],
            out_specs=[whole_spec, whole_spec, held((2, WIDTH, SIDE)), held((1, WIDTH))],
            scratch_shapes=[pltpu.VMEM((WIDTH, WIDTH), F32), pltpu.VMEM((WIDTH, WIDTH), BF16)],
        ),
        out_shape=[
            jax.ShapeDtypeStruct(slab, F32),
            jax.ShapeDtypeStruct(slab, F32),
            jax.ShapeDtypeStruct((2, WIDTH, SIDE), BF16),
            jax.ShapeDtypeStruct((1, WIDTH), F32),
        ],
        compiler_params=params(LESS),
        cost_estimate=pl.CostEstimate(
            flops=4 * 2 * LMAX * WIDTH * WIDTH, bytes_accessed=38 * LMAX * WIDTH, transcendentals=0
        ),
        name="close",
    )(
        sc,
        tokens.reshape(slab),
        *(x.reshape(half) for x in (res_own, res_got, out_own, out_got)),
        own,
        far,
        gain,
        w_own,
        w_far,
    )


PACK_DOWN, PACK_UP, PACK_OUT, PACK_VALUE, PACK_GAIN, PACK = 0, 192, 384, 432, 480, 496


def pack_kernel(sc, down, up, out, value, gain, down_far, up_far, out_far, value_far, gain_far, packed):
    first = sc[CORE] == 0

    def both(own, far, lanes):
        own, far = own[:, lanes], far[:, lanes]
        return jnp.concatenate([jnp.where(first, own, far), jnp.where(first, far, own)], axis=0)

    def side(own, far):
        return both(own, far, own_lanes(sc))

    packed[PACK_DOWN:PACK_UP] = side(down, down_far)
    for j in range(4):
        lanes = pl.ds(pl.multiple_of((4 * sc[CORE] + j) * SIDE, 128), SIDE)
        packed[PACK_UP + 48 * j : PACK_UP + 48 * (j + 1)] = both(up, up_far, lanes)
    packed[PACK_OUT:PACK_VALUE] = side(out, out_far)
    packed[PACK_VALUE:PACK_GAIN] = side(value, value_far)
    packed[PACK_GAIN:] = both(gain, gain_far, slice(0, SIDE))


def run_pack(sc, own, far):
    return pl.pallas_call(
        pack_kernel,
        grid_spec=pltpu.PrefetchScalarGridSpec(
            num_scalar_prefetch=1,
            grid=(1,),
            in_specs=[held(x.shape) for x in (*own, *far)],
            out_specs=held((PACK, SIDE)),
        ),
        out_shape=jax.ShapeDtypeStruct((PACK, SIDE), BF16),
        compiler_params=params(VMEM),
        cost_estimate=pl.CostEstimate(flops=0, bytes_accessed=6 * PACK * SIDE, transcendentals=0),
        name="pack",
    )(sc, *own, *far)


def chip_of(sc, k, rel):
    return plane_of(k, sc) * 4 + (sc[PLACE] ^ rel)


def place_kernel(moves, sc, *refs):
    pieces, targets, sems = refs[:16], refs[16:-1], refs[-1]
    copies = []
    for index, piece in enumerate(pieces):
        chip = chip_of(sc, index // 4, index % 4)
        for which, (start, count, lane, target, step, offset, column) in enumerate(moves):
            rows = pl.ds(pl.multiple_of(chip * step + offset, 16), count)
            copies.append(
                pltpu.make_async_copy(
                    piece.at[pl.ds(start, count), pl.ds(lane, SIDE)],
                    targets[target].at[rows, pl.ds(column, SIDE)],
                    sems.at[index, which],
                )
            )
    for copy in copies:
        copy.start()
    for copy in copies:
        copy.wait()


def run_place(sc, pieces, moves, shapes):
    return pl.pallas_call(
        partial(place_kernel, moves),
        grid_spec=pltpu.PrefetchScalarGridSpec(
            num_scalar_prefetch=1,
            grid=(1,),
            in_specs=anywhere(16),
            out_specs=[held(shape) for shape in shapes],
            scratch_shapes=[pltpu.SemaphoreType.DMA((16, len(moves)))],
        ),
        out_shape=[jax.ShapeDtypeStruct(shape, BF16) for shape in shapes],
        compiler_params=params(VMEM),
        cost_estimate=pl.CostEstimate(
            flops=0, bytes_accessed=4 * sum(a * b for a, b in shapes), transcendentals=0
        ),
        name="place",
    )(sc, *pieces)


def place_weights(sc, pieces):
    moves = (
        (PACK_DOWN, 192, 0, 0, 192, 0, 0),
        *((PACK_UP + 48 * j, 48, 0, 1, 48, 0, j * SIDE) for j in range(4)),
        (PACK_OUT, 48, 0, 2, 48, 0, 0),
        (PACK_VALUE, 48, 0, 3, 48, 0, 0),
        (PACK_GAIN, 16, 0, 4, 16, 0, 0),
    )
    shapes = [(FF, SIDE), (WIDTH, FF // 2), (WIDTH, SIDE), (WIDTH, SIDE), (256, SIDE)]
    return run_place(sc, pieces, moves, shapes)


def collect_kernel(sc, *refs):
    outs = refs[24:]
    for k in range(PLANES):

        @pl.when(pl.program_id(0) == k)
        def _():
            for rel in range(4):
                down, down_got, up, up_got, out, out_got = refs[6 * rel : 6 * rel + 6]
                packed = outs[4 * k + rel]
                packed[PACK_DOWN:PACK_UP] = add_low(down[...], down_got[...])
                for j in range(4):
                    lanes = slice(j * SIDE, (j + 1) * SIDE)
                    packed[PACK_UP + 48 * j : PACK_UP + 48 * (j + 1)] = add_low(up[:, lanes], up_got[:, lanes])
                packed[PACK_OUT:PACK_VALUE] = add_low(out[...], out_got[...])


def run_collect(sc, *sides):
    def rows(x, rel):
        return spec((x.shape[0] // 16, x.shape[1]), lambda k, s: (chip_of(s, k, rel), 0))

    return pl.pallas_call(
        collect_kernel,
        grid_spec=pltpu.PrefetchScalarGridSpec(
            num_scalar_prefetch=1,
            grid=(PLANES,),
            in_specs=[rows(x, rel) for rel in range(4) for x in sides],
            out_specs=[held((PACK_VALUE, SIDE))] * 16,
        ),
        out_shape=[jax.ShapeDtypeStruct((PACK_VALUE, SIDE), BF16)] * 16,
        compiler_params=params(LESS),
        cost_estimate=pl.CostEstimate(flops=0, bytes_accessed=3 * 16 * PACK_VALUE * SIDE * 2, transcendentals=0),
        name="collect",
    )(sc, *(x for _ in range(4) for x in sides))


def add_kernel(groups, *refs):
    for group, total in zip(groups, refs[-len(groups) :]):
        value = refs[group[0]][...].astype(F32)
        for index in group[1:]:
            value = value + refs[index][...].astype(F32)
        total[...] = value.astype(total.dtype)


def run_add(groups, values, dtype):
    shape = values[0].shape
    here = pl.BlockSpec(memory_space=pltpu.VMEM)
    return pl.pallas_call(
        partial(add_kernel, groups),
        in_specs=[here] * len(values),
        out_specs=[here] * len(groups),
        out_shape=[jax.ShapeDtypeStruct(shape, dtype)] * len(groups),
        compiler_params=params(LESS),
        cost_estimate=pl.CostEstimate(
            flops=0, bytes_accessed=2 * shape[0] * shape[1] * (len(values) + len(groups)), transcendentals=0
        ),
        name="add",
    )(*values)


DEVICES = 32
TO_CORE, TO_X, TO_Y = 1, 2, 4


def swap(x, bit):
    return lax.ppermute(x, BOTH, [(d, d ^ bit) for d in range(DEVICES)])


def ring(x, way=1):
    return lax.ppermute(x, BOTH, [(d, (d + 8 * way) % DEVICES) for d in range(DEVICES)])


def pick(x, index, axis=0):
    return lax.dynamic_index_in_dim(x, index, axis, keepdims=False)


def ordered(flag, one, two, axis=0, joined=jnp.stack):
    return jnp.where(flag == 0, joined([one, two], axis), joined([two, one], axis))


def add_low(one, two):
    return (one.astype(F32) + two.astype(F32)).astype(BF16)


STEPS = (
    ((0, 0, 1), (0, 1, 0), (1, 0, 0)),
    ((1, 0, 1), (0, 1, 1), (2, 0, 0)),
    ((2, 0, 1), (1, 1, 0), (3, 0, 0)),
    ((1, 1, 1), (2, 1, 1), (2, 1, 0)),
    ((3, 0, 1), (3, 1, 0), (3, 1, 1)),
)


def gather_step(have, step):
    by_x, by_y, by_z = STEPS[step]
    return {
        **have,
        by_z: ring(have[by_z[0] - 1, by_z[1], by_z[2]]),
        by_x: swap(have[by_x[0], by_x[1], 0], TO_X),
        by_y: swap(have[by_y[0], 0, by_y[2]], TO_Y),
    }


def in_order(have):
    return [have[k, y, x] for k in range(4) for y in range(2) for x in range(2)]


def by_place(shares, planes=range(PLANES)):
    return {(k, i // 2, i % 2): shares[4 * at + i] for at, k in enumerate(planes) for i in range(4)}


def scatter_send(have, step):
    by_x, by_y, by_z = STEPS[len(STEPS) - 1 - step]
    got = (ring(have[by_z], -1), swap(have[by_x], TO_X), swap(have[by_y], TO_Y))
    return {at: value for at, value in have.items() if at not in (by_x, by_y, by_z)}, got


def scatter_add(have, got, step):
    by_x, by_y, by_z = STEPS[len(STEPS) - 1 - step]
    targets = ((by_z[0] - 1, by_z[1], by_z[2]), (by_x[0], by_x[1], 0), (by_y[0], 0, by_y[2]))
    sums = list(dict.fromkeys(targets))
    groups = [(len(got) + i, *(j for j in range(len(got)) if targets[j] == at)) for i, at in enumerate(sums)]
    values = [*got, *(have[at] for at in sums)]
    dtype = F32 if step == len(STEPS) - 1 else BF16
    if values[0].shape[1] == LMAX:
        totals = run_add(groups, values, dtype)
    else:
        totals = [sum(values[i].astype(F32) for i in group).astype(dtype) for group in groups]
    return {**have, **dict(zip(sums, totals))}


together = lax.optimization_barrier


def item_masks(lengths):
    lane, column = jnp.arange(4 * HEAD) // HEAD, jnp.arange(128)
    position = jnp.arange(LMAX)[:, None]
    wide = position < jnp.repeat(lengths, HEAD)[None]
    adder = jnp.where((lane[:, None] == column[None] % 4) & (column[None] < 8), -1.0, 0.0)
    narrow = (position < jnp.tile(lengths, 32)[None]) & (column[None] < 8)
    return wide.astype(BF16), adder.astype(BF16), narrow.astype(BF16)


def chip_shards(tokens, lengths, rand_mix, w_value, w_out, w_up, w_down, gain_mix, gain_ffn, grad_out):
    wide = lax.axis_index("wide")
    core = lax.axis_index("narrow")
    z, y, x = wide // 4, (wide // 2) % 2, wide % 2
    other = lambda value: swap(value, TO_CORE)
    side = partial(ordered, core, joined=jnp.concatenate)
    slab = (2, RUNS, 2, HALF, WIDTH)
    tokens, grad_out = tokens.reshape(slab), grad_out.reshape(slab)

    gains = jnp.pad(jnp.concatenate([gain_mix, gain_ffn])[None], ((0, 7), (0, SIDE - 48)))
    own = (w_down, w_up, w_out, w_value, gains)
    far = tuple(other(value) for value in own)
    near_sc = jnp.concatenate([jnp.stack([core, z, wide % 4]).astype(jnp.int32), lengths, lengths])
    weights = {(0, 0, 0): run_pack(near_sc, own, far)}

    rand = rand_mix.reshape(3, 2, HALF, LMAX)
    blocks = side(pick(rand, core, 1), other(pick(rand, 1 - core, 1)), 0)
    weights, rands, late_tokens, late_grad = together(
        (gather_step(weights, 0), {(0, 0, 0): blocks.reshape(SUBS * HALF, LMAX)}, tokens, grad_out)
    )
    weights, tokens_far = together((gather_step(weights, 1), other(pick(late_tokens, 1 - core, 2))))
    weights, grad_far = together((gather_step(weights, 2), other(pick(late_grad, 1 - core, 2))))
    weights, far_lengths = together((gather_step(weights, 3), other(lengths)))
    sc = jnp.concatenate([near_sc[:5], far_lengths])
    masks = item_masks(sc[3:])
    weights, rands, masks = together((gather_step(weights, 4), rands, masks))

    rands = gather_step(rands, 0)
    down, up, out, value, gain_rows = place_weights(sc, in_order(weights))
    rands, value, value_far, gain_rows, out, down, up = together(
        (rands, value, other(value), gain_rows, out, down, up)
    )
    gain_rows = gain_rows.reshape(16, 2, 8, SIDE)[:, :, 0]
    gain_one = gain_rows[..., :24].reshape(1, WIDTH).astype(F32)
    gain_two = gain_rows[..., 24:48].reshape(1, WIDTH).astype(F32)
    rands = gather_step(rands, 1)
    v_own = run_values(sc, tokens.reshape(2, LMAX, WIDTH), gain_one, value, value_far)
    rands, v_own, out, down, up = together((rands, v_own, (out, other(out)), down, up))
    rands, v_own, v_far, grad_far, down, up = together(
        (gather_step(rands, 2), v_own, other(v_own), grad_far, down, up)
    )
    rands = gather_step(rands, 3)
    masked = run_masked(sc, grad_out, grad_far)
    rands, v_far, masked, down, up = together((rands, v_far, masked, down, up))
    near = [rands[k, y_at, x_at] for k in range(3) for y_at in range(2) for x_at in range(2)]
    rands = gather_step(rands, 4)
    mixing = run_mix(sc, (0, 1, 2), near, v_own, v_far, masks[0], ())
    rands, down, up, mixing = together((rands, down, up, mixing))
    heads, mean, exps, inverse = run_mix(sc, (3,), in_order(rands)[12:], v_own, v_far, masks[0], mixing)
    down, up = (down, other(down)), (up, other(up))

    mixed, resid, normed = run_pre(sc, tokens, tokens_far, heads, out, gain_two)
    active, up_grad = run_units(sc, normed, masked, up, down)
    res_own, res_far, grad_heads, d_gain_two = run_post(sc, resid, up_grad, masked, up, out, gain_two)

    backward = lambda planes, carry: run_unmix(
        sc, planes, v_own, v_far, grad_heads, mean, exps, inverse, masks, carry
    )
    *far, back_own, back_far = backward((3,), ())
    far, back_own, back_far, res_got = together((far, back_own, back_far, other(res_far)))
    have, got = scatter_send(by_place(far, (3,)), 0)
    *near, back_own, back_far = backward((2, 1, 0), (back_own, back_far))
    have, got, near, back_own, back_far = together((have, got, near, back_own, back_far))
    have = scatter_add({**have, **by_place(near, (2, 1, 0))}, got, 0)

    have, got = scatter_send(have, 1)
    up_own, up_far = run_up_grad(sc, normed, up_grad)
    have, got, up_own, up_far, back_got = together((have, got, up_own, up_far, other(back_far)))
    have = scatter_add(have, got, 1)

    have, got = scatter_send(have, 2)
    down_own, down_far = run_down_grad(sc, active, masked)
    have, got, down_own, down_far, up_got = together((have, got, down_own, down_far, other(up_far)))
    have = scatter_add(have, got, 2)

    have, got = scatter_send(have, 3)
    out_own, out_far = run_out(sc, active, resid, down)
    have, got, out_own, out_far, down_got, res_own, res_far = together(
        (have, got, out_own, out_far, other(down_far), res_own, res_far)
    )
    have = scatter_add(have, got, 3)

    have, got = scatter_send(have, 4)
    d_out_own, d_out_far = run_out_grad(sc, mixed, res_own, res_far)
    packed = run_collect(sc, down_own, down_got, up_own, up_got, d_out_own, other(d_out_far))
    have, got, packed, out_got = together((have, got, packed, other(out_far)))
    rand_sum = scatter_add(have, got, 4)[0, 0, 0].reshape(2, 3, HALF, LMAX)

    sums, got = scatter_send(by_place(packed), 0)
    output, tokens_grad, d_value, d_gain_one = run_close(
        sc, tokens, res_own, res_got, out_own, out_got, back_own, back_got, gain_one, value, value_far
    )
    gain_pair = jnp.concatenate([d_gain_one, d_gain_two]).reshape(2, 16, 1, 48).astype(BF16)
    gain_pair = jnp.pad(gain_pair, ((0, 0), (0, 0), (0, 15), (0, SIDE - 48)))
    small = jnp.concatenate([d_value.reshape(2, 16, 48, SIDE), gain_pair], 2)
    sums, got, output, tokens_grad, small = together((sums, got, output, tokens_grad, small))
    sums = scatter_add(sums, got, 0)

    sums, got = scatter_send(sums, 1)
    small = add_low(pick(small, core), other(pick(small, 1 - core))).reshape(4, 2, 2, 64, SIDE)
    sums, got, small = together((sums, got, small))
    sums = scatter_add(sums, got, 1)

    sums, got = scatter_send(sums, 2)
    small = add_low(pick(small, x, 2), swap(pick(small, 1 - x, 2), TO_X))
    sums, got, small = together((sums, got, small))
    sums = scatter_add(sums, got, 2)

    sums, got = scatter_send(sums, 3)
    small = add_low(pick(small, y, 1), swap(pick(small, 1 - y, 1), TO_Y))
    blocks, blocks_far = pick(rand_sum, core), other(pick(rand_sum, 1 - core))
    sums, got, small, blocks, blocks_far = together((sums, got, small, blocks, blocks_far))
    sums = scatter_add(sums, got, 3)

    sums, got = scatter_send(sums, 4)
    small_sum = pick(small, z).astype(F32)
    for k in range(1, PLANES):
        small_sum = small_sum + ring(pick(small, lax.rem(z + PLANES - k, PLANES)), -k).astype(F32)
    sums, got, small_sum = together((sums, got, small_sum))
    big_sum = scatter_add(sums, got, 4)[0, 0, 0]
    big_far, small_far = other(big_sum), other(small_sum)

    rows_of = lambda value, rows: pick(value.reshape(-1, 2, rows, SIDE), core, 1)
    mine = lambda own, far, rows: side(rows_of(own, rows)[0], rows_of(far, rows)[0], 1)
    down_shard = mine(big_sum[PACK_DOWN:PACK_UP], big_far[PACK_DOWN:PACK_UP], 96)
    up_side = lambda value: rows_of(value[PACK_UP:PACK_OUT], 24).transpose(1, 0, 2).reshape(24, 4 * SIDE)
    up_shard = side(up_side(big_sum), up_side(big_far), 1)
    outproj_shard = mine(big_sum[PACK_OUT:PACK_VALUE], big_far[PACK_OUT:PACK_VALUE], 24)
    value_shard = mine(small_sum[:48], small_far[:48], 24)
    gains_pair = ordered(core, small_sum[48, :48], small_far[48, :48])
    gain_pair = pick(gains_pair.reshape(2, 2, 24), core, 1)

    rand_shard = ordered(core, blocks, blocks_far, 1)

    return (
        output.reshape(2, LMAX, WIDTH),
        tokens_grad.reshape(2, LMAX, WIDTH),
        rand_shard.reshape(3 * 128, LMAX),
        value_shard,
        outproj_shard,
        up_shard,
        down_shard,
        gain_pair[0],
        gain_pair[1],
    )


def rms_norm(values, gain):
    scale = lax.rsqrt(jnp.mean(values * values, axis=-1, keepdims=True) + EPSILON)
    return values * scale * gain


def split_heads(block):
    return block.reshape(LMAX, HEADS, HEAD).transpose(1, 0, 2)


def merge_heads(block):
    return block.transpose(1, 0, 2).reshape(LMAX, HEADS * HEAD)


def masked_scores(key_mask, rand_head):
    return jnp.where(key_mask[None, :] > 0, rand_head.astype(jnp.float32), -1e30)


def head_forward(key_mask, paired):
    rand_head, value_head = paired
    scores = masked_scores(key_mask, rand_head)
    row_peak = jnp.max(scores, axis=-1, keepdims=True)
    exponent = jnp.exp(scores - row_peak)
    denom_sum = jnp.sum(exponent, axis=-1, keepdims=True)
    attention = exponent / denom_sum * key_mask[:, None]
    mixed = jnp.dot(attention.astype(jnp.bfloat16), value_head, preferred_element_type=jnp.float32)
    return (mixed.astype(jnp.bfloat16), row_peak + jnp.log(denom_sum))


def head_backward(key_mask, paired):
    rand_head, value_head, mix_grad, log_total = paired
    scores = masked_scores(key_mask, rand_head)
    attention = jnp.exp(scores - log_total) * key_mask[:, None]
    prob_grad = jnp.einsum("id,jd->ij", mix_grad, value_head, preferred_element_type=jnp.float32)
    value_grad = jnp.einsum(
        "ij,id->jd", attention.astype(jnp.bfloat16), mix_grad, preferred_element_type=jnp.float32
    )
    score_grad = attention * (prob_grad - jnp.sum(prob_grad * attention, axis=-1, keepdims=True))
    return (score_grad, value_grad)


def shards(tokens, lengths, rand_mix, w_value, w_out, w_up, w_down, gain_mix, gain_ffn, grad_out):
    item_count = tokens.shape[0]
    width = tokens.shape[2]
    row_count = item_count * LMAX
    tokens_flat = tokens.reshape(row_count, width).astype(jnp.float32)
    positions = jnp.arange(LMAX, dtype=jnp.int32)
    valid_table = (positions[None, :] < lengths[:, None]).astype(jnp.float32)
    row_valid = valid_table.reshape(row_count, 1)
    forward_set = (
        lax.all_gather(rand_mix, ("wide", "narrow"), axis=0, tiled=True),
        lax.all_gather(w_value, ("wide", "narrow"), axis=0, tiled=True),
        lax.all_gather(w_out, ("wide", "narrow"), axis=0, tiled=True),
        lax.all_gather(w_up, ("wide", "narrow"), axis=0, tiled=True),
        lax.all_gather(w_down, ("wide", "narrow"), axis=0, tiled=True),
        lax.all_gather(gain_mix, ("wide", "narrow"), axis=0, tiled=True),
        lax.all_gather(gain_ffn, ("wide", "narrow"), axis=0, tiled=True),
    )
    rand_all, value_all, out_all, up_all, down_all, gain_first, gain_second = forward_set
    normed = rms_norm(tokens_flat, gain_first.astype(jnp.float32)).astype(jnp.bfloat16)
    values = jnp.dot(normed, value_all, preferred_element_type=jnp.float32).astype(jnp.bfloat16)
    rand_heads = rand_all.reshape(HEADS, LMAX, LMAX)
    mixed_parts = []
    totals_kept = []
    for item_index in range(item_count):
        item_values = split_heads(values[item_index * LMAX : (item_index + 1) * LMAX])
        mixed_heads, log_total = lax.map(
            partial(head_forward, valid_table[item_index]), (rand_heads, item_values)
        )
        mixed_parts.append(merge_heads(mixed_heads))
        totals_kept.append(log_total)
    mixed = jnp.concatenate(mixed_parts, axis=0)
    residual = tokens_flat + jnp.dot(mixed, out_all, preferred_element_type=jnp.float32)
    normed_two = rms_norm(residual, gain_second.astype(jnp.float32)).astype(jnp.bfloat16)
    up_proj = jnp.dot(normed_two, up_all, preferred_element_type=jnp.float32)
    active = jax.nn.gelu(up_proj).astype(jnp.bfloat16)
    branch = jnp.dot(active, down_all, preferred_element_type=jnp.float32)
    output = row_valid * (residual + branch)
    back_set = (
        lax.all_gather(rand_mix, ("wide", "narrow"), axis=0, tiled=True),
        lax.all_gather(w_value, ("wide", "narrow"), axis=0, tiled=True),
        lax.all_gather(w_out, ("wide", "narrow"), axis=0, tiled=True),
        lax.all_gather(w_up, ("wide", "narrow"), axis=0, tiled=True),
        lax.all_gather(w_down, ("wide", "narrow"), axis=0, tiled=True),
        lax.all_gather(gain_mix, ("wide", "narrow"), axis=0, tiled=True),
        lax.all_gather(gain_ffn, ("wide", "narrow"), axis=0, tiled=True),
    )
    rand_back, value_back, out_back, up_back, down_back, gain_back_one, gain_back_two = back_set
    cotangent = grad_out.reshape(row_count, width).astype(jnp.float32)
    masked = row_valid * cotangent
    branch_grad = masked.astype(jnp.bfloat16)
    grad_down = jnp.einsum("rk,rd->kd", active, branch_grad, preferred_element_type=jnp.float32)
    active_grad = jnp.einsum(
        "rd,kd->rk", branch_grad, down_back, preferred_element_type=jnp.float32
    )
    gelu_value, gelu_pull = jax.vjp(jax.nn.gelu, up_proj)
    up_grad = gelu_pull(active_grad)[0].astype(jnp.bfloat16)
    grad_up = jnp.einsum("rd,rk->dk", normed_two, up_grad, preferred_element_type=jnp.float32)
    normed_two_grad = jnp.einsum("rk,dk->rd", up_grad, up_back, preferred_element_type=jnp.float32)
    norm_value, norm_pull = jax.vjp(rms_norm, residual, gain_back_two.astype(jnp.float32))
    residual_part, gain_two_grad = norm_pull(normed_two_grad)
    residual_grad = masked + residual_part
    attn_grad = residual_grad.astype(jnp.bfloat16)
    grad_outproj = jnp.einsum("rd,re->de", mixed, attn_grad, preferred_element_type=jnp.float32)
    mixed_grad = jnp.einsum(
        "re,de->rd", attn_grad, out_back, preferred_element_type=jnp.float32
    ).astype(jnp.bfloat16)
    rand_heads_back = rand_back.reshape(HEADS, LMAX, LMAX)
    rand_grad = jnp.zeros((HEADS, LMAX, LMAX), jnp.float32)
    value_parts = []
    for item_index in range(item_count):
        lower_row = item_index * LMAX
        upper_row = lower_row + LMAX
        item_values = split_heads(values[lower_row:upper_row])
        item_mix_grad = split_heads(mixed_grad[lower_row:upper_row])
        score_grad, value_grad = lax.map(
            partial(head_backward, valid_table[item_index]),
            (rand_heads_back, item_values, item_mix_grad, totals_kept[item_index]),
        )
        rand_grad = rand_grad + score_grad
        value_parts.append(merge_heads(value_grad))
    values_grad = jnp.concatenate(value_parts, axis=0).astype(jnp.bfloat16)
    grad_value = jnp.einsum("rd,re->de", normed, values_grad, preferred_element_type=jnp.float32)
    normed_grad = jnp.einsum(
        "re,de->rd", values_grad, value_back, preferred_element_type=jnp.float32
    )
    norm_first, first_pull = jax.vjp(rms_norm, tokens_flat, gain_back_one.astype(jnp.float32))
    token_part, gain_one_grad = first_pull(normed_grad)
    tokens_grad = residual_grad + token_part
    rand_flat = rand_grad.reshape(HEADS * LMAX, LMAX)
    all_shards = (
        lax.psum_scatter(rand_flat, ("wide", "narrow"), scatter_dimension=0, tiled=True),
        lax.psum_scatter(grad_value, ("wide", "narrow"), scatter_dimension=0, tiled=True),
        lax.psum_scatter(grad_outproj, ("wide", "narrow"), scatter_dimension=0, tiled=True),
        lax.psum_scatter(grad_up, ("wide", "narrow"), scatter_dimension=0, tiled=True),
        lax.psum_scatter(grad_down, ("wide", "narrow"), scatter_dimension=0, tiled=True),
        lax.psum_scatter(gain_one_grad, ("wide", "narrow"), scatter_dimension=0, tiled=True),
        lax.psum_scatter(gain_two_grad, ("wide", "narrow"), scatter_dimension=0, tiled=True),
    )
    rand_shard, value_shard, outproj_shard, up_shard, down_shard, gain_one_shard, gain_two_shard = (
        all_shards
    )
    return (
        output.reshape(item_count, LMAX, width),
        tokens_grad.reshape(item_count, LMAX, width),
        rand_shard,
        value_shard,
        outproj_shard,
        up_shard,
        down_shard,
        gain_one_shard,
        gain_two_shard,
    )


def solution(mesh):
    in_specs = (
        P(("wide", "narrow"), None, None),
        P(("wide", "narrow")),
        P(("wide", "narrow"), None),
        P(("wide", "narrow"), None),
        P(("wide", "narrow"), None),
        P(("wide", "narrow"), None),
        P(("wide", "narrow"), None),
        P(("wide", "narrow")),
        P(("wide", "narrow")),
        P(("wide", "narrow"), None, None),
    )
    out_specs = (
        P(("wide", "narrow"), None, None),
        P(("wide", "narrow"), None, None),
        P(("wide", "narrow"), None),
        P(("wide", "narrow"), None),
        P(("wide", "narrow"), None),
        P(("wide", "narrow"), None),
        P(("wide", "narrow"), None),
        P(("wide", "narrow")),
        P(("wide", "narrow")),
    )
    fits = dict(mesh.shape) == {"wide": 16, "narrow": 2}
    return jax.shard_map(chip_shards if fits else shards, mesh=mesh, in_specs=in_specs, out_specs=out_specs, check_vma=False)
```

```python
from functools import partial

import jax
import jax.numpy as jnp
from jax import lax
from jax.experimental import pallas as pl
from jax.experimental.pallas import tpu as pltpu
from jax.sharding import PartitionSpec as P

HEADS = 12
HEAD = 64
LMAX = 1024
WIDTH = 768
FF = 3072
EPSILON = 1e-05

BOTH = ("wide", "narrow")
BF16 = jnp.bfloat16
F32 = jnp.float32
VMEM = 61 << 20
LESS = 34 << 20

SUBS = 6
RUNS = 8
HALF = 64
HROWS = RUNS * HALF
PLANES = 4
PHEADS = HEADS // PLANES
ROWS = 2 * LMAX
FSTEP = 768
FSIDE = FF // 2 // FSTEP
TILE = 512
SIDE = WIDTH // 2
SPAN = 2 * HALF


def dot(a, b, ca, cb):
    return lax.dot_general(a, b, (((ca,), (cb,)), ((), ())), preferred_element_type=F32)


CORE, PLANE, PLACE, LENGTHS = 0, 1, 2, 3


def spec(shape, index):
    return pl.BlockSpec(shape, index)


def held(shape):
    zeros = (0,) * len(shape)
    return pl.BlockSpec(shape, lambda *_: zeros, pipeline_mode=pl.Buffered(1))


def params(limit):
    return pltpu.CompilerParams(vmem_limit_bytes=limit)


def whole_weight(sc, step, own, far, weight):
    @pl.when(step == 0)
    def _():
        weight[:, pl.ds(pl.multiple_of(sc[CORE] * SIDE, 128), SIDE)] = own[...]
        weight[:, pl.ds(pl.multiple_of((1 - sc[CORE]) * SIDE, 128), SIDE)] = far[...]


def values_kernel(sc, tok, gain, w_own, w_far, out, weight):
    step = pl.program_id(0)
    whole_weight(sc, step, w_own, w_far, weight)
    rows = tok.shape[1]
    position = step * rows + lax.broadcasted_iota(jnp.int32, (rows, 1), 0)
    for item in range(2):
        x = tok[item].astype(F32)
        scale = lax.rsqrt(jnp.mean(x * x, axis=-1, keepdims=True) + EPSILON)
        normed = (x * scale * gain[...]).astype(BF16)
        found = dot(normed, weight[...], 1, 0)
        found = jnp.where(position < sc[LENGTHS + item], found, 0.0).astype(BF16)
        for head in range(HEADS):
            out[head, :, item * HEAD : (item + 1) * HEAD] = found[:, head * HEAD : (head + 1) * HEAD]


def run_values(sc, tokens, gain, w_own, w_far):
    rows = 256
    return pl.pallas_call(
        values_kernel,
        grid_spec=pltpu.PrefetchScalarGridSpec(
            num_scalar_prefetch=1,
            grid=(LMAX // rows,),
            in_specs=[
                spec((2, rows, WIDTH), lambda j, s: (0, j, 0)),
                held((1, WIDTH)),
                held((WIDTH, SIDE)),
                held((WIDTH, SIDE)),
            ],
            out_specs=spec((HEADS, rows, 2 * HEAD), lambda j, s: (0, j, 0)),
            scratch_shapes=[pltpu.VMEM((WIDTH, WIDTH), BF16)],
        ),
        out_shape=jax.ShapeDtypeStruct((HEADS, LMAX, 2 * HEAD), BF16),
        compiler_params=params(VMEM),
        cost_estimate=pl.CostEstimate(
            flops=2 * 2 * LMAX * WIDTH * WIDTH, bytes_accessed=8 * LMAX * WIDTH, transcendentals=0
        ),
        name="values",
    )(sc, tokens, gain, w_own, w_far)


def lane_lengths(sc, shape):
    slot = lax.broadcasted_iota(jnp.int32, shape, 1) // HEAD
    length = jnp.where(slot == 0, sc[LENGTHS], sc[LENGTHS + 1])
    return jnp.where(slot >= 2, jnp.where(slot == 2, sc[LENGTHS + 2], sc[LENGTHS + 3]), length)


def plane_of(k, sc):
    return lax.rem(sc[PLANE] + PLANES - k, PLANES)


def plane_spec(planes, rows, lanes):
    def index(step, sc):
        return (plane_of(planes[0] + step * (planes[-1] - planes[0]) // max(len(planes) - 1, 1), sc), 0, 0)

    return spec((PHEADS, rows, lanes), index)


def anywhere(count):
    return [pl.BlockSpec(memory_space=pl.ANY)] * count


def plane_fetch(place, shards, raw, sems, slot):
    return [
        pltpu.make_async_copy(
            shards[4 * slot + rel],
            raw.at[slot, pl.ds(pl.multiple_of((place ^ rel) * SUBS * HALF, SUBS * HALF), SUBS * HALF)],
            sems.at[slot, rel],
        )
        for rel in range(4)
    ]


def take_plane(place, shards, raw, sems):
    step = pl.program_id(0)
    count = len(shards) // 4

    @pl.when(step == 0)
    def _():
        for slot in range(count):
            for copy in plane_fetch(place, shards, raw, sems, slot):
                copy.start()

    for slot in range(count):

        @pl.when(step == slot)
        def _():
            for copy in plane_fetch(place, shards, raw, sems, slot):
                copy.wait()

    return step


def head_rows(head):
    return slice(head * HROWS, (head + 1) * HROWS)


def fill_mask(sc, mask):
    @pl.when(pl.program_id(0) == 0)
    def _():
        shape = (LMAX, 4 * HEAD)
        column = lax.broadcasted_iota(jnp.int32, shape, 0)
        mask[...] = (column < lane_lengths(sc, shape)).astype(F32).astype(BF16)


def mix_kernel(count, carried, sc, *refs):
    shards, (v_own, v_far, *rest) = refs[: 4 * count], refs[4 * count :]
    mixed, mean, exps, inverse, raw, mask, sems = rest[4:] if carried else rest
    fill_mask(sc, mask)
    slot = take_plane(sc[PLACE], shards, raw, sems)
    shape = (HROWS, 4 * HEAD)
    line = lax.broadcasted_iota(jnp.int32, shape, 0)
    position = 128 * (line // HALF) + HALF * sc[CORE] + line % HALF
    valid = position < lane_lengths(sc, shape)
    for head in range(PHEADS):
        weights = jnp.exp(raw[slot, head_rows(head)].astype(F32)).astype(BF16)
        exps[head] = weights
        both = dot(weights, jnp.concatenate([v_own[head], v_far[head], mask[...]], axis=1), 1, 0)
        flip = jnp.where(valid, 1.0 / both[:, 4 * HEAD :], 0.0)
        found = both[:, : 4 * HEAD] * flip
        inverse[head] = flip.astype(BF16)
        mean[head] = found
        mixed[head] = found.astype(BF16)


def run_mix(sc, planes, shards, v_own, v_far, carry):
    carry, count = list(carry), len(planes)
    shape = (HEADS, HROWS, 4 * HEAD)
    return pl.pallas_call(
        partial(mix_kernel, count, bool(carry)),
        grid_spec=pltpu.PrefetchScalarGridSpec(
            num_scalar_prefetch=1,
            grid=(count,),
            in_specs=anywhere(4 * count) + [plane_spec(planes, LMAX, 2 * HEAD)] * 2 + anywhere(len(carry)),
            out_specs=[
                plane_spec(planes, HROWS, 4 * HEAD),
                plane_spec(planes, HROWS, 4 * HEAD),
                plane_spec(planes, HROWS, LMAX),
                plane_spec(planes, HROWS, 4 * HEAD),
            ],
            scratch_shapes=[
                pltpu.VMEM((count, 4 * SUBS * HALF, LMAX), BF16),
                pltpu.VMEM((LMAX, 4 * HEAD), BF16),
                pltpu.SemaphoreType.DMA((count, 4)),
            ],
        ),
        out_shape=[
            jax.ShapeDtypeStruct(shape, BF16),
            jax.ShapeDtypeStruct(shape, F32),
            jax.ShapeDtypeStruct((HEADS, HROWS, LMAX), BF16),
            jax.ShapeDtypeStruct(shape, BF16),
        ],
        input_output_aliases={3 + 4 * count + i: i for i in range(len(carry))},
        compiler_params=params(VMEM),
        cost_estimate=pl.CostEstimate(
            flops=2 * HEADS * HROWS * LMAX * 4 * HEAD,
            bytes_accessed=HEADS * (2 * HROWS * LMAX + 5 * HROWS * 256),
            transcendentals=HEADS * HROWS * LMAX // 2,
        ),
        name="mix",
    )(sc, *shards, v_own, v_far, *carry)


def row_valid(sc, step):
    line = lax.broadcasted_iota(jnp.int32, (4 * SPAN, 1), 0)
    item = line // SPAN
    row = step * SPAN + line % SPAN
    low = jnp.where(item == 0, sc[LENGTHS], sc[LENGTHS + 1])
    high = jnp.where(item == 2, sc[LENGTHS + 2], sc[LENGTHS + 3])
    return 128 * (row // HALF) + HALF * sc[CORE] + row % HALF < jnp.where(item >= 2, high, low)


def four_items(own, far):
    return jnp.concatenate([own[:, :, 0], far[...]], axis=0).reshape(4 * SPAN, WIDTH)


def pre_kernel(sc, tok, tok_far, heads, wo_own, wo_far, gain, mixed, resid, normed, weight):
    step = pl.program_id(0)
    whole_weight(sc, step, wo_own, wo_far, weight)
    for item in range(4):
        lanes = slice(item * HEAD, (item + 1) * HEAD)
        for pair in range(HEADS // 2):
            both = jnp.concatenate([heads[2 * pair, :, lanes], heads[2 * pair + 1, :, lanes]], axis=1)
            mixed[item, :, pair * 128 : (pair + 1) * 128] = both
    res = four_items(tok, tok_far).astype(F32) + dot(mixed[...].reshape(4 * SPAN, WIDTH), weight[...], 1, 0)
    resid[...] = res.astype(BF16).reshape(4, SPAN, WIDTH)
    scale = lax.rsqrt(jnp.mean(res * res, axis=-1, keepdims=True) + EPSILON)
    valid = row_valid(sc, step)
    normed[...] = jnp.where(valid, res * scale * gain[...], 0.0).astype(BF16).reshape(4, SPAN, WIDTH)


def slab_spec(items=4):
    return spec((items, SPAN, WIDTH), lambda r, s: (0, r, 0))


def half_specs():
    return [
        spec((2, SPAN // HALF, 1, HALF, WIDTH), lambda r, s: (0, r, s[CORE], 0, 0)),
        spec((2, SPAN // HALF, HALF, WIDTH), lambda r, s: (0, r, 0, 0)),
    ]


def heads_spec():
    return spec((HEADS, SPAN, 4 * HEAD), lambda r, s: (0, r, 0))


def run_pre(sc, tokens, tokens_far, heads, wo, gain):
    return pl.pallas_call(
        pre_kernel,
        grid_spec=pltpu.PrefetchScalarGridSpec(
            num_scalar_prefetch=1,
            grid=(HROWS // SPAN,),
            in_specs=half_specs()
            + [heads_spec(), held((WIDTH, SIDE)), held((WIDTH, SIDE)), held((1, WIDTH))],
            out_specs=[slab_spec()] * 3,
            scratch_shapes=[pltpu.VMEM((WIDTH, WIDTH), BF16)],
        ),
        out_shape=[
            jax.ShapeDtypeStruct((4, HROWS, WIDTH), BF16),
            jax.ShapeDtypeStruct((4, HROWS, WIDTH), BF16),
            jax.ShapeDtypeStruct((4, HROWS, WIDTH), BF16),
        ],
        compiler_params=params(VMEM),
        cost_estimate=pl.CostEstimate(
            flops=2 * ROWS * WIDTH * WIDTH, bytes_accessed=16 * ROWS * WIDTH, transcendentals=0
        ),
        name="pre",
    )(sc, tokens, tokens_far, heads, *wo, gain)


def masked_kernel(sc, cot, cot_far, masked):
    value = jnp.where(row_valid(sc, pl.program_id(0)), four_items(cot, cot_far).astype(F32), 0.0)
    masked[...] = value.astype(BF16).reshape(4, SPAN, WIDTH)


def run_masked(sc, cotangent, cotangent_far):
    return pl.pallas_call(
        masked_kernel,
        grid_spec=pltpu.PrefetchScalarGridSpec(
            num_scalar_prefetch=1, grid=(HROWS // SPAN,), in_specs=half_specs(), out_specs=slab_spec()
        ),
        out_shape=jax.ShapeDtypeStruct((4, HROWS, WIDTH), BF16),
        compiler_params=params(VMEM),
        cost_estimate=pl.CostEstimate(flops=0, bytes_accessed=4 * ROWS * WIDTH, transcendentals=0),
        name="masked",
    )(sc, cotangent, cotangent_far)


def own_lanes(sc):
    return pl.ds(pl.multiple_of(sc[CORE] * SIDE, 128), SIDE)


def far_lanes(sc):
    return pl.ds(pl.multiple_of((1 - sc[CORE]) * SIDE, 128), SIDE)


def unit_rows(f, sc):
    return (lax.rem(FSIDE * sc[CORE] + f, 2 * FSIDE), 0)


def unit_columns(f, sc):
    return (0, lax.rem(FSIDE * sc[CORE] + f, 2 * FSIDE))


def early(f, sc):
    return (0, lax.min(f, FSIDE - 1))


def late(f, sc):
    return (0, lax.max(f - FSIDE, 0))


def units_kernel(sc, normed, cot, up_own, up_far, dn_own, dn_far, active, up_grad, w_up, w_down):
    step = pl.program_id(0)
    w_down[:, own_lanes(sc)] = dn_own[...]
    w_down[:, far_lanes(sc)] = dn_far[...]

    @pl.when(step < FSIDE)
    def _():
        w_up[...] = up_own[...]

    @pl.when(step >= FSIDE)
    def _():
        w_up[...] = up_far[...]

    for row in range(0, ROWS, 256):
        rows = slice(row, row + 256)
        for column in range(0, FSTEP, 256):
            columns = slice(column, column + 256)
            up = dot(normed[rows], w_up[:, columns], 1, 0)
            square = up * up
            bend = jnp.tanh(up * (0.7978845608028654 + (0.044715 * 0.7978845608028654) * square))
            share = 0.5 + 0.5 * bend
            act = up * share
            active[rows, columns] = act.astype(BF16)
            slope = share + act * (1.0 - share) * (
                2 * 0.7978845608028654 + (6 * 0.044715 * 0.7978845608028654) * square
            )
            up_grad[rows, columns] = (dot(cot[rows], w_down[columns], 1, 1) * slope).astype(BF16)


def run_units(sc, normed, cotangent, up, down):
    return pl.pallas_call(
        units_kernel,
        grid_spec=pltpu.PrefetchScalarGridSpec(
            num_scalar_prefetch=1,
            grid=(2 * FSIDE,),
            in_specs=[
                held((ROWS, WIDTH)),
                held((ROWS, WIDTH)),
                spec((WIDTH, FSTEP), early),
                spec((WIDTH, FSTEP), late),
                spec((FSTEP, SIDE), unit_rows),
                spec((FSTEP, SIDE), unit_rows),
            ],
            out_specs=[spec((ROWS, FSTEP), unit_columns), spec((ROWS, FSTEP), unit_columns)],
            scratch_shapes=[pltpu.VMEM((WIDTH, FSTEP), BF16), pltpu.VMEM((FSTEP, WIDTH), BF16)],
        ),
        out_shape=[jax.ShapeDtypeStruct((ROWS, FF), BF16), jax.ShapeDtypeStruct((ROWS, FF), BF16)],
        compiler_params=params(VMEM),
        cost_estimate=pl.CostEstimate(
            flops=4 * ROWS * WIDTH * FF, bytes_accessed=6 * ROWS * WIDTH + 4 * ROWS * FF, transcendentals=ROWS * FF
        ),
        name="units",
    )(sc, normed.reshape(ROWS, WIDTH), cotangent.reshape(ROWS, WIDTH), *up, *down)


def down_grad_kernel(sc, active, cot, own, far, total):
    total[...] = dot(active[...], cot[...], 0, 0).astype(BF16)
    own[...] = total[:, own_lanes(sc)]
    far[...] = total[:, far_lanes(sc)]


def run_down_grad(sc, active, cotangent):
    return pl.pallas_call(
        down_grad_kernel,
        grid_spec=pltpu.PrefetchScalarGridSpec(
            num_scalar_prefetch=1,
            grid=(FF // 512,),
            in_specs=[spec((ROWS, 512), lambda f, s: (0, f)), held((ROWS, WIDTH))],
            out_specs=[spec((512, SIDE), lambda f, s: (f, 0))] * 2,
            scratch_shapes=[pltpu.VMEM((512, WIDTH), BF16)],
        ),
        out_shape=[jax.ShapeDtypeStruct((FF, SIDE), BF16)] * 2,
        compiler_params=params(57 << 20),
        cost_estimate=pl.CostEstimate(
            flops=2 * ROWS * WIDTH * FF, bytes_accessed=2 * ROWS * (WIDTH + FF), transcendentals=0
        ),
        name="down_grad",
    )(sc, active, cotangent.reshape(ROWS, WIDTH))


def up_grad_kernel(sc, normed, up_grad, own, far):
    total = dot(normed[...], up_grad[...], 0, 0).astype(BF16)

    @pl.when(pl.program_id(0) < 3)
    def _():
        own[...] = total

    @pl.when(pl.program_id(0) >= 3)
    def _():
        far[...] = total


def run_up_grad(sc, normed, up_grad):
    return pl.pallas_call(
        up_grad_kernel,
        grid_spec=pltpu.PrefetchScalarGridSpec(
            num_scalar_prefetch=1,
            grid=(6,),
            in_specs=[held((ROWS, WIDTH)), spec((ROWS, 512), lambda f, s: (0, lax.rem(3 * s[CORE] + f, 6)))],
            out_specs=[
                spec((WIDTH, 512), lambda f, s: (0, lax.min(f, 2))),
                spec((WIDTH, 512), lambda f, s: (0, lax.max(f - 3, 0))),
            ],
        ),
        out_shape=[jax.ShapeDtypeStruct((WIDTH, FF // 2), BF16)] * 2,
        compiler_params=params(57 << 20),
        cost_estimate=pl.CostEstimate(
            flops=2 * ROWS * WIDTH * FF, bytes_accessed=2 * ROWS * (WIDTH + FF), transcendentals=0
        ),
        name="up_grad",
    )(sc, normed.reshape(ROWS, WIDTH), up_grad)


def out_grad_kernel(sc, mixed, res_own, res_far, own, far, total):
    step = pl.program_id(0)
    grad = jnp.concatenate([res_own[...], res_far[...]], axis=0).reshape(4 * SPAN, WIDTH)
    found = dot(mixed[...].reshape(4 * SPAN, WIDTH), grad, 0, 0)

    @pl.when(step == 0)
    def _():
        total[...] = found

    @pl.when(step > 0)
    def _():
        total[...] += found

    @pl.when(step == pl.num_programs(0) - 1)
    def _():
        own[...] = total[:, own_lanes(sc)].astype(BF16)
        far[...] = total[:, far_lanes(sc)].astype(BF16)


def run_out_grad(sc, mixed, res_own, res_far):
    return pl.pallas_call(
        out_grad_kernel,
        grid_spec=pltpu.PrefetchScalarGridSpec(
            num_scalar_prefetch=1,
            grid=(HROWS // SPAN,),
            in_specs=[slab_spec(), slab_spec(2), slab_spec(2)],
            out_specs=[held((WIDTH, SIDE))] * 2,
            scratch_shapes=[pltpu.VMEM((WIDTH, WIDTH), F32)],
        ),
        out_shape=[jax.ShapeDtypeStruct((WIDTH, SIDE), BF16)] * 2,
        compiler_params=params(LESS),
        cost_estimate=pl.CostEstimate(
            flops=2 * ROWS * WIDTH * WIDTH, bytes_accessed=4 * ROWS * WIDTH, transcendentals=0
        ),
        name="out_grad",
    )(sc, mixed, res_own, res_far)


def out_kernel(sc, active, resid, dn_own, dn_far, own, far, w_down):
    step = pl.program_id(0)

    @pl.when(step == 0)
    def _():
        w_down[:, own_lanes(sc)] = dn_own[...]
        w_down[:, far_lanes(sc)] = dn_far[...]

    branch = dot(active[...].reshape(4 * SPAN, FF), w_down[...], 1, 0)
    output = jnp.where(row_valid(sc, step), resid[...].reshape(4 * SPAN, WIDTH).astype(F32) + branch, 0.0)
    output = output.astype(BF16).reshape(4, SPAN, WIDTH)
    own[...] = output[:2]
    far[...] = output[2:]


def run_out(sc, active, resid, down):
    return pl.pallas_call(
        out_kernel,
        grid_spec=pltpu.PrefetchScalarGridSpec(
            num_scalar_prefetch=1,
            grid=(HROWS // SPAN,),
            in_specs=[
                spec((4, SPAN, FF), lambda r, s: (0, r, 0)),
                slab_spec(),
                held((FF, SIDE)),
                held((FF, SIDE)),
            ],
            out_specs=[slab_spec(2)] * 2,
            scratch_shapes=[pltpu.VMEM((FF, WIDTH), BF16)],
        ),
        out_shape=[
            jax.ShapeDtypeStruct((2, HROWS, WIDTH), BF16),
            jax.ShapeDtypeStruct((2, HROWS, WIDTH), BF16),
        ],
        compiler_params=params(LESS),
        cost_estimate=pl.CostEstimate(
            flops=2 * ROWS * WIDTH * FF, bytes_accessed=ROWS * (2 * FF + 7 * WIDTH), transcendentals=0
        ),
        name="out",
    )(sc, active.reshape(4, HROWS, FF), resid, *down)


def post_kernel(sc, resid, grad_own, grad_far, cot, up_own, up_far, wo_own, wo_far, gain, *refs):
    (res_own, res_far, heads, d_gain, weight, spread) = refs
    step = pl.program_id(0)
    whole_weight(sc, step, wo_own, wo_far, weight)
    shape, slab = (4 * SPAN, WIDTH), (4, SPAN, WIDTH)
    valid = row_valid(sc, step)
    res = resid[...].reshape(shape).astype(F32)
    scale = lax.rsqrt(jnp.mean(res * res, axis=-1, keepdims=True) + EPSILON)
    unit = res * scale
    units = (4 * SPAN, FF // 2)
    back = dot(grad_own[...].reshape(units), up_own[...], 1, 1) + dot(grad_far[...].reshape(units), up_far[...], 1, 1)
    two_grad = jnp.where(valid, back, 0.0)
    gained = two_grad * gain[...]
    masked = cot[...].reshape(shape).astype(F32)
    grad = masked + scale * (gained - unit * jnp.mean(gained * unit, axis=-1, keepdims=True))
    low = grad.astype(BF16)
    res_own[...] = low.reshape(slab)[:2]
    res_far[...] = low.reshape(slab)[2:]
    gain_sum = jnp.sum(two_grad * unit, axis=0, keepdims=True)

    @pl.when(step == 0)
    def _():
        d_gain[...] = gain_sum

    @pl.when(step > 0)
    def _():
        d_gain[...] += gain_sum

    spread[...] = dot(low, weight[...], 1, 1).astype(BF16).reshape(slab)
    for pair in range(HEADS // 2):
        lanes = slice(pair * 128, (pair + 1) * 128)
        for side in range(2):
            one, two = spread[2 * side, :, lanes], spread[2 * side + 1, :, lanes]
            half = slice(side * 128, (side + 1) * 128)
            heads[2 * pair, :, half] = jnp.concatenate([one[:, :HEAD], two[:, :HEAD]], axis=1)
            heads[2 * pair + 1, :, half] = jnp.concatenate([one[:, HEAD:], two[:, HEAD:]], axis=1)


def run_post(sc, resid, up_grad, cotangent, up, wo, gain):
    side = lambda which: spec((4, SPAN, FF // 2), lambda r, s: (0, r, s[CORE] if which == 0 else 1 - s[CORE]))
    up_grad = up_grad.reshape(4, HROWS, FF)
    return pl.pallas_call(
        post_kernel,
        grid_spec=pltpu.PrefetchScalarGridSpec(
            num_scalar_prefetch=1,
            grid=(HROWS // SPAN,),
            in_specs=[
                slab_spec(),
                side(0),
                side(1),
                slab_spec(),
                held((WIDTH, FF // 2)),
                held((WIDTH, FF // 2)),
                held((WIDTH, SIDE)),
                held((WIDTH, SIDE)),
                held((1, WIDTH)),
            ],
            out_specs=[slab_spec(2)] * 2 + [heads_spec(), held((1, WIDTH))],
            scratch_shapes=[
                pltpu.VMEM((WIDTH, WIDTH), BF16),
                pltpu.VMEM((4, SPAN, WIDTH), BF16),
            ],
        ),
        out_shape=[
            jax.ShapeDtypeStruct((2, HROWS, WIDTH), BF16),
            jax.ShapeDtypeStruct((2, HROWS, WIDTH), BF16),
            jax.ShapeDtypeStruct((HEADS, HROWS, 4 * HEAD), BF16),
            jax.ShapeDtypeStruct((1, WIDTH), F32),
        ],
        compiler_params=params(VMEM),
        cost_estimate=pl.CostEstimate(
            flops=2 * ROWS * WIDTH * (WIDTH + FF), bytes_accessed=ROWS * (16 * WIDTH + 2 * FF), transcendentals=0
        ),
        name="post",
    )(sc, resid, up_grad, up_grad, cotangent, *up, *wo, gain)


def unmix_kernel(count, carried, sc, v_own, v_far, grad_heads, mean, exps, inverse, *refs):
    refs = refs[2:] if carried else refs
    outs, (own, far, grads, mask, adder, bound, out_sems) = refs[: 4 * count], refs[4 * count :]
    place = sc[PLACE]
    step = pl.program_id(0)

    def leave(slot):
        return [
            pltpu.make_async_copy(
                grads.at[slot, pl.ds(pl.multiple_of((place ^ rel) * SUBS * HALF, SUBS * HALF), SUBS * HALF)],
                outs[4 * slot + rel],
                out_sems.at[slot, rel],
            )
            for rel in range(4)
        ]

    fill_mask(sc, mask)

    @pl.when(step == 0)
    def _():
        lane = lax.broadcasted_iota(jnp.int32, (4 * HEAD, 128), 0) // HEAD
        column = lax.broadcasted_iota(jnp.int32, (4 * HEAD, 128), 1)
        adder[...] = jnp.where((lane == column) | (lane + 4 == column), -1.0, 0.0).astype(BF16)
        row = lax.broadcasted_iota(jnp.int32, (LMAX, 128), 0)
        item = lax.broadcasted_iota(jnp.int32, (LMAX, 128), 1)
        length = jnp.where(item % 4 == 0, sc[LENGTHS], sc[LENGTHS + 1])
        length = jnp.where(item % 4 == 2, sc[LENGTHS + 2], length)
        length = jnp.where(item % 4 == 3, sc[LENGTHS + 3], length)
        bound[...] = jnp.where((item < 8) & (row < length), 1.0, 0.0).astype(BF16)

    high_lanes = lax.broadcasted_iota(jnp.int32, (HROWS, 128), 1) < 4
    for head in range(PHEADS):
        weights = exps[head]
        low = (grad_heads[head].astype(F32) * inverse[head].astype(F32)).astype(BF16)
        product = low.astype(F32) * mean[head]
        coarse = product.astype(BF16)
        fine = (product - coarse.astype(F32)).astype(BF16)
        delta = dot(coarse, adder[...], 1, 0) + dot(fine, adder[...], 1, 0)
        coarse = delta.astype(BF16)
        fine = (delta - coarse.astype(F32)).astype(BF16)
        left = jnp.concatenate([low, jnp.where(high_lanes, coarse, fine)], axis=1)
        score = dot(left, jnp.concatenate([v_own[head], v_far[head], bound[...]], axis=1), 1, 1)
        grads[step, head_rows(head)] = (score * weights.astype(F32)).astype(BF16)
        back = (dot(weights, low, 0, 0) * mask[...].astype(F32)).astype(BF16)
        own[head] = back[:, : 2 * HEAD]
        far[head] = back[:, 2 * HEAD :]
    for which in range(count):

        @pl.when(step == which)
        def _():
            for copy in leave(which):
                copy.start()
            if which == count - 1:
                for slot in range(count):
                    for copy in leave(slot):
                        copy.wait()


def run_unmix(sc, planes, v_own, v_far, grad_heads, mean, exps, inverse, carry):
    carry, count = list(carry), len(planes)
    return pl.pallas_call(
        partial(unmix_kernel, count, bool(carry)),
        grid_spec=pltpu.PrefetchScalarGridSpec(
            num_scalar_prefetch=1,
            grid=(count,),
            in_specs=[
                plane_spec(planes, LMAX, 2 * HEAD),
                plane_spec(planes, LMAX, 2 * HEAD),
                plane_spec(planes, HROWS, 4 * HEAD),
                plane_spec(planes, HROWS, 4 * HEAD),
                plane_spec(planes, HROWS, LMAX),
                plane_spec(planes, HROWS, 4 * HEAD),
            ]
            + anywhere(len(carry)),
            out_specs=anywhere(4 * count) + [plane_spec(planes, LMAX, 2 * HEAD)] * 2,
            scratch_shapes=[
                pltpu.VMEM((count, 4 * SUBS * HALF, LMAX), BF16),
                pltpu.VMEM((LMAX, 4 * HEAD), BF16),
                pltpu.VMEM((4 * HEAD, 128), BF16),
                pltpu.VMEM((LMAX, 128), BF16),
                pltpu.SemaphoreType.DMA((count, 4)),
            ],
        ),
        out_shape=[jax.ShapeDtypeStruct((SUBS * HALF, LMAX), BF16)] * (4 * count)
        + [jax.ShapeDtypeStruct((HEADS, LMAX, 2 * HEAD), BF16)] * 2,
        input_output_aliases={7 + i: 4 * count + i for i in range(len(carry))},
        compiler_params=params(VMEM),
        cost_estimate=pl.CostEstimate(
            flops=3 * HEADS * HROWS * LMAX * 4 * HEAD,
            bytes_accessed=HEADS * (2 * HROWS * LMAX + 5 * HROWS * 256 + 4 * LMAX * 256),
            transcendentals=0,
        ),
        name="unmix",
    )(sc, v_own, v_far, grad_heads, mean, exps, inverse, *carry)


def close_kernel(sc, tok, res_own, res_got, own, far, gain, w_own, w_far, *refs):
    (tok_grad, d_value, d_gain, total, weight) = refs
    step = pl.program_id(0)
    whole_weight(sc, step, w_own, w_far, weight)
    core = sc[CORE]
    tok_grad[:, :, core] = res_own[...].astype(F32)
    tok_grad[:, :, 1 - core] = res_got[...].astype(F32)
    runs = tok.shape[1]
    rows = runs * 128
    for item in range(2):
        lanes = slice(item * HEAD, (item + 1) * HEAD)
        pieces = [
            add_low(own[head, :, lanes], far[head, :, lanes]) for head in range(HEADS)
        ]
        back = jnp.concatenate(pieces, axis=1)
        x = tok[item].reshape(rows, WIDTH).astype(F32)
        scale = lax.rsqrt(jnp.mean(x * x, axis=-1, keepdims=True) + EPSILON)
        unit = x * scale
        normed = (unit * gain[...]).astype(BF16)
        normed_grad = dot(back, weight[...], 1, 1)
        gained = normed_grad * gain[...]
        update = scale * (gained - unit * jnp.mean(gained * unit, axis=-1, keepdims=True))
        tok_grad[item] += update.reshape(runs, 2, HALF, WIDTH)
        gain_sum = jnp.sum(normed_grad * unit, axis=0, keepdims=True)
        value_sum = dot(normed, back, 0, 0)
        if item == 0:
            gain_total, value_total = gain_sum, value_sum
        else:
            gain_total, value_total = gain_total + gain_sum, value_total + value_sum

    @pl.when(step == 0)
    def _():
        d_gain[...] = gain_total
        total[...] = value_total

    @pl.when(step > 0)
    def _():
        d_gain[...] += gain_total
        total[...] += value_total

    @pl.when(step == pl.num_programs(0) - 1)
    def _():
        low = total[...].astype(BF16)
        d_value[0] = low[:, :SIDE]
        d_value[1] = low[:, SIDE:]


def run_close(sc, tokens, res_own, res_got, own, far, gain, w_own, w_far):
    runs = 2
    slab = (2, RUNS, 2, HALF, WIDTH)
    half = (2, RUNS, HALF, WIDTH)
    whole_spec = spec((2, runs, 2, HALF, WIDTH), lambda j, s: (0, j, 0, 0, 0))
    half_spec = spec((2, runs, HALF, WIDTH), lambda j, s: (0, j, 0, 0))
    back_spec = spec((HEADS, runs * 128, 2 * HEAD), lambda j, s: (0, j, 0))
    return pl.pallas_call(
        close_kernel,
        grid_spec=pltpu.PrefetchScalarGridSpec(
            num_scalar_prefetch=1,
            grid=(RUNS // runs,),
            in_specs=[whole_spec]
            + [half_spec] * 2
            + [back_spec, back_spec, held((1, WIDTH)), held((WIDTH, SIDE)), held((WIDTH, SIDE))],
            out_specs=[whole_spec, held((2, WIDTH, SIDE)), held((1, WIDTH))],
            scratch_shapes=[pltpu.VMEM((WIDTH, WIDTH), F32), pltpu.VMEM((WIDTH, WIDTH), BF16)],
        ),
        out_shape=[
            jax.ShapeDtypeStruct(slab, F32),
            jax.ShapeDtypeStruct((2, WIDTH, SIDE), BF16),
            jax.ShapeDtypeStruct((1, WIDTH), F32),
        ],
        compiler_params=params(LESS),
        cost_estimate=pl.CostEstimate(
            flops=4 * 2 * LMAX * WIDTH * WIDTH, bytes_accessed=38 * LMAX * WIDTH, transcendentals=0
        ),
        name="close",
    )(
        sc,
        tokens.reshape(slab),
        *(x.reshape(half) for x in (res_own, res_got)),
        own,
        far,
        gain,
        w_own,
        w_far,
    )


def join_kernel(sc, own, got, output):
    output[:, :, sc[CORE]] = own[...].astype(F32)
    output[:, :, 1 - sc[CORE]] = got[...].astype(F32)


def run_join(sc, own, got):
    half = (2, RUNS, HALF, WIDTH)
    half_spec = spec((2, 2, HALF, WIDTH), lambda j, s: (0, j, 0, 0))
    return pl.pallas_call(
        join_kernel,
        grid_spec=pltpu.PrefetchScalarGridSpec(
            num_scalar_prefetch=1,
            grid=(RUNS // 2,),
            in_specs=[half_spec, half_spec],
            out_specs=spec((2, 2, 2, HALF, WIDTH), lambda j, s: (0, j, 0, 0, 0)),
        ),
        out_shape=jax.ShapeDtypeStruct((2, RUNS, 2, HALF, WIDTH), F32),
        compiler_params=params(LESS),
        cost_estimate=pl.CostEstimate(flops=0, bytes_accessed=12 * LMAX * WIDTH, transcendentals=0),
        name="join",
    )(sc, own.reshape(half), got.reshape(half))


PACK_DOWN, PACK_UP, PACK_OUT, PACK_VALUE, PACK_GAIN, PACK = 0, 192, 384, 432, 480, 496


def pack_kernel(sc, down, up, out, value, gain, down_far, up_far, out_far, value_far, gain_far, packed):
    first = sc[CORE] == 0

    def both(own, far, lanes):
        own, far = own[:, lanes], far[:, lanes]
        return jnp.concatenate([jnp.where(first, own, far), jnp.where(first, far, own)], axis=0)

    def side(own, far):
        return both(own, far, own_lanes(sc))

    packed[PACK_DOWN:PACK_UP] = side(down, down_far)
    for j in range(4):
        lanes = pl.ds(pl.multiple_of((4 * sc[CORE] + j) * SIDE, 128), SIDE)
        packed[PACK_UP + 48 * j : PACK_UP + 48 * (j + 1)] = both(up, up_far, lanes)
    packed[PACK_OUT:PACK_VALUE] = side(out, out_far)
    packed[PACK_VALUE:PACK_GAIN] = side(value, value_far)
    packed[PACK_GAIN:] = both(gain, gain_far, slice(0, SIDE))


def run_pack(sc, own, far):
    return pl.pallas_call(
        pack_kernel,
        grid_spec=pltpu.PrefetchScalarGridSpec(
            num_scalar_prefetch=1,
            grid=(1,),
            in_specs=[held(x.shape) for x in (*own, *far)],
            out_specs=held((PACK, SIDE)),
        ),
        out_shape=jax.ShapeDtypeStruct((PACK, SIDE), BF16),
        compiler_params=params(VMEM),
        cost_estimate=pl.CostEstimate(flops=0, bytes_accessed=6 * PACK * SIDE, transcendentals=0),
        name="pack",
    )(sc, *own, *far)


def chip_of(sc, k, rel):
    return plane_of(k, sc) * 4 + (sc[PLACE] ^ rel)


def place_kernel(moves, sc, *refs):
    pieces, targets, sems = refs[:16], refs[16:-1], refs[-1]
    copies = []
    for index, piece in enumerate(pieces):
        chip = chip_of(sc, index // 4, index % 4)
        for which, (start, count, lane, target, step, offset, column) in enumerate(moves):
            rows = pl.ds(pl.multiple_of(chip * step + offset, 16), count)
            copies.append(
                pltpu.make_async_copy(
                    piece.at[pl.ds(start, count), pl.ds(lane, SIDE)],
                    targets[target].at[rows, pl.ds(column, SIDE)],
                    sems.at[index, which],
                )
            )
    for copy in copies:
        copy.start()
    for copy in copies:
        copy.wait()


def run_place(sc, pieces, moves, shapes):
    return pl.pallas_call(
        partial(place_kernel, moves),
        grid_spec=pltpu.PrefetchScalarGridSpec(
            num_scalar_prefetch=1,
            grid=(1,),
            in_specs=anywhere(16),
            out_specs=[held(shape) for shape in shapes],
            scratch_shapes=[pltpu.SemaphoreType.DMA((16, len(moves)))],
        ),
        out_shape=[jax.ShapeDtypeStruct(shape, BF16) for shape in shapes],
        compiler_params=params(VMEM),
        cost_estimate=pl.CostEstimate(
            flops=0, bytes_accessed=4 * sum(a * b for a, b in shapes), transcendentals=0
        ),
        name="place",
    )(sc, *pieces)


def place_weights(sc, pieces):
    moves = (
        (PACK_DOWN, 192, 0, 0, 192, 0, 0),
        *((PACK_UP + 48 * j, 48, 0, 1, 48, 0, j * SIDE) for j in range(4)),
        (PACK_OUT, 48, 0, 2, 48, 0, 0),
        (PACK_VALUE, 48, 0, 3, 48, 0, 0),
        (PACK_GAIN, 16, 0, 4, 16, 0, 0),
    )
    shapes = [(FF, SIDE), (WIDTH, FF // 2), (WIDTH, SIDE), (WIDTH, SIDE), (256, SIDE)]
    return run_place(sc, pieces, moves, shapes)


def collect_kernel(sc, *refs):
    outs = refs[24:]
    for k in range(PLANES):

        @pl.when(pl.program_id(0) == k)
        def _():
            for rel in range(4):
                down, down_got, up, up_got, out, out_got = refs[6 * rel : 6 * rel + 6]
                packed = outs[4 * k + rel]
                packed[PACK_DOWN:PACK_UP] = add_low(down[...], down_got[...])
                for j in range(4):
                    lanes = slice(j * SIDE, (j + 1) * SIDE)
                    packed[PACK_UP + 48 * j : PACK_UP + 48 * (j + 1)] = add_low(up[:, lanes], up_got[:, lanes])
                packed[PACK_OUT:PACK_VALUE] = add_low(out[...], out_got[...])


def run_collect(sc, *sides):
    def rows(x, rel):
        return spec((x.shape[0] // 16, x.shape[1]), lambda k, s: (chip_of(s, k, rel), 0))

    return pl.pallas_call(
        collect_kernel,
        grid_spec=pltpu.PrefetchScalarGridSpec(
            num_scalar_prefetch=1,
            grid=(PLANES,),
            in_specs=[rows(x, rel) for rel in range(4) for x in sides],
            out_specs=[held((PACK_VALUE, SIDE))] * 16,
        ),
        out_shape=[jax.ShapeDtypeStruct((PACK_VALUE, SIDE), BF16)] * 16,
        compiler_params=params(LESS),
        cost_estimate=pl.CostEstimate(flops=0, bytes_accessed=3 * 16 * PACK_VALUE * SIDE * 2, transcendentals=0),
        name="collect",
    )(sc, *(x for _ in range(4) for x in sides))


def add_kernel(groups, *refs):
    for group, total in zip(groups, refs[-len(groups) :]):
        value = refs[group[0]][...].astype(F32)
        for index in group[1:]:
            value = value + refs[index][...].astype(F32)
        total[...] = value.astype(total.dtype)


def run_add(groups, values, dtype):
    shape = values[0].shape
    here = pl.BlockSpec(memory_space=pltpu.VMEM)
    return pl.pallas_call(
        partial(add_kernel, groups),
        in_specs=[here] * len(values),
        out_specs=[here] * len(groups),
        out_shape=[jax.ShapeDtypeStruct(shape, dtype)] * len(groups),
        compiler_params=params(LESS),
        cost_estimate=pl.CostEstimate(
            flops=0, bytes_accessed=2 * shape[0] * shape[1] * (len(values) + len(groups)), transcendentals=0
        ),
        name="add",
    )(*values)


DEVICES = 32
TO_CORE, TO_X, TO_Y = 1, 2, 4


def swap(x, bit):
    return lax.ppermute(x, BOTH, [(d, d ^ bit) for d in range(DEVICES)])


def ring(x, way=1):
    return lax.ppermute(x, BOTH, [(d, (d + 8 * way) % DEVICES) for d in range(DEVICES)])


def pick(x, index, axis=0):
    return lax.dynamic_index_in_dim(x, index, axis, keepdims=False)


def ordered(flag, one, two, axis=0, joined=jnp.stack):
    return jnp.where(flag == 0, joined([one, two], axis), joined([two, one], axis))


def add_low(one, two):
    return (one.astype(F32) + two.astype(F32)).astype(BF16)


STEPS = (
    ((0, 0, 1), (0, 1, 0), (1, 0, 0)),
    ((1, 0, 1), (0, 1, 1), (2, 0, 0)),
    ((2, 0, 1), (1, 1, 0), (3, 0, 0)),
    ((1, 1, 1), (2, 1, 1), (2, 1, 0)),
    ((3, 0, 1), (3, 1, 0), (3, 1, 1)),
)


def gather_step(have, step):
    by_x, by_y, by_z = STEPS[step]
    return {
        **have,
        by_z: ring(have[by_z[0] - 1, by_z[1], by_z[2]]),
        by_x: swap(have[by_x[0], by_x[1], 0], TO_X),
        by_y: swap(have[by_y[0], 0, by_y[2]], TO_Y),
    }


def in_order(have):
    return [have[k, y, x] for k in range(4) for y in range(2) for x in range(2)]


def by_place(shares, planes=range(PLANES)):
    return {(k, i // 2, i % 2): shares[4 * at + i] for at, k in enumerate(planes) for i in range(4)}


def scatter_send(have, step):
    by_x, by_y, by_z = STEPS[len(STEPS) - 1 - step]
    got = (ring(have[by_z], -1), swap(have[by_x], TO_X), swap(have[by_y], TO_Y))
    return {at: value for at, value in have.items() if at not in (by_x, by_y, by_z)}, got


def scatter_add(have, got, step):
    by_x, by_y, by_z = STEPS[len(STEPS) - 1 - step]
    targets = ((by_z[0] - 1, by_z[1], by_z[2]), (by_x[0], by_x[1], 0), (by_y[0], 0, by_y[2]))
    sums = list(dict.fromkeys(targets))
    groups = [(len(got) + i, *(j for j in range(len(got)) if targets[j] == at)) for i, at in enumerate(sums)]
    values = [*got, *(have[at] for at in sums)]
    dtype = F32 if step == len(STEPS) - 1 else BF16
    if values[0].shape[1] == LMAX:
        totals = run_add(groups, values, dtype)
    else:
        totals = [sum(values[i].astype(F32) for i in group).astype(dtype) for group in groups]
    return {**have, **dict(zip(sums, totals))}


together = lax.optimization_barrier


def chip_shards(tokens, lengths, rand_mix, w_value, w_out, w_up, w_down, gain_mix, gain_ffn, grad_out):
    wide = lax.axis_index("wide")
    core = lax.axis_index("narrow")
    z, y, x = wide // 4, (wide // 2) % 2, wide % 2
    other = lambda value: swap(value, TO_CORE)
    side = partial(ordered, core, joined=jnp.concatenate)
    slab = (2, RUNS, 2, HALF, WIDTH)
    tokens, grad_out = tokens.reshape(slab), grad_out.reshape(slab)

    gains = jnp.pad(jnp.concatenate([gain_mix, gain_ffn])[None], ((0, 7), (0, SIDE - 48)))
    own = (w_down, w_up, w_out, w_value, gains)
    far = tuple(other(value) for value in own)
    near_sc = jnp.concatenate([jnp.stack([core, z, wide % 4]).astype(jnp.int32), lengths, lengths])
    weights = {(0, 0, 0): run_pack(near_sc, own, far)}

    rand = rand_mix.reshape(3, 2, HALF, LMAX)
    blocks = side(pick(rand, core, 1), other(pick(rand, 1 - core, 1)), 0)
    weights, rands, late_tokens, late_grad = together(
        (gather_step(weights, 0), {(0, 0, 0): blocks.reshape(SUBS * HALF, LMAX)}, tokens, grad_out)
    )
    weights, tokens_far = together((gather_step(weights, 1), other(pick(late_tokens, 1 - core, 2))))
    weights, grad_far = together((gather_step(weights, 2), other(pick(late_grad, 1 - core, 2))))
    weights, far_lengths = together((gather_step(weights, 3), other(lengths)))
    sc = jnp.concatenate([near_sc[:5], far_lengths])
    weights, rands = together((gather_step(weights, 4), rands))

    rands = gather_step(rands, 0)
    down, up, out, value, gain_rows = place_weights(sc, in_order(weights))
    rands, value, value_far, gain_rows, out, down, up = together(
        (rands, value, other(value), gain_rows, out, down, up)
    )
    gain_rows = gain_rows.reshape(16, 2, 8, SIDE)[:, :, 0]
    gain_one = gain_rows[..., :24].reshape(1, WIDTH).astype(F32)
    gain_two = gain_rows[..., 24:48].reshape(1, WIDTH).astype(F32)
    rands = gather_step(rands, 1)
    v_own = run_values(sc, tokens.reshape(2, LMAX, WIDTH), gain_one, value, value_far)
    rands, v_own, out, down, up = together((rands, v_own, (out, other(out)), down, up))
    rands, v_own, v_far, grad_far, down, up = together(
        (gather_step(rands, 2), v_own, other(v_own), grad_far, down, up)
    )
    rands = gather_step(rands, 3)
    masked = run_masked(sc, grad_out, grad_far)
    rands, v_far, masked, down, up = together((rands, v_far, masked, down, up))
    near = [rands[k, y_at, x_at] for k in range(3) for y_at in range(2) for x_at in range(2)]
    rands = gather_step(rands, 4)
    mixing = run_mix(sc, (0, 1, 2), near, v_own, v_far, ())
    rands, down, up, mixing = together((rands, down, up, mixing))
    heads, mean, exps, inverse = run_mix(sc, (3,), in_order(rands)[12:], v_own, v_far, mixing)
    down, up = (down, other(down)), (up, other(up))

    mixed, resid, normed = run_pre(sc, tokens, tokens_far, heads, out, gain_two)
    active, up_grad = run_units(sc, normed, masked, up, down)
    res_own, res_far, grad_heads, d_gain_two = run_post(sc, resid, up_grad, masked, up, out, gain_two)

    backward = lambda planes, carry: run_unmix(sc, planes, v_own, v_far, grad_heads, mean, exps, inverse, carry)
    *far, back_own, back_far = backward((3,), ())
    far, back_own, back_far, res_got = together((far, back_own, back_far, other(res_far)))
    have, got = scatter_send(by_place(far, (3,)), 0)
    *near, back_own, back_far = backward((2, 1, 0), (back_own, back_far))
    have, got, near, back_own, back_far = together((have, got, near, back_own, back_far))
    have = scatter_add({**have, **by_place(near, (2, 1, 0))}, got, 0)

    have, got = scatter_send(have, 1)
    up_own, up_far = run_up_grad(sc, normed, up_grad)
    have, got, up_own, up_far, back_got = together((have, got, up_own, up_far, other(back_far)))
    have = scatter_add(have, got, 1)

    have, got = scatter_send(have, 2)
    down_own, down_far = run_down_grad(sc, active, masked)
    have, got, down_own, down_far, up_got = together((have, got, down_own, down_far, other(up_far)))
    have = scatter_add(have, got, 2)

    have, got = scatter_send(have, 3)
    d_out_own, d_out_far = run_out_grad(sc, mixed, res_own, res_far)
    packed = run_collect(sc, down_own, other(down_far), up_own, up_got, d_out_own, other(d_out_far))
    have, got, packed = together((have, got, packed))
    have = scatter_add(have, got, 3)

    have, got = scatter_send(have, 4)
    out_own, out_far = run_out(sc, active, resid, down)
    have, got, packed, out_own, out_far = together((have, got, packed, out_own, out_far))
    rand_sum = scatter_add(have, got, 4)[0, 0, 0].reshape(2, 3, HALF, LMAX)

    sums, got = scatter_send(by_place(packed), 0)
    tokens_grad, d_value, d_gain_one = run_close(
        sc, tokens, res_own, res_got, back_own, back_got, gain_one, value, value_far
    )
    gain_pair = jnp.concatenate([d_gain_one, d_gain_two]).reshape(2, 16, 1, 48).astype(BF16)
    gain_pair = jnp.pad(gain_pair, ((0, 0), (0, 0), (0, 15), (0, SIDE - 48)))
    small = jnp.concatenate([d_value.reshape(2, 16, 48, SIDE), gain_pair], 2)
    sums, got, tokens_grad, small, out_got = together((sums, got, tokens_grad, small, other(out_far)))
    sums = scatter_add(sums, got, 0)

    sums, got = scatter_send(sums, 1)
    small = add_low(pick(small, core), other(pick(small, 1 - core))).reshape(4, 2, 2, 64, SIDE)
    output = run_join(sc, out_own, out_got)
    sums, got, small, output = together((sums, got, small, output))
    sums = scatter_add(sums, got, 1)

    sums, got = scatter_send(sums, 2)
    small = add_low(pick(small, x, 2), swap(pick(small, 1 - x, 2), TO_X))
    sums, got, small = together((sums, got, small))
    sums = scatter_add(sums, got, 2)

    sums, got = scatter_send(sums, 3)
    small = add_low(pick(small, y, 1), swap(pick(small, 1 - y, 1), TO_Y))
    blocks, blocks_far = pick(rand_sum, core), other(pick(rand_sum, 1 - core))
    sums, got, small, blocks, blocks_far = together((sums, got, small, blocks, blocks_far))
    sums = scatter_add(sums, got, 3)

    sums, got = scatter_send(sums, 4)
    small_sum = pick(small, z).astype(F32)
    for k in range(1, PLANES):
        small_sum = small_sum + ring(pick(small, lax.rem(z + PLANES - k, PLANES)), -k).astype(F32)
    sums, got, small_sum = together((sums, got, small_sum))
    big_sum = scatter_add(sums, got, 4)[0, 0, 0]
    big_far, small_far = other(big_sum), other(small_sum)

    rows_of = lambda value, rows: pick(value.reshape(-1, 2, rows, SIDE), core, 1)
    mine = lambda own, far, rows: side(rows_of(own, rows)[0], rows_of(far, rows)[0], 1)
    down_shard = mine(big_sum[PACK_DOWN:PACK_UP], big_far[PACK_DOWN:PACK_UP], 96)
    up_side = lambda value: rows_of(value[PACK_UP:PACK_OUT], 24).transpose(1, 0, 2).reshape(24, 4 * SIDE)
    up_shard = side(up_side(big_sum), up_side(big_far), 1)
    outproj_shard = mine(big_sum[PACK_OUT:PACK_VALUE], big_far[PACK_OUT:PACK_VALUE], 24)
    value_shard = mine(small_sum[:48], small_far[:48], 24)
    gains_pair = ordered(core, small_sum[48, :48], small_far[48, :48])
    gain_pair = pick(gains_pair.reshape(2, 2, 24), core, 1)

    rand_shard = ordered(core, blocks, blocks_far, 1)

    return (
        output.reshape(2, LMAX, WIDTH),
        tokens_grad.reshape(2, LMAX, WIDTH),
        rand_shard.reshape(3 * 128, LMAX),
        value_shard,
        outproj_shard,
        up_shard,
        down_shard,
        gain_pair[0],
        gain_pair[1],
    )


def rms_norm(values, gain):
    scale = lax.rsqrt(jnp.mean(values * values, axis=-1, keepdims=True) + EPSILON)
    return values * scale * gain


def split_heads(block):
    return block.reshape(LMAX, HEADS, HEAD).transpose(1, 0, 2)


def merge_heads(block):
    return block.transpose(1, 0, 2).reshape(LMAX, HEADS * HEAD)


def masked_scores(key_mask, rand_head):
    return jnp.where(key_mask[None, :] > 0, rand_head.astype(jnp.float32), -1e30)


def head_forward(key_mask, paired):
    rand_head, value_head = paired
    scores = masked_scores(key_mask, rand_head)
    row_peak = jnp.max(scores, axis=-1, keepdims=True)
    exponent = jnp.exp(scores - row_peak)
    denom_sum = jnp.sum(exponent, axis=-1, keepdims=True)
    attention = exponent / denom_sum * key_mask[:, None]
    mixed = jnp.dot(attention.astype(jnp.bfloat16), value_head, preferred_element_type=jnp.float32)
    return (mixed.astype(jnp.bfloat16), row_peak + jnp.log(denom_sum))


def head_backward(key_mask, paired):
    rand_head, value_head, mix_grad, log_total = paired
    scores = masked_scores(key_mask, rand_head)
    attention = jnp.exp(scores - log_total) * key_mask[:, None]
    prob_grad = jnp.einsum("id,jd->ij", mix_grad, value_head, preferred_element_type=jnp.float32)
    value_grad = jnp.einsum(
        "ij,id->jd", attention.astype(jnp.bfloat16), mix_grad, preferred_element_type=jnp.float32
    )
    score_grad = attention * (prob_grad - jnp.sum(prob_grad * attention, axis=-1, keepdims=True))
    return (score_grad, value_grad)


def shards(tokens, lengths, rand_mix, w_value, w_out, w_up, w_down, gain_mix, gain_ffn, grad_out):
    item_count = tokens.shape[0]
    width = tokens.shape[2]
    row_count = item_count * LMAX
    tokens_flat = tokens.reshape(row_count, width).astype(jnp.float32)
    positions = jnp.arange(LMAX, dtype=jnp.int32)
    valid_table = (positions[None, :] < lengths[:, None]).astype(jnp.float32)
    row_valid = valid_table.reshape(row_count, 1)
    forward_set = (
        lax.all_gather(rand_mix, ("wide", "narrow"), axis=0, tiled=True),
        lax.all_gather(w_value, ("wide", "narrow"), axis=0, tiled=True),
        lax.all_gather(w_out, ("wide", "narrow"), axis=0, tiled=True),
        lax.all_gather(w_up, ("wide", "narrow"), axis=0, tiled=True),
        lax.all_gather(w_down, ("wide", "narrow"), axis=0, tiled=True),
        lax.all_gather(gain_mix, ("wide", "narrow"), axis=0, tiled=True),
        lax.all_gather(gain_ffn, ("wide", "narrow"), axis=0, tiled=True),
    )
    rand_all, value_all, out_all, up_all, down_all, gain_first, gain_second = forward_set
    normed = rms_norm(tokens_flat, gain_first.astype(jnp.float32)).astype(jnp.bfloat16)
    values = jnp.dot(normed, value_all, preferred_element_type=jnp.float32).astype(jnp.bfloat16)
    rand_heads = rand_all.reshape(HEADS, LMAX, LMAX)
    mixed_parts = []
    totals_kept = []
    for item_index in range(item_count):
        item_values = split_heads(values[item_index * LMAX : (item_index + 1) * LMAX])
        mixed_heads, log_total = lax.map(
            partial(head_forward, valid_table[item_index]), (rand_heads, item_values)
        )
        mixed_parts.append(merge_heads(mixed_heads))
        totals_kept.append(log_total)
    mixed = jnp.concatenate(mixed_parts, axis=0)
    residual = tokens_flat + jnp.dot(mixed, out_all, preferred_element_type=jnp.float32)
    normed_two = rms_norm(residual, gain_second.astype(jnp.float32)).astype(jnp.bfloat16)
    up_proj = jnp.dot(normed_two, up_all, preferred_element_type=jnp.float32)
    active = jax.nn.gelu(up_proj).astype(jnp.bfloat16)
    branch = jnp.dot(active, down_all, preferred_element_type=jnp.float32)
    output = row_valid * (residual + branch)
    back_set = (
        lax.all_gather(rand_mix, ("wide", "narrow"), axis=0, tiled=True),
        lax.all_gather(w_value, ("wide", "narrow"), axis=0, tiled=True),
        lax.all_gather(w_out, ("wide", "narrow"), axis=0, tiled=True),
        lax.all_gather(w_up, ("wide", "narrow"), axis=0, tiled=True),
        lax.all_gather(w_down, ("wide", "narrow"), axis=0, tiled=True),
        lax.all_gather(gain_mix, ("wide", "narrow"), axis=0, tiled=True),
        lax.all_gather(gain_ffn, ("wide", "narrow"), axis=0, tiled=True),
    )
    rand_back, value_back, out_back, up_back, down_back, gain_back_one, gain_back_two = back_set
    cotangent = grad_out.reshape(row_count, width).astype(jnp.float32)
    masked = row_valid * cotangent
    branch_grad = masked.astype(jnp.bfloat16)
    grad_down = jnp.einsum("rk,rd->kd", active, branch_grad, preferred_element_type=jnp.float32)
    active_grad = jnp.einsum(
        "rd,kd->rk", branch_grad, down_back, preferred_element_type=jnp.float32
    )
    gelu_value, gelu_pull = jax.vjp(jax.nn.gelu, up_proj)
    up_grad = gelu_pull(active_grad)[0].astype(jnp.bfloat16)
    grad_up = jnp.einsum("rd,rk->dk", normed_two, up_grad, preferred_element_type=jnp.float32)
    normed_two_grad = jnp.einsum("rk,dk->rd", up_grad, up_back, preferred_element_type=jnp.float32)
    norm_value, norm_pull = jax.vjp(rms_norm, residual, gain_back_two.astype(jnp.float32))
    residual_part, gain_two_grad = norm_pull(normed_two_grad)
    residual_grad = masked + residual_part
    attn_grad = residual_grad.astype(jnp.bfloat16)
    grad_outproj = jnp.einsum("rd,re->de", mixed, attn_grad, preferred_element_type=jnp.float32)
    mixed_grad = jnp.einsum(
        "re,de->rd", attn_grad, out_back, preferred_element_type=jnp.float32
    ).astype(jnp.bfloat16)
    rand_heads_back = rand_back.reshape(HEADS, LMAX, LMAX)
    rand_grad = jnp.zeros((HEADS, LMAX, LMAX), jnp.float32)
    value_parts = []
    for item_index in range(item_count):
        lower_row = item_index * LMAX
        upper_row = lower_row + LMAX
        item_values = split_heads(values[lower_row:upper_row])
        item_mix_grad = split_heads(mixed_grad[lower_row:upper_row])
        score_grad, value_grad = lax.map(
            partial(head_backward, valid_table[item_index]),
            (rand_heads_back, item_values, item_mix_grad, totals_kept[item_index]),
        )
        rand_grad = rand_grad + score_grad
        value_parts.append(merge_heads(value_grad))
    values_grad = jnp.concatenate(value_parts, axis=0).astype(jnp.bfloat16)
    grad_value = jnp.einsum("rd,re->de", normed, values_grad, preferred_element_type=jnp.float32)
    normed_grad = jnp.einsum(
        "re,de->rd", values_grad, value_back, preferred_element_type=jnp.float32
    )
    norm_first, first_pull = jax.vjp(rms_norm, tokens_flat, gain_back_one.astype(jnp.float32))
    token_part, gain_one_grad = first_pull(normed_grad)
    tokens_grad = residual_grad + token_part
    rand_flat = rand_grad.reshape(HEADS * LMAX, LMAX)
    all_shards = (
        lax.psum_scatter(rand_flat, ("wide", "narrow"), scatter_dimension=0, tiled=True),
        lax.psum_scatter(grad_value, ("wide", "narrow"), scatter_dimension=0, tiled=True),
        lax.psum_scatter(grad_outproj, ("wide", "narrow"), scatter_dimension=0, tiled=True),
        lax.psum_scatter(grad_up, ("wide", "narrow"), scatter_dimension=0, tiled=True),
        lax.psum_scatter(grad_down, ("wide", "narrow"), scatter_dimension=0, tiled=True),
        lax.psum_scatter(gain_one_grad, ("wide", "narrow"), scatter_dimension=0, tiled=True),
        lax.psum_scatter(gain_two_grad, ("wide", "narrow"), scatter_dimension=0, tiled=True),
    )
    rand_shard, value_shard, outproj_shard, up_shard, down_shard, gain_one_shard, gain_two_shard = (
        all_shards
    )
    return (
        output.reshape(item_count, LMAX, width),
        tokens_grad.reshape(item_count, LMAX, width),
        rand_shard,
        value_shard,
        outproj_shard,
        up_shard,
        down_shard,
        gain_one_shard,
        gain_two_shard,
    )


def solution(mesh):
    in_specs = (
        P(("wide", "narrow"), None, None),
        P(("wide", "narrow")),
        P(("wide", "narrow"), None),
        P(("wide", "narrow"), None),
        P(("wide", "narrow"), None),
        P(("wide", "narrow"), None),
        P(("wide", "narrow"), None),
        P(("wide", "narrow")),
        P(("wide", "narrow")),
        P(("wide", "narrow"), None, None),
    )
    out_specs = (
        P(("wide", "narrow"), None, None),
        P(("wide", "narrow"), None, None),
        P(("wide", "narrow"), None),
        P(("wide", "narrow"), None),
        P(("wide", "narrow"), None),
        P(("wide", "narrow"), None),
        P(("wide", "narrow"), None),
        P(("wide", "narrow")),
        P(("wide", "narrow")),
    )
    fits = dict(mesh.shape) == {"wide": 16, "narrow": 2}
    return jax.shard_map(chip_shards if fits else shards, mesh=mesh, in_specs=in_specs, out_specs=out_specs, check_vma=False)
```

```python
from functools import partial

import jax
import jax.numpy as jnp
from jax import lax
from jax.experimental import pallas as pl
from jax.experimental.pallas import tpu as pltpu
from jax.sharding import PartitionSpec as P

HEADS = 12
HEAD = 64
LMAX = 1024
WIDTH = 768
FF = 3072
EPSILON = 1e-05

BOTH = ("wide", "narrow")
BF16 = jnp.bfloat16
F32 = jnp.float32
VMEM = 61 << 20
LESS = 34 << 20

SUBS = 6
RUNS = 8
HALF = 64
HROWS = RUNS * HALF
PLANES = 4
PHEADS = HEADS // PLANES
ROWS = 2 * LMAX
FSTEP = 768
FSIDE = FF // 2 // FSTEP
TILE = 512
SIDE = WIDTH // 2
SPAN = 2 * HALF


def dot(a, b, ca, cb):
    return lax.dot_general(a, b, (((ca,), (cb,)), ((), ())), preferred_element_type=F32)


CORE, PLANE, PLACE, LENGTHS = 0, 1, 2, 3


def spec(shape, index):
    return pl.BlockSpec(shape, index)


def held(shape):
    zeros = (0,) * len(shape)
    return pl.BlockSpec(shape, lambda *_: zeros, pipeline_mode=pl.Buffered(1))


def params(limit):
    return pltpu.CompilerParams(vmem_limit_bytes=limit)


def whole_weight(sc, step, own, far, weight):
    @pl.when(step == 0)
    def _():
        weight[:, pl.ds(pl.multiple_of(sc[CORE] * SIDE, 128), SIDE)] = own[...]
        weight[:, pl.ds(pl.multiple_of((1 - sc[CORE]) * SIDE, 128), SIDE)] = far[...]


def values_kernel(sc, tok, gain, w_own, w_far, out, weight):
    step = pl.program_id(0)
    whole_weight(sc, step, w_own, w_far, weight)
    rows = tok.shape[1]
    position = step * rows + lax.broadcasted_iota(jnp.int32, (rows, 1), 0)
    for item in range(2):
        x = tok[item].astype(F32)
        scale = lax.rsqrt(jnp.mean(x * x, axis=-1, keepdims=True) + EPSILON)
        normed = (x * scale * gain[...]).astype(BF16)
        found = dot(normed, weight[...], 1, 0)
        found = jnp.where(position < sc[LENGTHS + item], found, 0.0).astype(BF16)
        for head in range(HEADS):
            out[head, :, item * HEAD : (item + 1) * HEAD] = found[:, head * HEAD : (head + 1) * HEAD]


def run_values(sc, tokens, gain, w_own, w_far):
    rows = 256
    return pl.pallas_call(
        values_kernel,
        grid_spec=pltpu.PrefetchScalarGridSpec(
            num_scalar_prefetch=1,
            grid=(LMAX // rows,),
            in_specs=[
                spec((2, rows, WIDTH), lambda j, s: (0, j, 0)),
                held((1, WIDTH)),
                held((WIDTH, SIDE)),
                held((WIDTH, SIDE)),
            ],
            out_specs=spec((HEADS, rows, 2 * HEAD), lambda j, s: (0, j, 0)),
            scratch_shapes=[pltpu.VMEM((WIDTH, WIDTH), BF16)],
        ),
        out_shape=jax.ShapeDtypeStruct((HEADS, LMAX, 2 * HEAD), BF16),
        compiler_params=params(VMEM),
        cost_estimate=pl.CostEstimate(
            flops=2 * 2 * LMAX * WIDTH * WIDTH, bytes_accessed=8 * LMAX * WIDTH, transcendentals=0
        ),
        name="values",
    )(sc, tokens, gain, w_own, w_far)


def lane_lengths(sc, shape):
    slot = lax.broadcasted_iota(jnp.int32, shape, 1) // HEAD
    length = jnp.where(slot == 0, sc[LENGTHS], sc[LENGTHS + 1])
    return jnp.where(slot >= 2, jnp.where(slot == 2, sc[LENGTHS + 2], sc[LENGTHS + 3]), length)


def plane_of(k, sc):
    return lax.rem(sc[PLANE] + PLANES - k, PLANES)


def plane_spec(planes, rows, lanes):
    def index(step, sc):
        return (plane_of(planes[0] + step * (planes[-1] - planes[0]) // max(len(planes) - 1, 1), sc), 0, 0)

    return spec((PHEADS, rows, lanes), index)


def anywhere(count):
    return [pl.BlockSpec(memory_space=pl.ANY)] * count


def plane_fetch(place, shards, raw, sems, slot):
    return [
        pltpu.make_async_copy(
            shards[4 * slot + rel],
            raw.at[slot, pl.ds(pl.multiple_of((place ^ rel) * SUBS * HALF, SUBS * HALF), SUBS * HALF)],
            sems.at[slot, rel],
        )
        for rel in range(4)
    ]


def take_plane(place, shards, raw, sems):
    step = pl.program_id(0)
    count = len(shards) // 4

    @pl.when(step == 0)
    def _():
        for slot in range(count):
            for copy in plane_fetch(place, shards, raw, sems, slot):
                copy.start()

    for slot in range(count):

        @pl.when(step == slot)
        def _():
            for copy in plane_fetch(place, shards, raw, sems, slot):
                copy.wait()

    return step


def head_rows(head):
    return slice(head * HROWS, (head + 1) * HROWS)


def fill_mask(sc, mask):
    @pl.when(pl.program_id(0) == 0)
    def _():
        shape = (LMAX, 4 * HEAD)
        column = lax.broadcasted_iota(jnp.int32, shape, 0)
        mask[...] = (column < lane_lengths(sc, shape)).astype(F32).astype(BF16)


def mix_kernel(count, carried, sc, *refs):
    shards, (v_own, v_far, *rest) = refs[: 4 * count], refs[4 * count :]
    mixed, mean, exps, inverse, raw, mask, sems = rest[4:] if carried else rest
    fill_mask(sc, mask)
    slot = take_plane(sc[PLACE], shards, raw, sems)
    shape = (HROWS, 4 * HEAD)
    line = lax.broadcasted_iota(jnp.int32, shape, 0)
    position = 128 * (line // HALF) + HALF * sc[CORE] + line % HALF
    valid = position < lane_lengths(sc, shape)
    for head in range(PHEADS):
        weights = jnp.exp(raw[slot, head_rows(head)].astype(F32)).astype(BF16)
        exps[head] = weights
        both = dot(weights, jnp.concatenate([v_own[head], v_far[head], mask[...]], axis=1), 1, 0)
        flip = jnp.where(valid, 1.0 / both[:, 4 * HEAD :], 0.0)
        found = both[:, : 4 * HEAD] * flip
        inverse[head] = flip.astype(BF16)
        mean[head] = found
        mixed[head] = found.astype(BF16)


def run_mix(sc, planes, shards, v_own, v_far, carry):
    carry, count = list(carry), len(planes)
    shape = (HEADS, HROWS, 4 * HEAD)
    return pl.pallas_call(
        partial(mix_kernel, count, bool(carry)),
        grid_spec=pltpu.PrefetchScalarGridSpec(
            num_scalar_prefetch=1,
            grid=(count,),
            in_specs=anywhere(4 * count) + [plane_spec(planes, LMAX, 2 * HEAD)] * 2 + anywhere(len(carry)),
            out_specs=[
                plane_spec(planes, HROWS, 4 * HEAD),
                plane_spec(planes, HROWS, 4 * HEAD),
                plane_spec(planes, HROWS, LMAX),
                plane_spec(planes, HROWS, 4 * HEAD),
            ],
            scratch_shapes=[
                pltpu.VMEM((count, 4 * SUBS * HALF, LMAX), BF16),
                pltpu.VMEM((LMAX, 4 * HEAD), BF16),
                pltpu.SemaphoreType.DMA((count, 4)),
            ],
        ),
        out_shape=[
            jax.ShapeDtypeStruct(shape, BF16),
            jax.ShapeDtypeStruct(shape, F32),
            jax.ShapeDtypeStruct((HEADS, HROWS, LMAX), BF16),
            jax.ShapeDtypeStruct(shape, BF16),
        ],
        input_output_aliases={3 + 4 * count + i: i for i in range(len(carry))},
        compiler_params=params(VMEM),
        cost_estimate=pl.CostEstimate(
            flops=2 * HEADS * HROWS * LMAX * 4 * HEAD,
            bytes_accessed=HEADS * (2 * HROWS * LMAX + 5 * HROWS * 256),
            transcendentals=HEADS * HROWS * LMAX // 2,
        ),
        name="mix",
    )(sc, *shards, v_own, v_far, *carry)


def row_valid(sc, step):
    line = lax.broadcasted_iota(jnp.int32, (4 * SPAN, 1), 0)
    item = line // SPAN
    row = step * SPAN + line % SPAN
    low = jnp.where(item == 0, sc[LENGTHS], sc[LENGTHS + 1])
    high = jnp.where(item == 2, sc[LENGTHS + 2], sc[LENGTHS + 3])
    return 128 * (row // HALF) + HALF * sc[CORE] + row % HALF < jnp.where(item >= 2, high, low)


def four_items(own, far):
    return jnp.concatenate([own[:, :, 0], far[...]], axis=0).reshape(4 * SPAN, WIDTH)


def pre_kernel(sc, tok, tok_far, heads, wo_own, wo_far, gain, mixed, resid, normed, weight):
    step = pl.program_id(0)
    whole_weight(sc, step, wo_own, wo_far, weight)
    for item in range(4):
        lanes = slice(item * HEAD, (item + 1) * HEAD)
        for pair in range(HEADS // 2):
            both = jnp.concatenate([heads[2 * pair, :, lanes], heads[2 * pair + 1, :, lanes]], axis=1)
            mixed[item, :, pair * 128 : (pair + 1) * 128] = both
    res = four_items(tok, tok_far).astype(F32) + dot(mixed[...].reshape(4 * SPAN, WIDTH), weight[...], 1, 0)
    resid[...] = res.astype(BF16).reshape(4, SPAN, WIDTH)
    scale = lax.rsqrt(jnp.mean(res * res, axis=-1, keepdims=True) + EPSILON)
    valid = row_valid(sc, step)
    normed[...] = jnp.where(valid, res * scale * gain[...], 0.0).astype(BF16).reshape(4, SPAN, WIDTH)


def slab_spec(items=4):
    return spec((items, SPAN, WIDTH), lambda r, s: (0, r, 0))


def half_specs():
    return [
        spec((2, SPAN // HALF, 1, HALF, WIDTH), lambda r, s: (0, r, s[CORE], 0, 0)),
        spec((2, SPAN // HALF, HALF, WIDTH), lambda r, s: (0, r, 0, 0)),
    ]


def heads_spec():
    return spec((HEADS, SPAN, 4 * HEAD), lambda r, s: (0, r, 0))


def run_pre(sc, tokens, tokens_far, heads, wo, gain):
    return pl.pallas_call(
        pre_kernel,
        grid_spec=pltpu.PrefetchScalarGridSpec(
            num_scalar_prefetch=1,
            grid=(HROWS // SPAN,),
            in_specs=half_specs()
            + [heads_spec(), held((WIDTH, SIDE)), held((WIDTH, SIDE)), held((1, WIDTH))],
            out_specs=[slab_spec()] * 3,
            scratch_shapes=[pltpu.VMEM((WIDTH, WIDTH), BF16)],
        ),
        out_shape=[
            jax.ShapeDtypeStruct((4, HROWS, WIDTH), BF16),
            jax.ShapeDtypeStruct((4, HROWS, WIDTH), BF16),
            jax.ShapeDtypeStruct((4, HROWS, WIDTH), BF16),
        ],
        compiler_params=params(VMEM),
        cost_estimate=pl.CostEstimate(
            flops=2 * ROWS * WIDTH * WIDTH, bytes_accessed=16 * ROWS * WIDTH, transcendentals=0
        ),
        name="pre",
    )(sc, tokens, tokens_far, heads, *wo, gain)


def masked_kernel(sc, cot, cot_far, masked):
    value = jnp.where(row_valid(sc, pl.program_id(0)), four_items(cot, cot_far).astype(F32), 0.0)
    masked[...] = value.astype(BF16).reshape(4, SPAN, WIDTH)


def run_masked(sc, cotangent, cotangent_far):
    return pl.pallas_call(
        masked_kernel,
        grid_spec=pltpu.PrefetchScalarGridSpec(
            num_scalar_prefetch=1, grid=(HROWS // SPAN,), in_specs=half_specs(), out_specs=slab_spec()
        ),
        out_shape=jax.ShapeDtypeStruct((4, HROWS, WIDTH), BF16),
        compiler_params=params(VMEM),
        cost_estimate=pl.CostEstimate(flops=0, bytes_accessed=4 * ROWS * WIDTH, transcendentals=0),
        name="masked",
    )(sc, cotangent, cotangent_far)


def own_lanes(sc):
    return pl.ds(pl.multiple_of(sc[CORE] * SIDE, 128), SIDE)


def far_lanes(sc):
    return pl.ds(pl.multiple_of((1 - sc[CORE]) * SIDE, 128), SIDE)


def unit_rows(f, sc):
    return (lax.rem(FSIDE * sc[CORE] + f, 2 * FSIDE), 0)


def unit_columns(f, sc):
    return (0, lax.rem(FSIDE * sc[CORE] + f, 2 * FSIDE))


def early(f, sc):
    return (0, lax.min(f, FSIDE - 1))


def late(f, sc):
    return (0, lax.max(f - FSIDE, 0))


def units_kernel(sc, normed, cot, up_own, up_far, dn_own, dn_far, active, up_grad, w_up, w_down):
    step = pl.program_id(0)
    w_down[:, own_lanes(sc)] = dn_own[...]
    w_down[:, far_lanes(sc)] = dn_far[...]

    @pl.when(step < FSIDE)
    def _():
        w_up[...] = up_own[...]

    @pl.when(step >= FSIDE)
    def _():
        w_up[...] = up_far[...]

    for row in range(0, ROWS, 256):
        rows = slice(row, row + 256)
        for column in range(0, FSTEP, 256):
            columns = slice(column, column + 256)
            up = dot(normed[rows], w_up[:, columns], 1, 0)
            square = up * up
            bend = jnp.tanh(up * (0.7978845608028654 + (0.044715 * 0.7978845608028654) * square))
            share = 0.5 + 0.5 * bend
            act = up * share
            active[rows, columns] = act.astype(BF16)
            slope = share + act * (1.0 - share) * (
                2 * 0.7978845608028654 + (6 * 0.044715 * 0.7978845608028654) * square
            )
            up_grad[rows, columns] = (dot(cot[rows], w_down[columns], 1, 1) * slope).astype(BF16)


def run_units(sc, normed, cotangent, up, down):
    return pl.pallas_call(
        units_kernel,
        grid_spec=pltpu.PrefetchScalarGridSpec(
            num_scalar_prefetch=1,
            grid=(2 * FSIDE,),
            in_specs=[
                held((ROWS, WIDTH)),
                held((ROWS, WIDTH)),
                spec((WIDTH, FSTEP), early),
                spec((WIDTH, FSTEP), late),
                spec((FSTEP, SIDE), unit_rows),
                spec((FSTEP, SIDE), unit_rows),
            ],
            out_specs=[spec((ROWS, FSTEP), unit_columns), spec((ROWS, FSTEP), unit_columns)],
            scratch_shapes=[pltpu.VMEM((WIDTH, FSTEP), BF16), pltpu.VMEM((FSTEP, WIDTH), BF16)],
        ),
        out_shape=[jax.ShapeDtypeStruct((ROWS, FF), BF16), jax.ShapeDtypeStruct((ROWS, FF), BF16)],
        compiler_params=params(VMEM),
        cost_estimate=pl.CostEstimate(
            flops=4 * ROWS * WIDTH * FF, bytes_accessed=6 * ROWS * WIDTH + 4 * ROWS * FF, transcendentals=ROWS * FF
        ),
        name="units",
    )(sc, normed.reshape(ROWS, WIDTH), cotangent.reshape(ROWS, WIDTH), *up, *down)


def down_grad_kernel(sc, active, cot, own, far, total):
    total[...] = dot(active[...], cot[...], 0, 0).astype(BF16)
    own[...] = total[:, own_lanes(sc)]
    far[...] = total[:, far_lanes(sc)]


def run_down_grad(sc, active, cotangent):
    return pl.pallas_call(
        down_grad_kernel,
        grid_spec=pltpu.PrefetchScalarGridSpec(
            num_scalar_prefetch=1,
            grid=(FF // 512,),
            in_specs=[spec((ROWS, 512), lambda f, s: (0, f)), held((ROWS, WIDTH))],
            out_specs=[spec((512, SIDE), lambda f, s: (f, 0))] * 2,
            scratch_shapes=[pltpu.VMEM((512, WIDTH), BF16)],
        ),
        out_shape=[jax.ShapeDtypeStruct((FF, SIDE), BF16)] * 2,
        compiler_params=params(57 << 20),
        cost_estimate=pl.CostEstimate(
            flops=2 * ROWS * WIDTH * FF, bytes_accessed=2 * ROWS * (WIDTH + FF), transcendentals=0
        ),
        name="down_grad",
    )(sc, active, cotangent.reshape(ROWS, WIDTH))


def up_grad_kernel(sc, normed, up_grad, own, far):
    total = dot(normed[...], up_grad[...], 0, 0).astype(BF16)

    @pl.when(pl.program_id(0) < 3)
    def _():
        own[...] = total

    @pl.when(pl.program_id(0) >= 3)
    def _():
        far[...] = total


def run_up_grad(sc, normed, up_grad):
    return pl.pallas_call(
        up_grad_kernel,
        grid_spec=pltpu.PrefetchScalarGridSpec(
            num_scalar_prefetch=1,
            grid=(6,),
            in_specs=[held((ROWS, WIDTH)), spec((ROWS, 512), lambda f, s: (0, lax.rem(3 * s[CORE] + f, 6)))],
            out_specs=[
                spec((WIDTH, 512), lambda f, s: (0, lax.min(f, 2))),
                spec((WIDTH, 512), lambda f, s: (0, lax.max(f - 3, 0))),
            ],
        ),
        out_shape=[jax.ShapeDtypeStruct((WIDTH, FF // 2), BF16)] * 2,
        compiler_params=params(57 << 20),
        cost_estimate=pl.CostEstimate(
            flops=2 * ROWS * WIDTH * FF, bytes_accessed=2 * ROWS * (WIDTH + FF), transcendentals=0
        ),
        name="up_grad",
    )(sc, normed.reshape(ROWS, WIDTH), up_grad)


def out_grad_kernel(sc, mixed, res_own, res_far, own, far, total):
    step = pl.program_id(0)
    grad = jnp.concatenate([res_own[...], res_far[...]], axis=0).reshape(4 * SPAN, WIDTH)
    found = dot(mixed[...].reshape(4 * SPAN, WIDTH), grad, 0, 0)

    @pl.when(step == 0)
    def _():
        total[...] = found

    @pl.when(step > 0)
    def _():
        total[...] += found

    @pl.when(step == pl.num_programs(0) - 1)
    def _():
        own[...] = total[:, own_lanes(sc)].astype(BF16)
        far[...] = total[:, far_lanes(sc)].astype(BF16)


def run_out_grad(sc, mixed, res_own, res_far):
    return pl.pallas_call(
        out_grad_kernel,
        grid_spec=pltpu.PrefetchScalarGridSpec(
            num_scalar_prefetch=1,
            grid=(HROWS // SPAN,),
            in_specs=[slab_spec(), slab_spec(2), slab_spec(2)],
            out_specs=[held((WIDTH, SIDE))] * 2,
            scratch_shapes=[pltpu.VMEM((WIDTH, WIDTH), F32)],
        ),
        out_shape=[jax.ShapeDtypeStruct((WIDTH, SIDE), BF16)] * 2,
        compiler_params=params(LESS),
        cost_estimate=pl.CostEstimate(
            flops=2 * ROWS * WIDTH * WIDTH, bytes_accessed=4 * ROWS * WIDTH, transcendentals=0
        ),
        name="out_grad",
    )(sc, mixed, res_own, res_far)


def out_kernel(sc, active, resid, dn_own, dn_far, own, far, w_down):
    step = pl.program_id(0)

    @pl.when(step == 0)
    def _():
        w_down[:, own_lanes(sc)] = dn_own[...]
        w_down[:, far_lanes(sc)] = dn_far[...]

    branch = dot(active[...].reshape(4 * SPAN, FF), w_down[...], 1, 0)
    output = jnp.where(row_valid(sc, step), resid[...].reshape(4 * SPAN, WIDTH).astype(F32) + branch, 0.0)
    output = output.astype(BF16).reshape(4, SPAN, WIDTH)
    own[...] = output[:2]
    far[...] = output[2:]


def run_out(sc, active, resid, down):
    return pl.pallas_call(
        out_kernel,
        grid_spec=pltpu.PrefetchScalarGridSpec(
            num_scalar_prefetch=1,
            grid=(HROWS // SPAN,),
            in_specs=[
                spec((4, SPAN, FF), lambda r, s: (0, r, 0)),
                slab_spec(),
                held((FF, SIDE)),
                held((FF, SIDE)),
            ],
            out_specs=[slab_spec(2)] * 2,
            scratch_shapes=[pltpu.VMEM((FF, WIDTH), BF16)],
        ),
        out_shape=[
            jax.ShapeDtypeStruct((2, HROWS, WIDTH), BF16),
            jax.ShapeDtypeStruct((2, HROWS, WIDTH), BF16),
        ],
        compiler_params=params(LESS),
        cost_estimate=pl.CostEstimate(
            flops=2 * ROWS * WIDTH * FF, bytes_accessed=ROWS * (2 * FF + 7 * WIDTH), transcendentals=0
        ),
        name="out",
    )(sc, active.reshape(4, HROWS, FF), resid, *down)


def post_kernel(sc, resid, grad_own, grad_far, cot, up_own, up_far, wo_own, wo_far, gain, *refs):
    (res_own, res_far, heads, d_gain, weight, spread) = refs
    step = pl.program_id(0)
    whole_weight(sc, step, wo_own, wo_far, weight)
    shape, slab = (4 * SPAN, WIDTH), (4, SPAN, WIDTH)
    valid = row_valid(sc, step)
    res = resid[...].reshape(shape).astype(F32)
    scale = lax.rsqrt(jnp.mean(res * res, axis=-1, keepdims=True) + EPSILON)
    unit = res * scale
    units = (4 * SPAN, FF // 2)
    back = dot(grad_own[...].reshape(units), up_own[...], 1, 1) + dot(grad_far[...].reshape(units), up_far[...], 1, 1)
    two_grad = jnp.where(valid, back, 0.0)
    gained = two_grad * gain[...]
    masked = cot[...].reshape(shape).astype(F32)
    grad = masked + scale * (gained - unit * jnp.mean(gained * unit, axis=-1, keepdims=True))
    low = grad.astype(BF16)
    res_own[...] = low.reshape(slab)[:2]
    res_far[...] = low.reshape(slab)[2:]
    gain_sum = jnp.sum(two_grad * unit, axis=0, keepdims=True)

    @pl.when(step == 0)
    def _():
        d_gain[...] = gain_sum

    @pl.when(step > 0)
    def _():
        d_gain[...] += gain_sum

    spread[...] = dot(low, weight[...], 1, 1).astype(BF16).reshape(slab)
    for pair in range(HEADS // 2):
        lanes = slice(pair * 128, (pair + 1) * 128)
        for side in range(2):
            one, two = spread[2 * side, :, lanes], spread[2 * side + 1, :, lanes]
            half = slice(side * 128, (side + 1) * 128)
            heads[2 * pair, :, half] = jnp.concatenate([one[:, :HEAD], two[:, :HEAD]], axis=1)
            heads[2 * pair + 1, :, half] = jnp.concatenate([one[:, HEAD:], two[:, HEAD:]], axis=1)


def run_post(sc, resid, up_grad, cotangent, up, wo, gain):
    side = lambda which: spec((4, SPAN, FF // 2), lambda r, s: (0, r, s[CORE] if which == 0 else 1 - s[CORE]))
    up_grad = up_grad.reshape(4, HROWS, FF)
    return pl.pallas_call(
        post_kernel,
        grid_spec=pltpu.PrefetchScalarGridSpec(
            num_scalar_prefetch=1,
            grid=(HROWS // SPAN,),
            in_specs=[
                slab_spec(),
                side(0),
                side(1),
                slab_spec(),
                held((WIDTH, FF // 2)),
                held((WIDTH, FF // 2)),
                held((WIDTH, SIDE)),
                held((WIDTH, SIDE)),
                held((1, WIDTH)),
            ],
            out_specs=[slab_spec(2)] * 2 + [heads_spec(), held((1, WIDTH))],
            scratch_shapes=[
                pltpu.VMEM((WIDTH, WIDTH), BF16),
                pltpu.VMEM((4, SPAN, WIDTH), BF16),
            ],
        ),
        out_shape=[
            jax.ShapeDtypeStruct((2, HROWS, WIDTH), BF16),
            jax.ShapeDtypeStruct((2, HROWS, WIDTH), BF16),
            jax.ShapeDtypeStruct((HEADS, HROWS, 4 * HEAD), BF16),
            jax.ShapeDtypeStruct((1, WIDTH), F32),
        ],
        compiler_params=params(VMEM),
        cost_estimate=pl.CostEstimate(
            flops=2 * ROWS * WIDTH * (WIDTH + FF), bytes_accessed=ROWS * (16 * WIDTH + 2 * FF), transcendentals=0
        ),
        name="post",
    )(sc, resid, up_grad, up_grad, cotangent, *up, *wo, gain)


def unmix_kernel(count, carried, sc, v_own, v_far, grad_heads, mean, exps, inverse, *refs):
    refs = refs[2:] if carried else refs
    outs, (own, far, grads, mask, adder, bound, out_sems) = refs[: 4 * count], refs[4 * count :]
    place = sc[PLACE]
    step = pl.program_id(0)

    def leave(slot):
        return [
            pltpu.make_async_copy(
                grads.at[slot, pl.ds(pl.multiple_of((place ^ rel) * SUBS * HALF, SUBS * HALF), SUBS * HALF)],
                outs[4 * slot + rel],
                out_sems.at[slot, rel],
            )
            for rel in range(4)
        ]

    fill_mask(sc, mask)

    @pl.when(step == 0)
    def _():
        lane = lax.broadcasted_iota(jnp.int32, (4 * HEAD, 128), 0) // HEAD
        column = lax.broadcasted_iota(jnp.int32, (4 * HEAD, 128), 1)
        adder[...] = jnp.where((lane == column) | (lane + 4 == column), -1.0, 0.0).astype(BF16)
        row = lax.broadcasted_iota(jnp.int32, (LMAX, 128), 0)
        item = lax.broadcasted_iota(jnp.int32, (LMAX, 128), 1)
        length = jnp.where(item % 4 == 0, sc[LENGTHS], sc[LENGTHS + 1])
        length = jnp.where(item % 4 == 2, sc[LENGTHS + 2], length)
        length = jnp.where(item % 4 == 3, sc[LENGTHS + 3], length)
        bound[...] = jnp.where((item < 8) & (row < length), 1.0, 0.0).astype(BF16)

    high_lanes = lax.broadcasted_iota(jnp.int32, (HROWS, 128), 1) < 4
    for head in range(PHEADS):
        weights = exps[head]
        low = (grad_heads[head].astype(F32) * inverse[head].astype(F32)).astype(BF16)
        product = low.astype(F32) * mean[head]
        coarse = product.astype(BF16)
        fine = (product - coarse.astype(F32)).astype(BF16)
        delta = dot(coarse, adder[...], 1, 0) + dot(fine, adder[...], 1, 0)
        coarse = delta.astype(BF16)
        fine = (delta - coarse.astype(F32)).astype(BF16)
        left = jnp.concatenate([low, jnp.where(high_lanes, coarse, fine)], axis=1)
        score = dot(left, jnp.concatenate([v_own[head], v_far[head], bound[...]], axis=1), 1, 1)
        grads[step, head_rows(head)] = (score * weights.astype(F32)).astype(BF16)
        back = (dot(weights, low, 0, 0) * mask[...].astype(F32)).astype(BF16)
        own[head] = back[:, : 2 * HEAD]
        far[head] = back[:, 2 * HEAD :]
    for which in range(count):

        @pl.when(step == which)
        def _():
            for copy in leave(which):
                copy.start()
            if which == count - 1:
                for slot in range(count):
                    for copy in leave(slot):
                        copy.wait()


def run_unmix(sc, planes, v_own, v_far, grad_heads, mean, exps, inverse, carry):
    carry, count = list(carry), len(planes)
    return pl.pallas_call(
        partial(unmix_kernel, count, bool(carry)),
        grid_spec=pltpu.PrefetchScalarGridSpec(
            num_scalar_prefetch=1,
            grid=(count,),
            in_specs=[
                plane_spec(planes, LMAX, 2 * HEAD),
                plane_spec(planes, LMAX, 2 * HEAD),
                plane_spec(planes, HROWS, 4 * HEAD),
                plane_spec(planes, HROWS, 4 * HEAD),
                plane_spec(planes, HROWS, LMAX),
                plane_spec(planes, HROWS, 4 * HEAD),
            ]
            + anywhere(len(carry)),
            out_specs=anywhere(4 * count) + [plane_spec(planes, LMAX, 2 * HEAD)] * 2,
            scratch_shapes=[
                pltpu.VMEM((count, 4 * SUBS * HALF, LMAX), BF16),
                pltpu.VMEM((LMAX, 4 * HEAD), BF16),
                pltpu.VMEM((4 * HEAD, 128), BF16),
                pltpu.VMEM((LMAX, 128), BF16),
                pltpu.SemaphoreType.DMA((count, 4)),
            ],
        ),
        out_shape=[jax.ShapeDtypeStruct((SUBS * HALF, LMAX), BF16)] * (4 * count)
        + [jax.ShapeDtypeStruct((HEADS, LMAX, 2 * HEAD), BF16)] * 2,
        input_output_aliases={7 + i: 4 * count + i for i in range(len(carry))},
        compiler_params=params(VMEM),
        cost_estimate=pl.CostEstimate(
            flops=3 * HEADS * HROWS * LMAX * 4 * HEAD,
            bytes_accessed=HEADS * (2 * HROWS * LMAX + 5 * HROWS * 256 + 4 * LMAX * 256),
            transcendentals=0,
        ),
        name="unmix",
    )(sc, v_own, v_far, grad_heads, mean, exps, inverse, *carry)


def close_kernel(sc, tok, res_own, res_got, own, far, gain, w_own, w_far, *refs):
    (tok_grad, d_value, d_gain, total, weight) = refs
    step = pl.program_id(0)
    whole_weight(sc, step, w_own, w_far, weight)
    core = sc[CORE]
    tok_grad[:, :, core] = res_own[...].astype(F32)
    tok_grad[:, :, 1 - core] = res_got[...].astype(F32)
    runs = tok.shape[1]
    rows = runs * 128
    for item in range(2):
        lanes = slice(item * HEAD, (item + 1) * HEAD)
        pieces = [
            add_low(own[head, :, lanes], far[head, :, lanes]) for head in range(HEADS)
        ]
        back = jnp.concatenate(pieces, axis=1)
        x = tok[item].reshape(rows, WIDTH).astype(F32)
        scale = lax.rsqrt(jnp.mean(x * x, axis=-1, keepdims=True) + EPSILON)
        unit = x * scale
        normed = (unit * gain[...]).astype(BF16)
        normed_grad = dot(back, weight[...], 1, 1)
        gained = normed_grad * gain[...]
        update = scale * (gained - unit * jnp.mean(gained * unit, axis=-1, keepdims=True))
        tok_grad[item] += update.reshape(runs, 2, HALF, WIDTH)
        gain_sum = jnp.sum(normed_grad * unit, axis=0, keepdims=True)
        value_sum = dot(normed, back, 0, 0)
        if item == 0:
            gain_total, value_total = gain_sum, value_sum
        else:
            gain_total, value_total = gain_total + gain_sum, value_total + value_sum

    @pl.when(step == 0)
    def _():
        d_gain[...] = gain_total
        total[...] = value_total

    @pl.when(step > 0)
    def _():
        d_gain[...] += gain_total
        total[...] += value_total

    @pl.when(step == pl.num_programs(0) - 1)
    def _():
        low = total[...].astype(BF16)
        d_value[0] = low[:, :SIDE]
        d_value[1] = low[:, SIDE:]


def run_close(sc, tokens, res_own, res_got, own, far, gain, w_own, w_far):
    runs = 2
    slab = (2, RUNS, 2, HALF, WIDTH)
    half = (2, RUNS, HALF, WIDTH)
    whole_spec = spec((2, runs, 2, HALF, WIDTH), lambda j, s: (0, j, 0, 0, 0))
    half_spec = spec((2, runs, HALF, WIDTH), lambda j, s: (0, j, 0, 0))
    back_spec = spec((HEADS, runs * 128, 2 * HEAD), lambda j, s: (0, j, 0))
    return pl.pallas_call(
        close_kernel,
        grid_spec=pltpu.PrefetchScalarGridSpec(
            num_scalar_prefetch=1,
            grid=(RUNS // runs,),
            in_specs=[whole_spec]
            + [half_spec] * 2
            + [back_spec, back_spec, held((1, WIDTH)), held((WIDTH, SIDE)), held((WIDTH, SIDE))],
            out_specs=[whole_spec, held((2, WIDTH, SIDE)), held((1, WIDTH))],
            scratch_shapes=[pltpu.VMEM((WIDTH, WIDTH), F32), pltpu.VMEM((WIDTH, WIDTH), BF16)],
        ),
        out_shape=[
            jax.ShapeDtypeStruct(slab, F32),
            jax.ShapeDtypeStruct((2, WIDTH, SIDE), BF16),
            jax.ShapeDtypeStruct((1, WIDTH), F32),
        ],
        compiler_params=params(LESS),
        cost_estimate=pl.CostEstimate(
            flops=4 * 2 * LMAX * WIDTH * WIDTH, bytes_accessed=38 * LMAX * WIDTH, transcendentals=0
        ),
        name="close",
    )(
        sc,
        tokens.reshape(slab),
        *(x.reshape(half) for x in (res_own, res_got)),
        own,
        far,
        gain,
        w_own,
        w_far,
    )


def join_kernel(sc, own, got, output):
    output[:, :, sc[CORE]] = own[...].astype(F32)
    output[:, :, 1 - sc[CORE]] = got[...].astype(F32)


def run_join(sc, own, got):
    half = (2, RUNS, HALF, WIDTH)
    half_spec = spec((2, 2, HALF, WIDTH), lambda j, s: (0, j, 0, 0))
    return pl.pallas_call(
        join_kernel,
        grid_spec=pltpu.PrefetchScalarGridSpec(
            num_scalar_prefetch=1,
            grid=(RUNS // 2,),
            in_specs=[half_spec, half_spec],
            out_specs=spec((2, 2, 2, HALF, WIDTH), lambda j, s: (0, j, 0, 0, 0)),
        ),
        out_shape=jax.ShapeDtypeStruct((2, RUNS, 2, HALF, WIDTH), F32),
        compiler_params=params(LESS),
        cost_estimate=pl.CostEstimate(flops=0, bytes_accessed=12 * LMAX * WIDTH, transcendentals=0),
        name="join",
    )(sc, own.reshape(half), got.reshape(half))


PACK_DOWN, PACK_UP, PACK_OUT, PACK_VALUE, PACK_GAIN, PACK = 0, 192, 384, 432, 480, 496


def pack_kernel(sc, down, up, out, value, gain, down_far, up_far, out_far, value_far, gain_far, packed):
    first = sc[CORE] == 0

    def both(own, far, lanes):
        own, far = own[:, lanes], far[:, lanes]
        return jnp.concatenate([jnp.where(first, own, far), jnp.where(first, far, own)], axis=0)

    def side(own, far):
        return both(own, far, own_lanes(sc))

    packed[PACK_DOWN:PACK_UP] = side(down, down_far)
    for j in range(4):
        lanes = pl.ds(pl.multiple_of((4 * sc[CORE] + j) * SIDE, 128), SIDE)
        packed[PACK_UP + 48 * j : PACK_UP + 48 * (j + 1)] = both(up, up_far, lanes)
    packed[PACK_OUT:PACK_VALUE] = side(out, out_far)
    packed[PACK_VALUE:PACK_GAIN] = side(value, value_far)
    packed[PACK_GAIN:] = both(gain, gain_far, slice(0, SIDE))


def run_pack(sc, own, far):
    return pl.pallas_call(
        pack_kernel,
        grid_spec=pltpu.PrefetchScalarGridSpec(
            num_scalar_prefetch=1,
            grid=(1,),
            in_specs=[held(x.shape) for x in (*own, *far)],
            out_specs=held((PACK, SIDE)),
        ),
        out_shape=jax.ShapeDtypeStruct((PACK, SIDE), BF16),
        compiler_params=params(VMEM),
        cost_estimate=pl.CostEstimate(flops=0, bytes_accessed=6 * PACK * SIDE, transcendentals=0),
        name="pack",
    )(sc, *own, *far)


def chip_of(sc, k, rel):
    return plane_of(k, sc) * 4 + (sc[PLACE] ^ rel)


def place_kernel(moves, sc, *refs):
    pieces, targets, sems = refs[:16], refs[16:-1], refs[-1]
    copies = []
    for index, piece in enumerate(pieces):
        chip = chip_of(sc, index // 4, index % 4)
        for which, (start, count, lane, target, step, offset, column) in enumerate(moves):
            rows = pl.ds(pl.multiple_of(chip * step + offset, 16), count)
            copies.append(
                pltpu.make_async_copy(
                    piece.at[pl.ds(start, count), pl.ds(lane, SIDE)],
                    targets[target].at[rows, pl.ds(column, SIDE)],
                    sems.at[index, which],
                )
            )
    for copy in copies:
        copy.start()
    for copy in copies:
        copy.wait()


def run_place(sc, pieces, moves, shapes):
    return pl.pallas_call(
        partial(place_kernel, moves),
        grid_spec=pltpu.PrefetchScalarGridSpec(
            num_scalar_prefetch=1,
            grid=(1,),
            in_specs=anywhere(16),
            out_specs=[held(shape) for shape in shapes],
            scratch_shapes=[pltpu.SemaphoreType.DMA((16, len(moves)))],
        ),
        out_shape=[jax.ShapeDtypeStruct(shape, BF16) for shape in shapes],
        compiler_params=params(VMEM),
        cost_estimate=pl.CostEstimate(
            flops=0, bytes_accessed=4 * sum(a * b for a, b in shapes), transcendentals=0
        ),
        name="place",
    )(sc, *pieces)


def place_weights(sc, pieces):
    moves = (
        (PACK_DOWN, 192, 0, 0, 192, 0, 0),
        *((PACK_UP + 48 * j, 48, 0, 1, 48, 0, j * SIDE) for j in range(4)),
        (PACK_OUT, 48, 0, 2, 48, 0, 0),
        (PACK_VALUE, 48, 0, 3, 48, 0, 0),
        (PACK_GAIN, 16, 0, 4, 16, 0, 0),
    )
    shapes = [(FF, SIDE), (WIDTH, FF // 2), (WIDTH, SIDE), (WIDTH, SIDE), (256, SIDE)]
    return run_place(sc, pieces, moves, shapes)


def collect_kernel(sc, *refs):
    outs = refs[24:]
    for k in range(PLANES):

        @pl.when(pl.program_id(0) == k)
        def _():
            for rel in range(4):
                down, down_got, up, up_got, out, out_got = refs[6 * rel : 6 * rel + 6]
                packed = outs[4 * k + rel]
                packed[PACK_DOWN:PACK_UP] = add_low(down[...], down_got[...])
                for j in range(4):
                    lanes = slice(j * SIDE, (j + 1) * SIDE)
                    packed[PACK_UP + 48 * j : PACK_UP + 48 * (j + 1)] = add_low(up[:, lanes], up_got[:, lanes])
                packed[PACK_OUT:PACK_VALUE] = add_low(out[...], out_got[...])


def run_collect(sc, *sides):
    def rows(x, rel):
        return spec((x.shape[0] // 16, x.shape[1]), lambda k, s: (chip_of(s, k, rel), 0))

    return pl.pallas_call(
        collect_kernel,
        grid_spec=pltpu.PrefetchScalarGridSpec(
            num_scalar_prefetch=1,
            grid=(PLANES,),
            in_specs=[rows(x, rel) for rel in range(4) for x in sides],
            out_specs=[pl.BlockSpec(memory_space=pltpu.VMEM)] * 16,
        ),
        out_shape=[jax.ShapeDtypeStruct((PACK_VALUE, SIDE), BF16)] * 16,
        compiler_params=params(LESS),
        cost_estimate=pl.CostEstimate(flops=0, bytes_accessed=3 * 16 * PACK_VALUE * SIDE * 2, transcendentals=0),
        name="collect",
    )(sc, *(x for _ in range(4) for x in sides))


def add_kernel(groups, *refs):
    for group, total in zip(groups, refs[-len(groups) :]):
        value = refs[group[0]][...].astype(F32)
        for index in group[1:]:
            value = value + refs[index][...].astype(F32)
        total[...] = value.astype(total.dtype)


def run_add(groups, values, dtype):
    shape = values[0].shape
    here = pl.BlockSpec(memory_space=pltpu.VMEM)
    return pl.pallas_call(
        partial(add_kernel, groups),
        in_specs=[here] * len(values),
        out_specs=[here] * len(groups),
        out_shape=[jax.ShapeDtypeStruct(shape, dtype)] * len(groups),
        compiler_params=params(LESS),
        cost_estimate=pl.CostEstimate(
            flops=0, bytes_accessed=2 * shape[0] * shape[1] * (len(values) + len(groups)), transcendentals=0
        ),
        name="add",
    )(*values)


DEVICES = 32
TO_CORE, TO_X, TO_Y = 1, 2, 4


def swap(x, bit):
    return lax.ppermute(x, BOTH, [(d, d ^ bit) for d in range(DEVICES)])


def ring(x, way=1):
    return lax.ppermute(x, BOTH, [(d, (d + 8 * way) % DEVICES) for d in range(DEVICES)])


def pick(x, index, axis=0):
    return lax.dynamic_index_in_dim(x, index, axis, keepdims=False)


def ordered(flag, one, two, axis=0, joined=jnp.stack):
    return jnp.where(flag == 0, joined([one, two], axis), joined([two, one], axis))


def add_low(one, two):
    return (one.astype(F32) + two.astype(F32)).astype(BF16)


STEPS = (
    ((0, 0, 1), (0, 1, 0), (1, 0, 0)),
    ((1, 0, 1), (0, 1, 1), (2, 0, 0)),
    ((2, 0, 1), (1, 1, 0), (3, 0, 0)),
    ((1, 1, 1), (2, 1, 1), (2, 1, 0)),
    ((3, 0, 1), (3, 1, 0), (3, 1, 1)),
)


def gather_step(have, step):
    by_x, by_y, by_z = STEPS[step]
    return {
        **have,
        by_z: ring(have[by_z[0] - 1, by_z[1], by_z[2]]),
        by_x: swap(have[by_x[0], by_x[1], 0], TO_X),
        by_y: swap(have[by_y[0], 0, by_y[2]], TO_Y),
    }


def in_order(have):
    return [have[k, y, x] for k in range(4) for y in range(2) for x in range(2)]


def by_place(shares, planes=range(PLANES)):
    return {(k, i // 2, i % 2): shares[4 * at + i] for at, k in enumerate(planes) for i in range(4)}


def scatter_send(have, step):
    by_x, by_y, by_z = STEPS[len(STEPS) - 1 - step]
    got = (ring(have[by_z], -1), swap(have[by_x], TO_X), swap(have[by_y], TO_Y))
    return {at: value for at, value in have.items() if at not in (by_x, by_y, by_z)}, got


def scatter_add(have, got, step):
    by_x, by_y, by_z = STEPS[len(STEPS) - 1 - step]
    targets = ((by_z[0] - 1, by_z[1], by_z[2]), (by_x[0], by_x[1], 0), (by_y[0], 0, by_y[2]))
    sums = list(dict.fromkeys(targets))
    groups = [(len(got) + i, *(j for j in range(len(got)) if targets[j] == at)) for i, at in enumerate(sums)]
    values = [*got, *(have[at] for at in sums)]
    dtype = F32 if step == len(STEPS) - 1 else BF16
    if values[0].shape[1] == LMAX:
        totals = run_add(groups, values, dtype)
    else:
        totals = [sum(values[i].astype(F32) for i in group).astype(dtype) for group in groups]
    return {**have, **dict(zip(sums, totals))}


together = lax.optimization_barrier


def chip_shards(tokens, lengths, rand_mix, w_value, w_out, w_up, w_down, gain_mix, gain_ffn, grad_out):
    wide = lax.axis_index("wide")
    core = lax.axis_index("narrow")
    z, y, x = wide // 4, (wide // 2) % 2, wide % 2
    other = lambda value: swap(value, TO_CORE)
    side = partial(ordered, core, joined=jnp.concatenate)
    slab = (2, RUNS, 2, HALF, WIDTH)
    tokens, grad_out = tokens.reshape(slab), grad_out.reshape(slab)

    gains = jnp.pad(jnp.concatenate([gain_mix, gain_ffn])[None], ((0, 7), (0, SIDE - 48)))
    own = (w_down, w_up, w_out, w_value, gains)
    far = tuple(other(value) for value in own)
    near_sc = jnp.concatenate([jnp.stack([core, z, wide % 4]).astype(jnp.int32), lengths, lengths])
    weights = {(0, 0, 0): run_pack(near_sc, own, far)}

    rand = rand_mix.reshape(3, 2, HALF, LMAX)
    blocks = side(pick(rand, core, 1), other(pick(rand, 1 - core, 1)), 0)
    weights, rands, late_tokens, late_grad = together(
        (gather_step(weights, 0), {(0, 0, 0): blocks.reshape(SUBS * HALF, LMAX)}, tokens, grad_out)
    )
    weights, tokens_far = together((gather_step(weights, 1), other(pick(late_tokens, 1 - core, 2))))
    weights, grad_far = together((gather_step(weights, 2), other(pick(late_grad, 1 - core, 2))))
    weights, far_lengths = together((gather_step(weights, 3), other(lengths)))
    sc = jnp.concatenate([near_sc[:5], far_lengths])
    weights, rands = together((gather_step(weights, 4), rands))

    rands = gather_step(rands, 0)
    down, up, out, value, gain_rows = place_weights(sc, in_order(weights))
    rands, value, value_far, gain_rows, out, down, up = together(
        (rands, value, other(value), gain_rows, out, down, up)
    )
    gain_rows = gain_rows.reshape(16, 2, 8, SIDE)[:, :, 0]
    gain_one = gain_rows[..., :24].reshape(1, WIDTH).astype(F32)
    gain_two = gain_rows[..., 24:48].reshape(1, WIDTH).astype(F32)
    rands = gather_step(rands, 1)
    v_own = run_values(sc, tokens.reshape(2, LMAX, WIDTH), gain_one, value, value_far)
    rands, v_own, out, down, up = together((rands, v_own, (out, other(out)), down, up))
    rands, v_own, v_far, grad_far, down, up = together(
        (gather_step(rands, 2), v_own, other(v_own), grad_far, down, up)
    )
    rands = gather_step(rands, 3)
    masked = run_masked(sc, grad_out, grad_far)
    rands, v_far, masked, down, up = together((rands, v_far, masked, down, up))
    near = [rands[k, y_at, x_at] for k in range(3) for y_at in range(2) for x_at in range(2)]
    rands = gather_step(rands, 4)
    mixing = run_mix(sc, (0, 1, 2), near, v_own, v_far, ())
    rands, down, up, mixing = together((rands, down, up, mixing))
    heads, mean, exps, inverse = run_mix(sc, (3,), in_order(rands)[12:], v_own, v_far, mixing)
    down, up = (down, other(down)), (up, other(up))

    mixed, resid, normed = run_pre(sc, tokens, tokens_far, heads, out, gain_two)
    active, up_grad = run_units(sc, normed, masked, up, down)
    res_own, res_far, grad_heads, d_gain_two = run_post(sc, resid, up_grad, masked, up, out, gain_two)

    backward = lambda planes, carry: run_unmix(sc, planes, v_own, v_far, grad_heads, mean, exps, inverse, carry)
    *far, back_own, back_far = backward((3,), ())
    far, back_own, back_far, res_got = together((far, back_own, back_far, other(res_far)))
    have, got = scatter_send(by_place(far, (3,)), 0)
    *near, back_own, back_far = backward((2, 1, 0), (back_own, back_far))
    have, got, near, back_own, back_far = together((have, got, near, back_own, back_far))
    have = scatter_add({**have, **by_place(near, (2, 1, 0))}, got, 0)

    have, got = scatter_send(have, 1)
    up_own, up_far = run_up_grad(sc, normed, up_grad)
    have, got, up_own, up_far, back_got = together((have, got, up_own, up_far, other(back_far)))
    have = scatter_add(have, got, 1)

    have, got = scatter_send(have, 2)
    down_own, down_far = run_down_grad(sc, active, masked)
    have, got, down_own, down_far, up_got = together((have, got, down_own, down_far, other(up_far)))
    have = scatter_add(have, got, 2)

    have, got = scatter_send(have, 3)
    d_out_own, d_out_far = run_out_grad(sc, mixed, res_own, res_far)
    packed = run_collect(sc, down_own, other(down_far), up_own, up_got, d_out_own, other(d_out_far))
    have, got, packed = together((have, got, packed))
    have = scatter_add(have, got, 3)

    have, got = scatter_send(have, 4)
    out_own, out_far = run_out(sc, active, resid, down)
    have, got, packed, out_own, out_far = together((have, got, packed, out_own, out_far))
    rand_sum = scatter_add(have, got, 4)[0, 0, 0].reshape(2, 3, HALF, LMAX)

    sums, got = scatter_send(by_place(packed), 0)
    tokens_grad, d_value, d_gain_one = run_close(
        sc, tokens, res_own, res_got, back_own, back_got, gain_one, value, value_far
    )
    gain_pair = jnp.concatenate([d_gain_one, d_gain_two]).reshape(2, 16, 1, 48).astype(BF16)
    gain_pair = jnp.pad(gain_pair, ((0, 0), (0, 0), (0, 15), (0, SIDE - 48)))
    small = jnp.concatenate([d_value.reshape(2, 16, 48, SIDE), gain_pair], 2)
    sums, got, tokens_grad, small, out_got = together((sums, got, tokens_grad, small, other(out_far)))
    sums = scatter_add(sums, got, 0)

    sums, got = scatter_send(sums, 1)
    small = add_low(pick(small, core), other(pick(small, 1 - core))).reshape(4, 2, 2, 64, SIDE)
    output = run_join(sc, out_own, out_got)
    sums, got, small, output = together((sums, got, small, output))
    sums = scatter_add(sums, got, 1)

    sums, got = scatter_send(sums, 2)
    small = add_low(pick(small, x, 2), swap(pick(small, 1 - x, 2), TO_X))
    sums, got, small = together((sums, got, small))
    sums = scatter_add(sums, got, 2)

    sums, got = scatter_send(sums, 3)
    small = add_low(pick(small, y, 1), swap(pick(small, 1 - y, 1), TO_Y))
    blocks, blocks_far = pick(rand_sum, core), other(pick(rand_sum, 1 - core))
    sums, got, small, blocks, blocks_far = together((sums, got, small, blocks, blocks_far))
    sums = scatter_add(sums, got, 3)

    sums, got = scatter_send(sums, 4)
    small_sum = pick(small, z).astype(F32)
    for k in range(1, PLANES):
        small_sum = small_sum + ring(pick(small, lax.rem(z + PLANES - k, PLANES)), -k).astype(F32)
    sums, got, small_sum = together((sums, got, small_sum))
    big_sum = scatter_add(sums, got, 4)[0, 0, 0]
    big_far, small_far = other(big_sum), other(small_sum)

    rows_of = lambda value, rows: pick(value.reshape(-1, 2, rows, SIDE), core, 1)
    mine = lambda own, far, rows: side(rows_of(own, rows)[0], rows_of(far, rows)[0], 1)
    down_shard = mine(big_sum[PACK_DOWN:PACK_UP], big_far[PACK_DOWN:PACK_UP], 96)
    up_side = lambda value: rows_of(value[PACK_UP:PACK_OUT], 24).transpose(1, 0, 2).reshape(24, 4 * SIDE)
    up_shard = side(up_side(big_sum), up_side(big_far), 1)
    outproj_shard = mine(big_sum[PACK_OUT:PACK_VALUE], big_far[PACK_OUT:PACK_VALUE], 24)
    value_shard = mine(small_sum[:48], small_far[:48], 24)
    gains_pair = ordered(core, small_sum[48, :48], small_far[48, :48])
    gain_pair = pick(gains_pair.reshape(2, 2, 24), core, 1)

    rand_shard = ordered(core, blocks, blocks_far, 1)

    return (
        output.reshape(2, LMAX, WIDTH),
        tokens_grad.reshape(2, LMAX, WIDTH),
        rand_shard.reshape(3 * 128, LMAX),
        value_shard,
        outproj_shard,
        up_shard,
        down_shard,
        gain_pair[0],
        gain_pair[1],
    )


def rms_norm(values, gain):
    scale = lax.rsqrt(jnp.mean(values * values, axis=-1, keepdims=True) + EPSILON)
    return values * scale * gain


def split_heads(block):
    return block.reshape(LMAX, HEADS, HEAD).transpose(1, 0, 2)


def merge_heads(block):
    return block.transpose(1, 0, 2).reshape(LMAX, HEADS * HEAD)


def masked_scores(key_mask, rand_head):
    return jnp.where(key_mask[None, :] > 0, rand_head.astype(jnp.float32), -1e30)


def head_forward(key_mask, paired):
    rand_head, value_head = paired
    scores = masked_scores(key_mask, rand_head)
    row_peak = jnp.max(scores, axis=-1, keepdims=True)
    exponent = jnp.exp(scores - row_peak)
    denom_sum = jnp.sum(exponent, axis=-1, keepdims=True)
    attention = exponent / denom_sum * key_mask[:, None]
    mixed = jnp.dot(attention.astype(jnp.bfloat16), value_head, preferred_element_type=jnp.float32)
    return (mixed.astype(jnp.bfloat16), row_peak + jnp.log(denom_sum))


def head_backward(key_mask, paired):
    rand_head, value_head, mix_grad, log_total = paired
    scores = masked_scores(key_mask, rand_head)
    attention = jnp.exp(scores - log_total) * key_mask[:, None]
    prob_grad = jnp.einsum("id,jd->ij", mix_grad, value_head, preferred_element_type=jnp.float32)
    value_grad = jnp.einsum(
        "ij,id->jd", attention.astype(jnp.bfloat16), mix_grad, preferred_element_type=jnp.float32
    )
    score_grad = attention * (prob_grad - jnp.sum(prob_grad * attention, axis=-1, keepdims=True))
    return (score_grad, value_grad)


def shards(tokens, lengths, rand_mix, w_value, w_out, w_up, w_down, gain_mix, gain_ffn, grad_out):
    item_count = tokens.shape[0]
    width = tokens.shape[2]
    row_count = item_count * LMAX
    tokens_flat = tokens.reshape(row_count, width).astype(jnp.float32)
    positions = jnp.arange(LMAX, dtype=jnp.int32)
    valid_table = (positions[None, :] < lengths[:, None]).astype(jnp.float32)
    row_valid = valid_table.reshape(row_count, 1)
    forward_set = (
        lax.all_gather(rand_mix, ("wide", "narrow"), axis=0, tiled=True),
        lax.all_gather(w_value, ("wide", "narrow"), axis=0, tiled=True),
        lax.all_gather(w_out, ("wide", "narrow"), axis=0, tiled=True),
        lax.all_gather(w_up, ("wide", "narrow"), axis=0, tiled=True),
        lax.all_gather(w_down, ("wide", "narrow"), axis=0, tiled=True),
        lax.all_gather(gain_mix, ("wide", "narrow"), axis=0, tiled=True),
        lax.all_gather(gain_ffn, ("wide", "narrow"), axis=0, tiled=True),
    )
    rand_all, value_all, out_all, up_all, down_all, gain_first, gain_second = forward_set
    normed = rms_norm(tokens_flat, gain_first.astype(jnp.float32)).astype(jnp.bfloat16)
    values = jnp.dot(normed, value_all, preferred_element_type=jnp.float32).astype(jnp.bfloat16)
    rand_heads = rand_all.reshape(HEADS, LMAX, LMAX)
    mixed_parts = []
    totals_kept = []
    for item_index in range(item_count):
        item_values = split_heads(values[item_index * LMAX : (item_index + 1) * LMAX])
        mixed_heads, log_total = lax.map(
            partial(head_forward, valid_table[item_index]), (rand_heads, item_values)
        )
        mixed_parts.append(merge_heads(mixed_heads))
        totals_kept.append(log_total)
    mixed = jnp.concatenate(mixed_parts, axis=0)
    residual = tokens_flat + jnp.dot(mixed, out_all, preferred_element_type=jnp.float32)
    normed_two = rms_norm(residual, gain_second.astype(jnp.float32)).astype(jnp.bfloat16)
    up_proj = jnp.dot(normed_two, up_all, preferred_element_type=jnp.float32)
    active = jax.nn.gelu(up_proj).astype(jnp.bfloat16)
    branch = jnp.dot(active, down_all, preferred_element_type=jnp.float32)
    output = row_valid * (residual + branch)
    back_set = (
        lax.all_gather(rand_mix, ("wide", "narrow"), axis=0, tiled=True),
        lax.all_gather(w_value, ("wide", "narrow"), axis=0, tiled=True),
        lax.all_gather(w_out, ("wide", "narrow"), axis=0, tiled=True),
        lax.all_gather(w_up, ("wide", "narrow"), axis=0, tiled=True),
        lax.all_gather(w_down, ("wide", "narrow"), axis=0, tiled=True),
        lax.all_gather(gain_mix, ("wide", "narrow"), axis=0, tiled=True),
        lax.all_gather(gain_ffn, ("wide", "narrow"), axis=0, tiled=True),
    )
    rand_back, value_back, out_back, up_back, down_back, gain_back_one, gain_back_two = back_set
    cotangent = grad_out.reshape(row_count, width).astype(jnp.float32)
    masked = row_valid * cotangent
    branch_grad = masked.astype(jnp.bfloat16)
    grad_down = jnp.einsum("rk,rd->kd", active, branch_grad, preferred_element_type=jnp.float32)
    active_grad = jnp.einsum(
        "rd,kd->rk", branch_grad, down_back, preferred_element_type=jnp.float32
    )
    gelu_value, gelu_pull = jax.vjp(jax.nn.gelu, up_proj)
    up_grad = gelu_pull(active_grad)[0].astype(jnp.bfloat16)
    grad_up = jnp.einsum("rd,rk->dk", normed_two, up_grad, preferred_element_type=jnp.float32)
    normed_two_grad = jnp.einsum("rk,dk->rd", up_grad, up_back, preferred_element_type=jnp.float32)
    norm_value, norm_pull = jax.vjp(rms_norm, residual, gain_back_two.astype(jnp.float32))
    residual_part, gain_two_grad = norm_pull(normed_two_grad)
    residual_grad = masked + residual_part
    attn_grad = residual_grad.astype(jnp.bfloat16)
    grad_outproj = jnp.einsum("rd,re->de", mixed, attn_grad, preferred_element_type=jnp.float32)
    mixed_grad = jnp.einsum(
        "re,de->rd", attn_grad, out_back, preferred_element_type=jnp.float32
    ).astype(jnp.bfloat16)
    rand_heads_back = rand_back.reshape(HEADS, LMAX, LMAX)
    rand_grad = jnp.zeros((HEADS, LMAX, LMAX), jnp.float32)
    value_parts = []
    for item_index in range(item_count):
        lower_row = item_index * LMAX
        upper_row = lower_row + LMAX
        item_values = split_heads(values[lower_row:upper_row])
        item_mix_grad = split_heads(mixed_grad[lower_row:upper_row])
        score_grad, value_grad = lax.map(
            partial(head_backward, valid_table[item_index]),
            (rand_heads_back, item_values, item_mix_grad, totals_kept[item_index]),
        )
        rand_grad = rand_grad + score_grad
        value_parts.append(merge_heads(value_grad))
    values_grad = jnp.concatenate(value_parts, axis=0).astype(jnp.bfloat16)
    grad_value = jnp.einsum("rd,re->de", normed, values_grad, preferred_element_type=jnp.float32)
    normed_grad = jnp.einsum(
        "re,de->rd", values_grad, value_back, preferred_element_type=jnp.float32
    )
    norm_first, first_pull = jax.vjp(rms_norm, tokens_flat, gain_back_one.astype(jnp.float32))
    token_part, gain_one_grad = first_pull(normed_grad)
    tokens_grad = residual_grad + token_part
    rand_flat = rand_grad.reshape(HEADS * LMAX, LMAX)
    all_shards = (
        lax.psum_scatter(rand_flat, ("wide", "narrow"), scatter_dimension=0, tiled=True),
        lax.psum_scatter(grad_value, ("wide", "narrow"), scatter_dimension=0, tiled=True),
        lax.psum_scatter(grad_outproj, ("wide", "narrow"), scatter_dimension=0, tiled=True),
        lax.psum_scatter(grad_up, ("wide", "narrow"), scatter_dimension=0, tiled=True),
        lax.psum_scatter(grad_down, ("wide", "narrow"), scatter_dimension=0, tiled=True),
        lax.psum_scatter(gain_one_grad, ("wide", "narrow"), scatter_dimension=0, tiled=True),
        lax.psum_scatter(gain_two_grad, ("wide", "narrow"), scatter_dimension=0, tiled=True),
    )
    rand_shard, value_shard, outproj_shard, up_shard, down_shard, gain_one_shard, gain_two_shard = (
        all_shards
    )
    return (
        output.reshape(item_count, LMAX, width),
        tokens_grad.reshape(item_count, LMAX, width),
        rand_shard,
        value_shard,
        outproj_shard,
        up_shard,
        down_shard,
        gain_one_shard,
        gain_two_shard,
    )


def solution(mesh):
    in_specs = (
        P(("wide", "narrow"), None, None),
        P(("wide", "narrow")),
        P(("wide", "narrow"), None),
        P(("wide", "narrow"), None),
        P(("wide", "narrow"), None),
        P(("wide", "narrow"), None),
        P(("wide", "narrow"), None),
        P(("wide", "narrow")),
        P(("wide", "narrow")),
        P(("wide", "narrow"), None, None),
    )
    out_specs = (
        P(("wide", "narrow"), None, None),
        P(("wide", "narrow"), None, None),
        P(("wide", "narrow"), None),
        P(("wide", "narrow"), None),
        P(("wide", "narrow"), None),
        P(("wide", "narrow"), None),
        P(("wide", "narrow"), None),
        P(("wide", "narrow")),
        P(("wide", "narrow")),
    )
    fits = dict(mesh.shape) == {"wide": 16, "narrow": 2}
    return jax.shard_map(chip_shards if fits else shards, mesh=mesh, in_specs=in_specs, out_specs=out_specs, check_vma=False)
```

```python
from functools import partial

import jax
import jax.numpy as jnp
from jax import lax
from jax.experimental import pallas as pl
from jax.experimental.pallas import tpu as pltpu
from jax.sharding import PartitionSpec as P

HEADS = 12
HEAD = 64
LMAX = 1024
WIDTH = 768
FF = 3072
EPSILON = 1e-05

BOTH = ("wide", "narrow")
BF16 = jnp.bfloat16
F32 = jnp.float32
VMEM = 61 << 20
LESS = 34 << 20

SUBS = 6
RUNS = 8
HALF = 64
HROWS = RUNS * HALF
PLANES = 4
PHEADS = HEADS // PLANES
ROWS = 2 * LMAX
FSTEP = 768
FSIDE = FF // 2 // FSTEP
TILE = 512
SIDE = WIDTH // 2
SPAN = 2 * HALF


def dot(a, b, ca, cb):
    return lax.dot_general(a, b, (((ca,), (cb,)), ((), ())), preferred_element_type=F32)


CORE, PLANE, PLACE, LENGTHS = 0, 1, 2, 3


def spec(shape, index):
    return pl.BlockSpec(shape, index)


def held(shape):
    zeros = (0,) * len(shape)
    return pl.BlockSpec(shape, lambda *_: zeros, pipeline_mode=pl.Buffered(1))


def params(limit):
    return pltpu.CompilerParams(vmem_limit_bytes=limit)


def whole_weight(sc, step, own, far, weight):
    @pl.when(step == 0)
    def _():
        weight[:, pl.ds(pl.multiple_of(sc[CORE] * SIDE, 128), SIDE)] = own[...]
        weight[:, pl.ds(pl.multiple_of((1 - sc[CORE]) * SIDE, 128), SIDE)] = far[...]


def values_kernel(sc, tok, gain, w_own, w_far, out, weight):
    step = pl.program_id(0)
    whole_weight(sc, step, w_own, w_far, weight)
    rows = tok.shape[1]
    position = step * rows + lax.broadcasted_iota(jnp.int32, (rows, 1), 0)
    for item in range(2):
        x = tok[item].astype(F32)
        scale = lax.rsqrt(jnp.mean(x * x, axis=-1, keepdims=True) + EPSILON)
        normed = (x * scale * gain[...]).astype(BF16)
        found = dot(normed, weight[...], 1, 0)
        found = jnp.where(position < sc[LENGTHS + item], found, 0.0).astype(BF16)
        for head in range(HEADS):
            out[head, :, item * HEAD : (item + 1) * HEAD] = found[:, head * HEAD : (head + 1) * HEAD]


def run_values(sc, tokens, gain, w_own, w_far):
    rows = 256
    return pl.pallas_call(
        values_kernel,
        grid_spec=pltpu.PrefetchScalarGridSpec(
            num_scalar_prefetch=1,
            grid=(LMAX // rows,),
            in_specs=[
                spec((2, rows, WIDTH), lambda j, s: (0, j, 0)),
                held((1, WIDTH)),
                held((WIDTH, SIDE)),
                held((WIDTH, SIDE)),
            ],
            out_specs=spec((HEADS, rows, 2 * HEAD), lambda j, s: (0, j, 0)),
            scratch_shapes=[pltpu.VMEM((WIDTH, WIDTH), BF16)],
        ),
        out_shape=jax.ShapeDtypeStruct((HEADS, LMAX, 2 * HEAD), BF16),
        compiler_params=params(VMEM),
        cost_estimate=pl.CostEstimate(
            flops=2 * 2 * LMAX * WIDTH * WIDTH, bytes_accessed=8 * LMAX * WIDTH, transcendentals=0
        ),
        name="values",
    )(sc, tokens, gain, w_own, w_far)


def lane_lengths(sc, shape):
    slot = lax.broadcasted_iota(jnp.int32, shape, 1) // HEAD
    length = jnp.where(slot == 0, sc[LENGTHS], sc[LENGTHS + 1])
    return jnp.where(slot >= 2, jnp.where(slot == 2, sc[LENGTHS + 2], sc[LENGTHS + 3]), length)


def plane_of(k, sc):
    return lax.rem(sc[PLANE] + PLANES - k, PLANES)


def plane_spec(planes, rows, lanes):
    def index(step, sc):
        return (plane_of(planes[0] + step * (planes[-1] - planes[0]) // max(len(planes) - 1, 1), sc), 0, 0)

    return spec((PHEADS, rows, lanes), index)


def anywhere(count):
    return [pl.BlockSpec(memory_space=pl.ANY)] * count


def plane_fetch(place, shards, raw, sems, slot):
    return [
        pltpu.make_async_copy(
            shards[4 * slot + rel],
            raw.at[slot, pl.ds(pl.multiple_of((place ^ rel) * SUBS * HALF, SUBS * HALF), SUBS * HALF)],
            sems.at[slot, rel],
        )
        for rel in range(4)
    ]


def take_plane(place, shards, raw, sems):
    step = pl.program_id(0)
    count = len(shards) // 4

    @pl.when(step == 0)
    def _():
        for slot in range(count):
            for copy in plane_fetch(place, shards, raw, sems, slot):
                copy.start()

    for slot in range(count):

        @pl.when(step == slot)
        def _():
            for copy in plane_fetch(place, shards, raw, sems, slot):
                copy.wait()

    return step


def head_rows(head):
    return slice(head * HROWS, (head + 1) * HROWS)


def fill_mask(sc, mask):
    @pl.when(pl.program_id(0) == 0)
    def _():
        shape = (LMAX, 4 * HEAD)
        column = lax.broadcasted_iota(jnp.int32, shape, 0)
        mask[...] = (column < lane_lengths(sc, shape)).astype(F32).astype(BF16)


def mix_kernel(count, carried, sc, *refs):
    shards, (v_own, v_far, *rest) = refs[: 4 * count], refs[4 * count :]
    mixed, mean, exps, inverse, raw, mask, sems = rest[4:] if carried else rest
    fill_mask(sc, mask)
    slot = take_plane(sc[PLACE], shards, raw, sems)
    shape = (HROWS, 4 * HEAD)
    line = lax.broadcasted_iota(jnp.int32, shape, 0)
    position = 128 * (line // HALF) + HALF * sc[CORE] + line % HALF
    valid = position < lane_lengths(sc, shape)
    for head in range(PHEADS):
        weights = jnp.exp(raw[slot, head_rows(head)].astype(F32)).astype(BF16)
        exps[head] = weights
        both = dot(weights, jnp.concatenate([v_own[head], v_far[head], mask[...]], axis=1), 1, 0)
        flip = jnp.where(valid, 1.0 / both[:, 4 * HEAD :], 0.0)
        found = both[:, : 4 * HEAD] * flip
        inverse[head] = flip.astype(BF16)
        mean[head] = found
        mixed[head] = found.astype(BF16)


def run_mix(sc, planes, shards, v_own, v_far, carry):
    carry, count = list(carry), len(planes)
    shape = (HEADS, HROWS, 4 * HEAD)
    return pl.pallas_call(
        partial(mix_kernel, count, bool(carry)),
        grid_spec=pltpu.PrefetchScalarGridSpec(
            num_scalar_prefetch=1,
            grid=(count,),
            in_specs=anywhere(4 * count) + [plane_spec(planes, LMAX, 2 * HEAD)] * 2 + anywhere(len(carry)),
            out_specs=[
                plane_spec(planes, HROWS, 4 * HEAD),
                plane_spec(planes, HROWS, 4 * HEAD),
                plane_spec(planes, HROWS, LMAX),
                plane_spec(planes, HROWS, 4 * HEAD),
            ],
            scratch_shapes=[
                pltpu.VMEM((count, 4 * SUBS * HALF, LMAX), BF16),
                pltpu.VMEM((LMAX, 4 * HEAD), BF16),
                pltpu.SemaphoreType.DMA((count, 4)),
            ],
        ),
        out_shape=[
            jax.ShapeDtypeStruct(shape, BF16),
            jax.ShapeDtypeStruct(shape, F32),
            jax.ShapeDtypeStruct((HEADS, HROWS, LMAX), BF16),
            jax.ShapeDtypeStruct(shape, BF16),
        ],
        input_output_aliases={3 + 4 * count + i: i for i in range(len(carry))},
        compiler_params=params(VMEM),
        cost_estimate=pl.CostEstimate(
            flops=2 * HEADS * HROWS * LMAX * 4 * HEAD,
            bytes_accessed=HEADS * (2 * HROWS * LMAX + 5 * HROWS * 256),
            transcendentals=HEADS * HROWS * LMAX // 2,
        ),
        name="mix",
    )(sc, *shards, v_own, v_far, *carry)


def row_valid(sc, step):
    line = lax.broadcasted_iota(jnp.int32, (4 * SPAN, 1), 0)
    item = line // SPAN
    row = step * SPAN + line % SPAN
    low = jnp.where(item == 0, sc[LENGTHS], sc[LENGTHS + 1])
    high = jnp.where(item == 2, sc[LENGTHS + 2], sc[LENGTHS + 3])
    return 128 * (row // HALF) + HALF * sc[CORE] + row % HALF < jnp.where(item >= 2, high, low)


def four_items(own, far):
    return jnp.concatenate([own[:, :, 0], far[...]], axis=0).reshape(4 * SPAN, WIDTH)


def pre_kernel(sc, tok, tok_far, heads, wo_own, wo_far, gain, mixed, resid, normed, weight):
    step = pl.program_id(0)
    whole_weight(sc, step, wo_own, wo_far, weight)
    for item in range(4):
        lanes = slice(item * HEAD, (item + 1) * HEAD)
        for pair in range(HEADS // 2):
            both = jnp.concatenate([heads[2 * pair, :, lanes], heads[2 * pair + 1, :, lanes]], axis=1)
            mixed[item, :, pair * 128 : (pair + 1) * 128] = both
    res = four_items(tok, tok_far).astype(F32) + dot(mixed[...].reshape(4 * SPAN, WIDTH), weight[...], 1, 0)
    resid[...] = res.astype(BF16).reshape(4, SPAN, WIDTH)
    scale = lax.rsqrt(jnp.mean(res * res, axis=-1, keepdims=True) + EPSILON)
    valid = row_valid(sc, step)
    normed[...] = jnp.where(valid, res * scale * gain[...], 0.0).astype(BF16).reshape(4, SPAN, WIDTH)


def slab_spec(items=4):
    return spec((items, SPAN, WIDTH), lambda r, s: (0, r, 0))


def half_specs():
    return [
        spec((2, SPAN // HALF, 1, HALF, WIDTH), lambda r, s: (0, r, s[CORE], 0, 0)),
        spec((2, SPAN // HALF, HALF, WIDTH), lambda r, s: (0, r, 0, 0)),
    ]


def heads_spec():
    return spec((HEADS, SPAN, 4 * HEAD), lambda r, s: (0, r, 0))


def run_pre(sc, tokens, tokens_far, heads, wo, gain):
    return pl.pallas_call(
        pre_kernel,
        grid_spec=pltpu.PrefetchScalarGridSpec(
            num_scalar_prefetch=1,
            grid=(HROWS // SPAN,),
            in_specs=half_specs()
            + [heads_spec(), held((WIDTH, SIDE)), held((WIDTH, SIDE)), held((1, WIDTH))],
            out_specs=[slab_spec()] * 3,
            scratch_shapes=[pltpu.VMEM((WIDTH, WIDTH), BF16)],
        ),
        out_shape=[
            jax.ShapeDtypeStruct((4, HROWS, WIDTH), BF16),
            jax.ShapeDtypeStruct((4, HROWS, WIDTH), BF16),
            jax.ShapeDtypeStruct((4, HROWS, WIDTH), BF16),
        ],
        compiler_params=params(VMEM),
        cost_estimate=pl.CostEstimate(
            flops=2 * ROWS * WIDTH * WIDTH, bytes_accessed=16 * ROWS * WIDTH, transcendentals=0
        ),
        name="pre",
    )(sc, tokens, tokens_far, heads, *wo, gain)


def masked_kernel(sc, cot, cot_far, masked):
    value = jnp.where(row_valid(sc, pl.program_id(0)), four_items(cot, cot_far).astype(F32), 0.0)
    masked[...] = value.astype(BF16).reshape(4, SPAN, WIDTH)


def run_masked(sc, cotangent, cotangent_far):
    return pl.pallas_call(
        masked_kernel,
        grid_spec=pltpu.PrefetchScalarGridSpec(
            num_scalar_prefetch=1, grid=(HROWS // SPAN,), in_specs=half_specs(), out_specs=slab_spec()
        ),
        out_shape=jax.ShapeDtypeStruct((4, HROWS, WIDTH), BF16),
        compiler_params=params(VMEM),
        cost_estimate=pl.CostEstimate(flops=0, bytes_accessed=4 * ROWS * WIDTH, transcendentals=0),
        name="masked",
    )(sc, cotangent, cotangent_far)


def own_lanes(sc):
    return pl.ds(pl.multiple_of(sc[CORE] * SIDE, 128), SIDE)


def far_lanes(sc):
    return pl.ds(pl.multiple_of((1 - sc[CORE]) * SIDE, 128), SIDE)


def unit_rows(f, sc):
    return (lax.rem(FSIDE * sc[CORE] + f, 2 * FSIDE), 0)


def unit_columns(f, sc):
    return (0, lax.rem(FSIDE * sc[CORE] + f, 2 * FSIDE))


def early(f, sc):
    return (0, lax.min(f, FSIDE - 1))


def late(f, sc):
    return (0, lax.max(f - FSIDE, 0))


def units_kernel(sc, normed, cot, up_own, up_far, dn_own, dn_far, active, up_grad, w_up, w_down):
    step = pl.program_id(0)
    w_down[:, own_lanes(sc)] = dn_own[...]
    w_down[:, far_lanes(sc)] = dn_far[...]

    @pl.when(step < FSIDE)
    def _():
        w_up[...] = up_own[...]

    @pl.when(step >= FSIDE)
    def _():
        w_up[...] = up_far[...]

    for row in range(0, ROWS, 256):
        rows = slice(row, row + 256)
        for column in range(0, FSTEP, 256):
            columns = slice(column, column + 256)
            up = dot(normed[rows], w_up[:, columns], 1, 0)
            square = up * up
            bend = jnp.tanh(up * (0.7978845608028654 + (0.044715 * 0.7978845608028654) * square))
            share = 0.5 + 0.5 * bend
            act = up * share
            active[rows, columns] = act.astype(BF16)
            slope = share + act * (1.0 - share) * (
                2 * 0.7978845608028654 + (6 * 0.044715 * 0.7978845608028654) * square
            )
            up_grad[rows, columns] = (dot(cot[rows], w_down[columns], 1, 1) * slope).astype(BF16)


def run_units(sc, normed, cotangent, up, down):
    return pl.pallas_call(
        units_kernel,
        grid_spec=pltpu.PrefetchScalarGridSpec(
            num_scalar_prefetch=1,
            grid=(2 * FSIDE,),
            in_specs=[
                held((ROWS, WIDTH)),
                held((ROWS, WIDTH)),
                spec((WIDTH, FSTEP), early),
                spec((WIDTH, FSTEP), late),
                spec((FSTEP, SIDE), unit_rows),
                spec((FSTEP, SIDE), unit_rows),
            ],
            out_specs=[spec((ROWS, FSTEP), unit_columns), spec((ROWS, FSTEP), unit_columns)],
            scratch_shapes=[pltpu.VMEM((WIDTH, FSTEP), BF16), pltpu.VMEM((FSTEP, WIDTH), BF16)],
        ),
        out_shape=[jax.ShapeDtypeStruct((ROWS, FF), BF16), jax.ShapeDtypeStruct((ROWS, FF), BF16)],
        compiler_params=params(VMEM),
        cost_estimate=pl.CostEstimate(
            flops=4 * ROWS * WIDTH * FF, bytes_accessed=6 * ROWS * WIDTH + 4 * ROWS * FF, transcendentals=ROWS * FF
        ),
        name="units",
    )(sc, normed.reshape(ROWS, WIDTH), cotangent.reshape(ROWS, WIDTH), *up, *down)


def down_grad_kernel(sc, active, cot, own, far, total):
    total[...] = dot(active[...], cot[...], 0, 0).astype(BF16)
    own[...] = total[:, own_lanes(sc)]
    far[...] = total[:, far_lanes(sc)]


def run_down_grad(sc, active, cotangent):
    return pl.pallas_call(
        down_grad_kernel,
        grid_spec=pltpu.PrefetchScalarGridSpec(
            num_scalar_prefetch=1,
            grid=(FF // 512,),
            in_specs=[spec((ROWS, 512), lambda f, s: (0, f)), held((ROWS, WIDTH))],
            out_specs=[spec((512, SIDE), lambda f, s: (f, 0))] * 2,
            scratch_shapes=[pltpu.VMEM((512, WIDTH), BF16)],
        ),
        out_shape=[jax.ShapeDtypeStruct((FF, SIDE), BF16)] * 2,
        compiler_params=params(57 << 20),
        cost_estimate=pl.CostEstimate(
            flops=2 * ROWS * WIDTH * FF, bytes_accessed=2 * ROWS * (WIDTH + FF), transcendentals=0
        ),
        name="down_grad",
    )(sc, active, cotangent.reshape(ROWS, WIDTH))


def up_grad_kernel(sc, normed, up_grad, own, far):
    total = dot(normed[...], up_grad[...], 0, 0).astype(BF16)

    @pl.when(pl.program_id(0) < 3)
    def _():
        own[...] = total

    @pl.when(pl.program_id(0) >= 3)
    def _():
        far[...] = total


def run_up_grad(sc, normed, up_grad):
    return pl.pallas_call(
        up_grad_kernel,
        grid_spec=pltpu.PrefetchScalarGridSpec(
            num_scalar_prefetch=1,
            grid=(6,),
            in_specs=[held((ROWS, WIDTH)), spec((ROWS, 512), lambda f, s: (0, lax.rem(3 * s[CORE] + f, 6)))],
            out_specs=[
                spec((WIDTH, 512), lambda f, s: (0, lax.min(f, 2))),
                spec((WIDTH, 512), lambda f, s: (0, lax.max(f - 3, 0))),
            ],
        ),
        out_shape=[jax.ShapeDtypeStruct((WIDTH, FF // 2), BF16)] * 2,
        compiler_params=params(57 << 20),
        cost_estimate=pl.CostEstimate(
            flops=2 * ROWS * WIDTH * FF, bytes_accessed=2 * ROWS * (WIDTH + FF), transcendentals=0
        ),
        name="up_grad",
    )(sc, normed.reshape(ROWS, WIDTH), up_grad)


def out_grad_kernel(sc, mixed, res_own, res_far, own, far, total):
    step = pl.program_id(0)
    grad = jnp.concatenate([res_own[...], res_far[...]], axis=0).reshape(4 * SPAN, WIDTH)
    found = dot(mixed[...].reshape(4 * SPAN, WIDTH), grad, 0, 0)

    @pl.when(step == 0)
    def _():
        total[...] = found

    @pl.when(step > 0)
    def _():
        total[...] += found

    @pl.when(step == pl.num_programs(0) - 1)
    def _():
        own[...] = total[:, own_lanes(sc)].astype(BF16)
        far[...] = total[:, far_lanes(sc)].astype(BF16)


def run_out_grad(sc, mixed, res_own, res_far):
    return pl.pallas_call(
        out_grad_kernel,
        grid_spec=pltpu.PrefetchScalarGridSpec(
            num_scalar_prefetch=1,
            grid=(HROWS // SPAN,),
            in_specs=[slab_spec(), slab_spec(2), slab_spec(2)],
            out_specs=[held((WIDTH, SIDE))] * 2,
            scratch_shapes=[pltpu.VMEM((WIDTH, WIDTH), F32)],
        ),
        out_shape=[jax.ShapeDtypeStruct((WIDTH, SIDE), BF16)] * 2,
        compiler_params=params(LESS),
        cost_estimate=pl.CostEstimate(
            flops=2 * ROWS * WIDTH * WIDTH, bytes_accessed=4 * ROWS * WIDTH, transcendentals=0
        ),
        name="out_grad",
    )(sc, mixed, res_own, res_far)


def out_kernel(sc, active, resid, dn_own, dn_far, own, far, w_down):
    step = pl.program_id(0)

    @pl.when(step == 0)
    def _():
        w_down[:, own_lanes(sc)] = dn_own[...]
        w_down[:, far_lanes(sc)] = dn_far[...]

    branch = dot(active[...].reshape(4 * SPAN, FF), w_down[...], 1, 0)
    output = jnp.where(row_valid(sc, step), resid[...].reshape(4 * SPAN, WIDTH).astype(F32) + branch, 0.0)
    output = output.astype(BF16).reshape(4, SPAN, WIDTH)
    own[...] = output[:2]
    far[...] = output[2:]


def run_out(sc, active, resid, down):
    return pl.pallas_call(
        out_kernel,
        grid_spec=pltpu.PrefetchScalarGridSpec(
            num_scalar_prefetch=1,
            grid=(HROWS // SPAN,),
            in_specs=[
                spec((4, SPAN, FF), lambda r, s: (0, r, 0)),
                slab_spec(),
                held((FF, SIDE)),
                held((FF, SIDE)),
            ],
            out_specs=[slab_spec(2)] * 2,
            scratch_shapes=[pltpu.VMEM((FF, WIDTH), BF16)],
        ),
        out_shape=[
            jax.ShapeDtypeStruct((2, HROWS, WIDTH), BF16),
            jax.ShapeDtypeStruct((2, HROWS, WIDTH), BF16),
        ],
        compiler_params=params(LESS),
        cost_estimate=pl.CostEstimate(
            flops=2 * ROWS * WIDTH * FF, bytes_accessed=ROWS * (2 * FF + 7 * WIDTH), transcendentals=0
        ),
        name="out",
    )(sc, active.reshape(4, HROWS, FF), resid, *down)


def post_kernel(sc, resid, grad_own, grad_far, cot, up_own, up_far, wo_own, wo_far, gain, *refs):
    (res_own, res_far, heads, d_gain, weight, spread) = refs
    step = pl.program_id(0)
    whole_weight(sc, step, wo_own, wo_far, weight)
    shape, slab = (4 * SPAN, WIDTH), (4, SPAN, WIDTH)
    valid = row_valid(sc, step)
    res = resid[...].reshape(shape).astype(F32)
    scale = lax.rsqrt(jnp.mean(res * res, axis=-1, keepdims=True) + EPSILON)
    unit = res * scale
    units = (4 * SPAN, FF // 2)
    back = dot(grad_own[...].reshape(units), up_own[...], 1, 1) + dot(grad_far[...].reshape(units), up_far[...], 1, 1)
    two_grad = jnp.where(valid, back, 0.0)
    gained = two_grad * gain[...]
    masked = cot[...].reshape(shape).astype(F32)
    grad = masked + scale * (gained - unit * jnp.mean(gained * unit, axis=-1, keepdims=True))
    low = grad.astype(BF16)
    res_own[...] = low.reshape(slab)[:2]
    res_far[...] = low.reshape(slab)[2:]
    gain_sum = jnp.sum(two_grad * unit, axis=0, keepdims=True)

    @pl.when(step == 0)
    def _():
        d_gain[...] = gain_sum

    @pl.when(step > 0)
    def _():
        d_gain[...] += gain_sum

    spread[...] = dot(low, weight[...], 1, 1).astype(BF16).reshape(slab)
    for pair in range(HEADS // 2):
        lanes = slice(pair * 128, (pair + 1) * 128)
        for side in range(2):
            one, two = spread[2 * side, :, lanes], spread[2 * side + 1, :, lanes]
            half = slice(side * 128, (side + 1) * 128)
            heads[2 * pair, :, half] = jnp.concatenate([one[:, :HEAD], two[:, :HEAD]], axis=1)
            heads[2 * pair + 1, :, half] = jnp.concatenate([one[:, HEAD:], two[:, HEAD:]], axis=1)


def run_post(sc, resid, up_grad, cotangent, up, wo, gain):
    side = lambda which: spec((4, SPAN, FF // 2), lambda r, s: (0, r, s[CORE] if which == 0 else 1 - s[CORE]))
    up_grad = up_grad.reshape(4, HROWS, FF)
    return pl.pallas_call(
        post_kernel,
        grid_spec=pltpu.PrefetchScalarGridSpec(
            num_scalar_prefetch=1,
            grid=(HROWS // SPAN,),
            in_specs=[
                slab_spec(),
                side(0),
                side(1),
                slab_spec(),
                held((WIDTH, FF // 2)),
                held((WIDTH, FF // 2)),
                held((WIDTH, SIDE)),
                held((WIDTH, SIDE)),
                held((1, WIDTH)),
            ],
            out_specs=[slab_spec(2)] * 2 + [heads_spec(), held((1, WIDTH))],
            scratch_shapes=[
                pltpu.VMEM((WIDTH, WIDTH), BF16),
                pltpu.VMEM((4, SPAN, WIDTH), BF16),
            ],
        ),
        out_shape=[
            jax.ShapeDtypeStruct((2, HROWS, WIDTH), BF16),
            jax.ShapeDtypeStruct((2, HROWS, WIDTH), BF16),
            jax.ShapeDtypeStruct((HEADS, HROWS, 4 * HEAD), BF16),
            jax.ShapeDtypeStruct((1, WIDTH), F32),
        ],
        compiler_params=params(VMEM),
        cost_estimate=pl.CostEstimate(
            flops=2 * ROWS * WIDTH * (WIDTH + FF), bytes_accessed=ROWS * (16 * WIDTH + 2 * FF), transcendentals=0
        ),
        name="post",
    )(sc, resid, up_grad, up_grad, cotangent, *up, *wo, gain)


def unmix_kernel(count, carried, sc, v_own, v_far, grad_heads, mean, exps, inverse, *refs):
    refs = refs[2:] if carried else refs
    outs, (own, far, grads, mask, adder, bound, out_sems) = refs[: 4 * count], refs[4 * count :]
    place = sc[PLACE]
    step = pl.program_id(0)

    def leave(slot):
        return [
            pltpu.make_async_copy(
                grads.at[slot, pl.ds(pl.multiple_of((place ^ rel) * SUBS * HALF, SUBS * HALF), SUBS * HALF)],
                outs[4 * slot + rel],
                out_sems.at[slot, rel],
            )
            for rel in range(4)
        ]

    fill_mask(sc, mask)

    @pl.when(step == 0)
    def _():
        lane = lax.broadcasted_iota(jnp.int32, (4 * HEAD, 128), 0) // HEAD
        column = lax.broadcasted_iota(jnp.int32, (4 * HEAD, 128), 1)
        adder[...] = jnp.where((lane == column) | (lane + 4 == column), -1.0, 0.0).astype(BF16)
        row = lax.broadcasted_iota(jnp.int32, (LMAX, 128), 0)
        item = lax.broadcasted_iota(jnp.int32, (LMAX, 128), 1)
        length = jnp.where(item % 4 == 0, sc[LENGTHS], sc[LENGTHS + 1])
        length = jnp.where(item % 4 == 2, sc[LENGTHS + 2], length)
        length = jnp.where(item % 4 == 3, sc[LENGTHS + 3], length)
        bound[...] = jnp.where((item < 8) & (row < length), 1.0, 0.0).astype(BF16)

    high_lanes = lax.broadcasted_iota(jnp.int32, (HROWS, 128), 1) < 4
    for head in range(PHEADS):
        weights = exps[head]
        low = (grad_heads[head].astype(F32) * inverse[head].astype(F32)).astype(BF16)
        product = low.astype(F32) * mean[head]
        coarse = product.astype(BF16)
        fine = (product - coarse.astype(F32)).astype(BF16)
        delta = dot(coarse, adder[...], 1, 0) + dot(fine, adder[...], 1, 0)
        coarse = delta.astype(BF16)
        fine = (delta - coarse.astype(F32)).astype(BF16)
        left = jnp.concatenate([low, jnp.where(high_lanes, coarse, fine)], axis=1)
        score = dot(left, jnp.concatenate([v_own[head], v_far[head], bound[...]], axis=1), 1, 1)
        grads[step, head_rows(head)] = (score * weights.astype(F32)).astype(BF16)
        back = (dot(weights, low, 0, 0) * mask[...].astype(F32)).astype(BF16)
        own[head] = back[:, : 2 * HEAD]
        far[head] = back[:, 2 * HEAD :]
    for which in range(count):

        @pl.when(step == which)
        def _():
            for copy in leave(which):
                copy.start()
            if which == count - 1:
                for slot in range(count):
                    for copy in leave(slot):
                        copy.wait()


def run_unmix(sc, planes, v_own, v_far, grad_heads, mean, exps, inverse, carry):
    carry, count = list(carry), len(planes)
    return pl.pallas_call(
        partial(unmix_kernel, count, bool(carry)),
        grid_spec=pltpu.PrefetchScalarGridSpec(
            num_scalar_prefetch=1,
            grid=(count,),
            in_specs=[
                plane_spec(planes, LMAX, 2 * HEAD),
                plane_spec(planes, LMAX, 2 * HEAD),
                plane_spec(planes, HROWS, 4 * HEAD),
                plane_spec(planes, HROWS, 4 * HEAD),
                plane_spec(planes, HROWS, LMAX),
                plane_spec(planes, HROWS, 4 * HEAD),
            ]
            + anywhere(len(carry)),
            out_specs=anywhere(4 * count) + [plane_spec(planes, LMAX, 2 * HEAD)] * 2,
            scratch_shapes=[
                pltpu.VMEM((count, 4 * SUBS * HALF, LMAX), BF16),
                pltpu.VMEM((LMAX, 4 * HEAD), BF16),
                pltpu.VMEM((4 * HEAD, 128), BF16),
                pltpu.VMEM((LMAX, 128), BF16),
                pltpu.SemaphoreType.DMA((count, 4)),
            ],
        ),
        out_shape=[jax.ShapeDtypeStruct((SUBS * HALF, LMAX), BF16)] * (4 * count)
        + [jax.ShapeDtypeStruct((HEADS, LMAX, 2 * HEAD), BF16)] * 2,
        input_output_aliases={7 + i: 4 * count + i for i in range(len(carry))},
        compiler_params=params(VMEM),
        cost_estimate=pl.CostEstimate(
            flops=3 * HEADS * HROWS * LMAX * 4 * HEAD,
            bytes_accessed=HEADS * (2 * HROWS * LMAX + 5 * HROWS * 256 + 4 * LMAX * 256),
            transcendentals=0,
        ),
        name="unmix",
    )(sc, v_own, v_far, grad_heads, mean, exps, inverse, *carry)


def close_kernel(sc, tok, res_own, res_got, own, far, gain, w_own, w_far, *refs):
    (tok_grad, d_value, d_gain, total, weight) = refs
    step = pl.program_id(0)
    whole_weight(sc, step, w_own, w_far, weight)
    core = sc[CORE]
    tok_grad[:, :, core] = res_own[...].astype(F32)
    tok_grad[:, :, 1 - core] = res_got[...].astype(F32)
    runs = tok.shape[1]
    rows = runs * 128
    for item in range(2):
        lanes = slice(item * HEAD, (item + 1) * HEAD)
        pieces = [
            add_low(own[head, :, lanes], far[head, :, lanes]) for head in range(HEADS)
        ]
        back = jnp.concatenate(pieces, axis=1)
        x = tok[item].reshape(rows, WIDTH).astype(F32)
        scale = lax.rsqrt(jnp.mean(x * x, axis=-1, keepdims=True) + EPSILON)
        unit = x * scale
        normed = (unit * gain[...]).astype(BF16)
        normed_grad = dot(back, weight[...], 1, 1)
        gained = normed_grad * gain[...]
        update = scale * (gained - unit * jnp.mean(gained * unit, axis=-1, keepdims=True))
        tok_grad[item] += update.reshape(runs, 2, HALF, WIDTH)
        gain_sum = jnp.sum(normed_grad * unit, axis=0, keepdims=True)
        value_sum = dot(normed, back, 0, 0)
        if item == 0:
            gain_total, value_total = gain_sum, value_sum
        else:
            gain_total, value_total = gain_total + gain_sum, value_total + value_sum

    @pl.when(step == 0)
    def _():
        d_gain[...] = gain_total
        total[...] = value_total

    @pl.when(step > 0)
    def _():
        d_gain[...] += gain_total
        total[...] += value_total

    @pl.when(step == pl.num_programs(0) - 1)
    def _():
        low = total[...].astype(BF16)
        d_value[0] = low[:, :SIDE]
        d_value[1] = low[:, SIDE:]


def run_close(sc, tokens, res_own, res_got, own, far, gain, w_own, w_far):
    runs = 2
    slab = (2, RUNS, 2, HALF, WIDTH)
    half = (2, RUNS, HALF, WIDTH)
    whole_spec = spec((2, runs, 2, HALF, WIDTH), lambda j, s: (0, j, 0, 0, 0))
    half_spec = spec((2, runs, HALF, WIDTH), lambda j, s: (0, j, 0, 0))
    back_spec = spec((HEADS, runs * 128, 2 * HEAD), lambda j, s: (0, j, 0))
    return pl.pallas_call(
        close_kernel,
        grid_spec=pltpu.PrefetchScalarGridSpec(
            num_scalar_prefetch=1,
            grid=(RUNS // runs,),
            in_specs=[whole_spec]
            + [half_spec] * 2
            + [back_spec, back_spec, held((1, WIDTH)), held((WIDTH, SIDE)), held((WIDTH, SIDE))],
            out_specs=[whole_spec, held((2, WIDTH, SIDE)), held((1, WIDTH))],
            scratch_shapes=[pltpu.VMEM((WIDTH, WIDTH), F32), pltpu.VMEM((WIDTH, WIDTH), BF16)],
        ),
        out_shape=[
            jax.ShapeDtypeStruct(slab, F32),
            jax.ShapeDtypeStruct((2, WIDTH, SIDE), BF16),
            jax.ShapeDtypeStruct((1, WIDTH), F32),
        ],
        compiler_params=params(LESS),
        cost_estimate=pl.CostEstimate(
            flops=4 * 2 * LMAX * WIDTH * WIDTH, bytes_accessed=38 * LMAX * WIDTH, transcendentals=0
        ),
        name="close",
    )(
        sc,
        tokens.reshape(slab),
        *(x.reshape(half) for x in (res_own, res_got)),
        own,
        far,
        gain,
        w_own,
        w_far,
    )


def join_kernel(sc, own, got, output):
    output[:, :, sc[CORE]] = own[...].astype(F32)
    output[:, :, 1 - sc[CORE]] = got[...].astype(F32)


def run_join(sc, own, got):
    half = (2, RUNS, HALF, WIDTH)
    half_spec = spec((2, 2, HALF, WIDTH), lambda j, s: (0, j, 0, 0))
    return pl.pallas_call(
        join_kernel,
        grid_spec=pltpu.PrefetchScalarGridSpec(
            num_scalar_prefetch=1,
            grid=(RUNS // 2,),
            in_specs=[half_spec, half_spec],
            out_specs=spec((2, 2, 2, HALF, WIDTH), lambda j, s: (0, j, 0, 0, 0)),
        ),
        out_shape=jax.ShapeDtypeStruct((2, RUNS, 2, HALF, WIDTH), F32),
        compiler_params=params(LESS),
        cost_estimate=pl.CostEstimate(flops=0, bytes_accessed=12 * LMAX * WIDTH, transcendentals=0),
        name="join",
    )(sc, own.reshape(half), got.reshape(half))


PACK_DOWN, PACK_UP, PACK_OUT, PACK_VALUE, PACK_GAIN, PACK = 0, 192, 384, 432, 480, 496


def pack_kernel(sc, down, up, out, value, gain, down_far, up_far, out_far, value_far, gain_far, packed):
    first = sc[CORE] == 0

    def both(own, far, lanes):
        own, far = own[:, lanes], far[:, lanes]
        return jnp.concatenate([jnp.where(first, own, far), jnp.where(first, far, own)], axis=0)

    def side(own, far):
        return both(own, far, own_lanes(sc))

    packed[PACK_DOWN:PACK_UP] = side(down, down_far)
    for j in range(4):
        lanes = pl.ds(pl.multiple_of((4 * sc[CORE] + j) * SIDE, 128), SIDE)
        packed[PACK_UP + 48 * j : PACK_UP + 48 * (j + 1)] = both(up, up_far, lanes)
    packed[PACK_OUT:PACK_VALUE] = side(out, out_far)
    packed[PACK_VALUE:PACK_GAIN] = side(value, value_far)
    packed[PACK_GAIN:] = both(gain, gain_far, slice(0, SIDE))


def run_pack(sc, own, far):
    return pl.pallas_call(
        pack_kernel,
        grid_spec=pltpu.PrefetchScalarGridSpec(
            num_scalar_prefetch=1,
            grid=(1,),
            in_specs=[held(x.shape) for x in (*own, *far)],
            out_specs=held((PACK, SIDE)),
        ),
        out_shape=jax.ShapeDtypeStruct((PACK, SIDE), BF16),
        compiler_params=params(VMEM),
        cost_estimate=pl.CostEstimate(flops=0, bytes_accessed=6 * PACK * SIDE, transcendentals=0),
        name="pack",
    )(sc, *own, *far)


def chip_of(sc, k, rel):
    return plane_of(k, sc) * 4 + (sc[PLACE] ^ rel)


def place_kernel(moves, sc, *refs):
    pieces, targets, sems = refs[:16], refs[16:-1], refs[-1]
    copies = []
    for index, piece in enumerate(pieces):
        chip = chip_of(sc, index // 4, index % 4)
        for which, (start, count, lane, target, step, offset, column) in enumerate(moves):
            rows = pl.ds(pl.multiple_of(chip * step + offset, 16), count)
            copies.append(
                pltpu.make_async_copy(
                    piece.at[pl.ds(start, count), pl.ds(lane, SIDE)],
                    targets[target].at[rows, pl.ds(column, SIDE)],
                    sems.at[index, which],
                )
            )
    for copy in copies:
        copy.start()
    for copy in copies:
        copy.wait()


def run_place(sc, pieces, moves, shapes):
    return pl.pallas_call(
        partial(place_kernel, moves),
        grid_spec=pltpu.PrefetchScalarGridSpec(
            num_scalar_prefetch=1,
            grid=(1,),
            in_specs=anywhere(16),
            out_specs=[held(shape) for shape in shapes],
            scratch_shapes=[pltpu.SemaphoreType.DMA((16, len(moves)))],
        ),
        out_shape=[jax.ShapeDtypeStruct(shape, BF16) for shape in shapes],
        compiler_params=params(VMEM),
        cost_estimate=pl.CostEstimate(
            flops=0, bytes_accessed=4 * sum(a * b for a, b in shapes), transcendentals=0
        ),
        name="place",
    )(sc, *pieces)


def place_weights(sc, pieces):
    moves = (
        (PACK_DOWN, 192, 0, 0, 192, 0, 0),
        *((PACK_UP + 48 * j, 48, 0, 1, 48, 0, j * SIDE) for j in range(4)),
        (PACK_OUT, 48, 0, 2, 48, 0, 0),
        (PACK_VALUE, 48, 0, 3, 48, 0, 0),
        (PACK_GAIN, 16, 0, 4, 16, 0, 0),
    )
    shapes = [(FF, SIDE), (WIDTH, FF // 2), (WIDTH, SIDE), (WIDTH, SIDE), (256, SIDE)]
    return run_place(sc, pieces, moves, shapes)


def collect_kernel(sc, *refs):
    outs = refs[24:]
    for k in range(PLANES):

        @pl.when(pl.program_id(0) == k)
        def _():
            for rel in range(4):
                down, down_got, up, up_got, out, out_got = refs[6 * rel : 6 * rel + 6]
                packed = outs[4 * k + rel]
                packed[PACK_DOWN:PACK_UP] = add_low(down[...], down_got[...])
                for j in range(4):
                    lanes = slice(j * SIDE, (j + 1) * SIDE)
                    packed[PACK_UP + 48 * j : PACK_UP + 48 * (j + 1)] = add_low(up[:, lanes], up_got[:, lanes])
                packed[PACK_OUT:PACK_VALUE] = add_low(out[...], out_got[...])


def run_collect(sc, *sides):
    def rows(x, rel):
        return spec((x.shape[0] // 16, x.shape[1]), lambda k, s: (chip_of(s, k, rel), 0))

    return pl.pallas_call(
        collect_kernel,
        grid_spec=pltpu.PrefetchScalarGridSpec(
            num_scalar_prefetch=1,
            grid=(PLANES,),
            in_specs=[rows(x, rel) for rel in range(4) for x in sides],
            out_specs=[held((PACK_VALUE, SIDE))] * 16,
        ),
        out_shape=[jax.ShapeDtypeStruct((PACK_VALUE, SIDE), BF16)] * 16,
        compiler_params=params(LESS),
        cost_estimate=pl.CostEstimate(flops=0, bytes_accessed=3 * 16 * PACK_VALUE * SIDE * 2, transcendentals=0),
        name="collect",
    )(sc, *(x for _ in range(4) for x in sides))


def add_kernel(groups, *refs):
    for group, total in zip(groups, refs[-len(groups) :]):
        value = refs[group[0]][...].astype(F32)
        for index in group[1:]:
            value = value + refs[index][...].astype(F32)
        total[...] = value.astype(total.dtype)


def run_add(groups, values, dtype):
    shape = values[0].shape
    here = pl.BlockSpec(memory_space=pltpu.VMEM)
    return pl.pallas_call(
        partial(add_kernel, groups),
        in_specs=[here] * len(values),
        out_specs=[here] * len(groups),
        out_shape=[jax.ShapeDtypeStruct(shape, dtype)] * len(groups),
        compiler_params=params(LESS),
        cost_estimate=pl.CostEstimate(
            flops=0, bytes_accessed=2 * shape[0] * shape[1] * (len(values) + len(groups)), transcendentals=0
        ),
        name="add",
    )(*values)


DEVICES = 32
TO_CORE, TO_X, TO_Y = 1, 2, 4


def swap(x, bit):
    return lax.ppermute(x, BOTH, [(d, d ^ bit) for d in range(DEVICES)])


def ring(x, way=1):
    return lax.ppermute(x, BOTH, [(d, (d + 8 * way) % DEVICES) for d in range(DEVICES)])


def pick(x, index, axis=0):
    return lax.dynamic_index_in_dim(x, index, axis, keepdims=False)


def ordered(flag, one, two, axis=0, joined=jnp.stack):
    return jnp.where(flag == 0, joined([one, two], axis), joined([two, one], axis))


def add_low(one, two):
    return (one.astype(F32) + two.astype(F32)).astype(BF16)


STEPS = (
    ((0, 0, 1), (0, 1, 0), (1, 0, 0)),
    ((1, 0, 1), (0, 1, 1), (2, 0, 0)),
    ((2, 0, 1), (1, 1, 0), (3, 0, 0)),
    ((1, 1, 1), (2, 1, 1), (2, 1, 0)),
    ((3, 0, 1), (3, 1, 0), (3, 1, 1)),
)


def gather_step(have, step):
    by_x, by_y, by_z = STEPS[step]
    return {
        **have,
        by_z: ring(have[by_z[0] - 1, by_z[1], by_z[2]]),
        by_x: swap(have[by_x[0], by_x[1], 0], TO_X),
        by_y: swap(have[by_y[0], 0, by_y[2]], TO_Y),
    }


def in_order(have):
    return [have[k, y, x] for k in range(4) for y in range(2) for x in range(2)]


def by_place(shares, planes=range(PLANES)):
    return {(k, i // 2, i % 2): shares[4 * at + i] for at, k in enumerate(planes) for i in range(4)}


def scatter_send(have, step):
    by_x, by_y, by_z = STEPS[len(STEPS) - 1 - step]
    got = (ring(have[by_z], -1), swap(have[by_x], TO_X), swap(have[by_y], TO_Y))
    return {at: value for at, value in have.items() if at not in (by_x, by_y, by_z)}, got


def scatter_add(have, got, step):
    by_x, by_y, by_z = STEPS[len(STEPS) - 1 - step]
    targets = ((by_z[0] - 1, by_z[1], by_z[2]), (by_x[0], by_x[1], 0), (by_y[0], 0, by_y[2]))
    sums = list(dict.fromkeys(targets))
    groups = [(len(got) + i, *(j for j in range(len(got)) if targets[j] == at)) for i, at in enumerate(sums)]
    values = [*got, *(have[at] for at in sums)]
    dtype = F32 if step == len(STEPS) - 1 else BF16
    if values[0].shape[1] == LMAX:
        totals = run_add(groups, values, dtype)
    else:
        totals = [sum(values[i].astype(F32) for i in group).astype(dtype) for group in groups]
    return {**have, **dict(zip(sums, totals))}


together = lax.optimization_barrier


def chip_shards(tokens, lengths, rand_mix, w_value, w_out, w_up, w_down, gain_mix, gain_ffn, grad_out):
    wide = lax.axis_index("wide")
    core = lax.axis_index("narrow")
    z, y, x = wide // 4, (wide // 2) % 2, wide % 2
    other = lambda value: swap(value, TO_CORE)
    side = partial(ordered, core, joined=jnp.concatenate)
    slab = (2, RUNS, 2, HALF, WIDTH)
    tokens, grad_out = tokens.reshape(slab), grad_out.reshape(slab)

    gains = jnp.pad(jnp.concatenate([gain_mix, gain_ffn])[None], ((0, 7), (0, SIDE - 48)))
    own = (w_down, w_up, w_out, w_value, gains)
    far = tuple(other(value) for value in own)
    near_sc = jnp.concatenate([jnp.stack([core, z, wide % 4]).astype(jnp.int32), lengths, lengths])
    weights = {(0, 0, 0): run_pack(near_sc, own, far)}

    rand = rand_mix.reshape(3, 2, HALF, LMAX)
    blocks = side(pick(rand, core, 1), other(pick(rand, 1 - core, 1)), 0)
    weights, rands, late_tokens, late_grad = together(
        (gather_step(weights, 0), {(0, 0, 0): blocks.reshape(SUBS * HALF, LMAX)}, tokens, grad_out)
    )
    weights, tokens_far = together((gather_step(weights, 1), other(pick(late_tokens, 1 - core, 2))))
    weights, grad_far = together((gather_step(weights, 2), other(pick(late_grad, 1 - core, 2))))
    weights, far_lengths = together((gather_step(weights, 3), other(lengths)))
    sc = jnp.concatenate([near_sc[:5], far_lengths])
    weights, rands = together((gather_step(weights, 4), rands))

    rands = gather_step(rands, 0)
    down, up, out, value, gain_rows = place_weights(sc, in_order(weights))
    rands, value, value_far, gain_rows, out, down, up = together(
        (rands, value, other(value), gain_rows, out, down, up)
    )
    gain_rows = gain_rows.reshape(16, 2, 8, SIDE)[:, :, 0]
    gain_one = gain_rows[..., :24].reshape(1, WIDTH).astype(F32)
    gain_two = gain_rows[..., 24:48].reshape(1, WIDTH).astype(F32)
    rands = gather_step(rands, 1)
    v_own = run_values(sc, tokens.reshape(2, LMAX, WIDTH), gain_one, value, value_far)
    rands, v_own, out, down, up = together((rands, v_own, (out, other(out)), down, up))
    rands, v_own, v_far, grad_far, down, up = together(
        (gather_step(rands, 2), v_own, other(v_own), grad_far, down, up)
    )
    rands = gather_step(rands, 3)
    masked = run_masked(sc, grad_out, grad_far)
    rands, v_far, masked, down, up = together((rands, v_far, masked, down, up))
    near = [rands[k, y_at, x_at] for k in range(3) for y_at in range(2) for x_at in range(2)]
    rands = gather_step(rands, 4)
    mixing = run_mix(sc, (0, 1, 2), near, v_own, v_far, ())
    rands, down, up, mixing = together((rands, down, up, mixing))
    heads, mean, exps, inverse = run_mix(sc, (3,), in_order(rands)[12:], v_own, v_far, mixing)
    down, up = (down, other(down)), (up, other(up))

    mixed, resid, normed = run_pre(sc, tokens, tokens_far, heads, out, gain_two)
    active, up_grad = run_units(sc, normed, masked, up, down)
    res_own, res_far, grad_heads, d_gain_two = run_post(sc, resid, up_grad, masked, up, out, gain_two)

    backward = lambda planes, carry: run_unmix(sc, planes, v_own, v_far, grad_heads, mean, exps, inverse, carry)
    *far, back_own, back_far = backward((3,), ())
    far, back_own, back_far, res_got = together((far, back_own, back_far, other(res_far)))
    have, got = scatter_send(by_place(far, (3,)), 0)
    *near, back_own, back_far = backward((2, 1, 0), (back_own, back_far))
    have, got, near, back_own, back_far = together((have, got, near, back_own, back_far))
    have = scatter_add({**have, **by_place(near, (2, 1, 0))}, got, 0)

    have, got = scatter_send(have, 1)
    up_own, up_far = run_up_grad(sc, normed, up_grad)
    have, got, up_own, up_far, back_got = together((have, got, up_own, up_far, other(back_far)))
    have = scatter_add(have, got, 1)

    have, got = scatter_send(have, 2)
    down_own, down_far = run_down_grad(sc, active, masked)
    have, got, down_own, down_far, up_got = together((have, got, down_own, down_far, other(up_far)))
    have = scatter_add(have, got, 2)

    have, got = scatter_send(have, 3)
    d_out_own, d_out_far = run_out_grad(sc, mixed, res_own, res_far)
    packed = run_collect(sc, down_own, other(down_far), up_own, up_got, d_out_own, other(d_out_far))
    have, got, packed = together((have, got, packed))
    have = scatter_add(have, got, 3)

    have, got = scatter_send(have, 4)
    sums, sums_got = scatter_send(by_place(packed), 0)
    out_own, out_far = run_out(sc, active, resid, down)
    have, got, sums, sums_got, out_own, out_far = together((have, got, sums, sums_got, out_own, out_far))
    rand_sum = scatter_add(have, got, 4)[0, 0, 0].reshape(2, 3, HALF, LMAX)

    sums, got = scatter_send(scatter_add(sums, sums_got, 0), 1)
    tokens_grad, d_value, d_gain_one = run_close(
        sc, tokens, res_own, res_got, back_own, back_got, gain_one, value, value_far
    )
    sums, got, tokens_grad, d_value, d_gain_one, out_got = together(
        (sums, got, tokens_grad, d_value, d_gain_one, other(out_far))
    )
    sums = scatter_add(sums, got, 1)

    sums, got = scatter_send(sums, 2)
    gain_pair = jnp.concatenate([d_gain_one, d_gain_two]).reshape(2, 16, 1, 48).astype(BF16)
    gain_pair = jnp.pad(gain_pair, ((0, 0), (0, 0), (0, 15), (0, SIDE - 48)))
    small = jnp.concatenate([d_value.reshape(2, 16, 48, SIDE), gain_pair], 2)
    small = add_low(pick(small, core), other(pick(small, 1 - core))).reshape(4, 2, 2, 64, SIDE)
    small = add_low(pick(small, x, 2), swap(pick(small, 1 - x, 2), TO_X))
    output = run_join(sc, out_own, out_got)
    sums, got, small, output = together((sums, got, small, output))
    sums = scatter_add(sums, got, 2)

    sums, got = scatter_send(sums, 3)
    small = add_low(pick(small, y, 1), swap(pick(small, 1 - y, 1), TO_Y))
    blocks, blocks_far = pick(rand_sum, core), other(pick(rand_sum, 1 - core))
    sums, got, small, blocks, blocks_far = together((sums, got, small, blocks, blocks_far))
    sums = scatter_add(sums, got, 3)

    sums, got = scatter_send(sums, 4)
    small_sum = pick(small, z).astype(F32)
    for k in range(1, PLANES):
        small_sum = small_sum + ring(pick(small, lax.rem(z + PLANES - k, PLANES)), -k).astype(F32)
    sums, got, small_sum = together((sums, got, small_sum))
    big_sum = scatter_add(sums, got, 4)[0, 0, 0]
    big_far, small_far = other(big_sum), other(small_sum)

    rows_of = lambda value, rows: pick(value.reshape(-1, 2, rows, SIDE), core, 1)
    mine = lambda own, far, rows: side(rows_of(own, rows)[0], rows_of(far, rows)[0], 1)
    down_shard = mine(big_sum[PACK_DOWN:PACK_UP], big_far[PACK_DOWN:PACK_UP], 96)
    up_side = lambda value: rows_of(value[PACK_UP:PACK_OUT], 24).transpose(1, 0, 2).reshape(24, 4 * SIDE)
    up_shard = side(up_side(big_sum), up_side(big_far), 1)
    outproj_shard = mine(big_sum[PACK_OUT:PACK_VALUE], big_far[PACK_OUT:PACK_VALUE], 24)
    value_shard = mine(small_sum[:48], small_far[:48], 24)
    gains_pair = ordered(core, small_sum[48, :48], small_far[48, :48])
    gain_pair = pick(gains_pair.reshape(2, 2, 24), core, 1)

    rand_shard = ordered(core, blocks, blocks_far, 1)

    return (
        output.reshape(2, LMAX, WIDTH),
        tokens_grad.reshape(2, LMAX, WIDTH),
        rand_shard.reshape(3 * 128, LMAX),
        value_shard,
        outproj_shard,
        up_shard,
        down_shard,
        gain_pair[0],
        gain_pair[1],
    )


def rms_norm(values, gain):
    scale = lax.rsqrt(jnp.mean(values * values, axis=-1, keepdims=True) + EPSILON)
    return values * scale * gain


def split_heads(block):
    return block.reshape(LMAX, HEADS, HEAD).transpose(1, 0, 2)


def merge_heads(block):
    return block.transpose(1, 0, 2).reshape(LMAX, HEADS * HEAD)


def masked_scores(key_mask, rand_head):
    return jnp.where(key_mask[None, :] > 0, rand_head.astype(jnp.float32), -1e30)


def head_forward(key_mask, paired):
    rand_head, value_head = paired
    scores = masked_scores(key_mask, rand_head)
    row_peak = jnp.max(scores, axis=-1, keepdims=True)
    exponent = jnp.exp(scores - row_peak)
    denom_sum = jnp.sum(exponent, axis=-1, keepdims=True)
    attention = exponent / denom_sum * key_mask[:, None]
    mixed = jnp.dot(attention.astype(jnp.bfloat16), value_head, preferred_element_type=jnp.float32)
    return (mixed.astype(jnp.bfloat16), row_peak + jnp.log(denom_sum))


def head_backward(key_mask, paired):
    rand_head, value_head, mix_grad, log_total = paired
    scores = masked_scores(key_mask, rand_head)
    attention = jnp.exp(scores - log_total) * key_mask[:, None]
    prob_grad = jnp.einsum("id,jd->ij", mix_grad, value_head, preferred_element_type=jnp.float32)
    value_grad = jnp.einsum(
        "ij,id->jd", attention.astype(jnp.bfloat16), mix_grad, preferred_element_type=jnp.float32
    )
    score_grad = attention * (prob_grad - jnp.sum(prob_grad * attention, axis=-1, keepdims=True))
    return (score_grad, value_grad)


def shards(tokens, lengths, rand_mix, w_value, w_out, w_up, w_down, gain_mix, gain_ffn, grad_out):
    item_count = tokens.shape[0]
    width = tokens.shape[2]
    row_count = item_count * LMAX
    tokens_flat = tokens.reshape(row_count, width).astype(jnp.float32)
    positions = jnp.arange(LMAX, dtype=jnp.int32)
    valid_table = (positions[None, :] < lengths[:, None]).astype(jnp.float32)
    row_valid = valid_table.reshape(row_count, 1)
    forward_set = (
        lax.all_gather(rand_mix, ("wide", "narrow"), axis=0, tiled=True),
        lax.all_gather(w_value, ("wide", "narrow"), axis=0, tiled=True),
        lax.all_gather(w_out, ("wide", "narrow"), axis=0, tiled=True),
        lax.all_gather(w_up, ("wide", "narrow"), axis=0, tiled=True),
        lax.all_gather(w_down, ("wide", "narrow"), axis=0, tiled=True),
        lax.all_gather(gain_mix, ("wide", "narrow"), axis=0, tiled=True),
        lax.all_gather(gain_ffn, ("wide", "narrow"), axis=0, tiled=True),
    )
    rand_all, value_all, out_all, up_all, down_all, gain_first, gain_second = forward_set
    normed = rms_norm(tokens_flat, gain_first.astype(jnp.float32)).astype(jnp.bfloat16)
    values = jnp.dot(normed, value_all, preferred_element_type=jnp.float32).astype(jnp.bfloat16)
    rand_heads = rand_all.reshape(HEADS, LMAX, LMAX)
    mixed_parts = []
    totals_kept = []
    for item_index in range(item_count):
        item_values = split_heads(values[item_index * LMAX : (item_index + 1) * LMAX])
        mixed_heads, log_total = lax.map(
            partial(head_forward, valid_table[item_index]), (rand_heads, item_values)
        )
        mixed_parts.append(merge_heads(mixed_heads))
        totals_kept.append(log_total)
    mixed = jnp.concatenate(mixed_parts, axis=0)
    residual = tokens_flat + jnp.dot(mixed, out_all, preferred_element_type=jnp.float32)
    normed_two = rms_norm(residual, gain_second.astype(jnp.float32)).astype(jnp.bfloat16)
    up_proj = jnp.dot(normed_two, up_all, preferred_element_type=jnp.float32)
    active = jax.nn.gelu(up_proj).astype(jnp.bfloat16)
    branch = jnp.dot(active, down_all, preferred_element_type=jnp.float32)
    output = row_valid * (residual + branch)
    back_set = (
        lax.all_gather(rand_mix, ("wide", "narrow"), axis=0, tiled=True),
        lax.all_gather(w_value, ("wide", "narrow"), axis=0, tiled=True),
        lax.all_gather(w_out, ("wide", "narrow"), axis=0, tiled=True),
        lax.all_gather(w_up, ("wide", "narrow"), axis=0, tiled=True),
        lax.all_gather(w_down, ("wide", "narrow"), axis=0, tiled=True),
        lax.all_gather(gain_mix, ("wide", "narrow"), axis=0, tiled=True),
        lax.all_gather(gain_ffn, ("wide", "narrow"), axis=0, tiled=True),
    )
    rand_back, value_back, out_back, up_back, down_back, gain_back_one, gain_back_two = back_set
    cotangent = grad_out.reshape(row_count, width).astype(jnp.float32)
    masked = row_valid * cotangent
    branch_grad = masked.astype(jnp.bfloat16)
    grad_down = jnp.einsum("rk,rd->kd", active, branch_grad, preferred_element_type=jnp.float32)
    active_grad = jnp.einsum(
        "rd,kd->rk", branch_grad, down_back, preferred_element_type=jnp.float32
    )
    gelu_value, gelu_pull = jax.vjp(jax.nn.gelu, up_proj)
    up_grad = gelu_pull(active_grad)[0].astype(jnp.bfloat16)
    grad_up = jnp.einsum("rd,rk->dk", normed_two, up_grad, preferred_element_type=jnp.float32)
    normed_two_grad = jnp.einsum("rk,dk->rd", up_grad, up_back, preferred_element_type=jnp.float32)
    norm_value, norm_pull = jax.vjp(rms_norm, residual, gain_back_two.astype(jnp.float32))
    residual_part, gain_two_grad = norm_pull(normed_two_grad)
    residual_grad = masked + residual_part
    attn_grad = residual_grad.astype(jnp.bfloat16)
    grad_outproj = jnp.einsum("rd,re->de", mixed, attn_grad, preferred_element_type=jnp.float32)
    mixed_grad = jnp.einsum(
        "re,de->rd", attn_grad, out_back, preferred_element_type=jnp.float32
    ).astype(jnp.bfloat16)
    rand_heads_back = rand_back.reshape(HEADS, LMAX, LMAX)
    rand_grad = jnp.zeros((HEADS, LMAX, LMAX), jnp.float32)
    value_parts = []
    for item_index in range(item_count):
        lower_row = item_index * LMAX
        upper_row = lower_row + LMAX
        item_values = split_heads(values[lower_row:upper_row])
        item_mix_grad = split_heads(mixed_grad[lower_row:upper_row])
        score_grad, value_grad = lax.map(
            partial(head_backward, valid_table[item_index]),
            (rand_heads_back, item_values, item_mix_grad, totals_kept[item_index]),
        )
        rand_grad = rand_grad + score_grad
        value_parts.append(merge_heads(value_grad))
    values_grad = jnp.concatenate(value_parts, axis=0).astype(jnp.bfloat16)
    grad_value = jnp.einsum("rd,re->de", normed, values_grad, preferred_element_type=jnp.float32)
    normed_grad = jnp.einsum(
        "re,de->rd", values_grad, value_back, preferred_element_type=jnp.float32
    )
    norm_first, first_pull = jax.vjp(rms_norm, tokens_flat, gain_back_one.astype(jnp.float32))
    token_part, gain_one_grad = first_pull(normed_grad)
    tokens_grad = residual_grad + token_part
    rand_flat = rand_grad.reshape(HEADS * LMAX, LMAX)
    all_shards = (
        lax.psum_scatter(rand_flat, ("wide", "narrow"), scatter_dimension=0, tiled=True),
        lax.psum_scatter(grad_value, ("wide", "narrow"), scatter_dimension=0, tiled=True),
        lax.psum_scatter(grad_outproj, ("wide", "narrow"), scatter_dimension=0, tiled=True),
        lax.psum_scatter(grad_up, ("wide", "narrow"), scatter_dimension=0, tiled=True),
        lax.psum_scatter(grad_down, ("wide", "narrow"), scatter_dimension=0, tiled=True),
        lax.psum_scatter(gain_one_grad, ("wide", "narrow"), scatter_dimension=0, tiled=True),
        lax.psum_scatter(gain_two_grad, ("wide", "narrow"), scatter_dimension=0, tiled=True),
    )
    rand_shard, value_shard, outproj_shard, up_shard, down_shard, gain_one_shard, gain_two_shard = (
        all_shards
    )
    return (
        output.reshape(item_count, LMAX, width),
        tokens_grad.reshape(item_count, LMAX, width),
        rand_shard,
        value_shard,
        outproj_shard,
        up_shard,
        down_shard,
        gain_one_shard,
        gain_two_shard,
    )


def solution(mesh):
    in_specs = (
        P(("wide", "narrow"), None, None),
        P(("wide", "narrow")),
        P(("wide", "narrow"), None),
        P(("wide", "narrow"), None),
        P(("wide", "narrow"), None),
        P(("wide", "narrow"), None),
        P(("wide", "narrow"), None),
        P(("wide", "narrow")),
        P(("wide", "narrow")),
        P(("wide", "narrow"), None, None),
    )
    out_specs = (
        P(("wide", "narrow"), None, None),
        P(("wide", "narrow"), None, None),
        P(("wide", "narrow"), None),
        P(("wide", "narrow"), None),
        P(("wide", "narrow"), None),
        P(("wide", "narrow"), None),
        P(("wide", "narrow"), None),
        P(("wide", "narrow")),
        P(("wide", "narrow")),
    )
    fits = dict(mesh.shape) == {"wide": 16, "narrow": 2}
    return jax.shard_map(chip_shards if fits else shards, mesh=mesh, in_specs=in_specs, out_specs=out_specs, check_vma=False)
```

```python
from functools import partial

import jax
import jax.numpy as jnp
from jax import lax
from jax.experimental import pallas as pl
from jax.experimental.pallas import tpu as pltpu
from jax.sharding import PartitionSpec as P

HEADS = 12
HEAD = 64
LMAX = 1024
WIDTH = 768
FF = 3072
EPSILON = 1e-05

BOTH = ("wide", "narrow")
BF16 = jnp.bfloat16
F32 = jnp.float32
VMEM = 61 << 20
LESS = 34 << 20

SUBS = 6
RUNS = 8
HALF = 64
HROWS = RUNS * HALF
PLANES = 4
PHEADS = HEADS // PLANES
ROWS = 2 * LMAX
FSTEP = 768
FSIDE = FF // 2 // FSTEP
TILE = 512
SIDE = WIDTH // 2
SPAN = 2 * HALF


def dot(a, b, ca, cb):
    return lax.dot_general(a, b, (((ca,), (cb,)), ((), ())), preferred_element_type=F32)


CORE, PLANE, PLACE, LENGTHS = 0, 1, 2, 3


def spec(shape, index):
    return pl.BlockSpec(shape, index)


def held(shape):
    zeros = (0,) * len(shape)
    return pl.BlockSpec(shape, lambda *_: zeros, pipeline_mode=pl.Buffered(1))


def params(limit):
    return pltpu.CompilerParams(vmem_limit_bytes=limit)


def whole_weight(sc, step, own, far, weight):
    @pl.when(step == 0)
    def _():
        weight[:, pl.ds(pl.multiple_of(sc[CORE] * SIDE, 128), SIDE)] = own[...]
        weight[:, pl.ds(pl.multiple_of((1 - sc[CORE]) * SIDE, 128), SIDE)] = far[...]


def values_kernel(sc, tok, gain, w_own, w_far, out, weight):
    step = pl.program_id(0)
    whole_weight(sc, step, w_own, w_far, weight)
    rows = tok.shape[1]
    position = step * rows + lax.broadcasted_iota(jnp.int32, (rows, 1), 0)
    for item in range(2):
        x = tok[item].astype(F32)
        scale = lax.rsqrt(jnp.mean(x * x, axis=-1, keepdims=True) + EPSILON)
        normed = (x * scale * gain[...]).astype(BF16)
        found = dot(normed, weight[...], 1, 0)
        found = jnp.where(position < sc[LENGTHS + item], found, 0.0).astype(BF16)
        for head in range(HEADS):
            out[head, :, item * HEAD : (item + 1) * HEAD] = found[:, head * HEAD : (head + 1) * HEAD]


def run_values(sc, tokens, gain, w_own, w_far):
    rows = 256
    return pl.pallas_call(
        values_kernel,
        grid_spec=pltpu.PrefetchScalarGridSpec(
            num_scalar_prefetch=1,
            grid=(LMAX // rows,),
            in_specs=[
                spec((2, rows, WIDTH), lambda j, s: (0, j, 0)),
                held((1, WIDTH)),
                held((WIDTH, SIDE)),
                held((WIDTH, SIDE)),
            ],
            out_specs=spec((HEADS, rows, 2 * HEAD), lambda j, s: (0, j, 0)),
            scratch_shapes=[pltpu.VMEM((WIDTH, WIDTH), BF16)],
        ),
        out_shape=jax.ShapeDtypeStruct((HEADS, LMAX, 2 * HEAD), BF16),
        compiler_params=params(VMEM),
        cost_estimate=pl.CostEstimate(
            flops=2 * 2 * LMAX * WIDTH * WIDTH, bytes_accessed=8 * LMAX * WIDTH, transcendentals=0
        ),
        name="values",
    )(sc, tokens, gain, w_own, w_far)


def lane_lengths(sc, shape):
    slot = lax.broadcasted_iota(jnp.int32, shape, 1) // HEAD
    length = jnp.where(slot == 0, sc[LENGTHS], sc[LENGTHS + 1])
    return jnp.where(slot >= 2, jnp.where(slot == 2, sc[LENGTHS + 2], sc[LENGTHS + 3]), length)


def plane_of(k, sc):
    return lax.rem(sc[PLANE] + PLANES - k, PLANES)


def plane_spec(planes, rows, lanes):
    def index(step, sc):
        return (plane_of(planes[0] + step * (planes[-1] - planes[0]) // max(len(planes) - 1, 1), sc), 0, 0)

    return spec((PHEADS, rows, lanes), index)


def anywhere(count):
    return [pl.BlockSpec(memory_space=pl.ANY)] * count


def plane_fetch(place, shards, raw, sems, slot):
    return [
        pltpu.make_async_copy(
            shards[4 * slot + rel],
            raw.at[slot, pl.ds(pl.multiple_of((place ^ rel) * SUBS * HALF, SUBS * HALF), SUBS * HALF)],
            sems.at[slot, rel],
        )
        for rel in range(4)
    ]


def take_plane(place, shards, raw, sems):
    step = pl.program_id(0)
    count = len(shards) // 4

    @pl.when(step == 0)
    def _():
        for slot in range(count):
            for copy in plane_fetch(place, shards, raw, sems, slot):
                copy.start()

    for slot in range(count):

        @pl.when(step == slot)
        def _():
            for copy in plane_fetch(place, shards, raw, sems, slot):
                copy.wait()

    return step


def head_rows(head):
    return slice(head * HROWS, (head + 1) * HROWS)


def fill_mask(sc, mask):
    @pl.when(pl.program_id(0) == 0)
    def _():
        shape = (LMAX, 4 * HEAD)
        column = lax.broadcasted_iota(jnp.int32, shape, 0)
        mask[...] = (column < lane_lengths(sc, shape)).astype(F32).astype(BF16)


def mix_kernel(count, carried, sc, *refs):
    shards, (v_own, v_far, *rest) = refs[: 4 * count], refs[4 * count :]
    mixed, mean, exps, inverse, raw, mask, sems = rest[4:] if carried else rest
    fill_mask(sc, mask)
    slot = take_plane(sc[PLACE], shards, raw, sems)
    shape = (HROWS, 4 * HEAD)
    line = lax.broadcasted_iota(jnp.int32, shape, 0)
    position = 128 * (line // HALF) + HALF * sc[CORE] + line % HALF
    valid = position < lane_lengths(sc, shape)
    for head in range(PHEADS):
        weights = jnp.exp(raw[slot, head_rows(head)].astype(F32)).astype(BF16)
        exps[head] = weights
        both = dot(weights, jnp.concatenate([v_own[head], v_far[head], mask[...]], axis=1), 1, 0)
        flip = jnp.where(valid, 1.0 / both[:, 4 * HEAD :], 0.0)
        found = both[:, : 4 * HEAD] * flip
        inverse[head] = flip.astype(BF16)
        mean[head] = found
        mixed[head] = found.astype(BF16)


def run_mix(sc, planes, shards, v_own, v_far, carry):
    carry, count = list(carry), len(planes)
    shape = (HEADS, HROWS, 4 * HEAD)
    return pl.pallas_call(
        partial(mix_kernel, count, bool(carry)),
        grid_spec=pltpu.PrefetchScalarGridSpec(
            num_scalar_prefetch=1,
            grid=(count,),
            in_specs=anywhere(4 * count) + [plane_spec(planes, LMAX, 2 * HEAD)] * 2 + anywhere(len(carry)),
            out_specs=[
                plane_spec(planes, HROWS, 4 * HEAD),
                plane_spec(planes, HROWS, 4 * HEAD),
                plane_spec(planes, HROWS, LMAX),
                plane_spec(planes, HROWS, 4 * HEAD),
            ],
            scratch_shapes=[
                pltpu.VMEM((count, 4 * SUBS * HALF, LMAX), BF16),
                pltpu.VMEM((LMAX, 4 * HEAD), BF16),
                pltpu.SemaphoreType.DMA((count, 4)),
            ],
        ),
        out_shape=[
            jax.ShapeDtypeStruct(shape, BF16),
            jax.ShapeDtypeStruct(shape, F32),
            jax.ShapeDtypeStruct((HEADS, HROWS, LMAX), BF16),
            jax.ShapeDtypeStruct(shape, BF16),
        ],
        input_output_aliases={3 + 4 * count + i: i for i in range(len(carry))},
        compiler_params=params(VMEM),
        cost_estimate=pl.CostEstimate(
            flops=2 * HEADS * HROWS * LMAX * 4 * HEAD,
            bytes_accessed=HEADS * (2 * HROWS * LMAX + 5 * HROWS * 256),
            transcendentals=HEADS * HROWS * LMAX // 2,
        ),
        name="mix",
    )(sc, *shards, v_own, v_far, *carry)


def row_valid(sc, step):
    line = lax.broadcasted_iota(jnp.int32, (4 * SPAN, 1), 0)
    item = line // SPAN
    row = step * SPAN + line % SPAN
    low = jnp.where(item == 0, sc[LENGTHS], sc[LENGTHS + 1])
    high = jnp.where(item == 2, sc[LENGTHS + 2], sc[LENGTHS + 3])
    return 128 * (row // HALF) + HALF * sc[CORE] + row % HALF < jnp.where(item >= 2, high, low)


def four_items(own, far):
    return jnp.concatenate([own[:, :, 0], far[...]], axis=0).reshape(4 * SPAN, WIDTH)


def pre_kernel(sc, tok, tok_far, heads, wo_own, wo_far, gain, mixed, resid, normed, weight):
    step = pl.program_id(0)
    whole_weight(sc, step, wo_own, wo_far, weight)
    for item in range(4):
        lanes = slice(item * HEAD, (item + 1) * HEAD)
        for pair in range(HEADS // 2):
            both = jnp.concatenate([heads[2 * pair, :, lanes], heads[2 * pair + 1, :, lanes]], axis=1)
            mixed[item, :, pair * 128 : (pair + 1) * 128] = both
    res = four_items(tok, tok_far).astype(F32) + dot(mixed[...].reshape(4 * SPAN, WIDTH), weight[...], 1, 0)
    resid[...] = res.astype(BF16).reshape(4, SPAN, WIDTH)
    scale = lax.rsqrt(jnp.mean(res * res, axis=-1, keepdims=True) + EPSILON)
    valid = row_valid(sc, step)
    normed[...] = jnp.where(valid, res * scale * gain[...], 0.0).astype(BF16).reshape(4, SPAN, WIDTH)


def slab_spec(items=4):
    return spec((items, SPAN, WIDTH), lambda r, s: (0, r, 0))


def half_specs():
    return [
        spec((2, SPAN // HALF, 1, HALF, WIDTH), lambda r, s: (0, r, s[CORE], 0, 0)),
        spec((2, SPAN // HALF, HALF, WIDTH), lambda r, s: (0, r, 0, 0)),
    ]


def heads_spec():
    return spec((HEADS, SPAN, 4 * HEAD), lambda r, s: (0, r, 0))


def run_pre(sc, tokens, tokens_far, heads, wo, gain):
    return pl.pallas_call(
        pre_kernel,
        grid_spec=pltpu.PrefetchScalarGridSpec(
            num_scalar_prefetch=1,
            grid=(HROWS // SPAN,),
            in_specs=half_specs()
            + [heads_spec(), held((WIDTH, SIDE)), held((WIDTH, SIDE)), held((1, WIDTH))],
            out_specs=[slab_spec()] * 3,
            scratch_shapes=[pltpu.VMEM((WIDTH, WIDTH), BF16)],
        ),
        out_shape=[
            jax.ShapeDtypeStruct((4, HROWS, WIDTH), BF16),
            jax.ShapeDtypeStruct((4, HROWS, WIDTH), BF16),
            jax.ShapeDtypeStruct((4, HROWS, WIDTH), BF16),
        ],
        compiler_params=params(VMEM),
        cost_estimate=pl.CostEstimate(
            flops=2 * ROWS * WIDTH * WIDTH, bytes_accessed=16 * ROWS * WIDTH, transcendentals=0
        ),
        name="pre",
    )(sc, tokens, tokens_far, heads, *wo, gain)


def masked_kernel(sc, cot, cot_far, masked):
    value = jnp.where(row_valid(sc, pl.program_id(0)), four_items(cot, cot_far).astype(F32), 0.0)
    masked[...] = value.astype(BF16).reshape(4, SPAN, WIDTH)


def run_masked(sc, cotangent, cotangent_far):
    return pl.pallas_call(
        masked_kernel,
        grid_spec=pltpu.PrefetchScalarGridSpec(
            num_scalar_prefetch=1, grid=(HROWS // SPAN,), in_specs=half_specs(), out_specs=slab_spec()
        ),
        out_shape=jax.ShapeDtypeStruct((4, HROWS, WIDTH), BF16),
        compiler_params=params(VMEM),
        cost_estimate=pl.CostEstimate(flops=0, bytes_accessed=4 * ROWS * WIDTH, transcendentals=0),
        name="masked",
    )(sc, cotangent, cotangent_far)


def own_lanes(sc):
    return pl.ds(pl.multiple_of(sc[CORE] * SIDE, 128), SIDE)


def far_lanes(sc):
    return pl.ds(pl.multiple_of((1 - sc[CORE]) * SIDE, 128), SIDE)


def unit_rows(f, sc):
    return (lax.rem(FSIDE * sc[CORE] + f, 2 * FSIDE), 0)


def unit_columns(f, sc):
    return (0, lax.rem(FSIDE * sc[CORE] + f, 2 * FSIDE))


def early(f, sc):
    return (0, lax.min(f, FSIDE - 1))


def late(f, sc):
    return (0, lax.max(f - FSIDE, 0))


def units_kernel(sc, normed, cot, up_own, up_far, dn_own, dn_far, active, up_grad, w_up, w_down):
    step = pl.program_id(0)
    w_down[:, own_lanes(sc)] = dn_own[...]
    w_down[:, far_lanes(sc)] = dn_far[...]

    @pl.when(step < FSIDE)
    def _():
        w_up[...] = up_own[...]

    @pl.when(step >= FSIDE)
    def _():
        w_up[...] = up_far[...]

    for row in range(0, ROWS, 256):
        rows = slice(row, row + 256)
        for column in range(0, FSTEP, 256):
            columns = slice(column, column + 256)
            up = dot(normed[rows], w_up[:, columns], 1, 0)
            square = up * up
            bend = jnp.tanh(up * (0.7978845608028654 + (0.044715 * 0.7978845608028654) * square))
            share = 0.5 + 0.5 * bend
            act = up * share
            active[rows, columns] = act.astype(BF16)
            slope = share + act * (1.0 - share) * (
                2 * 0.7978845608028654 + (6 * 0.044715 * 0.7978845608028654) * square
            )
            up_grad[rows, columns] = (dot(cot[rows], w_down[columns], 1, 1) * slope).astype(BF16)


def run_units(sc, normed, cotangent, up, down):
    return pl.pallas_call(
        units_kernel,
        grid_spec=pltpu.PrefetchScalarGridSpec(
            num_scalar_prefetch=1,
            grid=(2 * FSIDE,),
            in_specs=[
                held((ROWS, WIDTH)),
                held((ROWS, WIDTH)),
                spec((WIDTH, FSTEP), early),
                spec((WIDTH, FSTEP), late),
                spec((FSTEP, SIDE), unit_rows),
                spec((FSTEP, SIDE), unit_rows),
            ],
            out_specs=[spec((ROWS, FSTEP), unit_columns), spec((ROWS, FSTEP), unit_columns)],
            scratch_shapes=[pltpu.VMEM((WIDTH, FSTEP), BF16), pltpu.VMEM((FSTEP, WIDTH), BF16)],
        ),
        out_shape=[jax.ShapeDtypeStruct((ROWS, FF), BF16), jax.ShapeDtypeStruct((ROWS, FF), BF16)],
        compiler_params=params(VMEM),
        cost_estimate=pl.CostEstimate(
            flops=4 * ROWS * WIDTH * FF, bytes_accessed=6 * ROWS * WIDTH + 4 * ROWS * FF, transcendentals=ROWS * FF
        ),
        name="units",
    )(sc, normed.reshape(ROWS, WIDTH), cotangent.reshape(ROWS, WIDTH), *up, *down)


def down_grad_kernel(sc, active, cot, own, far, total):
    total[...] = dot(active[...], cot[...], 0, 0).astype(BF16)
    own[...] = total[:, own_lanes(sc)]
    far[...] = total[:, far_lanes(sc)]


def run_down_grad(sc, active, cotangent):
    return pl.pallas_call(
        down_grad_kernel,
        grid_spec=pltpu.PrefetchScalarGridSpec(
            num_scalar_prefetch=1,
            grid=(FF // 512,),
            in_specs=[spec((ROWS, 512), lambda f, s: (0, f)), held((ROWS, WIDTH))],
            out_specs=[spec((512, SIDE), lambda f, s: (f, 0))] * 2,
            scratch_shapes=[pltpu.VMEM((512, WIDTH), BF16)],
        ),
        out_shape=[jax.ShapeDtypeStruct((FF, SIDE), BF16)] * 2,
        compiler_params=params(LESS),
        cost_estimate=pl.CostEstimate(
            flops=2 * ROWS * WIDTH * FF, bytes_accessed=2 * ROWS * (WIDTH + FF), transcendentals=0
        ),
        name="down_grad",
    )(sc, active, cotangent.reshape(ROWS, WIDTH))


def up_grad_kernel(sc, normed, up_grad, own, far):
    total = dot(normed[...], up_grad[...], 0, 0).astype(BF16)

    @pl.when(pl.program_id(0) < 3)
    def _():
        own[...] = total

    @pl.when(pl.program_id(0) >= 3)
    def _():
        far[...] = total


def run_up_grad(sc, normed, up_grad):
    return pl.pallas_call(
        up_grad_kernel,
        grid_spec=pltpu.PrefetchScalarGridSpec(
            num_scalar_prefetch=1,
            grid=(6,),
            in_specs=[held((ROWS, WIDTH)), spec((ROWS, 512), lambda f, s: (0, lax.rem(3 * s[CORE] + f, 6)))],
            out_specs=[
                spec((WIDTH, 512), lambda f, s: (0, lax.min(f, 2))),
                spec((WIDTH, 512), lambda f, s: (0, lax.max(f - 3, 0))),
            ],
        ),
        out_shape=[jax.ShapeDtypeStruct((WIDTH, FF // 2), BF16)] * 2,
        compiler_params=params(LESS),
        cost_estimate=pl.CostEstimate(
            flops=2 * ROWS * WIDTH * FF, bytes_accessed=2 * ROWS * (WIDTH + FF), transcendentals=0
        ),
        name="up_grad",
    )(sc, normed.reshape(ROWS, WIDTH), up_grad)


def out_grad_kernel(sc, mixed, res_own, res_far, own, far, total):
    step = pl.program_id(0)
    grad = jnp.concatenate([res_own[...], res_far[...]], axis=0).reshape(4 * SPAN, WIDTH)
    found = dot(mixed[...].reshape(4 * SPAN, WIDTH), grad, 0, 0)

    @pl.when(step == 0)
    def _():
        total[...] = found

    @pl.when(step > 0)
    def _():
        total[...] += found

    @pl.when(step == pl.num_programs(0) - 1)
    def _():
        own[...] = total[:, own_lanes(sc)].astype(BF16)
        far[...] = total[:, far_lanes(sc)].astype(BF16)


def run_out_grad(sc, mixed, res_own, res_far):
    return pl.pallas_call(
        out_grad_kernel,
        grid_spec=pltpu.PrefetchScalarGridSpec(
            num_scalar_prefetch=1,
            grid=(HROWS // SPAN,),
            in_specs=[slab_spec(), slab_spec(2), slab_spec(2)],
            out_specs=[held((WIDTH, SIDE))] * 2,
            scratch_shapes=[pltpu.VMEM((WIDTH, WIDTH), F32)],
        ),
        out_shape=[jax.ShapeDtypeStruct((WIDTH, SIDE), BF16)] * 2,
        compiler_params=params(LESS),
        cost_estimate=pl.CostEstimate(
            flops=2 * ROWS * WIDTH * WIDTH, bytes_accessed=4 * ROWS * WIDTH, transcendentals=0
        ),
        name="out_grad",
    )(sc, mixed, res_own, res_far)


def out_kernel(sc, active, resid, dn_own, dn_far, own, far, w_down):
    step = pl.program_id(0)

    @pl.when(step == 0)
    def _():
        w_down[:, own_lanes(sc)] = dn_own[...]
        w_down[:, far_lanes(sc)] = dn_far[...]

    branch = dot(active[...].reshape(4 * SPAN, FF), w_down[...], 1, 0)
    output = jnp.where(row_valid(sc, step), resid[...].reshape(4 * SPAN, WIDTH).astype(F32) + branch, 0.0)
    output = output.astype(BF16).reshape(4, SPAN, WIDTH)
    own[...] = output[:2]
    far[...] = output[2:]


def run_out(sc, active, resid, down):
    return pl.pallas_call(
        out_kernel,
        grid_spec=pltpu.PrefetchScalarGridSpec(
            num_scalar_prefetch=1,
            grid=(HROWS // SPAN,),
            in_specs=[
                spec((4, SPAN, FF), lambda r, s: (0, r, 0)),
                slab_spec(),
                held((FF, SIDE)),
                held((FF, SIDE)),
            ],
            out_specs=[slab_spec(2)] * 2,
            scratch_shapes=[pltpu.VMEM((FF, WIDTH), BF16)],
        ),
        out_shape=[
            jax.ShapeDtypeStruct((2, HROWS, WIDTH), BF16),
            jax.ShapeDtypeStruct((2, HROWS, WIDTH), BF16),
        ],
        compiler_params=params(LESS),
        cost_estimate=pl.CostEstimate(
            flops=2 * ROWS * WIDTH * FF, bytes_accessed=ROWS * (2 * FF + 7 * WIDTH), transcendentals=0
        ),
        name="out",
    )(sc, active.reshape(4, HROWS, FF), resid, *down)


def post_kernel(sc, resid, grad_own, grad_far, cot, up_own, up_far, wo_own, wo_far, gain, *refs):
    (res_own, res_far, heads, d_gain, weight, spread) = refs
    step = pl.program_id(0)
    whole_weight(sc, step, wo_own, wo_far, weight)
    shape, slab = (4 * SPAN, WIDTH), (4, SPAN, WIDTH)
    valid = row_valid(sc, step)
    res = resid[...].reshape(shape).astype(F32)
    scale = lax.rsqrt(jnp.mean(res * res, axis=-1, keepdims=True) + EPSILON)
    unit = res * scale
    units = (4 * SPAN, FF // 2)
    back = dot(grad_own[...].reshape(units), up_own[...], 1, 1) + dot(grad_far[...].reshape(units), up_far[...], 1, 1)
    two_grad = jnp.where(valid, back, 0.0)
    gained = two_grad * gain[...]
    masked = cot[...].reshape(shape).astype(F32)
    grad = masked + scale * (gained - unit * jnp.mean(gained * unit, axis=-1, keepdims=True))
    low = grad.astype(BF16)
    res_own[...] = low.reshape(slab)[:2]
    res_far[...] = low.reshape(slab)[2:]
    gain_sum = jnp.sum(two_grad * unit, axis=0, keepdims=True)

    @pl.when(step == 0)
    def _():
        d_gain[...] = gain_sum

    @pl.when(step > 0)
    def _():
        d_gain[...] += gain_sum

    spread[...] = dot(low, weight[...], 1, 1).astype(BF16).reshape(slab)
    for pair in range(HEADS // 2):
        lanes = slice(pair * 128, (pair + 1) * 128)
        for side in range(2):
            one, two = spread[2 * side, :, lanes], spread[2 * side + 1, :, lanes]
            half = slice(side * 128, (side + 1) * 128)
            heads[2 * pair, :, half] = jnp.concatenate([one[:, :HEAD], two[:, :HEAD]], axis=1)
            heads[2 * pair + 1, :, half] = jnp.concatenate([one[:, HEAD:], two[:, HEAD:]], axis=1)


def run_post(sc, resid, up_grad, cotangent, up, wo, gain):
    side = lambda which: spec((4, SPAN, FF // 2), lambda r, s: (0, r, s[CORE] if which == 0 else 1 - s[CORE]))
    up_grad = up_grad.reshape(4, HROWS, FF)
    return pl.pallas_call(
        post_kernel,
        grid_spec=pltpu.PrefetchScalarGridSpec(
            num_scalar_prefetch=1,
            grid=(HROWS // SPAN,),
            in_specs=[
                slab_spec(),
                side(0),
                side(1),
                slab_spec(),
                held((WIDTH, FF // 2)),
                held((WIDTH, FF // 2)),
                held((WIDTH, SIDE)),
                held((WIDTH, SIDE)),
                held((1, WIDTH)),
            ],
            out_specs=[slab_spec(2)] * 2 + [heads_spec(), held((1, WIDTH))],
            scratch_shapes=[
                pltpu.VMEM((WIDTH, WIDTH), BF16),
                pltpu.VMEM((4, SPAN, WIDTH), BF16),
            ],
        ),
        out_shape=[
            jax.ShapeDtypeStruct((2, HROWS, WIDTH), BF16),
            jax.ShapeDtypeStruct((2, HROWS, WIDTH), BF16),
            jax.ShapeDtypeStruct((HEADS, HROWS, 4 * HEAD), BF16),
            jax.ShapeDtypeStruct((1, WIDTH), F32),
        ],
        compiler_params=params(VMEM),
        cost_estimate=pl.CostEstimate(
            flops=2 * ROWS * WIDTH * (WIDTH + FF), bytes_accessed=ROWS * (16 * WIDTH + 2 * FF), transcendentals=0
        ),
        name="post",
    )(sc, resid, up_grad, up_grad, cotangent, *up, *wo, gain)


def unmix_kernel(count, carried, sc, v_own, v_far, grad_heads, mean, exps, inverse, *refs):
    refs = refs[2:] if carried else refs
    outs, (own, far, grads, mask, adder, bound, out_sems) = refs[: 4 * count], refs[4 * count :]
    place = sc[PLACE]
    step = pl.program_id(0)

    def leave(slot):
        return [
            pltpu.make_async_copy(
                grads.at[slot, pl.ds(pl.multiple_of((place ^ rel) * SUBS * HALF, SUBS * HALF), SUBS * HALF)],
                outs[4 * slot + rel],
                out_sems.at[slot, rel],
            )
            for rel in range(4)
        ]

    fill_mask(sc, mask)

    @pl.when(step == 0)
    def _():
        lane = lax.broadcasted_iota(jnp.int32, (4 * HEAD, 128), 0) // HEAD
        column = lax.broadcasted_iota(jnp.int32, (4 * HEAD, 128), 1)
        adder[...] = jnp.where((lane == column) | (lane + 4 == column), -1.0, 0.0).astype(BF16)
        row = lax.broadcasted_iota(jnp.int32, (LMAX, 128), 0)
        item = lax.broadcasted_iota(jnp.int32, (LMAX, 128), 1)
        length = jnp.where(item % 4 == 0, sc[LENGTHS], sc[LENGTHS + 1])
        length = jnp.where(item % 4 == 2, sc[LENGTHS + 2], length)
        length = jnp.where(item % 4 == 3, sc[LENGTHS + 3], length)
        bound[...] = jnp.where((item < 8) & (row < length), 1.0, 0.0).astype(BF16)

    high_lanes = lax.broadcasted_iota(jnp.int32, (HROWS, 128), 1) < 4
    for head in range(PHEADS):
        weights = exps[head]
        low = (grad_heads[head].astype(F32) * inverse[head].astype(F32)).astype(BF16)
        product = low.astype(F32) * mean[head]
        coarse = product.astype(BF16)
        fine = (product - coarse.astype(F32)).astype(BF16)
        delta = dot(coarse, adder[...], 1, 0) + dot(fine, adder[...], 1, 0)
        coarse = delta.astype(BF16)
        fine = (delta - coarse.astype(F32)).astype(BF16)
        left = jnp.concatenate([low, jnp.where(high_lanes, coarse, fine)], axis=1)
        score = dot(left, jnp.concatenate([v_own[head], v_far[head], bound[...]], axis=1), 1, 1)
        grads[step, head_rows(head)] = (score * weights.astype(F32)).astype(BF16)
        back = (dot(weights, low, 0, 0) * mask[...].astype(F32)).astype(BF16)
        own[head] = back[:, : 2 * HEAD]
        far[head] = back[:, 2 * HEAD :]
    for which in range(count):

        @pl.when(step == which)
        def _():
            for copy in leave(which):
                copy.start()
            if which == count - 1:
                for slot in range(count):
                    for copy in leave(slot):
                        copy.wait()


def run_unmix(sc, planes, v_own, v_far, grad_heads, mean, exps, inverse, carry):
    carry, count = list(carry), len(planes)
    return pl.pallas_call(
        partial(unmix_kernel, count, bool(carry)),
        grid_spec=pltpu.PrefetchScalarGridSpec(
            num_scalar_prefetch=1,
            grid=(count,),
            in_specs=[
                plane_spec(planes, LMAX, 2 * HEAD),
                plane_spec(planes, LMAX, 2 * HEAD),
                plane_spec(planes, HROWS, 4 * HEAD),
                plane_spec(planes, HROWS, 4 * HEAD),
                plane_spec(planes, HROWS, LMAX),
                plane_spec(planes, HROWS, 4 * HEAD),
            ]
            + anywhere(len(carry)),
            out_specs=anywhere(4 * count) + [plane_spec(planes, LMAX, 2 * HEAD)] * 2,
            scratch_shapes=[
                pltpu.VMEM((count, 4 * SUBS * HALF, LMAX), BF16),
                pltpu.VMEM((LMAX, 4 * HEAD), BF16),
                pltpu.VMEM((4 * HEAD, 128), BF16),
                pltpu.VMEM((LMAX, 128), BF16),
                pltpu.SemaphoreType.DMA((count, 4)),
            ],
        ),
        out_shape=[jax.ShapeDtypeStruct((SUBS * HALF, LMAX), BF16)] * (4 * count)
        + [jax.ShapeDtypeStruct((HEADS, LMAX, 2 * HEAD), BF16)] * 2,
        input_output_aliases={7 + i: 4 * count + i for i in range(len(carry))},
        compiler_params=params(VMEM),
        cost_estimate=pl.CostEstimate(
            flops=3 * HEADS * HROWS * LMAX * 4 * HEAD,
            bytes_accessed=HEADS * (2 * HROWS * LMAX + 5 * HROWS * 256 + 4 * LMAX * 256),
            transcendentals=0,
        ),
        name="unmix",
    )(sc, v_own, v_far, grad_heads, mean, exps, inverse, *carry)


def close_kernel(sc, tok, res_own, res_got, out_own, out_got, own, far, gain, w_own, w_far, *refs):
    (output, tok_grad, d_value, d_gain, total, weight) = refs
    step = pl.program_id(0)
    whole_weight(sc, step, w_own, w_far, weight)
    core = sc[CORE]
    output[:, :, core] = out_own[...].astype(F32)
    output[:, :, 1 - core] = out_got[...].astype(F32)
    tok_grad[:, :, core] = res_own[...].astype(F32)
    tok_grad[:, :, 1 - core] = res_got[...].astype(F32)
    runs = tok.shape[1]
    rows = runs * 128
    for item in range(2):
        lanes = slice(item * HEAD, (item + 1) * HEAD)
        pieces = [
            add_low(own[head, :, lanes], far[head, :, lanes]) for head in range(HEADS)
        ]
        back = jnp.concatenate(pieces, axis=1)
        x = tok[item].reshape(rows, WIDTH).astype(F32)
        scale = lax.rsqrt(jnp.mean(x * x, axis=-1, keepdims=True) + EPSILON)
        unit = x * scale
        normed = (unit * gain[...]).astype(BF16)
        normed_grad = dot(back, weight[...], 1, 1)
        gained = normed_grad * gain[...]
        update = scale * (gained - unit * jnp.mean(gained * unit, axis=-1, keepdims=True))
        tok_grad[item] += update.reshape(runs, 2, HALF, WIDTH)
        gain_sum = jnp.sum(normed_grad * unit, axis=0, keepdims=True)
        value_sum = dot(normed, back, 0, 0)
        if item == 0:
            gain_total, value_total = gain_sum, value_sum
        else:
            gain_total, value_total = gain_total + gain_sum, value_total + value_sum

    @pl.when(step == 0)
    def _():
        d_gain[...] = gain_total
        total[...] = value_total

    @pl.when(step > 0)
    def _():
        d_gain[...] += gain_total
        total[...] += value_total

    @pl.when(step == pl.num_programs(0) - 1)
    def _():
        d_value[...] = total[...].astype(BF16)


def run_close(sc, tokens, res_own, res_got, out_own, out_got, own, far, gain, w_own, w_far):
    runs = 2
    slab = (2, RUNS, 2, HALF, WIDTH)
    half = (2, RUNS, HALF, WIDTH)
    whole_spec = spec((2, runs, 2, HALF, WIDTH), lambda j, s: (0, j, 0, 0, 0))
    half_spec = spec((2, runs, HALF, WIDTH), lambda j, s: (0, j, 0, 0))
    back_spec = spec((HEADS, runs * 128, 2 * HEAD), lambda j, s: (0, j, 0))
    return pl.pallas_call(
        close_kernel,
        grid_spec=pltpu.PrefetchScalarGridSpec(
            num_scalar_prefetch=1,
            grid=(RUNS // runs,),
            in_specs=[whole_spec]
            + [half_spec] * 4
            + [back_spec, back_spec, held((1, WIDTH)), held((WIDTH, SIDE)), held((WIDTH, SIDE))],
            out_specs=[whole_spec, whole_spec, held((WIDTH, WIDTH)), held((1, WIDTH))],
            scratch_shapes=[pltpu.VMEM((WIDTH, WIDTH), F32), pltpu.VMEM((WIDTH, WIDTH), BF16)],
        ),
        out_shape=[
            jax.ShapeDtypeStruct(slab, F32),
            jax.ShapeDtypeStruct(slab, F32),
            jax.ShapeDtypeStruct((WIDTH, WIDTH), BF16),
            jax.ShapeDtypeStruct((1, WIDTH), F32),
        ],
        compiler_params=params(LESS),
        cost_estimate=pl.CostEstimate(
            flops=4 * 2 * LMAX * WIDTH * WIDTH, bytes_accessed=38 * LMAX * WIDTH, transcendentals=0
        ),
        name="close",
    )(
        sc,
        tokens.reshape(slab),
        *(x.reshape(half) for x in (res_own, res_got, out_own, out_got)),
        own,
        far,
        gain,
        w_own,
        w_far,
    )


PACK_DOWN, PACK_UP, PACK_OUT, PACK_VALUE, PACK_GAIN, PACK = 0, 192, 384, 432, 480, 496


def pack_kernel(sc, down, up, out, value, gain, down_far, up_far, out_far, value_far, gain_far, packed):
    first = sc[CORE] == 0

    def both(own, far, lanes):
        own, far = own[:, lanes], far[:, lanes]
        return jnp.concatenate([jnp.where(first, own, far), jnp.where(first, far, own)], axis=0)

    def side(own, far):
        return both(own, far, own_lanes(sc))

    packed[PACK_DOWN:PACK_UP] = side(down, down_far)
    for j in range(4):
        lanes = pl.ds(pl.multiple_of((4 * sc[CORE] + j) * SIDE, 128), SIDE)
        packed[PACK_UP + 48 * j : PACK_UP + 48 * (j + 1)] = both(up, up_far, lanes)
    packed[PACK_OUT:PACK_VALUE] = side(out, out_far)
    packed[PACK_VALUE:PACK_GAIN] = side(value, value_far)
    packed[PACK_GAIN:] = both(gain, gain_far, slice(0, SIDE))


def run_pack(sc, own, far):
    return pl.pallas_call(
        pack_kernel,
        grid_spec=pltpu.PrefetchScalarGridSpec(
            num_scalar_prefetch=1,
            grid=(1,),
            in_specs=[held(x.shape) for x in (*own, *far)],
            out_specs=held((PACK, SIDE)),
        ),
        out_shape=jax.ShapeDtypeStruct((PACK, SIDE), BF16),
        compiler_params=params(VMEM),
        cost_estimate=pl.CostEstimate(flops=0, bytes_accessed=6 * PACK * SIDE, transcendentals=0),
        name="pack",
    )(sc, *own, *far)


def chip_of(sc, k, rel):
    return plane_of(k, sc) * 4 + (sc[PLACE] ^ rel)


def place_kernel(moves, sc, *refs):
    pieces, targets, sems = refs[:16], refs[16:-1], refs[-1]
    copies = []
    for index, piece in enumerate(pieces):
        chip = chip_of(sc, index // 4, index % 4)
        for which, (start, count, lane, target, step, offset, column) in enumerate(moves):
            rows = pl.ds(pl.multiple_of(chip * step + offset, 16), count)
            copies.append(
                pltpu.make_async_copy(
                    piece.at[pl.ds(start, count), pl.ds(lane, SIDE)],
                    targets[target].at[rows, pl.ds(column, SIDE)],
                    sems.at[index, which],
                )
            )
    for copy in copies:
        copy.start()
    for copy in copies:
        copy.wait()


def run_place(sc, pieces, moves, shapes):
    return pl.pallas_call(
        partial(place_kernel, moves),
        grid_spec=pltpu.PrefetchScalarGridSpec(
            num_scalar_prefetch=1,
            grid=(1,),
            in_specs=anywhere(16),
            out_specs=[held(shape) for shape in shapes],
            scratch_shapes=[pltpu.SemaphoreType.DMA((16, len(moves)))],
        ),
        out_shape=[jax.ShapeDtypeStruct(shape, BF16) for shape in shapes],
        compiler_params=params(VMEM),
        cost_estimate=pl.CostEstimate(
            flops=0, bytes_accessed=4 * sum(a * b for a, b in shapes), transcendentals=0
        ),
        name="place",
    )(sc, *pieces)


def place_weights(sc, pieces):
    moves = (
        (PACK_DOWN, 192, 0, 0, 192, 0, 0),
        *((PACK_UP + 48 * j, 48, 0, 1, 48, 0, j * SIDE) for j in range(4)),
        (PACK_OUT, 48, 0, 2, 48, 0, 0),
        (PACK_VALUE, 48, 0, 3, 48, 0, 0),
        (PACK_GAIN, 16, 0, 4, 16, 0, 0),
    )
    shapes = [(FF, SIDE), (WIDTH, FF // 2), (WIDTH, SIDE), (WIDTH, SIDE), (256, SIDE)]
    return run_place(sc, pieces, moves, shapes)


def collect_kernel(sc, *refs):
    outs = refs[24:]
    for k in range(PLANES):

        @pl.when(pl.program_id(0) == k)
        def _():
            for rel in range(4):
                down, down_got, up, up_got, out, out_got = refs[6 * rel : 6 * rel + 6]
                packed = outs[4 * k + rel]
                packed[PACK_DOWN:PACK_UP] = add_low(down[...], down_got[...])
                for j in range(4):
                    lanes = slice(j * SIDE, (j + 1) * SIDE)
                    packed[PACK_UP + 48 * j : PACK_UP + 48 * (j + 1)] = add_low(up[:, lanes], up_got[:, lanes])
                packed[PACK_OUT:PACK_VALUE] = add_low(out[...], out_got[...])


def run_collect(sc, *sides):
    def rows(x, rel):
        return spec((x.shape[0] // 16, x.shape[1]), lambda k, s: (chip_of(s, k, rel), 0))

    return pl.pallas_call(
        collect_kernel,
        grid_spec=pltpu.PrefetchScalarGridSpec(
            num_scalar_prefetch=1,
            grid=(PLANES,),
            in_specs=[rows(x, rel) for rel in range(4) for x in sides],
            out_specs=[held((PACK_VALUE, SIDE))] * 16,
        ),
        out_shape=[jax.ShapeDtypeStruct((PACK_VALUE, SIDE), BF16)] * 16,
        compiler_params=params(LESS),
        cost_estimate=pl.CostEstimate(flops=0, bytes_accessed=3 * 16 * PACK_VALUE * SIDE * 2, transcendentals=0),
        name="collect",
    )(sc, *(x for _ in range(4) for x in sides))


def add_kernel(groups, *refs):
    for group, total in zip(groups, refs[-len(groups) :]):
        value = refs[group[0]][...].astype(F32)
        for index in group[1:]:
            value = value + refs[index][...].astype(F32)
        total[...] = value.astype(total.dtype)


def run_add(groups, values, dtype):
    shape = values[0].shape
    here = pl.BlockSpec(memory_space=pltpu.VMEM)
    return pl.pallas_call(
        partial(add_kernel, groups),
        in_specs=[here] * len(values),
        out_specs=[here] * len(groups),
        out_shape=[jax.ShapeDtypeStruct(shape, dtype)] * len(groups),
        compiler_params=params(LESS),
        cost_estimate=pl.CostEstimate(
            flops=0, bytes_accessed=2 * shape[0] * shape[1] * (len(values) + len(groups)), transcendentals=0
        ),
        name="add",
    )(*values)


DEVICES = 32
TO_CORE, TO_X, TO_Y = 1, 2, 4


def swap(x, bit):
    return lax.ppermute(x, BOTH, [(d, d ^ bit) for d in range(DEVICES)])


def ring(x, way=1):
    return lax.ppermute(x, BOTH, [(d, (d + 8 * way) % DEVICES) for d in range(DEVICES)])


def pick(x, index, axis=0):
    return lax.dynamic_index_in_dim(x, index, axis, keepdims=False)


def ordered(flag, one, two, axis=0, joined=jnp.stack):
    return jnp.where(flag == 0, joined([one, two], axis), joined([two, one], axis))


def add_low(one, two):
    return (one.astype(F32) + two.astype(F32)).astype(BF16)


STEPS = (
    ((0, 0, 1), (0, 1, 0), (1, 0, 0)),
    ((1, 0, 1), (0, 1, 1), (2, 0, 0)),
    ((2, 0, 1), (1, 1, 0), (3, 0, 0)),
    ((1, 1, 1), (2, 1, 1), (2, 1, 0)),
    ((3, 0, 1), (3, 1, 0), (3, 1, 1)),
)


def gather_step(have, step):
    by_x, by_y, by_z = STEPS[step]
    return {
        **have,
        by_z: ring(have[by_z[0] - 1, by_z[1], by_z[2]]),
        by_x: swap(have[by_x[0], by_x[1], 0], TO_X),
        by_y: swap(have[by_y[0], 0, by_y[2]], TO_Y),
    }


def in_order(have):
    return [have[k, y, x] for k in range(4) for y in range(2) for x in range(2)]


def by_place(shares, planes=range(PLANES)):
    return {(k, i // 2, i % 2): shares[4 * at + i] for at, k in enumerate(planes) for i in range(4)}


def scatter_send(have, step):
    by_x, by_y, by_z = STEPS[len(STEPS) - 1 - step]
    got = (ring(have[by_z], -1), swap(have[by_x], TO_X), swap(have[by_y], TO_Y))
    return {at: value for at, value in have.items() if at not in (by_x, by_y, by_z)}, got


def scatter_add(have, got, step):
    by_x, by_y, by_z = STEPS[len(STEPS) - 1 - step]
    targets = ((by_z[0] - 1, by_z[1], by_z[2]), (by_x[0], by_x[1], 0), (by_y[0], 0, by_y[2]))
    sums = list(dict.fromkeys(targets))
    groups = [(len(got) + i, *(j for j in range(len(got)) if targets[j] == at)) for i, at in enumerate(sums)]
    values = [*got, *(have[at] for at in sums)]
    dtype = F32 if step == len(STEPS) - 1 else BF16
    if values[0].shape[1] == LMAX:
        totals = run_add(groups, values, dtype)
    else:
        totals = [sum(values[i].astype(F32) for i in group).astype(dtype) for group in groups]
    return {**have, **dict(zip(sums, totals))}


together = lax.optimization_barrier


def chip_shards(tokens, lengths, rand_mix, w_value, w_out, w_up, w_down, gain_mix, gain_ffn, grad_out):
    wide = lax.axis_index("wide")
    core = lax.axis_index("narrow")
    z, y, x = wide // 4, (wide // 2) % 2, wide % 2
    other = lambda value: swap(value, TO_CORE)
    side = partial(ordered, core, joined=jnp.concatenate)
    slab = (2, RUNS, 2, HALF, WIDTH)
    tokens, grad_out = tokens.reshape(slab), grad_out.reshape(slab)

    gains = jnp.pad(jnp.concatenate([gain_mix, gain_ffn])[None], ((0, 7), (0, SIDE - 48)))
    own = (w_down, w_up, w_out, w_value, gains)
    far = tuple(other(value) for value in own)
    near_sc = jnp.concatenate([jnp.stack([core, z, wide % 4]).astype(jnp.int32), lengths, lengths])
    weights = {(0, 0, 0): run_pack(near_sc, own, far)}

    rand = rand_mix.reshape(3, 2, HALF, LMAX)
    blocks = side(pick(rand, core, 1), other(pick(rand, 1 - core, 1)), 0)
    weights, rands, late_tokens, late_grad = together(
        (gather_step(weights, 0), {(0, 0, 0): blocks.reshape(SUBS * HALF, LMAX)}, tokens, grad_out)
    )
    weights, tokens_far = together((gather_step(weights, 1), other(pick(late_tokens, 1 - core, 2))))
    weights, grad_far = together((gather_step(weights, 2), other(pick(late_grad, 1 - core, 2))))
    weights, far_lengths = together((gather_step(weights, 3), other(lengths)))
    sc = jnp.concatenate([near_sc[:5], far_lengths])
    weights, rands = together((gather_step(weights, 4), rands))

    rands = gather_step(rands, 0)
    down, up, out, value, gain_rows = place_weights(sc, in_order(weights))
    rands, value, value_far, gain_rows, out, down, up = together(
        (rands, value, other(value), gain_rows, out, down, up)
    )
    gain_rows = gain_rows.reshape(16, 2, 8, SIDE)[:, :, 0]
    gain_one = gain_rows[..., :24].reshape(1, WIDTH).astype(F32)
    gain_two = gain_rows[..., 24:48].reshape(1, WIDTH).astype(F32)
    rands = gather_step(rands, 1)
    v_own = run_values(sc, tokens.reshape(2, LMAX, WIDTH), gain_one, value, value_far)
    rands, v_own, out, down, up = together((rands, v_own, (out, other(out)), down, up))
    rands, v_own, v_far, grad_far, down, up = together(
        (gather_step(rands, 2), v_own, other(v_own), grad_far, down, up)
    )
    rands = gather_step(rands, 3)
    masked = run_masked(sc, grad_out, grad_far)
    rands, v_far, masked, down, up = together((rands, v_far, masked, down, up))
    near = [rands[k, y_at, x_at] for k in range(3) for y_at in range(2) for x_at in range(2)]
    rands = gather_step(rands, 4)
    mixing = run_mix(sc, (0, 1, 2), near, v_own, v_far, ())
    rands, down, up, mixing = together((rands, down, up, mixing))
    heads, mean, exps, inverse = run_mix(sc, (3,), in_order(rands)[12:], v_own, v_far, mixing)
    down, up = (down, other(down)), (up, other(up))

    mixed, resid, normed = run_pre(sc, tokens, tokens_far, heads, out, gain_two)
    active, up_grad = run_units(sc, normed, masked, up, down)
    res_own, res_far, grad_heads, d_gain_two = run_post(sc, resid, up_grad, masked, up, out, gain_two)

    backward = lambda planes, carry: run_unmix(sc, planes, v_own, v_far, grad_heads, mean, exps, inverse, carry)
    *far, back_own, back_far = backward((3,), ())
    far, back_own, back_far, res_got = together((far, back_own, back_far, other(res_far)))
    have, got = scatter_send(by_place(far, (3,)), 0)
    *near, back_own, back_far = backward((2, 1, 0), (back_own, back_far))
    have, got, near, back_own, back_far = together((have, got, near, back_own, back_far))
    have = scatter_add({**have, **by_place(near, (2, 1, 0))}, got, 0)

    have, got = scatter_send(have, 1)
    up_own, up_far = run_up_grad(sc, normed, up_grad)
    have, got, up_own, up_far, back_got = together((have, got, up_own, up_far, other(back_far)))
    have = scatter_add(have, got, 1)

    have, got = scatter_send(have, 2)
    down_own, down_far = run_down_grad(sc, active, masked)
    have, got, down_own, down_far, up_got = together((have, got, down_own, down_far, other(up_far)))
    have = scatter_add(have, got, 2)

    have, got = scatter_send(have, 3)
    d_out_own, d_out_far = run_out_grad(sc, mixed, res_own, res_far)
    packed = run_collect(sc, down_own, other(down_far), up_own, up_got, d_out_own, other(d_out_far))
    have, got, packed = together((have, got, packed))
    have = scatter_add(have, got, 3)

    have, got = scatter_send(have, 4)
    sums, sums_got = scatter_send(by_place(packed), 0)
    out_own, out_far = run_out(sc, active, resid, down)
    have, got, sums, sums_got, out_own, out_far = together((have, got, sums, sums_got, out_own, out_far))
    rand_sum = scatter_add(have, got, 4)[0, 0, 0].reshape(2, 3, HALF, LMAX)

    sums, got = scatter_send(scatter_add(sums, sums_got, 0), 1)
    output, tokens_grad, d_value, d_gain_one = run_close(
        sc, tokens, res_own, res_got, out_own, other(out_far), back_own, back_got, gain_one, value, value_far
    )
    sums, got, output, tokens_grad, d_value, d_gain_one = together(
        (sums, got, output, tokens_grad, d_value, d_gain_one)
    )
    sums = scatter_add(sums, got, 1)

    sums, got = scatter_send(sums, 2)
    gain_pair = jnp.stack([d_gain_one.reshape(16, 2, 24), d_gain_two.reshape(16, 2, 24)], 2).reshape(16, 2, 1, 48)
    gain_pair = jnp.pad(gain_pair.astype(BF16), ((0, 0), (0, 0), (0, 7), (0, WIDTH - 48)))
    small = jnp.concatenate([d_value.reshape(16, 2, 24, WIDTH), gain_pair], 2).reshape(4, 2, 2, 2, 32, WIDTH)
    small = add_low(pick(small, core, 3), other(pick(small, 1 - core, 3)))
    small = add_low(pick(small, x, 2), swap(pick(small, 1 - x, 2), TO_X))
    sums, got, small = together((sums, got, small))
    sums = scatter_add(sums, got, 2)

    sums, got = scatter_send(sums, 3)
    small = add_low(pick(small, y, 1), swap(pick(small, 1 - y, 1), TO_Y))
    blocks, blocks_far = pick(rand_sum, core), other(pick(rand_sum, 1 - core))
    sums, got, small, blocks, blocks_far = together((sums, got, small, blocks, blocks_far))
    sums = scatter_add(sums, got, 3)

    sums, got = scatter_send(sums, 4)
    small_sum = pick(small, z).astype(F32)
    for k in range(1, PLANES):
        small_sum = small_sum + ring(pick(small, lax.rem(z + PLANES - k, PLANES)), -k).astype(F32)
    sums, got, small_sum = together((sums, got, small_sum))
    big_sum = scatter_add(sums, got, 4)[0, 0, 0]
    big_far = other(big_sum.astype(BF16)).astype(F32)

    rows_of = lambda value, rows: pick(value.reshape(-1, 2, rows, SIDE), core, 1)
    mine = lambda own, far, rows: side(rows_of(own, rows)[0], rows_of(far, rows)[0], 1)
    down_shard = mine(big_sum[PACK_DOWN:PACK_UP], big_far[PACK_DOWN:PACK_UP], 96)
    up_side = lambda value: rows_of(value[PACK_UP:PACK_OUT], 24).transpose(1, 0, 2).reshape(24, 4 * SIDE)
    up_shard = side(up_side(big_sum), up_side(big_far), 1)
    outproj_shard = mine(big_sum[PACK_OUT:PACK_VALUE], big_far[PACK_OUT:PACK_VALUE], 24)
    rand_shard = ordered(core, blocks, blocks_far, 1)

    return (
        output.reshape(2, LMAX, WIDTH),
        tokens_grad.reshape(2, LMAX, WIDTH),
        rand_shard.reshape(3 * 128, LMAX),
        small_sum[:24],
        outproj_shard,
        up_shard,
        down_shard,
        small_sum[24, :24],
        small_sum[24, 24:48],
    )


def rms_norm(values, gain):
    scale = lax.rsqrt(jnp.mean(values * values, axis=-1, keepdims=True) + EPSILON)
    return values * scale * gain


def split_heads(block):
    return block.reshape(LMAX, HEADS, HEAD).transpose(1, 0, 2)


def merge_heads(block):
    return block.transpose(1, 0, 2).reshape(LMAX, HEADS * HEAD)


def masked_scores(key_mask, rand_head):
    return jnp.where(key_mask[None, :] > 0, rand_head.astype(jnp.float32), -1e30)


def head_forward(key_mask, paired):
    rand_head, value_head = paired
    scores = masked_scores(key_mask, rand_head)
    row_peak = jnp.max(scores, axis=-1, keepdims=True)
    exponent = jnp.exp(scores - row_peak)
    denom_sum = jnp.sum(exponent, axis=-1, keepdims=True)
    attention = exponent / denom_sum * key_mask[:, None]
    mixed = jnp.dot(attention.astype(jnp.bfloat16), value_head, preferred_element_type=jnp.float32)
    return (mixed.astype(jnp.bfloat16), row_peak + jnp.log(denom_sum))


def head_backward(key_mask, paired):
    rand_head, value_head, mix_grad, log_total = paired
    scores = masked_scores(key_mask, rand_head)
    attention = jnp.exp(scores - log_total) * key_mask[:, None]
    prob_grad = jnp.einsum("id,jd->ij", mix_grad, value_head, preferred_element_type=jnp.float32)
    value_grad = jnp.einsum(
        "ij,id->jd", attention.astype(jnp.bfloat16), mix_grad, preferred_element_type=jnp.float32
    )
    score_grad = attention * (prob_grad - jnp.sum(prob_grad * attention, axis=-1, keepdims=True))
    return (score_grad, value_grad)


def shards(tokens, lengths, rand_mix, w_value, w_out, w_up, w_down, gain_mix, gain_ffn, grad_out):
    item_count = tokens.shape[0]
    width = tokens.shape[2]
    row_count = item_count * LMAX
    tokens_flat = tokens.reshape(row_count, width).astype(jnp.float32)
    positions = jnp.arange(LMAX, dtype=jnp.int32)
    valid_table = (positions[None, :] < lengths[:, None]).astype(jnp.float32)
    row_valid = valid_table.reshape(row_count, 1)
    forward_set = (
        lax.all_gather(rand_mix, ("wide", "narrow"), axis=0, tiled=True),
        lax.all_gather(w_value, ("wide", "narrow"), axis=0, tiled=True),
        lax.all_gather(w_out, ("wide", "narrow"), axis=0, tiled=True),
        lax.all_gather(w_up, ("wide", "narrow"), axis=0, tiled=True),
        lax.all_gather(w_down, ("wide", "narrow"), axis=0, tiled=True),
        lax.all_gather(gain_mix, ("wide", "narrow"), axis=0, tiled=True),
        lax.all_gather(gain_ffn, ("wide", "narrow"), axis=0, tiled=True),
    )
    rand_all, value_all, out_all, up_all, down_all, gain_first, gain_second = forward_set
    normed = rms_norm(tokens_flat, gain_first.astype(jnp.float32)).astype(jnp.bfloat16)
    values = jnp.dot(normed, value_all, preferred_element_type=jnp.float32).astype(jnp.bfloat16)
    rand_heads = rand_all.reshape(HEADS, LMAX, LMAX)
    mixed_parts = []
    totals_kept = []
    for item_index in range(item_count):
        item_values = split_heads(values[item_index * LMAX : (item_index + 1) * LMAX])
        mixed_heads, log_total = lax.map(
            partial(head_forward, valid_table[item_index]), (rand_heads, item_values)
        )
        mixed_parts.append(merge_heads(mixed_heads))
        totals_kept.append(log_total)
    mixed = jnp.concatenate(mixed_parts, axis=0)
    residual = tokens_flat + jnp.dot(mixed, out_all, preferred_element_type=jnp.float32)
    normed_two = rms_norm(residual, gain_second.astype(jnp.float32)).astype(jnp.bfloat16)
    up_proj = jnp.dot(normed_two, up_all, preferred_element_type=jnp.float32)
    active = jax.nn.gelu(up_proj).astype(jnp.bfloat16)
    branch = jnp.dot(active, down_all, preferred_element_type=jnp.float32)
    output = row_valid * (residual + branch)
    back_set = (
        lax.all_gather(rand_mix, ("wide", "narrow"), axis=0, tiled=True),
        lax.all_gather(w_value, ("wide", "narrow"), axis=0, tiled=True),
        lax.all_gather(w_out, ("wide", "narrow"), axis=0, tiled=True),
        lax.all_gather(w_up, ("wide", "narrow"), axis=0, tiled=True),
        lax.all_gather(w_down, ("wide", "narrow"), axis=0, tiled=True),
        lax.all_gather(gain_mix, ("wide", "narrow"), axis=0, tiled=True),
        lax.all_gather(gain_ffn, ("wide", "narrow"), axis=0, tiled=True),
    )
    rand_back, value_back, out_back, up_back, down_back, gain_back_one, gain_back_two = back_set
    cotangent = grad_out.reshape(row_count, width).astype(jnp.float32)
    masked = row_valid * cotangent
    branch_grad = masked.astype(jnp.bfloat16)
    grad_down = jnp.einsum("rk,rd->kd", active, branch_grad, preferred_element_type=jnp.float32)
    active_grad = jnp.einsum(
        "rd,kd->rk", branch_grad, down_back, preferred_element_type=jnp.float32
    )
    gelu_value, gelu_pull = jax.vjp(jax.nn.gelu, up_proj)
    up_grad = gelu_pull(active_grad)[0].astype(jnp.bfloat16)
    grad_up = jnp.einsum("rd,rk->dk", normed_two, up_grad, preferred_element_type=jnp.float32)
    normed_two_grad = jnp.einsum("rk,dk->rd", up_grad, up_back, preferred_element_type=jnp.float32)
    norm_value, norm_pull = jax.vjp(rms_norm, residual, gain_back_two.astype(jnp.float32))
    residual_part, gain_two_grad = norm_pull(normed_two_grad)
    residual_grad = masked + residual_part
    attn_grad = residual_grad.astype(jnp.bfloat16)
    grad_outproj = jnp.einsum("rd,re->de", mixed, attn_grad, preferred_element_type=jnp.float32)
    mixed_grad = jnp.einsum(
        "re,de->rd", attn_grad, out_back, preferred_element_type=jnp.float32
    ).astype(jnp.bfloat16)
    rand_heads_back = rand_back.reshape(HEADS, LMAX, LMAX)
    rand_grad = jnp.zeros((HEADS, LMAX, LMAX), jnp.float32)
    value_parts = []
    for item_index in range(item_count):
        lower_row = item_index * LMAX
        upper_row = lower_row + LMAX
        item_values = split_heads(values[lower_row:upper_row])
        item_mix_grad = split_heads(mixed_grad[lower_row:upper_row])
        score_grad, value_grad = lax.map(
            partial(head_backward, valid_table[item_index]),
            (rand_heads_back, item_values, item_mix_grad, totals_kept[item_index]),
        )
        rand_grad = rand_grad + score_grad
        value_parts.append(merge_heads(value_grad))
    values_grad = jnp.concatenate(value_parts, axis=0).astype(jnp.bfloat16)
    grad_value = jnp.einsum("rd,re->de", normed, values_grad, preferred_element_type=jnp.float32)
    normed_grad = jnp.einsum(
        "re,de->rd", values_grad, value_back, preferred_element_type=jnp.float32
    )
    norm_first, first_pull = jax.vjp(rms_norm, tokens_flat, gain_back_one.astype(jnp.float32))
    token_part, gain_one_grad = first_pull(normed_grad)
    tokens_grad = residual_grad + token_part
    rand_flat = rand_grad.reshape(HEADS * LMAX, LMAX)
    all_shards = (
        lax.psum_scatter(rand_flat, ("wide", "narrow"), scatter_dimension=0, tiled=True),
        lax.psum_scatter(grad_value, ("wide", "narrow"), scatter_dimension=0, tiled=True),
        lax.psum_scatter(grad_outproj, ("wide", "narrow"), scatter_dimension=0, tiled=True),
        lax.psum_scatter(grad_up, ("wide", "narrow"), scatter_dimension=0, tiled=True),
        lax.psum_scatter(grad_down, ("wide", "narrow"), scatter_dimension=0, tiled=True),
        lax.psum_scatter(gain_one_grad, ("wide", "narrow"), scatter_dimension=0, tiled=True),
        lax.psum_scatter(gain_two_grad, ("wide", "narrow"), scatter_dimension=0, tiled=True),
    )
    rand_shard, value_shard, outproj_shard, up_shard, down_shard, gain_one_shard, gain_two_shard = (
        all_shards
    )
    return (
        output.reshape(item_count, LMAX, width),
        tokens_grad.reshape(item_count, LMAX, width),
        rand_shard,
        value_shard,
        outproj_shard,
        up_shard,
        down_shard,
        gain_one_shard,
        gain_two_shard,
    )


def solution(mesh):
    in_specs = (
        P(("wide", "narrow"), None, None),
        P(("wide", "narrow")),
        P(("wide", "narrow"), None),
        P(("wide", "narrow"), None),
        P(("wide", "narrow"), None),
        P(("wide", "narrow"), None),
        P(("wide", "narrow"), None),
        P(("wide", "narrow")),
        P(("wide", "narrow")),
        P(("wide", "narrow"), None, None),
    )
    out_specs = (
        P(("wide", "narrow"), None, None),
        P(("wide", "narrow"), None, None),
        P(("wide", "narrow"), None),
        P(("wide", "narrow"), None),
        P(("wide", "narrow"), None),
        P(("wide", "narrow"), None),
        P(("wide", "narrow"), None),
        P(("wide", "narrow")),
        P(("wide", "narrow")),
    )
    fits = dict(mesh.shape) == {"wide": 16, "narrow": 2}
    return jax.shard_map(chip_shards if fits else shards, mesh=mesh, in_specs=in_specs, out_specs=out_specs, check_vma=False)
```
